32 devices in a mesh: dp: 8 (over y, x, core), fsdp: 4 (over z).
Axes of the slice: x: 2, y: 2, z: 4, core: 2. Of those that a mesh axis runs over, the one named last changes fastest.
Arguments:
- tokens: bfloat16 [32768, 768], P(('dp', 'fsdp')), may hold values from -6 to 6
- segment: int32 [64, 512], P(('dp', 'fsdp')), may hold values from 0 to 3, never falling along the last dimension, each value on 1 to 256 neighbouring positions
- blocks: float32 [24, 768, 768], P(None, ('dp', 'fsdp')), may hold values from -0.8660254 to 0.8660254
- vectors: float32 [2, 12, 768], P(None, None, ('dp', 'fsdp')), may hold values from -1.2 to 1.2
- owner: int32 [24], replicated, may hold values from 0 to 7, as said below
- left_basis: float32 [40, 8, 96, 768], P('dp', None, 'fsdp'), may hold values from -1 to 1, as said below
- right_basis: float32 [40, 768, 768], P('dp', None, 'fsdp'), may hold values from -1 to 1, as said below
- rot_first: float32 [40, 768, 768], P('dp', None, 'fsdp'), may hold values from -512 to 512
- rot_second: float32 [40, 768, 768], P('dp', None, 'fsdp'), may hold values from 8192 to 32768
- vec_first: float32 [2, 12, 768], P(None, None, ('dp', 'fsdp')), may hold values from -512 to 512
- vec_second: float32 [2, 12, 768], P(None, None, ('dp', 'fsdp')), may hold values from 8192 to 32768
- cotangent: bfloat16 [32768, 768], P(('dp', 'fsdp')), may hold values from -6 to 6
Outputs:
- layer_out: bfloat16 [32768, 768], P(('dp', 'fsdp'))
- input_grad: float32 [32768, 768], P(('dp', 'fsdp'))
- new_blocks: float32 [24, 768, 768], P(None, ('dp', 'fsdp'))
- new_blocks_low: bfloat16 [24, 768, 768], P(None, ('dp', 'fsdp'))
- first_new: float32 [40, 768, 768], P('dp', None, 'fsdp')
- second_new: float32 [40, 768, 768], P('dp', None, 'fsdp')
- vector_first: float32 [2, 12, 768], P(None, None, ('dp', 'fsdp'))
- vector_second: float32 [2, 12, 768], P(None, None, ('dp', 'fsdp'))
- vector_new: float32 [2, 12, 768], P(None, None, ('dp', 'fsdp'))
The draws below stay inside these ranges and needn't reach their ends.
Inputs may be any that keep to these rules, and one draw needn't show every extreme that they name: `segment`: each row holds 4 segments numbered from 0, never falling along the row, each of 1 to 256 tokens, one of exactly 256. `owner`: no dp index is named by more than 5 blocks, and one is named by exactly 5. `left_basis`: each slot's matrix, read as [768, 768], is orthogonal. `right_basis`: each slot's matrix is orthogonal.
All inputs are finite; a program needn't handle non-finite values.
Results may differ from the reference program's by a relative error of at most 0.02.
Values may be sent and summed in bfloat16 or wider, within the bound.
A program may use at most 320 MiB of HBM per device.

```python
import math
import jax
import jax.numpy as jnp
import numpy as np
from jax import lax

D = 768
H = 12
HD = 64
FF = 3072
L = 512
LAYERS = 2
SEGS = 4
STEP = 5
ROWS = 64
TOKENS = 32768
NBLK = 24
SLOTS = 5
SLOTS_ALL = 40
N_DP = 8


def orthogonal_stack(key, number):
    sign_key, order_key = jax.random.split(key)
    position = jnp.arange(D, dtype=jnp.float32)
    frequency = jnp.arange(D, dtype=jnp.float32)
    cosine_table = jnp.cos(jnp.pi * (position[:, None] + 0.5) * frequency[None, :] / D) * jnp.sqrt(2.0 / D)
    cosine_table = cosine_table * jnp.where(jnp.arange(D) == 0, 0.5 ** 0.5, 1.0)[None, :]
    signs = (jax.random.randint(sign_key, (number, D), 0, 2) * 2 - 1).astype(jnp.float32)
    orders = jax.vmap(lambda sub_key: jax.random.permutation(sub_key, D))(jax.random.split(order_key, number))
    columns = jnp.transpose(cosine_table[:, orders], (1, 0, 2))
    return signs[:, :, None] * columns


def draw_blocks(key, part):
    key = jax.random.fold_in(key, 11)
    block_kind = jnp.arange(NBLK) % 12
    spread = jnp.where(block_kind >= 8, (1.0 / FF) ** 0.5, (1.0 / D) ** 0.5)
    spread = spread * jnp.where(block_kind == 3, 6.0, 1.0)
    values = jax.random.truncated_normal(key, -4.0, 4.0, (NBLK, D, D), jnp.float32)
    return values * spread[:, None, None]


def draw_vectors(key, part):
    key = jax.random.fold_in(key, 12)
    gain_key, bias_key = jax.random.split(key)
    row_kind = jnp.arange(12)
    is_gain = (row_kind == 3) | (row_kind == 10)
    gains = 1.0 + 0.2 * jax.random.uniform(gain_key, (LAYERS, 12, D), jnp.float32, -1.0, 1.0)
    biases = 0.3 * jax.random.truncated_normal(bias_key, -4.0, 4.0, (LAYERS, 12, D), jnp.float32)
    return jnp.where(is_gain[None, :, None], gains, biases)


def draw_owner(key, part):
    key = jax.random.fold_in(key, 13)
    first_key, second_key, third_key = jax.random.split(key, 3)
    busiest = jax.random.randint(first_key, (), 0, N_DP)
    others = (busiest + 1 + jnp.arange((N_DP - 1) * SLOTS) // SLOTS) % N_DP
    others = jax.random.permutation(second_key, others)[:NBLK - SLOTS]
    owner_rows = jnp.concatenate([jnp.full((SLOTS,), busiest, dtype=jnp.int32), others.astype(jnp.int32)])
    return jax.random.permutation(third_key, owner_rows).astype(jnp.int32)


def draw_left_basis(key, part):
    key = jax.random.fold_in(key, 14)
    return orthogonal_stack(key, SLOTS_ALL).reshape(SLOTS_ALL, N_DP, D // N_DP, D)


def draw_right_basis(key, part):
    key = jax.random.fold_in(key, 15)
    return orthogonal_stack(key, SLOTS_ALL)


def levels(stream_key, extent, cuts, least, top_value):
    gain, own = 1.0, jax.random.fold_in(stream_key, 6)
    for axis_at, parts in cuts:
        steps = jnp.exp(jax.random.uniform(jax.random.fold_in(own, axis_at), (parts,), jnp.float32, least / len(cuts), top_value / len(cuts)))
        gain = gain * jnp.repeat(steps, extent[axis_at] // parts).reshape([-1 if axis == axis_at else 1 for axis in range(len(extent))])
    return gain


def length_profile(amount, total, bound, lean):
    portions = [(1 << 20) // math.isqrt(rank ** lean) + 1 for rank in range(2, amount + 1)]
    rest, counts = total - bound - (amount - 1), [1] * (amount - 1)
    while rest > 0:
        movable = [i for i in range(amount - 1) if counts[i] < bound]
        mass, budget = sum([portions[i] for i in movable]), rest
        for i in movable:
            addition = min(bound - counts[i], max(1, budget * portions[i] // mass), rest)
            counts[i] = counts[i] + addition
            rest = rest - addition
    return np.array([bound] + counts)


def uneven(own_key, amount, total, bound, slope):
    if amount == 2:
        one = jax.random.randint(own_key, (), max(1, total - bound), min(bound, total - 1) + 1)
        return jnp.stack([one, total - one])
    tallies = jnp.asarray(length_profile(amount, total, bound, slope), jnp.int32)
    twos = (amount - 1) // 2
    donor, sink = tallies[1:1 + 2 * twos:2], tallies[2:2 + 2 * twos:2]
    room = jnp.minimum(donor - 1, bound - sink)
    passed = jax.random.randint(jax.random.fold_in(own_key, 1), (twos,), 0, 1 << 20) % (room + 1)
    tallies = tallies.at[1:1 + 2 * twos:2].set(donor - passed).at[2:2 + 2 * twos:2].set(sink + passed)
    return tallies[jax.random.permutation(jax.random.fold_in(own_key, 2), amount)]


def normal_values(stream_key, extent, deviation, most, shards=(), kind=jnp.bfloat16):
    array = jax.random.normal(stream_key, extent, jnp.float32) * deviation
    if len(shards) > 0:
        array = levels(stream_key, extent, shards, -0.22, 0.18) * array
    return jnp.clip(array, min=-most, max=most).astype(kind)


def setup_inputs(seed: int = 0) -> dict:
    keys = jax.random.split(jax.random.key(seed), 13)
    return {
        "tokens": normal_values(keys[0], (TOKENS, D), 1.0, 6.0, ((0, 32),)),
        "segment": jax.vmap(lambda own: jnp.searchsorted(jnp.cumsum(uneven(own, SEGS, L, L // 2, 1)), jnp.arange(L), side="right"))(jax.random.split(keys[1], ROWS)).reshape((ROWS, L)).astype(jnp.int32),
        "blocks": draw_blocks(jax.random.fold_in(keys[12], 71), 0),
        "vectors": draw_vectors(jax.random.fold_in(keys[12], 71), 0),
        "owner": draw_owner(jax.random.fold_in(keys[12], 71), 0),
        "left_basis": draw_left_basis(jax.random.fold_in(keys[12], 71), 0),
        "right_basis": draw_right_basis(jax.random.fold_in(keys[12], 71), 0),
        "rot_first": normal_values(keys[7], (SLOTS_ALL, D, D), (0.5 * TOKENS ** 0.5), 512.0, ((0, 8), (2, 4)), jnp.float32),
        "rot_second": jnp.clip(jnp.exp(math.log(32768.0) - 1.3862944 * jax.random.uniform(keys[8], (SLOTS_ALL, D, D), jnp.float32) ** levels(keys[8], (SLOTS_ALL, D, D), ((0, 8), (2, 4)), -0.2, 0.2)), 8192.0, 32768.0),
        "vec_first": normal_values(keys[9], (LAYERS, 12, D), (0.5 * TOKENS ** 0.5), 512.0, ((2, 32),), jnp.float32),
        "vec_second": jnp.clip(jnp.exp(math.log(32768.0) - 1.3862944 * jax.random.uniform(keys[10], (LAYERS, 12, D), jnp.float32) ** levels(keys[10], (LAYERS, 12, D), ((2, 32),), -0.2, 0.2)), 8192.0, 32768.0),
        "cotangent": normal_values(keys[11], (TOKENS, D), 1.0, 6.0, ((0, 32),)),
    }


@jax.custom_vjp
def low(v):
    return lax.optimization_barrier(v.astype(jnp.bfloat16)).astype(jnp.float32)

@jax.custom_vjp
def low_back(v):
    return v

def low_keep(v):
    return (low(v), None)

def low_pass(kept, grad):
    return (grad,)

def back_keep(v):
    return (v, None)

def back_low(kept, grad):
    return (low(grad),)
low.defvjp(low_keep, low_pass)
low_back.defvjp(back_keep, back_low)
highest = lax.Precision.HIGHEST
beta_one = 0.5
beta_two = 0.5
adam_epsilon = 1e-08
norm_epsilon = 1e-06
matrix_rate = 0.03
vector_rate = 0.2
weight_decay = 0.01
masked_score = -1e+30

def layer_norm(residual, norm_gain, norm_shift):
    average = lax.optimization_barrier(jnp.mean(residual, axis=-1, keepdims=True))
    centered = residual - average
    variance = lax.optimization_barrier(jnp.mean(centered * centered, axis=-1, keepdims=True))
    return centered * lax.rsqrt(variance + norm_epsilon) * norm_gain + norm_shift

def project(values, matrix):
    return jnp.einsum('gld,de->gle', values, matrix, precision=highest)

def encoder_layer(hidden_in, segment_block, weights, vectors):
    groups, length, model_width = hidden_in.shape
    inputs_low = low(hidden_in)
    query_rows = low_back(low(project(inputs_low, weights[0]) + vectors[0]))
    key_rows = low_back(low(project(inputs_low, weights[1])))
    value_rows = low_back(low(project(inputs_low, weights[2]) + vectors[1]))
    query_heads = query_rows.reshape(groups, length, H, HD)
    key_heads = key_rows.reshape(groups, length, H, HD)
    value_heads = value_rows.reshape(groups, length, H, HD)
    scores = low_back(jnp.einsum('gqhc,gkhc->ghqk', query_heads, key_heads, precision=highest) * HD ** (-0.5))
    allowed = segment_block[:, :, None] == segment_block[:, None, :]
    scores = jnp.where(allowed[:, None, :, :], scores, masked_score)
    attention = low(jax.nn.softmax(scores, axis=-1))
    context = jnp.einsum('ghqk,gkhc->gqhc', attention, value_heads, precision=highest).reshape(groups, length, model_width)
    context = low_back(low(context))
    attended = low_back(project(context, weights[3]) + vectors[2])
    normed = layer_norm(hidden_in + attended, vectors[3], vectors[4])
    expanded = jnp.einsum('gld,cde->glce', low(normed), weights[4:8], precision=highest)
    preact = low_back(expanded + vectors[5:9])
    active = low(jax.nn.gelu(preact, approximate=False))
    branch = low_back(jnp.einsum('glce,ced->gld', active, weights[8:12], precision=highest) + vectors[9])
    return layer_norm(normed + branch, vectors[10], vectors[11])

def encode_all(inputs, blocks, vectors, segment):
    weights = low(blocks)
    vector_low = low(vectors)
    rows_total = segment.shape[0]
    per_group = math.gcd(rows_total, max(1, 4096 // L))
    grouped = inputs.reshape(rows_total // per_group, per_group, L, D)
    segment_groups = segment.reshape(rows_total // per_group, per_group, L)

    def run_group(carried):
        hidden_state, segment_block = carried
        for layer_index in range(LAYERS):
            hidden_state = encoder_layer(hidden_state, segment_block, weights[12 * layer_index:12 * layer_index + 12], vector_low[layer_index])
        return hidden_state
    outputs = lax.map(jax.checkpoint(run_group), (grouped, segment_groups))
    return outputs.reshape(rows_total * L, D)

def slot_table(owner, slots, owner_rows):
    block_count = owner.shape[0]
    same_owner = owner[:, None] == owner[None, :]
    ordering = jnp.arange(block_count, dtype=jnp.int32)
    earlier = ordering[None, :] < ordering[:, None]
    ranking = lax.optimization_barrier(jnp.sum(jnp.where(same_owner & earlier, 1, 0), axis=1)).astype(jnp.int32)
    owner_match = owner[None, :] == jnp.arange(owner_rows, dtype=jnp.int32)[:, None]
    slot_match = ranking[None, :] == jnp.arange(slots, dtype=jnp.int32)[:, None]
    return jnp.where(slot_match[:, None, :] & owner_match[None, :, :], 1.0, 0.0).astype(jnp.float32)

def reference(tokens, segment, blocks, vectors, owner, left_basis, right_basis, rot_first, rot_second, vec_first, vec_second, cotangent):
    inputs = tokens.astype(jnp.float32)

    def forward_all(input_values, block_values, vector_values):
        return encode_all(input_values, block_values, vector_values, segment)
    outputs, pullback = jax.vjp(forward_all, inputs, blocks, vectors)
    input_grad, block_grad, vector_grad = pullback(cotangent.astype(jnp.float32))
    layer_out = outputs.astype(jnp.bfloat16)
    selector = slot_table(owner, SLOTS, N_DP)
    owned = jnp.einsum('srk,kab->rsab', selector, block_grad, precision=highest).reshape(SLOTS * N_DP, D, D)
    left_full = left_basis.reshape(SLOTS * N_DP, D, D)
    turned = jnp.matmul(owned, right_basis, precision=highest)
    rotated = jnp.einsum('sra,srb->sab', left_full, turned, precision=highest)
    first_new = beta_one * rot_first + (1.0 - beta_one) * rotated
    second_new = beta_two * rot_second + (1.0 - beta_two) * rotated * rotated
    direction = first_new / (1.0 - beta_one ** STEP) / (jnp.sqrt(second_new / (1.0 - beta_two ** STEP)) + adam_epsilon)
    back_right = jnp.einsum('sab,scb->sac', direction, right_basis, precision=highest)
    slot_steps = jnp.matmul(left_full, back_right, precision=highest)
    block_steps = jnp.einsum('srk,rsab->kab', selector, slot_steps.reshape(N_DP, SLOTS, D, D), precision=highest)
    new_blocks = blocks - matrix_rate * (block_steps + weight_decay * blocks)
    vector_first = beta_one * vec_first + (1.0 - beta_one) * vector_grad
    vector_second = beta_two * vec_second + (1.0 - beta_two) * vector_grad * vector_grad
    vector_step = vector_first / (1.0 - beta_one ** STEP) / (jnp.sqrt(vector_second / (1.0 - beta_two ** STEP)) + adam_epsilon)
    vector_new = vectors - vector_rate * (vector_step + weight_decay * vectors)
    return (layer_out, input_grad, new_blocks, new_blocks.astype(jnp.bfloat16), first_new, second_new, vector_first, vector_second, vector_new)
```

```python
import functools

import jax
import jax.numpy as jnp
from jax import lax
from jax.experimental import pallas as pl
from jax.experimental.pallas import tpu as pltpu
from jax.sharding import PartitionSpec as P

H = 12
HD = 64
L = 512
STEP = 5
PAIR = 2 * HD
MIB = 1 << 20

beta_one = 0.5
beta_two = 0.5
adam_epsilon = 1e-08
norm_epsilon = 1e-06
matrix_rate = 0.03
vector_rate = 0.2
weight_decay = 0.01
masked_score = -1e30
low = jnp.bfloat16
full = jnp.float32


def dot_nn(a, b):
    return lax.dot_general(a, b, (((1,), (0,)), ((), ())), preferred_element_type=full)


def dot_nt(a, b):
    return lax.dot_general(a, b, (((1,), (1,)), ((), ())), preferred_element_type=full)


def dot_tn(a, b):
    return lax.dot_general(a, b, (((0,), (0,)), ((), ())), preferred_element_type=full)


def gelu_parts(z):
    size = jnp.abs(z) * 0.7071067811865476
    t = 1.0 / (1.0 + 0.3275911 * size)
    bell = jnp.exp(-0.5 * z * z)
    poly = ((((1.061405429 * t - 1.453152027) * t + 1.421413741) * t - 0.284496736) * t + 0.254829592) * t
    half_tail = 0.5 * poly * bell
    phi = jnp.where(z >= 0, 1.0 - half_tail, half_tail)
    return z * phi, phi + z * bell * 0.3989422804014327


def norm_parts(residual):
    average = jnp.mean(residual, axis=-1, keepdims=True)
    centered = residual - average
    inverse = lax.rsqrt(jnp.mean(centered * centered, axis=-1, keepdims=True) + norm_epsilon)
    return centered * inverse, inverse


def norm_back(upstream, unit, inverse, gain):
    scaled = upstream * gain
    return inverse * (
        scaled
        - jnp.mean(scaled, axis=-1, keepdims=True)
        - unit * jnp.mean(scaled * unit, axis=-1, keepdims=True)
    )


def column_sum(values):
    return jnp.sum(values, axis=0, keepdims=True)


def half_masks(dtype):
    lane = lax.broadcasted_iota(jnp.int32, (1, PAIR), 1)
    first = (lane < HD).astype(full)
    return first.astype(dtype), (1.0 - first).astype(dtype)


def segment_bias(seg_column, seg_row):
    return jnp.where(seg_column == seg_row, 0.0, masked_score)


def forward_kernel(
    x_ref, segc_ref, segr_ref, vec_ref, w_hbm,
    q_ref, k_ref, v_ref, ctxt_ref, lse_ref, x1_ref, inv1_ref, n1_ref, u_ref, gp_ref, x2_ref, inv2_ref, out_ref,
    w, bias, vt, n1_keep, w_sem,
):
    first = pl.program_id(0) == 0
    blocks = w.shape[0]
    width = x_ref.shape[1]
    tokens = x_ref.shape[0]

    def arrive(j):
        @pl.when(first)
        def _():
            pltpu.make_async_copy(w_hbm.at[j], w.at[j], w_sem.at[j]).wait()

    @pl.when(first)
    def _():
        for j in range(blocks):
            pltpu.make_async_copy(w_hbm.at[j], w.at[j], w_sem.at[j]).start()

    xin = x_ref[...].astype(low)
    bias[...] = segment_bias(segc_ref[0], segr_ref[0])
    arrive(0)
    q_ref[...] = (dot_nn(xin, w[0]) + vec_ref[0:1, :]).astype(low)
    arrive(1)
    k_ref[...] = dot_nn(xin, w[1]).astype(low)
    arrive(2)
    value = dot_nn(xin, w[2]) + vec_ref[1:2, :]
    v_ref[...] = value.astype(low)
    vt[...] = value.T.astype(low)
    masks = half_masks(low)

    def pair_step(p, carry):
        lanes = pl.ds(pl.multiple_of(p * PAIR, PAIR), PAIR)
        q_pair = q_ref[:, lanes] * jnp.asarray(HD ** (-0.5), low)
        k_pair = k_ref[:, lanes]
        for h in range(2):
            scores = dot_nt(k_pair, q_pair * masks[h]) + bias[...]
            largest = jnp.max(scores, axis=0, keepdims=True)
            expanded = jnp.exp(scores - largest)
            total = column_sum(expanded)
            rows = pl.ds(pl.multiple_of(p * PAIR + h * HD, HD), HD)
            context = dot_nn(vt[rows, :], expanded.astype(low)) * (1.0 / total)
            ctxt_ref[rows, :] = context.astype(low)
            lse_ref[0, pl.ds(2 * p + h, 1), :] = largest + jnp.log(total)
        return carry

    lax.fori_loop(0, width // PAIR, pair_step, 0)
    arrive(3)
    context = ctxt_ref[...].astype(full).T.astype(low)
    attended = dot_nn(context, w[3]) + vec_ref[2:3, :]
    unit, inverse = norm_parts(x_ref[...].astype(full) + attended)
    x1_ref[...] = unit
    inv1_ref[...] = inverse
    normed = unit * vec_ref[3:4, :] + vec_ref[4:5, :]
    n1_keep[...] = normed
    n1_ref[...] = normed.astype(low)
    for j in range(4, blocks):
        arrive(j)
    tile = tokens // 2
    inner = (blocks - 4) // 2

    def token_step(i, carry):
        rows = pl.ds(pl.multiple_of(i * tile, tile), tile)
        n1_low = n1_ref[rows, :]
        branch = jnp.zeros((tile, width), full)
        for c in range(inner):
            columns = slice(c * width, (c + 1) * width)
            value, slope = gelu_parts(dot_nn(n1_low, w[4 + c]) + vec_ref[5 + c : 6 + c, :])
            active = value.astype(low)
            u_ref[rows, columns] = active
            gp_ref[rows, columns] = slope.astype(low)
            branch = branch + dot_nn(active, w[4 + inner + c])
        base = 5 + inner
        unit, inverse = norm_parts(n1_keep[rows, :] + branch + vec_ref[base : base + 1, :])
        x2_ref[rows, :] = unit
        inv2_ref[rows, :] = inverse
        out_ref[rows, :] = (unit * vec_ref[base + 1 : base + 2, :] + vec_ref[base + 2 : base + 3, :]).astype(out_ref.dtype)
        return carry

    lax.fori_loop(0, 2, token_step, 0)


def forward_layer(hidden, seg_column, seg_row, vectors, weights, out_dtype):
    tokens, width = hidden.shape
    blocks = weights.shape[0]
    wide = width * (blocks - 4) // 2
    rows = tokens // L
    heads = width // HD
    shape = jax.ShapeDtypeStruct

    def row_block(columns):
        return pl.BlockSpec((L, columns), lambda r: (r, 0))

    out_shape = (
        shape((tokens, width), low), shape((tokens, width), low), shape((tokens, width), low),
        shape((width, tokens), low), shape((rows, heads, L), full),
        shape((tokens, width), full), shape((tokens, 1), full), shape((tokens, width), low),
        shape((tokens, wide), low), shape((tokens, wide), low),
        shape((tokens, width), full), shape((tokens, 1), full), shape((tokens, width), out_dtype),
    )
    out_specs = (
        row_block(width), row_block(width), row_block(width),
        pl.BlockSpec((width, L), lambda r: (0, r)), pl.BlockSpec((1, heads, L), lambda r: (r, 0, 0)),
        row_block(width), row_block(1), row_block(width),
        row_block(wide), row_block(wide),
        row_block(width), row_block(1), row_block(width),
    )
    return pl.pallas_call(
        forward_kernel,
        grid=(rows,),
        out_shape=out_shape,
        in_specs=[
            row_block(width),
            pl.BlockSpec((1, L, 1), lambda r: (r, 0, 0)),
            pl.BlockSpec((1, 1, L), lambda r: (r, 0, 0)),
            pl.BlockSpec(vectors.shape, lambda r: (0, 0)),
            pl.BlockSpec(memory_space=pl.ANY),
        ],
        out_specs=out_specs,
        scratch_shapes=[
            pltpu.VMEM((blocks, width, width), low),
            pltpu.VMEM((L, L), full),
            pltpu.VMEM((width, L), low),
            pltpu.VMEM((L, width), full),
            pltpu.SemaphoreType.DMA((blocks,)),
        ],
        compiler_params=pltpu.CompilerParams(
            dimension_semantics=("arbitrary",), vmem_limit_bytes=60 * MIB
        ),
        cost_estimate=pl.CostEstimate(
            flops=2 * tokens * width * width * blocks + 4 * tokens * L * width,
            bytes_accessed=40 * MIB,
            transcendentals=tokens * (L * heads + wide),
        ),
        name="layer_forward",
    )(hidden, seg_column, seg_row, vectors, weights)


def wide_back_kernel(
    up_ref, x2_ref, inv2_ref, x1_ref, inv1_ref, n1_ref, vec_ref, wup_ref, wdown_ref, u_ref, gp_ref,
    dwup_ref, dwdown_ref, dr1_ref, da_ref, dvec_ref,
    dy, dn1, n1t, dz,
):
    c = pl.program_id(0)
    steps = pl.num_programs(0)
    tokens, width = dn1.shape
    inner = vec_ref.shape[0] - 8
    tile = tokens // 4
    pick = [slice(i * tile, (i + 1) * tile) for i in range(4)]
    base = 5 + inner

    @pl.when(c == 0)
    def _():
        gain = vec_ref[base + 1 : base + 2, :]

        def body(i, carry):
            gain_sum, shift_sum, bias_sum = carry
            rows = pl.ds(pl.multiple_of(i * tile, tile), tile)
            upstream = up_ref[rows, :].astype(full)
            unit = x2_ref[rows, :]
            back = norm_back(upstream, unit, inv2_ref[rows, :], gain)
            dn1[rows, :] = back
            branch = back.astype(low)
            dy[rows, :] = branch
            return (
                gain_sum + column_sum(upstream * unit),
                shift_sum + column_sum(upstream),
                bias_sum + column_sum(branch.astype(full)),
            )

        zero = jnp.zeros((1, width), full)
        gain_sum, shift_sum, bias_sum = lax.fori_loop(0, 4, body, (zero, zero, zero))
        dvec_ref[...] = jnp.zeros(dvec_ref.shape, full)
        dvec_ref[base : base + 1, :] = bias_sum
        dvec_ref[base + 1 : base + 2, :] = gain_sum
        dvec_ref[base + 2 : base + 3, :] = shift_sum
        n1t[...] = n1_ref[...].astype(full).T.astype(low)

    def token_step(i, carry):
        rows = pl.ds(pl.multiple_of(i * tile, tile), tile)
        slope = gp_ref[rows, :].astype(full)
        piece = (dot_nt(dy[rows, :], wdown_ref[0]) * slope).astype(low)
        dz[rows, :] = piece
        dn1[rows, :] += dot_nt(piece, wup_ref[0])
        return carry + column_sum(piece.astype(full))

    bias_sum = lax.fori_loop(0, 4, token_step, jnp.zeros((1, width), full))
    for j in range(inner):
        @pl.when(c == j)
        def _():
            dvec_ref[5 + j : 6 + j, :] = bias_sum
    shards = dwup_ref.shape[0]
    part = width // shards
    dwdown = dot_tn(u_ref[...], dy[...]).astype(low)
    dwdown_ref[...] = dwdown.reshape(shards, 1, part, width)
    dwup = dot_nn(n1t[...], dz[...]).astype(low)
    dwup_ref[...] = dwup.reshape(shards, 1, part, width)

    @pl.when(c == steps - 1)
    def _():
        gain = vec_ref[3:4, :]

        def body(i, carry):
            gain_sum, shift_sum, bias_sum = carry
            rows = pl.ds(pl.multiple_of(i * tile, tile), tile)
            upstream = dn1[rows, :]
            unit = x1_ref[rows, :]
            back = norm_back(upstream, unit, inv1_ref[rows, :], gain)
            dr1_ref[rows, :] = back
            branch = back.astype(low)
            da_ref[rows, :] = branch
            return (
                gain_sum + column_sum(upstream * unit),
                shift_sum + column_sum(upstream),
                bias_sum + column_sum(branch.astype(full)),
            )

        zero = jnp.zeros((1, width), full)
        gain_sum, shift_sum, bias_sum = lax.fori_loop(0, 4, body, (zero, zero, zero))
        dvec_ref[2:3, :] = bias_sum
        dvec_ref[3:4, :] = gain_sum
        dvec_ref[4:5, :] = shift_sum


def wide_back(upstream, kept, vectors, weights, shards):
    x1, inv1, n1, u, gp, x2, inv2 = kept
    tokens, width = x1.shape
    inner = (weights.shape[0] - 4) // 2
    part = width // shards
    shape = jax.ShapeDtypeStruct

    def whole(array):
        return pl.BlockSpec(array.shape, lambda c: (0, 0))

    return pl.pallas_call(
        wide_back_kernel,
        grid=(inner,),
        out_shape=(
            shape((shards, inner, part, width), low), shape((shards, inner, part, width), low),
            shape((tokens, width), full), shape((tokens, width), low), shape((16, width), full),
        ),
        in_specs=[
            whole(upstream), whole(x2), whole(inv2), whole(x1), whole(inv1), whole(n1), whole(vectors),
            pl.BlockSpec((1, width, width), lambda c: (4 + c, 0, 0)),
            pl.BlockSpec((1, width, width), lambda c: (4 + inner + c, 0, 0)),
            pl.BlockSpec((tokens, width), lambda c: (0, c)),
            pl.BlockSpec((tokens, width), lambda c: (0, c)),
        ],
        out_specs=(
            pl.BlockSpec((shards, 1, part, width), lambda c: (0, c, 0, 0)),
            pl.BlockSpec((shards, 1, part, width), lambda c: (0, c, 0, 0)),
            pl.BlockSpec((tokens, width), lambda c: (0, 0)),
            pl.BlockSpec((tokens, width), lambda c: (0, 0)),
            pl.BlockSpec((16, width), lambda c: (0, 0)),
        ),
        scratch_shapes=[
            pltpu.VMEM((tokens, width), low),
            pltpu.VMEM((tokens, width), full),
            pltpu.VMEM((width, tokens), low),
            pltpu.VMEM((tokens, width), low),
        ],
        compiler_params=pltpu.CompilerParams(
            dimension_semantics=("arbitrary",), vmem_limit_bytes=60 * MIB
        ),
        cost_estimate=pl.CostEstimate(
            flops=8 * tokens * width * width * inner, bytes_accessed=50 * MIB, transcendentals=0
        ),
        name="wide_backward",
    )(upstream, x2, inv2, x1, inv1, n1, vectors, weights, weights, u, gp)


def attend_back_kernel(
    da_ref, dr1_ref, x_ref, q_ref, k_ref, v_ref, ctxt_ref, lse_ref, segc_ref, segr_ref, w_ref,
    dw_ref, dx_ref, dvec_ref,
    bias, dctx, kt, delta, dqt, xt, ctx_all, da_all, dq_all, dk_all, dv_all,
):
    r = pl.program_id(0)
    tokens, width = da_ref.shape
    here = pl.ds(pl.multiple_of(r * tokens, tokens), tokens)
    xt[:, here] = x_ref[...].astype(low).astype(full).T.astype(low)
    ctx_all[:, here] = ctxt_ref[...]
    da_all[here, :] = da_ref[...]
    bias[...] = segment_bias(segc_ref[0], segr_ref[0])
    context_grad = dot_nt(da_ref[...], w_ref[3]).astype(low)
    dctx[...] = context_grad
    kt[...] = k_ref[...].astype(full).T.astype(low)
    products = context_grad.astype(full) * ctxt_ref[...].astype(full).T
    feature = lax.broadcasted_iota(jnp.int32, (16, width), 1)
    head = lax.broadcasted_iota(jnp.int32, (16, width), 0)
    member = ((feature >= head * HD) & (feature < (head + 1) * HD)).astype(full).astype(low)
    high = products.astype(low)
    rest = (products - high.astype(full)).astype(low)
    delta[...] = dot_nt(member, high) + dot_nt(member, rest)
    masks = half_masks(low)
    scale = HD ** (-0.5)

    def pair_step(p, carry):
        lanes = pl.ds(pl.multiple_of(p * PAIR, PAIR), PAIR)
        q_pair = q_ref[:, lanes] * jnp.asarray(scale, low)
        k_pair = k_ref[:, lanes]
        v_pair = v_ref[:, lanes]
        g_pair = dctx[:, lanes]
        key_grad = jnp.zeros((tokens, PAIR), full)
        value_grad = jnp.zeros((tokens, PAIR), full)
        for h in range(2):
            q_half = q_pair * masks[h]
            g_half = g_pair * masks[h]
            scores = dot_nt(k_pair, q_half) + bias[...]
            attention = jnp.exp(scores - lse_ref[0, pl.ds(2 * p + h, 1), :])
            value_grad = value_grad + dot_nn(attention.astype(low), g_half)
            attention_grad = dot_nt(v_pair, g_half)
            score_grad = (attention * (attention_grad - delta[pl.ds(2 * p + h, 1), :])).astype(low)
            key_grad = key_grad + dot_nn(score_grad, q_half)
            rows = pl.ds(pl.multiple_of(p * PAIR + h * HD, HD), HD)
            dqt[rows, :] = dot_nn(kt[rows, :], score_grad) * scale
        dk_all[here, lanes] = key_grad.astype(low)
        dv_all[here, lanes] = value_grad.astype(low)
        return carry

    lax.fori_loop(0, width // PAIR, pair_step, 0)
    query_grad = dqt[...].T.astype(low)
    dq_all[here, :] = query_grad
    key_grad = dk_all[here, :]
    value_grad = dv_all[here, :]
    dx_ref[...] = (
        dr1_ref[...]
        + dot_nt(query_grad, w_ref[0])
        + dot_nt(key_grad, w_ref[1])
        + dot_nt(value_grad, w_ref[2])
    )

    @pl.when(r == 0)
    def _():
        dvec_ref[...] = jnp.zeros(dvec_ref.shape, full)

    dvec_ref[0:1, :] += column_sum(query_grad.astype(full))
    dvec_ref[1:2, :] += column_sum(value_grad.astype(full))

    @pl.when(r == pl.num_programs(0) - 1)
    def _():
        shards = dw_ref.shape[0]
        part = width // shards
        for j, grad in enumerate((dq_all, dk_all, dv_all)):
            dw_ref[:, j] = dot_nn(xt[...], grad[...]).astype(low).reshape(shards, part, width)
        dw_ref[:, 3] = dot_nn(ctx_all[...], da_all[...]).astype(low).reshape(shards, part, width)


def attend_back(da, dr1, hidden, kept, seg_column, seg_row, weights, shards):
    q, k, v, ctxt, lse = kept
    tokens, width = da.shape
    rows = tokens // L
    heads = width // HD
    part = width // shards
    shape = jax.ShapeDtypeStruct

    def row_block():
        return pl.BlockSpec((L, width), lambda r: (r, 0))

    return pl.pallas_call(
        attend_back_kernel,
        grid=(rows,),
        out_shape=(
            shape((shards, 4, part, width), low), shape((tokens, width), full), shape((8, width), full),
        ),
        in_specs=[
            row_block(), row_block(), row_block(), row_block(), row_block(), row_block(),
            pl.BlockSpec((width, L), lambda r: (0, r)),
            pl.BlockSpec((1, heads, L), lambda r: (r, 0, 0)),
            pl.BlockSpec((1, L, 1), lambda r: (r, 0, 0)),
            pl.BlockSpec((1, 1, L), lambda r: (r, 0, 0)),
            pl.BlockSpec((4, width, width), lambda r: (0, 0, 0)),
        ],
        out_specs=(
            pl.BlockSpec((shards, 4, part, width), lambda r: (0, 0, 0, 0)),
            row_block(),
            pl.BlockSpec((8, width), lambda r: (0, 0)),
        ),
        scratch_shapes=[
            pltpu.VMEM((L, L), full),
            pltpu.VMEM((L, width), low),
            pltpu.VMEM((width, L), low),
            pltpu.VMEM((16, L), full),
            pltpu.VMEM((width, L), full),
            pltpu.VMEM((width, tokens), low),
            pltpu.VMEM((width, tokens), low),
            pltpu.VMEM((tokens, width), low),
            pltpu.VMEM((tokens, width), low),
            pltpu.VMEM((tokens, width), low),
            pltpu.VMEM((tokens, width), low),
        ],
        compiler_params=pltpu.CompilerParams(
            dimension_semantics=("arbitrary",), vmem_limit_bytes=60 * MIB
        ),
        cost_estimate=pl.CostEstimate(
            flops=16 * tokens * width * width + 10 * tokens * L * width,
            bytes_accessed=30 * MIB,
            transcendentals=tokens * L * heads,
        ),
        name="attend_backward",
    )(da, dr1, hidden, q, k, v, ctxt, lse, seg_column, seg_row, weights)


def slot_table(owner, slots, owner_rows):
    block_count = owner.shape[0]
    same_owner = owner[:, None] == owner[None, :]
    ordering = jnp.arange(block_count, dtype=jnp.int32)
    earlier = ordering[None, :] < ordering[:, None]
    ranking = jnp.sum(jnp.where(same_owner & earlier, 1, 0), axis=1).astype(jnp.int32)
    owner_match = owner[None, :] == jnp.arange(owner_rows, dtype=jnp.int32)[:, None]
    slot_match = ranking[None, :] == jnp.arange(slots, dtype=jnp.int32)[:, None]
    return jnp.where(slot_match[:, None, :] & owner_match[None, :, :], 1.0, 0.0).astype(full)


def scatter_sum(grads):
    outer = lax.psum_scatter(grads, "dp", scatter_dimension=0, tiled=False)
    blocks, rows, width = outer.shape
    count = lax.axis_size("fsdp")
    cut = outer.reshape(blocks, count, rows // count, width).transpose(1, 0, 2, 3)
    return lax.psum_scatter(cut, "fsdp", scatter_dimension=0, tiled=False)


def scatter_vectors(grads):
    rows, width = grads.shape
    count = lax.axis_size("dp") * lax.axis_size("fsdp")
    cut = grads.reshape(rows, count, width // count).transpose(1, 0, 2)
    return lax.psum_scatter(cut, ("dp", "fsdp"), scatter_dimension=0, tiled=False)


def shards(
    tokens,
    segment,
    blocks,
    vectors,
    owner,
    left_basis,
    right_basis,
    rot_first,
    rot_second,
    vec_first,
    vec_second,
    cotangent,
):
    layers = vectors.shape[0]
    per_layer = blocks.shape[0] // layers
    width = blocks.shape[2]
    owner_rows = lax.axis_size("dp")
    slots = rot_first.shape[0]
    selector = slot_table(owner, slots, owner_rows)

    vector_parts = lax.all_gather(vectors.astype(low), ("dp", "fsdp"), axis=0, tiled=False)
    vector_full = vector_parts.transpose(1, 2, 0, 3).reshape(layers, vectors.shape[1], width).astype(full)
    blocks_low, vector_full = lax.optimization_barrier((blocks.astype(low), vector_full))

    def fetch(layer_index):
        start = per_layer * layer_index
        return lax.all_gather(blocks_low[start : start + per_layer], ("dp", "fsdp"), axis=1, tiled=True)

    seg_column = segment[:, :, None]
    seg_row = segment[:, None, :]
    state = tokens
    kept = []
    for layer_index in range(layers):
        weights = fetch(layer_index)
        out_dtype = low if layer_index == layers - 1 else full
        results = forward_layer(state, seg_column, seg_row, vector_full[layer_index], weights, out_dtype)
        kept.append((state, weights, results[:5], results[5:12]))
        state = results[12]
    layer_out = state

    right_low = lax.all_gather(right_basis.astype(low), "fsdp", axis=2, tiled=True)
    upstream = cotangent
    block_shards = [None] * layers
    vector_shards = [None] * layers
    for layer_index in reversed(range(layers)):
        hidden, weights, attend_kept, wide_kept = kept[layer_index]
        dwup, dwdown, dr1, da, dvec_wide = wide_back(
            upstream, wide_kept, vector_full[layer_index], weights, owner_rows
        )
        up_shard = scatter_sum(dwup)
        down_shard = scatter_sum(dwdown)
        dwattend, upstream, dvec_attend = attend_back(
            da, dr1, hidden, attend_kept, seg_column, seg_row, weights, owner_rows
        )
        attend_shard = scatter_sum(dwattend)
        count = vectors.shape[1]
        dvec = jnp.concatenate([dvec_attend[:2], dvec_wide[2:count]], axis=0)
        block_shards[layer_index] = jnp.concatenate([attend_shard, up_shard, down_shard], axis=0)
        vector_shards[layer_index] = scatter_vectors(dvec)

    vector_grad = jnp.stack(vector_shards)
    block_grad = jnp.concatenate(block_shards, axis=0)
    outgoing = jnp.einsum("srk,kid->srid", selector.astype(low), block_grad, preferred_element_type=full)
    incoming = lax.all_to_all(outgoing.astype(low), "dp", split_axis=1, concat_axis=1, tiled=True)
    owned = incoming.reshape(slots, -1, width)
    turned = jnp.einsum("sik,skj->sij", owned, right_low, preferred_element_type=full).astype(low)
    left_rows = left_basis.reshape(slots, -1, width).astype(low)
    partial_sums = jnp.einsum("sra,srb->sab", left_rows, turned, preferred_element_type=full)
    rotated = lax.psum_scatter(
        partial_sums.astype(low), "fsdp", scatter_dimension=2, tiled=True
    ).astype(full)
    first_new = beta_one * rot_first + (1.0 - beta_one) * rotated
    second_new = beta_two * rot_second + (1.0 - beta_two) * rotated * rotated
    direction = (
        first_new
        / (1.0 - beta_one**STEP)
        / (jnp.sqrt(second_new / (1.0 - beta_two**STEP)) + adam_epsilon)
    )
    direction_full = lax.all_gather(direction.astype(low), "fsdp", axis=2, tiled=True)
    back_right = jnp.einsum("sab,scb->sac", direction_full, right_low, preferred_element_type=full)
    step_rows = jnp.einsum(
        "sia,sac->sic", left_rows, back_right.astype(low), preferred_element_type=full
    )
    returned = lax.all_to_all(
        step_rows.reshape(slots, owner_rows, -1, width).astype(low),
        "dp",
        split_axis=1,
        concat_axis=1,
        tiled=True,
    )
    step_shard = jnp.einsum("srk,srid->kid", selector.astype(low), returned, preferred_element_type=full)
    new_blocks = blocks - matrix_rate * (step_shard + weight_decay * blocks)
    vector_first = beta_one * vec_first + (1.0 - beta_one) * vector_grad
    vector_second = beta_two * vec_second + (1.0 - beta_two) * vector_grad * vector_grad
    vector_step = (
        vector_first
        / (1.0 - beta_one**STEP)
        / (jnp.sqrt(vector_second / (1.0 - beta_two**STEP)) + adam_epsilon)
    )
    vector_new = vectors - vector_rate * (vector_step + weight_decay * vectors)
    return (
        layer_out,
        upstream,
        new_blocks,
        new_blocks.astype(low),
        first_new,
        second_new,
        vector_first,
        vector_second,
        vector_new,
    )


def solution(mesh):
    return jax.shard_map(
        shards,
        mesh=mesh,
        in_specs=(
            P(("dp", "fsdp"), None),
            P(("dp", "fsdp"), None),
            P(None, ("dp", "fsdp"), None),
            P(None, None, ("dp", "fsdp")),
            P(),
            P("dp", None, "fsdp", None),
            P("dp", None, "fsdp"),
            P("dp", None, "fsdp"),
            P("dp", None, "fsdp"),
            P(None, None, ("dp", "fsdp")),
            P(None, None, ("dp", "fsdp")),
            P(("dp", "fsdp"), None),
        ),
        out_specs=(
            P(("dp", "fsdp"), None),
            P(("dp", "fsdp"), None),
            P(None, ("dp", "fsdp"), None),
            P(None, ("dp", "fsdp"), None),
            P("dp", None, "fsdp"),
            P("dp", None, "fsdp"),
            P(None, None, ("dp", "fsdp")),
            P(None, None, ("dp", "fsdp")),
            P(None, None, ("dp", "fsdp")),
        ),
        check_vma=False,
    )
```

```python
import functools

import jax
import jax.numpy as jnp
from jax import lax
from jax.experimental import pallas as pl
from jax.experimental.pallas import tpu as pltpu
from jax.sharding import PartitionSpec as P

H = 12
HD = 64
L = 512
STEP = 5
PAIR = 2 * HD
MIB = 1 << 20

beta_one = 0.5
beta_two = 0.5
adam_epsilon = 1e-08
norm_epsilon = 1e-06
matrix_rate = 0.03
vector_rate = 0.2
weight_decay = 0.01
masked_score = -1e30
low = jnp.bfloat16
full = jnp.float32


def dot_nn(a, b):
    return lax.dot_general(a, b, (((1,), (0,)), ((), ())), preferred_element_type=full)


def dot_nt(a, b):
    return lax.dot_general(a, b, (((1,), (1,)), ((), ())), preferred_element_type=full)


def dot_tn(a, b):
    return lax.dot_general(a, b, (((0,), (0,)), ((), ())), preferred_element_type=full)


def gelu_parts(z):
    size = jnp.abs(z) * 0.7071067811865476
    t = 1.0 / (1.0 + 0.3275911 * size)
    bell = jnp.exp(-0.5 * z * z)
    poly = ((((1.061405429 * t - 1.453152027) * t + 1.421413741) * t - 0.284496736) * t + 0.254829592) * t
    half_tail = 0.5 * poly * bell
    phi = jnp.where(z >= 0, 1.0 - half_tail, half_tail)
    return z * phi, phi + z * bell * 0.3989422804014327


def norm_parts(residual):
    average = jnp.mean(residual, axis=-1, keepdims=True)
    centered = residual - average
    inverse = lax.rsqrt(jnp.mean(centered * centered, axis=-1, keepdims=True) + norm_epsilon)
    return centered * inverse, inverse


def norm_back(upstream, unit, inverse, gain):
    scaled = upstream * gain
    return inverse * (
        scaled
        - jnp.mean(scaled, axis=-1, keepdims=True)
        - unit * jnp.mean(scaled * unit, axis=-1, keepdims=True)
    )


def column_sum(values):
    return jnp.sum(values, axis=0, keepdims=True)


def half_masks(dtype):
    lane = lax.broadcasted_iota(jnp.int32, (1, PAIR), 1)
    first = (lane < HD).astype(full)
    return first.astype(dtype), (1.0 - first).astype(dtype)


def segment_bias(seg_column, seg_row):
    return jnp.where(seg_column == seg_row, 0.0, masked_score)


def flip(index, bit):
    return index + bit * (1 - 2 * lax.rem(lax.div(index, bit), 2))


def place():
    dp = lax.axis_index("dp")
    return dp, lax.axis_index("fsdp"), lax.rem(dp, 2), lax.div(dp, 2)


def greet(partners):
    barrier = pltpu.get_barrier_semaphore()
    for device in partners:
        pl.semaphore_signal(barrier, inc=1, device_id=device, device_id_type=pl.DeviceIdType.MESH)
    pl.semaphore_wait(barrier, len(partners))


def z_partners(count):
    dp, z, _, _ = place()
    return [(dp, lax.rem(z + d, count)) for d in range(1, count)]


def chip_partners():
    dp, z, core, spot = place()
    return [
        (flip(dp, 1), z),
        (2 * flip(spot, 1) + core, z),
        (2 * flip(spot, 2) + core, z),
    ]


def remote(source, target, send, receive, device):
    return pltpu.make_async_remote_copy(
        src_ref=source,
        dst_ref=target,
        send_sem=send,
        recv_sem=receive,
        device_id=device,
        device_id_type=pl.DeviceIdType.MESH,
    )


def fold(piece):
    half = piece.shape[1] // 2
    return jnp.concatenate([piece[:, :half], piece[:, half:]], axis=0)


def unfold(piece):
    rows = piece.shape[0] // 2
    return jnp.concatenate([piece[:rows], piece[rows:]], axis=1)


def sum_scratch(count, part, width, z_count, kind=low):
    piece = (2 * part // z_count, width // 2) if kind == low else (part // z_count, width)
    return [
        pltpu.VMEM((2, 4, part, width), kind),
        pltpu.VMEM((count, 4, part, width), kind),
        pltpu.VMEM((count, 2, part, width), kind),
        pltpu.VMEM((count, part, width), kind),
        pltpu.VMEM((count, z_count) + piece, kind),
        pltpu.VMEM((count, z_count) + piece, kind),
        pltpu.SemaphoreType.DMA((2,)),
        pltpu.SemaphoreType.DMA((count, 2)),
        pltpu.SemaphoreType.DMA((count, 2, 2)),
        pltpu.SemaphoreType.DMA((count, 2)),
        pltpu.SemaphoreType.DMA((count, 2, z_count)),
    ]


SUM_REFS = 11


class BlockSum:
    def __init__(self, source, refs):
        self.source = source
        (self.own, self.c, self.b, self.a, self.zs, self.zr,
         self.own_sem, self.c_sem, self.b_sem, self.a_sem, self.z_sem) = refs
        self.count = self.c.shape[0]
        self.kind = self.c.dtype
        self.z_count = self.zs.shape[1]

    def load(self, i):
        core = place()[2]
        slot = lax.rem(i, 2)
        return pltpu.make_async_copy(self.source.at[i, :, core], self.own.at[slot], self.own_sem.at[slot])

    def core_copy(self, i):
        dp, z, core, _ = place()
        return remote(
            self.source.at[i, :, 1 - core], self.c.at[i], self.c_sem.at[i, 0], self.c_sem.at[i, 1], (flip(dp, 1), z)
        )

    def second_copy(self, i, k):
        _, z, core, spot = place()
        other = flip(spot, 2 - core)
        chunk = other if k == 0 else flip(other, 1 + core)
        return remote(
            self.c.at[i, chunk], self.b.at[i, k], self.b_sem.at[i, 0, k], self.b_sem.at[i, 1, k], (2 * other + core, z)
        )

    def third_copy(self, i):
        _, z, core, spot = place()
        other = flip(spot, 1 + core)
        return remote(self.c.at[i, other], self.a.at[i], self.a_sem.at[i, 0], self.a_sem.at[i, 1], (2 * other + core, z))

    def z_copy(self, i, d):
        dp, z, _, _ = place()
        other = lax.rem(z + d, self.z_count)
        return remote(
            self.zs.at[i, other], self.zr.at[i, z], self.z_sem.at[i, 0, d], self.z_sem.at[i, 1, self.z_count - d], (dp, other)
        )

    def open(self, i):
        self.core_copy(i).start()
        self.load(i).start()

    def after_core(self, i):
        self.core_copy(i).wait()
        self.load(i).wait()
        slot = lax.rem(i, 2)
        for k in range(4):
            self.c[i, k] = (self.c[i, k].astype(full) + self.own[slot, k].astype(full)).astype(self.kind)
        self.second_copy(i, 0).start()
        self.second_copy(i, 1).start()

    def after_second(self, i):
        _, _, core, spot = place()
        other = flip(spot, 1 + core)
        self.second_copy(i, 1).wait()
        self.c[i, other] = (self.c[i, other].astype(full) + self.b[i, 1].astype(full)).astype(self.kind)
        self.third_copy(i).start()
        self.second_copy(i, 0).wait()
        self.c[i, spot] = (self.c[i, spot].astype(full) + self.b[i, 0].astype(full)).astype(self.kind)

    def after_third(self, i):
        _, _, _, spot = place()
        self.third_copy(i).wait()
        total = self.c[i, spot].astype(full) + self.a[i].astype(full)
        rows = total.shape[0] // self.z_count
        for k in range(self.z_count):
            piece = total[k * rows : (k + 1) * rows]
            self.zs[i, k] = fold(piece).astype(low) if self.kind == low else piece
        for d in range(1, self.z_count):
            self.z_copy(i, d).start()

    def finish(self, i):
        z = lax.axis_index("fsdp")
        for d in range(1, self.z_count):
            self.z_copy(i, d).wait()
        total = self.zs[i, z].astype(full)
        for d in range(1, self.z_count):
            total = total + self.zr[i, lax.rem(z + d, self.z_count)].astype(full)
        return total

    def tick(self, t):
        for late, stage in enumerate((self.open, self.after_core, self.after_second, self.after_third)):
            @pl.when((t >= late) & (t < self.count + late))
            def _():
                stage(t - late)


class BasisGather:
    def __init__(self, sources, targets, local_sem, sems):
        self.sources, self.targets, self.local_sem, self.sems = sources, targets, local_sem, sems
        self.z_count = sems.shape[2]

    def copies(self):
        dp, z, _, _ = place()
        result = []
        for n, (source, target) in enumerate(zip(self.sources, self.targets)):
            result.append(pltpu.make_async_copy(source, target.at[z], self.local_sem.at[n]))
            for d in range(1, self.z_count):
                other = lax.rem(z + d, self.z_count)
                result.append(
                    remote(
                        source, target.at[z], self.sems.at[n, 0, d], self.sems.at[n, 1, self.z_count - d], (dp, other)
                    )
                )
        return result

    def start(self):
        for copy in self.copies():
            copy.start()

    def wait(self):
        for copy in self.copies():
            copy.wait()


def basis_scratch(count, z_count):
    return [pltpu.SemaphoreType.DMA((count,)), pltpu.SemaphoreType.DMA((count, 2, z_count))]


def forward_kernel(
    x_ref, segc_ref, segr_ref, vec_ref, w_hbm,
    q_ref, k_ref, v_ref, ctxt_ref, lse_ref, x1_ref, inv1_ref, n1_ref, u_ref, gp_ref, x2_ref, inv2_ref, out_ref,
    w, bias, vt, n1_keep, w_sem,
):
    first = pl.program_id(0) == 0
    blocks = w.shape[0]
    width = x_ref.shape[1]
    tokens = x_ref.shape[0]

    def arrive(j):
        @pl.when(first)
        def _():
            pltpu.make_async_copy(w_hbm.at[j], w.at[j], w_sem.at[j]).wait()

    @pl.when(first)
    def _():
        for j in range(blocks):
            pltpu.make_async_copy(w_hbm.at[j], w.at[j], w_sem.at[j]).start()

    xin = x_ref[...].astype(low)
    bias[...] = segment_bias(segc_ref[0], segr_ref[0])
    arrive(0)
    q_ref[...] = (dot_nn(xin, w[0]) + vec_ref[0:1, :]).astype(low)
    arrive(1)
    k_ref[...] = dot_nn(xin, w[1]).astype(low)
    arrive(2)
    value = dot_nn(xin, w[2]) + vec_ref[1:2, :]
    v_ref[...] = value.astype(low)
    vt[...] = value.T.astype(low)
    masks = half_masks(low)

    def pair_step(p, carry):
        lanes = pl.ds(pl.multiple_of(p * PAIR, PAIR), PAIR)
        q_pair = q_ref[:, lanes] * jnp.asarray(HD ** (-0.5), low)
        k_pair = k_ref[:, lanes]
        for h in range(2):
            scores = dot_nt(k_pair, q_pair * masks[h]) + bias[...]
            largest = jnp.max(scores, axis=0, keepdims=True)
            expanded = jnp.exp(scores - largest)
            total = column_sum(expanded)
            rows = pl.ds(pl.multiple_of(p * PAIR + h * HD, HD), HD)
            context = dot_nn(vt[rows, :], expanded.astype(low)) * (1.0 / total)
            ctxt_ref[rows, :] = context.astype(low)
            lse_ref[0, pl.ds(2 * p + h, 1), :] = largest + jnp.log(total)
        return carry

    lax.fori_loop(0, width // PAIR, pair_step, 0)
    arrive(3)
    context = ctxt_ref[...].astype(full).T.astype(low)
    attended = dot_nn(context, w[3]) + vec_ref[2:3, :]
    unit, inverse = norm_parts(x_ref[...].astype(full) + attended)
    x1_ref[...] = unit
    inv1_ref[...] = inverse
    normed = unit * vec_ref[3:4, :] + vec_ref[4:5, :]
    n1_keep[...] = normed
    n1_ref[...] = normed.astype(low)
    for j in range(4, blocks):
        arrive(j)
    tile = tokens // 2
    inner = (blocks - 4) // 2

    def token_step(i, carry):
        rows = pl.ds(pl.multiple_of(i * tile, tile), tile)
        n1_low = n1_ref[rows, :]
        branch = jnp.zeros((tile, width), full)
        for c in range(inner):
            columns = slice(c * width, (c + 1) * width)
            value, slope = gelu_parts(dot_nn(n1_low, w[4 + c]) + vec_ref[5 + c : 6 + c, :])
            active = value.astype(low)
            u_ref[rows, columns] = active
            gp_ref[rows, columns] = slope.astype(low)
            branch = branch + dot_nn(active, w[4 + inner + c])
        base = 5 + inner
        unit, inverse = norm_parts(n1_keep[rows, :] + branch + vec_ref[base : base + 1, :])
        x2_ref[rows, :] = unit
        inv2_ref[rows, :] = inverse
        out_ref[rows, :] = (unit * vec_ref[base + 1 : base + 2, :] + vec_ref[base + 2 : base + 3, :]).astype(out_ref.dtype)
        return carry

    lax.fori_loop(0, 2, token_step, 0)


def forward_layer(hidden, seg_column, seg_row, vectors, weights, out_dtype):
    tokens, width = hidden.shape
    blocks = weights.shape[0]
    wide = width * (blocks - 4) // 2
    rows = tokens // L
    heads = width // HD
    shape = jax.ShapeDtypeStruct

    def row_block(columns):
        return pl.BlockSpec((L, columns), lambda r: (r, 0))

    out_shape = (
        shape((tokens, width), low), shape((tokens, width), low), shape((tokens, width), low),
        shape((width, tokens), low), shape((rows, heads, L), full),
        shape((tokens, width), full), shape((tokens, 1), full), shape((tokens, width), low),
        shape((tokens, wide), low), shape((tokens, wide), low),
        shape((tokens, width), full), shape((tokens, 1), full), shape((tokens, width), out_dtype),
    )
    out_specs = (
        row_block(width), row_block(width), row_block(width),
        pl.BlockSpec((width, L), lambda r: (0, r)), pl.BlockSpec((1, heads, L), lambda r: (r, 0, 0)),
        row_block(width), row_block(1), row_block(width),
        row_block(wide), row_block(wide),
        row_block(width), row_block(1), row_block(width),
    )
    return pl.pallas_call(
        forward_kernel,
        grid=(rows,),
        out_shape=out_shape,
        in_specs=[
            row_block(width),
            pl.BlockSpec((1, L, 1), lambda r: (r, 0, 0)),
            pl.BlockSpec((1, 1, L), lambda r: (r, 0, 0)),
            pl.BlockSpec(vectors.shape, lambda r: (0, 0)),
            pl.BlockSpec(memory_space=pl.ANY),
        ],
        out_specs=out_specs,
        scratch_shapes=[
            pltpu.VMEM((blocks, width, width), low),
            pltpu.VMEM((L, L), full),
            pltpu.VMEM((width, L), low),
            pltpu.VMEM((L, width), full),
            pltpu.SemaphoreType.DMA((blocks,)),
        ],
        compiler_params=pltpu.CompilerParams(
            dimension_semantics=("arbitrary",), vmem_limit_bytes=60 * MIB
        ),
        cost_estimate=pl.CostEstimate(
            flops=2 * tokens * width * width * blocks + 4 * tokens * L * width,
            bytes_accessed=40 * MIB,
            transcendentals=tokens * (L * heads + wide),
        ),
        name="layer_forward",
    )(hidden, seg_column, seg_row, vectors, weights)


def split_refs(refs, *counts):
    result, start = [], 0
    for count in counts:
        result.append(refs[start : start + count])
        start += count
    return result


def wide_back_kernel(sums, bases, *refs):
    inputs, sources, outputs, targets, scratch, sum_refs, basis_refs = split_refs(
        refs, 11, sums + bases, 4, sums + bases, 4, SUM_REFS * sums, 2 * min(bases, 1)
    )
    up_ref, x2_ref, inv2_ref, x1_ref, inv1_ref, n1_ref, vec_ref, wup_ref, wdown_ref, u_ref, gp_ref = inputs
    dw_ref, dr1_ref, da_ref, dvec_ref = outputs
    dy, dn1, n1t, dz = scratch
    c = pl.program_id(0)
    side = Side(sums, bases, sources, targets, sum_refs, basis_refs)
    side.enter(c == 0)
    steps = pl.num_programs(0)
    tokens, width = dn1.shape
    inner = vec_ref.shape[0] - 8
    tile = tokens // 4
    pick = [slice(i * tile, (i + 1) * tile) for i in range(4)]
    base = 5 + inner

    @pl.when(c == 0)
    def _():
        gain = vec_ref[base + 1 : base + 2, :]

        def body(i, carry):
            gain_sum, shift_sum, bias_sum = carry
            rows = pl.ds(pl.multiple_of(i * tile, tile), tile)
            upstream = up_ref[rows, :].astype(full)
            unit = x2_ref[rows, :]
            back = norm_back(upstream, unit, inv2_ref[rows, :], gain)
            dn1[rows, :] = back
            branch = back.astype(low)
            dy[rows, :] = branch
            return (
                gain_sum + column_sum(upstream * unit),
                shift_sum + column_sum(upstream),
                bias_sum + column_sum(branch.astype(full)),
            )

        zero = jnp.zeros((1, width), full)
        gain_sum, shift_sum, bias_sum = lax.fori_loop(0, 4, body, (zero, zero, zero))
        dvec_ref[...] = jnp.zeros(dvec_ref.shape, full)
        dvec_ref[base : base + 1, :] = bias_sum
        dvec_ref[base + 1 : base + 2, :] = gain_sum
        dvec_ref[base + 2 : base + 3, :] = shift_sum
        n1t[...] = n1_ref[...].astype(full).T.astype(low)

    def token_step(i, carry):
        rows = pl.ds(pl.multiple_of(i * tile, tile), tile)
        slope = gp_ref[rows, :].astype(full)
        piece = (dot_nt(dy[rows, :], wdown_ref[0]) * slope).astype(low)
        dz[rows, :] = piece
        dn1[rows, :] += dot_nt(piece, wup_ref[0])
        if sums:
            @pl.when(lax.rem(i, 2) == 0)
            def _():
                side.sum.tick(2 * c + lax.div(i, 2))
        return carry + column_sum(piece.astype(full))

    bias_sum = lax.fori_loop(0, 4, token_step, jnp.zeros((1, width), full))
    for j in range(inner):
        @pl.when(c == j)
        def _():
            dvec_ref[5 + j : 6 + j, :] = bias_sum
    dw_ref[0, 0] = dot_nn(n1t[...], dz[...]).astype(low)
    dw_ref[1, 0] = dot_tn(u_ref[...], dy[...]).astype(low)

    @pl.when(c == steps - 1)
    def _():
        gain = vec_ref[3:4, :]

        def body(i, carry):
            gain_sum, shift_sum, bias_sum = carry
            rows = pl.ds(pl.multiple_of(i * tile, tile), tile)
            upstream = dn1[rows, :]
            unit = x1_ref[rows, :]
            back = norm_back(upstream, unit, inv1_ref[rows, :], gain)
            dr1_ref[rows, :] = back
            branch = back.astype(low)
            da_ref[rows, :] = branch
            return (
                gain_sum + column_sum(upstream * unit),
                shift_sum + column_sum(upstream),
                bias_sum + column_sum(branch.astype(full)),
            )

        zero = jnp.zeros((1, width), full)
        gain_sum, shift_sum, bias_sum = lax.fori_loop(0, 4, body, (zero, zero, zero))
        dvec_ref[2:3, :] = bias_sum
        dvec_ref[3:4, :] = gain_sum
        dvec_ref[4:5, :] = shift_sum

    side.leave(c == steps - 1)


class Side:
    def __init__(self, sums, bases, sources, targets, sum_refs, basis_refs):
        self.sums, self.bases = sums, bases
        self.sum = BlockSum(sources[0], sum_refs) if sums else None
        self.result = targets[0] if sums else None
        self.basis = BasisGather(sources[sums:], targets[sums:], *basis_refs) if bases else None

    def enter(self, now):
        if not (self.sums or self.bases):
            return

        @pl.when(now)
        def _():
            z_count = self.sum.z_count if self.sums else self.basis.z_count
            greet((chip_partners() if self.sums else []) + z_partners(z_count))
            if self.bases:
                self.basis.start()

    def leave(self, now):
        if not (self.sums or self.bases):
            return

        @pl.when(now)
        def _():
            if self.sums:
                for i in range(self.sum.count):
                    self.result[i] = self.sum.finish(i).astype(low)
            if self.bases:
                self.basis.wait()


ANYWHERE = pl.BlockSpec(memory_space=pl.ANY)
IN_VMEM = pl.BlockSpec(memory_space=pltpu.VMEM)


def side_parts(pending, bases, z_count):
    arguments, results, result_specs, scratch = [], [], [], []
    if pending is not None:
        count, part, width = pending.shape[0], pending.shape[3], pending.shape[4]
        arguments.append(pending)
        results.append(jax.ShapeDtypeStruct((count, 2 * part // z_count, width // 2), low))
        result_specs.append(pl.BlockSpec(results[0].shape, lambda i: (0, 0, 0), pipeline_mode=pl.Buffered(1)))
        scratch += sum_scratch(count, part, width, z_count)
    for basis in bases:
        arguments.append(basis)
        results.append(jax.ShapeDtypeStruct((z_count,) + basis.shape, low))
        result_specs.append(ANYWHERE)
    if bases:
        scratch += basis_scratch(len(bases), z_count)
    return arguments, [ANYWHERE] * len(arguments), results, result_specs, scratch


def wide_back(upstream, kept, vectors, weights, pending=None, bases=(), z_count=1, identity=None):
    x1, inv1, n1, u, gp, x2, inv2 = kept
    tokens, width = x1.shape
    inner = (weights.shape[0] - 4) // 2
    shape = jax.ShapeDtypeStruct
    arguments, argument_specs, results, result_specs, scratch = side_parts(pending, bases, z_count)

    def whole(array):
        return pl.BlockSpec(array.shape, lambda c: (0, 0), pipeline_mode=pl.Buffered(1))

    return pl.pallas_call(
        functools.partial(wide_back_kernel, int(pending is not None), len(bases)),
        grid=(inner,),
        out_shape=(
            shape((2, inner, width, width), low),
            shape((tokens, width), full), shape((tokens, width), low), shape((16, width), full),
            *results,
        ),
        in_specs=[
            whole(upstream), whole(x2), whole(inv2), whole(x1), whole(inv1), whole(n1), whole(vectors),
            pl.BlockSpec((1, width, width), lambda c: (4 + c, 0, 0)),
            pl.BlockSpec((1, width, width), lambda c: (4 + inner + c, 0, 0)),
            pl.BlockSpec((tokens, width), lambda c: (0, c)),
            pl.BlockSpec((tokens, width), lambda c: (0, c)),
            *argument_specs,
        ],
        out_specs=(
            pl.BlockSpec((2, 1, width, width), lambda c: (0, c, 0, 0)),
            pl.BlockSpec((tokens, width), lambda c: (0, 0), pipeline_mode=pl.Buffered(1)),
            pl.BlockSpec((tokens, width), lambda c: (0, 0), pipeline_mode=pl.Buffered(1)),
            pl.BlockSpec((16, width), lambda c: (0, 0)),
            *result_specs,
        ),
        scratch_shapes=[
            pltpu.VMEM((tokens, width), low),
            pltpu.VMEM((tokens, width), full),
            pltpu.VMEM((width, tokens), low),
            pltpu.VMEM((tokens, width), low),
            *scratch,
        ],
        compiler_params=pltpu.CompilerParams(
            dimension_semantics=("arbitrary",), vmem_limit_bytes=60 * MIB,
            collective_id=identity, has_side_effects=identity is not None,
        ),
        cost_estimate=pl.CostEstimate(
            flops=8 * tokens * width * width * inner, bytes_accessed=50 * MIB, transcendentals=0
        ),
        name="wide_backward",
    )(upstream, x2, inv2, x1, inv1, n1, vectors, weights, weights, u, gp, *arguments)


def attend_back_kernel(sums, bases, *refs):
    inputs, sources, outputs, targets, scratch, sum_refs, basis_refs = split_refs(
        refs, 11, sums + bases, 3, sums + bases, 11, SUM_REFS * sums, 2 * min(bases, 1)
    )
    da_ref, dr1_ref, x_ref, q_ref, k_ref, v_ref, ctxt_ref, lse_ref, segc_ref, segr_ref, w_ref = inputs
    dw_ref, dx_ref, dvec_ref = outputs
    bias, dctx, kt, delta, dqt, xt, ctx_all, da_all, dq_all, dk_all, dv_all = scratch
    r = pl.program_id(0)
    side = Side(sums, bases, sources, targets, sum_refs, basis_refs)
    side.enter(r == 0)
    tokens, width = da_ref.shape
    here = pl.ds(pl.multiple_of(r * tokens, tokens), tokens)
    xt[:, here] = x_ref[...].astype(low).astype(full).T.astype(low)
    ctx_all[:, here] = ctxt_ref[...]
    da_all[here, :] = da_ref[...]
    bias[...] = segment_bias(segc_ref[0], segr_ref[0])
    context_grad = dot_nt(da_ref[...], w_ref[3]).astype(low)
    dctx[...] = context_grad
    kt[...] = k_ref[...].astype(full).T.astype(low)
    products = context_grad.astype(full) * ctxt_ref[...].astype(full).T
    feature = lax.broadcasted_iota(jnp.int32, (16, width), 1)
    head = lax.broadcasted_iota(jnp.int32, (16, width), 0)
    member = ((feature >= head * HD) & (feature < (head + 1) * HD)).astype(full).astype(low)
    high = products.astype(low)
    rest = (products - high.astype(full)).astype(low)
    delta[...] = dot_nt(member, high) + dot_nt(member, rest)
    masks = half_masks(low)
    scale = HD ** (-0.5)

    def pair_step(p, carry):
        lanes = pl.ds(pl.multiple_of(p * PAIR, PAIR), PAIR)
        q_pair = q_ref[:, lanes] * jnp.asarray(scale, low)
        k_pair = k_ref[:, lanes]
        v_pair = v_ref[:, lanes]
        g_pair = dctx[:, lanes]
        key_grad = jnp.zeros((tokens, PAIR), full)
        value_grad = jnp.zeros((tokens, PAIR), full)
        for h in range(2):
            q_half = q_pair * masks[h]
            g_half = g_pair * masks[h]
            scores = dot_nt(k_pair, q_half) + bias[...]
            attention = jnp.exp(scores - lse_ref[0, pl.ds(2 * p + h, 1), :])
            value_grad = value_grad + dot_nn(attention.astype(low), g_half)
            attention_grad = dot_nt(v_pair, g_half)
            score_grad = (attention * (attention_grad - delta[pl.ds(2 * p + h, 1), :])).astype(low)
            key_grad = key_grad + dot_nn(score_grad, q_half)
            rows = pl.ds(pl.multiple_of(p * PAIR + h * HD, HD), HD)
            dqt[rows, :] = dot_nn(kt[rows, :], score_grad) * scale
        dk_all[here, lanes] = key_grad.astype(low)
        dv_all[here, lanes] = value_grad.astype(low)
        if sums:
            side.sum.tick(r * (width // PAIR) + p)
        return carry

    lax.fori_loop(0, width // PAIR, pair_step, 0)
    query_grad = dqt[...].T.astype(low)
    dq_all[here, :] = query_grad
    key_grad = dk_all[here, :]
    value_grad = dv_all[here, :]
    dx_ref[...] = (
        dr1_ref[...]
        + dot_nt(query_grad, w_ref[0])
        + dot_nt(key_grad, w_ref[1])
        + dot_nt(value_grad, w_ref[2])
    )

    @pl.when(r == 0)
    def _():
        dvec_ref[...] = jnp.zeros(dvec_ref.shape, full)

    dvec_ref[0:1, :] += column_sum(query_grad.astype(full))
    dvec_ref[1:2, :] += column_sum(value_grad.astype(full))

    @pl.when(r == pl.num_programs(0) - 1)
    def _():
        for j, grad in enumerate((dq_all, dk_all, dv_all)):
            dw_ref[j] = dot_nn(xt[...], grad[...]).astype(low)
        dw_ref[3] = dot_nn(ctx_all[...], da_all[...]).astype(low)

    side.leave(r == pl.num_programs(0) - 1)


def attend_back(
    da, dr1, hidden, kept, seg_column, seg_row, weights, pending=None, bases=(), z_count=1, identity=None
):
    q, k, v, ctxt, lse = kept
    tokens, width = da.shape
    rows = tokens // L
    heads = width // HD
    shape = jax.ShapeDtypeStruct
    arguments, argument_specs, results, result_specs, scratch = side_parts(pending, bases, z_count)

    def row_block():
        return pl.BlockSpec((L, width), lambda r: (r, 0))

    return pl.pallas_call(
        functools.partial(attend_back_kernel, int(pending is not None), len(bases)),
        grid=(rows,),
        out_shape=(
            shape((4, width, width), low), shape((tokens, width), full), shape((8, width), full), *results,
        ),
        in_specs=[
            row_block(), row_block(), row_block(), row_block(), row_block(), row_block(),
            pl.BlockSpec((width, L), lambda r: (0, r)),
            pl.BlockSpec((1, heads, L), lambda r: (r, 0, 0)),
            pl.BlockSpec((1, L, 1), lambda r: (r, 0, 0)),
            pl.BlockSpec((1, 1, L), lambda r: (r, 0, 0)),
            pl.BlockSpec((4, width, width), lambda r: (0, 0, 0), pipeline_mode=pl.Buffered(1)),
            *argument_specs,
        ],
        out_specs=(
            pl.BlockSpec((4, width, width), lambda r: (0, 0, 0), pipeline_mode=pl.Buffered(1)),
            row_block(),
            pl.BlockSpec((8, width), lambda r: (0, 0)),
            *result_specs,
        ),
        scratch_shapes=[
            pltpu.VMEM((L, L), full),
            pltpu.VMEM((L, width), low),
            pltpu.VMEM((width, L), low),
            pltpu.VMEM((16, L), full),
            pltpu.VMEM((width, L), full),
            pltpu.VMEM((width, tokens), low),
            pltpu.VMEM((width, tokens), low),
            pltpu.VMEM((tokens, width), low),
            pltpu.VMEM((tokens, width), low),
            pltpu.VMEM((tokens, width), low),
            pltpu.VMEM((tokens, width), low),
            *scratch,
        ],
        compiler_params=pltpu.CompilerParams(
            dimension_semantics=("arbitrary",), vmem_limit_bytes=60 * MIB,
            collective_id=identity, has_side_effects=identity is not None,
        ),
        cost_estimate=pl.CostEstimate(
            flops=16 * tokens * width * width + 10 * tokens * L * width,
            bytes_accessed=30 * MIB,
            transcendentals=tokens * L * heads,
        ),
        name="attend_backward",
    )(da, dr1, hidden, q, k, v, ctxt, lse, seg_column, seg_row, weights, *arguments)


def moments(rotated, first, second):
    first_new = beta_one * first + (1.0 - beta_one) * rotated
    second_new = beta_two * second + (1.0 - beta_two) * rotated * rotated
    direction = (
        first_new
        / (1.0 - beta_one**STEP)
        / (jnp.sqrt(second_new / (1.0 - beta_two**STEP)) + adam_epsilon)
    )
    return first_new, second_new, direction


def optimizer_kernel(*refs):
    inputs, outputs, scratch, sum_refs, vec_refs = split_refs(refs, 10, 5, 20, SUM_REFS, SUM_REFS)
    index_ref, place_ref, tail_hbm, vec_hbm, ready, left_hbm, right_hbm, first_hbm, second_hbm, blocks = inputs
    new_ref, low_ref, first_out, second_out, vec_out = outputs
    (store, left, right, first_in, second_in, g_out, g_in, t_out, t_in, e_out, e_in, w_out, w_in,
     load_sem, g_sem, t_sem, e_sem, w_sem, load_sem_left, load_sem_right) = scratch
    dp, z, core, spot = place()
    slots, owners = g_in.shape[0], g_in.shape[1]
    z_count = t_in.shape[1]
    count = blocks.shape[0]
    tail = BlockSum(tail_hbm, sum_refs)
    vec = BlockSum(vec_hbm, vec_refs)
    greet([(lax.rem(dp + d, owners), z) for d in range(1, owners)] + z_partners(z_count))
    loads = []
    for s in range(slots):
        loads.append(
            [
                pltpu.make_async_copy(right_hbm.at[:, s], right.at[:, s], load_sem_right.at[s]),
                pltpu.make_async_copy(left_hbm.at[:, s], left.at[:, s], load_sem_left.at[s]),
                pltpu.make_async_copy(first_hbm.at[s], first_in.at[s], load_sem.at[0, s]),
                pltpu.make_async_copy(second_hbm.at[s], second_in.at[s], load_sem.at[1, s]),
            ]
        )

    def sum_step(t, carry):
        tail.tick(t)
        vec.tick(t)
        return carry

    lax.fori_loop(0, tail.count + 3, sum_step, 0)
    for slot_loads in loads:
        for copy in slot_loads:
            copy.start()
    store[tail.count : count] = ready[...]
    store[count] = jnp.zeros(store.shape[1:], low)
    for i in range(tail.count):
        store[i] = tail.finish(i).astype(low)

    def g_copy(s, d):
        other = lax.rem(dp + d, owners)
        return remote(g_out.at[s, d], g_in.at[s, dp], g_sem.at[0, s, d], g_sem.at[1, s, owners - d], (other, z))

    def t_copy(s, d):
        other = lax.rem(z + d, z_count)
        return remote(t_out.at[s, d], t_in.at[s, z], t_sem.at[0, s, d], t_sem.at[1, s, z_count - d], (dp, other))

    def e_copy(s, d):
        other = lax.rem(z + d, z_count)
        return remote(e_out.at[s, d], e_in.at[s, z], e_sem.at[0, s, d], e_sem.at[1, s, z_count - d], (dp, other))

    def w_copy(s, d):
        other = lax.rem(dp + d, owners)
        return remote(
            w_out.at[s, other], w_in.at[s * owners + dp], w_sem.at[0, s, d], w_sem.at[1, s, owners - d], (other, z)
        )

    for s in range(slots):
        for d in range(1, owners):
            g_out[s, d] = store[index_ref[s * owners + lax.rem(dp + d, owners)]]
            g_copy(s, d).start()
        g_in[s, dp] = store[index_ref[s * owners + dp]]

    for s in range(slots):
        for d in range(1, owners):
            g_copy(s, d).wait()
        loads[s][0].wait()
        grad = jnp.concatenate([unfold(g_in[s, c].astype(full)) for c in range(owners)], axis=0).astype(low)
        for d in range(1, z_count):
            t_out[s, d] = dot_nt(grad, right[lax.rem(z + d, z_count), s]).astype(low)
            t_copy(s, d).start()
        t_in[s, z] = dot_nt(grad, right[z, s]).astype(low)

    for s in range(slots):
        for d in range(1, z_count):
            t_copy(s, d).wait()
        for copy in loads[s][1:]:
            copy.wait()
        rotated = dot_tn(left[0, s], t_in[s, 0])
        for f in range(1, z_count):
            rotated = rotated + dot_tn(left[f, s], t_in[s, f])
        first_new, second_new, direction = moments(rotated, first_in[s], second_in[s])
        first_out[s] = first_new
        second_out[s] = second_new
        direction = direction.astype(low)
        for d in range(1, z_count):
            e_out[s, d] = dot_nn(left[lax.rem(z + d, z_count), s], direction).astype(low)
            e_copy(s, d).start()
        e_in[s, z] = dot_nn(left[z, s], direction).astype(low)

    rows = left.shape[2] // owners
    for s in range(slots):
        for d in range(1, z_count):
            e_copy(s, d).wait()
        step = dot_nn(e_in[s, 0], right[0, s])
        for f in range(1, z_count):
            step = step + dot_nn(e_in[s, f], right[f, s])
        for c in range(owners):
            w_out[s, c] = fold(step[c * rows : (c + 1) * rows]).astype(low)
        for d in range(1, owners):
            w_copy(s, d).start()
        w_in[s * owners + dp] = w_out[s, dp]

    vec_out[...] = vec.finish(0)
    for s in range(slots):
        for d in range(1, owners):
            w_copy(s, d).wait()

    def block_step(b, carry):
        step = unfold(w_in[place_ref[b]].astype(full))
        block = blocks[b]
        new = block - matrix_rate * (step + weight_decay * block)
        new_ref[b] = new
        low_ref[b] = new.astype(low)
        return carry

    lax.fori_loop(0, count, block_step, 0)


def optimizer(index, places, tail, vec, ready, left, right, first, second, blocks, z_count, identity):
    slots, width, columns = first.shape
    owners = index.shape[0] // slots
    count, rows = blocks.shape[0], blocks.shape[1]
    span = left.shape[2]
    shape = jax.ShapeDtypeStruct
    piece = (2 * rows, width // 2)
    smem = pl.BlockSpec(memory_space=pltpu.SMEM)
    return pl.pallas_call(
        optimizer_kernel,
        out_shape=(
            shape(blocks.shape, full), shape(blocks.shape, low), shape(first.shape, full), shape(first.shape, full),
            shape((rows, vec.shape[-1]), full),
        ),
        in_specs=[smem, smem, ANYWHERE, ANYWHERE, IN_VMEM, ANYWHERE, ANYWHERE, ANYWHERE, ANYWHERE, IN_VMEM],
        out_specs=(IN_VMEM,) * 5,
        scratch_shapes=[
            pltpu.VMEM((count + 1,) + piece, low),
            pltpu.VMEM((z_count, slots, span, width), low),
            pltpu.VMEM((z_count, slots, columns, width), low),
            pltpu.VMEM((slots, width, columns), full),
            pltpu.VMEM((slots, width, columns), full),
            pltpu.VMEM((slots, owners) + piece, low),
            pltpu.VMEM((slots, owners) + piece, low),
            pltpu.VMEM((slots, z_count, span, columns), low),
            pltpu.VMEM((slots, z_count, span, columns), low),
            pltpu.VMEM((slots, z_count, span, columns), low),
            pltpu.VMEM((slots, z_count, span, columns), low),
            pltpu.VMEM((slots, owners) + piece, low),
            pltpu.VMEM((slots * owners,) + piece, low),
            pltpu.SemaphoreType.DMA((2, slots)),
            pltpu.SemaphoreType.DMA((2, slots, owners)),
            pltpu.SemaphoreType.DMA((2, slots, z_count)),
            pltpu.SemaphoreType.DMA((2, slots, z_count)),
            pltpu.SemaphoreType.DMA((2, slots, owners)),
            pltpu.SemaphoreType.DMA((slots,)),
            pltpu.SemaphoreType.DMA((slots,)),
            *sum_scratch(tail.shape[0], tail.shape[3], width, z_count),
            *sum_scratch(1, vec.shape[3], vec.shape[4], z_count, full),
        ],
        compiler_params=pltpu.CompilerParams(
            vmem_limit_bytes=60 * MIB, collective_id=identity, has_side_effects=True
        ),
        cost_estimate=pl.CostEstimate(
            flops=8 * slots * span * width * width, bytes_accessed=40 * MIB, transcendentals=slots * width * columns
        ),
        name="optimizer",
    )(index, places, tail, vec, ready, left, right, first, second, blocks)


def slot_table(owner, slots, owner_rows):
    block_count = owner.shape[0]
    same_owner = owner[:, None] == owner[None, :]
    ordering = jnp.arange(block_count, dtype=jnp.int32)
    earlier = ordering[None, :] < ordering[:, None]
    ranking = jnp.sum(jnp.where(same_owner & earlier, 1, 0), axis=1).astype(jnp.int32)
    owner_match = owner[None, :] == jnp.arange(owner_rows, dtype=jnp.int32)[:, None]
    slot_match = ranking[None, :] == jnp.arange(slots, dtype=jnp.int32)[:, None]
    return jnp.where(slot_match[:, None, :] & owner_match[None, :, :], 1.0, 0.0).astype(full)


def scatter_sum(grads):
    blocks, width = grads.shape[0], grads.shape[2]
    cut = grads.reshape(blocks, lax.axis_size("dp"), -1, width).transpose(1, 0, 2, 3)
    outer = lax.psum_scatter(cut, "dp", scatter_dimension=0, tiled=False)
    blocks, rows, width = outer.shape
    count = lax.axis_size("fsdp")
    cut = outer.reshape(blocks, count, rows // count, width).transpose(1, 0, 2, 3)
    return lax.psum_scatter(cut, "fsdp", scatter_dimension=0, tiled=False)


def scatter_vectors(grads):
    rows, width = grads.shape
    count = lax.axis_size("dp") * lax.axis_size("fsdp")
    cut = grads.reshape(rows, count, width // count).transpose(1, 0, 2)
    return lax.psum_scatter(cut, ("dp", "fsdp"), scatter_dimension=0, tiled=False)


def reduce_and_step(
    upstream, kept, vector_full, seg_column, seg_row, owner, selector, left_basis, right_basis,
    rot_first, rot_second, blocks, vector_rows, z_count,
):
    slots, owners, count = selector.shape
    width = blocks.shape[2]
    part = width // owners
    left_low = left_basis.reshape(slots, -1, width).astype(low)
    right_low = right_basis.transpose(0, 2, 1).astype(low)

    def cut(grads):
        return grads.reshape(-1, owners // 2, 2, part, width)

    def wide(layer, upstream, pending, bases, identity):
        _, weights, _, wide_kept = kept[layer]
        return wide_back(upstream, wide_kept, vector_full[layer], weights, pending, bases, z_count, identity)

    def attend(layer, da, dr1, pending, bases, identity):
        hidden, weights, attend_kept, _ = kept[layer]
        return attend_back(
            da, dr1, hidden, attend_kept, seg_column, seg_row, weights, pending, bases, z_count, identity
        )

    dw_wide, dr1, da, dvec_wide_b, right_full = wide(1, upstream, None, (right_low,), 1)
    dw_attend, upstream, dvec_attend_b, wide_sum_b = attend(1, da, dr1, cut(dw_wide), (), 2)
    dw_wide, dr1, da, dvec_wide_a, attend_sum_b, left_full = wide(0, upstream, cut(dw_attend), (left_low,), 3)
    dw_attend, upstream, dvec_attend_a, wide_sum_a = attend(0, da, dr1, cut(dw_wide), (), 5)

    ready = jnp.concatenate([wide_sum_a, attend_sum_b, wide_sum_b], axis=0)
    lanes = 128
    dvec = jnp.concatenate(
        [dvec_attend_a[:2], dvec_wide_a[2:vector_rows], dvec_attend_b[:2], dvec_wide_b[2:vector_rows]], axis=0
    )
    vec = jnp.pad(dvec, ((0, lanes - dvec.shape[0]), (0, 0))).T.reshape(1, owners // 2, 2, part, lanes)
    numbers = jnp.arange(count, dtype=jnp.int32)
    table = selector.reshape(slots * owners, count)
    held = jnp.sum(table, axis=1)
    index = jnp.where(held > 0, jnp.sum(table * numbers, axis=1), count).astype(jnp.int32)
    places = jnp.sum(table * jnp.arange(slots * owners, dtype=jnp.int32)[:, None], axis=0).astype(jnp.int32)
    new_blocks, new_low, first_new, second_new, vec_sum = optimizer(
        index, places, cut(dw_attend), vec, ready, left_full, right_full, rot_first, rot_second, blocks, z_count, 4
    )
    vector_grad = vec_sum[:, : dvec.shape[0]].T.reshape(-1, vector_rows, vec_sum.shape[0])
    return upstream, new_blocks, new_low, first_new, second_new, vector_grad


def plain_reduce_and_step(
    upstream, kept, vector_full, seg_column, seg_row, selector, left_basis, right_basis,
    rot_first, rot_second, blocks, vector_rows, owner_rows,
):
    slots = selector.shape[0]
    width = blocks.shape[2]
    layers = len(kept)
    right_low = lax.all_gather(right_basis.astype(low), "fsdp", axis=2, tiled=True)
    block_shards = [None] * layers
    vector_shards = [None] * layers
    for layer_index in reversed(range(layers)):
        hidden, weights, attend_kept, wide_kept = kept[layer_index]
        dw_wide, dr1, da, dvec_wide = wide_back(upstream, wide_kept, vector_full[layer_index], weights)
        wide_shard = scatter_sum(dw_wide.reshape(-1, width, width))
        dw_attend, upstream, dvec_attend = attend_back(
            da, dr1, hidden, attend_kept, seg_column, seg_row, weights
        )
        dvec = jnp.concatenate([dvec_attend[:2], dvec_wide[2:vector_rows]], axis=0)
        block_shards[layer_index] = jnp.concatenate([scatter_sum(dw_attend), wide_shard], axis=0)
        vector_shards[layer_index] = scatter_vectors(dvec)
    vector_grad = jnp.stack(vector_shards)
    block_grad = jnp.concatenate(block_shards, axis=0)
    outgoing = jnp.einsum("srk,kid->srid", selector.astype(low), block_grad, preferred_element_type=full)
    incoming = lax.all_to_all(outgoing.astype(low), "dp", split_axis=1, concat_axis=1, tiled=True)
    owned = incoming.reshape(slots, -1, width)
    turned = jnp.einsum("sik,skj->sij", owned, right_low, preferred_element_type=full).astype(low)
    left_rows = left_basis.reshape(slots, -1, width).astype(low)
    partial_sums = jnp.einsum("sra,srb->sab", left_rows, turned, preferred_element_type=full)
    rotated = lax.psum_scatter(
        partial_sums.astype(low), "fsdp", scatter_dimension=2, tiled=True
    ).astype(full)
    first_new, second_new, direction = moments(rotated, rot_first, rot_second)
    direction_full = lax.all_gather(direction.astype(low), "fsdp", axis=2, tiled=True)
    back_right = jnp.einsum("sab,scb->sac", direction_full, right_low, preferred_element_type=full)
    step_rows = jnp.einsum(
        "sia,sac->sic", left_rows, back_right.astype(low), preferred_element_type=full
    )
    returned = lax.all_to_all(
        step_rows.reshape(slots, owner_rows, -1, width).astype(low),
        "dp",
        split_axis=1,
        concat_axis=1,
        tiled=True,
    )
    step_shard = jnp.einsum("srk,srid->kid", selector.astype(low), returned, preferred_element_type=full)
    new_blocks = blocks - matrix_rate * (step_shard + weight_decay * blocks)
    return upstream, new_blocks, new_blocks.astype(low), first_new, second_new, vector_grad


def shards(
    tokens,
    segment,
    blocks,
    vectors,
    owner,
    left_basis,
    right_basis,
    rot_first,
    rot_second,
    vec_first,
    vec_second,
    cotangent,
):
    layers = vectors.shape[0]
    per_layer = blocks.shape[0] // layers
    width = blocks.shape[2]
    owner_rows = lax.axis_size("dp")
    slots = rot_first.shape[0]
    selector = slot_table(owner, slots, owner_rows)

    vector_parts = lax.all_gather(vectors.astype(low), ("dp", "fsdp"), axis=0, tiled=False)
    vector_full = vector_parts.transpose(1, 2, 0, 3).reshape(layers, vectors.shape[1], width).astype(full)
    blocks_low, vector_full = lax.optimization_barrier((blocks.astype(low), vector_full))

    def fetch(layer_index):
        start = per_layer * layer_index
        return lax.all_gather(blocks_low[start : start + per_layer], ("dp", "fsdp"), axis=1, tiled=True)

    seg_column = segment[:, :, None]
    seg_row = segment[:, None, :]
    state = tokens
    kept = []
    for layer_index in range(layers):
        weights = fetch(layer_index)
        out_dtype = low if layer_index == layers - 1 else full
        results = forward_layer(state, seg_column, seg_row, vector_full[layer_index], weights, out_dtype)
        kept.append((state, weights, results[:5], results[5:12]))
        state = results[12]
    layer_out = state

    owner_count = owner_rows
    z_count = lax.axis_size("fsdp")
    upstream = cotangent
    if owner_rows == 8 and z_count == 4:
        step_pieces = reduce_and_step(
            upstream, kept, vector_full, seg_column, seg_row, owner, selector, left_basis, right_basis,
            rot_first, rot_second, blocks, vectors.shape[1], z_count,
        )
    else:
        step_pieces = plain_reduce_and_step(
            upstream, kept, vector_full, seg_column, seg_row, selector, left_basis, right_basis,
            rot_first, rot_second, blocks, vectors.shape[1], owner_count,
        )
    upstream, new_blocks, new_low, first_new, second_new, vector_grad = step_pieces
    vector_first = beta_one * vec_first + (1.0 - beta_one) * vector_grad
    vector_second = beta_two * vec_second + (1.0 - beta_two) * vector_grad * vector_grad
    vector_step = (
        vector_first
        / (1.0 - beta_one**STEP)
        / (jnp.sqrt(vector_second / (1.0 - beta_two**STEP)) + adam_epsilon)
    )
    vector_new = vectors - vector_rate * (vector_step + weight_decay * vectors)
    return (
        layer_out,
        upstream,
        new_blocks,
        new_low,
        first_new,
        second_new,
        vector_first,
        vector_second,
        vector_new,
    )


def solution(mesh):
    return jax.shard_map(
        shards,
        mesh=mesh,
        in_specs=(
            P(("dp", "fsdp"), None),
            P(("dp", "fsdp"), None),
            P(None, ("dp", "fsdp"), None),
            P(None, None, ("dp", "fsdp")),
            P(),
            P("dp", None, "fsdp", None),
            P("dp", None, "fsdp"),
            P("dp", None, "fsdp"),
            P("dp", None, "fsdp"),
            P(None, None, ("dp", "fsdp")),
            P(None, None, ("dp", "fsdp")),
            P(("dp", "fsdp"), None),
        ),
        out_specs=(
            P(("dp", "fsdp"), None),
            P(("dp", "fsdp"), None),
            P(None, ("dp", "fsdp"), None),
            P(None, ("dp", "fsdp"), None),
            P("dp", None, "fsdp"),
            P("dp", None, "fsdp"),
            P(None, None, ("dp", "fsdp")),
            P(None, None, ("dp", "fsdp")),
            P(None, None, ("dp", "fsdp")),
        ),
        check_vma=False,
    )
```

```python
import functools

import jax
import jax.numpy as jnp
from jax import lax
from jax.experimental import pallas as pl
from jax.experimental.pallas import tpu as pltpu
from jax.sharding import PartitionSpec as P

H = 12
HD = 64
L = 512
STEP = 5
PAIR = 2 * HD
MIB = 1 << 20

beta_one = 0.5
beta_two = 0.5
adam_epsilon = 1e-08
norm_epsilon = 1e-06
matrix_rate = 0.03
vector_rate = 0.2
weight_decay = 0.01
masked_score = -1e30
low = jnp.bfloat16
full = jnp.float32


def dot_nn(a, b):
    return lax.dot_general(a, b, (((1,), (0,)), ((), ())), preferred_element_type=full)


def dot_nt(a, b):
    return lax.dot_general(a, b, (((1,), (1,)), ((), ())), preferred_element_type=full)


def dot_tn(a, b):
    return lax.dot_general(a, b, (((0,), (0,)), ((), ())), preferred_element_type=full)


def gelu_parts(z):
    size = jnp.abs(z) * 0.7071067811865476
    t = 1.0 / (1.0 + 0.3275911 * size)
    bell = jnp.exp(-0.5 * z * z)
    poly = ((((1.061405429 * t - 1.453152027) * t + 1.421413741) * t - 0.284496736) * t + 0.254829592) * t
    half_tail = 0.5 * poly * bell
    phi = jnp.where(z >= 0, 1.0 - half_tail, half_tail)
    return z * phi, phi + z * bell * 0.3989422804014327


def norm_parts(residual):
    average = jnp.mean(residual, axis=-1, keepdims=True)
    centered = residual - average
    inverse = lax.rsqrt(jnp.mean(centered * centered, axis=-1, keepdims=True) + norm_epsilon)
    return centered * inverse, inverse


def norm_back(upstream, unit, inverse, gain):
    scaled = upstream * gain
    return inverse * (
        scaled
        - jnp.mean(scaled, axis=-1, keepdims=True)
        - unit * jnp.mean(scaled * unit, axis=-1, keepdims=True)
    )


def column_sum(values):
    return jnp.sum(values, axis=0, keepdims=True)


def half_masks(dtype):
    lane = lax.broadcasted_iota(jnp.int32, (1, PAIR), 1)
    first = (lane < HD).astype(full)
    return first.astype(dtype), (1.0 - first).astype(dtype)


def segment_bias(seg_column, seg_row):
    return jnp.where(seg_column == seg_row, 0.0, masked_score)


def flip(index, bit):
    return index + bit * (1 - 2 * lax.rem(lax.div(index, bit), 2))


def place():
    dp = lax.axis_index("dp")
    return dp, lax.axis_index("fsdp"), lax.rem(dp, 2), lax.div(dp, 2)


def greet(partners):
    barrier = pltpu.get_barrier_semaphore()
    for device in partners:
        pl.semaphore_signal(barrier, inc=1, device_id=device, device_id_type=pl.DeviceIdType.MESH)
    pl.semaphore_wait(barrier, len(partners))


def z_partners(count):
    dp, z, _, _ = place()
    return [(dp, lax.rem(z + d, count)) for d in range(1, count)]


def chip_partners():
    dp, z, core, spot = place()
    return [
        (flip(dp, 1), z),
        (2 * flip(spot, 1) + core, z),
        (2 * flip(spot, 2) + core, z),
    ]


def remote(source, target, send, receive, device):
    return pltpu.make_async_remote_copy(
        src_ref=source,
        dst_ref=target,
        send_sem=send,
        recv_sem=receive,
        device_id=device,
        device_id_type=pl.DeviceIdType.MESH,
    )


def fold(piece):
    half = piece.shape[1] // 2
    return jnp.concatenate([piece[:, :half], piece[:, half:]], axis=0)


def unfold(piece):
    rows = piece.shape[0] // 2
    return jnp.concatenate([piece[:rows], piece[rows:]], axis=1)


def sum_scratch(count, part, width, z_count, kind=low):
    piece = (2 * part // z_count, width // 2) if kind == low else (part // z_count, width)
    return [
        pltpu.VMEM((2, 4, part, width), kind),
        pltpu.VMEM((count, 4, part, width), kind),
        pltpu.VMEM((count, 2, part, width), kind),
        pltpu.VMEM((count, part, width), kind),
        pltpu.VMEM((count, z_count) + piece, kind),
        pltpu.VMEM((count, z_count) + piece, kind),
        pltpu.SemaphoreType.DMA((2,)),
        pltpu.SemaphoreType.DMA((count, 2)),
        pltpu.SemaphoreType.DMA((count, 2, 2)),
        pltpu.SemaphoreType.DMA((count, 2)),
        pltpu.SemaphoreType.DMA((count, 2, z_count)),
    ]


SUM_REFS = 11


class BlockSum:
    def __init__(self, source, refs):
        self.source = source
        (self.own, self.c, self.b, self.a, self.zs, self.zr,
         self.own_sem, self.c_sem, self.b_sem, self.a_sem, self.z_sem) = refs
        self.count = self.c.shape[0]
        self.kind = self.c.dtype
        self.z_count = self.zs.shape[1]

    def load(self, i):
        core = place()[2]
        slot = lax.rem(i, 2)
        return pltpu.make_async_copy(self.source.at[i, :, core], self.own.at[slot], self.own_sem.at[slot])

    def core_copy(self, i):
        dp, z, core, _ = place()
        return remote(
            self.source.at[i, :, 1 - core], self.c.at[i], self.c_sem.at[i, 0], self.c_sem.at[i, 1], (flip(dp, 1), z)
        )

    def second_copy(self, i, k):
        _, z, core, spot = place()
        other = flip(spot, 2 - core)
        chunk = other if k == 0 else flip(other, 1 + core)
        return remote(
            self.c.at[i, chunk], self.b.at[i, k], self.b_sem.at[i, 0, k], self.b_sem.at[i, 1, k], (2 * other + core, z)
        )

    def third_copy(self, i):
        _, z, core, spot = place()
        other = flip(spot, 1 + core)
        return remote(self.c.at[i, other], self.a.at[i], self.a_sem.at[i, 0], self.a_sem.at[i, 1], (2 * other + core, z))

    def z_copy(self, i, d):
        dp, z, _, _ = place()
        other = lax.rem(z + d, self.z_count)
        return remote(
            self.zs.at[i, other], self.zr.at[i, z], self.z_sem.at[i, 0, d], self.z_sem.at[i, 1, self.z_count - d], (dp, other)
        )

    def open(self, i):
        self.core_copy(i).start()
        self.load(i).start()

    def after_core(self, i):
        self.core_copy(i).wait()
        self.load(i).wait()
        slot = lax.rem(i, 2)
        for k in range(4):
            self.c[i, k] = (self.c[i, k].astype(full) + self.own[slot, k].astype(full)).astype(self.kind)
        self.second_copy(i, 0).start()
        self.second_copy(i, 1).start()

    def after_second(self, i):
        _, _, core, spot = place()
        other = flip(spot, 1 + core)
        self.second_copy(i, 1).wait()
        self.c[i, other] = (self.c[i, other].astype(full) + self.b[i, 1].astype(full)).astype(self.kind)
        self.third_copy(i).start()
        self.second_copy(i, 0).wait()
        self.c[i, spot] = (self.c[i, spot].astype(full) + self.b[i, 0].astype(full)).astype(self.kind)

    def after_third(self, i):
        _, _, _, spot = place()
        self.third_copy(i).wait()
        total = self.c[i, spot].astype(full) + self.a[i].astype(full)
        rows = total.shape[0] // self.z_count
        for k in range(self.z_count):
            piece = total[k * rows : (k + 1) * rows]
            self.zs[i, k] = fold(piece).astype(low) if self.kind == low else piece
        for d in range(1, self.z_count):
            self.z_copy(i, d).start()

    def finish(self, i):
        z = lax.axis_index("fsdp")
        for d in range(1, self.z_count):
            self.z_copy(i, d).wait()
        total = self.zs[i, z].astype(full)
        for d in range(1, self.z_count):
            total = total + self.zr[i, lax.rem(z + d, self.z_count)].astype(full)
        return total

    def tick(self, t):
        for late, stage in enumerate((self.open, self.after_core, self.after_second, self.after_third)):
            @pl.when((t >= late) & (t < self.count + late))
            def _():
                stage(t - late)


class LineGather:
    def __init__(self, source, target, first, local_sem, sem, z_count):
        self.source = source.at[pl.ds(first, target.shape[1])]
        self.target, self.local_sem, self.sem, self.z_count = target, local_sem, sem, z_count

    def hop_copy(self, hop, way):
        dp, z, _, _ = place()
        if way == 0:
            piece, other, coming = z - hop + 1, z + 1, z - hop
            sends = (piece >= 0) & (other < self.z_count)
            receives = coming >= 0
        else:
            piece, other, coming = z + hop - 1, z - 1, z + hop
            sends = (piece < self.z_count) & (other >= 0)
            receives = coming < self.z_count
        piece = jnp.clip(piece, 0, self.z_count - 1)
        other = jnp.clip(other, 0, self.z_count - 1)
        source = self.source if hop == 1 else self.target.at[piece]
        copy = remote(source, self.target.at[piece], self.sem.at[way, 0, hop - 1], self.sem.at[way, 1, hop - 1], (dp, other))
        return copy, sends, receives

    def local(self):
        return pltpu.make_async_copy(self.source, self.target.at[lax.axis_index("fsdp")], self.local_sem)

    def start(self, hop):
        if hop == 1:
            self.local().start()
        for way in range(2):
            copy, sends, _ = self.hop_copy(hop, way)

            @pl.when(sends)
            def _():
                copy.start()

    def wait(self, hop):
        if hop == 1:
            self.local().wait()
        for way in range(2):
            copy, sends, receives = self.hop_copy(hop, way)

            @pl.when(sends)
            def _():
                copy.wait_send()

            @pl.when(receives)
            def _():
                copy.wait_recv()

    def advance(self, hop):
        if hop > 1:
            self.wait(hop - 1)
        if hop < self.z_count:
            self.start(hop)


def gather_scratch(count, rows, width, z_count, kind=low):
    piece = (2 * rows // z_count, width // 2) if kind == low else (rows // z_count, width)
    return [
        pltpu.VMEM((count, z_count) + piece, kind),
        pltpu.SemaphoreType.DMA((count, 2, z_count)),
        pltpu.SemaphoreType.DMA((count, 2)),
        pltpu.SemaphoreType.DMA((count, 2, 2)),
        pltpu.SemaphoreType.DMA((count, 2, 4)),
    ]


GATHER_REFS = 5


class BlockGather:
    def __init__(self, source, whole, base, refs):
        self.source, self.whole, self.base = source, whole, base
        self.zr, self.z_sem, self.a_sem, self.b_sem, self.c_sem = refs
        self.count, self.z_count = self.zr.shape[0], self.zr.shape[1]
        self.rows = self.whole.shape[1] // (2 * 4)

    def z_copy(self, i, d):
        dp, z, _, _ = place()
        other = lax.rem(z + d, self.z_count)
        return remote(
            self.source.at[i], self.zr.at[i, z], self.z_sem.at[i, 0, d], self.z_sem.at[i, 1, self.z_count - d], (dp, other)
        )

    def chunk(self, i, spot, core):
        start = pl.multiple_of((2 * spot + core) * self.rows, self.rows)
        return self.whole.at[self.base + i, pl.ds(start, self.rows)]

    def hop(self, i, spot, sem, target):
        core = place()[2]
        chunk = self.chunk(i, spot, core)
        return remote(chunk, chunk, sem.at[0], sem.at[1], target)

    def first_copy(self, i):
        _, z, core, spot = place()
        return self.one(i, spot, self.a_sem.at[i, 0], self.a_sem.at[i, 1], (2 * flip(spot, 1 + core) + core, z))

    def second_copy(self, i, k):
        _, z, core, spot = place()
        chunk = spot if k == 0 else flip(spot, 1 + core)
        return self.one(
            i, chunk, self.b_sem.at[i, 0, k], self.b_sem.at[i, 1, k], (2 * flip(spot, 2 - core) + core, z)
        )

    def core_copy(self, i, k):
        dp, z, core, spot = place()
        chunk = spot
        if k & 1:
            chunk = flip(chunk, 1 + core)
        if k & 2:
            chunk = flip(chunk, 2 - core)
        return self.one(i, chunk, self.c_sem.at[i, 0, k], self.c_sem.at[i, 1, k], (flip(dp, 1), z))

    def one(self, i, spot, send, receive, device):
        chunk = self.chunk(i, spot, place()[2])
        return remote(chunk, chunk, send, receive, device)

    def begin(self):
        z = lax.axis_index("fsdp")

        def body(i, carry):
            for d in range(1, self.z_count):
                self.z_copy(i, d).start()
            self.zr[i, z] = self.source[i]
            return carry

        lax.fori_loop(0, self.count, body, 0)

    def open(self, i):
        dp = lax.axis_index("dp")
        for d in range(1, self.z_count):
            self.z_copy(i, d).wait()
        pieces = [self.zr[i, k].astype(full) for k in range(self.z_count)]
        if self.zr.dtype == low:
            pieces = [unfold(piece) for piece in pieces]
        start = pl.multiple_of(dp * self.rows, self.rows)
        self.whole[self.base + i, pl.ds(start, self.rows)] = jnp.concatenate(pieces, axis=0).astype(self.whole.dtype)
        self.first_copy(i).start()
        self.second_copy(i, 0).start()
        self.core_copy(i, 0).start()

    def after_first(self, i):
        self.first_copy(i).wait()
        self.second_copy(i, 1).start()
        self.core_copy(i, 1).start()

    def after_second(self, i):
        self.second_copy(i, 0).wait()
        self.core_copy(i, 2).start()
        self.second_copy(i, 1).wait()
        self.core_copy(i, 3).start()

    def close(self, i):
        for k in range(4):
            self.core_copy(i, k).wait()

    def tick(self, t, done=None):
        for late, stage in enumerate((self.open, self.after_first, self.after_second, self.close)):
            @pl.when((t >= late) & (t < self.count + late))
            def _():
                stage(t - late)
                if late == 3 and done is not None:
                    done(t - late)


def split_refs(refs, *counts):
    result, start = [], 0
    for count in counts:
        result.append(refs[start : start + count])
        start += count
    return result


class Side:
    def __init__(self, plan, sources, targets, sum_refs, line_refs):
        self.plan = plan
        sums = plan.sums
        self.sum = BlockSum(sources[0], sum_refs) if sums else None
        self.result = targets[0] if sums else None
        self.lines = line_gathers(plan.lines, sources[sums:], targets[sums:], line_refs, plan.z_count)

    def enter(self, now):
        if not self.plan.active:
            return

        @pl.when(now)
        def _():
            greet((chip_partners() if self.plan.sums else []) + z_partners(self.plan.z_count))
            for line in self.lines:
                line.advance(1)

    def leave(self, now):
        if not self.plan.active:
            return

        @pl.when(now)
        def _():
            if self.plan.sums:
                for i in range(self.sum.count):
                    self.result[i] = self.sum.finish(i).astype(low)
            for line in self.lines:
                line.advance(self.plan.z_count)

    def advance(self, now, hop):
        if self.lines and hop < self.plan.z_count:
            @pl.when(now)
            def _():
                for line in self.lines:
                    line.advance(hop)


class Plan:
    def __init__(self, pending=None, lines=(), z_count=1):
        self.z_count = z_count
        self.sums = int(pending is not None)
        self.lines = [(first, count) for _, first, count in lines]
        self.active = bool(self.sums or lines)
        self.arguments, self.results, self.result_specs, self.scratch = [], [], [], []
        if pending is not None:
            count, part, width = pending.shape[0], pending.shape[3], pending.shape[4]
            self.arguments.append(pending)
            self.results.append(jax.ShapeDtypeStruct((count, 2 * part // z_count, width // 2), low))
            self.result_specs.append(
                pl.BlockSpec(self.results[0].shape, lambda i: (0, 0, 0), pipeline_mode=pl.Buffered(1))
            )
            self.scratch += sum_scratch(count, part, width, z_count)
        for basis, _, count in lines:
            self.arguments.append(basis)
            self.results.append(jax.ShapeDtypeStruct((z_count, count) + basis.shape[1:], low))
            self.result_specs.append(ANYWHERE)
        self.scratch += line_scratch(len(lines), z_count)
        self.argument_specs = [ANYWHERE] * len(self.arguments)

    def split(self, refs, inputs, outputs, scratch):
        extra = self.sums + len(self.lines)
        return split_refs(
            refs, inputs, extra, outputs, extra, scratch, SUM_REFS * self.sums, 2 * bool(self.lines)
        )


def line_scratch(count, z_count):
    if not count:
        return []
    return [pltpu.SemaphoreType.DMA((count,)), pltpu.SemaphoreType.DMA((count, 2, 2, z_count - 1))]


def line_gathers(spans, sources, targets, refs, z_count):
    return [
        LineGather(source, target, first, refs[0].at[n], refs[1].at[n], z_count)
        for n, (source, target, (first, _)) in enumerate(zip(sources, targets, spans))
    ]


ANYWHERE = pl.BlockSpec(memory_space=pl.ANY)
IN_VMEM = pl.BlockSpec(memory_space=pltpu.VMEM)


def forward_kernel(plan, *refs):
    inputs, sources, outputs, targets, scratch, gather_refs, vec_refs, line_refs = plan.split(refs)
    x_ref, segc_ref, segr_ref, vec_ref, w_hbm = inputs
    (q_ref, k_ref, v_ref, ctxt_ref, lse_ref, x1_ref, inv1_ref, n1_ref, u_ref, gp_ref, x2_ref, inv2_ref,
     out_ref) = outputs
    w, bias, vt, n1_all, acc, w_sem = scratch
    s = pl.program_id(0)
    tokens, width = acc.shape
    rows_now = x_ref.shape[0]
    rows = tokens // rows_now
    inner = plan.inner
    local = plan.local
    gather = vec_gather = None
    if plan.gathered:
        w_out, out_sem = targets[0], scratch_tail(plan, refs)
        gather = BlockGather(sources[0], w, local, gather_refs)
        if plan.vectors:
            vec_gather = BlockGather(sources[1], plan.vec_whole(refs), 0, vec_refs)
            vec_ref = targets[1]
    lines = line_gathers(plan.lines, sources[plan.line_at :], targets[plan.line_target_at :], line_refs, plan.z_count)

    def keep(i):
        return pltpu.make_async_copy(w.at[local + i], w_out.at[i], out_sem.at[i])

    def load(j):
        return pltpu.make_async_copy(w_hbm.at[plan.order[j]], w.at[j], w_sem.at[j])

    def arrive(j):
        if j < local:
            load(j).wait()

    def tick(t):
        if gather is not None:
            gather.tick(t, lambda i: keep(i).start())
            if vec_gather is not None:
                vec_gather.tick(t)

    @pl.when(s == 0)
    def _():
        for j in range(local):
            load(j).start()
        if gather is not None:
            greet(chip_partners() + z_partners(plan.z_count))
            if vec_gather is not None:
                vec_gather.begin()
            gather.begin()
            lax.fori_loop(0, plan.lead, lambda t, carry: (tick(t), carry)[1], 0)
            for line in lines:
                line.advance(1)
            if vec_gather is not None:
                turned = vec_gather.whole[0].T
                for layer in range(2):
                    count = plan.vector_rows
                    targets[1 + layer][0:count, :] = turned[layer * count : (layer + 1) * count, :]
        for j in range(min(local, 3)):
            arrive(j)

    @pl.when(s < rows)
    def _():
        xin = x_ref[...].astype(low)
        bias[...] = segment_bias(segc_ref[0], segr_ref[0])
        q_ref[...] = (dot_nn(xin, w[0]) + vec_ref[0:1, :]).astype(low)
        k_ref[...] = dot_nn(xin, w[1]).astype(low)
        value = dot_nn(xin, w[2]) + vec_ref[1:2, :]
        v_ref[...] = value.astype(low)
        vt[...] = value.T.astype(low)
        masks = half_masks(low)
        pairs = width // PAIR

        def pair_step(p, carry):
            lanes = pl.ds(pl.multiple_of(p * PAIR, PAIR), PAIR)
            q_pair = q_ref[:, lanes] * jnp.asarray(HD ** (-0.5), low)
            k_pair = k_ref[:, lanes]
            for h in range(2):
                scores = dot_nt(k_pair, q_pair * masks[h]) + bias[...]
                largest = jnp.max(scores, axis=0, keepdims=True)
                expanded = jnp.exp(scores - largest)
                total = column_sum(expanded)
                here = pl.ds(pl.multiple_of(p * PAIR + h * HD, HD), HD)
                context = dot_nn(vt[here, :], expanded.astype(low)) * (1.0 / total)
                ctxt_ref[here, :] = context.astype(low)
                lse_ref[0, pl.ds(2 * p + h, 1), :] = largest + jnp.log(total)
            if plan.gathered:
                every = plan.every
                @pl.when(lax.rem(p, every) == every - 1)
                def _():
                    tick(plan.lead + (s * pairs + p) // every)
            return carry

        lax.fori_loop(0, pairs, pair_step, 0)

        @pl.when(s == 0)
        def _():
            if local > 3:
                arrive(3)
            for line in lines:
                line.advance(2)

        context = ctxt_ref[...].astype(full).T.astype(low)
        attended = dot_nn(context, w[3]) + vec_ref[2:3, :]
        unit, inverse = norm_parts(x_ref[...].astype(full) + attended)
        x1_ref[...] = unit
        inv1_ref[...] = inverse
        normed = unit * vec_ref[3:4, :] + vec_ref[4:5, :]
        here = pl.ds(pl.multiple_of(s * rows_now, rows_now), rows_now)
        acc[here, :] = normed + vec_ref[5 + inner : 6 + inner, :]
        normed = normed.astype(low)
        n1_ref[...] = normed
        n1_all[here, :] = normed

    tile = tokens // 4
    after = plan.lead + rows * (width // PAIR) // plan.every

    @pl.when(s >= rows)
    def _():
        c = s - rows

        @pl.when(c == 0)
        def _():
            for j in range(4, local):
                arrive(j)
            for line in lines:
                line.advance(3)

        def token_step(i, carry):
            for half in range(2):
                here = pl.ds(pl.multiple_of((2 * i + half) * tile, tile), tile)
                value, slope = gelu_parts(dot_nn(n1_all[here, :], w[4 + 2 * c]) + vec_ref[pl.ds(5 + c, 1), :])
                active = value.astype(low)
                u_ref[here, :] = active
                gp_ref[here, :] = slope.astype(low)
                acc[here, :] += dot_nn(active, w[5 + 2 * c])
            tick(after + 2 * c + i)
            return carry

        lax.fori_loop(0, 2, token_step, 0)

        @pl.when(c == inner - 1)
        def _():
            base = 5 + inner

            def last(i, carry):
                here = pl.ds(pl.multiple_of(i * tile, tile), tile)
                unit, inverse = norm_parts(acc[here, :])
                x2_ref[here, :] = unit
                inv2_ref[here, :] = inverse
                out_ref[here, :] = (
                    unit * vec_ref[base + 1 : base + 2, :] + vec_ref[base + 2 : base + 3, :]
                ).astype(out_ref.dtype)
                return carry

            lax.fori_loop(0, 4, last, 0)
            if gather is not None:
                for t in range(after + 2 * inner, gather.count + 3):
                    tick(t)
                for line in lines:
                    line.advance(plan.z_count)
                for i in range(gather.count):
                    keep(i).wait()


class ForwardPlan:
    def __init__(self, inner, local, shards=None, vec_shard=None, vector_rows=0, lines=(), lead=0, every=1, z_count=1):
        self.inner, self.local, self.lead, self.every, self.z_count = inner, local, lead, every, z_count
        self.vector_rows = vector_rows
        self.order = [0, 1, 2, 3]
        for c in range(inner):
            self.order += [4 + c, 4 + inner + c]
        self.gathered = 0 if shards is None else shards.shape[0]
        self.vectors = vec_shard is not None
        self.lines = [(first, count) for _, first, count in lines]
        self.line_at = int(self.gathered > 0) + int(self.vectors)
        self.line_target_at = int(self.gathered > 0) + 2 * int(self.vectors)
        self.arguments, self.argument_specs, self.results, self.result_specs, self.scratch = [], [], [], [], []
        shape = jax.ShapeDtypeStruct
        if self.gathered:
            width = 2 * shards.shape[2]
            self.arguments.append(shards)
            self.argument_specs.append(IN_VMEM)
            self.results.append(shape((self.gathered, width, width), low))
            self.result_specs.append(ANYWHERE)
            self.scratch += gather_scratch(self.gathered, width // 8, width, z_count)
        if self.vectors:
            rows, lanes = vec_shard.shape[1:]
            self.arguments.append(vec_shard)
            self.argument_specs.append(IN_VMEM)
            for _ in range(2):
                self.results.append(shape((16, width), full))
                self.result_specs.append(pl.BlockSpec((16, width), lambda s: (0, 0)))
            self.scratch += gather_scratch(1, width // 8, lanes, z_count, full)
        for basis, _, count in lines:
            self.arguments.append(basis)
            self.argument_specs.append(ANYWHERE)
            self.results.append(shape((z_count, count) + basis.shape[1:], low))
            self.result_specs.append(ANYWHERE)
        self.scratch += line_scratch(len(lines), z_count)
        if self.gathered:
            self.scratch.append(pltpu.SemaphoreType.DMA((self.gathered,)))
        if self.vectors:
            self.scratch.append(pltpu.VMEM((1, width, lanes), full))

    def split(self, refs):
        return split_refs(
            refs, 5, len(self.arguments), 13, len(self.results), 6, GATHER_REFS * bool(self.gathered),
            GATHER_REFS * self.vectors, 2 * bool(self.lines),
        )

    def vec_whole(self, refs):
        return refs[-1]


def scratch_tail(plan, refs):
    return refs[-2] if plan.vectors else refs[-1]


def forward_layer(hidden, seg_column, seg_row, vectors, weights, out_dtype, plan, identity=None):
    tokens, width = hidden.shape
    inner = plan.inner
    wide = width * inner
    rows = tokens // L
    heads = width // HD
    shape = jax.ShapeDtypeStruct

    def here(s):
        return jnp.minimum(s, rows - 1)

    def column(s):
        return jnp.maximum(s - rows, 0)

    def row_block(columns):
        return pl.BlockSpec((L, columns), lambda s: (here(s), 0))

    def whole(columns):
        return pl.BlockSpec((tokens, columns), lambda s: (0, 0), pipeline_mode=pl.Buffered(1))

    wide_block = pl.BlockSpec((tokens, width), lambda s: (0, column(s)))
    out_shape = (
        shape((tokens, width), low), shape((tokens, width), low), shape((tokens, width), low),
        shape((width, tokens), low), shape((rows, heads, L), full),
        shape((tokens, width), full), shape((tokens, 1), full), shape((tokens, width), low),
        shape((tokens, wide), low), shape((tokens, wide), low),
        shape((tokens, width), full), shape((tokens, 1), full), shape((tokens, width), out_dtype),
        *plan.results,
    )
    out_specs = (
        row_block(width), row_block(width), row_block(width),
        pl.BlockSpec((width, L), lambda s: (0, here(s))), pl.BlockSpec((1, heads, L), lambda s: (here(s), 0, 0)),
        row_block(width), row_block(1), row_block(width),
        wide_block, wide_block,
        whole(width), whole(1), whole(width),
        *plan.result_specs,
    )
    total = 4 + 2 * inner
    held = max(total, plan.local + plan.gathered)
    return pl.pallas_call(
        functools.partial(forward_kernel, plan),
        grid=(rows + inner,),
        out_shape=out_shape,
        in_specs=[
            row_block(width),
            pl.BlockSpec((1, L, 1), lambda s: (here(s), 0, 0)),
            pl.BlockSpec((1, 1, L), lambda s: (here(s), 0, 0)),
            pl.BlockSpec(vectors.shape, lambda s: (0, 0)),
            ANYWHERE,
            *plan.argument_specs,
        ],
        out_specs=out_specs,
        scratch_shapes=[
            pltpu.VMEM((held, width, width), low),
            pltpu.VMEM((L, L), full),
            pltpu.VMEM((width, L), low),
            pltpu.VMEM((tokens, width), low),
            pltpu.VMEM((tokens, width), full),
            pltpu.SemaphoreType.DMA((total,)),
            *plan.scratch,
        ],
        compiler_params=pltpu.CompilerParams(
            dimension_semantics=("arbitrary",), vmem_limit_bytes=62 * MIB,
            collective_id=identity, has_side_effects=identity is not None,
        ),
        cost_estimate=pl.CostEstimate(
            flops=2 * tokens * width * width * total + 4 * tokens * L * width,
            bytes_accessed=40 * MIB,
            transcendentals=tokens * (L * heads + wide),
        ),
        name="layer_forward",
    )(hidden, seg_column, seg_row, vectors, weights, *plan.arguments)


def wide_back_kernel(plan, inner, *refs):
    inputs, sources, outputs, targets, scratch, sum_refs, line_refs = plan.split(refs, 11, 4, 4)
    up_ref, x2_ref, inv2_ref, x1_ref, inv1_ref, n1_ref, vec_ref, wup_ref, wdown_ref, u_ref, gp_ref = inputs
    dw_ref, dr1_ref, da_ref, dvec_ref = outputs
    dy, dn1, n1t, dz = scratch
    c = pl.program_id(0)
    side = Side(plan, sources, targets, sum_refs, line_refs)
    side.enter(c == 0)
    side.advance(c == 1, 2)
    side.advance(c == 3, 3)
    steps = pl.num_programs(0)
    tokens, width = dn1.shape
    tile = tokens // 4
    pick = [slice(i * tile, (i + 1) * tile) for i in range(4)]
    base = 5 + inner

    @pl.when(c == 0)
    def _():
        gain = vec_ref[base + 1 : base + 2, :]

        def body(i, carry):
            gain_sum, shift_sum, bias_sum = carry
            rows = pl.ds(pl.multiple_of(i * tile, tile), tile)
            upstream = up_ref[rows, :].astype(full)
            unit = x2_ref[rows, :]
            back = norm_back(upstream, unit, inv2_ref[rows, :], gain)
            dn1[rows, :] = back
            branch = back.astype(low)
            dy[rows, :] = branch
            return (
                gain_sum + column_sum(upstream * unit),
                shift_sum + column_sum(upstream),
                bias_sum + column_sum(branch.astype(full)),
            )

        zero = jnp.zeros((1, width), full)
        gain_sum, shift_sum, bias_sum = lax.fori_loop(0, 4, body, (zero, zero, zero))
        dvec_ref[...] = jnp.zeros(dvec_ref.shape, full)
        dvec_ref[base : base + 1, :] = bias_sum
        dvec_ref[base + 1 : base + 2, :] = gain_sum
        dvec_ref[base + 2 : base + 3, :] = shift_sum
        n1t[...] = n1_ref[...].astype(full).T.astype(low)

    def token_step(i, carry):
        rows = pl.ds(pl.multiple_of(i * tile, tile), tile)
        slope = gp_ref[rows, :].astype(full)
        piece = (dot_nt(dy[rows, :], wdown_ref[0]) * slope).astype(low)
        dz[rows, :] = piece
        dn1[rows, :] += dot_nt(piece, wup_ref[0])
        if plan.sums:
            @pl.when(lax.rem(i, 2) == 0)
            def _():
                side.sum.tick(2 * c + lax.div(i, 2))
        return carry + column_sum(piece.astype(full))

    bias_sum = lax.fori_loop(0, 4, token_step, jnp.zeros((1, width), full))
    for j in range(inner):
        @pl.when(c == j)
        def _():
            dvec_ref[5 + j : 6 + j, :] = bias_sum
    dw_ref[0, 0] = dot_nn(n1t[...], dz[...]).astype(low)
    dw_ref[1, 0] = dot_tn(u_ref[...], dy[...]).astype(low)

    @pl.when(c == steps - 1)
    def _():
        gain = vec_ref[3:4, :]

        def body(i, carry):
            gain_sum, shift_sum, bias_sum = carry
            rows = pl.ds(pl.multiple_of(i * tile, tile), tile)
            upstream = dn1[rows, :]
            unit = x1_ref[rows, :]
            back = norm_back(upstream, unit, inv1_ref[rows, :], gain)
            dr1_ref[rows, :] = back
            branch = back.astype(low)
            da_ref[rows, :] = branch
            return (
                gain_sum + column_sum(upstream * unit),
                shift_sum + column_sum(upstream),
                bias_sum + column_sum(branch.astype(full)),
            )

        zero = jnp.zeros((1, width), full)
        gain_sum, shift_sum, bias_sum = lax.fori_loop(0, 4, body, (zero, zero, zero))
        dvec_ref[2:3, :] = bias_sum
        dvec_ref[3:4, :] = gain_sum
        dvec_ref[4:5, :] = shift_sum

    side.leave(c == steps - 1)


def wide_back(upstream, kept, vectors, weights, places, plan, identity=None):
    x1, inv1, n1, u, gp, x2, inv2 = kept
    tokens, width = x1.shape
    up_start, down_start, stride = places
    inner = u.shape[1] // width
    shape = jax.ShapeDtypeStruct

    def whole(array):
        return pl.BlockSpec(array.shape, lambda c: (0, 0), pipeline_mode=pl.Buffered(1))

    return pl.pallas_call(
        functools.partial(wide_back_kernel, plan, inner),
        grid=(inner,),
        out_shape=(
            shape((2, inner, width, width), low),
            shape((tokens, width), full), shape((tokens, width), low), shape((16, width), full),
            *plan.results,
        ),
        in_specs=[
            whole(upstream), whole(x2), whole(inv2), whole(x1), whole(inv1), whole(n1), whole(vectors),
            pl.BlockSpec((1, width, width), lambda c: (up_start + stride * c, 0, 0)),
            pl.BlockSpec((1, width, width), lambda c: (down_start + stride * c, 0, 0)),
            pl.BlockSpec((tokens, width), lambda c: (0, c)),
            pl.BlockSpec((tokens, width), lambda c: (0, c)),
            *plan.argument_specs,
        ],
        out_specs=(
            pl.BlockSpec((2, 1, width, width), lambda c: (0, c, 0, 0)),
            pl.BlockSpec((tokens, width), lambda c: (0, 0), pipeline_mode=pl.Buffered(1)),
            pl.BlockSpec((tokens, width), lambda c: (0, 0), pipeline_mode=pl.Buffered(1)),
            pl.BlockSpec((16, width), lambda c: (0, 0)),
            *plan.result_specs,
        ),
        scratch_shapes=[
            pltpu.VMEM((tokens, width), low),
            pltpu.VMEM((tokens, width), full),
            pltpu.VMEM((width, tokens), low),
            pltpu.VMEM((tokens, width), low),
            *plan.scratch,
        ],
        compiler_params=pltpu.CompilerParams(
            dimension_semantics=("arbitrary",), vmem_limit_bytes=60 * MIB,
            collective_id=identity, has_side_effects=identity is not None,
        ),
        cost_estimate=pl.CostEstimate(
            flops=8 * tokens * width * width * inner, bytes_accessed=50 * MIB, transcendentals=0
        ),
        name="wide_backward",
    )(upstream, x2, inv2, x1, inv1, n1, vectors, weights, weights, u, gp, *plan.arguments)


def attend_back_kernel(plan, *refs):
    inputs, sources, outputs, targets, scratch, sum_refs, line_refs = plan.split(refs, 11, 3, 11)
    da_ref, dr1_ref, x_ref, q_ref, k_ref, v_ref, ctxt_ref, lse_ref, segc_ref, segr_ref, w_ref = inputs
    dw_ref, dx_ref, dvec_ref = outputs
    bias, dctx, kt, delta, dqt, xt, ctx_all, da_all, dq_all, dk_all, dv_all = scratch
    r = pl.program_id(0)
    side = Side(plan, sources, targets, sum_refs, line_refs)
    side.enter(r == 0)
    side.advance(r == 1, 2)
    tokens, width = da_ref.shape
    here = pl.ds(pl.multiple_of(r * tokens, tokens), tokens)
    xt[:, here] = x_ref[...].astype(low).astype(full).T.astype(low)
    ctx_all[:, here] = ctxt_ref[...]
    da_all[here, :] = da_ref[...]
    bias[...] = segment_bias(segc_ref[0], segr_ref[0])
    context_grad = dot_nt(da_ref[...], w_ref[3]).astype(low)
    dctx[...] = context_grad
    kt[...] = k_ref[...].astype(full).T.astype(low)
    products = context_grad.astype(full) * ctxt_ref[...].astype(full).T
    feature = lax.broadcasted_iota(jnp.int32, (16, width), 1)
    head = lax.broadcasted_iota(jnp.int32, (16, width), 0)
    member = ((feature >= head * HD) & (feature < (head + 1) * HD)).astype(full).astype(low)
    high = products.astype(low)
    rest = (products - high.astype(full)).astype(low)
    delta[...] = dot_nt(member, high) + dot_nt(member, rest)
    masks = half_masks(low)
    scale = HD ** (-0.5)

    def pair_step(p, carry):
        lanes = pl.ds(pl.multiple_of(p * PAIR, PAIR), PAIR)
        q_pair = q_ref[:, lanes] * jnp.asarray(scale, low)
        k_pair = k_ref[:, lanes]
        v_pair = v_ref[:, lanes]
        g_pair = dctx[:, lanes]
        key_grad = jnp.zeros((tokens, PAIR), full)
        value_grad = jnp.zeros((tokens, PAIR), full)
        for h in range(2):
            q_half = q_pair * masks[h]
            g_half = g_pair * masks[h]
            scores = dot_nt(k_pair, q_half) + bias[...]
            attention = jnp.exp(scores - lse_ref[0, pl.ds(2 * p + h, 1), :])
            value_grad = value_grad + dot_nn(attention.astype(low), g_half)
            attention_grad = dot_nt(v_pair, g_half)
            score_grad = (attention * (attention_grad - delta[pl.ds(2 * p + h, 1), :])).astype(low)
            key_grad = key_grad + dot_nn(score_grad, q_half)
            rows = pl.ds(pl.multiple_of(p * PAIR + h * HD, HD), HD)
            dqt[rows, :] = dot_nn(kt[rows, :], score_grad) * scale
        dk_all[here, lanes] = key_grad.astype(low)
        dv_all[here, lanes] = value_grad.astype(low)
        if plan.sums:
            side.sum.tick(r * (width // PAIR) + p)
        return carry

    lax.fori_loop(0, width // PAIR, pair_step, 0)
    side.advance(r == 1, 3)
    query_grad = dqt[...].T.astype(low)
    dq_all[here, :] = query_grad
    key_grad = dk_all[here, :]
    value_grad = dv_all[here, :]
    dx_ref[...] = (
        dr1_ref[...]
        + dot_nt(query_grad, w_ref[0])
        + dot_nt(key_grad, w_ref[1])
        + dot_nt(value_grad, w_ref[2])
    )

    @pl.when(r == 0)
    def _():
        dvec_ref[...] = jnp.zeros(dvec_ref.shape, full)

    dvec_ref[0:1, :] += column_sum(query_grad.astype(full))
    dvec_ref[1:2, :] += column_sum(value_grad.astype(full))

    @pl.when(r == pl.num_programs(0) - 1)
    def _():
        for j, grad in enumerate((dq_all, dk_all, dv_all)):
            dw_ref[j] = dot_nn(xt[...], grad[...]).astype(low)
        dw_ref[3] = dot_nn(ctx_all[...], da_all[...]).astype(low)

    side.leave(r == pl.num_programs(0) - 1)


def attend_back(da, dr1, hidden, kept, seg_column, seg_row, weights, start, plan, identity=None):
    q, k, v, ctxt, lse = kept
    tokens, width = da.shape
    rows = tokens // L
    heads = width // HD
    shape = jax.ShapeDtypeStruct

    def row_block():
        return pl.BlockSpec((L, width), lambda r: (r, 0))

    return pl.pallas_call(
        functools.partial(attend_back_kernel, plan),
        grid=(rows,),
        out_shape=(
            shape((4, width, width), low), shape((tokens, width), full), shape((8, width), full), *plan.results,
        ),
        in_specs=[
            row_block(), row_block(), row_block(), row_block(), row_block(), row_block(),
            pl.BlockSpec((width, L), lambda r: (0, r)),
            pl.BlockSpec((1, heads, L), lambda r: (r, 0, 0)),
            pl.BlockSpec((1, L, 1), lambda r: (r, 0, 0)),
            pl.BlockSpec((1, 1, L), lambda r: (r, 0, 0)),
            pl.BlockSpec((4, width, width), lambda r: (start, 0, 0), pipeline_mode=pl.Buffered(1)),
            *plan.argument_specs,
        ],
        out_specs=(
            pl.BlockSpec((4, width, width), lambda r: (0, 0, 0), pipeline_mode=pl.Buffered(1)),
            row_block(),
            pl.BlockSpec((8, width), lambda r: (0, 0)),
            *plan.result_specs,
        ),
        scratch_shapes=[
            pltpu.VMEM((L, L), full),
            pltpu.VMEM((L, width), low),
            pltpu.VMEM((width, L), low),
            pltpu.VMEM((16, L), full),
            pltpu.VMEM((width, L), full),
            pltpu.VMEM((width, tokens), low),
            pltpu.VMEM((width, tokens), low),
            pltpu.VMEM((tokens, width), low),
            pltpu.VMEM((tokens, width), low),
            pltpu.VMEM((tokens, width), low),
            pltpu.VMEM((tokens, width), low),
            *plan.scratch,
        ],
        compiler_params=pltpu.CompilerParams(
            dimension_semantics=("arbitrary",), vmem_limit_bytes=60 * MIB,
            collective_id=identity, has_side_effects=identity is not None,
        ),
        cost_estimate=pl.CostEstimate(
            flops=16 * tokens * width * width + 10 * tokens * L * width,
            bytes_accessed=30 * MIB,
            transcendentals=tokens * L * heads,
        ),
        name="attend_backward",
    )(da, dr1, hidden, q, k, v, ctxt, lse, seg_column, seg_row, weights, *plan.arguments)


def moments(rotated, first, second):
    first_new = beta_one * first + (1.0 - beta_one) * rotated
    second_new = beta_two * second + (1.0 - beta_two) * rotated * rotated
    direction = (
        first_new
        / (1.0 - beta_one**STEP)
        / (jnp.sqrt(second_new / (1.0 - beta_two**STEP)) + adam_epsilon)
    )
    return first_new, second_new, direction


def optimizer_kernel(left_map, right_map, parts, *refs):
    inputs, bases, outputs, scratch, sum_refs, vec_refs = split_refs(refs, 8, parts, 5, 20, SUM_REFS, SUM_REFS)
    index_ref, place_ref, tail_hbm, vec_hbm, ready, first_hbm, second_hbm, blocks = inputs
    new_ref, low_ref, first_out, second_out, vec_out = outputs
    (store, left, right, first_in, second_in, g_out, g_in, t_out, t_in, e_out, e_in, w_out, w_in,
     load_sem, g_sem, t_sem, e_sem, w_sem, load_sem_left, load_sem_right) = scratch
    dp, z, core, spot = place()
    slots, owners = g_in.shape[0], g_in.shape[1]
    z_count = t_in.shape[1]
    count = blocks.shape[0]
    tail = BlockSum(tail_hbm, sum_refs)
    vec = BlockSum(vec_hbm, vec_refs)
    greet([(lax.rem(dp + d, owners), z) for d in range(1, owners)] + z_partners(z_count))
    loads = []
    for s in range(slots):
        loads.append(
            [
                pltpu.make_async_copy(
                    bases[right_map[s][0]].at[:, right_map[s][1]], right.at[:, s], load_sem_right.at[s]
                ),
                pltpu.make_async_copy(bases[left_map[s][0]].at[:, left_map[s][1]], left.at[:, s], load_sem_left.at[s]),
                pltpu.make_async_copy(first_hbm.at[s], first_in.at[s], load_sem.at[0, s]),
                pltpu.make_async_copy(second_hbm.at[s], second_in.at[s], load_sem.at[1, s]),
            ]
        )

    def sum_step(t, carry):
        tail.tick(t)
        vec.tick(t)
        return carry

    lax.fori_loop(0, tail.count + 3, sum_step, 0)
    for slot_loads in loads:
        for copy in slot_loads:
            copy.start()
    store[tail.count : count] = ready[...]
    store[count] = jnp.zeros(store.shape[1:], low)
    for i in range(tail.count):
        store[i] = tail.finish(i).astype(low)

    def g_copy(s, d):
        other = lax.rem(dp + d, owners)
        return remote(g_out.at[s, d], g_in.at[s, dp], g_sem.at[0, s, d], g_sem.at[1, s, owners - d], (other, z))

    def t_copy(s, d):
        other = lax.rem(z + d, z_count)
        return remote(t_out.at[s, d], t_in.at[s, z], t_sem.at[0, s, d], t_sem.at[1, s, z_count - d], (dp, other))

    def e_copy(s, d):
        other = lax.rem(z + d, z_count)
        return remote(e_out.at[s, d], e_in.at[s, z], e_sem.at[0, s, d], e_sem.at[1, s, z_count - d], (dp, other))

    def w_copy(s, d):
        other = lax.rem(dp + d, owners)
        return remote(
            w_out.at[s, other], w_in.at[s * owners + dp], w_sem.at[0, s, d], w_sem.at[1, s, owners - d], (other, z)
        )

    for s in range(slots):
        for d in range(1, owners):
            g_out[s, d] = store[index_ref[s * owners + lax.rem(dp + d, owners)]]
            g_copy(s, d).start()
        g_in[s, dp] = store[index_ref[s * owners + dp]]

    for s in range(slots):
        for d in range(1, owners):
            g_copy(s, d).wait()
        loads[s][0].wait()
        grad = jnp.concatenate([unfold(g_in[s, c].astype(full)) for c in range(owners)], axis=0).astype(low)
        for d in range(1, z_count):
            t_out[s, d] = dot_nt(grad, right[lax.rem(z + d, z_count), s]).astype(low)
            t_copy(s, d).start()
        t_in[s, z] = dot_nt(grad, right[z, s]).astype(low)

    for s in range(slots):
        for d in range(1, z_count):
            t_copy(s, d).wait()
        for copy in loads[s][1:]:
            copy.wait()
        rotated = dot_tn(left[0, s], t_in[s, 0])
        for f in range(1, z_count):
            rotated = rotated + dot_tn(left[f, s], t_in[s, f])
        first_new, second_new, direction = moments(rotated, first_in[s], second_in[s])
        first_out[s] = first_new
        second_out[s] = second_new
        direction = direction.astype(low)
        for d in range(1, z_count):
            e_out[s, d] = dot_nn(left[lax.rem(z + d, z_count), s], direction).astype(low)
            e_copy(s, d).start()
        e_in[s, z] = dot_nn(left[z, s], direction).astype(low)

    rows = left.shape[2] // owners
    for s in range(slots):
        for d in range(1, z_count):
            e_copy(s, d).wait()
        step = dot_nn(e_in[s, 0], right[0, s])
        for f in range(1, z_count):
            step = step + dot_nn(e_in[s, f], right[f, s])
        for c in range(owners):
            w_out[s, c] = fold(step[c * rows : (c + 1) * rows]).astype(low)
        for d in range(1, owners):
            w_copy(s, d).start()
        w_in[s * owners + dp] = w_out[s, dp]

    vec_out[...] = vec.finish(0)
    for s in range(slots):
        for d in range(1, owners):
            w_copy(s, d).wait()

    def block_step(b, carry):
        step = unfold(w_in[place_ref[b]].astype(full))
        block = blocks[b]
        new = block - matrix_rate * (step + weight_decay * block)
        new_ref[b] = new
        low_ref[b] = new.astype(low)
        return carry

    lax.fori_loop(0, count, block_step, 0)


def optimizer(index, places, tail, vec, ready, bases, left_map, right_map, first, second, blocks, z_count, identity):
    slots, width, columns = first.shape
    owners = index.shape[0] // slots
    count, rows = blocks.shape[0], blocks.shape[1]
    span = bases[0].shape[2]
    shape = jax.ShapeDtypeStruct
    piece = (2 * rows, width // 2)
    smem = pl.BlockSpec(memory_space=pltpu.SMEM)
    return pl.pallas_call(
        functools.partial(optimizer_kernel, left_map, right_map, len(bases)),
        out_shape=(
            shape(blocks.shape, full), shape(blocks.shape, low), shape(first.shape, full), shape(first.shape, full),
            shape((rows, vec.shape[-1]), full),
        ),
        in_specs=[smem, smem, ANYWHERE, ANYWHERE, IN_VMEM, ANYWHERE, ANYWHERE, IN_VMEM] + [ANYWHERE] * len(bases),
        out_specs=(IN_VMEM,) * 5,
        scratch_shapes=[
            pltpu.VMEM((count + 1,) + piece, low),
            pltpu.VMEM((z_count, slots, span, width), low),
            pltpu.VMEM((z_count, slots, columns, width), low),
            pltpu.VMEM((slots, width, columns), full),
            pltpu.VMEM((slots, width, columns), full),
            pltpu.VMEM((slots, owners) + piece, low),
            pltpu.VMEM((slots, owners) + piece, low),
            pltpu.VMEM((slots, z_count, span, columns), low),
            pltpu.VMEM((slots, z_count, span, columns), low),
            pltpu.VMEM((slots, z_count, span, columns), low),
            pltpu.VMEM((slots, z_count, span, columns), low),
            pltpu.VMEM((slots, owners) + piece, low),
            pltpu.VMEM((slots * owners,) + piece, low),
            pltpu.SemaphoreType.DMA((2, slots)),
            pltpu.SemaphoreType.DMA((2, slots, owners)),
            pltpu.SemaphoreType.DMA((2, slots, z_count)),
            pltpu.SemaphoreType.DMA((2, slots, z_count)),
            pltpu.SemaphoreType.DMA((2, slots, owners)),
            pltpu.SemaphoreType.DMA((slots,)),
            pltpu.SemaphoreType.DMA((slots,)),
            *sum_scratch(tail.shape[0], tail.shape[3], width, z_count),
            *sum_scratch(1, vec.shape[3], vec.shape[4], z_count, full),
        ],
        compiler_params=pltpu.CompilerParams(
            vmem_limit_bytes=60 * MIB, collective_id=identity, has_side_effects=True
        ),
        cost_estimate=pl.CostEstimate(
            flops=8 * slots * span * width * width, bytes_accessed=40 * MIB, transcendentals=slots * width * columns
        ),
        name="optimizer",
    )(index, places, tail, vec, ready, first, second, blocks, *bases)


def slot_table(owner, slots, owner_rows):
    block_count = owner.shape[0]
    same_owner = owner[:, None] == owner[None, :]
    ordering = jnp.arange(block_count, dtype=jnp.int32)
    earlier = ordering[None, :] < ordering[:, None]
    ranking = jnp.sum(jnp.where(same_owner & earlier, 1, 0), axis=1).astype(jnp.int32)
    owner_match = owner[None, :] == jnp.arange(owner_rows, dtype=jnp.int32)[:, None]
    slot_match = ranking[None, :] == jnp.arange(slots, dtype=jnp.int32)[:, None]
    return jnp.where(slot_match[:, None, :] & owner_match[None, :, :], 1.0, 0.0).astype(full)


def scatter_sum(grads):
    blocks, width = grads.shape[0], grads.shape[2]
    cut = grads.reshape(blocks, lax.axis_size("dp"), -1, width).transpose(1, 0, 2, 3)
    outer = lax.psum_scatter(cut, "dp", scatter_dimension=0, tiled=False)
    blocks, rows, width = outer.shape
    count = lax.axis_size("fsdp")
    cut = outer.reshape(blocks, count, rows // count, width).transpose(1, 0, 2, 3)
    return lax.psum_scatter(cut, "fsdp", scatter_dimension=0, tiled=False)


def scatter_vectors(grads):
    rows, width = grads.shape
    count = lax.axis_size("dp") * lax.axis_size("fsdp")
    cut = grads.reshape(rows, count, width // count).transpose(1, 0, 2)
    return lax.psum_scatter(cut, ("dp", "fsdp"), scatter_dimension=0, tiled=False)


def gathering_program(
    tokens, segment, blocks, vectors, owner, left_basis, right_basis, rot_first, rot_second, cotangent, z_count
):
    layers, vector_rows = vectors.shape[:2]
    count, shard_rows, width = blocks.shape
    per_layer = count // layers
    inner = (per_layer - 4) // 2
    owners = lax.axis_size("dp")
    slots = rot_first.shape[0]
    part = width // owners
    lanes = 128
    seg_column, seg_row = segment[:, :, None], segment[:, None, :]

    order = [0, 1, 2, 3]
    for c in range(inner):
        order += [4 + c, 4 + inner + c]
    folded = blocks.astype(low).reshape(count, shard_rows, 2, width // 2).transpose(0, 2, 1, 3)
    folded = folded.reshape(count, 2 * shard_rows, width // 2)

    def pick(numbers):
        return jnp.stack([folded[j] for j in numbers])

    head = pick(order + [per_layer + j for j in order[:4]])
    rest = pick([per_layer + j for j in order[4:]])
    vec_shard = vectors.astype(low).astype(full).reshape(layers * vector_rows, shard_rows).T
    vec_shard = jnp.pad(vec_shard, ((0, 0), (0, lanes - layers * vector_rows)))[None]
    left_low = left_basis.reshape(slots, -1, width).astype(low)
    right_low = right_basis.transpose(0, 2, 1).astype(low)

    plan = ForwardPlan(
        inner, 0, head, vec_shard, vector_rows, [(right_low, 0, 2)], lead=6, every=3, z_count=z_count
    )
    empty_vec = jnp.zeros((16, width), full)
    results = forward_layer(tokens, seg_column, seg_row, empty_vec, head, full, plan, 6)
    kept_a = results[:12]
    hidden, weights_a, vec_a, vec_b, right_01 = results[12:]
    plan = ForwardPlan(inner, 4, rest, lines=[(right_low, 2, 2)], lead=0, every=2, z_count=z_count)
    plan.order = [per_layer + j for j in range(4)]
    results = forward_layer(hidden, seg_column, seg_row, vec_b, weights_a, low, plan, 7)
    kept_b = results[:12]
    layer_out, weights_b, right_23 = results[12:]

    def cut(grads):
        return grads.reshape(-1, owners // 2, 2, part, width)

    plan = Plan(None, [(right_low, 4, 1), (left_low, 0, 1)], z_count)
    dw_wide, dr1, da, dvec_wide_b, right_4, left_0 = wide_back(
        cotangent, kept_b[5:], vec_b, weights_b, (0, 1, 2), plan, 1
    )
    plan = Plan(cut(dw_wide), [(left_low, 1, 1)], z_count)
    dw_attend, upstream, dvec_attend_b, wide_sum_b, left_1 = attend_back(
        da, dr1, hidden, kept_b[:5], seg_column, seg_row, weights_a, per_layer // 4, plan, 2
    )
    plan = Plan(cut(dw_attend), [(left_low, 2, 2)], z_count)
    dw_wide, dr1, da, dvec_wide_a, attend_sum_b, left_23 = wide_back(
        upstream, kept_a[5:], vec_a, weights_a, (4, 5, 2), plan, 3
    )
    plan = Plan(cut(dw_wide), [(left_low, 4, 1)], z_count)
    dw_attend, upstream, dvec_attend_a, wide_sum_a, left_4 = attend_back(
        da, dr1, tokens, kept_a[:5], seg_column, seg_row, weights_a, 0, plan, 5
    )

    ready = jnp.concatenate([wide_sum_a, attend_sum_b, wide_sum_b], axis=0)
    dvec = jnp.concatenate(
        [dvec_attend_a[:2], dvec_wide_a[2:vector_rows], dvec_attend_b[:2], dvec_wide_b[2:vector_rows]], axis=0
    )
    vec = jnp.pad(dvec, ((0, lanes - dvec.shape[0]), (0, 0))).T.reshape(1, owners // 2, 2, part, lanes)
    numbers = jnp.arange(count, dtype=jnp.int32)
    table = slot_table(owner, slots, owners).reshape(slots * owners, count)
    held = jnp.sum(table, axis=1)
    index = jnp.where(held > 0, jnp.sum(table * numbers, axis=1), count).astype(jnp.int32)
    places = jnp.sum(table * jnp.arange(slots * owners, dtype=jnp.int32)[:, None], axis=0).astype(jnp.int32)
    bases = (right_01, right_23, right_4, left_0, left_1, left_23, left_4)
    right_map = [(0, 0), (0, 1), (1, 0), (1, 1), (2, 0)]
    left_map = [(3, 0), (4, 0), (5, 0), (5, 1), (6, 0)]
    new_blocks, new_low, first_new, second_new, vec_sum = optimizer(
        index, places, cut(dw_attend), vec, ready, bases, left_map, right_map, rot_first, rot_second, blocks, z_count, 4
    )
    vector_grad = vec_sum[:, : dvec.shape[0]].T.reshape(-1, vector_rows, shard_rows)
    return layer_out, upstream, new_blocks, new_low, first_new, second_new, vector_grad


def plain_program(
    tokens, segment, blocks, vectors, owner, left_basis, right_basis, rot_first, rot_second, cotangent
):
    layers, vector_rows = vectors.shape[:2]
    per_layer = blocks.shape[0] // layers
    inner = (per_layer - 4) // 2
    width = blocks.shape[2]
    owner_rows = lax.axis_size("dp")
    slots = rot_first.shape[0]
    selector = slot_table(owner, slots, owner_rows)
    vector_parts = lax.all_gather(vectors.astype(low), ("dp", "fsdp"), axis=0, tiled=False)
    vector_full = vector_parts.transpose(1, 2, 0, 3).reshape(layers, vector_rows, width).astype(full)
    blocks_low, vector_full = lax.optimization_barrier((blocks.astype(low), vector_full))

    seg_column = segment[:, :, None]
    seg_row = segment[:, None, :]
    state = tokens
    kept = []
    for layer_index in range(layers):
        start = per_layer * layer_index
        weights = lax.all_gather(blocks_low[start : start + per_layer], ("dp", "fsdp"), axis=1, tiled=True)
        out_dtype = low if layer_index == layers - 1 else full
        results = forward_layer(
            state, seg_column, seg_row, vector_full[layer_index], weights, out_dtype, ForwardPlan(inner, per_layer)
        )
        kept.append((state, weights, results[:5], results[5:12]))
        state = results[12]
    layer_out = state
    upstream = cotangent
    right_low = lax.all_gather(right_basis.astype(low), "fsdp", axis=2, tiled=True)
    block_shards = [None] * layers
    vector_shards = [None] * layers
    for layer_index in reversed(range(layers)):
        hidden, weights, attend_kept, wide_kept = kept[layer_index]
        dw_wide, dr1, da, dvec_wide = wide_back(
            upstream, wide_kept, vector_full[layer_index], weights, (4, 4 + inner, 1), Plan()
        )
        wide_shard = scatter_sum(dw_wide.reshape(-1, width, width))
        dw_attend, upstream, dvec_attend = attend_back(
            da, dr1, hidden, attend_kept, seg_column, seg_row, weights, 0, Plan()
        )
        dvec = jnp.concatenate([dvec_attend[:2], dvec_wide[2:vector_rows]], axis=0)
        block_shards[layer_index] = jnp.concatenate([scatter_sum(dw_attend), wide_shard], axis=0)
        vector_shards[layer_index] = scatter_vectors(dvec)
    vector_grad = jnp.stack(vector_shards)
    block_grad = jnp.concatenate(block_shards, axis=0)
    outgoing = jnp.einsum("srk,kid->srid", selector.astype(low), block_grad, preferred_element_type=full)
    incoming = lax.all_to_all(outgoing.astype(low), "dp", split_axis=1, concat_axis=1, tiled=True)
    owned = incoming.reshape(slots, -1, width)
    turned = jnp.einsum("sik,skj->sij", owned, right_low, preferred_element_type=full).astype(low)
    left_rows = left_basis.reshape(slots, -1, width).astype(low)
    partial_sums = jnp.einsum("sra,srb->sab", left_rows, turned, preferred_element_type=full)
    rotated = lax.psum_scatter(
        partial_sums.astype(low), "fsdp", scatter_dimension=2, tiled=True
    ).astype(full)
    first_new, second_new, direction = moments(rotated, rot_first, rot_second)
    direction_full = lax.all_gather(direction.astype(low), "fsdp", axis=2, tiled=True)
    back_right = jnp.einsum("sab,scb->sac", direction_full, right_low, preferred_element_type=full)
    step_rows = jnp.einsum(
        "sia,sac->sic", left_rows, back_right.astype(low), preferred_element_type=full
    )
    returned = lax.all_to_all(
        step_rows.reshape(slots, owner_rows, -1, width).astype(low),
        "dp",
        split_axis=1,
        concat_axis=1,
        tiled=True,
    )
    step_shard = jnp.einsum("srk,srid->kid", selector.astype(low), returned, preferred_element_type=full)
    new_blocks = blocks - matrix_rate * (step_shard + weight_decay * blocks)
    return layer_out, upstream, new_blocks, new_blocks.astype(low), first_new, second_new, vector_grad


def shards(
    tokens,
    segment,
    blocks,
    vectors,
    owner,
    left_basis,
    right_basis,
    rot_first,
    rot_second,
    vec_first,
    vec_second,
    cotangent,
):
    operands = (
        tokens, segment, blocks, vectors, owner, left_basis, right_basis, rot_first, rot_second, cotangent
    )
    z_count = lax.axis_size("fsdp")
    if lax.axis_size("dp") == 8 and z_count == 4:
        results = gathering_program(*operands, z_count)
    else:
        results = plain_program(*operands)
    layer_out, upstream, new_blocks, new_low, first_new, second_new, vector_grad = results
    vector_first = beta_one * vec_first + (1.0 - beta_one) * vector_grad
    vector_second = beta_two * vec_second + (1.0 - beta_two) * vector_grad * vector_grad
    vector_step = (
        vector_first
        / (1.0 - beta_one**STEP)
        / (jnp.sqrt(vector_second / (1.0 - beta_two**STEP)) + adam_epsilon)
    )
    vector_new = vectors - vector_rate * (vector_step + weight_decay * vectors)
    return (
        layer_out,
        upstream,
        new_blocks,
        new_low,
        first_new,
        second_new,
        vector_first,
        vector_second,
        vector_new,
    )


def solution(mesh):
    return jax.shard_map(
        shards,
        mesh=mesh,
        in_specs=(
            P(("dp", "fsdp"), None),
            P(("dp", "fsdp"), None),
            P(None, ("dp", "fsdp"), None),
            P(None, None, ("dp", "fsdp")),
            P(),
            P("dp", None, "fsdp", None),
            P("dp", None, "fsdp"),
            P("dp", None, "fsdp"),
            P("dp", None, "fsdp"),
            P(None, None, ("dp", "fsdp")),
            P(None, None, ("dp", "fsdp")),
            P(("dp", "fsdp"), None),
        ),
        out_specs=(
            P(("dp", "fsdp"), None),
            P(("dp", "fsdp"), None),
            P(None, ("dp", "fsdp"), None),
            P(None, ("dp", "fsdp"), None),
            P("dp", None, "fsdp"),
            P("dp", None, "fsdp"),
            P(None, None, ("dp", "fsdp")),
            P(None, None, ("dp", "fsdp")),
            P(None, None, ("dp", "fsdp")),
        ),
        check_vma=False,
    )
```

```python
import functools

import jax
import jax.numpy as jnp
from jax import lax
from jax.experimental import pallas as pl
from jax.experimental.pallas import tpu as pltpu
from jax.sharding import PartitionSpec as P

H = 12
HD = 64
L = 512
STEP = 5
PAIR = 2 * HD
MIB = 1 << 20

beta_one = 0.5
beta_two = 0.5
adam_epsilon = 1e-08
norm_epsilon = 1e-06
matrix_rate = 0.03
vector_rate = 0.2
weight_decay = 0.01
masked_score = -1e30
low = jnp.bfloat16
full = jnp.float32


def dot_nn(a, b):
    return lax.dot_general(a, b, (((1,), (0,)), ((), ())), preferred_element_type=full)


def dot_nt(a, b):
    return lax.dot_general(a, b, (((1,), (1,)), ((), ())), preferred_element_type=full)


def dot_tn(a, b):
    return lax.dot_general(a, b, (((0,), (0,)), ((), ())), preferred_element_type=full)


def gelu_parts(z):
    size = jnp.abs(z) * 0.7071067811865476
    t = 1.0 / (1.0 + 0.3275911 * size)
    bell = jnp.exp(-0.5 * z * z)
    poly = ((((1.061405429 * t - 1.453152027) * t + 1.421413741) * t - 0.284496736) * t + 0.254829592) * t
    half_tail = 0.5 * poly * bell
    phi = jnp.where(z >= 0, 1.0 - half_tail, half_tail)
    return z * phi, phi + z * bell * 0.3989422804014327


def norm_parts(residual):
    average = jnp.mean(residual, axis=-1, keepdims=True)
    centered = residual - average
    inverse = lax.rsqrt(jnp.mean(centered * centered, axis=-1, keepdims=True) + norm_epsilon)
    return centered * inverse, inverse


def norm_back(upstream, unit, inverse, gain):
    scaled = upstream * gain
    return inverse * (
        scaled
        - jnp.mean(scaled, axis=-1, keepdims=True)
        - unit * jnp.mean(scaled * unit, axis=-1, keepdims=True)
    )


def column_sum(values):
    return jnp.sum(values, axis=0, keepdims=True)


def half_masks(dtype):
    lane = lax.broadcasted_iota(jnp.int32, (1, PAIR), 1)
    first = (lane < HD).astype(full)
    return first.astype(dtype), (1.0 - first).astype(dtype)


def segment_bias(seg_column, seg_row):
    return jnp.where(seg_column == seg_row, 0.0, masked_score)


def flip(index, bit):
    return index + bit * (1 - 2 * lax.rem(lax.div(index, bit), 2))


def place():
    dp = lax.axis_index("dp")
    return dp, lax.axis_index("fsdp"), lax.rem(dp, 2), lax.div(dp, 2)


def greet(partners):
    barrier = pltpu.get_barrier_semaphore()
    for device in partners:
        pl.semaphore_signal(barrier, inc=1, device_id=device, device_id_type=pl.DeviceIdType.MESH)
    pl.semaphore_wait(barrier, len(partners))


def z_partners(count):
    dp, z, _, _ = place()
    return [(dp, lax.rem(z + d, count)) for d in range(1, count)]


def chip_partners():
    dp, z, core, spot = place()
    return [
        (flip(dp, 1), z),
        (2 * flip(spot, 1) + core, z),
        (2 * flip(spot, 2) + core, z),
    ]


def remote(source, target, send, receive, device):
    return pltpu.make_async_remote_copy(
        src_ref=source,
        dst_ref=target,
        send_sem=send,
        recv_sem=receive,
        device_id=device,
        device_id_type=pl.DeviceIdType.MESH,
    )


def fold(piece):
    half = piece.shape[1] // 2
    return jnp.concatenate([piece[:, :half], piece[:, half:]], axis=0)


def unfold(piece):
    rows = piece.shape[0] // 2
    return jnp.concatenate([piece[:rows], piece[rows:]], axis=1)


def sum_scratch(count, part, width, z_count, kind=low):
    piece = (2 * part // z_count, width // 2) if kind == low else (part // z_count, width)
    return [
        pltpu.VMEM((2, 4, part, width), kind),
        pltpu.VMEM((count, 4, part, width), kind),
        pltpu.VMEM((count, 2, part, width), kind),
        pltpu.VMEM((count, part, width), kind),
        pltpu.VMEM((count, z_count) + piece, kind),
        pltpu.VMEM((count, z_count) + piece, kind),
        pltpu.SemaphoreType.DMA((2,)),
        pltpu.SemaphoreType.DMA((count, 2)),
        pltpu.SemaphoreType.DMA((count, 2, 2)),
        pltpu.SemaphoreType.DMA((count, 2)),
        pltpu.SemaphoreType.DMA((count, 2, z_count)),
    ]


SUM_REFS = 11


class BlockSum:
    def __init__(self, sources, refs):
        self.sources = sources
        (self.own, self.c, self.b, self.a, self.zs, self.zr,
         self.own_sem, self.c_sem, self.b_sem, self.a_sem, self.z_sem) = refs
        self.count = self.c.shape[0]
        self.kind = self.c.dtype
        self.z_count = self.zs.shape[1]

    def load(self, i, block):
        core = place()[2]
        slot = lax.rem(i, 2)
        return pltpu.make_async_copy(block.at[:, core], self.own.at[slot], self.own_sem.at[slot])

    def core_copy(self, i, block):
        dp, z, core, _ = place()
        return remote(
            block.at[:, 1 - core], self.c.at[i], self.c_sem.at[i, 0], self.c_sem.at[i, 1], (flip(dp, 1), z)
        )

    def second_copy(self, i, k):
        _, z, core, spot = place()
        other = flip(spot, 2 - core)
        chunk = other if k == 0 else flip(other, 1 + core)
        return remote(
            self.c.at[i, chunk], self.b.at[i, k], self.b_sem.at[i, 0, k], self.b_sem.at[i, 1, k], (2 * other + core, z)
        )

    def third_copy(self, i):
        _, z, core, spot = place()
        other = flip(spot, 1 + core)
        return remote(self.c.at[i, other], self.a.at[i], self.a_sem.at[i, 0], self.a_sem.at[i, 1], (2 * other + core, z))

    def z_copy(self, i, d):
        dp, z, _, _ = place()
        other = lax.rem(z + d, self.z_count)
        return remote(
            self.zs.at[i, other], self.zr.at[i, z], self.z_sem.at[i, 0, d], self.z_sem.at[i, 1, self.z_count - d], (dp, other)
        )

    def open(self, i):
        first = 0
        for source in self.sources:
            count = source.shape[0]

            @pl.when((i >= first) & (i < first + count))
            def _():
                block = source.at[jnp.clip(i - first, 0, count - 1)]
                self.core_copy(i, block).start()
                self.load(i, block).start()

            first += count

    def after_core(self, i):
        block = self.sources[0].at[0]
        self.core_copy(i, block).wait()
        self.load(i, block).wait()
        slot = lax.rem(i, 2)
        for k in range(4):
            self.c[i, k] = (self.c[i, k].astype(full) + self.own[slot, k].astype(full)).astype(self.kind)
        self.second_copy(i, 0).start()
        self.second_copy(i, 1).start()

    def after_second(self, i):
        _, _, core, spot = place()
        other = flip(spot, 1 + core)
        self.second_copy(i, 1).wait()
        self.c[i, other] = (self.c[i, other].astype(full) + self.b[i, 1].astype(full)).astype(self.kind)
        self.third_copy(i).start()
        self.second_copy(i, 0).wait()
        self.c[i, spot] = (self.c[i, spot].astype(full) + self.b[i, 0].astype(full)).astype(self.kind)

    def after_third(self, i):
        _, _, _, spot = place()
        self.third_copy(i).wait()
        total = self.c[i, spot].astype(full) + self.a[i].astype(full)
        rows = total.shape[0] // self.z_count
        for k in range(self.z_count):
            piece = total[k * rows : (k + 1) * rows]
            self.zs[i, k] = fold(piece).astype(low) if self.kind == low else piece
        for d in range(1, self.z_count):
            self.z_copy(i, d).start()

    def finish(self, i):
        z = lax.axis_index("fsdp")
        for d in range(1, self.z_count):
            self.z_copy(i, d).wait()
        total = self.zs[i, z].astype(full)
        for d in range(1, self.z_count):
            total = total + self.zr[i, lax.rem(z + d, self.z_count)].astype(full)
        return total

    def tick(self, t):
        for late, stage in enumerate((self.open, self.after_core, self.after_second, self.after_third)):
            @pl.when((t >= late) & (t < self.count + late))
            def _():
                stage(t - late)


class LineGather:
    def __init__(self, source, target, first, local_sem, sem, z_count):
        self.source = source.at[pl.ds(first, target.shape[1])]
        self.target, self.local_sem, self.sem, self.z_count = target, local_sem, sem, z_count

    def hop_copy(self, hop, way):
        dp, z, _, _ = place()
        if way == 0:
            piece, other, coming = z - hop + 1, z + 1, z - hop
            sends = (piece >= 0) & (other < self.z_count)
            receives = coming >= 0
        else:
            piece, other, coming = z + hop - 1, z - 1, z + hop
            sends = (piece < self.z_count) & (other >= 0)
            receives = coming < self.z_count
        piece = jnp.clip(piece, 0, self.z_count - 1)
        other = jnp.clip(other, 0, self.z_count - 1)
        source = self.source if hop == 1 else self.target.at[piece]
        copy = remote(source, self.target.at[piece], self.sem.at[way, 0, hop - 1], self.sem.at[way, 1, hop - 1], (dp, other))
        return copy, sends, receives

    def local(self):
        return pltpu.make_async_copy(self.source, self.target.at[lax.axis_index("fsdp")], self.local_sem)

    def start(self, hop):
        if hop == 1:
            self.local().start()
        for way in range(2):
            copy, sends, _ = self.hop_copy(hop, way)

            @pl.when(sends)
            def _():
                copy.start()

    def wait(self, hop):
        if hop == 1:
            self.local().wait()
        for way in range(2):
            copy, sends, receives = self.hop_copy(hop, way)

            @pl.when(sends)
            def _():
                copy.wait_send()

            @pl.when(receives)
            def _():
                copy.wait_recv()

    def advance(self, hop):
        if hop > 1:
            self.wait(hop - 1)
        if hop < self.z_count:
            self.start(hop)


def gather_scratch(count, rows, width, z_count, kind=low):
    piece = (2 * rows // z_count, width // 2) if kind == low else (rows // z_count, width)
    return [
        pltpu.VMEM((count, z_count) + piece, kind),
        pltpu.SemaphoreType.DMA((count, 2, z_count)),
        pltpu.SemaphoreType.DMA((count, 2)),
        pltpu.SemaphoreType.DMA((count, 2, 2)),
        pltpu.SemaphoreType.DMA((count, 2, 4)),
    ]


GATHER_REFS = 5


class BlockGather:
    def __init__(self, source, whole, base, refs):
        self.source, self.whole, self.base = source, whole, base
        self.zr, self.z_sem, self.a_sem, self.b_sem, self.c_sem = refs
        self.count, self.z_count = self.zr.shape[0], self.zr.shape[1]
        self.rows = self.whole.shape[1] // (2 * 4)

    def z_copy(self, i, d):
        dp, z, _, _ = place()
        other = lax.rem(z + d, self.z_count)
        return remote(
            self.source.at[i], self.zr.at[i, z], self.z_sem.at[i, 0, d], self.z_sem.at[i, 1, self.z_count - d], (dp, other)
        )

    def chunk(self, i, spot, core):
        start = pl.multiple_of((2 * spot + core) * self.rows, self.rows)
        return self.whole.at[self.base + i, pl.ds(start, self.rows)]

    def first_copy(self, i):
        _, z, core, spot = place()
        return self.one(i, spot, self.a_sem.at[i, 0], self.a_sem.at[i, 1], (2 * flip(spot, 1 + core) + core, z))

    def second_copy(self, i, k):
        _, z, core, spot = place()
        chunk = spot if k == 0 else flip(spot, 1 + core)
        return self.one(
            i, chunk, self.b_sem.at[i, 0, k], self.b_sem.at[i, 1, k], (2 * flip(spot, 2 - core) + core, z)
        )

    def core_copy(self, i, k):
        dp, z, core, spot = place()
        chunk = spot
        if k & 1:
            chunk = flip(chunk, 1 + core)
        if k & 2:
            chunk = flip(chunk, 2 - core)
        return self.one(i, chunk, self.c_sem.at[i, 0, k], self.c_sem.at[i, 1, k], (flip(dp, 1), z))

    def one(self, i, spot, send, receive, device):
        chunk = self.chunk(i, spot, place()[2])
        return remote(chunk, chunk, send, receive, device)

    AHEAD = 2

    def announce(self, i):
        for d in range(1, self.z_count):
            self.z_copy(i, d).start()
        self.zr[i, lax.axis_index("fsdp")] = self.source[i]

    def begin(self):
        for i in range(min(self.AHEAD, self.count)):
            self.announce(i)

    def open(self, i):
        dp = lax.axis_index("dp")
        for d in range(1, self.z_count):
            self.z_copy(i, d).wait()
        pieces = [self.zr[i, k].astype(full) for k in range(self.z_count)]
        if self.zr.dtype == low:
            pieces = [unfold(piece) for piece in pieces]
        start = pl.multiple_of(dp * self.rows, self.rows)
        self.whole[self.base + i, pl.ds(start, self.rows)] = jnp.concatenate(pieces, axis=0).astype(self.whole.dtype)
        self.first_copy(i).start()
        self.second_copy(i, 0).start()
        self.core_copy(i, 0).start()

    def after_first(self, i):
        self.first_copy(i).wait()
        self.second_copy(i, 1).start()
        self.core_copy(i, 1).start()

    def after_second(self, i):
        self.second_copy(i, 0).wait()
        self.core_copy(i, 2).start()
        self.second_copy(i, 1).wait()
        self.core_copy(i, 3).start()

    def close(self, i):
        for k in range(4):
            self.core_copy(i, k).wait()

    def tick(self, t, done=None):
        @pl.when(t + self.AHEAD < self.count)
        def _():
            self.announce(t + self.AHEAD)

        for late, stage in enumerate((self.open, self.after_first, self.after_second, self.close)):
            @pl.when((t >= late) & (t < self.count + late))
            def _():
                stage(t - late)
                if late == 3 and done is not None:
                    done(t - late)


def split_refs(refs, *counts):
    result, start = [], 0
    for count in counts:
        result.append(refs[start : start + count])
        start += count
    return result


class Side:
    def __init__(self, plan, sources, targets, sum_refs, line_refs, own=None):
        self.plan = plan
        sums = plan.sums
        blocks = list(sources[:sums]) + ([own] if plan.own else [])
        self.sum = BlockSum(blocks, sum_refs) if sums else None
        self.result = targets[0] if sums else None
        self.lines = line_gathers(plan.lines, sources[sums:], targets[sums:], line_refs, plan.z_count)

    def enter(self, now):
        if not self.plan.active:
            return

        @pl.when(now)
        def _():
            greet((chip_partners() if self.plan.sums else []) + z_partners(self.plan.z_count))
            for line in self.lines:
                line.advance(1)

    def leave(self, now):
        if not self.plan.active:
            return

        @pl.when(now)
        def _():
            if self.plan.sums:
                for i in range(self.sum.count):
                    self.result[i] = self.sum.finish(i).astype(low)
            for line in self.lines:
                line.advance(self.plan.z_count)

    def advance(self, now, hop):
        if self.lines and hop < self.plan.z_count:
            @pl.when(now)
            def _():
                for line in self.lines:
                    line.advance(hop)


class Plan:
    def __init__(self, pending=None, lines=(), z_count=1, own=0):
        self.z_count = z_count
        self.sums = int(pending is not None)
        self.own = own
        self.lines = [(first, count) for _, first, count in lines]
        self.active = bool(self.sums or lines)
        self.arguments, self.results, self.result_specs, self.scratch = [], [], [], []
        if pending is not None:
            count, part, width = pending.shape[0] + own, pending.shape[3], pending.shape[4]
            self.arguments.append(pending)
            self.results.append(jax.ShapeDtypeStruct((count, 2 * part // z_count, width // 2), low))
            self.result_specs.append(
                pl.BlockSpec(self.results[0].shape, lambda i: (0, 0, 0), pipeline_mode=pl.Buffered(1))
            )
            self.scratch += sum_scratch(count, part, width, z_count)
        for basis, _, count in lines:
            self.arguments.append(basis)
            self.results.append(jax.ShapeDtypeStruct((z_count, count) + basis.shape[1:], low))
            self.result_specs.append(ANYWHERE)
        self.scratch += line_scratch(len(lines), z_count)
        self.argument_specs = [ANYWHERE] * len(self.arguments)

    def split(self, refs, inputs, outputs, scratch):
        extra = self.sums + len(self.lines)
        return split_refs(
            refs, inputs, extra, outputs, extra, scratch, SUM_REFS * self.sums, 2 * bool(self.lines)
        )


def line_scratch(count, z_count):
    if not count:
        return []
    return [pltpu.SemaphoreType.DMA((count,)), pltpu.SemaphoreType.DMA((count, 2, 2, z_count - 1))]


def line_gathers(spans, sources, targets, refs, z_count):
    return [
        LineGather(source, target, first, refs[0].at[n], refs[1].at[n], z_count)
        for n, (source, target, (first, _)) in enumerate(zip(sources, targets, spans))
    ]


ANYWHERE = pl.BlockSpec(memory_space=pl.ANY)
IN_VMEM = pl.BlockSpec(memory_space=pltpu.VMEM)


def forward_kernel(plan, *refs):
    inputs, sources, outputs, targets, scratch, gather_refs, vec_refs, line_refs = plan.split(refs)
    x_ref, segc_ref, segr_ref, vec_ref, w_hbm = inputs
    (q_ref, k_ref, v_ref, ctxt_ref, lse_ref, x1_ref, inv1_ref, n1_ref, u_ref, gp_ref, x2_ref, inv2_ref,
     out_ref) = outputs
    w, bias, vt, n1_all, acc, w_sem = scratch
    s = pl.program_id(0)
    tokens, width = acc.shape
    rows_now = x_ref.shape[0]
    rows = tokens // rows_now
    inner = plan.inner
    local = plan.local
    gather = vec_gather = None
    if plan.gathered:
        w_out, out_sem = targets[0], scratch_tail(plan, refs)
        gather = BlockGather(sources[0], w, local, gather_refs)
        if plan.vectors:
            vec_gather = BlockGather(sources[1], plan.vec_whole(refs), 0, vec_refs)
            vec_ref = targets[1]
    lines = line_gathers(plan.lines, sources[plan.line_at :], targets[plan.line_target_at :], line_refs, plan.z_count)

    def keep(i):
        return pltpu.make_async_copy(w.at[local + i], w_out.at[i], out_sem.at[i])

    def load(j):
        return pltpu.make_async_copy(w_hbm.at[plan.order[j]], w.at[j], w_sem.at[j])

    def arrive(j):
        if j < local:
            load(j).wait()

    def tick(t):
        if gather is not None:
            gather.tick(t, lambda i: keep(i).start())
            if vec_gather is not None:
                vec_gather.tick(t)

    @pl.when(s == 0)
    def _():
        for j in range(local):
            load(j).start()
        if gather is not None:
            greet(chip_partners() + z_partners(plan.z_count))
            if vec_gather is not None:
                vec_gather.begin()
            gather.begin()
            lax.fori_loop(0, plan.lead, lambda t, carry: (tick(t), carry)[1], 0)
            for line in lines:
                line.advance(1)
            if vec_gather is not None:
                turned = vec_gather.whole[0].T
                for layer in range(2):
                    count = plan.vector_rows
                    targets[1 + layer][0:count, :] = turned[layer * count : (layer + 1) * count, :]
        for j in range(min(local, 3)):
            arrive(j)

    @pl.when(s < rows)
    def _():
        xin = x_ref[...].astype(low)
        bias[...] = segment_bias(segc_ref[0], segr_ref[0])
        q_ref[...] = (dot_nn(xin, w[0]) + vec_ref[0:1, :]).astype(low)
        k_ref[...] = dot_nn(xin, w[1]).astype(low)
        value = dot_nn(xin, w[2]) + vec_ref[1:2, :]
        v_ref[...] = value.astype(low)
        vt[...] = value.T.astype(low)
        masks = half_masks(low)
        pairs = width // PAIR

        def pair_step(p, carry):
            lanes = pl.ds(pl.multiple_of(p * PAIR, PAIR), PAIR)
            q_pair = q_ref[:, lanes] * jnp.asarray(HD ** (-0.5), low)
            k_pair = k_ref[:, lanes]
            for h in range(2):
                scores = dot_nt(k_pair, q_pair * masks[h]) + bias[...]
                largest = jnp.max(scores, axis=0, keepdims=True)
                expanded = jnp.exp(scores - largest)
                total = column_sum(expanded)
                here = pl.ds(pl.multiple_of(p * PAIR + h * HD, HD), HD)
                context = dot_nn(vt[here, :], expanded.astype(low)) * (1.0 / total)
                ctxt_ref[here, :] = context.astype(low)
                lse_ref[0, pl.ds(2 * p + h, 1), :] = largest + jnp.log(total)
            if plan.gathered:
                every = plan.every
                @pl.when(lax.rem(p, every) == every - 1)
                def _():
                    tick(plan.lead + (s * pairs + p) // every)
            return carry

        lax.fori_loop(0, pairs, pair_step, 0)

        @pl.when(s == 0)
        def _():
            if local > 3:
                arrive(3)
            for line in lines:
                line.advance(2)

        context = ctxt_ref[...].astype(full).T.astype(low)
        attended = dot_nn(context, w[3]) + vec_ref[2:3, :]
        unit, inverse = norm_parts(x_ref[...].astype(full) + attended)
        x1_ref[...] = unit
        inv1_ref[...] = inverse
        normed = unit * vec_ref[3:4, :] + vec_ref[4:5, :]
        here = pl.ds(pl.multiple_of(s * rows_now, rows_now), rows_now)
        acc[here, :] = normed + vec_ref[5 + inner : 6 + inner, :]
        normed = normed.astype(low)
        n1_ref[...] = normed
        n1_all[here, :] = normed

    tile = tokens // 4
    after = plan.lead + rows * (width // PAIR) // plan.every

    @pl.when(s >= rows)
    def _():
        c = s - rows

        @pl.when(c == 0)
        def _():
            for j in range(4, local):
                arrive(j)
            for line in lines:
                line.advance(3)

        def token_step(i, carry):
            for half in range(2):
                here = pl.ds(pl.multiple_of((2 * i + half) * tile, tile), tile)
                value, slope = gelu_parts(dot_nn(n1_all[here, :], w[4 + 2 * c]) + vec_ref[pl.ds(5 + c, 1), :])
                active = value.astype(low)
                u_ref[here, :] = active
                gp_ref[here, :] = slope.astype(low)
                acc[here, :] += dot_nn(active, w[5 + 2 * c])
            tick(after + 2 * c + i)
            return carry

        lax.fori_loop(0, 2, token_step, 0)

        @pl.when(c == inner - 1)
        def _():
            base = 5 + inner

            def last(i, carry):
                here = pl.ds(pl.multiple_of(i * tile, tile), tile)
                unit, inverse = norm_parts(acc[here, :])
                x2_ref[here, :] = unit
                inv2_ref[here, :] = inverse
                out_ref[here, :] = (
                    unit * vec_ref[base + 1 : base + 2, :] + vec_ref[base + 2 : base + 3, :]
                ).astype(out_ref.dtype)
                return carry

            lax.fori_loop(0, 4, last, 0)
            if gather is not None:
                for t in range(after + 2 * inner, gather.count + 3):
                    tick(t)
                for line in lines:
                    line.advance(plan.z_count)
                for i in range(gather.count):
                    keep(i).wait()


class ForwardPlan:
    def __init__(self, inner, local, shards=None, vec_shard=None, vector_rows=0, lines=(), lead=0, every=1, z_count=1):
        self.inner, self.local, self.lead, self.every, self.z_count = inner, local, lead, every, z_count
        self.vector_rows = vector_rows
        self.order = [0, 1, 2, 3]
        for c in range(inner):
            self.order += [4 + c, 4 + inner + c]
        self.gathered = 0 if shards is None else shards.shape[0]
        self.vectors = vec_shard is not None
        self.lines = [(first, count) for _, first, count in lines]
        self.line_at = int(self.gathered > 0) + int(self.vectors)
        self.line_target_at = int(self.gathered > 0) + 2 * int(self.vectors)
        self.arguments, self.argument_specs, self.results, self.result_specs, self.scratch = [], [], [], [], []
        shape = jax.ShapeDtypeStruct
        if self.gathered:
            width = 2 * shards.shape[2]
            self.arguments.append(shards)
            self.argument_specs.append(IN_VMEM)
            self.results.append(shape((self.gathered, width, width), low))
            self.result_specs.append(ANYWHERE)
            self.scratch += gather_scratch(self.gathered, width // 8, width, z_count)
        if self.vectors:
            rows, lanes = vec_shard.shape[1:]
            self.arguments.append(vec_shard)
            self.argument_specs.append(IN_VMEM)
            for _ in range(2):
                self.results.append(shape((16, width), full))
                self.result_specs.append(pl.BlockSpec((16, width), lambda s: (0, 0)))
            self.scratch += gather_scratch(1, width // 8, lanes, z_count, full)
        for basis, _, count in lines:
            self.arguments.append(basis)
            self.argument_specs.append(ANYWHERE)
            self.results.append(shape((z_count, count) + basis.shape[1:], low))
            self.result_specs.append(ANYWHERE)
        self.scratch += line_scratch(len(lines), z_count)
        if self.gathered:
            self.scratch.append(pltpu.SemaphoreType.DMA((self.gathered,)))
        if self.vectors:
            self.scratch.append(pltpu.VMEM((1, width, lanes), full))

    def split(self, refs):
        return split_refs(
            refs, 5, len(self.arguments), 13, len(self.results), 6, GATHER_REFS * bool(self.gathered),
            GATHER_REFS * self.vectors, 2 * bool(self.lines),
        )

    def vec_whole(self, refs):
        return refs[-1]


def scratch_tail(plan, refs):
    return refs[-2] if plan.vectors else refs[-1]


def forward_layer(hidden, seg_column, seg_row, vectors, weights, out_dtype, plan, identity=None):
    tokens, width = hidden.shape
    inner = plan.inner
    wide = width * inner
    rows = tokens // L
    heads = width // HD
    shape = jax.ShapeDtypeStruct

    def here(s):
        return jnp.minimum(s, rows - 1)

    def column(s):
        return jnp.maximum(s - rows, 0)

    def row_block(columns):
        return pl.BlockSpec((L, columns), lambda s: (here(s), 0))

    def whole(columns):
        return pl.BlockSpec((tokens, columns), lambda s: (0, 0), pipeline_mode=pl.Buffered(1))

    wide_block = pl.BlockSpec((tokens, width), lambda s: (0, column(s)))
    out_shape = (
        shape((tokens, width), low), shape((tokens, width), low), shape((tokens, width), low),
        shape((width, tokens), low), shape((rows, heads, L), full),
        shape((tokens, width), full), shape((tokens, 1), full), shape((tokens, width), low),
        shape((tokens, wide), low), shape((tokens, wide), low),
        shape((tokens, width), full), shape((tokens, 1), full), shape((tokens, width), out_dtype),
        *plan.results,
    )
    out_specs = (
        row_block(width), row_block(width), row_block(width),
        pl.BlockSpec((width, L), lambda s: (0, here(s))), pl.BlockSpec((1, heads, L), lambda s: (here(s), 0, 0)),
        row_block(width), row_block(1), row_block(width),
        wide_block, wide_block,
        whole(width), whole(1), whole(width),
        *plan.result_specs,
    )
    total = 4 + 2 * inner
    held = max(total, plan.local + plan.gathered)
    return pl.pallas_call(
        functools.partial(forward_kernel, plan),
        grid=(rows + inner,),
        out_shape=out_shape,
        in_specs=[
            row_block(width),
            pl.BlockSpec((1, L, 1), lambda s: (here(s), 0, 0)),
            pl.BlockSpec((1, 1, L), lambda s: (here(s), 0, 0)),
            pl.BlockSpec(vectors.shape, lambda s: (0, 0)),
            ANYWHERE,
            *plan.argument_specs,
        ],
        out_specs=out_specs,
        scratch_shapes=[
            pltpu.VMEM((held, width, width), low),
            pltpu.VMEM((L, L), full),
            pltpu.VMEM((width, L), low),
            pltpu.VMEM((tokens, width), low),
            pltpu.VMEM((tokens, width), full),
            pltpu.SemaphoreType.DMA((total,)),
            *plan.scratch,
        ],
        compiler_params=pltpu.CompilerParams(
            dimension_semantics=("arbitrary",), vmem_limit_bytes=62 * MIB,
            collective_id=identity, has_side_effects=identity is not None,
        ),
        cost_estimate=pl.CostEstimate(
            flops=2 * tokens * width * width * total + 4 * tokens * L * width,
            bytes_accessed=40 * MIB,
            transcendentals=tokens * (L * heads + wide),
        ),
        name="layer_forward",
    )(hidden, seg_column, seg_row, vectors, weights, *plan.arguments)


def wide_back_kernel(plan, inner, *refs):
    inputs, sources, outputs, targets, scratch, sum_refs, line_refs = plan.split(refs, 11, 4, 4)
    up_ref, x2_ref, inv2_ref, x1_ref, inv1_ref, n1_ref, vec_ref, wup_ref, wdown_ref, u_ref, gp_ref = inputs
    dw_ref, dr1_ref, da_ref, dvec_ref = outputs
    dy, dn1, n1t, dz = scratch
    c = pl.program_id(0)
    side = Side(plan, sources, targets, sum_refs, line_refs)
    side.enter(c == 0)
    steps = pl.num_programs(0)
    tokens, width = dn1.shape
    tile = tokens // 4
    pick = [slice(i * tile, (i + 1) * tile) for i in range(4)]
    base = 5 + inner

    @pl.when(c == 0)
    def _():
        gain = vec_ref[base + 1 : base + 2, :]

        def body(i, carry):
            gain_sum, shift_sum, bias_sum = carry
            rows = pl.ds(pl.multiple_of(i * tile, tile), tile)
            upstream = up_ref[rows, :].astype(full)
            unit = x2_ref[rows, :]
            back = norm_back(upstream, unit, inv2_ref[rows, :], gain)
            dn1[rows, :] = back
            branch = back.astype(low)
            dy[rows, :] = branch
            return (
                gain_sum + column_sum(upstream * unit),
                shift_sum + column_sum(upstream),
                bias_sum + column_sum(branch.astype(full)),
            )

        zero = jnp.zeros((1, width), full)
        gain_sum, shift_sum, bias_sum = lax.fori_loop(0, 4, body, (zero, zero, zero))
        dvec_ref[...] = jnp.zeros(dvec_ref.shape, full)
        dvec_ref[base : base + 1, :] = bias_sum
        dvec_ref[base + 1 : base + 2, :] = gain_sum
        dvec_ref[base + 2 : base + 3, :] = shift_sum
        n1t[...] = n1_ref[...].astype(full).T.astype(low)

    def token_step(i, carry):
        rows = pl.ds(pl.multiple_of(i * tile, tile), tile)
        slope = gp_ref[rows, :].astype(full)
        piece = (dot_nt(dy[rows, :], wdown_ref[0]) * slope).astype(low)
        dz[rows, :] = piece
        dn1[rows, :] += dot_nt(piece, wup_ref[0])
        side.advance(4 * c + i == 5, 2)
        side.advance(4 * c + i == 10, 3)
        if plan.sums:
            @pl.when(lax.rem(i, 2) == 0)
            def _():
                side.sum.tick(2 * c + lax.div(i, 2))
        return carry + column_sum(piece.astype(full))

    bias_sum = lax.fori_loop(0, 4, token_step, jnp.zeros((1, width), full))
    for j in range(inner):
        @pl.when(c == j)
        def _():
            dvec_ref[5 + j : 6 + j, :] = bias_sum
    dw_ref[0, 0] = dot_nn(n1t[...], dz[...]).astype(low)
    dw_ref[1, 0] = dot_tn(u_ref[...], dy[...]).astype(low)

    @pl.when(c == steps - 1)
    def _():
        gain = vec_ref[3:4, :]

        def body(i, carry):
            gain_sum, shift_sum, bias_sum = carry
            rows = pl.ds(pl.multiple_of(i * tile, tile), tile)
            upstream = dn1[rows, :]
            unit = x1_ref[rows, :]
            back = norm_back(upstream, unit, inv1_ref[rows, :], gain)
            dr1_ref[rows, :] = back
            branch = back.astype(low)
            da_ref[rows, :] = branch
            return (
                gain_sum + column_sum(upstream * unit),
                shift_sum + column_sum(upstream),
                bias_sum + column_sum(branch.astype(full)),
            )

        zero = jnp.zeros((1, width), full)
        gain_sum, shift_sum, bias_sum = lax.fori_loop(0, 4, body, (zero, zero, zero))
        dvec_ref[2:3, :] = bias_sum
        dvec_ref[3:4, :] = gain_sum
        dvec_ref[4:5, :] = shift_sum

    side.leave(c == steps - 1)


def wide_back(upstream, kept, vectors, weights, places, plan, identity=None):
    x1, inv1, n1, u, gp, x2, inv2 = kept
    tokens, width = x1.shape
    up_start, down_start, stride = places
    inner = u.shape[1] // width
    shape = jax.ShapeDtypeStruct

    def whole(array):
        return pl.BlockSpec(array.shape, lambda c: (0, 0), pipeline_mode=pl.Buffered(1))

    return pl.pallas_call(
        functools.partial(wide_back_kernel, plan, inner),
        grid=(inner,),
        out_shape=(
            shape((2, inner, width, width), low),
            shape((tokens, width), full), shape((tokens, width), low), shape((16, width), full),
            *plan.results,
        ),
        in_specs=[
            whole(upstream), whole(x2), whole(inv2), whole(x1), whole(inv1), whole(n1), whole(vectors),
            pl.BlockSpec((1, width, width), lambda c: (up_start + stride * c, 0, 0)),
            pl.BlockSpec((1, width, width), lambda c: (down_start + stride * c, 0, 0)),
            pl.BlockSpec((tokens, width), lambda c: (0, c)),
            pl.BlockSpec((tokens, width), lambda c: (0, c)),
            *plan.argument_specs,
        ],
        out_specs=(
            pl.BlockSpec((2, 1, width, width), lambda c: (0, c, 0, 0)),
            pl.BlockSpec((tokens, width), lambda c: (0, 0), pipeline_mode=pl.Buffered(1)),
            pl.BlockSpec((tokens, width), lambda c: (0, 0), pipeline_mode=pl.Buffered(1)),
            pl.BlockSpec((16, width), lambda c: (0, 0)),
            *plan.result_specs,
        ),
        scratch_shapes=[
            pltpu.VMEM((tokens, width), low),
            pltpu.VMEM((tokens, width), full),
            pltpu.VMEM((width, tokens), low),
            pltpu.VMEM((tokens, width), low),
            *plan.scratch,
        ],
        compiler_params=pltpu.CompilerParams(
            dimension_semantics=("arbitrary",), vmem_limit_bytes=60 * MIB,
            collective_id=identity, has_side_effects=identity is not None,
        ),
        cost_estimate=pl.CostEstimate(
            flops=8 * tokens * width * width * inner, bytes_accessed=50 * MIB, transcendentals=0
        ),
        name="wide_backward",
    )(upstream, x2, inv2, x1, inv1, n1, vectors, weights, weights, u, gp, *plan.arguments)


def attend_back_kernel(plan, *refs):
    inputs, sources, outputs, targets, scratch, sum_refs, line_refs = plan.split(refs, 11, 3, 10)
    da_ref, dr1_ref, x_ref, q_ref, k_ref, v_ref, ctxt_ref, lse_ref, segc_ref, segr_ref, w_ref = inputs
    dw_ref, dx_ref, dvec_ref = outputs
    bias, dctx, kt, delta, dqt, xt, dq_all, dk_all, dv_all, dwo = scratch
    r = pl.program_id(0)
    side = Side(plan, sources, targets, sum_refs, line_refs, dwo)
    side.enter(r == 0)
    tokens, width = dr1_ref.shape
    pairs = width // PAIR
    ticks = pairs + 2

    def tick(n):
        if plan.sums:
            side.sum.tick(r * ticks + n)

    tick(0)
    here = pl.ds(pl.multiple_of(r * tokens, tokens), tokens)

    @pl.when(r == 0)
    def _():
        grad = dot_nn(ctxt_ref[...], da_ref[...]).astype(low)
        if plan.own:
            dwo[0] = grad.reshape(dwo.shape[1:])
        else:
            dw_ref[3] = grad

    xt[:, here] = x_ref[...].astype(low).astype(full).T.astype(low)
    bias[...] = segment_bias(segc_ref[0], segr_ref[0])
    context_grad = dot_nt(da_ref[here, :], w_ref[3]).astype(low)
    dctx[...] = context_grad
    kt[...] = k_ref[...].astype(full).T.astype(low)
    products = context_grad.astype(full) * ctxt_ref[:, here].astype(full).T
    feature = lax.broadcasted_iota(jnp.int32, (16, width), 1)
    head = lax.broadcasted_iota(jnp.int32, (16, width), 0)
    member = ((feature >= head * HD) & (feature < (head + 1) * HD)).astype(full).astype(low)
    high = products.astype(low)
    rest = (products - high.astype(full)).astype(low)
    delta[...] = dot_nt(member, high) + dot_nt(member, rest)
    masks = half_masks(low)
    scale = HD ** (-0.5)

    def pair_step(p, carry):
        lanes = pl.ds(pl.multiple_of(p * PAIR, PAIR), PAIR)
        q_pair = q_ref[:, lanes] * jnp.asarray(scale, low)
        k_pair = k_ref[:, lanes]
        v_pair = v_ref[:, lanes]
        g_pair = dctx[:, lanes]
        key_grad = jnp.zeros((tokens, PAIR), full)
        value_grad = jnp.zeros((tokens, PAIR), full)
        for h in range(2):
            q_half = q_pair * masks[h]
            g_half = g_pair * masks[h]
            scores = dot_nt(k_pair, q_half) + bias[...]
            attention = jnp.exp(scores - lse_ref[0, pl.ds(2 * p + h, 1), :])
            value_grad = value_grad + dot_nn(attention.astype(low), g_half)
            attention_grad = dot_nt(v_pair, g_half)
            score_grad = (attention * (attention_grad - delta[pl.ds(2 * p + h, 1), :])).astype(low)
            key_grad = key_grad + dot_nn(score_grad, q_half)
            rows = pl.ds(pl.multiple_of(p * PAIR + h * HD, HD), HD)
            dqt[rows, :] = dot_nn(kt[rows, :], score_grad) * scale
        dk_all[here, lanes] = key_grad.astype(low)
        dv_all[here, lanes] = value_grad.astype(low)
        tick(1 + p)
        side.advance((r == 0) & (p == 4), 2)
        side.advance((r == 1) & (p == 3), 3)
        return carry

    lax.fori_loop(0, pairs, pair_step, 0)
    tick(1 + pairs)
    query_grad = dqt[...].T.astype(low)
    dq_all[here, :] = query_grad
    key_grad = dk_all[here, :]
    value_grad = dv_all[here, :]
    dx_ref[...] = (
        dr1_ref[...]
        + dot_nt(query_grad, w_ref[0])
        + dot_nt(key_grad, w_ref[1])
        + dot_nt(value_grad, w_ref[2])
    )

    @pl.when(r == 0)
    def _():
        dvec_ref[...] = jnp.zeros(dvec_ref.shape, full)

    dvec_ref[0:1, :] += column_sum(query_grad.astype(full))
    dvec_ref[1:2, :] += column_sum(value_grad.astype(full))

    @pl.when(r == pl.num_programs(0) - 1)
    def _():
        for j, grad in enumerate((dq_all, dk_all, dv_all)):
            dw_ref[j] = dot_nn(xt[...], grad[...]).astype(low)

    side.leave(r == pl.num_programs(0) - 1)


def attend_back(da, dr1, hidden, kept, seg_column, seg_row, weights, start, plan, identity=None):
    q, k, v, ctxt, lse = kept
    tokens, width = da.shape
    rows = tokens // L
    heads = width // HD
    shape = jax.ShapeDtypeStruct

    def row_block():
        return pl.BlockSpec((L, width), lambda r: (r, 0))

    return pl.pallas_call(
        functools.partial(attend_back_kernel, plan),
        grid=(rows,),
        out_shape=(
            shape((4 - plan.own, width, width), low), shape((tokens, width), full), shape((8, width), full),
            *plan.results,
        ),
        in_specs=[
            pl.BlockSpec((tokens, width), lambda r: (0, 0), pipeline_mode=pl.Buffered(1)),
            row_block(), row_block(), row_block(), row_block(), row_block(),
            pl.BlockSpec((width, tokens), lambda r: (0, 0), pipeline_mode=pl.Buffered(1)),
            pl.BlockSpec((1, heads, L), lambda r: (r, 0, 0)),
            pl.BlockSpec((1, L, 1), lambda r: (r, 0, 0)),
            pl.BlockSpec((1, 1, L), lambda r: (r, 0, 0)),
            pl.BlockSpec((4, width, width), lambda r: (start, 0, 0), pipeline_mode=pl.Buffered(1)),
            *plan.argument_specs,
        ],
        out_specs=(
            pl.BlockSpec((4 - plan.own, width, width), lambda r: (0, 0, 0), pipeline_mode=pl.Buffered(1)),
            row_block(),
            pl.BlockSpec((8, width), lambda r: (0, 0)),
            *plan.result_specs,
        ),
        scratch_shapes=[
            pltpu.VMEM((L, L), full),
            pltpu.VMEM((L, width), low),
            pltpu.VMEM((width, L), low),
            pltpu.VMEM((16, L), full),
            pltpu.VMEM((width, L), full),
            pltpu.VMEM((width, tokens), low),
            pltpu.VMEM((tokens, width), low),
            pltpu.VMEM((tokens, width), low),
            pltpu.VMEM((tokens, width), low),
            pltpu.VMEM((1, 4, 2, width // 8, width) if plan.own else (8, 128), low),
            *plan.scratch,
        ],
        compiler_params=pltpu.CompilerParams(
            dimension_semantics=("arbitrary",), vmem_limit_bytes=60 * MIB,
            collective_id=identity, has_side_effects=identity is not None,
        ),
        cost_estimate=pl.CostEstimate(
            flops=16 * tokens * width * width + 10 * tokens * L * width,
            bytes_accessed=30 * MIB,
            transcendentals=tokens * L * heads,
        ),
        name="attend_backward",
    )(da, dr1, hidden, q, k, v, ctxt, lse, seg_column, seg_row, weights, *plan.arguments)


def moments(rotated, first, second):
    first_new = beta_one * first + (1.0 - beta_one) * rotated
    second_new = beta_two * second + (1.0 - beta_two) * rotated * rotated
    direction = (
        first_new
        / (1.0 - beta_one**STEP)
        / (jnp.sqrt(second_new / (1.0 - beta_two**STEP)) + adam_epsilon)
    )
    return first_new, second_new, direction


def pack_lanes(piece):
    rows = piece.shape[0] // 2
    return jnp.concatenate([piece[:rows], piece[rows:]], axis=1)


def unpack_lanes(piece):
    columns = piece.shape[1] // 2
    return jnp.concatenate([piece[:, :columns], piece[:, columns:]], axis=0)


def optimizer_kernel(plan, *refs):
    inputs, ready, dvecs, bases, lines_in, outputs, lines_out, scratch, sum_refs, vec_refs, line_refs = split_refs(
        refs, 6, plan.ready, plan.dvecs, plan.bases, len(plan.spans), 5, len(plan.spans), 21, SUM_REFS, SUM_REFS,
        2 * bool(plan.spans),
    )
    index_ref, place_ref, tail_hbm, first_hbm, second_hbm, blocks = inputs
    new_ref, low_ref, first_out, second_out, vec_out = outputs
    (store, left, right, first_in, second_in, g_out, g_in, t_out, t_in, e_out, e_in, w_out, w_in, vec_source,
     load_sem, g_sem, t_sem, e_sem, w_sem, left_sem, right_sem) = scratch
    dp, z, core, spot = place()
    slots, owners = g_in.shape[0], g_in.shape[1]
    z_count = t_in.shape[1]
    count = blocks.shape[0]
    tail = BlockSum([tail_hbm], sum_refs)
    vec = BlockSum([vec_source], vec_refs)
    greet([(lax.rem(dp + d, owners), z) for d in range(1, owners)] + z_partners(z_count))
    lines = line_gathers(plan.spans, lines_in, lines_out, line_refs, z_count)
    for line in lines:
        line.advance(1)
    every = list(bases) + list(lines_out)
    tail.tick(0)
    rows = plan.vector_rows
    stacked = jnp.concatenate(
        [dvecs[0][0:2, :], dvecs[1][2:rows, :], dvecs[2][0:2, :], dvecs[3][2:rows, :],
         jnp.zeros((vec_source.shape[-1] - 2 * rows, blocks.shape[2]), full)], axis=0
    )
    vec_source[0] = stacked.T.reshape(vec_source.shape[1:])

    def load(refs_map, target, sem, s):
        n, at = refs_map[s]
        return pltpu.make_async_copy(every[n].at[:, at], target.at[:, s], sem.at[s])

    def load_first(s):
        return pltpu.make_async_copy(first_hbm.at[s], first_in.at[s], load_sem.at[0, s])

    def load_second(s):
        return pltpu.make_async_copy(second_hbm.at[s], second_in.at[s], load_sem.at[1, s])

    early = [s for s in range(slots) if plan.left_map[s][0] < len(bases)]
    for s in range(slots):
        load(plan.right_map, right, right_sem, s).start()
        load_first(s).start()
        load_second(s).start()
        if s in early:
            load(plan.left_map, left, left_sem, s).start()

    def sum_step(t, carry):
        tail.tick(t)
        vec.tick(t - 1)
        return carry

    lax.fori_loop(1, 4, sum_step, 0)
    for line in lines:
        line.advance(2)
    lax.fori_loop(4, tail.count + 4, sum_step, 0)
    start = tail.count
    for part in ready:
        store[start : start + part.shape[0]] = part[...]
        start += part.shape[0]
    store[count] = jnp.zeros(store.shape[1:], low)
    for i in range(tail.count):
        store[i] = tail.finish(i).astype(low)

    def g_copy(s, d):
        other = lax.rem(dp + d, owners)
        return remote(g_out.at[s, d], g_in.at[s, dp], g_sem.at[0, s, d], g_sem.at[1, s, owners - d], (other, z))

    def t_copy(s, d):
        other = lax.rem(z + d, z_count)
        return remote(t_out.at[s, d], t_in.at[s, z], t_sem.at[0, s, d], t_sem.at[1, s, z_count - d], (dp, other))

    def e_copy(s, d):
        other = lax.rem(z + d, z_count)
        return remote(e_out.at[s, d], e_in.at[s, z], e_sem.at[0, s, d], e_sem.at[1, s, z_count - d], (dp, other))

    def w_copy(s, d):
        other = lax.rem(dp + d, owners)
        return remote(
            w_out.at[s, other], w_in.at[s * owners + dp], w_sem.at[0, s, d], w_sem.at[1, s, owners - d], (other, z)
        )

    def send_out(s):
        for d in range(1, owners):
            g_out[s, d] = store[index_ref[s * owners + lax.rem(dp + d, owners)]]
            g_copy(s, d).start()
        g_in[s, dp] = store[index_ref[s * owners + dp]]

    def turn(s):
        for d in range(1, owners):
            g_copy(s, d).wait()
        if s + 2 < slots:
            send_out(s + 2)
        load(plan.right_map, right, right_sem, s).wait()
        grad = jnp.concatenate([unfold(g_in[s, c].astype(full)) for c in range(owners)], axis=0).astype(low)
        for d in range(1, z_count):
            t_out[s, d] = pack_lanes(dot_nt(right[lax.rem(z + d, z_count), s], grad)).astype(low)
            t_copy(s, d).start()
        t_in[s, z] = pack_lanes(dot_nt(right[z, s], grad)).astype(low)

    def adapt(s):
        for d in range(1, z_count):
            t_copy(s, d).wait()
        load_first(s).wait()
        load_second(s).wait()
        load(plan.left_map, left, left_sem, s).wait()
        rotated = jnp.zeros(first_in.shape[1:], full)
        for f in range(z_count):
            rotated = rotated + dot_nn(unpack_lanes(t_in[s, f].astype(full)).astype(low), left[f, s])
        first_new, second_new, direction = moments(rotated, first_in[s], second_in[s])
        first_out[s] = first_new
        second_out[s] = second_new
        direction = direction.astype(low)
        for d in range(1, z_count):
            e_out[s, d] = pack_lanes(dot_nt(left[lax.rem(z + d, z_count), s], direction)).astype(low)
            e_copy(s, d).start()
        e_in[s, z] = pack_lanes(dot_nt(left[z, s], direction)).astype(low)

    def step_back(s):
        for d in range(1, z_count):
            e_copy(s, d).wait()
        step = jnp.zeros((left.shape[2], left.shape[3]), full)
        for f in range(z_count):
            step = step + dot_nn(unpack_lanes(e_in[s, f].astype(full)).astype(low), right[f, s])
        share = step.shape[0] // owners
        for c in range(owners):
            w_out[s, c] = fold(step[c * share : (c + 1) * share]).astype(low)
        for d in range(1, owners):
            w_copy(s, d).start()
        w_in[s * owners + dp] = w_out[s, dp]

    send_out(0)
    send_out(1)
    for hop in range(3, z_count):
        for line in lines:
            line.advance(hop)
    for k in range(slots + 2):
        if k == 3:
            for line in lines:
                line.advance(z_count)
            for s in range(slots):
                if s not in early:
                    load(plan.left_map, left, left_sem, s).start()
        if k < slots:
            turn(k)
        if 0 <= k - 1 < slots:
            adapt(k - 1)
        if 0 <= k - 2 < slots:
            step_back(k - 2)

    vec_out[...] = vec.finish(0)
    for s in range(slots):
        for d in range(1, owners):
            w_copy(s, d).wait()

    def block_step(b, carry):
        step = unfold(w_in[place_ref[b]].astype(full))
        block = blocks[b]
        new = block - matrix_rate * (step + weight_decay * block)
        new_ref[b] = new
        low_ref[b] = new.astype(low)
        return carry

    lax.fori_loop(0, count, block_step, 0)


class OptimizerPlan:
    def __init__(self, ready, dvecs, bases, spans, left_map, right_map, vector_rows):
        self.ready, self.dvecs, self.bases, self.spans = ready, dvecs, bases, spans
        self.left_map, self.right_map, self.vector_rows = left_map, right_map, vector_rows


def optimizer(
    index, places, tail, ready, dvecs, vector_rows, bases, lines, left_map, right_map, first, second, blocks, z_count,
    identity,
):
    slots, columns, width = first.shape
    owners = index.shape[0] // slots
    count, rows = blocks.shape[0], blocks.shape[1]
    span = bases[0].shape[2]
    lanes = 128
    shape = jax.ShapeDtypeStruct
    piece = (2 * rows, width // 2)
    tile = (span // 2, 2 * columns)
    smem = pl.BlockSpec(memory_space=pltpu.SMEM)
    plan = OptimizerPlan(
        len(ready), len(dvecs), len(bases), [(first_slot, amount) for _, first_slot, amount in lines],
        left_map, right_map, vector_rows,
    )
    line_shapes = [shape((z_count, amount) + basis.shape[1:], low) for basis, _, amount in lines]
    return pl.pallas_call(
        functools.partial(optimizer_kernel, plan),
        out_shape=(
            shape(blocks.shape, full), shape(blocks.shape, low), shape(first.shape, full), shape(first.shape, full),
            shape((rows, lanes), full), *line_shapes,
        ),
        in_specs=[smem, smem, ANYWHERE, ANYWHERE, ANYWHERE, IN_VMEM]
        + [IN_VMEM] * (len(ready) + len(dvecs)) + [ANYWHERE] * (len(bases) + len(lines)),
        out_specs=(IN_VMEM,) * 5 + (ANYWHERE,) * len(lines),
        scratch_shapes=[
            pltpu.VMEM((count + 1,) + piece, low),
            pltpu.VMEM((z_count, slots, span, width), low),
            pltpu.VMEM((z_count, slots, columns, width), low),
            pltpu.VMEM((slots, columns, width), full),
            pltpu.VMEM((slots, columns, width), full),
            pltpu.VMEM((slots, owners) + piece, low),
            pltpu.VMEM((slots, owners) + piece, low),
            pltpu.VMEM((slots, z_count) + tile, low),
            pltpu.VMEM((slots, z_count) + tile, low),
            pltpu.VMEM((slots, z_count) + tile, low),
            pltpu.VMEM((slots, z_count) + tile, low),
            pltpu.VMEM((slots, owners) + piece, low),
            pltpu.VMEM((slots * owners,) + piece, low),
            pltpu.VMEM((1, owners // 2, 2, width // owners, lanes), full),
            pltpu.SemaphoreType.DMA((2, slots)),
            pltpu.SemaphoreType.DMA((2, slots, owners)),
            pltpu.SemaphoreType.DMA((2, slots, z_count)),
            pltpu.SemaphoreType.DMA((2, slots, z_count)),
            pltpu.SemaphoreType.DMA((2, slots, owners)),
            pltpu.SemaphoreType.DMA((slots,)),
            pltpu.SemaphoreType.DMA((slots,)),
            *sum_scratch(tail.shape[0], tail.shape[3], width, z_count),
            *sum_scratch(1, width // owners, lanes, z_count, full),
            *line_scratch(len(lines), z_count),
        ],
        compiler_params=pltpu.CompilerParams(
            vmem_limit_bytes=60 * MIB, collective_id=identity, has_side_effects=True
        ),
        cost_estimate=pl.CostEstimate(
            flops=8 * slots * span * width * width, bytes_accessed=40 * MIB, transcendentals=slots * width * columns
        ),
        name="optimizer",
    )(index, places, tail, first, second, blocks, *ready, *dvecs, *bases, *[basis for basis, _, _ in lines])


def slot_table(owner, slots, owner_rows):
    block_count = owner.shape[0]
    same_owner = owner[:, None] == owner[None, :]
    ordering = jnp.arange(block_count, dtype=jnp.int32)
    earlier = ordering[None, :] < ordering[:, None]
    ranking = jnp.sum(jnp.where(same_owner & earlier, 1, 0), axis=1).astype(jnp.int32)
    owner_match = owner[None, :] == jnp.arange(owner_rows, dtype=jnp.int32)[:, None]
    slot_match = ranking[None, :] == jnp.arange(slots, dtype=jnp.int32)[:, None]
    return jnp.where(slot_match[:, None, :] & owner_match[None, :, :], 1.0, 0.0).astype(full)


def scatter_sum(grads):
    blocks, width = grads.shape[0], grads.shape[2]
    cut = grads.reshape(blocks, lax.axis_size("dp"), -1, width).transpose(1, 0, 2, 3)
    outer = lax.psum_scatter(cut, "dp", scatter_dimension=0, tiled=False)
    blocks, rows, width = outer.shape
    count = lax.axis_size("fsdp")
    cut = outer.reshape(blocks, count, rows // count, width).transpose(1, 0, 2, 3)
    return lax.psum_scatter(cut, "fsdp", scatter_dimension=0, tiled=False)


def scatter_vectors(grads):
    rows, width = grads.shape
    count = lax.axis_size("dp") * lax.axis_size("fsdp")
    cut = grads.reshape(rows, count, width // count).transpose(1, 0, 2)
    return lax.psum_scatter(cut, ("dp", "fsdp"), scatter_dimension=0, tiled=False)


def gathering_program(
    tokens, segment, blocks, vectors, owner, left_basis, right_basis, rot_first, rot_second, cotangent, z_count
):
    layers, vector_rows = vectors.shape[:2]
    count, shard_rows, width = blocks.shape
    per_layer = count // layers
    inner = (per_layer - 4) // 2
    owners = lax.axis_size("dp")
    slots = rot_first.shape[0]
    part = width // owners
    lanes = 128
    seg_column, seg_row = segment[:, :, None], segment[:, None, :]

    order = [0, 1, 2, 3]
    for c in range(inner):
        order += [4 + c, 4 + inner + c]
    folded = blocks.astype(low).reshape(count, shard_rows, 2, width // 2).transpose(0, 2, 1, 3)
    folded = folded.reshape(count, 2 * shard_rows, width // 2)

    def pick(numbers):
        return jnp.stack([folded[j] for j in numbers])

    head = pick(order + [per_layer + j for j in order[:4]])
    rest = pick([per_layer + j for j in order[4:]])
    vec_shard = vectors.astype(low).astype(full).reshape(layers * vector_rows, shard_rows).T
    vec_shard = jnp.pad(vec_shard, ((0, 0), (0, lanes - layers * vector_rows)))[None]
    left_low = left_basis.reshape(slots, -1, width).astype(low)
    right_low = right_basis.transpose(0, 2, 1).astype(low)

    plan = ForwardPlan(
        inner, 0, head, vec_shard, vector_rows, [(right_low, 0, 2)], lead=6, every=3, z_count=z_count
    )
    empty_vec = jnp.zeros((16, width), full)
    results = forward_layer(tokens, seg_column, seg_row, empty_vec, head, full, plan, 6)
    kept_a = results[:12]
    hidden, weights_a, vec_a, vec_b, right_01 = results[12:]
    plan = ForwardPlan(inner, 4, rest, lines=[(right_low, 2, 1)], lead=0, every=2, z_count=z_count)
    plan.order = [per_layer + j for j in range(4)]
    results = forward_layer(hidden, seg_column, seg_row, vec_b, weights_a, low, plan, 7)
    kept_b = results[:12]
    layer_out, weights_b, right_2 = results[12:]

    def cut(grads):
        return grads.reshape(-1, owners // 2, 2, part, width)

    plan = Plan(None, [(right_low, 3, 2)], z_count)
    dw_wide, dr1, da, dvec_wide_b, right_34 = wide_back(
        cotangent, kept_b[5:], vec_b, weights_b, (0, 1, 2), plan, 1
    )
    plan = Plan(cut(dw_wide), [(left_low, 0, 1)], z_count, 1)
    dw_attend, upstream, dvec_attend_b, sum_b, left_0 = attend_back(
        da, dr1, hidden, kept_b[:5], seg_column, seg_row, weights_a, per_layer // 4, plan, 2
    )
    plan = Plan(cut(dw_attend), [(left_low, 1, 1)], z_count)
    dw_wide, dr1, da, dvec_wide_a, attend_sum_b, left_1 = wide_back(
        upstream, kept_a[5:], vec_a, weights_a, (4, 5, 2), plan, 3
    )
    plan = Plan(cut(dw_wide), [(left_low, 2, 1)], z_count, 1)
    dw_attend, upstream, dvec_attend_a, sum_a, left_2 = attend_back(
        da, dr1, tokens, kept_a[:5], seg_column, seg_row, weights_a, 0, plan, 5
    )

    three = list(range(3))
    wide_blocks = list(range(4, per_layer)) + [3]
    held_order = three + wide_blocks + [per_layer + j for j in three + wide_blocks]
    rank = jnp.asarray([held_order.index(j) for j in range(count)], jnp.int32)
    table = slot_table(owner, slots, owners).reshape(slots * owners, count)
    held = jnp.sum(table, axis=1)
    index = jnp.where(held > 0, jnp.sum(table * rank, axis=1), count).astype(jnp.int32)
    places = jnp.sum(table * jnp.arange(slots * owners, dtype=jnp.int32)[:, None], axis=0).astype(jnp.int32)
    bases = (right_01, right_2, right_34, left_0, left_1, left_2)
    right_map = [(0, 0), (0, 1), (1, 0), (2, 0), (2, 1)]
    left_map = [(3, 0), (4, 0), (5, 0), (6, 0), (6, 1)]
    new_blocks, new_low, first_new, second_new, vec_sum, _ = optimizer(
        index, places, cut(dw_attend), (sum_a, attend_sum_b, sum_b),
        (dvec_attend_a, dvec_wide_a, dvec_attend_b, dvec_wide_b), vector_rows, bases, [(left_low, 3, 2)], left_map, right_map,
        rot_first.transpose(0, 2, 1), rot_second.transpose(0, 2, 1), blocks, z_count, 4,
    )
    first_new, second_new = first_new.transpose(0, 2, 1), second_new.transpose(0, 2, 1)
    vector_grad = vec_sum[:, : layers * vector_rows].T.reshape(layers, vector_rows, shard_rows)
    return layer_out, upstream, new_blocks, new_low, first_new, second_new, vector_grad


def plain_program(
    tokens, segment, blocks, vectors, owner, left_basis, right_basis, rot_first, rot_second, cotangent
):
    layers, vector_rows = vectors.shape[:2]
    per_layer = blocks.shape[0] // layers
    inner = (per_layer - 4) // 2
    width = blocks.shape[2]
    owner_rows = lax.axis_size("dp")
    slots = rot_first.shape[0]
    selector = slot_table(owner, slots, owner_rows)
    vector_parts = lax.all_gather(vectors.astype(low), ("dp", "fsdp"), axis=0, tiled=False)
    vector_full = vector_parts.transpose(1, 2, 0, 3).reshape(layers, vector_rows, width).astype(full)
    blocks_low, vector_full = lax.optimization_barrier((blocks.astype(low), vector_full))

    seg_column = segment[:, :, None]
    seg_row = segment[:, None, :]
    state = tokens
    kept = []
    for layer_index in range(layers):
        start = per_layer * layer_index
        weights = lax.all_gather(blocks_low[start : start + per_layer], ("dp", "fsdp"), axis=1, tiled=True)
        out_dtype = low if layer_index == layers - 1 else full
        results = forward_layer(
            state, seg_column, seg_row, vector_full[layer_index], weights, out_dtype, ForwardPlan(inner, per_layer)
        )
        kept.append((state, weights, results[:5], results[5:12]))
        state = results[12]
    layer_out = state
    upstream = cotangent
    right_low = lax.all_gather(right_basis.astype(low), "fsdp", axis=2, tiled=True)
    block_shards = [None] * layers
    vector_shards = [None] * layers
    for layer_index in reversed(range(layers)):
        hidden, weights, attend_kept, wide_kept = kept[layer_index]
        dw_wide, dr1, da, dvec_wide = wide_back(
            upstream, wide_kept, vector_full[layer_index], weights, (4, 4 + inner, 1), Plan()
        )
        wide_shard = scatter_sum(dw_wide.reshape(-1, width, width))
        dw_attend, upstream, dvec_attend = attend_back(
            da, dr1, hidden, attend_kept, seg_column, seg_row, weights, 0, Plan()
        )
        dvec = jnp.concatenate([dvec_attend[:2], dvec_wide[2:vector_rows]], axis=0)
        block_shards[layer_index] = jnp.concatenate([scatter_sum(dw_attend), wide_shard], axis=0)
        vector_shards[layer_index] = scatter_vectors(dvec)
    vector_grad = jnp.stack(vector_shards)
    block_grad = jnp.concatenate(block_shards, axis=0)
    outgoing = jnp.einsum("srk,kid->srid", selector.astype(low), block_grad, preferred_element_type=full)
    incoming = lax.all_to_all(outgoing.astype(low), "dp", split_axis=1, concat_axis=1, tiled=True)
    owned = incoming.reshape(slots, -1, width)
    turned = jnp.einsum("sik,skj->sij", owned, right_low, preferred_element_type=full).astype(low)
    left_rows = left_basis.reshape(slots, -1, width).astype(low)
    partial_sums = jnp.einsum("sra,srb->sab", left_rows, turned, preferred_element_type=full)
    rotated = lax.psum_scatter(
        partial_sums.astype(low), "fsdp", scatter_dimension=2, tiled=True
    ).astype(full)
    first_new, second_new, direction = moments(rotated, rot_first, rot_second)
    direction_full = lax.all_gather(direction.astype(low), "fsdp", axis=2, tiled=True)
    back_right = jnp.einsum("sab,scb->sac", direction_full, right_low, preferred_element_type=full)
    step_rows = jnp.einsum(
        "sia,sac->sic", left_rows, back_right.astype(low), preferred_element_type=full
    )
    returned = lax.all_to_all(
        step_rows.reshape(slots, owner_rows, -1, width).astype(low),
        "dp",
        split_axis=1,
        concat_axis=1,
        tiled=True,
    )
    step_shard = jnp.einsum("srk,srid->kid", selector.astype(low), returned, preferred_element_type=full)
    new_blocks = blocks - matrix_rate * (step_shard + weight_decay * blocks)
    return layer_out, upstream, new_blocks, new_blocks.astype(low), first_new, second_new, vector_grad


def shards(
    tokens,
    segment,
    blocks,
    vectors,
    owner,
    left_basis,
    right_basis,
    rot_first,
    rot_second,
    vec_first,
    vec_second,
    cotangent,
):
    operands = (
        tokens, segment, blocks, vectors, owner, left_basis, right_basis, rot_first, rot_second, cotangent
    )
    z_count = lax.axis_size("fsdp")
    if lax.axis_size("dp") == 8 and z_count == 4:
        results = gathering_program(*operands, z_count)
    else:
        results = plain_program(*operands)
    layer_out, upstream, new_blocks, new_low, first_new, second_new, vector_grad = results
    vector_first = beta_one * vec_first + (1.0 - beta_one) * vector_grad
    vector_second = beta_two * vec_second + (1.0 - beta_two) * vector_grad * vector_grad
    vector_step = (
        vector_first
        / (1.0 - beta_one**STEP)
        / (jnp.sqrt(vector_second / (1.0 - beta_two**STEP)) + adam_epsilon)
    )
    vector_new = vectors - vector_rate * (vector_step + weight_decay * vectors)
    return (
        layer_out,
        upstream,
        new_blocks,
        new_low,
        first_new,
        second_new,
        vector_first,
        vector_second,
        vector_new,
    )


def solution(mesh):
    return jax.shard_map(
        shards,
        mesh=mesh,
        in_specs=(
            P(("dp", "fsdp"), None),
            P(("dp", "fsdp"), None),
            P(None, ("dp", "fsdp"), None),
            P(None, None, ("dp", "fsdp")),
            P(),
            P("dp", None, "fsdp", None),
            P("dp", None, "fsdp"),
            P("dp", None, "fsdp"),
            P("dp", None, "fsdp"),
            P(None, None, ("dp", "fsdp")),
            P(None, None, ("dp", "fsdp")),
            P(("dp", "fsdp"), None),
        ),
        out_specs=(
            P(("dp", "fsdp"), None),
            P(("dp", "fsdp"), None),
            P(None, ("dp", "fsdp"), None),
            P(None, ("dp", "fsdp"), None),
            P("dp", None, "fsdp"),
            P("dp", None, "fsdp"),
            P(None, None, ("dp", "fsdp")),
            P(None, None, ("dp", "fsdp")),
            P(None, None, ("dp", "fsdp")),
        ),
        check_vma=False,
    )
```

```python
import functools

import jax
import jax.numpy as jnp
from jax import lax
from jax.experimental import pallas as pl
from jax.experimental.pallas import tpu as pltpu
from jax.sharding import PartitionSpec as P

H = 12
HD = 64
L = 512
STEP = 5
PAIR = 2 * HD
MIB = 1 << 20

beta_one = 0.5
beta_two = 0.5
adam_epsilon = 1e-08
norm_epsilon = 1e-06
matrix_rate = 0.03
vector_rate = 0.2
weight_decay = 0.01
masked_score = -1e30
low = jnp.bfloat16
full = jnp.float32


def dot_nn(a, b):
    return lax.dot_general(a, b, (((1,), (0,)), ((), ())), preferred_element_type=full)


def dot_nt(a, b):
    return lax.dot_general(a, b, (((1,), (1,)), ((), ())), preferred_element_type=full)


def dot_tn(a, b):
    return lax.dot_general(a, b, (((0,), (0,)), ((), ())), preferred_element_type=full)


def gelu_parts(z):
    size = jnp.abs(z) * 0.7071067811865476
    t = 1.0 / (1.0 + 0.3275911 * size)
    bell = jnp.exp(-0.5 * z * z)
    poly = ((((1.061405429 * t - 1.453152027) * t + 1.421413741) * t - 0.284496736) * t + 0.254829592) * t
    half_tail = 0.5 * poly * bell
    phi = jnp.where(z >= 0, 1.0 - half_tail, half_tail)
    return z * phi, phi + z * bell * 0.3989422804014327


def norm_parts(residual):
    average = jnp.mean(residual, axis=-1, keepdims=True)
    centered = residual - average
    inverse = lax.rsqrt(jnp.mean(centered * centered, axis=-1, keepdims=True) + norm_epsilon)
    return centered * inverse, inverse


def norm_back(upstream, unit, inverse, gain):
    scaled = upstream * gain
    return inverse * (
        scaled
        - jnp.mean(scaled, axis=-1, keepdims=True)
        - unit * jnp.mean(scaled * unit, axis=-1, keepdims=True)
    )


def column_sum(values):
    return jnp.sum(values, axis=0, keepdims=True)


def half_masks(dtype):
    lane = lax.broadcasted_iota(jnp.int32, (1, PAIR), 1)
    first = (lane < HD).astype(full)
    return first.astype(dtype), (1.0 - first).astype(dtype)


def segment_bias(seg_column, seg_row):
    return jnp.where(seg_column == seg_row, 0.0, masked_score)


def flip(index, bit):
    return index + bit * (1 - 2 * lax.rem(lax.div(index, bit), 2))


def place():
    dp = lax.axis_index("dp")
    return dp, lax.axis_index("fsdp"), lax.rem(dp, 2), lax.div(dp, 2)


def greet(partners):
    barrier = pltpu.get_barrier_semaphore()
    for device in partners:
        pl.semaphore_signal(barrier, inc=1, device_id=device, device_id_type=pl.DeviceIdType.MESH)
    pl.semaphore_wait(barrier, len(partners))


def z_partners(count):
    dp, z, _, _ = place()
    return [(dp, lax.rem(z + d, count)) for d in range(1, count)]


def chip_partners():
    dp, z, core, spot = place()
    return [
        (flip(dp, 1), z),
        (2 * flip(spot, 1) + core, z),
        (2 * flip(spot, 2) + core, z),
    ]


def remote(source, target, send, receive, device):
    return pltpu.make_async_remote_copy(
        src_ref=source,
        dst_ref=target,
        send_sem=send,
        recv_sem=receive,
        device_id=device,
        device_id_type=pl.DeviceIdType.MESH,
    )


def fold(piece):
    half = piece.shape[1] // 2
    return jnp.concatenate([piece[:, :half], piece[:, half:]], axis=0)


def unfold(piece):
    rows = piece.shape[0] // 2
    return jnp.concatenate([piece[:rows], piece[rows:]], axis=1)


def sum_scratch(count, part, width, z_count, kind=low):
    piece = (2 * part // z_count, width // 2) if kind == low else (part // z_count, width)
    return [
        pltpu.VMEM((3, 4, part, width), kind),
        pltpu.VMEM((count, 4, part, width), kind),
        pltpu.VMEM((count, 2, part, width), kind),
        pltpu.VMEM((count, part, width), kind),
        pltpu.VMEM((count, z_count) + piece, kind),
        pltpu.VMEM((count, z_count) + piece, kind),
        pltpu.SemaphoreType.DMA((3,)),
        pltpu.SemaphoreType.DMA((count, 2)),
        pltpu.SemaphoreType.DMA((count, 2, 2)),
        pltpu.SemaphoreType.DMA((count, 2)),
        pltpu.SemaphoreType.DMA((count, 2, z_count)),
    ]


SUM_REFS = 11


class BlockSum:
    def __init__(self, sources, refs, at=None):
        self.sources = sources
        self.at = at or (lambda t: ((t >= 0) & (t < self.count), t))
        (self.own, self.c, self.b, self.a, self.zs, self.zr,
         self.own_sem, self.c_sem, self.b_sem, self.a_sem, self.z_sem) = refs
        self.count = self.c.shape[0]
        self.kind = self.c.dtype
        self.z_count = self.zs.shape[1]

    def load(self, i, block):
        core = place()[2]
        slot = lax.rem(i, 3)
        return pltpu.make_async_copy(block.at[:, core], self.own.at[slot], self.own_sem.at[slot])

    def core_copy(self, i, block):
        dp, z, core, _ = place()
        return remote(
            block.at[:, 1 - core], self.c.at[i], self.c_sem.at[i, 0], self.c_sem.at[i, 1], (flip(dp, 1), z)
        )

    def second_copy(self, i, k):
        _, z, core, spot = place()
        other = flip(spot, 2 - core)
        chunk = other if k == 0 else flip(other, 1 + core)
        return remote(
            self.c.at[i, chunk], self.b.at[i, k], self.b_sem.at[i, 0, k], self.b_sem.at[i, 1, k], (2 * other + core, z)
        )

    def third_copy(self, i):
        _, z, core, spot = place()
        other = flip(spot, 1 + core)
        return remote(self.c.at[i, other], self.a.at[i], self.a_sem.at[i, 0], self.a_sem.at[i, 1], (2 * other + core, z))

    def z_copy(self, i, d):
        dp, z, _, _ = place()
        other = lax.rem(z + d, self.z_count)
        return remote(
            self.zs.at[i, other], self.zr.at[i, z], self.z_sem.at[i, 0, d], self.z_sem.at[i, 1, self.z_count - d], (dp, other)
        )

    def open(self, i):
        first = 0
        for source in self.sources:
            count = source.shape[0]

            @pl.when((i >= first) & (i < first + count))
            def _():
                block = source.at[jnp.clip(i - first, 0, count - 1)]
                self.core_copy(i, block).start()
                self.load(i, block).start()

            first += count

    def after_core(self, i):
        block = self.sources[0].at[0]
        self.core_copy(i, block).wait()
        self.load(i, block).wait()
        slot = lax.rem(i, 3)
        for k in range(4):
            self.c[i, k] = (self.c[i, k].astype(full) + self.own[slot, k].astype(full)).astype(self.kind)
        self.second_copy(i, 0).start()
        self.second_copy(i, 1).start()

    def after_second(self, i):
        _, _, core, spot = place()
        other = flip(spot, 1 + core)
        self.second_copy(i, 1).wait()
        self.c[i, other] = (self.c[i, other].astype(full) + self.b[i, 1].astype(full)).astype(self.kind)
        self.third_copy(i).start()
        self.second_copy(i, 0).wait()
        self.c[i, spot] = (self.c[i, spot].astype(full) + self.b[i, 0].astype(full)).astype(self.kind)

    def after_third(self, i):
        _, _, _, spot = place()
        self.third_copy(i).wait()
        total = self.c[i, spot].astype(full) + self.a[i].astype(full)
        rows = total.shape[0] // self.z_count
        for k in range(self.z_count):
            piece = total[k * rows : (k + 1) * rows]
            self.zs[i, k] = fold(piece).astype(low) if self.kind == low else piece
        for d in range(1, self.z_count):
            self.z_copy(i, d).start()

    def finish(self, i):
        z = lax.axis_index("fsdp")
        for d in range(1, self.z_count):
            self.z_copy(i, d).wait()
        total = self.zs[i, z].astype(full)
        for d in range(1, self.z_count):
            total = total + self.zr[i, lax.rem(z + d, self.z_count)].astype(full)
        return total

    def tick(self, t):
        for late, stage in ((6, self.after_third), (4, self.after_second), (2, self.after_core), (0, self.open)):
            now, block = self.at(t - late)

            @pl.when(now)
            def _():
                stage(block)


class LineGather:
    def __init__(self, source, target, first, local_sem, sem, z_count):
        self.source = source.at[pl.ds(first, target.shape[1])]
        self.target, self.local_sem, self.sem, self.z_count = target, local_sem, sem, z_count

    def hop_copy(self, hop, way):
        dp, z, _, _ = place()
        if way == 0:
            piece, other, coming = z - hop + 1, z + 1, z - hop
            sends = (piece >= 0) & (other < self.z_count)
            receives = coming >= 0
        else:
            piece, other, coming = z + hop - 1, z - 1, z + hop
            sends = (piece < self.z_count) & (other >= 0)
            receives = coming < self.z_count
        piece = jnp.clip(piece, 0, self.z_count - 1)
        other = jnp.clip(other, 0, self.z_count - 1)
        source = self.source if hop == 1 else self.target.at[piece]
        copy = remote(source, self.target.at[piece], self.sem.at[way, 0, hop - 1], self.sem.at[way, 1, hop - 1], (dp, other))
        return copy, sends, receives

    def local(self):
        return pltpu.make_async_copy(self.source, self.target.at[lax.axis_index("fsdp")], self.local_sem)

    def start(self, hop):
        if hop == 1:
            self.local().start()
        for way in range(2):
            copy, sends, _ = self.hop_copy(hop, way)

            @pl.when(sends)
            def _():
                copy.start()

    def wait(self, hop):
        if hop == 1:
            self.local().wait()
        for way in range(2):
            copy, sends, receives = self.hop_copy(hop, way)

            @pl.when(sends)
            def _():
                copy.wait_send()

            @pl.when(receives)
            def _():
                copy.wait_recv()

    def advance(self, hop):
        if hop > 1:
            self.wait(hop - 1)
        if hop < self.z_count:
            self.start(hop)


def gather_scratch(count, rows, width, z_count, kind=low):
    piece = (2 * rows // z_count, width // 2) if kind == low else (rows // z_count, width)
    return [
        pltpu.VMEM((count, z_count) + piece, kind),
        pltpu.SemaphoreType.DMA((count, 2, z_count)),
        pltpu.SemaphoreType.DMA((count, 2)),
        pltpu.SemaphoreType.DMA((count, 2, 2)),
        pltpu.SemaphoreType.DMA((count, 2, 4)),
    ]


GATHER_REFS = 5


class BlockGather:
    def __init__(self, source, whole, base, refs):
        self.source, self.whole, self.base = source, whole, base
        self.zr, self.z_sem, self.a_sem, self.b_sem, self.c_sem = refs
        self.count, self.z_count = self.zr.shape[0], self.zr.shape[1]
        self.rows = self.whole.shape[1] // (2 * 4)

    def z_copy(self, i, d):
        dp, z, _, _ = place()
        other = lax.rem(z + d, self.z_count)
        return remote(
            self.source.at[i], self.zr.at[i, z], self.z_sem.at[i, 0, d], self.z_sem.at[i, 1, self.z_count - d], (dp, other)
        )

    def chunk(self, i, spot, core):
        start = pl.multiple_of((2 * spot + core) * self.rows, self.rows)
        return self.whole.at[self.base + i, pl.ds(start, self.rows)]

    def first_copy(self, i):
        _, z, core, spot = place()
        return self.one(i, spot, self.a_sem.at[i, 0], self.a_sem.at[i, 1], (2 * flip(spot, 1 + core) + core, z))

    def second_copy(self, i, k):
        _, z, core, spot = place()
        chunk = spot if k == 0 else flip(spot, 1 + core)
        return self.one(
            i, chunk, self.b_sem.at[i, 0, k], self.b_sem.at[i, 1, k], (2 * flip(spot, 2 - core) + core, z)
        )

    def core_copy(self, i, k):
        dp, z, core, spot = place()
        chunk = spot
        if k & 1:
            chunk = flip(chunk, 1 + core)
        if k & 2:
            chunk = flip(chunk, 2 - core)
        return self.one(i, chunk, self.c_sem.at[i, 0, k], self.c_sem.at[i, 1, k], (flip(dp, 1), z))

    def one(self, i, spot, send, receive, device):
        chunk = self.chunk(i, spot, place()[2])
        return remote(chunk, chunk, send, receive, device)

    AHEAD = 3

    def announce(self, i):
        for d in range(1, self.z_count):
            self.z_copy(i, d).start()
        self.zr[i, lax.axis_index("fsdp")] = self.source[i]

    def begin(self):
        for i in range(min(self.AHEAD, self.count)):
            self.announce(i)

    def open(self, i):
        dp = lax.axis_index("dp")
        for d in range(1, self.z_count):
            self.z_copy(i, d).wait()
        pieces = [self.zr[i, k].astype(full) for k in range(self.z_count)]
        if self.zr.dtype == low:
            pieces = [unfold(piece) for piece in pieces]
        start = pl.multiple_of(dp * self.rows, self.rows)
        self.whole[self.base + i, pl.ds(start, self.rows)] = jnp.concatenate(pieces, axis=0).astype(self.whole.dtype)
        self.first_copy(i).start()
        self.second_copy(i, 0).start()
        self.core_copy(i, 0).start()

    def after_first(self, i):
        self.first_copy(i).wait()
        self.second_copy(i, 1).start()
        self.core_copy(i, 1).start()

    def after_second(self, i):
        self.second_copy(i, 0).wait()
        self.core_copy(i, 2).start()
        self.second_copy(i, 1).wait()
        self.core_copy(i, 3).start()

    def close(self, i):
        for k in range(4):
            self.core_copy(i, k).wait()

    def tick(self, t, done=None):
        @pl.when(t + self.AHEAD < self.count)
        def _():
            self.announce(t + self.AHEAD)

        for late, stage in ((4, self.after_second), (2, self.after_first), (0, self.open), (6, self.close)):
            @pl.when((t >= late) & (t < self.count + late))
            def _():
                stage(t - late)
                if late == 6 and done is not None:
                    done(t - late)


def split_refs(refs, *counts):
    result, start = [], 0
    for count in counts:
        result.append(refs[start : start + count])
        start += count
    return result


class Side:
    def __init__(self, plan, sources, targets, sum_refs, line_refs, own=None):
        self.plan = plan
        sums = plan.sums
        blocks = list(sources[:sums]) + ([own] if plan.own else [])
        self.sum = BlockSum(blocks, sum_refs, plan.at) if plan.total else None
        self.result = targets[0] if plan.total else None
        self.lines = line_gathers(plan.lines, sources[sums:], targets[bool(plan.total) :], line_refs, plan.z_count)

    def enter(self, now):
        if not self.plan.active:
            return

        @pl.when(now)
        def _():
            greet((chip_partners() if self.plan.total else []) + z_partners(self.plan.z_count))
            for line in self.lines:
                line.advance(1)

    def leave(self, now):
        if not self.plan.active:
            return

        @pl.when(now)
        def _():
            if self.plan.total:
                for i in range(self.sum.count):
                    self.result[i] = self.sum.finish(i).astype(low)
            for line in self.lines:
                line.advance(self.plan.z_count)

    def advance(self, now, hop):
        if self.lines and hop < self.plan.z_count:
            @pl.when(now)
            def _():
                for line in self.lines:
                    line.advance(hop)


class Plan:
    def __init__(self, pending=None, lines=(), z_count=1, own=0, size=None, at=None):
        self.z_count = z_count
        self.sums = int(pending is not None)
        self.own, self.at = own, at
        self.total = own + (pending.shape[0] if self.sums else 0)
        self.lines = [(first, count) for _, first, count in lines]
        self.active = bool(self.total or lines)
        self.arguments, self.results, self.result_specs, self.scratch = [], [], [], []
        if self.sums:
            self.arguments.append(pending)
        if self.total:
            part, width = size
            self.results.append(jax.ShapeDtypeStruct((self.total, 2 * part // z_count, width // 2), low))
            self.result_specs.append(
                pl.BlockSpec(self.results[0].shape, lambda i: (0, 0, 0), pipeline_mode=pl.Buffered(1))
            )
            self.scratch += sum_scratch(self.total, part, width, z_count)
        for basis, _, count in lines:
            self.arguments.append(basis)
            self.results.append(jax.ShapeDtypeStruct((z_count, count) + basis.shape[1:], low))
            self.result_specs.append(ANYWHERE)
        self.scratch += line_scratch(len(lines), z_count)
        self.argument_specs = [ANYWHERE] * len(self.arguments)

    def split(self, refs, inputs, outputs, scratch):
        count = len(self.lines)
        return split_refs(
            refs, inputs, self.sums + count, outputs, bool(self.total) + count, scratch,
            SUM_REFS * bool(self.total), 2 * bool(self.lines),
        )


def line_scratch(count, z_count):
    if not count:
        return []
    return [pltpu.SemaphoreType.DMA((count,)), pltpu.SemaphoreType.DMA((count, 2, 2, z_count - 1))]


def line_gathers(spans, sources, targets, refs, z_count):
    return [
        LineGather(source, target, first, refs[0].at[n], refs[1].at[n], z_count)
        for n, (source, target, (first, _)) in enumerate(zip(sources, targets, spans))
    ]


ANYWHERE = pl.BlockSpec(memory_space=pl.ANY)
IN_VMEM = pl.BlockSpec(memory_space=pltpu.VMEM)


def forward_kernel(plan, *refs):
    inputs, sources, outputs, targets, scratch, gather_refs, vec_refs, line_refs = plan.split(refs)
    x_ref, segc_ref, segr_ref, vec_ref, w_hbm = inputs
    (q_ref, k_ref, v_ref, ctxt_ref, lse_ref, x1_ref, inv1_ref, n1_ref, u_ref, gp_ref, x2_ref, inv2_ref,
     out_ref) = outputs
    w, bias, vt, n1_all, acc, w_sem = scratch
    s = pl.program_id(0)
    tokens, width = acc.shape
    rows_now = x_ref.shape[0]
    rows = tokens // rows_now
    inner = plan.inner
    local = plan.local
    gather = vec_gather = None
    if plan.gathered:
        w_out, out_sem = targets[0], scratch_tail(plan, refs)
        gather = BlockGather(sources[0], w, local, gather_refs)
        if plan.vectors:
            vec_gather = BlockGather(sources[1], plan.vec_whole(refs), 0, vec_refs)
            vec_ref = targets[1]
    lines = line_gathers(plan.lines, sources[plan.line_at :], targets[plan.line_target_at :], line_refs, plan.z_count)

    def keep(i):
        return pltpu.make_async_copy(w.at[local + i], w_out.at[i], out_sem.at[i])

    def load(j):
        return pltpu.make_async_copy(w_hbm.at[plan.order[j]], w.at[j], w_sem.at[j])

    def arrive(j):
        if j < local:
            load(j).wait()

    def tick(t):
        if gather is not None:
            gather.tick(t, lambda i: keep(i).start())
            if vec_gather is not None:
                vec_gather.tick(t)

    @pl.when(s == 0)
    def _():
        for j in range(local):
            load(j).start()
        if gather is not None:
            greet(chip_partners() + z_partners(plan.z_count))
            if vec_gather is not None:
                vec_gather.begin()
            gather.begin()
            lax.fori_loop(0, plan.lead, lambda t, carry: (tick(t), carry)[1], 0)
            for line in lines:
                line.advance(1)
            if vec_gather is not None:
                turned = vec_gather.whole[0].T
                for layer in range(2):
                    count = plan.vector_rows
                    targets[1 + layer][0:count, :] = turned[layer * count : (layer + 1) * count, :]
        for j in range(min(local, 3)):
            arrive(j)

    @pl.when(s < rows)
    def _():
        xin = x_ref[...].astype(low)
        bias[...] = segment_bias(segc_ref[0], segr_ref[0])
        q_ref[...] = (dot_nn(xin, w[0]) + vec_ref[0:1, :]).astype(low)
        k_ref[...] = dot_nn(xin, w[1]).astype(low)
        value = dot_nn(xin, w[2]) + vec_ref[1:2, :]
        v_ref[...] = value.astype(low)
        vt[...] = value.T.astype(low)
        masks = half_masks(low)
        pairs = width // PAIR

        def pair_step(p, carry):
            lanes = pl.ds(pl.multiple_of(p * PAIR, PAIR), PAIR)
            q_pair = q_ref[:, lanes] * jnp.asarray(HD ** (-0.5), low)
            k_pair = k_ref[:, lanes]
            for h in range(2):
                scores = dot_nt(k_pair, q_pair * masks[h]) + bias[...]
                largest = jnp.max(scores, axis=0, keepdims=True)
                expanded = jnp.exp(scores - largest)
                total = column_sum(expanded)
                here = pl.ds(pl.multiple_of(p * PAIR + h * HD, HD), HD)
                context = dot_nn(vt[here, :], expanded.astype(low)) * (1.0 / total)
                ctxt_ref[here, :] = context.astype(low)
                lse_ref[0, pl.ds(2 * p + h, 1), :] = largest + jnp.log(total)
            if plan.gathered:
                many = plan.row_ticks

                @pl.when(lax.div((p + 1) * many, pairs) > lax.div(p * many, pairs))
                def _():
                    tick(plan.lead + s * many + lax.div(p * many, pairs))
            return carry

        lax.fori_loop(0, pairs, pair_step, 0)

        @pl.when(s == 0)
        def _():
            if local > 3:
                arrive(3)
            for line in lines:
                line.advance(2)

        context = ctxt_ref[...].astype(full).T.astype(low)
        attended = dot_nn(context, w[3]) + vec_ref[2:3, :]
        unit, inverse = norm_parts(x_ref[...].astype(full) + attended)
        x1_ref[...] = unit
        inv1_ref[...] = inverse
        normed = unit * vec_ref[3:4, :] + vec_ref[4:5, :]
        here = pl.ds(pl.multiple_of(s * rows_now, rows_now), rows_now)
        acc[here, :] = normed + vec_ref[5 + inner : 6 + inner, :]
        normed = normed.astype(low)
        n1_ref[...] = normed
        n1_all[here, :] = normed

    tile = tokens // 4
    after = plan.lead + rows * plan.row_ticks

    @pl.when(s >= rows)
    def _():
        c = s - rows

        @pl.when(c == 0)
        def _():
            for j in range(4, local):
                arrive(j)
            for line in lines:
                line.advance(3)

        def token_step(i, carry):
            for half in range(2):
                here = pl.ds(pl.multiple_of((2 * i + half) * tile, tile), tile)
                value, slope = gelu_parts(dot_nn(n1_all[here, :], w[4 + 2 * c]) + vec_ref[pl.ds(5 + c, 1), :])
                active = value.astype(low)
                u_ref[here, :] = active
                gp_ref[here, :] = slope.astype(low)
                acc[here, :] += dot_nn(active, w[5 + 2 * c])
            tick(after + 2 * c + i)
            return carry

        lax.fori_loop(0, 2, token_step, 0)

        @pl.when(c == inner - 1)
        def _():
            base = 5 + inner

            def last(i, carry):
                here = pl.ds(pl.multiple_of(i * tile, tile), tile)
                unit, inverse = norm_parts(acc[here, :])
                x2_ref[here, :] = unit
                inv2_ref[here, :] = inverse
                out_ref[here, :] = (
                    unit * vec_ref[base + 1 : base + 2, :] + vec_ref[base + 2 : base + 3, :]
                ).astype(out_ref.dtype)
                return carry

            lax.fori_loop(0, 4, last, 0)
            if gather is not None:
                for t in range(after + 2 * inner, gather.count + 6):
                    tick(t)
                for line in lines:
                    line.advance(plan.z_count)
                for i in range(gather.count):
                    keep(i).wait()


class ForwardPlan:
    def __init__(self, inner, local, shards=None, vec_shard=None, vector_rows=0, lines=(), lead=0, row_ticks=1, z_count=1):
        self.inner, self.local, self.lead, self.row_ticks, self.z_count = inner, local, lead, row_ticks, z_count
        self.vector_rows = vector_rows
        self.order = [0, 1, 2, 3]
        for c in range(inner):
            self.order += [4 + c, 4 + inner + c]
        self.gathered = 0 if shards is None else shards.shape[0]
        self.vectors = vec_shard is not None
        self.lines = [(first, count) for _, first, count in lines]
        self.line_at = int(self.gathered > 0) + int(self.vectors)
        self.line_target_at = int(self.gathered > 0) + 2 * int(self.vectors)
        self.arguments, self.argument_specs, self.results, self.result_specs, self.scratch = [], [], [], [], []
        shape = jax.ShapeDtypeStruct
        if self.gathered:
            width = 2 * shards.shape[2]
            self.arguments.append(shards)
            self.argument_specs.append(IN_VMEM)
            self.results.append(shape((self.gathered, width, width), low))
            self.result_specs.append(ANYWHERE)
            self.scratch += gather_scratch(self.gathered, width // 8, width, z_count)
        if self.vectors:
            rows, lanes = vec_shard.shape[1:]
            self.arguments.append(vec_shard)
            self.argument_specs.append(IN_VMEM)
            for _ in range(2):
                self.results.append(shape((16, width), full))
                self.result_specs.append(pl.BlockSpec((16, width), lambda s: (0, 0)))
            self.scratch += gather_scratch(1, width // 8, lanes, z_count, full)
        for basis, _, count in lines:
            self.arguments.append(basis)
            self.argument_specs.append(ANYWHERE)
            self.results.append(shape((z_count, count) + basis.shape[1:], low))
            self.result_specs.append(ANYWHERE)
        self.scratch += line_scratch(len(lines), z_count)
        if self.gathered:
            self.scratch.append(pltpu.SemaphoreType.DMA((self.gathered,)))
        if self.vectors:
            self.scratch.append(pltpu.VMEM((1, width, lanes), full))

    def split(self, refs):
        return split_refs(
            refs, 5, len(self.arguments), 13, len(self.results), 6, GATHER_REFS * bool(self.gathered),
            GATHER_REFS * self.vectors, 2 * bool(self.lines),
        )

    def vec_whole(self, refs):
        return refs[-1]


def scratch_tail(plan, refs):
    return refs[-2] if plan.vectors else refs[-1]


def forward_layer(hidden, seg_column, seg_row, vectors, weights, out_dtype, plan, identity=None):
    tokens, width = hidden.shape
    inner = plan.inner
    wide = width * inner
    rows = tokens // L
    heads = width // HD
    shape = jax.ShapeDtypeStruct

    def here(s):
        return jnp.minimum(s, rows - 1)

    def column(s):
        return jnp.maximum(s - rows, 0)

    def row_block(columns):
        return pl.BlockSpec((L, columns), lambda s: (here(s), 0))

    def whole(columns):
        return pl.BlockSpec((tokens, columns), lambda s: (0, 0), pipeline_mode=pl.Buffered(1))

    wide_block = pl.BlockSpec((tokens, width), lambda s: (0, column(s)))
    out_shape = (
        shape((tokens, width), low), shape((tokens, width), low), shape((tokens, width), low),
        shape((width, tokens), low), shape((rows, heads, L), full),
        shape((tokens, width), full), shape((tokens, 1), full), shape((tokens, width), low),
        shape((tokens, wide), low), shape((tokens, wide), low),
        shape((tokens, width), full), shape((tokens, 1), full), shape((tokens, width), out_dtype),
        *plan.results,
    )
    out_specs = (
        row_block(width), row_block(width), row_block(width),
        pl.BlockSpec((width, L), lambda s: (0, here(s))), pl.BlockSpec((1, heads, L), lambda s: (here(s), 0, 0)),
        row_block(width), row_block(1), row_block(width),
        wide_block, wide_block,
        whole(width), whole(1), whole(width),
        *plan.result_specs,
    )
    total = 4 + 2 * inner
    held = max(total, plan.local + plan.gathered)
    return pl.pallas_call(
        functools.partial(forward_kernel, plan),
        grid=(rows + inner,),
        out_shape=out_shape,
        in_specs=[
            row_block(width),
            pl.BlockSpec((1, L, 1), lambda s: (here(s), 0, 0)),
            pl.BlockSpec((1, 1, L), lambda s: (here(s), 0, 0)),
            pl.BlockSpec(vectors.shape, lambda s: (0, 0)),
            ANYWHERE,
            *plan.argument_specs,
        ],
        out_specs=out_specs,
        scratch_shapes=[
            pltpu.VMEM((held, width, width), low),
            pltpu.VMEM((L, L), full),
            pltpu.VMEM((width, L), low),
            pltpu.VMEM((tokens, width), low),
            pltpu.VMEM((tokens, width), full),
            pltpu.SemaphoreType.DMA((total,)),
            *plan.scratch,
        ],
        compiler_params=pltpu.CompilerParams(
            dimension_semantics=("arbitrary",), vmem_limit_bytes=62 * MIB,
            collective_id=identity, has_side_effects=identity is not None,
        ),
        cost_estimate=pl.CostEstimate(
            flops=2 * tokens * width * width * total + 4 * tokens * L * width,
            bytes_accessed=40 * MIB,
            transcendentals=tokens * (L * heads + wide),
        ),
        name="layer_forward",
    )(hidden, seg_column, seg_row, vectors, weights, *plan.arguments)


def wide_back_kernel(plan, inner, *refs):
    inputs, sources, outputs, targets, scratch, sum_refs, line_refs = plan.split(refs, 11, 4, 3)
    up_ref, x2_ref, inv2_ref, x1_ref, inv1_ref, n1_ref, vec_ref, wup_ref, wdown_ref, u_ref, gp_ref = inputs
    dw_ref, dr1_ref, da_ref, dvec_ref = outputs
    n1t, dz, kept_dw = scratch
    dy, dn1 = da_ref, dr1_ref
    c = pl.program_id(0)
    side = Side(plan, sources, targets, sum_refs, line_refs, kept_dw)
    side.enter(c == 0)
    steps = pl.num_programs(0)
    tokens, width = dn1.shape
    tile = tokens // 4
    pick = [slice(i * tile, (i + 1) * tile) for i in range(4)]
    base = 5 + inner

    @pl.when(c == 0)
    def _():
        gain = vec_ref[base + 1 : base + 2, :]

        def body(i, carry):
            gain_sum, shift_sum, bias_sum = carry
            rows = pl.ds(pl.multiple_of(i * tile, tile), tile)
            upstream = up_ref[rows, :].astype(full)
            unit = x2_ref[rows, :]
            back = norm_back(upstream, unit, inv2_ref[rows, :], gain)
            dn1[rows, :] = back
            branch = back.astype(low)
            dy[rows, :] = branch
            return (
                gain_sum + column_sum(upstream * unit),
                shift_sum + column_sum(upstream),
                bias_sum + column_sum(branch.astype(full)),
            )

        zero = jnp.zeros((1, width), full)
        gain_sum, shift_sum, bias_sum = lax.fori_loop(0, 4, body, (zero, zero, zero))
        dvec_ref[...] = jnp.zeros(dvec_ref.shape, full)
        dvec_ref[base : base + 1, :] = bias_sum
        dvec_ref[base + 1 : base + 2, :] = gain_sum
        dvec_ref[base + 2 : base + 3, :] = shift_sum
        n1t[...] = n1_ref[...].astype(full).T.astype(low)

    def token_step(i, carry):
        rows = pl.ds(pl.multiple_of(i * tile, tile), tile)
        slope = gp_ref[rows, :].astype(full)
        piece = (dot_nt(dy[rows, :], wdown_ref[0]) * slope).astype(low)
        dz[rows, :] = piece
        dn1[rows, :] += dot_nt(piece, wup_ref[0])
        side.advance(4 * c + i == 5, 2)
        side.advance(4 * c + i == 10, 3)
        if plan.total:
            side.sum.tick(4 * c + i)
        return carry + column_sum(piece.astype(full))

    bias_sum = lax.fori_loop(0, 4, token_step, jnp.zeros((1, width), full))
    for j in range(inner):
        @pl.when(c == j)
        def _():
            dvec_ref[5 + j : 6 + j, :] = bias_sum
    dw_up = dot_nn(n1t[...], dz[...]).astype(low)
    dw_down = dot_tn(u_ref[...], dy[...]).astype(low)
    if plan.own:
        @pl.when(2 * c < plan.own)
        def _():
            kept_dw[2 * c] = dw_up.reshape(kept_dw.shape[1:])
            kept_dw[2 * c + 1] = dw_down.reshape(kept_dw.shape[1:])

        @pl.when(2 * c >= plan.own)
        def _():
            dw_ref[0, 0] = dw_up
            dw_ref[1, 0] = dw_down
    else:
        dw_ref[0, 0] = dw_up
        dw_ref[1, 0] = dw_down

    @pl.when(c == steps - 1)
    def _():
        gain = vec_ref[3:4, :]

        def body(i, carry):
            gain_sum, shift_sum, bias_sum = carry
            rows = pl.ds(pl.multiple_of(i * tile, tile), tile)
            upstream = dn1[rows, :]
            unit = x1_ref[rows, :]
            back = norm_back(upstream, unit, inv1_ref[rows, :], gain)
            dr1_ref[rows, :] = back
            branch = back.astype(low)
            da_ref[rows, :] = branch
            return (
                gain_sum + column_sum(upstream * unit),
                shift_sum + column_sum(upstream),
                bias_sum + column_sum(branch.astype(full)),
            )

        zero = jnp.zeros((1, width), full)
        gain_sum, shift_sum, bias_sum = lax.fori_loop(0, 4, body, (zero, zero, zero))
        dvec_ref[2:3, :] = bias_sum
        dvec_ref[3:4, :] = gain_sum
        dvec_ref[4:5, :] = shift_sum

    side.leave(c == steps - 1)


def wide_back(upstream, kept, vectors, weights, places, plan, identity=None):
    x1, inv1, n1, u, gp, x2, inv2 = kept
    tokens, width = x1.shape
    up_start, down_start, stride = places
    inner = u.shape[1] // width
    shape = jax.ShapeDtypeStruct

    def whole(array):
        return pl.BlockSpec(array.shape, lambda c: (0, 0), pipeline_mode=pl.Buffered(1))

    return pl.pallas_call(
        functools.partial(wide_back_kernel, plan, inner),
        grid=(inner,),
        out_shape=(
            shape((2, inner - plan.own // 2, width, width), low),
            shape((tokens, width), full), shape((tokens, width), low), shape((16, width), full),
            *plan.results,
        ),
        in_specs=[
            whole(upstream), whole(x2), whole(inv2), whole(x1), whole(inv1), whole(n1), whole(vectors),
            pl.BlockSpec((1, width, width), lambda c: (up_start + stride * c, 0, 0)),
            pl.BlockSpec((1, width, width), lambda c: (down_start + stride * c, 0, 0)),
            pl.BlockSpec((tokens, width), lambda c: (0, c)),
            pl.BlockSpec((tokens, width), lambda c: (0, c)),
            *plan.argument_specs,
        ],
        out_specs=(
            pl.BlockSpec((2, 1, width, width), lambda c: (0, jnp.maximum(c - plan.own // 2, 0), 0, 0)),
            pl.BlockSpec((tokens, width), lambda c: (0, 0), pipeline_mode=pl.Buffered(1)),
            pl.BlockSpec((tokens, width), lambda c: (0, 0), pipeline_mode=pl.Buffered(1)),
            pl.BlockSpec((16, width), lambda c: (0, 0)),
            *plan.result_specs,
        ),
        scratch_shapes=[
            pltpu.VMEM((width, tokens), low),
            pltpu.VMEM((tokens, width), low),
            pltpu.VMEM((plan.own, 4, 2, width // 8, width) if plan.own else (8, 128), low),
            *plan.scratch,
        ],
        compiler_params=pltpu.CompilerParams(
            dimension_semantics=("arbitrary",), vmem_limit_bytes=60 * MIB,
            collective_id=identity, has_side_effects=identity is not None,
        ),
        cost_estimate=pl.CostEstimate(
            flops=8 * tokens * width * width * inner, bytes_accessed=50 * MIB, transcendentals=0
        ),
        name="wide_backward",
    )(upstream, x2, inv2, x1, inv1, n1, vectors, weights, weights, u, gp, *plan.arguments)


def attend_back_kernel(plan, *refs):
    inputs, sources, outputs, targets, scratch, sum_refs, line_refs = plan.split(refs, 11, 3, 10)
    da_ref, dr1_ref, x_ref, q_ref, k_ref, v_ref, ctxt_ref, lse_ref, segc_ref, segr_ref, w_ref = inputs
    dw_ref, dx_ref, dvec_ref = outputs
    bias, dctx, kt, delta, dqt, xt, dq_all, dk_all, dv_all, dwo = scratch
    r = pl.program_id(0)
    side = Side(plan, sources, targets, sum_refs, line_refs, dwo)
    side.enter(r == 0)
    tokens, width = dr1_ref.shape
    pairs = width // PAIR
    ticks = pairs + 2

    def tick(n):
        if plan.total:
            side.sum.tick(r * ticks + n)

    tick(0)
    here = pl.ds(pl.multiple_of(r * tokens, tokens), tokens)

    @pl.when(r == 0)
    def _():
        grad = dot_nn(ctxt_ref[...], da_ref[...]).astype(low)
        if plan.own:
            dwo[0] = grad.reshape(dwo.shape[1:])
        else:
            dw_ref[3] = grad

    xt[:, here] = x_ref[...].astype(low).astype(full).T.astype(low)
    bias[...] = segment_bias(segc_ref[0], segr_ref[0])
    context_grad = dot_nt(da_ref[here, :], w_ref[3]).astype(low)
    dctx[...] = context_grad
    kt[...] = k_ref[...].astype(full).T.astype(low)
    products = context_grad.astype(full) * ctxt_ref[:, here].astype(full).T
    feature = lax.broadcasted_iota(jnp.int32, (16, width), 1)
    head = lax.broadcasted_iota(jnp.int32, (16, width), 0)
    member = ((feature >= head * HD) & (feature < (head + 1) * HD)).astype(full).astype(low)
    high = products.astype(low)
    rest = (products - high.astype(full)).astype(low)
    delta[...] = dot_nt(member, high) + dot_nt(member, rest)
    masks = half_masks(low)
    scale = HD ** (-0.5)

    def pair_step(p, carry):
        lanes = pl.ds(pl.multiple_of(p * PAIR, PAIR), PAIR)
        q_pair = q_ref[:, lanes] * jnp.asarray(scale, low)
        k_pair = k_ref[:, lanes]
        v_pair = v_ref[:, lanes]
        g_pair = dctx[:, lanes]
        key_grad = jnp.zeros((tokens, PAIR), full)
        value_grad = jnp.zeros((tokens, PAIR), full)
        for h in range(2):
            q_half = q_pair * masks[h]
            g_half = g_pair * masks[h]
            scores = dot_nt(k_pair, q_half) + bias[...]
            attention = jnp.exp(scores - lse_ref[0, pl.ds(2 * p + h, 1), :])
            value_grad = value_grad + dot_nn(attention.astype(low), g_half)
            attention_grad = dot_nt(v_pair, g_half)
            score_grad = (attention * (attention_grad - delta[pl.ds(2 * p + h, 1), :])).astype(low)
            key_grad = key_grad + dot_nn(score_grad, q_half)
            rows = pl.ds(pl.multiple_of(p * PAIR + h * HD, HD), HD)
            dqt[rows, :] = dot_nn(kt[rows, :], score_grad) * scale
        dk_all[here, lanes] = key_grad.astype(low)
        dv_all[here, lanes] = value_grad.astype(low)
        tick(1 + p)
        side.advance((r == 0) & (p == 4), 2)
        side.advance((r == 1) & (p == 3), 3)
        return carry

    lax.fori_loop(0, pairs, pair_step, 0)
    tick(1 + pairs)
    query_grad = dqt[...].T.astype(low)
    dq_all[here, :] = query_grad
    key_grad = dk_all[here, :]
    value_grad = dv_all[here, :]
    dx_ref[...] = (
        dr1_ref[...]
        + dot_nt(query_grad, w_ref[0])
        + dot_nt(key_grad, w_ref[1])
        + dot_nt(value_grad, w_ref[2])
    )

    @pl.when(r == 0)
    def _():
        dvec_ref[...] = jnp.zeros(dvec_ref.shape, full)

    dvec_ref[0:1, :] += column_sum(query_grad.astype(full))
    dvec_ref[1:2, :] += column_sum(value_grad.astype(full))

    @pl.when(r == pl.num_programs(0) - 1)
    def _():
        for j, grad in enumerate((dq_all, dk_all, dv_all)):
            dw_ref[j] = dot_nn(xt[...], grad[...]).astype(low)

    side.leave(r == pl.num_programs(0) - 1)


def attend_back(da, dr1, hidden, kept, seg_column, seg_row, weights, start, plan, identity=None):
    q, k, v, ctxt, lse = kept
    tokens, width = da.shape
    rows = tokens // L
    heads = width // HD
    shape = jax.ShapeDtypeStruct

    def row_block():
        return pl.BlockSpec((L, width), lambda r: (r, 0))

    return pl.pallas_call(
        functools.partial(attend_back_kernel, plan),
        grid=(rows,),
        out_shape=(
            shape((4 - plan.own, width, width), low), shape((tokens, width), full), shape((8, width), full),
            *plan.results,
        ),
        in_specs=[
            pl.BlockSpec((tokens, width), lambda r: (0, 0), pipeline_mode=pl.Buffered(1)),
            row_block(), row_block(), row_block(), row_block(), row_block(),
            pl.BlockSpec((width, tokens), lambda r: (0, 0), pipeline_mode=pl.Buffered(1)),
            pl.BlockSpec((1, heads, L), lambda r: (r, 0, 0)),
            pl.BlockSpec((1, L, 1), lambda r: (r, 0, 0)),
            pl.BlockSpec((1, 1, L), lambda r: (r, 0, 0)),
            pl.BlockSpec((4, width, width), lambda r: (start, 0, 0), pipeline_mode=pl.Buffered(1)),
            *plan.argument_specs,
        ],
        out_specs=(
            pl.BlockSpec((4 - plan.own, width, width), lambda r: (0, 0, 0), pipeline_mode=pl.Buffered(1)),
            row_block(),
            pl.BlockSpec((8, width), lambda r: (0, 0)),
            *plan.result_specs,
        ),
        scratch_shapes=[
            pltpu.VMEM((L, L), full),
            pltpu.VMEM((L, width), low),
            pltpu.VMEM((width, L), low),
            pltpu.VMEM((16, L), full),
            pltpu.VMEM((width, L), full),
            pltpu.VMEM((width, tokens), low),
            pltpu.VMEM((tokens, width), low),
            pltpu.VMEM((tokens, width), low),
            pltpu.VMEM((tokens, width), low),
            pltpu.VMEM((1, 4, 2, width // 8, width) if plan.own else (8, 128), low),
            *plan.scratch,
        ],
        compiler_params=pltpu.CompilerParams(
            dimension_semantics=("arbitrary",), vmem_limit_bytes=60 * MIB,
            collective_id=identity, has_side_effects=identity is not None,
        ),
        cost_estimate=pl.CostEstimate(
            flops=16 * tokens * width * width + 10 * tokens * L * width,
            bytes_accessed=30 * MIB,
            transcendentals=tokens * L * heads,
        ),
        name="attend_backward",
    )(da, dr1, hidden, q, k, v, ctxt, lse, seg_column, seg_row, weights, *plan.arguments)


def moments(rotated, first, second):
    first_new = beta_one * first + (1.0 - beta_one) * rotated
    second_new = beta_two * second + (1.0 - beta_two) * rotated * rotated
    direction = (
        first_new
        / (1.0 - beta_one**STEP)
        / (jnp.sqrt(second_new / (1.0 - beta_two**STEP)) + adam_epsilon)
    )
    return first_new, second_new, direction


def pack_lanes(piece):
    rows = piece.shape[0] // 2
    return jnp.concatenate([piece[:rows], piece[rows:]], axis=1)


def unpack_lanes(piece):
    columns = piece.shape[1] // 2
    return jnp.concatenate([piece[:, :columns], piece[:, columns:]], axis=0)


def optimizer_kernel(plan, *refs):
    inputs, ready, dvecs, bases, lines_in, outputs, lines_out, scratch, sum_refs, vec_refs, line_refs = split_refs(
        refs, 6, plan.ready, plan.dvecs, plan.bases, len(plan.spans), 5, len(plan.spans), 21, SUM_REFS, SUM_REFS,
        2 * bool(plan.spans),
    )
    index_ref, place_ref, tail_hbm, first_hbm, second_hbm, blocks = inputs
    new_ref, low_ref, first_out, second_out, vec_out = outputs
    (store, left, right, first_in, second_in, g_out, g_in, t_out, t_in, e_out, e_in, w_out, w_in, vec_source,
     load_sem, g_sem, t_sem, e_sem, w_sem, left_sem, right_sem) = scratch
    dp, z, core, spot = place()
    slots, owners = g_in.shape[0], g_in.shape[1]
    z_count = t_in.shape[1]
    count = blocks.shape[0]
    tail = BlockSum([tail_hbm], sum_refs)
    vec = BlockSum([vec_source], vec_refs)
    greet([(lax.rem(dp + d, owners), z) for d in range(1, owners)] + z_partners(z_count))
    lines = line_gathers(plan.spans, lines_in, lines_out, line_refs, z_count)
    for line in lines:
        line.advance(1)
    every = list(bases) + list(lines_out)
    tail.tick(0)
    rows = plan.vector_rows
    stacked = jnp.concatenate(
        [dvecs[0][0:2, :], dvecs[1][2:rows, :], dvecs[2][0:2, :], dvecs[3][2:rows, :],
         jnp.zeros((vec_source.shape[-1] - 2 * rows, blocks.shape[2]), full)], axis=0
    )
    vec_source[0] = stacked.T.reshape(vec_source.shape[1:])

    def load(refs_map, target, sem, s):
        n, at = refs_map[s]
        return pltpu.make_async_copy(every[n].at[:, at], target.at[:, s], sem.at[s])

    def load_first(s):
        return pltpu.make_async_copy(first_hbm.at[s], first_in.at[s], load_sem.at[0, s])

    def load_second(s):
        return pltpu.make_async_copy(second_hbm.at[s], second_in.at[s], load_sem.at[1, s])

    early = [s for s in range(slots) if plan.left_map[s][0] < len(bases)]
    for s in range(slots):
        load(plan.right_map, right, right_sem, s).start()
        load_first(s).start()
        load_second(s).start()
        if s in early:
            load(plan.left_map, left, left_sem, s).start()

    def sum_step(t, carry):
        tail.tick(t)
        vec.tick(t - 1)
        return carry

    lax.fori_loop(1, 4, sum_step, 0)
    for line in lines:
        line.advance(2)
    lax.fori_loop(4, tail.count + 7, sum_step, 0)
    start = tail.count
    for part in ready:
        store[start : start + part.shape[0]] = part[...]
        start += part.shape[0]
    store[count] = jnp.zeros(store.shape[1:], low)
    for i in range(tail.count):
        store[i] = tail.finish(i).astype(low)

    def g_copy(s, d):
        other = lax.rem(dp + d, owners)
        return remote(g_out.at[s, d], g_in.at[s, dp], g_sem.at[0, s, d], g_sem.at[1, s, owners - d], (other, z))

    def t_copy(s, d):
        other = lax.rem(z + d, z_count)
        return remote(t_out.at[s, d], t_in.at[s, z], t_sem.at[0, s, d], t_sem.at[1, s, z_count - d], (dp, other))

    def e_copy(s, d):
        other = lax.rem(z + d, z_count)
        return remote(e_out.at[s, d], e_in.at[s, z], e_sem.at[0, s, d], e_sem.at[1, s, z_count - d], (dp, other))

    def w_copy(s, d):
        other = lax.rem(dp + d, owners)
        return remote(
            w_out.at[s, other], w_in.at[s * owners + dp], w_sem.at[0, s, d], w_sem.at[1, s, owners - d], (other, z)
        )

    def send_out(s):
        for d in range(1, owners):
            g_out[s, d] = store[index_ref[s * owners + lax.rem(dp + d, owners)]]
            g_copy(s, d).start()
        g_in[s, dp] = store[index_ref[s * owners + dp]]

    def turn(s):
        for d in range(1, owners):
            g_copy(s, d).wait()
        if s + 2 < slots:
            send_out(s + 2)
        load(plan.right_map, right, right_sem, s).wait()
        grad = jnp.concatenate([unfold(g_in[s, c].astype(full)) for c in range(owners)], axis=0).astype(low)
        for d in range(1, z_count):
            t_out[s, d] = pack_lanes(dot_nt(right[lax.rem(z + d, z_count), s], grad)).astype(low)
            t_copy(s, d).start()
        t_in[s, z] = pack_lanes(dot_nt(right[z, s], grad)).astype(low)

    def adapt(s):
        for d in range(1, z_count):
            t_copy(s, d).wait()
        load_first(s).wait()
        load_second(s).wait()
        load(plan.left_map, left, left_sem, s).wait()
        rotated = jnp.zeros(first_in.shape[1:], full)
        for f in range(z_count):
            rotated = rotated + dot_nn(unpack_lanes(t_in[s, f].astype(full)).astype(low), left[f, s])
        first_new, second_new, direction = moments(rotated, first_in[s], second_in[s])
        first_out[s] = first_new
        second_out[s] = second_new
        direction = direction.astype(low)
        for d in range(1, z_count):
            e_out[s, d] = pack_lanes(dot_nt(left[lax.rem(z + d, z_count), s], direction)).astype(low)
            e_copy(s, d).start()
        e_in[s, z] = pack_lanes(dot_nt(left[z, s], direction)).astype(low)

    def step_back(s):
        for d in range(1, z_count):
            e_copy(s, d).wait()
        step = jnp.zeros((left.shape[2], left.shape[3]), full)
        for f in range(z_count):
            step = step + dot_nn(unpack_lanes(e_in[s, f].astype(full)).astype(low), right[f, s])
        share = step.shape[0] // owners
        for c in range(owners):
            w_out[s, c] = fold(step[c * share : (c + 1) * share]).astype(low)
        for d in range(1, owners):
            w_copy(s, d).start()
        w_in[s * owners + dp] = w_out[s, dp]

    send_out(0)
    send_out(1)
    for hop in range(3, z_count):
        for line in lines:
            line.advance(hop)
    for k in range(slots + 2):
        if k == 3:
            for line in lines:
                line.advance(z_count)
            for s in range(slots):
                if s not in early:
                    load(plan.left_map, left, left_sem, s).start()
        if k < slots:
            turn(k)
        if 0 <= k - 1 < slots:
            adapt(k - 1)
        if 0 <= k - 2 < slots:
            step_back(k - 2)

    vec_out[...] = vec.finish(0)
    for s in range(slots):
        for d in range(1, owners):
            w_copy(s, d).wait()

    def block_step(b, carry):
        step = unfold(w_in[place_ref[b]].astype(full))
        block = blocks[b]
        new = block - matrix_rate * (step + weight_decay * block)
        new_ref[b] = new
        low_ref[b] = new.astype(low)
        return carry

    lax.fori_loop(0, count, block_step, 0)


class OptimizerPlan:
    def __init__(self, ready, dvecs, bases, spans, left_map, right_map, vector_rows):
        self.ready, self.dvecs, self.bases, self.spans = ready, dvecs, bases, spans
        self.left_map, self.right_map, self.vector_rows = left_map, right_map, vector_rows


def optimizer(
    index, places, tail, ready, dvecs, vector_rows, bases, lines, left_map, right_map, first, second, blocks, z_count,
    identity,
):
    slots, columns, width = first.shape
    owners = index.shape[0] // slots
    count, rows = blocks.shape[0], blocks.shape[1]
    span = bases[0].shape[2]
    lanes = 128
    shape = jax.ShapeDtypeStruct
    piece = (2 * rows, width // 2)
    tile = (span // 2, 2 * columns)
    smem = pl.BlockSpec(memory_space=pltpu.SMEM)
    plan = OptimizerPlan(
        len(ready), len(dvecs), len(bases), [(first_slot, amount) for _, first_slot, amount in lines],
        left_map, right_map, vector_rows,
    )
    line_shapes = [shape((z_count, amount) + basis.shape[1:], low) for basis, _, amount in lines]
    return pl.pallas_call(
        functools.partial(optimizer_kernel, plan),
        out_shape=(
            shape(blocks.shape, full), shape(blocks.shape, low), shape(first.shape, full), shape(first.shape, full),
            shape((rows, lanes), full), *line_shapes,
        ),
        in_specs=[smem, smem, ANYWHERE, ANYWHERE, ANYWHERE, IN_VMEM]
        + [IN_VMEM] * (len(ready) + len(dvecs)) + [ANYWHERE] * (len(bases) + len(lines)),
        out_specs=(IN_VMEM,) * 5 + (ANYWHERE,) * len(lines),
        scratch_shapes=[
            pltpu.VMEM((count + 1,) + piece, low),
            pltpu.VMEM((z_count, slots, span, width), low),
            pltpu.VMEM((z_count, slots, columns, width), low),
            pltpu.VMEM((slots, columns, width), full),
            pltpu.VMEM((slots, columns, width), full),
            pltpu.VMEM((slots, owners) + piece, low),
            pltpu.VMEM((slots, owners) + piece, low),
            pltpu.VMEM((slots, z_count) + tile, low),
            pltpu.VMEM((slots, z_count) + tile, low),
            pltpu.VMEM((slots, z_count) + tile, low),
            pltpu.VMEM((slots, z_count) + tile, low),
            pltpu.VMEM((slots, owners) + piece, low),
            pltpu.VMEM((slots * owners,) + piece, low),
            pltpu.VMEM((1, owners // 2, 2, width // owners, lanes), full),
            pltpu.SemaphoreType.DMA((2, slots)),
            pltpu.SemaphoreType.DMA((2, slots, owners)),
            pltpu.SemaphoreType.DMA((2, slots, z_count)),
            pltpu.SemaphoreType.DMA((2, slots, z_count)),
            pltpu.SemaphoreType.DMA((2, slots, owners)),
            pltpu.SemaphoreType.DMA((slots,)),
            pltpu.SemaphoreType.DMA((slots,)),
            *sum_scratch(tail.shape[0], tail.shape[3], width, z_count),
            *sum_scratch(1, width // owners, lanes, z_count, full),
            *line_scratch(len(lines), z_count),
        ],
        compiler_params=pltpu.CompilerParams(
            vmem_limit_bytes=60 * MIB, collective_id=identity, has_side_effects=True
        ),
        cost_estimate=pl.CostEstimate(
            flops=8 * slots * span * width * width, bytes_accessed=40 * MIB, transcendentals=slots * width * columns
        ),
        name="optimizer",
    )(index, places, tail, first, second, blocks, *ready, *dvecs, *bases, *[basis for basis, _, _ in lines])


def slot_table(owner, slots, owner_rows):
    block_count = owner.shape[0]
    same_owner = owner[:, None] == owner[None, :]
    ordering = jnp.arange(block_count, dtype=jnp.int32)
    earlier = ordering[None, :] < ordering[:, None]
    ranking = jnp.sum(jnp.where(same_owner & earlier, 1, 0), axis=1).astype(jnp.int32)
    owner_match = owner[None, :] == jnp.arange(owner_rows, dtype=jnp.int32)[:, None]
    slot_match = ranking[None, :] == jnp.arange(slots, dtype=jnp.int32)[:, None]
    return jnp.where(slot_match[:, None, :] & owner_match[None, :, :], 1.0, 0.0).astype(full)


def scatter_sum(grads):
    blocks, width = grads.shape[0], grads.shape[2]
    cut = grads.reshape(blocks, lax.axis_size("dp"), -1, width).transpose(1, 0, 2, 3)
    outer = lax.psum_scatter(cut, "dp", scatter_dimension=0, tiled=False)
    blocks, rows, width = outer.shape
    count = lax.axis_size("fsdp")
    cut = outer.reshape(blocks, count, rows // count, width).transpose(1, 0, 2, 3)
    return lax.psum_scatter(cut, "fsdp", scatter_dimension=0, tiled=False)


def scatter_vectors(grads):
    rows, width = grads.shape
    count = lax.axis_size("dp") * lax.axis_size("fsdp")
    cut = grads.reshape(rows, count, width // count).transpose(1, 0, 2)
    return lax.psum_scatter(cut, ("dp", "fsdp"), scatter_dimension=0, tiled=False)


def gathering_program(
    tokens, segment, blocks, vectors, owner, left_basis, right_basis, rot_first, rot_second, cotangent, z_count
):
    layers, vector_rows = vectors.shape[:2]
    count, shard_rows, width = blocks.shape
    per_layer = count // layers
    inner = (per_layer - 4) // 2
    owners = lax.axis_size("dp")
    slots = rot_first.shape[0]
    part = width // owners
    lanes = 128
    seg_column, seg_row = segment[:, :, None], segment[:, None, :]

    order = [0, 1, 2, 3]
    for c in range(inner):
        order += [4 + c, 4 + inner + c]
    folded = blocks.astype(low).reshape(count, shard_rows, 2, width // 2).transpose(0, 2, 1, 3)
    folded = folded.reshape(count, 2 * shard_rows, width // 2)

    def pick(numbers):
        return jnp.stack([folded[j] for j in numbers])

    head = pick(order + [per_layer + j for j in order[:4]])
    rest = pick([per_layer + j for j in order[4:]])
    vec_shard = vectors.astype(low).astype(full).reshape(layers * vector_rows, shard_rows).T
    vec_shard = jnp.pad(vec_shard, ((0, 0), (0, lanes - layers * vector_rows)))[None]
    left_low = left_basis.reshape(slots, -1, width).astype(low)
    right_low = right_basis.transpose(0, 2, 1).astype(low)

    plan = ForwardPlan(
        inner, 0, head, vec_shard, vector_rows, [(right_low, 0, 2)], lead=9, row_ticks=3, z_count=z_count
    )
    empty_vec = jnp.zeros((16, width), full)
    results = forward_layer(tokens, seg_column, seg_row, empty_vec, head, full, plan, 6)
    kept_a = results[:12]
    hidden, weights_a, vec_a, vec_b, right_01 = results[12:]
    plan = ForwardPlan(inner, 4, rest, lines=[(right_low, 2, 1)], lead=0, row_ticks=4, z_count=z_count)
    plan.order = [per_layer + j for j in range(4)]
    results = forward_layer(hidden, seg_column, seg_row, vec_b, weights_a, low, plan, 7)
    kept_b = results[:12]
    layer_out, weights_b, right_2 = results[12:]

    def cut(grads):
        return grads.reshape(-1, owners // 2, 2, part, width)

    size = (part, width)
    own = 2 * (inner // 2)

    def wide_at(pending):
        def at(t):
            mine = 2 * (lax.div(t, 4) - 1) + lax.rem(t, 4)
            is_mine = (t >= 4) & (lax.rem(t, 4) < 2) & (mine < own)
            return ((t >= 0) & (t < pending)) | is_mine, jnp.where(t >= 4, pending + mine, t)

        return at

    def attend_at(t):
        return (t >= 0) & (lax.rem(t, 2) == 0) & (t < 2 * (2 * inner - own + 1)), lax.div(t, 2)

    plan = Plan(None, [(right_low, 3, 2)], z_count, own, size, wide_at(0))
    dw_wide, dr1, da, dvec_wide_b, wide_sum_b, right_34 = wide_back(
        cotangent, kept_b[5:], vec_b, weights_b, (0, 1, 2), plan, 1
    )
    plan = Plan(cut(dw_wide), [(left_low, 0, 1)], z_count, 1, size, attend_at)
    dw_attend, upstream, dvec_attend_b, attend_sum_b, left_0 = attend_back(
        da, dr1, hidden, kept_b[:5], seg_column, seg_row, weights_a, per_layer // 4, plan, 2
    )
    plan = Plan(cut(dw_attend), [(left_low, 1, 1)], z_count, own, size, wide_at(3))
    dw_wide, dr1, da, dvec_wide_a, wide_sum_a, left_1 = wide_back(
        upstream, kept_a[5:], vec_a, weights_a, (4, 5, 2), plan, 3
    )
    plan = Plan(cut(dw_wide), [(left_low, 2, 1)], z_count, 1, size, attend_at)
    dw_attend, upstream, dvec_attend_a, attend_sum_a, left_2 = attend_back(
        da, dr1, tokens, kept_a[:5], seg_column, seg_row, weights_a, 0, plan, 5
    )

    three = list(range(3))
    early = [4 + c + inner * k for c in range(own // 2) for k in range(2)]
    late = [4 + c + inner * k for k in range(2) for c in range(own // 2, inner)] + [3]
    held_order = three + late + [per_layer + j for j in three] + early + [per_layer + j for j in late + early]
    rank = jnp.asarray([held_order.index(j) for j in range(count)], jnp.int32)
    table = slot_table(owner, slots, owners).reshape(slots * owners, count)
    held = jnp.sum(table, axis=1)
    index = jnp.where(held > 0, jnp.sum(table * rank, axis=1), count).astype(jnp.int32)
    places = jnp.sum(table * jnp.arange(slots * owners, dtype=jnp.int32)[:, None], axis=0).astype(jnp.int32)
    bases = (right_01, right_2, right_34, left_0, left_1, left_2)
    right_map = [(0, 0), (0, 1), (1, 0), (2, 0), (2, 1)]
    left_map = [(3, 0), (4, 0), (5, 0), (6, 0), (6, 1)]
    new_blocks, new_low, first_new, second_new, vec_sum, _ = optimizer(
        index, places, cut(dw_attend), (attend_sum_a, wide_sum_a, attend_sum_b, wide_sum_b),
        (dvec_attend_a, dvec_wide_a, dvec_attend_b, dvec_wide_b), vector_rows, bases, [(left_low, 3, 2)], left_map, right_map,
        rot_first.transpose(0, 2, 1), rot_second.transpose(0, 2, 1), blocks, z_count, 4,
    )
    first_new, second_new = first_new.transpose(0, 2, 1), second_new.transpose(0, 2, 1)
    vector_grad = vec_sum[:, : layers * vector_rows].T.reshape(layers, vector_rows, shard_rows)
    return layer_out, upstream, new_blocks, new_low, first_new, second_new, vector_grad


def plain_program(
    tokens, segment, blocks, vectors, owner, left_basis, right_basis, rot_first, rot_second, cotangent
):
    layers, vector_rows = vectors.shape[:2]
    per_layer = blocks.shape[0] // layers
    inner = (per_layer - 4) // 2
    width = blocks.shape[2]
    owner_rows = lax.axis_size("dp")
    slots = rot_first.shape[0]
    selector = slot_table(owner, slots, owner_rows)
    vector_parts = lax.all_gather(vectors.astype(low), ("dp", "fsdp"), axis=0, tiled=False)
    vector_full = vector_parts.transpose(1, 2, 0, 3).reshape(layers, vector_rows, width).astype(full)
    blocks_low, vector_full = lax.optimization_barrier((blocks.astype(low), vector_full))

    seg_column = segment[:, :, None]
    seg_row = segment[:, None, :]
    state = tokens
    kept = []
    for layer_index in range(layers):
        start = per_layer * layer_index
        weights = lax.all_gather(blocks_low[start : start + per_layer], ("dp", "fsdp"), axis=1, tiled=True)
        out_dtype = low if layer_index == layers - 1 else full
        results = forward_layer(
            state, seg_column, seg_row, vector_full[layer_index], weights, out_dtype, ForwardPlan(inner, per_layer)
        )
        kept.append((state, weights, results[:5], results[5:12]))
        state = results[12]
    layer_out = state
    upstream = cotangent
    right_low = lax.all_gather(right_basis.astype(low), "fsdp", axis=2, tiled=True)
    block_shards = [None] * layers
    vector_shards = [None] * layers
    for layer_index in reversed(range(layers)):
        hidden, weights, attend_kept, wide_kept = kept[layer_index]
        dw_wide, dr1, da, dvec_wide = wide_back(
            upstream, wide_kept, vector_full[layer_index], weights, (4, 4 + inner, 1), Plan()
        )
        wide_shard = scatter_sum(dw_wide.reshape(-1, width, width))
        dw_attend, upstream, dvec_attend = attend_back(
            da, dr1, hidden, attend_kept, seg_column, seg_row, weights, 0, Plan()
        )
        dvec = jnp.concatenate([dvec_attend[:2], dvec_wide[2:vector_rows]], axis=0)
        block_shards[layer_index] = jnp.concatenate([scatter_sum(dw_attend), wide_shard], axis=0)
        vector_shards[layer_index] = scatter_vectors(dvec)
    vector_grad = jnp.stack(vector_shards)
    block_grad = jnp.concatenate(block_shards, axis=0)
    outgoing = jnp.einsum("srk,kid->srid", selector.astype(low), block_grad, preferred_element_type=full)
    incoming = lax.all_to_all(outgoing.astype(low), "dp", split_axis=1, concat_axis=1, tiled=True)
    owned = incoming.reshape(slots, -1, width)
    turned = jnp.einsum("sik,skj->sij", owned, right_low, preferred_element_type=full).astype(low)
    left_rows = left_basis.reshape(slots, -1, width).astype(low)
    partial_sums = jnp.einsum("sra,srb->sab", left_rows, turned, preferred_element_type=full)
    rotated = lax.psum_scatter(
        partial_sums.astype(low), "fsdp", scatter_dimension=2, tiled=True
    ).astype(full)
    first_new, second_new, direction = moments(rotated, rot_first, rot_second)
    direction_full = lax.all_gather(direction.astype(low), "fsdp", axis=2, tiled=True)
    back_right = jnp.einsum("sab,scb->sac", direction_full, right_low, preferred_element_type=full)
    step_rows = jnp.einsum(
        "sia,sac->sic", left_rows, back_right.astype(low), preferred_element_type=full
    )
    returned = lax.all_to_all(
        step_rows.reshape(slots, owner_rows, -1, width).astype(low),
        "dp",
        split_axis=1,
        concat_axis=1,
        tiled=True,
    )
    step_shard = jnp.einsum("srk,srid->kid", selector.astype(low), returned, preferred_element_type=full)
    new_blocks = blocks - matrix_rate * (step_shard + weight_decay * blocks)
    return layer_out, upstream, new_blocks, new_blocks.astype(low), first_new, second_new, vector_grad


def shards(
    tokens,
    segment,
    blocks,
    vectors,
    owner,
    left_basis,
    right_basis,
    rot_first,
    rot_second,
    vec_first,
    vec_second,
    cotangent,
):
    operands = (
        tokens, segment, blocks, vectors, owner, left_basis, right_basis, rot_first, rot_second, cotangent
    )
    z_count = lax.axis_size("fsdp")
    if lax.axis_size("dp") == 8 and z_count == 4:
        results = gathering_program(*operands, z_count)
    else:
        results = plain_program(*operands)
    layer_out, upstream, new_blocks, new_low, first_new, second_new, vector_grad = results
    vector_first = beta_one * vec_first + (1.0 - beta_one) * vector_grad
    vector_second = beta_two * vec_second + (1.0 - beta_two) * vector_grad * vector_grad
    vector_step = (
        vector_first
        / (1.0 - beta_one**STEP)
        / (jnp.sqrt(vector_second / (1.0 - beta_two**STEP)) + adam_epsilon)
    )
    vector_new = vectors - vector_rate * (vector_step + weight_decay * vectors)
    return (
        layer_out,
        upstream,
        new_blocks,
        new_low,
        first_new,
        second_new,
        vector_first,
        vector_second,
        vector_new,
    )


def solution(mesh):
    return jax.shard_map(
        shards,
        mesh=mesh,
        in_specs=(
            P(("dp", "fsdp"), None),
            P(("dp", "fsdp"), None),
            P(None, ("dp", "fsdp"), None),
            P(None, None, ("dp", "fsdp")),
            P(),
            P("dp", None, "fsdp", None),
            P("dp", None, "fsdp"),
            P("dp", None, "fsdp"),
            P("dp", None, "fsdp"),
            P(None, None, ("dp", "fsdp")),
            P(None, None, ("dp", "fsdp")),
            P(("dp", "fsdp"), None),
        ),
        out_specs=(
            P(("dp", "fsdp"), None),
            P(("dp", "fsdp"), None),
            P(None, ("dp", "fsdp"), None),
            P(None, ("dp", "fsdp"), None),
            P("dp", None, "fsdp"),
            P("dp", None, "fsdp"),
            P(None, None, ("dp", "fsdp")),
            P(None, None, ("dp", "fsdp")),
            P(None, None, ("dp", "fsdp")),
        ),
        check_vma=False,
    )
```

```python
import functools

import jax
import jax.numpy as jnp
from jax import lax
from jax.experimental import pallas as pl
from jax.experimental.pallas import tpu as pltpu
from jax.sharding import PartitionSpec as P

H = 12
HD = 64
L = 512
STEP = 5
PAIR = 2 * HD
MIB = 1 << 20

beta_one = 0.5
beta_two = 0.5
adam_epsilon = 1e-08
norm_epsilon = 1e-06
matrix_rate = 0.03
vector_rate = 0.2
weight_decay = 0.01
masked_score = -1e30
low = jnp.bfloat16
full = jnp.float32


def dot_nn(a, b):
    return lax.dot_general(a, b, (((1,), (0,)), ((), ())), preferred_element_type=full)


def dot_nt(a, b):
    return lax.dot_general(a, b, (((1,), (1,)), ((), ())), preferred_element_type=full)


def dot_tn(a, b):
    return lax.dot_general(a, b, (((0,), (0,)), ((), ())), preferred_element_type=full)


def gelu_parts(z):
    size = jnp.abs(z) * 0.7071067811865476
    t = 1.0 / (1.0 + 0.3275911 * size)
    bell = jnp.exp(-0.5 * z * z)
    poly = ((((1.061405429 * t - 1.453152027) * t + 1.421413741) * t - 0.284496736) * t + 0.254829592) * t
    half_tail = 0.5 * poly * bell
    phi = jnp.where(z >= 0, 1.0 - half_tail, half_tail)
    return z * phi, phi + z * bell * 0.3989422804014327


def norm_parts(residual):
    average = jnp.mean(residual, axis=-1, keepdims=True)
    centered = residual - average
    inverse = lax.rsqrt(jnp.mean(centered * centered, axis=-1, keepdims=True) + norm_epsilon)
    return centered * inverse, inverse


def norm_back(upstream, unit, inverse, gain):
    scaled = upstream * gain
    return inverse * (
        scaled
        - jnp.mean(scaled, axis=-1, keepdims=True)
        - unit * jnp.mean(scaled * unit, axis=-1, keepdims=True)
    )


def column_sum(values):
    return jnp.sum(values, axis=0, keepdims=True)


def half_masks(dtype):
    lane = lax.broadcasted_iota(jnp.int32, (1, PAIR), 1)
    first = (lane < HD).astype(full)
    return first.astype(dtype), (1.0 - first).astype(dtype)


def segment_bias(seg_column, seg_row):
    return jnp.where(seg_column == seg_row, 0.0, masked_score)


class Place:
    def __init__(self, z_count):
        self.dp, self.z = lax.axis_index("dp"), lax.axis_index("fsdp")
        self.core, self.spot = lax.rem(self.dp, 2), lax.div(self.dp, 2)
        x_step = 1 - 2 * lax.rem(self.spot, 2)
        y_step = 2 - 4 * lax.div(self.spot, 2)
        self.spot_a = self.spot + (1 - self.core) * x_step + self.core * y_step
        self.spot_b = self.spot + self.core * x_step + (1 - self.core) * y_step
        self.spot_ab = self.spot + x_step + y_step
        self.sibling = (self.dp + 1 - 2 * self.core, self.z)
        self.near_a = (2 * self.spot_a + self.core, self.z)
        self.near_b = (2 * self.spot_b + self.core, self.z)
        self.z_count = z_count
        self.zs = [lax.rem(self.z + d, z_count) for d in range(z_count)]

    def chip_partners(self):
        return [self.sibling, self.near_a, self.near_b]

    def z_partners(self):
        return [(self.dp, other) for other in self.zs[1:]]


def greet(partners):
    barrier = pltpu.get_barrier_semaphore()
    for device in partners:
        pl.semaphore_signal(barrier, inc=1, device_id=device, device_id_type=pl.DeviceIdType.MESH)
    pl.semaphore_wait(barrier, len(partners))


def remote(source, target, send, receive, device):
    return pltpu.make_async_remote_copy(
        src_ref=source,
        dst_ref=target,
        send_sem=send,
        recv_sem=receive,
        device_id=device,
        device_id_type=pl.DeviceIdType.MESH,
    )


def fold(piece):
    half = piece.shape[1] // 2
    return jnp.concatenate([piece[:, :half], piece[:, half:]], axis=0)


def unfold(piece):
    rows = piece.shape[0] // 2
    return jnp.concatenate([piece[:rows], piece[rows:]], axis=1)


def sum_scratch(count, part, width, z_count, kind=low):
    piece = (2 * part // z_count, width // 2) if kind == low else (part // z_count, width)
    return [
        pltpu.VMEM((4, 4, part, width), kind),
        pltpu.VMEM((count, 4, part, width), kind),
        pltpu.VMEM((count, 2, part, width), kind),
        pltpu.VMEM((count, part, width), kind),
        pltpu.VMEM((count, z_count) + piece, kind),
        pltpu.VMEM((count, z_count) + piece, kind),
        pltpu.SemaphoreType.DMA((4,)),
        pltpu.SemaphoreType.DMA((count, 2)),
        pltpu.SemaphoreType.DMA((count, 2, 2)),
        pltpu.SemaphoreType.DMA((count, 2)),
        pltpu.SemaphoreType.DMA((count, 2, z_count)),
    ]


SUM_REFS = 11


class BlockSum:
    def __init__(self, place, sources, refs, at=None):
        self.place, self.sources = place, sources
        self.at = at or (lambda t: ((t >= 0) & (t < self.count), t))
        (self.own, self.c, self.b, self.a, self.zs, self.zr,
         self.own_sem, self.c_sem, self.b_sem, self.a_sem, self.z_sem) = refs
        self.count = self.c.shape[0]
        self.kind = self.c.dtype
        self.z_count = self.zs.shape[1]

    def load(self, i, block):
        slot = lax.rem(i, 4)
        return pltpu.make_async_copy(block.at[:, self.place.core], self.own.at[slot], self.own_sem.at[slot])

    def core_copy(self, i, block):
        return remote(
            block.at[:, 1 - self.place.core], self.c.at[i], self.c_sem.at[i, 0], self.c_sem.at[i, 1], self.place.sibling
        )

    def second_copy(self, i, k):
        chunk = self.place.spot_b if k == 0 else self.place.spot_ab
        return remote(
            self.c.at[i, chunk], self.b.at[i, k], self.b_sem.at[i, 0, k], self.b_sem.at[i, 1, k], self.place.near_b
        )

    def third_copy(self, i):
        return remote(
            self.c.at[i, self.place.spot_a], self.a.at[i], self.a_sem.at[i, 0], self.a_sem.at[i, 1], self.place.near_a
        )

    def z_copy(self, i, d):
        other = self.place.zs[d]
        return remote(
            self.zs.at[i, other], self.zr.at[i, self.place.z], self.z_sem.at[i, 0, d],
            self.z_sem.at[i, 1, self.z_count - d], (self.place.dp, other),
        )

    def open(self, i):
        first = 0
        for source in self.sources:
            count = source.shape[0]

            @pl.when((i >= first) & (i < first + count))
            def _():
                block = source.at[jnp.clip(i - first, 0, count - 1)]
                self.core_copy(i, block).start()
                self.load(i, block).start()

            first += count

    def after_core(self, i):
        block = self.sources[0].at[0]
        self.core_copy(i, block).wait()
        self.load(i, block).wait()
        slot = lax.rem(i, 4)
        for k in range(4):
            self.c[i, k] = (self.c[i, k].astype(full) + self.own[slot, k].astype(full)).astype(self.kind)
        self.second_copy(i, 0).start()
        self.second_copy(i, 1).start()

    def after_second(self, i):
        other, spot = self.place.spot_a, self.place.spot
        self.second_copy(i, 1).wait()
        self.c[i, other] = (self.c[i, other].astype(full) + self.b[i, 1].astype(full)).astype(self.kind)
        self.third_copy(i).start()
        self.second_copy(i, 0).wait()
        self.c[i, spot] = (self.c[i, spot].astype(full) + self.b[i, 0].astype(full)).astype(self.kind)

    def after_third(self, i):
        self.third_copy(i).wait()
        total = self.c[i, self.place.spot].astype(full) + self.a[i].astype(full)
        rows = total.shape[0] // self.z_count
        for k in range(self.z_count):
            piece = total[k * rows : (k + 1) * rows]
            self.zs[i, k] = fold(piece).astype(low) if self.kind == low else piece
        for d in range(1, self.z_count):
            self.z_copy(i, d).start()

    def finish(self, i):
        for d in range(1, self.z_count):
            self.z_copy(i, d).wait()
        total = self.zs[i, self.place.z].astype(full)
        for d in range(1, self.z_count):
            total = total + self.zr[i, self.place.zs[d]].astype(full)
        return total

    def tick(self, t):
        for late, stage in ((6, self.after_third), (4, self.after_second), (2, self.after_core), (0, self.open)):
            now, block = self.at(t - late)

            @pl.when(now)
            def _():
                stage(block)


class LineGather:
    def __init__(self, place, source, target, first, local_sem, sem, z_count):
        self.place = place
        self.source = source.at[pl.ds(first, target.shape[1])]
        self.target, self.local_sem, self.sem, self.z_count = target, local_sem, sem, z_count

    def hop_copy(self, hop, way):
        dp, z = self.place.dp, self.place.z
        if way == 0:
            piece, other, coming = z - hop + 1, z + 1, z - hop
            sends = (piece >= 0) & (other < self.z_count)
            receives = coming >= 0
        else:
            piece, other, coming = z + hop - 1, z - 1, z + hop
            sends = (piece < self.z_count) & (other >= 0)
            receives = coming < self.z_count
        piece = jnp.clip(piece, 0, self.z_count - 1)
        other = jnp.clip(other, 0, self.z_count - 1)
        source = self.source if hop == 1 else self.target.at[piece]
        copy = remote(source, self.target.at[piece], self.sem.at[way, 0, hop - 1], self.sem.at[way, 1, hop - 1], (dp, other))
        return copy, sends, receives

    def local(self):
        return pltpu.make_async_copy(self.source, self.target.at[self.place.z], self.local_sem)

    def start(self, hop):
        if hop == 1:
            self.local().start()
        for way in range(2):
            copy, sends, _ = self.hop_copy(hop, way)

            @pl.when(sends)
            def _():
                copy.start()

    def wait(self, hop):
        if hop == 1:
            self.local().wait()
        for way in range(2):
            copy, sends, receives = self.hop_copy(hop, way)

            @pl.when(sends)
            def _():
                copy.wait_send()

            @pl.when(receives)
            def _():
                copy.wait_recv()

    def advance(self, hop):
        if hop > 1:
            self.wait(hop - 1)
        if hop < self.z_count:
            self.start(hop)


def gather_scratch(count, rows, width, z_count, kind=low):
    piece = (2 * rows // z_count, width // 2) if kind == low else (rows // z_count, width)
    return [
        pltpu.VMEM((count, z_count) + piece, kind),
        pltpu.SemaphoreType.DMA((count, 2, z_count)),
        pltpu.SemaphoreType.DMA((count, 2)),
        pltpu.SemaphoreType.DMA((count, 2, 2)),
        pltpu.SemaphoreType.DMA((count, 2)),
    ]


GATHER_REFS = 5


class BlockGather:
    def __init__(self, place, source, whole, base, refs):
        self.place, self.source, self.whole, self.base = place, source, whole, base
        self.zr, self.z_sem, self.a_sem, self.b_sem, self.c_sem = refs
        self.count, self.z_count = self.zr.shape[0], self.zr.shape[1]

    def z_copy(self, i, d):
        place = self.place
        return remote(
            self.source.at[i], self.zr.at[i, place.z], self.z_sem.at[i, 0, d], self.z_sem.at[i, 1, self.z_count - d],
            (place.dp, place.zs[d]),
        )

    def chunk(self, i, spot):
        return self.whole.at[self.base + i, spot, self.place.core]

    def first_copy(self, i):
        chunk = self.chunk(i, self.place.spot)
        return remote(chunk, chunk, self.a_sem.at[i, 0], self.a_sem.at[i, 1], self.place.near_a)

    def second_copy(self, i, k):
        chunk = self.chunk(i, self.place.spot if k == 0 else self.place.spot_a)
        return remote(chunk, chunk, self.b_sem.at[i, 0, k], self.b_sem.at[i, 1, k], self.place.near_b)

    def core_copy(self, i):
        chunks = self.whole.at[self.base + i, :, self.place.core]
        return remote(chunks, chunks, self.c_sem.at[i, 0], self.c_sem.at[i, 1], self.place.sibling)

    AHEAD = 3

    def announce(self, i):
        for d in range(1, self.z_count):
            self.z_copy(i, d).start()
        self.zr[i, self.place.z] = self.source[i]

    def begin(self):
        for i in range(min(self.AHEAD, self.count)):
            self.announce(i)

    def open(self, i):
        for d in range(1, self.z_count):
            self.z_copy(i, d).wait()
        pieces = [self.zr[i, k].astype(full) for k in range(self.z_count)]
        if self.zr.dtype == low:
            pieces = [unfold(piece) for piece in pieces]
        whole = jnp.concatenate(pieces, axis=0).astype(self.whole.dtype)
        self.whole[self.base + i, self.place.spot, self.place.core] = whole
        self.first_copy(i).start()
        self.second_copy(i, 0).start()

    def after_first(self, i):
        self.first_copy(i).wait()
        self.second_copy(i, 1).start()

    def after_second(self, i):
        self.second_copy(i, 0).wait()
        self.second_copy(i, 1).wait()
        self.core_copy(i).start()

    def close(self, i):
        self.core_copy(i).wait()

    def tick(self, t, done=None):
        @pl.when(t + self.AHEAD < self.count)
        def _():
            self.announce(t + self.AHEAD)

        for late, stage in ((4, self.after_second), (2, self.after_first), (0, self.open), (6, self.close)):
            @pl.when((t >= late) & (t < self.count + late))
            def _():
                stage(t - late)
                if late == 6 and done is not None:
                    done(t - late)


def split_refs(refs, *counts):
    result, start = [], 0
    for count in counts:
        result.append(refs[start : start + count])
        start += count
    return result


class Side:
    def __init__(self, plan, sources, targets, sum_refs, line_refs, own=None):
        self.plan = plan
        sums = plan.sums
        blocks = list(sources[:sums]) + ([own] if plan.own else [])
        self.place = Place(plan.z_count) if plan.active else None
        self.sum = BlockSum(self.place, blocks, sum_refs, plan.at) if plan.total else None
        self.result = targets[0] if plan.total else None
        self.lines = line_gathers(self.place, plan.lines, sources[sums:], targets[bool(plan.total) :], line_refs, plan.z_count)

    def enter(self, now):
        if not self.plan.active:
            return

        @pl.when(now)
        def _():
            greet((self.place.chip_partners() if self.plan.total else []) + self.place.z_partners())
            for line in self.lines:
                line.advance(1)

    def leave(self, now):
        if not self.plan.active:
            return

        @pl.when(now)
        def _():
            if self.plan.total:
                for i in range(self.sum.count):
                    self.result[i] = self.sum.finish(i).astype(low)
            for line in self.lines:
                line.advance(self.plan.z_count)

    def advance(self, now, hop):
        if self.lines and hop < self.plan.z_count:
            @pl.when(now)
            def _():
                for line in self.lines:
                    line.advance(hop)


class Plan:
    def __init__(self, pending=None, lines=(), z_count=1, own=0, size=None, at=None):
        self.z_count = z_count
        self.sums = int(pending is not None)
        self.own, self.at = own, at
        self.total = own + (pending.shape[0] if self.sums else 0)
        self.lines = [(first, count) for _, first, count in lines]
        self.active = bool(self.total or lines)
        self.arguments, self.results, self.result_specs, self.scratch = [], [], [], []
        if self.sums:
            self.arguments.append(pending)
        if self.total:
            part, width = size
            self.results.append(jax.ShapeDtypeStruct((self.total, 2 * part // z_count, width // 2), low))
            self.result_specs.append(
                pl.BlockSpec(self.results[0].shape, lambda i: (0, 0, 0), pipeline_mode=pl.Buffered(1))
            )
            self.scratch += sum_scratch(self.total, part, width, z_count)
        for basis, _, count in lines:
            self.arguments.append(basis)
            self.results.append(jax.ShapeDtypeStruct((z_count, count) + basis.shape[1:], low))
            self.result_specs.append(ANYWHERE)
        self.scratch += line_scratch(len(lines), z_count)
        self.argument_specs = [ANYWHERE] * len(self.arguments)

    def split(self, refs, inputs, outputs, scratch):
        count = len(self.lines)
        return split_refs(
            refs, inputs, self.sums + count, outputs, bool(self.total) + count, scratch,
            SUM_REFS * bool(self.total), 2 * bool(self.lines),
        )


def line_scratch(count, z_count):
    if not count:
        return []
    return [pltpu.SemaphoreType.DMA((count,)), pltpu.SemaphoreType.DMA((count, 2, 2, z_count - 1))]


def line_gathers(place, spans, sources, targets, refs, z_count):
    return [
        LineGather(place, source, target, first, refs[0].at[n], refs[1].at[n], z_count)
        for n, (source, target, (first, _)) in enumerate(zip(sources, targets, spans))
    ]


ANYWHERE = pl.BlockSpec(memory_space=pl.ANY)
IN_VMEM = pl.BlockSpec(memory_space=pltpu.VMEM)


def forward_kernel(plan, *refs):
    inputs, sources, outputs, targets, scratch, gather_refs, vec_refs, line_refs = plan.split(refs)
    x_ref, segc_ref, segr_ref, vec_ref, w_hbm = inputs
    (q_ref, k_ref, v_ref, ctxt_ref, lse_ref, x1_ref, inv1_ref, n1_ref, u_ref, gp_ref, x2_ref, inv2_ref,
     out_ref) = outputs
    w, bias, vt, n1_all, acc, w_sem = scratch
    s = pl.program_id(0)
    tokens, width = acc.shape
    rows_now = x_ref.shape[0]
    rows = tokens // rows_now
    inner = plan.inner
    local = plan.local
    gather = vec_gather = None
    place = Place(plan.z_count) if plan.gathered else None
    if plan.gathered:
        w_out, out_sem = targets[0], scratch_tail(plan, refs)
        gather = BlockGather(place, sources[0], w, local, gather_refs)
        if plan.vectors:
            vec_gather = BlockGather(place, sources[1], plan.vec_whole(refs), 0, vec_refs)
            vec_ref = targets[1]
    lines = line_gathers(place, plan.lines, sources[plan.line_at :], targets[plan.line_target_at :], line_refs, plan.z_count)

    def keep(i):
        return pltpu.make_async_copy(w.at[local + i], w_out.at[i], out_sem.at[i])

    def load(j):
        return pltpu.make_async_copy(w_hbm.at[plan.order[j]], w.at[j], w_sem.at[j])

    def matrix(j):
        return w[j].reshape(width, width)

    def arrive(j):
        if j < local:
            load(j).wait()

    def tick(t):
        if gather is not None:
            gather.tick(t, lambda i: keep(i).start())
            if vec_gather is not None:
                vec_gather.tick(t)

    @pl.when(s == 0)
    def _():
        for j in range(local):
            load(j).start()
        if gather is not None:
            greet(place.chip_partners() + place.z_partners())
            if vec_gather is not None:
                vec_gather.begin()
            gather.begin()
            lax.fori_loop(0, plan.lead, lambda t, carry: (tick(t), carry)[1], 0)
            for line in lines:
                line.advance(1)
            if vec_gather is not None:
                turned = vec_gather.whole[0].reshape(width, vec_gather.whole.shape[-1]).T
                for layer in range(2):
                    count = plan.vector_rows
                    targets[1 + layer][0:count, :] = turned[layer * count : (layer + 1) * count, :]
        for j in range(min(local, 3)):
            arrive(j)

    @pl.when(s < rows)
    def _():
        xin = x_ref[...].astype(low)
        bias[...] = segment_bias(segc_ref[0], segr_ref[0])
        q_ref[...] = (dot_nn(xin, matrix(0)) + vec_ref[0:1, :]).astype(low)
        k_ref[...] = dot_nn(xin, matrix(1)).astype(low)
        value = dot_nn(xin, matrix(2)) + vec_ref[1:2, :]
        v_ref[...] = value.astype(low)
        vt[...] = value.T.astype(low)
        masks = half_masks(low)
        pairs = width // PAIR

        def pair_step(p, carry):
            lanes = pl.ds(pl.multiple_of(p * PAIR, PAIR), PAIR)
            q_pair = q_ref[:, lanes] * jnp.asarray(HD ** (-0.5), low)
            k_pair = k_ref[:, lanes]
            for h in range(2):
                scores = dot_nt(k_pair, q_pair * masks[h]) + bias[...]
                largest = jnp.max(scores, axis=0, keepdims=True)
                expanded = jnp.exp(scores - largest)
                total = column_sum(expanded)
                here = pl.ds(pl.multiple_of(p * PAIR + h * HD, HD), HD)
                context = dot_nn(vt[here, :], expanded.astype(low)) * (1.0 / total)
                ctxt_ref[here, :] = context.astype(low)
                lse_ref[0, pl.ds(2 * p + h, 1), :] = largest + jnp.log(total)
            if plan.gathered:
                many = plan.row_ticks
                spots = [p_now for p_now in range(pairs) if (p_now + 1) * many // pairs > p_now * many // pairs]
                now = functools.reduce(jnp.logical_or, [p == spot for spot in spots])

                @pl.when(now)
                def _():
                    passed = sum((p > spot).astype(jnp.int32) for spot in spots)
                    tick(plan.lead + s * many + passed)
            return carry

        lax.fori_loop(0, pairs, pair_step, 0)

        @pl.when(s == 0)
        def _():
            if local > 3:
                arrive(3)
            for line in lines:
                line.advance(2)

        context = ctxt_ref[...].astype(full).T.astype(low)
        attended = dot_nn(context, matrix(3)) + vec_ref[2:3, :]
        unit, inverse = norm_parts(x_ref[...].astype(full) + attended)
        x1_ref[...] = unit
        inv1_ref[...] = inverse
        normed = unit * vec_ref[3:4, :] + vec_ref[4:5, :]
        here = pl.ds(pl.multiple_of(s * rows_now, rows_now), rows_now)
        acc[here, :] = normed + vec_ref[5 + inner : 6 + inner, :]
        normed = normed.astype(low)
        n1_ref[...] = normed
        n1_all[here, :] = normed

    tile = tokens // 4
    after = plan.lead + rows * plan.row_ticks

    @pl.when(s >= rows)
    def _():
        c = s - rows

        @pl.when(c == 0)
        def _():
            for j in range(4, local):
                arrive(j)
            for line in lines:
                line.advance(3)

        def token_step(i, carry):
            for half in range(2):
                here = pl.ds(pl.multiple_of((2 * i + half) * tile, tile), tile)
                value, slope = gelu_parts(dot_nn(n1_all[here, :], matrix(4 + 2 * c)) + vec_ref[pl.ds(5 + c, 1), :])
                active = value.astype(low)
                u_ref[here, :] = active
                gp_ref[here, :] = slope.astype(low)
                acc[here, :] += dot_nn(active, matrix(5 + 2 * c))
            tick(after + 2 * c + i)
            return carry

        lax.fori_loop(0, 2, token_step, 0)

        @pl.when(c == inner - 1)
        def _():
            base = 5 + inner

            def last(i, carry):
                here = pl.ds(pl.multiple_of(i * tile, tile), tile)
                unit, inverse = norm_parts(acc[here, :])
                x2_ref[here, :] = unit
                inv2_ref[here, :] = inverse
                out_ref[here, :] = (
                    unit * vec_ref[base + 1 : base + 2, :] + vec_ref[base + 2 : base + 3, :]
                ).astype(out_ref.dtype)
                return carry

            lax.fori_loop(0, 4, last, 0)
            if gather is not None:
                for t in range(after + 2 * inner, gather.count + 6):
                    tick(t)
                for line in lines:
                    line.advance(plan.z_count)
                for i in range(gather.count):
                    keep(i).wait()


class ForwardPlan:
    def __init__(self, inner, local, shards=None, vec_shard=None, vector_rows=0, lines=(), lead=0, row_ticks=1, z_count=1):
        self.inner, self.local, self.lead, self.row_ticks, self.z_count = inner, local, lead, row_ticks, z_count
        self.vector_rows = vector_rows
        self.order = [0, 1, 2, 3]
        for c in range(inner):
            self.order += [4 + c, 4 + inner + c]
        self.gathered = 0 if shards is None else shards.shape[0]
        self.vectors = vec_shard is not None
        self.lines = [(first, count) for _, first, count in lines]
        self.line_at = int(self.gathered > 0) + int(self.vectors)
        self.line_target_at = int(self.gathered > 0) + 2 * int(self.vectors)
        self.arguments, self.argument_specs, self.results, self.result_specs, self.scratch = [], [], [], [], []
        shape = jax.ShapeDtypeStruct
        if self.gathered:
            width = 2 * shards.shape[2]
            self.arguments.append(shards)
            self.argument_specs.append(IN_VMEM)
            self.results.append(shape((self.gathered, 4, 2, width // 8, width), low))
            self.result_specs.append(ANYWHERE)
            self.scratch += gather_scratch(self.gathered, width // 8, width, z_count)
        if self.vectors:
            rows, lanes = vec_shard.shape[1:]
            self.arguments.append(vec_shard)
            self.argument_specs.append(IN_VMEM)
            for _ in range(2):
                self.results.append(shape((16, width), full))
                self.result_specs.append(pl.BlockSpec((16, width), lambda s: (0, 0)))
            self.scratch += gather_scratch(1, width // 8, lanes, z_count, full)
        for basis, _, count in lines:
            self.arguments.append(basis)
            self.argument_specs.append(ANYWHERE)
            self.results.append(shape((z_count, count) + basis.shape[1:], low))
            self.result_specs.append(ANYWHERE)
        self.scratch += line_scratch(len(lines), z_count)
        if self.gathered:
            self.scratch.append(pltpu.SemaphoreType.DMA((self.gathered,)))
        if self.vectors:
            self.scratch.append(pltpu.VMEM((1, 4, 2, width // 8, lanes), full))

    def split(self, refs):
        return split_refs(
            refs, 5, len(self.arguments), 13, len(self.results), 6, GATHER_REFS * bool(self.gathered),
            GATHER_REFS * self.vectors, 2 * bool(self.lines),
        )

    def vec_whole(self, refs):
        return refs[-1]


def scratch_tail(plan, refs):
    return refs[-2] if plan.vectors else refs[-1]


def forward_layer(hidden, seg_column, seg_row, vectors, weights, out_dtype, plan, identity=None):
    tokens, width = hidden.shape
    inner = plan.inner
    wide = width * inner
    rows = tokens // L
    heads = width // HD
    shape = jax.ShapeDtypeStruct

    def here(s):
        return jnp.minimum(s, rows - 1)

    def column(s):
        return jnp.maximum(s - rows, 0)

    def row_block(columns):
        return pl.BlockSpec((L, columns), lambda s: (here(s), 0))

    def whole(columns):
        return pl.BlockSpec((tokens, columns), lambda s: (0, 0), pipeline_mode=pl.Buffered(1))

    wide_block = pl.BlockSpec((tokens, width), lambda s: (0, column(s)))
    out_shape = (
        shape((tokens, width), low), shape((tokens, width), low), shape((tokens, width), low),
        shape((width, tokens), low), shape((rows, heads, L), full),
        shape((tokens, width), full), shape((tokens, 1), full), shape((tokens, width), low),
        shape((tokens, wide), low), shape((tokens, wide), low),
        shape((tokens, width), full), shape((tokens, 1), full), shape((tokens, width), out_dtype),
        *plan.results,
    )
    out_specs = (
        row_block(width), row_block(width), row_block(width),
        pl.BlockSpec((width, L), lambda s: (0, here(s))), pl.BlockSpec((1, heads, L), lambda s: (here(s), 0, 0)),
        row_block(width), row_block(1), row_block(width),
        wide_block, wide_block,
        whole(width), whole(1), whole(width),
        *plan.result_specs,
    )
    total = 4 + 2 * inner
    held = max(total, plan.local + plan.gathered)
    return pl.pallas_call(
        functools.partial(forward_kernel, plan),
        grid=(rows + inner,),
        out_shape=out_shape,
        in_specs=[
            row_block(width),
            pl.BlockSpec((1, L, 1), lambda s: (here(s), 0, 0)),
            pl.BlockSpec((1, 1, L), lambda s: (here(s), 0, 0)),
            pl.BlockSpec(vectors.shape, lambda s: (0, 0)),
            ANYWHERE,
            *plan.argument_specs,
        ],
        out_specs=out_specs,
        scratch_shapes=[
            pltpu.VMEM((held, 4, 2, width // 8, width), low),
            pltpu.VMEM((L, L), full),
            pltpu.VMEM((width, L), low),
            pltpu.VMEM((tokens, width), low),
            pltpu.VMEM((tokens, width), full),
            pltpu.SemaphoreType.DMA((total,)),
            *plan.scratch,
        ],
        compiler_params=pltpu.CompilerParams(
            dimension_semantics=("arbitrary",), vmem_limit_bytes=62 * MIB,
            collective_id=identity, has_side_effects=identity is not None,
        ),
        cost_estimate=pl.CostEstimate(
            flops=2 * tokens * width * width * total + 4 * tokens * L * width,
            bytes_accessed=40 * MIB,
            transcendentals=tokens * (L * heads + wide),
        ),
        name="layer_forward",
    )(hidden, seg_column, seg_row, vectors, weights.reshape(-1, 4, 2, width // 8, width), *plan.arguments)


def wide_back_kernel(plan, inner, *refs):
    inputs, sources, outputs, targets, scratch, sum_refs, line_refs = plan.split(refs, 11, 4, 3)
    up_ref, x2_ref, inv2_ref, x1_ref, inv1_ref, n1_ref, vec_ref, wup_ref, wdown_ref, u_ref, gp_ref = inputs
    dw_ref, dr1_ref, da_ref, dvec_ref = outputs
    n1t, dz, kept_dw = scratch
    dy, dn1 = da_ref, dr1_ref
    c = pl.program_id(0)
    side = Side(plan, sources, targets, sum_refs, line_refs, kept_dw)
    side.enter(c == 0)
    steps = pl.num_programs(0)
    tokens, width = dn1.shape
    tile = tokens // 4
    pick = [slice(i * tile, (i + 1) * tile) for i in range(4)]
    base = 5 + inner

    @pl.when(c == 0)
    def _():
        gain = vec_ref[base + 1 : base + 2, :]

        def body(i, carry):
            gain_sum, shift_sum, bias_sum = carry
            rows = pl.ds(pl.multiple_of(i * tile, tile), tile)
            upstream = up_ref[rows, :].astype(full)
            unit = x2_ref[rows, :]
            back = norm_back(upstream, unit, inv2_ref[rows, :], gain)
            dn1[rows, :] = back
            branch = back.astype(low)
            dy[rows, :] = branch
            return (
                gain_sum + column_sum(upstream * unit),
                shift_sum + column_sum(upstream),
                bias_sum + column_sum(branch.astype(full)),
            )

        zero = jnp.zeros((1, width), full)
        gain_sum, shift_sum, bias_sum = lax.fori_loop(0, 4, body, (zero, zero, zero))
        dvec_ref[...] = jnp.zeros(dvec_ref.shape, full)
        dvec_ref[base : base + 1, :] = bias_sum
        dvec_ref[base + 1 : base + 2, :] = gain_sum
        dvec_ref[base + 2 : base + 3, :] = shift_sum
        n1t[...] = n1_ref[...].astype(full).T.astype(low)

    def token_step(i, carry):
        rows = pl.ds(pl.multiple_of(i * tile, tile), tile)
        slope = gp_ref[rows, :].astype(full)
        piece = (dot_nt(dy[rows, :], wdown_ref[0]) * slope).astype(low)
        dz[rows, :] = piece
        dn1[rows, :] += dot_nt(piece, wup_ref[0])
        side.advance(4 * c + i == 5, 2)
        side.advance(4 * c + i == 10, 3)
        if plan.total:
            side.sum.tick(4 * c + i)
        return carry + column_sum(piece.astype(full))

    bias_sum = lax.fori_loop(0, 4, token_step, jnp.zeros((1, width), full))
    for j in range(inner):
        @pl.when(c == j)
        def _():
            dvec_ref[5 + j : 6 + j, :] = bias_sum
    dw_up = dot_nn(n1t[...], dz[...]).astype(low)
    dw_down = dot_tn(u_ref[...], dy[...]).astype(low)
    if plan.own:
        @pl.when(2 * c < plan.own)
        def _():
            kept_dw[2 * c] = dw_up.reshape(kept_dw.shape[1:])
            kept_dw[2 * c + 1] = dw_down.reshape(kept_dw.shape[1:])

        @pl.when(2 * c >= plan.own)
        def _():
            dw_ref[0, 0] = dw_up
            dw_ref[1, 0] = dw_down
    else:
        dw_ref[0, 0] = dw_up
        dw_ref[1, 0] = dw_down

    @pl.when(c == steps - 1)
    def _():
        gain = vec_ref[3:4, :]

        def body(i, carry):
            gain_sum, shift_sum, bias_sum = carry
            rows = pl.ds(pl.multiple_of(i * tile, tile), tile)
            upstream = dn1[rows, :]
            unit = x1_ref[rows, :]
            back = norm_back(upstream, unit, inv1_ref[rows, :], gain)
            dr1_ref[rows, :] = back
            branch = back.astype(low)
            da_ref[rows, :] = branch
            return (
                gain_sum + column_sum(upstream * unit),
                shift_sum + column_sum(upstream),
                bias_sum + column_sum(branch.astype(full)),
            )

        zero = jnp.zeros((1, width), full)
        gain_sum, shift_sum, bias_sum = lax.fori_loop(0, 4, body, (zero, zero, zero))
        dvec_ref[2:3, :] = bias_sum
        dvec_ref[3:4, :] = gain_sum
        dvec_ref[4:5, :] = shift_sum

    side.leave(c == steps - 1)


def wide_back(upstream, kept, vectors, weights, places, plan, identity=None):
    x1, inv1, n1, u, gp, x2, inv2 = kept
    tokens, width = x1.shape
    up_start, down_start, stride = places
    inner = u.shape[1] // width
    shape = jax.ShapeDtypeStruct

    def whole(array):
        return pl.BlockSpec(array.shape, lambda c: (0, 0), pipeline_mode=pl.Buffered(1))

    return pl.pallas_call(
        functools.partial(wide_back_kernel, plan, inner),
        grid=(inner,),
        out_shape=(
            shape((2, inner - plan.own // 2, width, width), low),
            shape((tokens, width), full), shape((tokens, width), low), shape((16, width), full),
            *plan.results,
        ),
        in_specs=[
            whole(upstream), whole(x2), whole(inv2), whole(x1), whole(inv1), whole(n1), whole(vectors),
            pl.BlockSpec((1, width, width), lambda c: (up_start + stride * c, 0, 0)),
            pl.BlockSpec((1, width, width), lambda c: (down_start + stride * c, 0, 0)),
            pl.BlockSpec((tokens, width), lambda c: (0, c)),
            pl.BlockSpec((tokens, width), lambda c: (0, c)),
            *plan.argument_specs,
        ],
        out_specs=(
            pl.BlockSpec((2, 1, width, width), lambda c: (0, jnp.maximum(c - plan.own // 2, 0), 0, 0)),
            pl.BlockSpec((tokens, width), lambda c: (0, 0), pipeline_mode=pl.Buffered(1)),
            pl.BlockSpec((tokens, width), lambda c: (0, 0), pipeline_mode=pl.Buffered(1)),
            pl.BlockSpec((16, width), lambda c: (0, 0)),
            *plan.result_specs,
        ),
        scratch_shapes=[
            pltpu.VMEM((width, tokens), low),
            pltpu.VMEM((tokens, width), low),
            pltpu.VMEM((plan.own, 4, 2, width // 8, width) if plan.own else (8, 128), low),
            *plan.scratch,
        ],
        compiler_params=pltpu.CompilerParams(
            dimension_semantics=("arbitrary",), vmem_limit_bytes=60 * MIB,
            collective_id=identity, has_side_effects=identity is not None,
        ),
        cost_estimate=pl.CostEstimate(
            flops=8 * tokens * width * width * inner, bytes_accessed=50 * MIB, transcendentals=0
        ),
        name="wide_backward",
    )(upstream, x2, inv2, x1, inv1, n1, vectors, weights, weights, u, gp, *plan.arguments)


def attend_back_kernel(plan, *refs):
    inputs, sources, outputs, targets, scratch, sum_refs, line_refs = plan.split(refs, 11, 3, 10)
    da_ref, dr1_ref, x_ref, q_ref, k_ref, v_ref, ctxt_ref, lse_ref, segc_ref, segr_ref, w_ref = inputs
    dw_ref, dx_ref, dvec_ref = outputs
    bias, dctx, kt, delta, dqt, xt, dq_all, dk_all, dv_all, dwo = scratch
    r = pl.program_id(0)
    side = Side(plan, sources, targets, sum_refs, line_refs, dwo)
    side.enter(r == 0)
    tokens, width = dr1_ref.shape
    pairs = width // PAIR
    ticks = pairs + 2

    def tick(n):
        if plan.total:
            side.sum.tick(r * ticks + n)

    tick(0)
    here = pl.ds(pl.multiple_of(r * tokens, tokens), tokens)

    @pl.when(r == 0)
    def _():
        grad = dot_nn(ctxt_ref[...], da_ref[...]).astype(low)
        if plan.own:
            dwo[0] = grad.reshape(dwo.shape[1:])
        else:
            dw_ref[3] = grad

    xt[:, here] = x_ref[...].astype(low).astype(full).T.astype(low)
    bias[...] = segment_bias(segc_ref[0], segr_ref[0])
    context_grad = dot_nt(da_ref[here, :], w_ref[3]).astype(low)
    dctx[...] = context_grad
    kt[...] = k_ref[...].astype(full).T.astype(low)
    products = context_grad.astype(full) * ctxt_ref[:, here].astype(full).T
    feature = lax.broadcasted_iota(jnp.int32, (16, width), 1)
    head = lax.broadcasted_iota(jnp.int32, (16, width), 0)
    member = ((feature >= head * HD) & (feature < (head + 1) * HD)).astype(full).astype(low)
    high = products.astype(low)
    rest = (products - high.astype(full)).astype(low)
    delta[...] = dot_nt(member, high) + dot_nt(member, rest)
    masks = half_masks(low)
    scale = HD ** (-0.5)

    def pair_step(p, carry):
        lanes = pl.ds(pl.multiple_of(p * PAIR, PAIR), PAIR)
        q_pair = q_ref[:, lanes] * jnp.asarray(scale, low)
        k_pair = k_ref[:, lanes]
        v_pair = v_ref[:, lanes]
        g_pair = dctx[:, lanes]
        key_grad = jnp.zeros((tokens, PAIR), full)
        value_grad = jnp.zeros((tokens, PAIR), full)
        for h in range(2):
            q_half = q_pair * masks[h]
            g_half = g_pair * masks[h]
            scores = dot_nt(k_pair, q_half) + bias[...]
            attention = jnp.exp(scores - lse_ref[0, pl.ds(2 * p + h, 1), :])
            value_grad = value_grad + dot_nn(attention.astype(low), g_half)
            attention_grad = dot_nt(v_pair, g_half)
            score_grad = (attention * (attention_grad - delta[pl.ds(2 * p + h, 1), :])).astype(low)
            key_grad = key_grad + dot_nn(score_grad, q_half)
            rows = pl.ds(pl.multiple_of(p * PAIR + h * HD, HD), HD)
            dqt[rows, :] = dot_nn(kt[rows, :], score_grad) * scale
        dk_all[here, lanes] = key_grad.astype(low)
        dv_all[here, lanes] = value_grad.astype(low)
        tick(1 + p)
        side.advance((r == 0) & (p == 4), 2)
        side.advance((r == 1) & (p == 3), 3)
        return carry

    lax.fori_loop(0, pairs, pair_step, 0)
    tick(1 + pairs)
    query_grad = dqt[...].T.astype(low)
    dq_all[here, :] = query_grad
    key_grad = dk_all[here, :]
    value_grad = dv_all[here, :]
    dx_ref[...] = (
        dr1_ref[...]
        + dot_nt(query_grad, w_ref[0])
        + dot_nt(key_grad, w_ref[1])
        + dot_nt(value_grad, w_ref[2])
    )

    @pl.when(r == 0)
    def _():
        dvec_ref[...] = jnp.zeros(dvec_ref.shape, full)

    dvec_ref[0:1, :] += column_sum(query_grad.astype(full))
    dvec_ref[1:2, :] += column_sum(value_grad.astype(full))

    @pl.when(r == pl.num_programs(0) - 1)
    def _():
        for j, grad in enumerate((dq_all, dk_all, dv_all)):
            dw_ref[j] = dot_nn(xt[...], grad[...]).astype(low)

    side.leave(r == pl.num_programs(0) - 1)


def attend_back(da, dr1, hidden, kept, seg_column, seg_row, weights, start, plan, identity=None):
    q, k, v, ctxt, lse = kept
    tokens, width = da.shape
    rows = tokens // L
    heads = width // HD
    shape = jax.ShapeDtypeStruct

    def row_block():
        return pl.BlockSpec((L, width), lambda r: (r, 0))

    return pl.pallas_call(
        functools.partial(attend_back_kernel, plan),
        grid=(rows,),
        out_shape=(
            shape((4 - plan.own, width, width), low), shape((tokens, width), full), shape((8, width), full),
            *plan.results,
        ),
        in_specs=[
            pl.BlockSpec((tokens, width), lambda r: (0, 0), pipeline_mode=pl.Buffered(1)),
            row_block(), row_block(), row_block(), row_block(), row_block(),
            pl.BlockSpec((width, tokens), lambda r: (0, 0), pipeline_mode=pl.Buffered(1)),
            pl.BlockSpec((1, heads, L), lambda r: (r, 0, 0)),
            pl.BlockSpec((1, L, 1), lambda r: (r, 0, 0)),
            pl.BlockSpec((1, 1, L), lambda r: (r, 0, 0)),
            pl.BlockSpec((4, width, width), lambda r: (start, 0, 0), pipeline_mode=pl.Buffered(1)),
            *plan.argument_specs,
        ],
        out_specs=(
            pl.BlockSpec((4 - plan.own, width, width), lambda r: (0, 0, 0), pipeline_mode=pl.Buffered(1)),
            row_block(),
            pl.BlockSpec((8, width), lambda r: (0, 0)),
            *plan.result_specs,
        ),
        scratch_shapes=[
            pltpu.VMEM((L, L), full),
            pltpu.VMEM((L, width), low),
            pltpu.VMEM((width, L), low),
            pltpu.VMEM((16, L), full),
            pltpu.VMEM((width, L), full),
            pltpu.VMEM((width, tokens), low),
            pltpu.VMEM((tokens, width), low),
            pltpu.VMEM((tokens, width), low),
            pltpu.VMEM((tokens, width), low),
            pltpu.VMEM((1, 4, 2, width // 8, width) if plan.own else (8, 128), low),
            *plan.scratch,
        ],
        compiler_params=pltpu.CompilerParams(
            dimension_semantics=("arbitrary",), vmem_limit_bytes=60 * MIB,
            collective_id=identity, has_side_effects=identity is not None,
        ),
        cost_estimate=pl.CostEstimate(
            flops=16 * tokens * width * width + 10 * tokens * L * width,
            bytes_accessed=30 * MIB,
            transcendentals=tokens * L * heads,
        ),
        name="attend_backward",
    )(da, dr1, hidden, q, k, v, ctxt, lse, seg_column, seg_row, weights, *plan.arguments)


def moments(rotated, first, second):
    first_new = beta_one * first + (1.0 - beta_one) * rotated
    second_new = beta_two * second + (1.0 - beta_two) * rotated * rotated
    direction = (
        first_new
        / (1.0 - beta_one**STEP)
        / (jnp.sqrt(second_new / (1.0 - beta_two**STEP)) + adam_epsilon)
    )
    return first_new, second_new, direction


def pack_lanes(piece):
    rows = piece.shape[0] // 2
    return jnp.concatenate([piece[:rows], piece[rows:]], axis=1)


def unpack_lanes(piece):
    columns = piece.shape[1] // 2
    return jnp.concatenate([piece[:, :columns], piece[:, columns:]], axis=0)


def optimizer_kernel(plan, *refs):
    inputs, ready, dvecs, bases, lines_in, outputs, lines_out, scratch, sum_refs, vec_refs, line_refs = split_refs(
        refs, 6, plan.ready, plan.dvecs, plan.bases, len(plan.spans), 5, len(plan.spans), 21, SUM_REFS, SUM_REFS,
        2 * bool(plan.spans),
    )
    index_ref, place_ref, tail_hbm, first_hbm, second_hbm, blocks = inputs
    new_ref, low_ref, first_out, second_out, vec_out = outputs
    (store, left, right, first_in, second_in, g_out, g_in, t_out, t_in, e_out, e_in, w_out, w_in, vec_source,
     load_sem, g_sem, t_sem, e_sem, w_sem, left_sem, right_sem) = scratch
    slots, owners = g_in.shape[0], g_in.shape[1]
    z_count = t_in.shape[1]
    place = Place(z_count)
    dp, z = place.dp, place.z
    dps = [lax.rem(dp + d, owners) for d in range(owners)]
    count = blocks.shape[0]
    tail = BlockSum(place, [tail_hbm], sum_refs)
    vec = BlockSum(place, [vec_source], vec_refs)
    greet([(other, z) for other in dps[1:]] + place.z_partners())
    lines = line_gathers(place, plan.spans, lines_in, lines_out, line_refs, z_count)
    for line in lines:
        line.advance(1)
    every = list(bases) + list(lines_out)
    tail.tick(0)
    rows = plan.vector_rows
    stacked = jnp.concatenate(
        [dvecs[0][0:2, :], dvecs[1][2:rows, :], dvecs[2][0:2, :], dvecs[3][2:rows, :],
         jnp.zeros((vec_source.shape[-1] - 2 * rows, blocks.shape[2]), full)], axis=0
    )
    vec_source[0] = stacked.T.reshape(vec_source.shape[1:])

    def load(refs_map, target, sem, s):
        n, at = refs_map[s]
        return pltpu.make_async_copy(every[n].at[:, at], target.at[:, s], sem.at[s])

    def load_first(s):
        return pltpu.make_async_copy(first_hbm.at[s], first_in.at[s], load_sem.at[0, s])

    def load_second(s):
        return pltpu.make_async_copy(second_hbm.at[s], second_in.at[s], load_sem.at[1, s])

    early = [s for s in range(slots) if plan.left_map[s][0] < len(bases)]
    for s in range(slots):
        load(plan.right_map, right, right_sem, s).start()
        load_first(s).start()
        load_second(s).start()
        if s in early:
            load(plan.left_map, left, left_sem, s).start()

    def sum_step(t, carry):
        tail.tick(t)
        vec.tick(t - 1)
        return carry

    lax.fori_loop(1, 4, sum_step, 0)
    for line in lines:
        line.advance(2)
    lax.fori_loop(4, tail.count + 7, sum_step, 0)
    start = tail.count
    for part in ready:
        store[start : start + part.shape[0]] = part[...]
        start += part.shape[0]
    store[count] = jnp.zeros(store.shape[1:], low)
    for i in range(tail.count):
        store[i] = tail.finish(i).astype(low)

    def g_copy(s, d):
        other = dps[d]
        return remote(g_out.at[s, d], g_in.at[s, dp], g_sem.at[0, s, d], g_sem.at[1, s, owners - d], (other, z))

    def t_copy(s, d):
        other = place.zs[d]
        return remote(t_out.at[s, d], t_in.at[s, z], t_sem.at[0, s, d], t_sem.at[1, s, z_count - d], (dp, other))

    def e_copy(s, d):
        other = place.zs[d]
        return remote(e_out.at[s, d], e_in.at[s, z], e_sem.at[0, s, d], e_sem.at[1, s, z_count - d], (dp, other))

    def w_copy(s, d):
        other = dps[d]
        return remote(
            w_out.at[s, other], w_in.at[s * owners + dp], w_sem.at[0, s, d], w_sem.at[1, s, owners - d], (other, z)
        )

    def send_out(s):
        for d in range(1, owners):
            g_out[s, d] = store[index_ref[s * owners + dps[d]]]
            g_copy(s, d).start()
        g_in[s, dp] = store[index_ref[s * owners + dp]]

    def turn(s):
        for d in range(1, owners):
            g_copy(s, d).wait()
        if s + 2 < slots:
            send_out(s + 2)
        load(plan.right_map, right, right_sem, s).wait()
        grad = jnp.concatenate([unfold(g_in[s, c].astype(full)) for c in range(owners)], axis=0).astype(low)
        for d in range(1, z_count):
            t_out[s, d] = pack_lanes(dot_nt(right[place.zs[d], s], grad)).astype(low)
            t_copy(s, d).start()
        t_in[s, z] = pack_lanes(dot_nt(right[z, s], grad)).astype(low)

    def adapt(s):
        for d in range(1, z_count):
            t_copy(s, d).wait()
        load_first(s).wait()
        load_second(s).wait()
        load(plan.left_map, left, left_sem, s).wait()
        rotated = jnp.zeros(first_in.shape[1:], full)
        for f in range(z_count):
            rotated = rotated + dot_nn(unpack_lanes(t_in[s, f].astype(full)).astype(low), left[f, s])
        first_new, second_new, direction = moments(rotated, first_in[s], second_in[s])
        first_out[s] = first_new
        second_out[s] = second_new
        direction = direction.astype(low)
        for d in range(1, z_count):
            e_out[s, d] = pack_lanes(dot_nt(left[place.zs[d], s], direction)).astype(low)
            e_copy(s, d).start()
        e_in[s, z] = pack_lanes(dot_nt(left[z, s], direction)).astype(low)

    def step_back(s):
        for d in range(1, z_count):
            e_copy(s, d).wait()
        step = jnp.zeros((left.shape[2], left.shape[3]), full)
        for f in range(z_count):
            step = step + dot_nn(unpack_lanes(e_in[s, f].astype(full)).astype(low), right[f, s])
        share = step.shape[0] // owners
        for c in range(owners):
            w_out[s, c] = fold(step[c * share : (c + 1) * share]).astype(low)
        for d in range(1, owners):
            w_copy(s, d).start()
        w_in[s * owners + dp] = w_out[s, dp]

    send_out(0)
    send_out(1)
    for hop in range(3, z_count):
        for line in lines:
            line.advance(hop)
    for k in range(slots + 2):
        if k == 3:
            for line in lines:
                line.advance(z_count)
            for s in range(slots):
                if s not in early:
                    load(plan.left_map, left, left_sem, s).start()
        if k < slots:
            turn(k)
        if 0 <= k - 1 < slots:
            adapt(k - 1)
        if 0 <= k - 2 < slots:
            step_back(k - 2)

    vec_out[...] = vec.finish(0)
    for s in range(slots):
        for d in range(1, owners):
            w_copy(s, d).wait()

    def block_step(b, carry):
        step = unfold(w_in[place_ref[b]].astype(full))
        block = blocks[b]
        new = block - matrix_rate * (step + weight_decay * block)
        new_ref[b] = new
        low_ref[b] = new.astype(low)
        return carry

    lax.fori_loop(0, count, block_step, 0)


class OptimizerPlan:
    def __init__(self, ready, dvecs, bases, spans, left_map, right_map, vector_rows):
        self.ready, self.dvecs, self.bases, self.spans = ready, dvecs, bases, spans
        self.left_map, self.right_map, self.vector_rows = left_map, right_map, vector_rows


def optimizer(
    index, places, tail, ready, dvecs, vector_rows, bases, lines, left_map, right_map, first, second, blocks, z_count,
    identity,
):
    slots, columns, width = first.shape
    owners = index.shape[0] // slots
    count, rows = blocks.shape[0], blocks.shape[1]
    span = bases[0].shape[2]
    lanes = 128
    shape = jax.ShapeDtypeStruct
    piece = (2 * rows, width // 2)
    tile = (span // 2, 2 * columns)
    smem = pl.BlockSpec(memory_space=pltpu.SMEM)
    plan = OptimizerPlan(
        len(ready), len(dvecs), len(bases), [(first_slot, amount) for _, first_slot, amount in lines],
        left_map, right_map, vector_rows,
    )
    line_shapes = [shape((z_count, amount) + basis.shape[1:], low) for basis, _, amount in lines]
    return pl.pallas_call(
        functools.partial(optimizer_kernel, plan),
        out_shape=(
            shape(blocks.shape, full), shape(blocks.shape, low), shape(first.shape, full), shape(first.shape, full),
            shape((rows, lanes), full), *line_shapes,
        ),
        in_specs=[smem, smem, ANYWHERE, ANYWHERE, ANYWHERE, IN_VMEM]
        + [IN_VMEM] * (len(ready) + len(dvecs)) + [ANYWHERE] * (len(bases) + len(lines)),
        out_specs=(IN_VMEM,) * 5 + (ANYWHERE,) * len(lines),
        scratch_shapes=[
            pltpu.VMEM((count + 1,) + piece, low),
            pltpu.VMEM((z_count, slots, span, width), low),
            pltpu.VMEM((z_count, slots, columns, width), low),
            pltpu.VMEM((slots, columns, width), full),
            pltpu.VMEM((slots, columns, width), full),
            pltpu.VMEM((slots, owners) + piece, low),
            pltpu.VMEM((slots, owners) + piece, low),
            pltpu.VMEM((slots, z_count) + tile, low),
            pltpu.VMEM((slots, z_count) + tile, low),
            pltpu.VMEM((slots, z_count) + tile, low),
            pltpu.VMEM((slots, z_count) + tile, low),
            pltpu.VMEM((slots, owners) + piece, low),
            pltpu.VMEM((slots * owners,) + piece, low),
            pltpu.VMEM((1, owners // 2, 2, width // owners, lanes), full),
            pltpu.SemaphoreType.DMA((2, slots)),
            pltpu.SemaphoreType.DMA((2, slots, owners)),
            pltpu.SemaphoreType.DMA((2, slots, z_count)),
            pltpu.SemaphoreType.DMA((2, slots, z_count)),
            pltpu.SemaphoreType.DMA((2, slots, owners)),
            pltpu.SemaphoreType.DMA((slots,)),
            pltpu.SemaphoreType.DMA((slots,)),
            *sum_scratch(tail.shape[0], tail.shape[3], width, z_count),
            *sum_scratch(1, width // owners, lanes, z_count, full),
            *line_scratch(len(lines), z_count),
        ],
        compiler_params=pltpu.CompilerParams(
            vmem_limit_bytes=60 * MIB, collective_id=identity, has_side_effects=True
        ),
        cost_estimate=pl.CostEstimate(
            flops=8 * slots * span * width * width, bytes_accessed=40 * MIB, transcendentals=slots * width * columns
        ),
        name="optimizer",
    )(index, places, tail, first, second, blocks, *ready, *dvecs, *bases, *[basis for basis, _, _ in lines])


def slot_table(owner, slots, owner_rows):
    block_count = owner.shape[0]
    same_owner = owner[:, None] == owner[None, :]
    ordering = jnp.arange(block_count, dtype=jnp.int32)
    earlier = ordering[None, :] < ordering[:, None]
    ranking = jnp.sum(jnp.where(same_owner & earlier, 1, 0), axis=1).astype(jnp.int32)
    owner_match = owner[None, :] == jnp.arange(owner_rows, dtype=jnp.int32)[:, None]
    slot_match = ranking[None, :] == jnp.arange(slots, dtype=jnp.int32)[:, None]
    return jnp.where(slot_match[:, None, :] & owner_match[None, :, :], 1.0, 0.0).astype(full)


def scatter_sum(grads):
    blocks, width = grads.shape[0], grads.shape[2]
    cut = grads.reshape(blocks, lax.axis_size("dp"), -1, width).transpose(1, 0, 2, 3)
    outer = lax.psum_scatter(cut, "dp", scatter_dimension=0, tiled=False)
    blocks, rows, width = outer.shape
    count = lax.axis_size("fsdp")
    cut = outer.reshape(blocks, count, rows // count, width).transpose(1, 0, 2, 3)
    return lax.psum_scatter(cut, "fsdp", scatter_dimension=0, tiled=False)


def scatter_vectors(grads):
    rows, width = grads.shape
    count = lax.axis_size("dp") * lax.axis_size("fsdp")
    cut = grads.reshape(rows, count, width // count).transpose(1, 0, 2)
    return lax.psum_scatter(cut, ("dp", "fsdp"), scatter_dimension=0, tiled=False)


def gathering_program(
    tokens, segment, blocks, vectors, owner, left_basis, right_basis, rot_first, rot_second, cotangent, z_count
):
    layers, vector_rows = vectors.shape[:2]
    count, shard_rows, width = blocks.shape
    per_layer = count // layers
    inner = (per_layer - 4) // 2
    owners = lax.axis_size("dp")
    slots = rot_first.shape[0]
    part = width // owners
    lanes = 128
    seg_column, seg_row = segment[:, :, None], segment[:, None, :]

    order = [0, 1, 2, 3]
    for c in range(inner):
        order += [4 + c, 4 + inner + c]
    folded = blocks.astype(low).reshape(count, shard_rows, 2, width // 2).transpose(0, 2, 1, 3)
    folded = folded.reshape(count, 2 * shard_rows, width // 2)

    def pick(numbers):
        return jnp.stack([folded[j] for j in numbers])

    head = pick(order + [per_layer + j for j in order[:4]])
    rest = pick([per_layer + j for j in order[4:]])
    vec_shard = vectors.astype(low).astype(full).reshape(layers * vector_rows, shard_rows).T
    vec_shard = jnp.pad(vec_shard, ((0, 0), (0, lanes - layers * vector_rows)))[None]
    left_low = left_basis.reshape(slots, -1, width).astype(low)
    right_low = right_basis.transpose(0, 2, 1).astype(low)

    plan = ForwardPlan(
        inner, 0, head, vec_shard, vector_rows, [(right_low, 0, 2)], lead=9, row_ticks=3, z_count=z_count
    )
    empty_vec = jnp.zeros((16, width), full)
    results = forward_layer(tokens, seg_column, seg_row, empty_vec, jnp.zeros((1, width, width), low), full, plan, 6)
    kept_a = results[:12]
    hidden, weights_a, vec_a, vec_b, right_01 = results[12:]
    weights_a = weights_a.reshape(-1, width, width)
    plan = ForwardPlan(inner, 4, rest, lines=[(right_low, 2, 1)], lead=0, row_ticks=4, z_count=z_count)
    plan.order = [per_layer + j for j in range(4)]
    results = forward_layer(hidden, seg_column, seg_row, vec_b, weights_a, low, plan, 7)
    kept_b = results[:12]
    layer_out, weights_b, right_2 = results[12:]
    weights_b = weights_b.reshape(-1, width, width)

    def cut(grads):
        return grads.reshape(-1, owners // 2, 2, part, width)

    size = (part, width)
    own = 2 * (inner // 2)

    def wide_at(pending):
        def at(t):
            mine = 2 * (lax.div(t, 4) - 1) + lax.rem(t, 4)
            is_mine = (t >= 4) & (lax.rem(t, 4) < 2) & (mine < own)
            return ((t >= 0) & (t < pending)) | is_mine, jnp.where(t >= 4, pending + mine, t)

        return at

    def attend_at(t):
        return (t >= 0) & (lax.rem(t, 2) == 0) & (t < 2 * (2 * inner - own + 1)), lax.div(t, 2)

    plan = Plan(None, [(right_low, 3, 2)], z_count, own, size, wide_at(0))
    dw_wide, dr1, da, dvec_wide_b, wide_sum_b, right_34 = wide_back(
        cotangent, kept_b[5:], vec_b, weights_b, (0, 1, 2), plan, 1
    )
    plan = Plan(cut(dw_wide), [(left_low, 0, 1)], z_count, 1, size, attend_at)
    dw_attend, upstream, dvec_attend_b, attend_sum_b, left_0 = attend_back(
        da, dr1, hidden, kept_b[:5], seg_column, seg_row, weights_a, per_layer // 4, plan, 2
    )
    plan = Plan(cut(dw_attend), [(left_low, 1, 1)], z_count, own, size, wide_at(3))
    dw_wide, dr1, da, dvec_wide_a, wide_sum_a, left_1 = wide_back(
        upstream, kept_a[5:], vec_a, weights_a, (4, 5, 2), plan, 3
    )
    plan = Plan(cut(dw_wide), [(left_low, 2, 1)], z_count, 1, size, attend_at)
    dw_attend, upstream, dvec_attend_a, attend_sum_a, left_2 = attend_back(
        da, dr1, tokens, kept_a[:5], seg_column, seg_row, weights_a, 0, plan, 5
    )

    three = list(range(3))
    early = [4 + c + inner * k for c in range(own // 2) for k in range(2)]
    late = [4 + c + inner * k for k in range(2) for c in range(own // 2, inner)] + [3]
    held_order = three + late + [per_layer + j for j in three] + early + [per_layer + j for j in late + early]
    rank = jnp.asarray([held_order.index(j) for j in range(count)], jnp.int32)
    table = slot_table(owner, slots, owners).reshape(slots * owners, count)
    held = jnp.sum(table, axis=1)
    index = jnp.where(held > 0, jnp.sum(table * rank, axis=1), count).astype(jnp.int32)
    places = jnp.sum(table * jnp.arange(slots * owners, dtype=jnp.int32)[:, None], axis=0).astype(jnp.int32)
    bases = (right_01, right_2, right_34, left_0, left_1, left_2)
    right_map = [(0, 0), (0, 1), (1, 0), (2, 0), (2, 1)]
    left_map = [(3, 0), (4, 0), (5, 0), (6, 0), (6, 1)]
    new_blocks, new_low, first_new, second_new, vec_sum, _ = optimizer(
        index, places, cut(dw_attend), (attend_sum_a, wide_sum_a, attend_sum_b, wide_sum_b),
        (dvec_attend_a, dvec_wide_a, dvec_attend_b, dvec_wide_b), vector_rows, bases, [(left_low, 3, 2)], left_map, right_map,
        rot_first.transpose(0, 2, 1), rot_second.transpose(0, 2, 1), blocks, z_count, 4,
    )
    first_new, second_new = first_new.transpose(0, 2, 1), second_new.transpose(0, 2, 1)
    vector_grad = vec_sum[:, : layers * vector_rows].T.reshape(layers, vector_rows, shard_rows)
    return layer_out, upstream, new_blocks, new_low, first_new, second_new, vector_grad


def plain_program(
    tokens, segment, blocks, vectors, owner, left_basis, right_basis, rot_first, rot_second, cotangent
):
    layers, vector_rows = vectors.shape[:2]
    per_layer = blocks.shape[0] // layers
    inner = (per_layer - 4) // 2
    width = blocks.shape[2]
    owner_rows = lax.axis_size("dp")
    slots = rot_first.shape[0]
    selector = slot_table(owner, slots, owner_rows)
    vector_parts = lax.all_gather(vectors.astype(low), ("dp", "fsdp"), axis=0, tiled=False)
    vector_full = vector_parts.transpose(1, 2, 0, 3).reshape(layers, vector_rows, width).astype(full)
    blocks_low, vector_full = lax.optimization_barrier((blocks.astype(low), vector_full))

    seg_column = segment[:, :, None]
    seg_row = segment[:, None, :]
    state = tokens
    kept = []
    for layer_index in range(layers):
        start = per_layer * layer_index
        weights = lax.all_gather(blocks_low[start : start + per_layer], ("dp", "fsdp"), axis=1, tiled=True)
        out_dtype = low if layer_index == layers - 1 else full
        results = forward_layer(
            state, seg_column, seg_row, vector_full[layer_index], weights, out_dtype, ForwardPlan(inner, per_layer)
        )
        kept.append((state, weights, results[:5], results[5:12]))
        state = results[12]
    layer_out = state
    upstream = cotangent
    right_low = lax.all_gather(right_basis.astype(low), "fsdp", axis=2, tiled=True)
    block_shards = [None] * layers
    vector_shards = [None] * layers
    for layer_index in reversed(range(layers)):
        hidden, weights, attend_kept, wide_kept = kept[layer_index]
        dw_wide, dr1, da, dvec_wide = wide_back(
            upstream, wide_kept, vector_full[layer_index], weights, (4, 4 + inner, 1), Plan()
        )
        wide_shard = scatter_sum(dw_wide.reshape(-1, width, width))
        dw_attend, upstream, dvec_attend = attend_back(
            da, dr1, hidden, attend_kept, seg_column, seg_row, weights, 0, Plan()
        )
        dvec = jnp.concatenate([dvec_attend[:2], dvec_wide[2:vector_rows]], axis=0)
        block_shards[layer_index] = jnp.concatenate([scatter_sum(dw_attend), wide_shard], axis=0)
        vector_shards[layer_index] = scatter_vectors(dvec)
    vector_grad = jnp.stack(vector_shards)
    block_grad = jnp.concatenate(block_shards, axis=0)
    outgoing = jnp.einsum("srk,kid->srid", selector.astype(low), block_grad, preferred_element_type=full)
    incoming = lax.all_to_all(outgoing.astype(low), "dp", split_axis=1, concat_axis=1, tiled=True)
    owned = incoming.reshape(slots, -1, width)
    turned = jnp.einsum("sik,skj->sij", owned, right_low, preferred_element_type=full).astype(low)
    left_rows = left_basis.reshape(slots, -1, width).astype(low)
    partial_sums = jnp.einsum("sra,srb->sab", left_rows, turned, preferred_element_type=full)
    rotated = lax.psum_scatter(
        partial_sums.astype(low), "fsdp", scatter_dimension=2, tiled=True
    ).astype(full)
    first_new, second_new, direction = moments(rotated, rot_first, rot_second)
    direction_full = lax.all_gather(direction.astype(low), "fsdp", axis=2, tiled=True)
    back_right = jnp.einsum("sab,scb->sac", direction_full, right_low, preferred_element_type=full)
    step_rows = jnp.einsum(
        "sia,sac->sic", left_rows, back_right.astype(low), preferred_element_type=full
    )
    returned = lax.all_to_all(
        step_rows.reshape(slots, owner_rows, -1, width).astype(low),
        "dp",
        split_axis=1,
        concat_axis=1,
        tiled=True,
    )
    step_shard = jnp.einsum("srk,srid->kid", selector.astype(low), returned, preferred_element_type=full)
    new_blocks = blocks - matrix_rate * (step_shard + weight_decay * blocks)
    return layer_out, upstream, new_blocks, new_blocks.astype(low), first_new, second_new, vector_grad


def shards(
    tokens,
    segment,
    blocks,
    vectors,
    owner,
    left_basis,
    right_basis,
    rot_first,
    rot_second,
    vec_first,
    vec_second,
    cotangent,
):
    operands = (
        tokens, segment, blocks, vectors, owner, left_basis, right_basis, rot_first, rot_second, cotangent
    )
    z_count = lax.axis_size("fsdp")
    if lax.axis_size("dp") == 8 and z_count == 4:
        results = gathering_program(*operands, z_count)
    else:
        results = plain_program(*operands)
    layer_out, upstream, new_blocks, new_low, first_new, second_new, vector_grad = results
    vector_first = beta_one * vec_first + (1.0 - beta_one) * vector_grad
    vector_second = beta_two * vec_second + (1.0 - beta_two) * vector_grad * vector_grad
    vector_step = (
        vector_first
        / (1.0 - beta_one**STEP)
        / (jnp.sqrt(vector_second / (1.0 - beta_two**STEP)) + adam_epsilon)
    )
    vector_new = vectors - vector_rate * (vector_step + weight_decay * vectors)
    return (
        layer_out,
        upstream,
        new_blocks,
        new_low,
        first_new,
        second_new,
        vector_first,
        vector_second,
        vector_new,
    )


def solution(mesh):
    return jax.shard_map(
        shards,
        mesh=mesh,
        in_specs=(
            P(("dp", "fsdp"), None),
            P(("dp", "fsdp"), None),
            P(None, ("dp", "fsdp"), None),
            P(None, None, ("dp", "fsdp")),
            P(),
            P("dp", None, "fsdp", None),
            P("dp", None, "fsdp"),
            P("dp", None, "fsdp"),
            P("dp", None, "fsdp"),
            P(None, None, ("dp", "fsdp")),
            P(None, None, ("dp", "fsdp")),
            P(("dp", "fsdp"), None),
        ),
        out_specs=(
            P(("dp", "fsdp"), None),
            P(("dp", "fsdp"), None),
            P(None, ("dp", "fsdp"), None),
            P(None, ("dp", "fsdp"), None),
            P("dp", None, "fsdp"),
            P("dp", None, "fsdp"),
            P(None, None, ("dp", "fsdp")),
            P(None, None, ("dp", "fsdp")),
            P(None, None, ("dp", "fsdp")),
        ),
        check_vma=False,
    )
```

```python
import functools

import jax
import jax.numpy as jnp
from jax import lax
from jax.experimental import pallas as pl
from jax.experimental.pallas import tpu as pltpu
from jax.sharding import PartitionSpec as P

H = 12
HD = 64
L = 512
STEP = 5
PAIR = 2 * HD
MIB = 1 << 20

beta_one = 0.5
beta_two = 0.5
adam_epsilon = 1e-08
norm_epsilon = 1e-06
matrix_rate = 0.03
vector_rate = 0.2
weight_decay = 0.01
masked_score = -1e30
low = jnp.bfloat16
full = jnp.float32


def dot_nn(a, b):
    return lax.dot_general(a, b, (((1,), (0,)), ((), ())), preferred_element_type=full)


def dot_nt(a, b):
    return lax.dot_general(a, b, (((1,), (1,)), ((), ())), preferred_element_type=full)


def dot_tn(a, b):
    return lax.dot_general(a, b, (((0,), (0,)), ((), ())), preferred_element_type=full)


def gelu_parts(z):
    size = jnp.abs(z) * 0.7071067811865476
    t = 1.0 / (1.0 + 0.3275911 * size)
    bell = jnp.exp(-0.5 * z * z)
    poly = ((((1.061405429 * t - 1.453152027) * t + 1.421413741) * t - 0.284496736) * t + 0.254829592) * t
    half_tail = 0.5 * poly * bell
    phi = jnp.where(z >= 0, 1.0 - half_tail, half_tail)
    return z * phi, phi + z * bell * 0.3989422804014327


def norm_parts(residual):
    average = jnp.mean(residual, axis=-1, keepdims=True)
    centered = residual - average
    inverse = lax.rsqrt(jnp.mean(centered * centered, axis=-1, keepdims=True) + norm_epsilon)
    return centered * inverse, inverse


def norm_back(upstream, unit, inverse, gain):
    scaled = upstream * gain
    return inverse * (
        scaled
        - jnp.mean(scaled, axis=-1, keepdims=True)
        - unit * jnp.mean(scaled * unit, axis=-1, keepdims=True)
    )


def column_sum(values):
    return jnp.sum(values, axis=0, keepdims=True)


def half_masks(dtype):
    lane = lax.broadcasted_iota(jnp.int32, (1, PAIR), 1)
    first = (lane < HD).astype(full)
    return first.astype(dtype), (1.0 - first).astype(dtype)


def segment_bias(seg_column, seg_row):
    return jnp.where(seg_column == seg_row, 0.0, masked_score)


class Place:
    def __init__(self, z_count):
        self.dp, self.z = lax.axis_index("dp"), lax.axis_index("fsdp")
        self.core, self.spot = lax.rem(self.dp, 2), lax.div(self.dp, 2)
        x_step = 1 - 2 * lax.rem(self.spot, 2)
        y_step = 2 - 4 * lax.div(self.spot, 2)
        self.spot_a = self.spot + (1 - self.core) * x_step + self.core * y_step
        self.spot_b = self.spot + self.core * x_step + (1 - self.core) * y_step
        self.spot_ab = self.spot + x_step + y_step
        self.sibling = (self.dp + 1 - 2 * self.core, self.z)
        self.near_a = (2 * self.spot_a + self.core, self.z)
        self.near_b = (2 * self.spot_b + self.core, self.z)
        self.z_count = z_count
        self.zs = [lax.rem(self.z + d, z_count) for d in range(z_count)]

    def chip_partners(self):
        return [self.sibling, self.near_a, self.near_b]

    def z_partners(self):
        return [(self.dp, other) for other in self.zs[1:]]


def greet(partners):
    barrier = pltpu.get_barrier_semaphore()
    for device in partners:
        pl.semaphore_signal(barrier, inc=1, device_id=device, device_id_type=pl.DeviceIdType.MESH)
    pl.semaphore_wait(barrier, len(partners))


def remote(source, target, send, receive, device):
    return pltpu.make_async_remote_copy(
        src_ref=source,
        dst_ref=target,
        send_sem=send,
        recv_sem=receive,
        device_id=device,
        device_id_type=pl.DeviceIdType.MESH,
    )


def fold(piece):
    half = piece.shape[1] // 2
    return jnp.concatenate([piece[:, :half], piece[:, half:]], axis=0)


def unfold(piece):
    rows = piece.shape[0] // 2
    return jnp.concatenate([piece[:rows], piece[rows:]], axis=1)


def looked_up(ticks, t):
    now = functools.reduce(jnp.logical_or, [t == tick for tick in ticks])
    which = sum(n * (t == tick).astype(jnp.int32) for n, tick in enumerate(ticks))
    return now, which


def run_due(stages, t):
    for ticks, stage in stages:
        if isinstance(t, int):
            if t in ticks:
                stage(ticks.index(t))
            continue
        now, block = looked_up(ticks, t)

        @pl.when(now)
        def _():
            stage(block)


PACE = 5


def sum_times(ready, pace=PACE, core=2, second=6, third=4):
    opens, cores = [], []
    for tick in ready:
        opens.append(max(tick, opens[-1] + 1) if opens else tick)
        cores.append(max(opens[-1] + core, cores[-1] + pace) if cores else opens[-1] + core)
    seconds = [tick + second for tick in cores]
    return opens, cores, seconds, [tick + third for tick in seconds]


def gather_times(opens, first=4, second=5, close=2):
    firsts = [tick + first for tick in opens]
    seconds = [tick + second for tick in firsts]
    return opens, firsts, seconds, [tick + close for tick in seconds]


def sum_scratch(count, part, width, z_count, kind=low):
    piece = (2 * part // z_count, width // 2) if kind == low else (part // z_count, width)
    return [
        pltpu.VMEM((count, 4, part, width), kind),
        pltpu.VMEM((count, 4, part, width), kind),
        pltpu.VMEM((count, 2, part, width), kind),
        pltpu.VMEM((count, part, width), kind),
        pltpu.VMEM((count, z_count) + piece, kind),
        pltpu.VMEM((count, z_count) + piece, kind),
        pltpu.SemaphoreType.DMA((count,)),
        pltpu.SemaphoreType.DMA((count, 2)),
        pltpu.SemaphoreType.DMA((count, 2, 2)),
        pltpu.SemaphoreType.DMA((count, 2)),
        pltpu.SemaphoreType.DMA((count, 2, z_count)),
    ]


SUM_REFS = 11


class BlockSum:
    def __init__(self, place, sources, refs, times):
        self.place, self.sources, self.times = place, sources, times
        (self.own, self.c, self.b, self.a, self.zs, self.zr,
         self.own_sem, self.c_sem, self.b_sem, self.a_sem, self.z_sem) = refs
        self.count = self.c.shape[0]
        self.kind = self.c.dtype
        self.z_count = self.zs.shape[1]

    def load(self, i, block):
        return pltpu.make_async_copy(block.at[:, self.place.core], self.own.at[i], self.own_sem.at[i])

    def core_copy(self, i, block):
        return remote(
            block.at[:, 1 - self.place.core], self.c.at[i], self.c_sem.at[i, 0], self.c_sem.at[i, 1], self.place.sibling
        )

    def second_copy(self, i, k):
        chunk = self.place.spot_b if k == 0 else self.place.spot_ab
        return remote(
            self.c.at[i, chunk], self.b.at[i, k], self.b_sem.at[i, 0, k], self.b_sem.at[i, 1, k], self.place.near_b
        )

    def third_copy(self, i):
        return remote(
            self.c.at[i, self.place.spot_a], self.a.at[i], self.a_sem.at[i, 0], self.a_sem.at[i, 1], self.place.near_a
        )

    def z_copy(self, i, d):
        other = self.place.zs[d]
        return remote(
            self.zs.at[i, other], self.zr.at[i, self.place.z], self.z_sem.at[i, 0, d],
            self.z_sem.at[i, 1, self.z_count - d], (self.place.dp, other),
        )

    def open(self, i):
        first = 0
        for source in self.sources:
            count = source.shape[0]

            @pl.when((i >= first) & (i < first + count))
            def _():
                block = source.at[jnp.clip(i - first, 0, count - 1)]
                self.core_copy(i, block).start()
                self.load(i, block).start()

            first += count

    def after_core(self, i):
        block = self.sources[0].at[0]
        self.core_copy(i, block).wait()
        self.load(i, block).wait()
        for k in range(4):
            self.c[i, k] = (self.c[i, k].astype(full) + self.own[i, k].astype(full)).astype(self.kind)
        self.second_copy(i, 0).start()
        self.second_copy(i, 1).start()

    def after_second(self, i):
        other, spot = self.place.spot_a, self.place.spot
        self.second_copy(i, 1).wait()
        self.c[i, other] = (self.c[i, other].astype(full) + self.b[i, 1].astype(full)).astype(self.kind)
        self.third_copy(i).start()
        self.second_copy(i, 0).wait()
        self.c[i, spot] = (self.c[i, spot].astype(full) + self.b[i, 0].astype(full)).astype(self.kind)

    def after_third(self, i):
        self.third_copy(i).wait()
        total = self.c[i, self.place.spot].astype(full) + self.a[i].astype(full)
        rows = total.shape[0] // self.z_count
        for k in range(self.z_count):
            piece = total[k * rows : (k + 1) * rows]
            self.zs[i, k] = fold(piece).astype(low) if self.kind == low else piece
        for d in range(1, self.z_count):
            self.z_copy(i, d).start()

    def finish(self, i):
        for d in range(1, self.z_count):
            self.z_copy(i, d).wait()
        total = self.zs[i, self.place.z].astype(full)
        for d in range(1, self.z_count):
            total = total + self.zr[i, self.place.zs[d]].astype(full)
        return total

    def tick(self, t):
        stages = (self.after_third, self.after_second, self.after_core, self.open)
        run_due(list(zip(self.times[::-1], stages)), t)

    @property
    def last(self):
        return self.times[3][-1]


class LineGather:
    def __init__(self, place, source, target, first, local_sem, sem, z_count):
        self.place = place
        self.source = source.at[pl.ds(first, target.shape[1])]
        self.target, self.local_sem, self.sem, self.z_count = target, local_sem, sem, z_count

    def hop_copy(self, hop, way):
        dp, z = self.place.dp, self.place.z
        if way == 0:
            piece, other, coming = z - hop + 1, z + 1, z - hop
            sends = (piece >= 0) & (other < self.z_count)
            receives = coming >= 0
        else:
            piece, other, coming = z + hop - 1, z - 1, z + hop
            sends = (piece < self.z_count) & (other >= 0)
            receives = coming < self.z_count
        piece = jnp.clip(piece, 0, self.z_count - 1)
        other = jnp.clip(other, 0, self.z_count - 1)
        source = self.source if hop == 1 else self.target.at[piece]
        copy = remote(source, self.target.at[piece], self.sem.at[way, 0, hop - 1], self.sem.at[way, 1, hop - 1], (dp, other))
        return copy, sends, receives

    def local(self):
        return pltpu.make_async_copy(self.source, self.target.at[self.place.z], self.local_sem)

    def start(self, hop):
        if hop == 1:
            self.local().start()
        for way in range(2):
            copy, sends, _ = self.hop_copy(hop, way)

            @pl.when(sends)
            def _():
                copy.start()

    def wait(self, hop):
        if hop == 1:
            self.local().wait()
        for way in range(2):
            copy, sends, receives = self.hop_copy(hop, way)

            @pl.when(sends)
            def _():
                copy.wait_send()

            @pl.when(receives)
            def _():
                copy.wait_recv()

    def advance(self, hop):
        if hop > 1:
            self.wait(hop - 1)
        if hop < self.z_count:
            self.start(hop)


def gather_scratch(count, rows, width, z_count, kind=low):
    piece = (2 * rows // z_count, width // 2) if kind == low else (rows // z_count, width)
    return [
        pltpu.VMEM((count, z_count) + piece, kind),
        pltpu.SemaphoreType.DMA((count, 2, z_count)),
        pltpu.SemaphoreType.DMA((count, 2)),
        pltpu.SemaphoreType.DMA((count, 2, 2)),
        pltpu.SemaphoreType.DMA((count, 2)),
    ]


GATHER_REFS = 5


class BlockGather:
    def __init__(self, place, source, whole, base, refs, times):
        self.times = times
        self.place, self.source, self.whole, self.base = place, source, whole, base
        self.zr, self.z_sem, self.a_sem, self.b_sem, self.c_sem = refs
        self.count, self.z_count = self.zr.shape[0], self.zr.shape[1]

    def z_copy(self, i, d):
        place = self.place
        return remote(
            self.source.at[i], self.zr.at[i, place.z], self.z_sem.at[i, 0, d], self.z_sem.at[i, 1, self.z_count - d],
            (place.dp, place.zs[d]),
        )

    def chunk(self, i, spot):
        return self.whole.at[self.base + i, spot, self.place.core]

    def first_copy(self, i):
        chunk = self.chunk(i, self.place.spot)
        return remote(chunk, chunk, self.a_sem.at[i, 0], self.a_sem.at[i, 1], self.place.near_a)

    def second_copy(self, i, k):
        chunk = self.chunk(i, self.place.spot if k == 0 else self.place.spot_a)
        return remote(chunk, chunk, self.b_sem.at[i, 0, k], self.b_sem.at[i, 1, k], self.place.near_b)

    def core_copy(self, i):
        chunks = self.whole.at[self.base + i, :, self.place.core]
        return remote(chunks, chunks, self.c_sem.at[i, 0], self.c_sem.at[i, 1], self.place.sibling)

    AHEAD = 3

    def announce(self, i):
        for d in range(1, self.z_count):
            self.z_copy(i, d).start()
        self.zr[i, self.place.z] = self.source[i]

    def begin(self):
        for i in range(min(self.AHEAD, self.count)):
            self.announce(i)

    def open(self, i):
        for d in range(1, self.z_count):
            self.z_copy(i, d).wait()
        pieces = [self.zr[i, k].astype(full) for k in range(self.z_count)]
        if self.zr.dtype == low:
            pieces = [unfold(piece) for piece in pieces]
        whole = jnp.concatenate(pieces, axis=0).astype(self.whole.dtype)
        self.whole[self.base + i, self.place.spot, self.place.core] = whole
        self.first_copy(i).start()
        self.second_copy(i, 0).start()

    def after_first(self, i):
        self.first_copy(i).wait()
        self.second_copy(i, 1).start()

    def after_second(self, i):
        self.second_copy(i, 0).wait()
        self.second_copy(i, 1).wait()
        self.core_copy(i).start()

    def close(self, i):
        self.core_copy(i).wait()

    def tick(self, t, done=None):
        def close(i):
            self.close(i)
            if done is not None:
                done(i)

        opens, firsts, seconds, closes = self.times
        run_due([(seconds, self.after_second), (firsts, self.after_first), (opens, self.open)], t)
        later = opens[: max(self.count - self.AHEAD, 0)]
        if later:
            run_due([(later, lambda i: self.announce(i + self.AHEAD))], t)
        run_due([(closes, close)], t)


def split_refs(refs, *counts):
    result, start = [], 0
    for count in counts:
        result.append(refs[start : start + count])
        start += count
    return result


class Side:
    def __init__(self, plan, sources, targets, sum_refs, line_refs, own=None):
        self.plan = plan
        sums = plan.sums
        blocks = [source.at[pl.ds(plan.skip, source.shape[0] - plan.skip)] for source in sources[:sums]]
        blocks += [own] if plan.own else []
        self.place = Place(plan.z_count) if plan.active else None
        self.sum = BlockSum(self.place, blocks, sum_refs, plan.times) if plan.total else None
        self.result = targets[0] if plan.total else None
        self.lines = line_gathers(self.place, plan.lines, sources[sums:], targets[bool(plan.total) :], line_refs, plan.z_count)

    def enter(self, now):
        if not self.plan.active:
            return

        @pl.when(now)
        def _():
            greet((self.place.chip_partners() if self.plan.total else []) + self.place.z_partners())
            for line in self.lines:
                line.advance(1)

    def tick(self, t):
        if self.plan.total:
            self.sum.tick(t)

    def leave(self, now, ticks):
        if not self.plan.active:
            return

        @pl.when(now)
        def _():
            if self.plan.total:
                if self.sum.last >= ticks:
                    lax.fori_loop(ticks, self.sum.last + 1, lambda t, carry: (self.tick(t), carry)[1], 0)
                for i in range(self.sum.count):
                    self.result[i] = self.sum.finish(i).astype(low)
            for line in self.lines:
                line.advance(self.plan.z_count)

    def advance(self, now, hop):
        if self.lines and hop < self.plan.z_count:
            @pl.when(now)
            def _():
                for line in self.lines:
                    line.advance(hop)


class Plan:
    def __init__(self, pending=None, lines=(), z_count=1, own=0, size=None, ready=(), skip=0):
        self.z_count = z_count
        self.sums = int(pending is not None)
        self.own, self.skip = own, skip
        self.total = own + (pending.shape[0] - skip if self.sums else 0)
        self.times = sum_times(ready) if self.total else None
        self.lines = [(first, count) for _, first, count in lines]
        self.active = bool(self.total or lines)
        self.arguments, self.results, self.result_specs, self.scratch = [], [], [], []
        if self.sums:
            self.arguments.append(pending)
        if self.total:
            part, width = size
            self.results.append(jax.ShapeDtypeStruct((self.total, 2 * part // z_count, width // 2), low))
            self.result_specs.append(
                pl.BlockSpec(self.results[0].shape, lambda i: (0, 0, 0), pipeline_mode=pl.Buffered(1))
            )
            self.scratch += sum_scratch(self.total, part, width, z_count)
        for basis, _, count in lines:
            self.arguments.append(basis)
            self.results.append(jax.ShapeDtypeStruct((z_count, count) + basis.shape[1:], low))
            self.result_specs.append(ANYWHERE)
        self.scratch += line_scratch(len(lines), z_count)
        self.argument_specs = [ANYWHERE] * len(self.arguments)

    def split(self, refs, inputs, outputs, scratch):
        count = len(self.lines)
        return split_refs(
            refs, inputs, self.sums + count, outputs, bool(self.total) + count, scratch,
            SUM_REFS * bool(self.total), 2 * bool(self.lines),
        )


def line_scratch(count, z_count):
    if not count:
        return []
    return [pltpu.SemaphoreType.DMA((count,)), pltpu.SemaphoreType.DMA((count, 2, 2, z_count - 1))]


def line_gathers(place, spans, sources, targets, refs, z_count):
    return [
        LineGather(place, source, target, first, refs[0].at[n], refs[1].at[n], z_count)
        for n, (source, target, (first, _)) in enumerate(zip(sources, targets, spans))
    ]


ANYWHERE = pl.BlockSpec(memory_space=pl.ANY)
IN_VMEM = pl.BlockSpec(memory_space=pltpu.VMEM)


def forward_kernel(plan, *refs):
    inputs, sources, outputs, targets, scratch, gather_refs, vec_refs, line_refs = plan.split(refs)
    x_ref, segc_ref, segr_ref, vec_ref, w_hbm = inputs
    (q_ref, k_ref, v_ref, ctxt_ref, lse_ref, x1_ref, inv1_ref, n1_ref, u_ref, gp_ref, x2_ref, inv2_ref,
     out_ref) = outputs
    w, bias, vt, n1_all, acc, w_sem = scratch
    s = pl.program_id(0)
    tokens, width = acc.shape
    rows_now = x_ref.shape[0]
    rows = tokens // rows_now
    inner = plan.inner
    local = plan.local
    gather = vec_gather = None
    place = Place(plan.z_count) if plan.gathered else None
    if plan.gathered:
        w_out, out_sem = targets[0], scratch_tail(plan, refs)
        gather = BlockGather(place, sources[0], w, local, gather_refs, plan.times)
        if plan.vectors:
            vec_gather = BlockGather(place, sources[1], plan.vec_whole(refs), 0, vec_refs, gather_times([0], 2, 3, 2))
            vec_ref = targets[1]
    lines = line_gathers(place, plan.lines, sources[plan.line_at :], targets[plan.line_target_at :], line_refs, plan.z_count)

    def keep(i):
        return pltpu.make_async_copy(w.at[local + i], w_out.at[i], out_sem.at[i])

    def load(j):
        return pltpu.make_async_copy(w_hbm.at[plan.order[j]], w.at[j], w_sem.at[j])

    def matrix(j):
        return w[j].reshape(width, width)

    def arrive(j):
        if j < local:
            load(j).wait()

    def tick(t):
        if gather is not None:
            gather.tick(t, lambda i: keep(i).start())
            if vec_gather is not None:
                vec_gather.tick(t)

    pairs = width // PAIR
    row_ticks = 2 * pairs + 1

    @pl.when(s == 0)
    def _():
        for j in range(local):
            load(j).start()
        if gather is not None:
            greet(place.chip_partners() + place.z_partners())
            if vec_gather is not None:
                vec_gather.begin()
            gather.begin()
            lax.fori_loop(0, plan.lead, lambda t, carry: (tick(t), carry)[1], 0)
            for line in lines:
                line.advance(1)
            if vec_gather is not None:
                turned = vec_gather.whole[0].reshape(width, vec_gather.whole.shape[-1]).T
                for layer in range(2):
                    count = plan.vector_rows
                    targets[1 + layer][0:count, :] = turned[layer * count : (layer + 1) * count, :]
        for j in range(min(local, 3)):
            arrive(j)

    @pl.when(s < rows)
    def _():
        xin = x_ref[...].astype(low)
        bias[...] = segment_bias(segc_ref[0], segr_ref[0])
        q_ref[...] = (dot_nn(xin, matrix(0)) + vec_ref[0:1, :]).astype(low)
        k_ref[...] = dot_nn(xin, matrix(1)).astype(low)
        value = dot_nn(xin, matrix(2)) + vec_ref[1:2, :]
        v_ref[...] = value.astype(low)
        vt[...] = value.T.astype(low)
        masks = half_masks(low)

        def pair_step(p, carry):
            lanes = pl.ds(pl.multiple_of(p * PAIR, PAIR), PAIR)
            q_pair = q_ref[:, lanes] * jnp.asarray(HD ** (-0.5), low)
            k_pair = k_ref[:, lanes]
            for h in range(2):
                scores = dot_nt(k_pair, q_pair * masks[h]) + bias[...]
                largest = jnp.max(scores, axis=0, keepdims=True)
                expanded = jnp.exp(scores - largest)
                total = column_sum(expanded)
                here = pl.ds(pl.multiple_of(p * PAIR + h * HD, HD), HD)
                context = dot_nn(vt[here, :], expanded.astype(low)) * (1.0 / total)
                ctxt_ref[here, :] = context.astype(low)
                lse_ref[0, pl.ds(2 * p + h, 1), :] = largest + jnp.log(total)
                tick(plan.lead + s * row_ticks + 2 * p + h)
            return carry

        lax.fori_loop(0, pairs, pair_step, 0)

        @pl.when(s == 0)
        def _():
            if local > 3:
                arrive(3)
            for line in lines:
                line.advance(2)

        context = ctxt_ref[...].astype(full).T.astype(low)
        attended = dot_nn(context, matrix(3)) + vec_ref[2:3, :]
        unit, inverse = norm_parts(x_ref[...].astype(full) + attended)
        x1_ref[...] = unit
        inv1_ref[...] = inverse
        normed = unit * vec_ref[3:4, :] + vec_ref[4:5, :]
        here = pl.ds(pl.multiple_of(s * rows_now, rows_now), rows_now)
        acc[here, :] = normed + vec_ref[5 + inner : 6 + inner, :]
        normed = normed.astype(low)
        n1_ref[...] = normed
        n1_all[here, :] = normed

        tick(plan.lead + s * row_ticks + 2 * pairs)

    tile = tokens // 4
    starts, firsts = plan.step_ticks(rows * row_ticks)

    @pl.when(s >= rows)
    def _():
        c = s - rows

        @pl.when(c == 0)
        def _():
            for j in range(4, local):
                arrive(j)
            for line in lines:
                line.advance(3)

        start = sum(n * (c == k).astype(jnp.int32) for k, n in enumerate(starts))
        first = sum(n * (c == k).astype(jnp.int32) for k, n in enumerate(firsts))
        if gather is not None:
            lax.fori_loop(start, first, lambda t, carry: (tick(t), carry)[1], 0)

        def token_step(i, carry):
            for half in range(2):
                here = pl.ds(pl.multiple_of((2 * i + half) * tile, tile), tile)
                value, slope = gelu_parts(dot_nn(n1_all[here, :], matrix(4 + 2 * c)) + vec_ref[pl.ds(5 + c, 1), :])
                active = value.astype(low)
                u_ref[here, :] = active
                gp_ref[here, :] = slope.astype(low)
                acc[here, :] += dot_nn(active, matrix(5 + 2 * c))
                tick(first + 2 * i + half)
            return carry

        lax.fori_loop(0, 2, token_step, 0)

        @pl.when(c == inner - 1)
        def _():
            base = 5 + inner

            def last(i, carry):
                here = pl.ds(pl.multiple_of(i * tile, tile), tile)
                unit, inverse = norm_parts(acc[here, :])
                x2_ref[here, :] = unit
                inv2_ref[here, :] = inverse
                out_ref[here, :] = (
                    unit * vec_ref[base + 1 : base + 2, :] + vec_ref[base + 2 : base + 3, :]
                ).astype(out_ref.dtype)
                return carry

            lax.fori_loop(0, 4, last, 0)
            if gather is not None:
                lax.fori_loop(
                    firsts[-1] + 4, plan.times[3][-1] + 1, lambda t, carry: (tick(t), carry)[1], 0
                )
                for line in lines:
                    line.advance(plan.z_count)
                for i in range(gather.count):
                    keep(i).wait()


class ForwardPlan:
    def __init__(self, inner, local, shards=None, vec_shard=None, vector_rows=0, lines=(), lead=0, opens=(), z_count=1):
        self.inner, self.local, self.lead, self.z_count = inner, local, lead, z_count
        self.times = gather_times(opens) if opens else None
        self.vector_rows = vector_rows
        self.order = [0, 1, 2, 3]
        for c in range(inner):
            self.order += [4 + c, 4 + inner + c]
        self.gathered = 0 if shards is None else shards.shape[0]
        self.vectors = vec_shard is not None
        self.lines = [(first, count) for _, first, count in lines]
        self.line_at = int(self.gathered > 0) + int(self.vectors)
        self.line_target_at = int(self.gathered > 0) + 2 * int(self.vectors)
        self.arguments, self.argument_specs, self.results, self.result_specs, self.scratch = [], [], [], [], []
        shape = jax.ShapeDtypeStruct
        if self.gathered:
            width = 2 * shards.shape[2]
            self.arguments.append(shards)
            self.argument_specs.append(IN_VMEM)
            self.results.append(shape((self.gathered, 4, 2, width // 8, width), low))
            self.result_specs.append(ANYWHERE)
            self.scratch += gather_scratch(self.gathered, width // 8, width, z_count)
        if self.vectors:
            rows, lanes = vec_shard.shape[1:]
            self.arguments.append(vec_shard)
            self.argument_specs.append(IN_VMEM)
            for _ in range(2):
                self.results.append(shape((16, width), full))
                self.result_specs.append(pl.BlockSpec((16, width), lambda s: (0, 0)))
            self.scratch += gather_scratch(1, width // 8, lanes, z_count, full)
        for basis, _, count in lines:
            self.arguments.append(basis)
            self.argument_specs.append(ANYWHERE)
            self.results.append(shape((z_count, count) + basis.shape[1:], low))
            self.result_specs.append(ANYWHERE)
        self.scratch += line_scratch(len(lines), z_count)
        if self.gathered:
            self.scratch.append(pltpu.SemaphoreType.DMA((self.gathered,)))
        if self.vectors:
            self.scratch.append(pltpu.VMEM((1, 4, 2, width // 8, lanes), full))

    def step_ticks(self, row_ticks):
        starts, firsts = [], []
        now = self.lead + row_ticks
        for c in range(self.inner):
            starts.append(now)
            needed = 5 + 2 * c - self.local
            firsts.append(max(now, self.times[3][needed] + 1) if self.times else now)
            now = firsts[-1] + 4
        return starts, firsts

    def split(self, refs):
        return split_refs(
            refs, 5, len(self.arguments), 13, len(self.results), 6, GATHER_REFS * bool(self.gathered),
            GATHER_REFS * self.vectors, 2 * bool(self.lines),
        )

    def vec_whole(self, refs):
        return refs[-1]


def scratch_tail(plan, refs):
    return refs[-2] if plan.vectors else refs[-1]


def forward_layer(hidden, seg_column, seg_row, vectors, weights, out_dtype, plan, identity=None):
    tokens, width = hidden.shape
    inner = plan.inner
    wide = width * inner
    rows = tokens // L
    heads = width // HD
    shape = jax.ShapeDtypeStruct

    def here(s):
        return jnp.minimum(s, rows - 1)

    def column(s):
        return jnp.maximum(s - rows, 0)

    def row_block(columns):
        return pl.BlockSpec((L, columns), lambda s: (here(s), 0))

    def whole(columns):
        return pl.BlockSpec((tokens, columns), lambda s: (0, 0), pipeline_mode=pl.Buffered(1))

    wide_block = pl.BlockSpec((tokens, width), lambda s: (0, column(s)))
    out_shape = (
        shape((tokens, width), low), shape((tokens, width), low), shape((tokens, width), low),
        shape((width, tokens), low), shape((rows, heads, L), full),
        shape((tokens, width), full), shape((tokens, 1), full), shape((tokens, width), low),
        shape((tokens, wide), low), shape((tokens, wide), low),
        shape((tokens, width), full), shape((tokens, 1), full), shape((tokens, width), out_dtype),
        *plan.results,
    )
    out_specs = (
        row_block(width), row_block(width), row_block(width),
        pl.BlockSpec((width, L), lambda s: (0, here(s))), pl.BlockSpec((1, heads, L), lambda s: (here(s), 0, 0)),
        row_block(width), row_block(1), row_block(width),
        wide_block, wide_block,
        whole(width), whole(1), whole(width),
        *plan.result_specs,
    )
    total = 4 + 2 * inner
    held = max(total, plan.local + plan.gathered)
    return pl.pallas_call(
        functools.partial(forward_kernel, plan),
        grid=(rows + inner,),
        out_shape=out_shape,
        in_specs=[
            row_block(width),
            pl.BlockSpec((1, L, 1), lambda s: (here(s), 0, 0)),
            pl.BlockSpec((1, 1, L), lambda s: (here(s), 0, 0)),
            pl.BlockSpec(vectors.shape, lambda s: (0, 0)),
            ANYWHERE,
            *plan.argument_specs,
        ],
        out_specs=out_specs,
        scratch_shapes=[
            pltpu.VMEM((held, 4, 2, width // 8, width), low),
            pltpu.VMEM((L, L), full),
            pltpu.VMEM((width, L), low),
            pltpu.VMEM((tokens, width), low),
            pltpu.VMEM((tokens, width), full),
            pltpu.SemaphoreType.DMA((total,)),
            *plan.scratch,
        ],
        compiler_params=pltpu.CompilerParams(
            dimension_semantics=("arbitrary",), vmem_limit_bytes=62 * MIB,
            collective_id=identity, has_side_effects=identity is not None,
        ),
        cost_estimate=pl.CostEstimate(
            flops=2 * tokens * width * width * total + 4 * tokens * L * width,
            bytes_accessed=40 * MIB,
            transcendentals=tokens * (L * heads + wide),
        ),
        name="layer_forward",
    )(hidden, seg_column, seg_row, vectors, weights.reshape(-1, 4, 2, width // 8, width), *plan.arguments)


WIDE_STEP_TICKS = 6


def wide_ready(own):
    return [4 + WIDE_STEP_TICKS * (n // 2) + 4 + n % 2 for n in range(own)]


def wide_back_kernel(plan, inner, *refs):
    inputs, sources, outputs, targets, scratch, sum_refs, line_refs = plan.split(refs, 11, 4, 11)
    up_hbm, x2_hbm, inv2_hbm, x1_hbm, inv1_hbm, n1_hbm, vec_ref, wup_ref, wdown_ref, u_ref, gp_ref = inputs
    dw_ref, dr1_ref, da_ref, dvec_ref = outputs
    n1t, dz, kept_dw, up_ref, x2_ref, inv2_ref, x1_ref, inv1_ref, n1_ref, tile_sem, load_sem = scratch
    dy, dn1 = da_ref, dr1_ref
    c = pl.program_id(0)
    steps = pl.num_programs(0)
    tokens, width = dn1.shape
    tile = tokens // 4
    base = 5 + inner
    side = Side(plan, sources, targets, sum_refs, line_refs, kept_dw)

    def tile_copies(i):
        rows = pl.ds(pl.multiple_of(i * tile, tile), tile)
        return [
            pltpu.make_async_copy(source.at[rows], target.at[rows], tile_sem.at[n, i])
            for n, (source, target) in enumerate(((up_hbm, up_ref), (x2_hbm, x2_ref), (inv2_hbm, inv2_ref)))
        ]

    late_copies = [
        pltpu.make_async_copy(source, target, load_sem.at[n])
        for n, (source, target) in enumerate(((n1_hbm, n1_ref), (x1_hbm, x1_ref), (inv1_hbm, inv1_ref)))
    ]

    @pl.when(c == 0)
    def _():
        for i in range(4):
            for copy in tile_copies(i):
                copy.start()
        for copy in late_copies:
            copy.start()

    side.enter(c == 0)

    @pl.when(c == 0)
    def _():
        gain = vec_ref[base + 1 : base + 2, :]

        def body(i, carry):
            for copy in tile_copies(i):
                copy.wait()
            gain_sum, shift_sum, bias_sum = carry
            rows = pl.ds(pl.multiple_of(i * tile, tile), tile)
            upstream = up_ref[rows, :].astype(full)
            unit = x2_ref[rows, :]
            back = norm_back(upstream, unit, inv2_ref[rows, :], gain)
            dn1[rows, :] = back
            branch = back.astype(low)
            dy[rows, :] = branch
            side.tick(i)
            return (
                gain_sum + column_sum(upstream * unit),
                shift_sum + column_sum(upstream),
                bias_sum + column_sum(branch.astype(full)),
            )

        zero = jnp.zeros((1, width), full)
        gain_sum, shift_sum, bias_sum = lax.fori_loop(0, 4, body, (zero, zero, zero))
        dvec_ref[...] = jnp.zeros(dvec_ref.shape, full)
        dvec_ref[base : base + 1, :] = bias_sum
        dvec_ref[base + 1 : base + 2, :] = gain_sum
        dvec_ref[base + 2 : base + 3, :] = shift_sum
        late_copies[0].wait()
        n1t[...] = n1_ref[...].astype(full).T.astype(low)

    first_tick = 4 + WIDE_STEP_TICKS * c

    def token_step(i, carry):
        rows = pl.ds(pl.multiple_of(i * tile, tile), tile)
        slope = gp_ref[rows, :].astype(full)
        piece = (dot_nt(dy[rows, :], wdown_ref[0]) * slope).astype(low)
        dz[rows, :] = piece
        dn1[rows, :] += dot_nt(piece, wup_ref[0])
        side.advance(4 * c + i == 5, 2)
        side.advance(4 * c + i == 10, 3)
        side.tick(first_tick + i)
        return carry + column_sum(piece.astype(full))

    bias_sum = lax.fori_loop(0, 4, token_step, jnp.zeros((1, width), full))
    for j in range(inner):
        @pl.when(c == j)
        def _():
            dvec_ref[5 + j : 6 + j, :] = bias_sum

    def store(k, grad):
        if plan.own:
            @pl.when(2 * c + k < plan.own)
            def _():
                kept_dw[2 * c + k] = grad.reshape(kept_dw.shape[1:])

            @pl.when(2 * c + k >= plan.own)
            def _():
                dw_ref[k, 0] = grad
        else:
            dw_ref[k, 0] = grad

    store(0, dot_nn(n1t[...], dz[...]).astype(low))
    side.tick(first_tick + 4)
    store(1, dot_tn(u_ref[...], dy[...]).astype(low))
    side.tick(first_tick + 5)
    final_tick = 4 + WIDE_STEP_TICKS * inner

    @pl.when(c == steps - 1)
    def _():
        for copy in late_copies[1:]:
            copy.wait()
        gain = vec_ref[3:4, :]

        def body(i, carry):
            gain_sum, shift_sum, bias_sum = carry
            rows = pl.ds(pl.multiple_of(i * tile, tile), tile)
            upstream = dn1[rows, :]
            unit = x1_ref[rows, :]
            back = norm_back(upstream, unit, inv1_ref[rows, :], gain)
            dr1_ref[rows, :] = back
            branch = back.astype(low)
            da_ref[rows, :] = branch
            side.tick(final_tick + i)
            return (
                gain_sum + column_sum(upstream * unit),
                shift_sum + column_sum(upstream),
                bias_sum + column_sum(branch.astype(full)),
            )

        zero = jnp.zeros((1, width), full)
        gain_sum, shift_sum, bias_sum = lax.fori_loop(0, 4, body, (zero, zero, zero))
        dvec_ref[2:3, :] = bias_sum
        dvec_ref[3:4, :] = gain_sum
        dvec_ref[4:5, :] = shift_sum

    side.leave(c == steps - 1, final_tick + 4)


def wide_back(upstream, kept, vectors, weights, places, plan, identity=None):
    x1, inv1, n1, u, gp, x2, inv2 = kept
    tokens, width = x1.shape
    up_start, down_start, stride = places
    inner = u.shape[1] // width
    shape = jax.ShapeDtypeStruct

    return pl.pallas_call(
        functools.partial(wide_back_kernel, plan, inner),
        grid=(inner,),
        out_shape=(
            shape((2, inner - plan.own // 2, width, width), low),
            shape((tokens, width), full), shape((tokens, width), low), shape((16, width), full),
            *plan.results,
        ),
        in_specs=[
            *[ANYWHERE] * 6,
            pl.BlockSpec(vectors.shape, lambda c: (0, 0), pipeline_mode=pl.Buffered(1)),
            pl.BlockSpec((1, width, width), lambda c: (up_start + stride * c, 0, 0)),
            pl.BlockSpec((1, width, width), lambda c: (down_start + stride * c, 0, 0)),
            pl.BlockSpec((tokens, width), lambda c: (0, c)),
            pl.BlockSpec((tokens, width), lambda c: (0, c)),
            *plan.argument_specs,
        ],
        out_specs=(
            pl.BlockSpec((2, 1, width, width), lambda c: (0, jnp.maximum(c - plan.own // 2, 0), 0, 0)),
            pl.BlockSpec((tokens, width), lambda c: (0, 0), pipeline_mode=pl.Buffered(1)),
            pl.BlockSpec((tokens, width), lambda c: (0, 0), pipeline_mode=pl.Buffered(1)),
            pl.BlockSpec((16, width), lambda c: (0, 0)),
            *plan.result_specs,
        ),
        scratch_shapes=[
            pltpu.VMEM((width, tokens), low),
            pltpu.VMEM((tokens, width), low),
            pltpu.VMEM((plan.own, 4, 2, width // 8, width) if plan.own else (8, 128), low),
            pltpu.VMEM((tokens, width), upstream.dtype),
            pltpu.VMEM((tokens, width), full),
            pltpu.VMEM((tokens, 1), full),
            pltpu.VMEM((tokens, width), full),
            pltpu.VMEM((tokens, 1), full),
            pltpu.VMEM((tokens, width), low),
            pltpu.SemaphoreType.DMA((3, 4)),
            pltpu.SemaphoreType.DMA((3,)),
            *plan.scratch,
        ],
        compiler_params=pltpu.CompilerParams(
            dimension_semantics=("arbitrary",), vmem_limit_bytes=60 * MIB,
            collective_id=identity, has_side_effects=identity is not None,
        ),
        cost_estimate=pl.CostEstimate(
            flops=8 * tokens * width * width * inner, bytes_accessed=50 * MIB, transcendentals=0
        ),
        name="wide_backward",
    )(upstream, x2, inv2, x1, inv1, n1, vectors, weights, weights, u, gp, *plan.arguments)


def attend_back_kernel(plan, *refs):
    inputs, sources, outputs, targets, scratch, sum_refs, line_refs = plan.split(refs, 11, 3, 14)
    da_hbm, dr1_ref, x_ref, q_ref, k_ref, v_ref, ctxt_hbm, lse_ref, segc_ref, segr_ref, w_hbm = inputs
    dw_ref, dx_ref, dvec_ref = outputs
    bias, dctx, kt, delta, dqt, xt, dq_all, dk_all, dv_all, dwo, da_ref, ctxt_ref, w_ref, load_sem = scratch
    r = pl.program_id(0)
    loads = [
        pltpu.make_async_copy(w_hbm.at[plan.start + 3], w_ref.at[3], load_sem.at[0]),
        pltpu.make_async_copy(da_hbm, da_ref, load_sem.at[1]),
        pltpu.make_async_copy(ctxt_hbm, ctxt_ref, load_sem.at[2]),
        pltpu.make_async_copy(w_hbm.at[pl.ds(plan.start, 3)], w_ref.at[pl.ds(0, 3)], load_sem.at[3]),
    ]

    @pl.when(r == 0)
    def _():
        for copy in loads:
            copy.start()

    side = Side(plan, sources, targets, sum_refs, line_refs, dwo)
    side.enter(r == 0)
    tokens, width = dr1_ref.shape
    pairs = width // PAIR
    ticks = 2 * pairs + 4

    def tick(n):
        side.tick(r * ticks + n)

    tick(0)
    here = pl.ds(pl.multiple_of(r * tokens, tokens), tokens)

    @pl.when(r == 0)
    def _():
        for copy in loads[:3]:
            copy.wait()
        grad = dot_nn(ctxt_ref[...], da_ref[...]).astype(low)
        if plan.own:
            dwo[0] = grad.reshape(dwo.shape[1:])
        else:
            dw_ref[3] = grad

    xt[:, here] = x_ref[...].astype(low).astype(full).T.astype(low)
    bias[...] = segment_bias(segc_ref[0], segr_ref[0])
    context_grad = dot_nt(da_ref[here, :], w_ref[3]).astype(low)
    dctx[...] = context_grad
    kt[...] = k_ref[...].astype(full).T.astype(low)
    products = context_grad.astype(full) * ctxt_ref[:, here].astype(full).T
    feature = lax.broadcasted_iota(jnp.int32, (16, width), 1)
    head = lax.broadcasted_iota(jnp.int32, (16, width), 0)
    member = ((feature >= head * HD) & (feature < (head + 1) * HD)).astype(full).astype(low)
    high = products.astype(low)
    rest = (products - high.astype(full)).astype(low)
    delta[...] = dot_nt(member, high) + dot_nt(member, rest)
    tick(1)
    masks = half_masks(low)
    scale = HD ** (-0.5)

    def pair_step(p, carry):
        lanes = pl.ds(pl.multiple_of(p * PAIR, PAIR), PAIR)
        q_pair = q_ref[:, lanes] * jnp.asarray(scale, low)
        k_pair = k_ref[:, lanes]
        v_pair = v_ref[:, lanes]
        g_pair = dctx[:, lanes]
        key_grad = jnp.zeros((tokens, PAIR), full)
        value_grad = jnp.zeros((tokens, PAIR), full)
        for h in range(2):
            q_half = q_pair * masks[h]
            g_half = g_pair * masks[h]
            scores = dot_nt(k_pair, q_half) + bias[...]
            attention = jnp.exp(scores - lse_ref[0, pl.ds(2 * p + h, 1), :])
            value_grad = value_grad + dot_nn(attention.astype(low), g_half)
            attention_grad = dot_nt(v_pair, g_half)
            score_grad = (attention * (attention_grad - delta[pl.ds(2 * p + h, 1), :])).astype(low)
            key_grad = key_grad + dot_nn(score_grad, q_half)
            rows = pl.ds(pl.multiple_of(p * PAIR + h * HD, HD), HD)
            dqt[rows, :] = dot_nn(kt[rows, :], score_grad) * scale
            tick(2 + 2 * p + h)
        dk_all[here, lanes] = key_grad.astype(low)
        dv_all[here, lanes] = value_grad.astype(low)
        side.advance((r == 0) & (p == 4), 2)
        side.advance((r == 1) & (p == 3), 3)
        return carry

    lax.fori_loop(0, pairs, pair_step, 0)
    tick(2 + 2 * pairs)

    @pl.when(r == 0)
    def _():
        loads[3].wait()

    query_grad = dqt[...].T.astype(low)
    dq_all[here, :] = query_grad
    key_grad = dk_all[here, :]
    value_grad = dv_all[here, :]
    dx_ref[...] = (
        dr1_ref[...]
        + dot_nt(query_grad, w_ref[0])
        + dot_nt(key_grad, w_ref[1])
        + dot_nt(value_grad, w_ref[2])
    )
    tick(3 + 2 * pairs)

    @pl.when(r == 0)
    def _():
        dvec_ref[...] = jnp.zeros(dvec_ref.shape, full)

    dvec_ref[0:1, :] += column_sum(query_grad.astype(full))
    dvec_ref[1:2, :] += column_sum(value_grad.astype(full))

    @pl.when(r == pl.num_programs(0) - 1)
    def _():
        for j, grad in enumerate((dq_all, dk_all, dv_all)):
            dw_ref[j] = dot_nn(xt[...], grad[...]).astype(low)
            side.tick(plan.rows * ticks + j)

    side.leave(r == pl.num_programs(0) - 1, plan.rows * ticks + 3)


def attend_back(da, dr1, hidden, kept, seg_column, seg_row, weights, start, plan, identity=None):
    q, k, v, ctxt, lse = kept
    tokens, width = da.shape
    rows = tokens // L
    heads = width // HD
    shape = jax.ShapeDtypeStruct
    plan.start, plan.rows = start, rows

    def row_block():
        return pl.BlockSpec((L, width), lambda r: (r, 0))

    return pl.pallas_call(
        functools.partial(attend_back_kernel, plan),
        grid=(rows,),
        out_shape=(
            shape((4 - plan.own, width, width), low), shape((tokens, width), full), shape((8, width), full),
            *plan.results,
        ),
        in_specs=[
            ANYWHERE,
            row_block(), row_block(), row_block(), row_block(), row_block(),
            ANYWHERE,
            pl.BlockSpec((1, heads, L), lambda r: (r, 0, 0)),
            pl.BlockSpec((1, L, 1), lambda r: (r, 0, 0)),
            pl.BlockSpec((1, 1, L), lambda r: (r, 0, 0)),
            ANYWHERE,
            *plan.argument_specs,
        ],
        out_specs=(
            pl.BlockSpec((4 - plan.own, width, width), lambda r: (0, 0, 0), pipeline_mode=pl.Buffered(1)),
            row_block(),
            pl.BlockSpec((8, width), lambda r: (0, 0)),
            *plan.result_specs,
        ),
        scratch_shapes=[
            pltpu.VMEM((L, L), full),
            pltpu.VMEM((L, width), low),
            pltpu.VMEM((width, L), low),
            pltpu.VMEM((16, L), full),
            pltpu.VMEM((width, L), full),
            pltpu.VMEM((width, tokens), low),
            pltpu.VMEM((tokens, width), low),
            pltpu.VMEM((tokens, width), low),
            pltpu.VMEM((tokens, width), low),
            pltpu.VMEM((1, 4, 2, width // 8, width) if plan.own else (8, 128), low),
            pltpu.VMEM((tokens, width), low),
            pltpu.VMEM((width, tokens), low),
            pltpu.VMEM((4, width, width), low),
            pltpu.SemaphoreType.DMA((4,)),
            *plan.scratch,
        ],
        compiler_params=pltpu.CompilerParams(
            dimension_semantics=("arbitrary",), vmem_limit_bytes=60 * MIB,
            collective_id=identity, has_side_effects=identity is not None,
        ),
        cost_estimate=pl.CostEstimate(
            flops=16 * tokens * width * width + 10 * tokens * L * width,
            bytes_accessed=30 * MIB,
            transcendentals=tokens * L * heads,
        ),
        name="attend_backward",
    )(da, dr1, hidden, q, k, v, ctxt, lse, seg_column, seg_row, weights, *plan.arguments)


def moments(rotated, first, second):
    first_new = beta_one * first + (1.0 - beta_one) * rotated
    second_new = beta_two * second + (1.0 - beta_two) * rotated * rotated
    direction = (
        first_new
        / (1.0 - beta_one**STEP)
        / (jnp.sqrt(second_new / (1.0 - beta_two**STEP)) + adam_epsilon)
    )
    return first_new, second_new, direction


def pack_lanes(piece):
    rows = piece.shape[0] // 2
    return jnp.concatenate([piece[:rows], piece[rows:]], axis=1)


def unpack_lanes(piece):
    columns = piece.shape[1] // 2
    return jnp.concatenate([piece[:, :columns], piece[:, columns:]], axis=0)


def optimizer_kernel(plan, *refs):
    inputs, ready, dvecs, bases, lines_in, outputs, lines_out, scratch, sum_refs, vec_refs, line_refs = split_refs(
        refs, 6, plan.ready, plan.dvecs, plan.bases, len(plan.spans), 5, len(plan.spans), 21, SUM_REFS, SUM_REFS,
        2 * bool(plan.spans),
    )
    index_ref, place_ref, tail_hbm, first_hbm, second_hbm, blocks = inputs
    new_ref, low_ref, first_out, second_out, vec_out = outputs
    (store, left, right, first_in, second_in, g_out, g_in, t_out, t_in, e_out, e_in, w_out, w_in, vec_source,
     load_sem, g_sem, t_sem, e_sem, w_sem, left_sem, right_sem) = scratch
    slots, owners = g_in.shape[0], g_in.shape[1]
    z_count = t_in.shape[1]
    place = Place(z_count)
    dp, z = place.dp, place.z
    dps = [lax.rem(dp + d, owners) for d in range(owners)]
    count = blocks.shape[0]
    many = tail_hbm.shape[0]
    tail_times = [[many * stage + n for n in range(many)] for stage in range(4)]
    tail = BlockSum(place, [tail_hbm], sum_refs, tail_times)
    vec = BlockSum(place, [vec_source], vec_refs, [[many * stage + 1] for stage in range(4)])
    greet([(other, z) for other in dps[1:]] + place.z_partners())
    lines = line_gathers(place, plan.spans, lines_in, lines_out, line_refs, z_count)
    for line in lines:
        line.advance(1)
    every = list(bases) + list(lines_out)
    tail.tick(0)
    rows = plan.vector_rows
    stacked = jnp.concatenate(
        [dvecs[0][0:2, :], dvecs[1][2:rows, :], dvecs[2][0:2, :], dvecs[3][2:rows, :],
         jnp.zeros((vec_source.shape[-1] - 2 * rows, blocks.shape[2]), full)], axis=0
    )
    vec_source[0] = stacked.T.reshape(vec_source.shape[1:])

    def load(refs_map, target, sem, s):
        n, at = refs_map[s]
        return pltpu.make_async_copy(every[n].at[:, at], target.at[:, s], sem.at[s])

    def load_first(s):
        return pltpu.make_async_copy(first_hbm.at[s], first_in.at[s], load_sem.at[0, s])

    def load_second(s):
        return pltpu.make_async_copy(second_hbm.at[s], second_in.at[s], load_sem.at[1, s])

    early = [s for s in range(slots) if plan.left_map[s][0] < len(bases)]
    for s in range(slots):
        load(plan.right_map, right, right_sem, s).start()
        load_first(s).start()
        load_second(s).start()
        if s in early:
            load(plan.left_map, left, left_sem, s).start()

    def sum_step(t, carry):
        tail.tick(t)
        vec.tick(t)
        return carry

    lax.fori_loop(1, 3 * many, sum_step, 0)
    for line in lines:
        line.advance(2)
    lax.fori_loop(3 * many, 4 * many, sum_step, 0)
    start = tail.count
    for part in ready:
        store[start : start + part.shape[0]] = part[...]
        start += part.shape[0]
    store[count] = jnp.zeros(store.shape[1:], low)
    for i in range(tail.count):
        store[i] = tail.finish(i).astype(low)

    def g_copy(s, d):
        other = dps[d]
        return remote(g_out.at[s, d], g_in.at[s, dp], g_sem.at[0, s, d], g_sem.at[1, s, owners - d], (other, z))

    def t_copy(s, d):
        other = place.zs[d]
        return remote(t_out.at[s, d], t_in.at[s, z], t_sem.at[0, s, d], t_sem.at[1, s, z_count - d], (dp, other))

    def e_copy(s, d):
        other = place.zs[d]
        return remote(e_out.at[s, d], e_in.at[s, z], e_sem.at[0, s, d], e_sem.at[1, s, z_count - d], (dp, other))

    def w_copy(s, d):
        other = dps[d]
        return remote(
            w_out.at[s, other], w_in.at[s * owners + dp], w_sem.at[0, s, d], w_sem.at[1, s, owners - d], (other, z)
        )

    def send_out(s):
        for d in range(1, owners):
            g_out[s, d] = store[index_ref[s * owners + dps[d]]]
            g_copy(s, d).start()
        g_in[s, dp] = store[index_ref[s * owners + dp]]

    def turn(s):
        for d in range(1, owners):
            g_copy(s, d).wait()
        if s + 2 < slots:
            send_out(s + 2)
        load(plan.right_map, right, right_sem, s).wait()
        grad = jnp.concatenate([unfold(g_in[s, c].astype(full)) for c in range(owners)], axis=0).astype(low)
        for d in range(1, z_count):
            t_out[s, d] = pack_lanes(dot_nt(right[place.zs[d], s], grad)).astype(low)
            t_copy(s, d).start()
        t_in[s, z] = pack_lanes(dot_nt(right[z, s], grad)).astype(low)

    def adapt(s):
        for d in range(1, z_count):
            t_copy(s, d).wait()
        load_first(s).wait()
        load_second(s).wait()
        load(plan.left_map, left, left_sem, s).wait()
        rotated = jnp.zeros(first_in.shape[1:], full)
        for f in range(z_count):
            rotated = rotated + dot_nn(unpack_lanes(t_in[s, f].astype(full)).astype(low), left[f, s])
        first_new, second_new, direction = moments(rotated, first_in[s], second_in[s])
        first_out[s] = first_new
        second_out[s] = second_new
        direction = direction.astype(low)
        for d in range(1, z_count):
            e_out[s, d] = pack_lanes(dot_nt(left[place.zs[d], s], direction)).astype(low)
            e_copy(s, d).start()
        e_in[s, z] = pack_lanes(dot_nt(left[z, s], direction)).astype(low)

    def step_back(s):
        for d in range(1, z_count):
            e_copy(s, d).wait()
        step = jnp.zeros((left.shape[2], left.shape[3]), full)
        for f in range(z_count):
            step = step + dot_nn(unpack_lanes(e_in[s, f].astype(full)).astype(low), right[f, s])
        share = step.shape[0] // owners
        for c in range(owners):
            w_out[s, c] = fold(step[c * share : (c + 1) * share]).astype(low)
        for d in range(1, owners):
            w_copy(s, d).start()
        w_in[s * owners + dp] = w_out[s, dp]

    send_out(0)
    send_out(1)
    for hop in range(3, z_count):
        for line in lines:
            line.advance(hop)
    for k in range(slots + 2):
        if k == 3:
            for line in lines:
                line.advance(z_count)
            for s in range(slots):
                if s not in early:
                    load(plan.left_map, left, left_sem, s).start()
        if k < slots:
            turn(k)
        if 0 <= k - 1 < slots:
            adapt(k - 1)
        if 0 <= k - 2 < slots:
            step_back(k - 2)

    vec_out[...] = vec.finish(0)
    for s in range(slots):
        for d in range(1, owners):
            w_copy(s, d).wait()

    def block_step(b, carry):
        step = unfold(w_in[place_ref[b]].astype(full))
        block = blocks[b]
        new = block - matrix_rate * (step + weight_decay * block)
        new_ref[b] = new
        low_ref[b] = new.astype(low)
        return carry

    lax.fori_loop(0, count, block_step, 0)


class OptimizerPlan:
    def __init__(self, ready, dvecs, bases, spans, left_map, right_map, vector_rows):
        self.ready, self.dvecs, self.bases, self.spans = ready, dvecs, bases, spans
        self.left_map, self.right_map, self.vector_rows = left_map, right_map, vector_rows


def optimizer(
    index, places, tail, ready, dvecs, vector_rows, bases, lines, left_map, right_map, first, second, blocks, z_count,
    identity,
):
    slots, columns, width = first.shape
    owners = index.shape[0] // slots
    count, rows = blocks.shape[0], blocks.shape[1]
    span = bases[0].shape[2]
    lanes = 128
    shape = jax.ShapeDtypeStruct
    piece = (2 * rows, width // 2)
    tile = (span // 2, 2 * columns)
    smem = pl.BlockSpec(memory_space=pltpu.SMEM)
    plan = OptimizerPlan(
        len(ready), len(dvecs), len(bases), [(first_slot, amount) for _, first_slot, amount in lines],
        left_map, right_map, vector_rows,
    )
    line_shapes = [shape((z_count, amount) + basis.shape[1:], low) for basis, _, amount in lines]
    return pl.pallas_call(
        functools.partial(optimizer_kernel, plan),
        out_shape=(
            shape(blocks.shape, full), shape(blocks.shape, low), shape(first.shape, full), shape(first.shape, full),
            shape((rows, lanes), full), *line_shapes,
        ),
        in_specs=[smem, smem, ANYWHERE, ANYWHERE, ANYWHERE, IN_VMEM]
        + [IN_VMEM] * (len(ready) + len(dvecs)) + [ANYWHERE] * (len(bases) + len(lines)),
        out_specs=(IN_VMEM,) * 5 + (ANYWHERE,) * len(lines),
        scratch_shapes=[
            pltpu.VMEM((count + 1,) + piece, low),
            pltpu.VMEM((z_count, slots, span, width), low),
            pltpu.VMEM((z_count, slots, columns, width), low),
            pltpu.VMEM((slots, columns, width), full),
            pltpu.VMEM((slots, columns, width), full),
            pltpu.VMEM((slots, owners) + piece, low),
            pltpu.VMEM((slots, owners) + piece, low),
            pltpu.VMEM((slots, z_count) + tile, low),
            pltpu.VMEM((slots, z_count) + tile, low),
            pltpu.VMEM((slots, z_count) + tile, low),
            pltpu.VMEM((slots, z_count) + tile, low),
            pltpu.VMEM((slots, owners) + piece, low),
            pltpu.VMEM((slots * owners,) + piece, low),
            pltpu.VMEM((1, owners // 2, 2, width // owners, lanes), full),
            pltpu.SemaphoreType.DMA((2, slots)),
            pltpu.SemaphoreType.DMA((2, slots, owners)),
            pltpu.SemaphoreType.DMA((2, slots, z_count)),
            pltpu.SemaphoreType.DMA((2, slots, z_count)),
            pltpu.SemaphoreType.DMA((2, slots, owners)),
            pltpu.SemaphoreType.DMA((slots,)),
            pltpu.SemaphoreType.DMA((slots,)),
            *sum_scratch(tail.shape[0], tail.shape[3], width, z_count),
            *sum_scratch(1, width // owners, lanes, z_count, full),
            *line_scratch(len(lines), z_count),
        ],
        compiler_params=pltpu.CompilerParams(
            vmem_limit_bytes=60 * MIB, collective_id=identity, has_side_effects=True
        ),
        cost_estimate=pl.CostEstimate(
            flops=8 * slots * span * width * width, bytes_accessed=40 * MIB, transcendentals=slots * width * columns
        ),
        name="optimizer",
    )(index, places, tail, first, second, blocks, *ready, *dvecs, *bases, *[basis for basis, _, _ in lines])


def slot_table(owner, slots, owner_rows):
    block_count = owner.shape[0]
    same_owner = owner[:, None] == owner[None, :]
    ordering = jnp.arange(block_count, dtype=jnp.int32)
    earlier = ordering[None, :] < ordering[:, None]
    ranking = jnp.sum(jnp.where(same_owner & earlier, 1, 0), axis=1).astype(jnp.int32)
    owner_match = owner[None, :] == jnp.arange(owner_rows, dtype=jnp.int32)[:, None]
    slot_match = ranking[None, :] == jnp.arange(slots, dtype=jnp.int32)[:, None]
    return jnp.where(slot_match[:, None, :] & owner_match[None, :, :], 1.0, 0.0).astype(full)


def scatter_sum(grads):
    blocks, width = grads.shape[0], grads.shape[2]
    cut = grads.reshape(blocks, lax.axis_size("dp"), -1, width).transpose(1, 0, 2, 3)
    outer = lax.psum_scatter(cut, "dp", scatter_dimension=0, tiled=False)
    blocks, rows, width = outer.shape
    count = lax.axis_size("fsdp")
    cut = outer.reshape(blocks, count, rows // count, width).transpose(1, 0, 2, 3)
    return lax.psum_scatter(cut, "fsdp", scatter_dimension=0, tiled=False)


def scatter_vectors(grads):
    rows, width = grads.shape
    count = lax.axis_size("dp") * lax.axis_size("fsdp")
    cut = grads.reshape(rows, count, width // count).transpose(1, 0, 2)
    return lax.psum_scatter(cut, ("dp", "fsdp"), scatter_dimension=0, tiled=False)


def gathering_program(
    tokens, segment, blocks, vectors, owner, left_basis, right_basis, rot_first, rot_second, cotangent, z_count
):
    layers, vector_rows = vectors.shape[:2]
    count, shard_rows, width = blocks.shape
    per_layer = count // layers
    inner = (per_layer - 4) // 2
    owners = lax.axis_size("dp")
    slots = rot_first.shape[0]
    part = width // owners
    lanes = 128
    seg_column, seg_row = segment[:, :, None], segment[:, None, :]

    order = [0, 1, 2, 3]
    for c in range(inner):
        order += [4 + c, 4 + inner + c]
    folded = blocks.astype(low).reshape(count, shard_rows, 2, width // 2).transpose(0, 2, 1, 3)
    folded = folded.reshape(count, 2 * shard_rows, width // 2)

    def pick(numbers):
        return jnp.stack([folded[j] for j in numbers])

    head = pick(order + [per_layer + j for j in order[:4]])
    rest = pick([per_layer + j for j in order[4:]])
    vec_shard = vectors.astype(low).astype(full).reshape(layers * vector_rows, shard_rows).T
    vec_shard = jnp.pad(vec_shard, ((0, 0), (0, lanes - layers * vector_rows)))[None]
    left_low = left_basis.reshape(slots, -1, width).astype(low)
    right_low = right_basis.transpose(0, 2, 1).astype(low)

    head_opens = [0, 1, 2, 5, 9] + [9 + PACE * n for n in range(1, head.shape[0] - 4)]
    plan = ForwardPlan(
        inner, 0, head, vec_shard, vector_rows, [(right_low, 0, 2)], lead=16, opens=head_opens, z_count=z_count
    )
    empty_vec = jnp.zeros((16, width), full)
    results = forward_layer(tokens, seg_column, seg_row, empty_vec, jnp.zeros((1, width, width), low), full, plan, 6)
    kept_a = results[:12]
    hidden, weights_a, vec_a, vec_b, right_01 = results[12:]
    weights_a = weights_a.reshape(-1, width, width)
    plan = ForwardPlan(inner, 4, rest, lines=[(right_low, 2, 1)], lead=0, opens=[PACE * n for n in range(rest.shape[0])], z_count=z_count)
    plan.order = [per_layer + j for j in range(4)]
    results = forward_layer(hidden, seg_column, seg_row, vec_b, weights_a, low, plan, 7)
    kept_b = results[:12]
    layer_out, weights_b, right_2 = results[12:]
    weights_b = weights_b.reshape(-1, width, width)

    def cut(grads):
        return grads.reshape(-1, owners // 2, 2, part, width)

    size = (part, width)
    own = 3
    skip = own % 2
    pending = 2 * inner - own

    plan = Plan(None, [(right_low, 3, 2)], z_count, own, size, wide_ready(own))
    dw_wide, dr1, da, dvec_wide_b, wide_sum_b, right_34 = wide_back(
        cotangent, kept_b[5:], vec_b, weights_b, (0, 1, 2), plan, 1
    )
    ready = list(range(pending + 1))
    plan = Plan(cut(dw_wide), [(left_low, 0, 1)], z_count, 1, size, ready, skip)
    dw_attend, upstream, dvec_attend_b, attend_sum_b, left_0 = attend_back(
        da, dr1, hidden, kept_b[:5], seg_column, seg_row, weights_a, per_layer, plan, 2
    )
    plan = Plan(cut(dw_attend), [(left_low, 1, 1)], z_count, own, size, [0, 1, 2] + wide_ready(own))
    dw_wide, dr1, da, dvec_wide_a, wide_sum_a, left_1 = wide_back(
        upstream, kept_a[5:], vec_a, weights_a, (4, 5, 2), plan, 3
    )
    plan = Plan(cut(dw_wide), [(left_low, 2, 1)], z_count, 1, size, ready, skip)
    dw_attend, upstream, dvec_attend_a, attend_sum_a, left_2 = attend_back(
        da, dr1, tokens, kept_a[:5], seg_column, seg_row, weights_a, 0, plan, 5
    )

    three = list(range(3))
    early = [4 + n // 2 + inner * (n % 2) for n in range(own)]
    late = [4 + c + inner * k for k in range(2) for c in range(inner) if 2 * c + k >= own] + [3]
    held_order = three + late + [per_layer + j for j in three] + early + [per_layer + j for j in late + early]
    rank = jnp.asarray([held_order.index(j) for j in range(count)], jnp.int32)
    table = slot_table(owner, slots, owners).reshape(slots * owners, count)
    held = jnp.sum(table, axis=1)
    index = jnp.where(held > 0, jnp.sum(table * rank, axis=1), count).astype(jnp.int32)
    places = jnp.sum(table * jnp.arange(slots * owners, dtype=jnp.int32)[:, None], axis=0).astype(jnp.int32)
    bases = (right_01, right_2, right_34, left_0, left_1, left_2)
    right_map = [(0, 0), (0, 1), (1, 0), (2, 0), (2, 1)]
    left_map = [(3, 0), (4, 0), (5, 0), (6, 0), (6, 1)]
    new_blocks, new_low, first_new, second_new, vec_sum, _ = optimizer(
        index, places, cut(dw_attend), (attend_sum_a, wide_sum_a, attend_sum_b, wide_sum_b),
        (dvec_attend_a, dvec_wide_a, dvec_attend_b, dvec_wide_b), vector_rows, bases, [(left_low, 3, 2)], left_map, right_map,
        rot_first.transpose(0, 2, 1), rot_second.transpose(0, 2, 1), blocks, z_count, 4,
    )
    first_new, second_new = first_new.transpose(0, 2, 1), second_new.transpose(0, 2, 1)
    vector_grad = vec_sum[:, : layers * vector_rows].T.reshape(layers, vector_rows, shard_rows)
    return layer_out, upstream, new_blocks, new_low, first_new, second_new, vector_grad


def plain_program(
    tokens, segment, blocks, vectors, owner, left_basis, right_basis, rot_first, rot_second, cotangent
):
    layers, vector_rows = vectors.shape[:2]
    per_layer = blocks.shape[0] // layers
    inner = (per_layer - 4) // 2
    width = blocks.shape[2]
    owner_rows = lax.axis_size("dp")
    slots = rot_first.shape[0]
    selector = slot_table(owner, slots, owner_rows)
    vector_parts = lax.all_gather(vectors.astype(low), ("dp", "fsdp"), axis=0, tiled=False)
    vector_full = vector_parts.transpose(1, 2, 0, 3).reshape(layers, vector_rows, width).astype(full)
    blocks_low, vector_full = lax.optimization_barrier((blocks.astype(low), vector_full))

    seg_column = segment[:, :, None]
    seg_row = segment[:, None, :]
    state = tokens
    kept = []
    for layer_index in range(layers):
        start = per_layer * layer_index
        weights = lax.all_gather(blocks_low[start : start + per_layer], ("dp", "fsdp"), axis=1, tiled=True)
        out_dtype = low if layer_index == layers - 1 else full
        results = forward_layer(
            state, seg_column, seg_row, vector_full[layer_index], weights, out_dtype, ForwardPlan(inner, per_layer)
        )
        kept.append((state, weights, results[:5], results[5:12]))
        state = results[12]
    layer_out = state
    upstream = cotangent
    right_low = lax.all_gather(right_basis.astype(low), "fsdp", axis=2, tiled=True)
    block_shards = [None] * layers
    vector_shards = [None] * layers
    for layer_index in reversed(range(layers)):
        hidden, weights, attend_kept, wide_kept = kept[layer_index]
        dw_wide, dr1, da, dvec_wide = wide_back(
            upstream, wide_kept, vector_full[layer_index], weights, (4, 4 + inner, 1), Plan()
        )
        wide_shard = scatter_sum(dw_wide.reshape(-1, width, width))
        dw_attend, upstream, dvec_attend = attend_back(
            da, dr1, hidden, attend_kept, seg_column, seg_row, weights, 0, Plan()
        )
        dvec = jnp.concatenate([dvec_attend[:2], dvec_wide[2:vector_rows]], axis=0)
        block_shards[layer_index] = jnp.concatenate([scatter_sum(dw_attend), wide_shard], axis=0)
        vector_shards[layer_index] = scatter_vectors(dvec)
    vector_grad = jnp.stack(vector_shards)
    block_grad = jnp.concatenate(block_shards, axis=0)
    outgoing = jnp.einsum("srk,kid->srid", selector.astype(low), block_grad, preferred_element_type=full)
    incoming = lax.all_to_all(outgoing.astype(low), "dp", split_axis=1, concat_axis=1, tiled=True)
    owned = incoming.reshape(slots, -1, width)
    turned = jnp.einsum("sik,skj->sij", owned, right_low, preferred_element_type=full).astype(low)
    left_rows = left_basis.reshape(slots, -1, width).astype(low)
    partial_sums = jnp.einsum("sra,srb->sab", left_rows, turned, preferred_element_type=full)
    rotated = lax.psum_scatter(
        partial_sums.astype(low), "fsdp", scatter_dimension=2, tiled=True
    ).astype(full)
    first_new, second_new, direction = moments(rotated, rot_first, rot_second)
    direction_full = lax.all_gather(direction.astype(low), "fsdp", axis=2, tiled=True)
    back_right = jnp.einsum("sab,scb->sac", direction_full, right_low, preferred_element_type=full)
    step_rows = jnp.einsum(
        "sia,sac->sic", left_rows, back_right.astype(low), preferred_element_type=full
    )
    returned = lax.all_to_all(
        step_rows.reshape(slots, owner_rows, -1, width).astype(low),
        "dp",
        split_axis=1,
        concat_axis=1,
        tiled=True,
    )
    step_shard = jnp.einsum("srk,srid->kid", selector.astype(low), returned, preferred_element_type=full)
    new_blocks = blocks - matrix_rate * (step_shard + weight_decay * blocks)
    return layer_out, upstream, new_blocks, new_blocks.astype(low), first_new, second_new, vector_grad


def shards(
    tokens,
    segment,
    blocks,
    vectors,
    owner,
    left_basis,
    right_basis,
    rot_first,
    rot_second,
    vec_first,
    vec_second,
    cotangent,
):
    operands = (
        tokens, segment, blocks, vectors, owner, left_basis, right_basis, rot_first, rot_second, cotangent
    )
    z_count = lax.axis_size("fsdp")
    if lax.axis_size("dp") == 8 and z_count == 4:
        results = gathering_program(*operands, z_count)
    else:
        results = plain_program(*operands)
    layer_out, upstream, new_blocks, new_low, first_new, second_new, vector_grad = results
    vector_first = beta_one * vec_first + (1.0 - beta_one) * vector_grad
    vector_second = beta_two * vec_second + (1.0 - beta_two) * vector_grad * vector_grad
    vector_step = (
        vector_first
        / (1.0 - beta_one**STEP)
        / (jnp.sqrt(vector_second / (1.0 - beta_two**STEP)) + adam_epsilon)
    )
    vector_new = vectors - vector_rate * (vector_step + weight_decay * vectors)
    return (
        layer_out,
        upstream,
        new_blocks,
        new_low,
        first_new,
        second_new,
        vector_first,
        vector_second,
        vector_new,
    )


def solution(mesh):
    return jax.shard_map(
        shards,
        mesh=mesh,
        in_specs=(
            P(("dp", "fsdp"), None),
            P(("dp", "fsdp"), None),
            P(None, ("dp", "fsdp"), None),
            P(None, None, ("dp", "fsdp")),
            P(),
            P("dp", None, "fsdp", None),
            P("dp", None, "fsdp"),
            P("dp", None, "fsdp"),
            P("dp", None, "fsdp"),
            P(None, None, ("dp", "fsdp")),
            P(None, None, ("dp", "fsdp")),
            P(("dp", "fsdp"), None),
        ),
        out_specs=(
            P(("dp", "fsdp"), None),
            P(("dp", "fsdp"), None),
            P(None, ("dp", "fsdp"), None),
            P(None, ("dp", "fsdp"), None),
            P("dp", None, "fsdp"),
            P("dp", None, "fsdp"),
            P(None, None, ("dp", "fsdp")),
            P(None, None, ("dp", "fsdp")),
            P(None, None, ("dp", "fsdp")),
        ),
        check_vma=False,
    )
```

```python
import functools

import jax
import jax.numpy as jnp
from jax import lax
from jax.experimental import pallas as pl
from jax.experimental.pallas import tpu as pltpu
from jax.sharding import PartitionSpec as P

H = 12
HD = 64
L = 512
STEP = 5
PAIR = 2 * HD
MIB = 1 << 20

beta_one = 0.5
beta_two = 0.5
adam_epsilon = 1e-08
norm_epsilon = 1e-06
matrix_rate = 0.03
vector_rate = 0.2
weight_decay = 0.01
masked_score = -1e30
low = jnp.bfloat16
full = jnp.float32


def dot_nn(a, b):
    return lax.dot_general(a, b, (((1,), (0,)), ((), ())), preferred_element_type=full)


def dot_nt(a, b):
    return lax.dot_general(a, b, (((1,), (1,)), ((), ())), preferred_element_type=full)


def dot_tn(a, b):
    return lax.dot_general(a, b, (((0,), (0,)), ((), ())), preferred_element_type=full)


def gelu_parts(z):
    size = jnp.abs(z) * 0.7071067811865476
    t = 1.0 / (1.0 + 0.3275911 * size)
    bell = jnp.exp(-0.5 * z * z)
    poly = ((((1.061405429 * t - 1.453152027) * t + 1.421413741) * t - 0.284496736) * t + 0.254829592) * t
    half_tail = 0.5 * poly * bell
    phi = jnp.where(z >= 0, 1.0 - half_tail, half_tail)
    return z * phi, phi + z * bell * 0.3989422804014327


def norm_parts(residual):
    average = jnp.mean(residual, axis=-1, keepdims=True)
    centered = residual - average
    inverse = lax.rsqrt(jnp.mean(centered * centered, axis=-1, keepdims=True) + norm_epsilon)
    return centered * inverse, inverse


def norm_back(upstream, unit, inverse, gain):
    scaled = upstream * gain
    return inverse * (
        scaled
        - jnp.mean(scaled, axis=-1, keepdims=True)
        - unit * jnp.mean(scaled * unit, axis=-1, keepdims=True)
    )


def column_sum(values):
    return jnp.sum(values, axis=0, keepdims=True)


def half_masks(dtype):
    lane = lax.broadcasted_iota(jnp.int32, (1, PAIR), 1)
    first = (lane < HD).astype(full)
    return first.astype(dtype), (1.0 - first).astype(dtype)


def segment_bias(seg_column, seg_row):
    return jnp.where(seg_column == seg_row, 0.0, masked_score)


class Place:
    def __init__(self, z_count):
        self.dp, self.z = lax.axis_index("dp"), lax.axis_index("fsdp")
        self.core, self.spot = lax.rem(self.dp, 2), lax.div(self.dp, 2)
        x_step = 1 - 2 * lax.rem(self.spot, 2)
        y_step = 2 - 4 * lax.div(self.spot, 2)
        self.spot_a = self.spot + (1 - self.core) * x_step + self.core * y_step
        self.spot_b = self.spot + self.core * x_step + (1 - self.core) * y_step
        self.spot_ab = self.spot + x_step + y_step
        self.sibling = (self.dp + 1 - 2 * self.core, self.z)
        self.near_a = (2 * self.spot_a + self.core, self.z)
        self.near_b = (2 * self.spot_b + self.core, self.z)
        self.z_count = z_count
        self.zs = [lax.rem(self.z + d, z_count) for d in range(z_count)]

    def chip_partners(self):
        return [self.sibling, self.near_a, self.near_b]

    def z_partners(self):
        return [(self.dp, other) for other in self.zs[1:]]


def greet(partners):
    barrier = pltpu.get_barrier_semaphore()
    for device in partners:
        pl.semaphore_signal(barrier, inc=1, device_id=device, device_id_type=pl.DeviceIdType.MESH)
    pl.semaphore_wait(barrier, len(partners))


def remote(source, target, send, receive, device):
    return pltpu.make_async_remote_copy(
        src_ref=source,
        dst_ref=target,
        send_sem=send,
        recv_sem=receive,
        device_id=device,
        device_id_type=pl.DeviceIdType.MESH,
    )


def fold(piece):
    half = piece.shape[1] // 2
    return jnp.concatenate([piece[:, :half], piece[:, half:]], axis=0)


def unfold(piece):
    rows = piece.shape[0] // 2
    return jnp.concatenate([piece[:rows], piece[rows:]], axis=1)


def looked_up(ticks, t):
    now = functools.reduce(jnp.logical_or, [t == tick for tick in ticks])
    which = sum(n * (t == tick).astype(jnp.int32) for n, tick in enumerate(ticks))
    return now, which


def run_due(stages, t):
    for ticks, stage in stages:
        if isinstance(t, int):
            if t in ticks:
                stage(ticks.index(t))
            continue
        now, block = looked_up(ticks, t)

        @pl.when(now)
        def _():
            stage(block)


PACE = 3


def sum_times(ready, pace=PACE, core=1, second=4, third=2):
    opens, cores = [], []
    for tick in ready:
        opens.append(max(tick, opens[-1] + 1) if opens else tick)
        cores.append(max(opens[-1] + core, cores[-1] + pace) if cores else opens[-1] + core)
    seconds = [tick + second for tick in cores]
    return opens, cores, seconds, [tick + third for tick in seconds]


FIRST, SECOND, CLOSE = 3, 7, 9


class Openings:
    def __init__(self, count, head=(0,)):
        self.count, self.head = count, list(head)[:count]

    def tick(self, i):
        return self.head[i] if i < len(self.head) else self.head[-1] + 2 * (i - len(self.head) + 1)

    def close(self, i):
        return self.tick(i) + CLOSE

    def at(self, t):
        now, block = looked_up(self.head, t)
        beyond = t - self.head[-1]
        other = len(self.head) - 1 + lax.div(beyond, 2)
        later = (beyond > 0) & (lax.rem(beyond, 2) == 0) & (other < self.count)
        return now | later, jnp.where(beyond > 0, other, block)


def sum_scratch(count, part, width, z_count, kind=low):
    piece = (2 * part // z_count, width // 2) if kind == low else (part // z_count, width)
    return [
        pltpu.VMEM((count, 4, part, width), kind),
        pltpu.VMEM((count, 4, part, width), kind),
        pltpu.VMEM((count, 2, part, width), kind),
        pltpu.VMEM((count, part, width), kind),
        pltpu.VMEM((count, z_count) + piece, kind),
        pltpu.VMEM((count, z_count) + piece, kind),
        pltpu.SemaphoreType.DMA((count,)),
        pltpu.SemaphoreType.DMA((count, 2)),
        pltpu.SemaphoreType.DMA((count, 2, 2)),
        pltpu.SemaphoreType.DMA((count, 2)),
        pltpu.SemaphoreType.DMA((count, 2, z_count)),
    ]


SUM_REFS = 11


class BlockSum:
    def __init__(self, place, sources, refs, times):
        self.place, self.sources, self.times = place, sources, times
        (self.own, self.c, self.b, self.a, self.zs, self.zr,
         self.own_sem, self.c_sem, self.b_sem, self.a_sem, self.z_sem) = refs
        self.count = self.c.shape[0]
        self.kind = self.c.dtype
        self.z_count = self.zs.shape[1]

    def load(self, i, block):
        return pltpu.make_async_copy(block.at[:, self.place.core], self.own.at[i], self.own_sem.at[i])

    def core_copy(self, i, block):
        return remote(
            block.at[:, 1 - self.place.core], self.c.at[i], self.c_sem.at[i, 0], self.c_sem.at[i, 1], self.place.sibling
        )

    def second_copy(self, i, k):
        chunk = self.place.spot_b if k == 0 else self.place.spot_ab
        return remote(
            self.c.at[i, chunk], self.b.at[i, k], self.b_sem.at[i, 0, k], self.b_sem.at[i, 1, k], self.place.near_b
        )

    def third_copy(self, i):
        return remote(
            self.c.at[i, self.place.spot_a], self.a.at[i], self.a_sem.at[i, 0], self.a_sem.at[i, 1], self.place.near_a
        )

    def z_copy(self, i, d):
        other = self.place.zs[d]
        return remote(
            self.zs.at[i, other], self.zr.at[i, self.place.z], self.z_sem.at[i, 0, d],
            self.z_sem.at[i, 1, self.z_count - d], (self.place.dp, other),
        )

    def open(self, i):
        first = 0
        for source in self.sources:
            count = source.shape[0]

            @pl.when((i >= first) & (i < first + count))
            def _():
                block = source.at[jnp.clip(i - first, 0, count - 1)]
                self.core_copy(i, block).start()
                self.load(i, block).start()

            first += count

    def after_core(self, i):
        block = self.sources[0].at[0]
        self.core_copy(i, block).wait()
        self.load(i, block).wait()
        for k in range(4):
            self.c[i, k] = (self.c[i, k].astype(full) + self.own[i, k].astype(full)).astype(self.kind)
        self.second_copy(i, 0).start()
        self.second_copy(i, 1).start()

    def after_second(self, i):
        other, spot = self.place.spot_a, self.place.spot
        self.second_copy(i, 1).wait()
        self.c[i, other] = (self.c[i, other].astype(full) + self.b[i, 1].astype(full)).astype(self.kind)
        self.third_copy(i).start()
        self.second_copy(i, 0).wait()
        self.c[i, spot] = (self.c[i, spot].astype(full) + self.b[i, 0].astype(full)).astype(self.kind)

    def after_third(self, i):
        self.third_copy(i).wait()
        total = self.c[i, self.place.spot].astype(full) + self.a[i].astype(full)
        rows = total.shape[0] // self.z_count
        for k in range(self.z_count):
            piece = total[k * rows : (k + 1) * rows]
            self.zs[i, k] = fold(piece).astype(low) if self.kind == low else piece
        for d in range(1, self.z_count):
            self.z_copy(i, d).start()

    def finish(self, i):
        for d in range(1, self.z_count):
            self.z_copy(i, d).wait()
        total = self.zs[i, self.place.z].astype(full)
        for d in range(1, self.z_count):
            total = total + self.zr[i, self.place.zs[d]].astype(full)
        return total

    def tick(self, t):
        stages = (self.after_third, self.after_second, self.after_core, self.open)
        run_due(list(zip(self.times[::-1], stages)), t)

    @property
    def last(self):
        return self.times[3][-1]


class LineGather:
    def __init__(self, place, source, target, first, local_sem, sem, z_count):
        self.place = place
        self.source = source.at[pl.ds(first, target.shape[1])]
        self.target, self.local_sem, self.sem, self.z_count = target, local_sem, sem, z_count

    def hop_copy(self, hop, way):
        dp, z = self.place.dp, self.place.z
        if way == 0:
            piece, other, coming = z - hop + 1, z + 1, z - hop
            sends = (piece >= 0) & (other < self.z_count)
            receives = coming >= 0
        else:
            piece, other, coming = z + hop - 1, z - 1, z + hop
            sends = (piece < self.z_count) & (other >= 0)
            receives = coming < self.z_count
        piece = jnp.clip(piece, 0, self.z_count - 1)
        other = jnp.clip(other, 0, self.z_count - 1)
        source = self.source if hop == 1 else self.target.at[piece]
        copy = remote(source, self.target.at[piece], self.sem.at[way, 0, hop - 1], self.sem.at[way, 1, hop - 1], (dp, other))
        return copy, sends, receives

    def local(self):
        return pltpu.make_async_copy(self.source, self.target.at[self.place.z], self.local_sem)

    def start(self, hop):
        if hop == 1:
            self.local().start()
        for way in range(2):
            copy, sends, _ = self.hop_copy(hop, way)

            @pl.when(sends)
            def _():
                copy.start()

    def wait(self, hop):
        if hop == 1:
            self.local().wait()
        for way in range(2):
            copy, sends, receives = self.hop_copy(hop, way)

            @pl.when(sends)
            def _():
                copy.wait_send()

            @pl.when(receives)
            def _():
                copy.wait_recv()

    def advance(self, hop):
        if hop > 1:
            self.wait(hop - 1)
        if hop < self.z_count:
            self.start(hop)


def gather_scratch(count, rows, width, z_count, kind=low):
    piece = (2 * rows // z_count, width // 2) if kind == low else (rows // z_count, width)
    return [
        pltpu.VMEM((count, z_count) + piece, kind),
        pltpu.SemaphoreType.DMA((count, 2, z_count)),
        pltpu.SemaphoreType.DMA((count, 2)),
        pltpu.SemaphoreType.DMA((count, 2, 2)),
        pltpu.SemaphoreType.DMA((count, 2)),
    ]


GATHER_REFS = 5


class BlockGather:
    def __init__(self, place, source, whole, base, refs, openings):
        self.openings = openings
        self.place, self.source, self.whole, self.base = place, source, whole, base
        self.zr, self.z_sem, self.a_sem, self.b_sem, self.c_sem = refs
        self.count, self.z_count = self.zr.shape[0], self.zr.shape[1]

    def z_copy(self, i, d):
        place = self.place
        return remote(
            self.source.at[i], self.zr.at[i, place.z], self.z_sem.at[i, 0, d], self.z_sem.at[i, 1, self.z_count - d],
            (place.dp, place.zs[d]),
        )

    def chunk(self, i, spot):
        return self.whole.at[self.base + i, spot, self.place.core]

    def first_copy(self, i):
        chunk = self.chunk(i, self.place.spot)
        return remote(chunk, chunk, self.a_sem.at[i, 0], self.a_sem.at[i, 1], self.place.near_a)

    def second_copy(self, i, k):
        chunk = self.chunk(i, self.place.spot if k == 0 else self.place.spot_a)
        return remote(chunk, chunk, self.b_sem.at[i, 0, k], self.b_sem.at[i, 1, k], self.place.near_b)

    def core_copy(self, i):
        chunks = self.whole.at[self.base + i, :, self.place.core]
        return remote(chunks, chunks, self.c_sem.at[i, 0], self.c_sem.at[i, 1], self.place.sibling)

    AHEAD = 4

    def announce(self, i):
        for d in range(1, self.z_count):
            self.z_copy(i, d).start()
        self.zr[i, self.place.z] = self.source[i]

    def begin(self):
        for i in range(self.count):
            if self.openings.tick(i) < self.AHEAD:
                self.announce(i)

    def open(self, i):
        for d in range(1, self.z_count):
            self.z_copy(i, d).wait()
        pieces = [self.zr[i, k].astype(full) for k in range(self.z_count)]
        if self.zr.dtype == low:
            pieces = [unfold(piece) for piece in pieces]
        whole = jnp.concatenate(pieces, axis=0).astype(self.whole.dtype)
        self.whole[self.base + i, self.place.spot, self.place.core] = whole
        self.first_copy(i).start()
        self.second_copy(i, 0).start()

    def after_first(self, i):
        self.first_copy(i).wait()
        self.second_copy(i, 1).start()

    def after_second(self, i):
        self.second_copy(i, 0).wait()
        self.second_copy(i, 1).wait()
        self.core_copy(i).start()

    def close(self, i):
        self.core_copy(i).wait()

    def tick(self, t, done=None):
        def close(i):
            self.close(i)
            if done is not None:
                done(i)

        stages = ((SECOND, self.after_second), (FIRST, self.after_first), (0, self.open), (-self.AHEAD, self.announce))
        for late, stage in stages + ((CLOSE, close),):
            now, block = self.openings.at(jnp.asarray(t - late, jnp.int32))

            @pl.when(now)
            def _():
                stage(block)


def split_refs(refs, *counts):
    result, start = [], 0
    for count in counts:
        result.append(refs[start : start + count])
        start += count
    return result


class Side:
    def __init__(self, plan, sources, targets, sum_refs, line_refs, own=None):
        self.plan = plan
        sums = plan.sums
        blocks = [source.at[pl.ds(plan.skip, source.shape[0] - plan.skip)] for source in sources[:sums]]
        blocks += [own] if plan.own else []
        self.place = Place(plan.z_count) if plan.active else None
        self.sum = BlockSum(self.place, blocks, sum_refs, plan.times) if plan.total else None
        self.result = targets[0] if plan.total else None
        self.lines = line_gathers(self.place, plan.lines, sources[sums:], targets[bool(plan.total) :], line_refs, plan.z_count)

    def enter(self, now):
        if not self.plan.active:
            return

        @pl.when(now)
        def _():
            greet((self.place.chip_partners() if self.plan.total else []) + self.place.z_partners())
            for line in self.lines:
                line.advance(1)

    def tick(self, t):
        if self.plan.total:
            self.sum.tick(t)

    def leave(self, now, ticks):
        if not self.plan.active:
            return

        @pl.when(now)
        def _():
            if self.plan.total:
                if self.sum.last >= ticks:
                    lax.fori_loop(ticks, self.sum.last + 1, lambda t, carry: (self.tick(t), carry)[1], 0)
                for i in range(self.sum.count):
                    self.result[i] = self.sum.finish(i).astype(low)
            for line in self.lines:
                line.advance(self.plan.z_count)

    def advance(self, now, hop):
        if self.lines and hop < self.plan.z_count:
            @pl.when(now)
            def _():
                for line in self.lines:
                    line.advance(hop)


class Plan:
    def __init__(self, pending=None, lines=(), z_count=1, own=0, size=None, ready=(), skip=0):
        self.z_count = z_count
        self.sums = int(pending is not None)
        self.own, self.skip = own, skip
        self.total = own + (pending.shape[0] - skip if self.sums else 0)
        self.times = sum_times(ready) if self.total else None
        self.lines = [(first, count) for _, first, count in lines]
        self.active = bool(self.total or lines)
        self.arguments, self.results, self.result_specs, self.scratch = [], [], [], []
        if self.sums:
            self.arguments.append(pending)
        if self.total:
            part, width = size
            self.results.append(jax.ShapeDtypeStruct((self.total, 2 * part // z_count, width // 2), low))
            self.result_specs.append(
                pl.BlockSpec(self.results[0].shape, lambda i: (0, 0, 0), pipeline_mode=pl.Buffered(1))
            )
            self.scratch += sum_scratch(self.total, part, width, z_count)
        for basis, _, count in lines:
            self.arguments.append(basis)
            self.results.append(jax.ShapeDtypeStruct((z_count, count) + basis.shape[1:], low))
            self.result_specs.append(ANYWHERE)
        self.scratch += line_scratch(len(lines), z_count)
        self.argument_specs = [ANYWHERE] * len(self.arguments)

    def split(self, refs, inputs, outputs, scratch):
        count = len(self.lines)
        return split_refs(
            refs, inputs, self.sums + count, outputs, bool(self.total) + count, scratch,
            SUM_REFS * bool(self.total), 2 * bool(self.lines),
        )


def line_scratch(count, z_count):
    if not count:
        return []
    return [pltpu.SemaphoreType.DMA((count,)), pltpu.SemaphoreType.DMA((count, 2, 2, z_count - 1))]


def line_gathers(place, spans, sources, targets, refs, z_count):
    return [
        LineGather(place, source, target, first, refs[0].at[n], refs[1].at[n], z_count)
        for n, (source, target, (first, _)) in enumerate(zip(sources, targets, spans))
    ]


ANYWHERE = pl.BlockSpec(memory_space=pl.ANY)
IN_VMEM = pl.BlockSpec(memory_space=pltpu.VMEM)


def forward_kernel(plan, *refs):
    inputs, sources, outputs, targets, scratch, gather_refs, vec_refs, line_refs = plan.split(refs)
    x_ref, segc_ref, segr_ref, vec_ref, w_hbm = inputs
    (q_ref, k_ref, v_ref, ctxt_ref, lse_ref, x1_ref, inv1_ref, n1_ref, u_ref, gp_ref, x2_ref, inv2_ref,
     out_ref) = outputs
    w, bias, vt, n1_all, acc, w_sem = scratch
    s = pl.program_id(0)
    tokens, width = acc.shape
    rows_now = x_ref.shape[0]
    rows = tokens // rows_now
    inner = plan.inner
    local = plan.local
    gather = vec_gather = None
    place = Place(plan.z_count) if plan.gathered else None
    if plan.gathered:
        w_out, out_sem = targets[0], scratch_tail(plan, refs)
        gather = BlockGather(place, sources[0], w, local, gather_refs, plan.openings)
        if plan.vectors:
            vec_gather = BlockGather(place, sources[1], plan.vec_whole(refs), 0, vec_refs, Openings(1))
            vec_ref = targets[1]
    lines = line_gathers(place, plan.lines, sources[plan.line_at :], targets[plan.line_target_at :], line_refs, plan.z_count)

    def keep(i):
        return pltpu.make_async_copy(w.at[local + i], w_out.at[i], out_sem.at[i])

    def load(j):
        return pltpu.make_async_copy(w_hbm.at[plan.order[j]], w.at[j], w_sem.at[j])

    def matrix(j):
        return w[j].reshape(width, width)

    def arrive(j):
        if j < local:
            load(j).wait()

    def tick(t):
        if gather is not None:
            gather.tick(t, lambda i: keep(i).start())
            if vec_gather is not None:
                vec_gather.tick(t)

    pairs = width // PAIR
    row_ticks = pairs

    @pl.when(s == 0)
    def _():
        for j in range(local):
            load(j).start()
        if gather is not None:
            greet(place.chip_partners() + place.z_partners())
            if vec_gather is not None:
                vec_gather.begin()
            gather.begin()
            lax.fori_loop(0, plan.lead, lambda t, carry: (tick(t), carry)[1], 0)
            for line in lines:
                line.advance(1)
            if vec_gather is not None:
                turned = vec_gather.whole[0].reshape(width, vec_gather.whole.shape[-1]).T
                for layer in range(2):
                    count = plan.vector_rows
                    targets[1 + layer][0:count, :] = turned[layer * count : (layer + 1) * count, :]
        for j in range(min(local, 3)):
            arrive(j)

    @pl.when(s < rows)
    def _():
        xin = x_ref[...].astype(low)
        bias[...] = segment_bias(segc_ref[0], segr_ref[0])
        q_ref[...] = (dot_nn(xin, matrix(0)) + vec_ref[0:1, :]).astype(low)
        k_ref[...] = dot_nn(xin, matrix(1)).astype(low)
        value = dot_nn(xin, matrix(2)) + vec_ref[1:2, :]
        v_ref[...] = value.astype(low)
        vt[...] = value.T.astype(low)
        masks = half_masks(low)

        def pair_step(p, carry):
            lanes = pl.ds(pl.multiple_of(p * PAIR, PAIR), PAIR)
            q_pair = q_ref[:, lanes] * jnp.asarray(HD ** (-0.5), low)
            k_pair = k_ref[:, lanes]
            for h in range(2):
                scores = dot_nt(k_pair, q_pair * masks[h]) + bias[...]
                largest = jnp.max(scores, axis=0, keepdims=True)
                expanded = jnp.exp(scores - largest)
                total = column_sum(expanded)
                here = pl.ds(pl.multiple_of(p * PAIR + h * HD, HD), HD)
                context = dot_nn(vt[here, :], expanded.astype(low)) * (1.0 / total)
                ctxt_ref[here, :] = context.astype(low)
                lse_ref[0, pl.ds(2 * p + h, 1), :] = largest + jnp.log(total)
            tick(plan.lead + s * row_ticks + p)
            return carry

        lax.fori_loop(0, pairs, pair_step, 0)

        @pl.when(s == 0)
        def _():
            if local > 3:
                arrive(3)
            for line in lines:
                line.advance(2)

        context = ctxt_ref[...].astype(full).T.astype(low)
        attended = dot_nn(context, matrix(3)) + vec_ref[2:3, :]
        unit, inverse = norm_parts(x_ref[...].astype(full) + attended)
        x1_ref[...] = unit
        inv1_ref[...] = inverse
        normed = unit * vec_ref[3:4, :] + vec_ref[4:5, :]
        here = pl.ds(pl.multiple_of(s * rows_now, rows_now), rows_now)
        acc[here, :] = normed + vec_ref[5 + inner : 6 + inner, :]
        normed = normed.astype(low)
        n1_ref[...] = normed
        n1_all[here, :] = normed

    tile = tokens // 4
    starts, firsts = plan.step_ticks(rows * row_ticks)

    @pl.when(s >= rows)
    def _():
        c = s - rows

        @pl.when(c == 0)
        def _():
            for j in range(4, local):
                arrive(j)
            for line in lines:
                line.advance(3)

        start = sum(n * (c == k).astype(jnp.int32) for k, n in enumerate(starts))
        first = sum(n * (c == k).astype(jnp.int32) for k, n in enumerate(firsts))
        if gather is not None:
            lax.fori_loop(start, first, lambda t, carry: (tick(t), carry)[1], 0)

        def token_step(i, carry):
            for half in range(2):
                here = pl.ds(pl.multiple_of((2 * i + half) * tile, tile), tile)
                value, slope = gelu_parts(dot_nn(n1_all[here, :], matrix(4 + 2 * c)) + vec_ref[pl.ds(5 + c, 1), :])
                active = value.astype(low)
                u_ref[here, :] = active
                gp_ref[here, :] = slope.astype(low)
                acc[here, :] += dot_nn(active, matrix(5 + 2 * c))
            tick(first + i)
            return carry

        lax.fori_loop(0, 2, token_step, 0)

        @pl.when(c == inner - 1)
        def _():
            base = 5 + inner

            def last(i, carry):
                here = pl.ds(pl.multiple_of(i * tile, tile), tile)
                unit, inverse = norm_parts(acc[here, :])
                x2_ref[here, :] = unit
                inv2_ref[here, :] = inverse
                out_ref[here, :] = (
                    unit * vec_ref[base + 1 : base + 2, :] + vec_ref[base + 2 : base + 3, :]
                ).astype(out_ref.dtype)
                return carry

            lax.fori_loop(0, 4, last, 0)
            if gather is not None:
                last_tick = plan.openings.close(gather.count - 1)
                lax.fori_loop(firsts[-1] + 2, last_tick + 1, lambda t, carry: (tick(t), carry)[1], 0)
                for line in lines:
                    line.advance(plan.z_count)
                for i in range(gather.count):
                    keep(i).wait()


class ForwardPlan:
    def __init__(self, inner, local, shards=None, vec_shard=None, vector_rows=0, lines=(), lead=0, openings=None, z_count=1):
        self.inner, self.local, self.lead, self.z_count = inner, local, lead, z_count
        self.openings = openings
        self.vector_rows = vector_rows
        self.order = [0, 1, 2, 3]
        for c in range(inner):
            self.order += [4 + c, 4 + inner + c]
        self.gathered = 0 if shards is None else shards.shape[0]
        self.vectors = vec_shard is not None
        self.lines = [(first, count) for _, first, count in lines]
        self.line_at = int(self.gathered > 0) + int(self.vectors)
        self.line_target_at = int(self.gathered > 0) + 2 * int(self.vectors)
        self.arguments, self.argument_specs, self.results, self.result_specs, self.scratch = [], [], [], [], []
        shape = jax.ShapeDtypeStruct
        if self.gathered:
            width = 2 * shards.shape[2]
            self.arguments.append(shards)
            self.argument_specs.append(IN_VMEM)
            self.results.append(shape((self.gathered, 4, 2, width // 8, width), low))
            self.result_specs.append(ANYWHERE)
            self.scratch += gather_scratch(self.gathered, width // 8, width, z_count)
        if self.vectors:
            rows, lanes = vec_shard.shape[1:]
            self.arguments.append(vec_shard)
            self.argument_specs.append(IN_VMEM)
            for _ in range(2):
                self.results.append(shape((16, width), full))
                self.result_specs.append(pl.BlockSpec((16, width), lambda s: (0, 0)))
            self.scratch += gather_scratch(1, width // 8, lanes, z_count, full)
        for basis, _, count in lines:
            self.arguments.append(basis)
            self.argument_specs.append(ANYWHERE)
            self.results.append(shape((z_count, count) + basis.shape[1:], low))
            self.result_specs.append(ANYWHERE)
        self.scratch += line_scratch(len(lines), z_count)
        if self.gathered:
            self.scratch.append(pltpu.SemaphoreType.DMA((self.gathered,)))
        if self.vectors:
            self.scratch.append(pltpu.VMEM((1, 4, 2, width // 8, lanes), full))

    def step_ticks(self, row_ticks):
        starts, firsts = [], []
        now = self.lead + row_ticks
        for c in range(self.inner):
            starts.append(now)
            needed = 5 + 2 * c - self.local
            firsts.append(max(now, self.openings.close(needed) + 1) if self.openings else now)
            now = firsts[-1] + 2
        return starts, firsts

    def split(self, refs):
        return split_refs(
            refs, 5, len(self.arguments), 13, len(self.results), 6, GATHER_REFS * bool(self.gathered),
            GATHER_REFS * self.vectors, 2 * bool(self.lines),
        )

    def vec_whole(self, refs):
        return refs[-1]


def scratch_tail(plan, refs):
    return refs[-2] if plan.vectors else refs[-1]


def forward_layer(hidden, seg_column, seg_row, vectors, weights, out_dtype, plan, identity=None):
    tokens, width = hidden.shape
    inner = plan.inner
    wide = width * inner
    rows = tokens // L
    heads = width // HD
    shape = jax.ShapeDtypeStruct

    def here(s):
        return jnp.minimum(s, rows - 1)

    def column(s):
        return jnp.maximum(s - rows, 0)

    def row_block(columns):
        return pl.BlockSpec((L, columns), lambda s: (here(s), 0))

    def whole(columns):
        return pl.BlockSpec((tokens, columns), lambda s: (0, 0), pipeline_mode=pl.Buffered(1))

    wide_block = pl.BlockSpec((tokens, width), lambda s: (0, column(s)))
    out_shape = (
        shape((tokens, width), low), shape((tokens, width), low), shape((tokens, width), low),
        shape((width, tokens), low), shape((rows, heads, L), full),
        shape((tokens, width), full), shape((tokens, 1), full), shape((tokens, width), low),
        shape((tokens, wide), low), shape((tokens, wide), low),
        shape((tokens, width), full), shape((tokens, 1), full), shape((tokens, width), out_dtype),
        *plan.results,
    )
    out_specs = (
        row_block(width), row_block(width), row_block(width),
        pl.BlockSpec((width, L), lambda s: (0, here(s))), pl.BlockSpec((1, heads, L), lambda s: (here(s), 0, 0)),
        row_block(width), row_block(1), row_block(width),
        wide_block, wide_block,
        whole(width), whole(1), whole(width),
        *plan.result_specs,
    )
    total = 4 + 2 * inner
    held = max(total, plan.local + plan.gathered)
    return pl.pallas_call(
        functools.partial(forward_kernel, plan),
        grid=(rows + inner,),
        out_shape=out_shape,
        in_specs=[
            row_block(width),
            pl.BlockSpec((1, L, 1), lambda s: (here(s), 0, 0)),
            pl.BlockSpec((1, 1, L), lambda s: (here(s), 0, 0)),
            pl.BlockSpec(vectors.shape, lambda s: (0, 0)),
            ANYWHERE,
            *plan.argument_specs,
        ],
        out_specs=out_specs,
        scratch_shapes=[
            pltpu.VMEM((held, 4, 2, width // 8, width), low),
            pltpu.VMEM((L, L), full),
            pltpu.VMEM((width, L), low),
            pltpu.VMEM((tokens, width), low),
            pltpu.VMEM((tokens, width), full),
            pltpu.SemaphoreType.DMA((total,)),
            *plan.scratch,
        ],
        compiler_params=pltpu.CompilerParams(
            dimension_semantics=("arbitrary",), vmem_limit_bytes=62 * MIB,
            collective_id=identity, has_side_effects=identity is not None,
        ),
        cost_estimate=pl.CostEstimate(
            flops=2 * tokens * width * width * total + 4 * tokens * L * width,
            bytes_accessed=40 * MIB,
            transcendentals=tokens * (L * heads + wide),
        ),
        name="layer_forward",
    )(hidden, seg_column, seg_row, vectors, weights.reshape(-1, 4, 2, width // 8, width), *plan.arguments)


WIDE_HEAD_TICKS, WIDE_STEP_TICKS = 2, 4


def wide_ready(own):
    return [WIDE_HEAD_TICKS + WIDE_STEP_TICKS * (n // 2) + 2 + n % 2 for n in range(own)]


def wide_back_kernel(plan, inner, *refs):
    inputs, sources, outputs, targets, scratch, sum_refs, line_refs = plan.split(refs, 11, 4, 11)
    up_hbm, x2_hbm, inv2_hbm, x1_hbm, inv1_hbm, n1_hbm, vec_ref, wup_ref, wdown_ref, u_ref, gp_ref = inputs
    dw_ref, dr1_ref, da_ref, dvec_ref = outputs
    n1t, dz, kept_dw, up_ref, x2_ref, inv2_ref, x1_ref, inv1_ref, n1_ref, tile_sem, load_sem = scratch
    dy, dn1 = da_ref, dr1_ref
    c = pl.program_id(0)
    steps = pl.num_programs(0)
    tokens, width = dn1.shape
    tile = tokens // 4
    base = 5 + inner
    side = Side(plan, sources, targets, sum_refs, line_refs, kept_dw)

    def tile_copies(i):
        rows = pl.ds(pl.multiple_of(i * tile, tile), tile)
        return [
            pltpu.make_async_copy(source.at[rows], target.at[rows], tile_sem.at[n, i])
            for n, (source, target) in enumerate(((up_hbm, up_ref), (x2_hbm, x2_ref), (inv2_hbm, inv2_ref)))
        ]

    late_copies = [
        pltpu.make_async_copy(source, target, load_sem.at[n])
        for n, (source, target) in enumerate(((n1_hbm, n1_ref), (x1_hbm, x1_ref), (inv1_hbm, inv1_ref)))
    ]

    @pl.when(c == 0)
    def _():
        for i in range(4):
            for copy in tile_copies(i):
                copy.start()
        for copy in late_copies:
            copy.start()

    side.enter(c == 0)

    @pl.when(c == 0)
    def _():
        gain = vec_ref[base + 1 : base + 2, :]

        def body(i, carry):
            for copy in tile_copies(i):
                copy.wait()
            gain_sum, shift_sum, bias_sum = carry
            rows = pl.ds(pl.multiple_of(i * tile, tile), tile)
            upstream = up_ref[rows, :].astype(full)
            unit = x2_ref[rows, :]
            back = norm_back(upstream, unit, inv2_ref[rows, :], gain)
            dn1[rows, :] = back
            branch = back.astype(low)
            dy[rows, :] = branch
            @pl.when(lax.rem(i, 2) == 1)
            def _():
                side.tick(lax.div(i, 2))

            return (
                gain_sum + column_sum(upstream * unit),
                shift_sum + column_sum(upstream),
                bias_sum + column_sum(branch.astype(full)),
            )

        zero = jnp.zeros((1, width), full)
        gain_sum, shift_sum, bias_sum = lax.fori_loop(0, 4, body, (zero, zero, zero))
        dvec_ref[...] = jnp.zeros(dvec_ref.shape, full)
        dvec_ref[base : base + 1, :] = bias_sum
        dvec_ref[base + 1 : base + 2, :] = gain_sum
        dvec_ref[base + 2 : base + 3, :] = shift_sum
        late_copies[0].wait()
        n1t[...] = n1_ref[...].astype(full).T.astype(low)

    first_tick = WIDE_HEAD_TICKS + WIDE_STEP_TICKS * c

    def token_step(i, carry):
        for half in range(2):
            rows = pl.ds(pl.multiple_of((2 * i + half) * tile, tile), tile)
            slope = gp_ref[rows, :].astype(full)
            piece = (dot_nt(dy[rows, :], wdown_ref[0]) * slope).astype(low)
            dz[rows, :] = piece
            dn1[rows, :] += dot_nt(piece, wup_ref[0])
            carry = carry + column_sum(piece.astype(full))
        side.tick(first_tick + i)
        return carry

    bias_sum = lax.fori_loop(0, 2, token_step, jnp.zeros((1, width), full))
    side.advance(c == 1, 2)
    side.advance(c == 3, 3)
    for j in range(inner):
        @pl.when(c == j)
        def _():
            dvec_ref[5 + j : 6 + j, :] = bias_sum

    def store(k, grad):
        if plan.own:
            @pl.when(2 * c + k < plan.own)
            def _():
                kept_dw[2 * c + k] = grad.reshape(kept_dw.shape[1:])

            @pl.when(2 * c + k >= plan.own)
            def _():
                dw_ref[k, 0] = grad
        else:
            dw_ref[k, 0] = grad

    store(0, dot_nn(n1t[...], dz[...]).astype(low))
    side.tick(first_tick + 2)
    store(1, dot_tn(u_ref[...], dy[...]).astype(low))
    side.tick(first_tick + 3)
    final_tick = WIDE_HEAD_TICKS + WIDE_STEP_TICKS * inner

    @pl.when(c == steps - 1)
    def _():
        for copy in late_copies[1:]:
            copy.wait()
        gain = vec_ref[3:4, :]

        def body(i, carry):
            gain_sum, shift_sum, bias_sum = carry
            rows = pl.ds(pl.multiple_of(i * tile, tile), tile)
            upstream = dn1[rows, :]
            unit = x1_ref[rows, :]
            back = norm_back(upstream, unit, inv1_ref[rows, :], gain)
            dr1_ref[rows, :] = back
            branch = back.astype(low)
            da_ref[rows, :] = branch
            @pl.when(lax.rem(i, 2) == 1)
            def _():
                side.tick(final_tick + lax.div(i, 2))

            return (
                gain_sum + column_sum(upstream * unit),
                shift_sum + column_sum(upstream),
                bias_sum + column_sum(branch.astype(full)),
            )

        zero = jnp.zeros((1, width), full)
        gain_sum, shift_sum, bias_sum = lax.fori_loop(0, 4, body, (zero, zero, zero))
        dvec_ref[2:3, :] = bias_sum
        dvec_ref[3:4, :] = gain_sum
        dvec_ref[4:5, :] = shift_sum

    side.leave(c == steps - 1, final_tick + 2)


def wide_back(upstream, kept, vectors, weights, places, plan, identity=None):
    x1, inv1, n1, u, gp, x2, inv2 = kept
    tokens, width = x1.shape
    up_start, down_start, stride = places
    inner = u.shape[1] // width
    shape = jax.ShapeDtypeStruct

    return pl.pallas_call(
        functools.partial(wide_back_kernel, plan, inner),
        grid=(inner,),
        out_shape=(
            shape((2, inner - plan.own // 2, width, width), low),
            shape((tokens, width), full), shape((tokens, width), low), shape((16, width), full),
            *plan.results,
        ),
        in_specs=[
            *[ANYWHERE] * 6,
            pl.BlockSpec(vectors.shape, lambda c: (0, 0), pipeline_mode=pl.Buffered(1)),
            pl.BlockSpec((1, width, width), lambda c: (up_start + stride * c, 0, 0)),
            pl.BlockSpec((1, width, width), lambda c: (down_start + stride * c, 0, 0)),
            pl.BlockSpec((tokens, width), lambda c: (0, c)),
            pl.BlockSpec((tokens, width), lambda c: (0, c)),
            *plan.argument_specs,
        ],
        out_specs=(
            pl.BlockSpec((2, 1, width, width), lambda c: (0, jnp.maximum(c - plan.own // 2, 0), 0, 0)),
            pl.BlockSpec((tokens, width), lambda c: (0, 0), pipeline_mode=pl.Buffered(1)),
            pl.BlockSpec((tokens, width), lambda c: (0, 0), pipeline_mode=pl.Buffered(1)),
            pl.BlockSpec((16, width), lambda c: (0, 0)),
            *plan.result_specs,
        ),
        scratch_shapes=[
            pltpu.VMEM((width, tokens), low),
            pltpu.VMEM((tokens, width), low),
            pltpu.VMEM((plan.own, 4, 2, width // 8, width) if plan.own else (8, 128), low),
            pltpu.VMEM((tokens, width), upstream.dtype),
            pltpu.VMEM((tokens, width), full),
            pltpu.VMEM((tokens, 1), full),
            pltpu.VMEM((tokens, width), full),
            pltpu.VMEM((tokens, 1), full),
            pltpu.VMEM((tokens, width), low),
            pltpu.SemaphoreType.DMA((3, 4)),
            pltpu.SemaphoreType.DMA((3,)),
            *plan.scratch,
        ],
        compiler_params=pltpu.CompilerParams(
            dimension_semantics=("arbitrary",), vmem_limit_bytes=60 * MIB,
            collective_id=identity, has_side_effects=identity is not None,
        ),
        cost_estimate=pl.CostEstimate(
            flops=8 * tokens * width * width * inner, bytes_accessed=50 * MIB, transcendentals=0
        ),
        name="wide_backward",
    )(upstream, x2, inv2, x1, inv1, n1, vectors, weights, weights, u, gp, *plan.arguments)


def attend_back_kernel(plan, *refs):
    inputs, sources, outputs, targets, scratch, sum_refs, line_refs = plan.split(refs, 11, 3, 14)
    da_hbm, dr1_ref, x_ref, q_ref, k_ref, v_ref, ctxt_hbm, lse_ref, segc_ref, segr_ref, w_hbm = inputs
    dw_ref, dx_ref, dvec_ref = outputs
    bias, dctx, kt, delta, dqt, xt, dq_all, dk_all, dv_all, dwo, da_ref, ctxt_ref, w_ref, load_sem = scratch
    r = pl.program_id(0)
    loads = [
        pltpu.make_async_copy(w_hbm.at[plan.start + 3], w_ref.at[3], load_sem.at[0]),
        pltpu.make_async_copy(da_hbm, da_ref, load_sem.at[1]),
        pltpu.make_async_copy(ctxt_hbm, ctxt_ref, load_sem.at[2]),
        pltpu.make_async_copy(w_hbm.at[pl.ds(plan.start, 3)], w_ref.at[pl.ds(0, 3)], load_sem.at[3]),
    ]

    @pl.when(r == 0)
    def _():
        for copy in loads:
            copy.start()

    side = Side(plan, sources, targets, sum_refs, line_refs, dwo)
    side.enter(r == 0)
    tokens, width = dr1_ref.shape
    pairs = width // PAIR
    ticks = pairs + 4

    def tick(n):
        side.tick(r * ticks + n)

    tick(0)
    here = pl.ds(pl.multiple_of(r * tokens, tokens), tokens)

    @pl.when(r == 0)
    def _():
        for copy in loads[:3]:
            copy.wait()
        grad = dot_nn(ctxt_ref[...], da_ref[...]).astype(low)
        if plan.own:
            dwo[0] = grad.reshape(dwo.shape[1:])
        else:
            dw_ref[3] = grad

    xt[:, here] = x_ref[...].astype(low).astype(full).T.astype(low)
    bias[...] = segment_bias(segc_ref[0], segr_ref[0])
    context_grad = dot_nt(da_ref[here, :], w_ref[3]).astype(low)
    dctx[...] = context_grad
    kt[...] = k_ref[...].astype(full).T.astype(low)
    products = context_grad.astype(full) * ctxt_ref[:, here].astype(full).T
    feature = lax.broadcasted_iota(jnp.int32, (16, width), 1)
    head = lax.broadcasted_iota(jnp.int32, (16, width), 0)
    member = ((feature >= head * HD) & (feature < (head + 1) * HD)).astype(full).astype(low)
    high = products.astype(low)
    rest = (products - high.astype(full)).astype(low)
    delta[...] = dot_nt(member, high) + dot_nt(member, rest)
    tick(1)
    masks = half_masks(low)
    scale = HD ** (-0.5)

    def pair_step(p, carry):
        lanes = pl.ds(pl.multiple_of(p * PAIR, PAIR), PAIR)
        q_pair = q_ref[:, lanes] * jnp.asarray(scale, low)
        k_pair = k_ref[:, lanes]
        v_pair = v_ref[:, lanes]
        g_pair = dctx[:, lanes]
        key_grad = jnp.zeros((tokens, PAIR), full)
        value_grad = jnp.zeros((tokens, PAIR), full)
        for h in range(2):
            q_half = q_pair * masks[h]
            g_half = g_pair * masks[h]
            scores = dot_nt(k_pair, q_half) + bias[...]
            attention = jnp.exp(scores - lse_ref[0, pl.ds(2 * p + h, 1), :])
            value_grad = value_grad + dot_nn(attention.astype(low), g_half)
            attention_grad = dot_nt(v_pair, g_half)
            score_grad = (attention * (attention_grad - delta[pl.ds(2 * p + h, 1), :])).astype(low)
            key_grad = key_grad + dot_nn(score_grad, q_half)
            rows = pl.ds(pl.multiple_of(p * PAIR + h * HD, HD), HD)
            dqt[rows, :] = dot_nn(kt[rows, :], score_grad) * scale
        dk_all[here, lanes] = key_grad.astype(low)
        dv_all[here, lanes] = value_grad.astype(low)
        tick(2 + p)
        side.advance((r == 0) & (p == 4), 2)
        side.advance((r == 1) & (p == 3), 3)
        return carry

    lax.fori_loop(0, pairs, pair_step, 0)
    tick(2 + pairs)

    @pl.when(r == 0)
    def _():
        loads[3].wait()

    query_grad = dqt[...].T.astype(low)
    dq_all[here, :] = query_grad
    key_grad = dk_all[here, :]
    value_grad = dv_all[here, :]
    dx_ref[...] = (
        dr1_ref[...]
        + dot_nt(query_grad, w_ref[0])
        + dot_nt(key_grad, w_ref[1])
        + dot_nt(value_grad, w_ref[2])
    )
    tick(3 + pairs)

    @pl.when(r == 0)
    def _():
        dvec_ref[...] = jnp.zeros(dvec_ref.shape, full)

    dvec_ref[0:1, :] += column_sum(query_grad.astype(full))
    dvec_ref[1:2, :] += column_sum(value_grad.astype(full))

    @pl.when(r == pl.num_programs(0) - 1)
    def _():
        for j, grad in enumerate((dq_all, dk_all, dv_all)):
            dw_ref[j] = dot_nn(xt[...], grad[...]).astype(low)
            side.tick(plan.rows * ticks + j)

    side.leave(r == pl.num_programs(0) - 1, plan.rows * ticks + 3)


def attend_back(da, dr1, hidden, kept, seg_column, seg_row, weights, start, plan, identity=None):
    q, k, v, ctxt, lse = kept
    tokens, width = da.shape
    rows = tokens // L
    heads = width // HD
    shape = jax.ShapeDtypeStruct
    plan.start, plan.rows = start, rows

    def row_block():
        return pl.BlockSpec((L, width), lambda r: (r, 0))

    return pl.pallas_call(
        functools.partial(attend_back_kernel, plan),
        grid=(rows,),
        out_shape=(
            shape((4 - plan.own, width, width), low), shape((tokens, width), full), shape((8, width), full),
            *plan.results,
        ),
        in_specs=[
            ANYWHERE,
            row_block(), row_block(), row_block(), row_block(), row_block(),
            ANYWHERE,
            pl.BlockSpec((1, heads, L), lambda r: (r, 0, 0)),
            pl.BlockSpec((1, L, 1), lambda r: (r, 0, 0)),
            pl.BlockSpec((1, 1, L), lambda r: (r, 0, 0)),
            ANYWHERE,
            *plan.argument_specs,
        ],
        out_specs=(
            pl.BlockSpec((4 - plan.own, width, width), lambda r: (0, 0, 0), pipeline_mode=pl.Buffered(1)),
            row_block(),
            pl.BlockSpec((8, width), lambda r: (0, 0)),
            *plan.result_specs,
        ),
        scratch_shapes=[
            pltpu.VMEM((L, L), full),
            pltpu.VMEM((L, width), low),
            pltpu.VMEM((width, L), low),
            pltpu.VMEM((16, L), full),
            pltpu.VMEM((width, L), full),
            pltpu.VMEM((width, tokens), low),
            pltpu.VMEM((tokens, width), low),
            pltpu.VMEM((tokens, width), low),
            pltpu.VMEM((tokens, width), low),
            pltpu.VMEM((1, 4, 2, width // 8, width) if plan.own else (8, 128), low),
            pltpu.VMEM((tokens, width), low),
            pltpu.VMEM((width, tokens), low),
            pltpu.VMEM((4, width, width), low),
            pltpu.SemaphoreType.DMA((4,)),
            *plan.scratch,
        ],
        compiler_params=pltpu.CompilerParams(
            dimension_semantics=("arbitrary",), vmem_limit_bytes=60 * MIB,
            collective_id=identity, has_side_effects=identity is not None,
        ),
        cost_estimate=pl.CostEstimate(
            flops=16 * tokens * width * width + 10 * tokens * L * width,
            bytes_accessed=30 * MIB,
            transcendentals=tokens * L * heads,
        ),
        name="attend_backward",
    )(da, dr1, hidden, q, k, v, ctxt, lse, seg_column, seg_row, weights, *plan.arguments)


def moments(rotated, first, second):
    first_new = beta_one * first + (1.0 - beta_one) * rotated
    second_new = beta_two * second + (1.0 - beta_two) * rotated * rotated
    direction = (
        first_new
        / (1.0 - beta_one**STEP)
        / (jnp.sqrt(second_new / (1.0 - beta_two**STEP)) + adam_epsilon)
    )
    return first_new, second_new, direction


def pack_lanes(piece):
    rows = piece.shape[0] // 2
    return jnp.concatenate([piece[:rows], piece[rows:]], axis=1)


def unpack_lanes(piece):
    columns = piece.shape[1] // 2
    return jnp.concatenate([piece[:, :columns], piece[:, columns:]], axis=0)


def optimizer_kernel(plan, *refs):
    inputs, ready, dvecs, bases, outputs, scratch, sum_refs, vec_refs = split_refs(
        refs, 6, plan.ready, plan.dvecs, plan.bases, 5, 21, SUM_REFS, SUM_REFS
    )
    index_ref, place_ref, tail_hbm, first_hbm, second_hbm, blocks = inputs
    new_ref, low_ref, first_out, second_out, vec_out = outputs
    (store, left, right, first_in, second_in, g_out, g_in, t_out, t_in, e_out, e_in, w_out, w_in, vec_source,
     load_sem, g_sem, t_sem, e_sem, w_sem, left_sem, right_sem) = scratch
    slots, owners = g_in.shape[0], g_in.shape[1]
    z_count = t_in.shape[1]
    place = Place(z_count)
    dp, z = place.dp, place.z
    dps = [lax.rem(dp + d, owners) for d in range(owners)]
    count = blocks.shape[0]
    many = tail_hbm.shape[0]
    tail_times = [[many * stage + n for n in range(many)] for stage in range(4)]
    tail = BlockSum(place, [tail_hbm], sum_refs, tail_times)
    vec = BlockSum(place, [vec_source], vec_refs, [[many * stage + 1] for stage in range(4)])
    order = plan.free + [s for s in range(slots) if s not in plan.free]

    def load(refs_map, target, sem, s):
        n, at = refs_map[s]
        return pltpu.make_async_copy(bases[n].at[:, at], target.at[:, s], sem.at[s])

    def load_first(s):
        return pltpu.make_async_copy(first_hbm.at[s], first_in.at[s], load_sem.at[0, s])

    def load_second(s):
        return pltpu.make_async_copy(second_hbm.at[s], second_in.at[s], load_sem.at[1, s])

    for s in order:
        load(plan.right_map, right, right_sem, s).start()
        load(plan.left_map, left, left_sem, s).start()
        load_first(s).start()
        load_second(s).start()
    greet([(other, z) for other in dps[1:]] + place.z_partners())
    start = many
    for part in ready:
        store[start : start + part.shape[0]] = part[...]
        start += part.shape[0]
    store[0:many] = jnp.zeros((many,) + store.shape[1:], low)
    store[count] = jnp.zeros(store.shape[1:], low)
    rows = plan.vector_rows
    stacked = jnp.concatenate(
        [dvecs[0][0:2, :], dvecs[1][2:rows, :], dvecs[2][0:2, :], dvecs[3][2:rows, :],
         jnp.zeros((vec_source.shape[-1] - 2 * rows, blocks.shape[2]), full)], axis=0
    )
    vec_source[0] = stacked.T.reshape(vec_source.shape[1:])

    def g_copy(s, d):
        other = dps[d]
        return remote(g_out.at[s, d], g_in.at[s, dp], g_sem.at[0, s, d], g_sem.at[1, s, owners - d], (other, z))

    def t_copy(s, d):
        other = place.zs[d]
        return remote(t_out.at[s, d], t_in.at[s, z], t_sem.at[0, s, d], t_sem.at[1, s, z_count - d], (dp, other))

    def e_copy(s, d):
        other = place.zs[d]
        return remote(e_out.at[s, d], e_in.at[s, z], e_sem.at[0, s, d], e_sem.at[1, s, z_count - d], (dp, other))

    def w_copy(s, d):
        other = dps[d]
        return remote(
            w_out.at[s, other], w_in.at[s * owners + dp], w_sem.at[0, s, d], w_sem.at[1, s, owners - d], (other, z)
        )

    def send_out(s):
        for d in range(1, owners):
            g_out[s, d] = store[index_ref[s * owners + dps[d]]]
            g_copy(s, d).start()
        g_in[s, dp] = store[index_ref[s * owners + dp]]

    def turn(s):
        for d in range(1, owners):
            g_copy(s, d).wait()
        load(plan.right_map, right, right_sem, s).wait()
        grad = jnp.concatenate([unfold(g_in[s, c].astype(full)) for c in range(owners)], axis=0).astype(low)
        for d in range(1, z_count):
            t_out[s, d] = pack_lanes(dot_nt(right[place.zs[d], s], grad)).astype(low)
            t_copy(s, d).start()
        t_in[s, z] = pack_lanes(dot_nt(right[z, s], grad)).astype(low)

    def adapt(s):
        for d in range(1, z_count):
            t_copy(s, d).wait()
        load_first(s).wait()
        load_second(s).wait()
        load(plan.left_map, left, left_sem, s).wait()
        rotated = jnp.zeros(first_in.shape[1:], full)
        for f in range(z_count):
            rotated = rotated + dot_nn(unpack_lanes(t_in[s, f].astype(full)).astype(low), left[f, s])
        first_new, second_new, direction = moments(rotated, first_in[s], second_in[s])
        first_out[s] = first_new
        second_out[s] = second_new
        direction = direction.astype(low)
        for d in range(1, z_count):
            e_out[s, d] = pack_lanes(dot_nt(left[place.zs[d], s], direction)).astype(low)
            e_copy(s, d).start()
        e_in[s, z] = pack_lanes(dot_nt(left[z, s], direction)).astype(low)

    def step_back(s):
        for d in range(1, z_count):
            e_copy(s, d).wait()
        step = jnp.zeros((left.shape[2], left.shape[3]), full)
        for f in range(z_count):
            step = step + dot_nn(unpack_lanes(e_in[s, f].astype(full)).astype(low), right[f, s])
        share = step.shape[0] // owners
        for c in range(owners):
            w_out[s, c] = fold(step[c * share : (c + 1) * share]).astype(low)
        for d in range(1, owners):
            w_copy(s, d).start()
        w_in[s * owners + dp] = w_out[s, dp]

    def sums(stage):
        for t in range(many * stage, many * (stage + 1)):
            tail.tick(t)
            vec.tick(t)

    free = plan.free
    sums(0)
    for s in free:
        send_out(s)
    sums(1)
    for s in free:
        turn(s)
    sums(2)
    for s in free:
        adapt(s)
    sums(3)
    for i in range(many):
        store[i] = tail.finish(i).astype(low)
    rest = order[len(free) :]
    for s in rest[:2]:
        send_out(s)
    for s in free:
        step_back(s)
    for k in range(len(rest) + 2):
        if k < len(rest):
            turn(rest[k])
            if k + 2 < len(rest):
                send_out(rest[k + 2])
        if 0 <= k - 1 < len(rest):
            adapt(rest[k - 1])
        if 0 <= k - 2 < len(rest):
            step_back(rest[k - 2])

    vec_out[...] = vec.finish(0)
    for s in range(slots):
        for d in range(1, owners):
            w_copy(s, d).wait()

    def block_step(b, carry):
        step = unfold(w_in[place_ref[b]].astype(full))
        block = blocks[b]
        new = block - matrix_rate * (step + weight_decay * block)
        new_ref[b] = new
        low_ref[b] = new.astype(low)
        return carry

    lax.fori_loop(0, count, block_step, 0)


class OptimizerPlan:
    def __init__(self, ready, dvecs, bases, left_map, right_map, free, vector_rows):
        self.ready, self.dvecs, self.bases = ready, dvecs, bases
        self.left_map, self.right_map, self.free, self.vector_rows = left_map, right_map, free, vector_rows


def optimizer(
    index, places, tail, ready, dvecs, vector_rows, bases, left_map, right_map, free, first, second, blocks, z_count,
    identity,
):
    slots, columns, width = first.shape
    owners = index.shape[0] // slots
    count, rows = blocks.shape[0], blocks.shape[1]
    span = bases[0].shape[2]
    lanes = 128
    shape = jax.ShapeDtypeStruct
    piece = (2 * rows, width // 2)
    tile = (span // 2, 2 * columns)
    smem = pl.BlockSpec(memory_space=pltpu.SMEM)
    plan = OptimizerPlan(len(ready), len(dvecs), len(bases), left_map, right_map, free, vector_rows)
    return pl.pallas_call(
        functools.partial(optimizer_kernel, plan),
        out_shape=(
            shape(blocks.shape, full), shape(blocks.shape, low), shape(first.shape, full), shape(first.shape, full),
            shape((rows, lanes), full),
        ),
        in_specs=[smem, smem, ANYWHERE, ANYWHERE, ANYWHERE, IN_VMEM]
        + [IN_VMEM] * (len(ready) + len(dvecs)) + [ANYWHERE] * len(bases),
        out_specs=(IN_VMEM,) * 5,
        scratch_shapes=[
            pltpu.VMEM((count + 1,) + piece, low),
            pltpu.VMEM((z_count, slots, span, width), low),
            pltpu.VMEM((z_count, slots, columns, width), low),
            pltpu.VMEM((slots, columns, width), full),
            pltpu.VMEM((slots, columns, width), full),
            pltpu.VMEM((slots, owners) + piece, low),
            pltpu.VMEM((slots, owners) + piece, low),
            pltpu.VMEM((slots, z_count) + tile, low),
            pltpu.VMEM((slots, z_count) + tile, low),
            pltpu.VMEM((slots, z_count) + tile, low),
            pltpu.VMEM((slots, z_count) + tile, low),
            pltpu.VMEM((slots, owners) + piece, low),
            pltpu.VMEM((slots * owners,) + piece, low),
            pltpu.VMEM((1, owners // 2, 2, width // owners, lanes), full),
            pltpu.SemaphoreType.DMA((2, slots)),
            pltpu.SemaphoreType.DMA((2, slots, owners)),
            pltpu.SemaphoreType.DMA((2, slots, z_count)),
            pltpu.SemaphoreType.DMA((2, slots, z_count)),
            pltpu.SemaphoreType.DMA((2, slots, owners)),
            pltpu.SemaphoreType.DMA((slots,)),
            pltpu.SemaphoreType.DMA((slots,)),
            *sum_scratch(tail.shape[0], tail.shape[3], width, z_count),
            *sum_scratch(1, width // owners, lanes, z_count, full),
        ],
        compiler_params=pltpu.CompilerParams(
            vmem_limit_bytes=60 * MIB, collective_id=identity, has_side_effects=True
        ),
        cost_estimate=pl.CostEstimate(
            flops=8 * slots * span * width * width, bytes_accessed=40 * MIB, transcendentals=slots * width * columns
        ),
        name="optimizer",
    )(index, places, tail, first, second, blocks, *ready, *dvecs, *bases)


def slot_table(owner, slots, owner_rows):
    block_count = owner.shape[0]
    same_owner = owner[:, None] == owner[None, :]
    ordering = jnp.arange(block_count, dtype=jnp.int32)
    earlier = ordering[None, :] < ordering[:, None]
    ranking = jnp.sum(jnp.where(same_owner & earlier, 1, 0), axis=1).astype(jnp.int32)
    owner_match = owner[None, :] == jnp.arange(owner_rows, dtype=jnp.int32)[:, None]
    slot_match = ranking[None, :] == jnp.arange(slots, dtype=jnp.int32)[:, None]
    return jnp.where(slot_match[:, None, :] & owner_match[None, :, :], 1.0, 0.0).astype(full)


def scatter_sum(grads):
    blocks, width = grads.shape[0], grads.shape[2]
    cut = grads.reshape(blocks, lax.axis_size("dp"), -1, width).transpose(1, 0, 2, 3)
    outer = lax.psum_scatter(cut, "dp", scatter_dimension=0, tiled=False)
    blocks, rows, width = outer.shape
    count = lax.axis_size("fsdp")
    cut = outer.reshape(blocks, count, rows // count, width).transpose(1, 0, 2, 3)
    return lax.psum_scatter(cut, "fsdp", scatter_dimension=0, tiled=False)


def scatter_vectors(grads):
    rows, width = grads.shape
    count = lax.axis_size("dp") * lax.axis_size("fsdp")
    cut = grads.reshape(rows, count, width // count).transpose(1, 0, 2)
    return lax.psum_scatter(cut, ("dp", "fsdp"), scatter_dimension=0, tiled=False)


def gathering_program(
    tokens, segment, blocks, vectors, owner, left_basis, right_basis, rot_first, rot_second, cotangent, z_count
):
    layers, vector_rows = vectors.shape[:2]
    count, shard_rows, width = blocks.shape
    per_layer = count // layers
    inner = (per_layer - 4) // 2
    owners = lax.axis_size("dp")
    slots = rot_first.shape[0]
    part = width // owners
    lanes = 128
    seg_column, seg_row = segment[:, :, None], segment[:, None, :]

    order = [0, 1, 2, 3]
    for c in range(inner):
        order += [4 + c, 4 + inner + c]
    folded = blocks.astype(low).reshape(count, shard_rows, 2, width // 2).transpose(0, 2, 1, 3)
    folded = folded.reshape(count, 2 * shard_rows, width // 2)

    def pick(numbers):
        return jnp.stack([folded[j] for j in numbers])

    head = pick(order + [per_layer + j for j in order[:4]])
    rest = pick([per_layer + j for j in order[4:]])
    vec_shard = vectors.astype(low).astype(full).reshape(layers * vector_rows, shard_rows).T
    vec_shard = jnp.pad(vec_shard, ((0, 0), (0, lanes - layers * vector_rows)))[None]
    left_low = left_basis.reshape(slots, -1, width).astype(low)
    right_low = right_basis.transpose(0, 2, 1).astype(low)

    head_openings = Openings(head.shape[0], (0, 1, 2, 6, 9, 12))
    plan = ForwardPlan(
        inner, 0, head, vec_shard, vector_rows, [(right_low, 0, 2)], lead=12, openings=head_openings, z_count=z_count
    )
    empty_vec = jnp.zeros((16, width), full)
    results = forward_layer(tokens, seg_column, seg_row, empty_vec, jnp.zeros((1, width, width), low), full, plan, 6)
    kept_a = results[:12]
    hidden, weights_a, vec_a, vec_b, right_01 = results[12:]
    weights_a = weights_a.reshape(-1, width, width)
    plan = ForwardPlan(inner, 4, rest, lines=[(right_low, 2, 2)], lead=0, openings=Openings(rest.shape[0]), z_count=z_count)
    plan.order = [per_layer + j for j in range(4)]
    results = forward_layer(hidden, seg_column, seg_row, vec_b, weights_a, low, plan, 7)
    kept_b = results[:12]
    layer_out, weights_b, right_23 = results[12:]
    weights_b = weights_b.reshape(-1, width, width)

    def cut(grads):
        return grads.reshape(-1, owners // 2, 2, part, width)

    size = (part, width)
    own = 3
    skip = own % 2
    pending = 2 * inner - own

    plan = Plan(None, [(right_low, 4, 1), (left_low, 3, 1)], z_count, own, size, wide_ready(own))
    dw_wide, dr1, da, dvec_wide_b, wide_sum_b, right_4, left_3 = wide_back(
        cotangent, kept_b[5:], vec_b, weights_b, (0, 1, 2), plan, 1
    )
    ready = list(range(pending + 1))
    plan = Plan(cut(dw_wide), [(left_low, 4, 1)], z_count, 1, size, ready, skip)
    dw_attend, upstream, dvec_attend_b, attend_sum_b, left_4 = attend_back(
        da, dr1, hidden, kept_b[:5], seg_column, seg_row, weights_a, per_layer, plan, 2
    )
    plan = Plan(cut(dw_attend), [(left_low, 0, 1)], z_count, own, size, [0, 1, 2] + wide_ready(own))
    dw_wide, dr1, da, dvec_wide_a, wide_sum_a, left_0 = wide_back(
        upstream, kept_a[5:], vec_a, weights_a, (4, 5, 2), plan, 3
    )
    plan = Plan(cut(dw_wide), [(left_low, 1, 2)], z_count, 1, size, ready, skip)
    dw_attend, upstream, dvec_attend_a, attend_sum_a, left_12 = attend_back(
        da, dr1, tokens, kept_a[:5], seg_column, seg_row, weights_a, 0, plan, 5
    )

    three = list(range(3))
    early = [4 + n // 2 + inner * (n % 2) for n in range(own)]
    late = [4 + c + inner * k for k in range(2) for c in range(inner) if 2 * c + k >= own] + [3]
    held_order = three + late + [per_layer + j for j in three] + early + [per_layer + j for j in late + early]
    rank = jnp.asarray([held_order.index(j) for j in range(count)], jnp.int32)
    table = slot_table(owner, slots, owners).reshape(slots * owners, count)
    held = jnp.sum(table, axis=1)
    index = jnp.where(held > 0, jnp.sum(table * rank, axis=1), count).astype(jnp.int32)
    places = jnp.sum(table * jnp.arange(slots * owners, dtype=jnp.int32)[:, None], axis=0).astype(jnp.int32)
    bases = (right_01, right_23, right_4, left_0, left_12, left_3, left_4)
    right_map = [(0, 0), (0, 1), (1, 0), (1, 1), (2, 0)]
    left_map = [(3, 0), (4, 0), (4, 1), (5, 0), (6, 0)]
    free = list(range(3, slots))
    new_blocks, new_low, first_new, second_new, vec_sum = optimizer(
        index, places, cut(dw_attend), (attend_sum_a, wide_sum_a, attend_sum_b, wide_sum_b),
        (dvec_attend_a, dvec_wide_a, dvec_attend_b, dvec_wide_b), vector_rows, bases, left_map, right_map, free,
        rot_first.transpose(0, 2, 1), rot_second.transpose(0, 2, 1), blocks, z_count, 4,
    )
    first_new, second_new = first_new.transpose(0, 2, 1), second_new.transpose(0, 2, 1)
    vector_grad = vec_sum[:, : layers * vector_rows].T.reshape(layers, vector_rows, shard_rows)
    return layer_out, upstream, new_blocks, new_low, first_new, second_new, vector_grad


def plain_program(
    tokens, segment, blocks, vectors, owner, left_basis, right_basis, rot_first, rot_second, cotangent
):
    layers, vector_rows = vectors.shape[:2]
    per_layer = blocks.shape[0] // layers
    inner = (per_layer - 4) // 2
    width = blocks.shape[2]
    owner_rows = lax.axis_size("dp")
    slots = rot_first.shape[0]
    selector = slot_table(owner, slots, owner_rows)
    vector_parts = lax.all_gather(vectors.astype(low), ("dp", "fsdp"), axis=0, tiled=False)
    vector_full = vector_parts.transpose(1, 2, 0, 3).reshape(layers, vector_rows, width).astype(full)
    blocks_low, vector_full = lax.optimization_barrier((blocks.astype(low), vector_full))

    seg_column = segment[:, :, None]
    seg_row = segment[:, None, :]
    state = tokens
    kept = []
    for layer_index in range(layers):
        start = per_layer * layer_index
        weights = lax.all_gather(blocks_low[start : start + per_layer], ("dp", "fsdp"), axis=1, tiled=True)
        out_dtype = low if layer_index == layers - 1 else full
        results = forward_layer(
            state, seg_column, seg_row, vector_full[layer_index], weights, out_dtype, ForwardPlan(inner, per_layer)
        )
        kept.append((state, weights, results[:5], results[5:12]))
        state = results[12]
    layer_out = state
    upstream = cotangent
    right_low = lax.all_gather(right_basis.astype(low), "fsdp", axis=2, tiled=True)
    block_shards = [None] * layers
    vector_shards = [None] * layers
    for layer_index in reversed(range(layers)):
        hidden, weights, attend_kept, wide_kept = kept[layer_index]
        dw_wide, dr1, da, dvec_wide = wide_back(
            upstream, wide_kept, vector_full[layer_index], weights, (4, 4 + inner, 1), Plan()
        )
        wide_shard = scatter_sum(dw_wide.reshape(-1, width, width))
        dw_attend, upstream, dvec_attend = attend_back(
            da, dr1, hidden, attend_kept, seg_column, seg_row, weights, 0, Plan()
        )
        dvec = jnp.concatenate([dvec_attend[:2], dvec_wide[2:vector_rows]], axis=0)
        block_shards[layer_index] = jnp.concatenate([scatter_sum(dw_attend), wide_shard], axis=0)
        vector_shards[layer_index] = scatter_vectors(dvec)
    vector_grad = jnp.stack(vector_shards)
    block_grad = jnp.concatenate(block_shards, axis=0)
    outgoing = jnp.einsum("srk,kid->srid", selector.astype(low), block_grad, preferred_element_type=full)
    incoming = lax.all_to_all(outgoing.astype(low), "dp", split_axis=1, concat_axis=1, tiled=True)
    owned = incoming.reshape(slots, -1, width)
    turned = jnp.einsum("sik,skj->sij", owned, right_low, preferred_element_type=full).astype(low)
    left_rows = left_basis.reshape(slots, -1, width).astype(low)
    partial_sums = jnp.einsum("sra,srb->sab", left_rows, turned, preferred_element_type=full)
    rotated = lax.psum_scatter(
        partial_sums.astype(low), "fsdp", scatter_dimension=2, tiled=True
    ).astype(full)
    first_new, second_new, direction = moments(rotated, rot_first, rot_second)
    direction_full = lax.all_gather(direction.astype(low), "fsdp", axis=2, tiled=True)
    back_right = jnp.einsum("sab,scb->sac", direction_full, right_low, preferred_element_type=full)
    step_rows = jnp.einsum(
        "sia,sac->sic", left_rows, back_right.astype(low), preferred_element_type=full
    )
    returned = lax.all_to_all(
        step_rows.reshape(slots, owner_rows, -1, width).astype(low),
        "dp",
        split_axis=1,
        concat_axis=1,
        tiled=True,
    )
    step_shard = jnp.einsum("srk,srid->kid", selector.astype(low), returned, preferred_element_type=full)
    new_blocks = blocks - matrix_rate * (step_shard + weight_decay * blocks)
    return layer_out, upstream, new_blocks, new_blocks.astype(low), first_new, second_new, vector_grad


def shards(
    tokens,
    segment,
    blocks,
    vectors,
    owner,
    left_basis,
    right_basis,
    rot_first,
    rot_second,
    vec_first,
    vec_second,
    cotangent,
):
    operands = (
        tokens, segment, blocks, vectors, owner, left_basis, right_basis, rot_first, rot_second, cotangent
    )
    z_count = lax.axis_size("fsdp")
    if lax.axis_size("dp") == 8 and z_count == 4:
        results = gathering_program(*operands, z_count)
    else:
        results = plain_program(*operands)
    layer_out, upstream, new_blocks, new_low, first_new, second_new, vector_grad = results
    vector_first = beta_one * vec_first + (1.0 - beta_one) * vector_grad
    vector_second = beta_two * vec_second + (1.0 - beta_two) * vector_grad * vector_grad
    vector_step = (
        vector_first
        / (1.0 - beta_one**STEP)
        / (jnp.sqrt(vector_second / (1.0 - beta_two**STEP)) + adam_epsilon)
    )
    vector_new = vectors - vector_rate * (vector_step + weight_decay * vectors)
    return (
        layer_out,
        upstream,
        new_blocks,
        new_low,
        first_new,
        second_new,
        vector_first,
        vector_second,
        vector_new,
    )


def solution(mesh):
    return jax.shard_map(
        shards,
        mesh=mesh,
        in_specs=(
            P(("dp", "fsdp"), None),
            P(("dp", "fsdp"), None),
            P(None, ("dp", "fsdp"), None),
            P(None, None, ("dp", "fsdp")),
            P(),
            P("dp", None, "fsdp", None),
            P("dp", None, "fsdp"),
            P("dp", None, "fsdp"),
            P("dp", None, "fsdp"),
            P(None, None, ("dp", "fsdp")),
            P(None, None, ("dp", "fsdp")),
            P(("dp", "fsdp"), None),
        ),
        out_specs=(
            P(("dp", "fsdp"), None),
            P(("dp", "fsdp"), None),
            P(None, ("dp", "fsdp"), None),
            P(None, ("dp", "fsdp"), None),
            P("dp", None, "fsdp"),
            P("dp", None, "fsdp"),
            P(None, None, ("dp", "fsdp")),
            P(None, None, ("dp", "fsdp")),
            P(None, None, ("dp", "fsdp")),
        ),
        check_vma=False,
    )
```

```python
import functools

import jax
import jax.numpy as jnp
from jax import lax
from jax.experimental import pallas as pl
from jax.experimental.pallas import tpu as pltpu
from jax.sharding import PartitionSpec as P

H = 12
HD = 64
L = 512
STEP = 5
PAIR = 2 * HD
MIB = 1 << 20

beta_one = 0.5
beta_two = 0.5
adam_epsilon = 1e-08
norm_epsilon = 1e-06
matrix_rate = 0.03
vector_rate = 0.2
weight_decay = 0.01
masked_score = -1e30
low = jnp.bfloat16
full = jnp.float32


def dot_nn(a, b):
    return lax.dot_general(a, b, (((1,), (0,)), ((), ())), preferred_element_type=full)


def dot_nt(a, b):
    return lax.dot_general(a, b, (((1,), (1,)), ((), ())), preferred_element_type=full)


def dot_tn(a, b):
    return lax.dot_general(a, b, (((0,), (0,)), ((), ())), preferred_element_type=full)


def gelu_parts(z):
    size = jnp.abs(z) * 0.7071067811865476
    t = 1.0 / (1.0 + 0.3275911 * size)
    bell = jnp.exp(-0.5 * z * z)
    poly = ((((1.061405429 * t - 1.453152027) * t + 1.421413741) * t - 0.284496736) * t + 0.254829592) * t
    half_tail = 0.5 * poly * bell
    phi = jnp.where(z >= 0, 1.0 - half_tail, half_tail)
    return z * phi, phi + z * bell * 0.3989422804014327


def norm_parts(residual):
    average = jnp.mean(residual, axis=-1, keepdims=True)
    centered = residual - average
    inverse = lax.rsqrt(jnp.mean(centered * centered, axis=-1, keepdims=True) + norm_epsilon)
    return centered * inverse, inverse


def norm_back(upstream, unit, inverse, gain):
    scaled = upstream * gain
    return inverse * (
        scaled
        - jnp.mean(scaled, axis=-1, keepdims=True)
        - unit * jnp.mean(scaled * unit, axis=-1, keepdims=True)
    )


def column_sum(values):
    return jnp.sum(values, axis=0, keepdims=True)


def half_masks(dtype):
    lane = lax.broadcasted_iota(jnp.int32, (1, PAIR), 1)
    first = (lane < HD).astype(full)
    return first.astype(dtype), (1.0 - first).astype(dtype)


def segment_bias(seg_column, seg_row):
    return jnp.where(seg_column == seg_row, 0.0, masked_score)


class Place:
    def __init__(self, z_count):
        self.dp, self.z = lax.axis_index("dp"), lax.axis_index("fsdp")
        self.core, self.spot = lax.rem(self.dp, 2), lax.div(self.dp, 2)
        x_step = 1 - 2 * lax.rem(self.spot, 2)
        y_step = 2 - 4 * lax.div(self.spot, 2)
        self.spot_a = self.spot + (1 - self.core) * x_step + self.core * y_step
        self.spot_b = self.spot + self.core * x_step + (1 - self.core) * y_step
        self.spot_ab = self.spot + x_step + y_step
        self.sibling = (self.dp + 1 - 2 * self.core, self.z)
        self.near_a = (2 * self.spot_a + self.core, self.z)
        self.near_b = (2 * self.spot_b + self.core, self.z)
        self.z_count = z_count
        self.zs = [lax.rem(self.z + d, z_count) for d in range(z_count)]
        self.has_up, self.has_down = self.z < z_count - 1, self.z > 0
        self.middle = self.has_up & self.has_down
        self.across = lax.rem(self.z + 2, z_count)
        self.beside = jnp.where(self.z < 2, 1 - self.z, 5 - self.z)

    def line_sends(self, d):
        return {1: self.has_up, 2: self.z >= 0, 3: self.has_down}[d]

    def line_receives(self, d):
        return {1: self.has_down, 2: self.z >= 0, 3: self.has_up}[d]

    def chip_partners(self):
        return [self.sibling, self.near_a, self.near_b]

    def z_partners(self):
        return [(self.dp, other) for other in self.zs[1:]]


def greet(partners):
    barrier = pltpu.get_barrier_semaphore()
    for device in partners:
        pl.semaphore_signal(barrier, inc=1, device_id=device, device_id_type=pl.DeviceIdType.MESH)
    pl.semaphore_wait(barrier, len(partners))


def remote(source, target, send, receive, device):
    return pltpu.make_async_remote_copy(
        src_ref=source,
        dst_ref=target,
        send_sem=send,
        recv_sem=receive,
        device_id=device,
        device_id_type=pl.DeviceIdType.MESH,
    )


def fold(piece):
    half = piece.shape[1] // 2
    return jnp.concatenate([piece[:, :half], piece[:, half:]], axis=0)


def unfold(piece):
    rows = piece.shape[0] // 2
    return jnp.concatenate([piece[:rows], piece[rows:]], axis=1)


def looked_up(ticks, t):
    now = functools.reduce(jnp.logical_or, [t == tick for tick in ticks])
    which = sum(n * (t == tick).astype(jnp.int32) for n, tick in enumerate(ticks))
    return now, which


def run_due(stages, t):
    for ticks, stage in stages:
        if isinstance(t, int):
            if t in ticks:
                stage(ticks.index(t))
            continue
        now, block = looked_up(ticks, t)

        @pl.when(now)
        def _():
            stage(block)


def sum_times(ready):
    opens, cores, seconds = [], [], []
    for tick in ready:
        opens.append(max(tick, opens[-1] + 1) if opens else tick)
        cores.append(max(opens[-1] + 1, cores[-1] + 1) if cores else opens[-1] + 1)
        seconds.append(max(cores[-1] + 3, seconds[-1] + 3) if seconds else cores[-1] + 3)
    thirds = [tick + 2 for tick in seconds]
    return opens, cores, seconds, thirds, [tick + 2 for tick in thirds]


ANNOUNCE, FORWARD, FIRST, SECOND, CLOSE = -4, -2, 2, 4, 6


def sum_scratch(count, part, width, z_count, kind=low):
    piece = (2 * part // z_count, width // 2) if kind == low else (part // z_count, width)
    return [
        pltpu.VMEM((count, 4, part, width), kind),
        pltpu.VMEM((count, 4, part, width), kind),
        pltpu.VMEM((count, 2, part, width), kind),
        pltpu.VMEM((count, part, width), kind),
        pltpu.VMEM((count, z_count) + piece, kind),
        pltpu.VMEM((count, z_count) + piece, kind),
        pltpu.VMEM((count,) + piece, kind),
        pltpu.SemaphoreType.DMA((count,)),
        pltpu.SemaphoreType.DMA((count, 2)),
        pltpu.SemaphoreType.DMA((count, 2, 2)),
        pltpu.SemaphoreType.DMA((count, 2)),
        pltpu.SemaphoreType.DMA((count, 2, z_count)),
        pltpu.SemaphoreType.DMA((count, 2)),
    ]


SUM_REFS = 13


class BlockSum:
    def __init__(self, place, sources, refs, times):
        self.place, self.sources, self.times = place, sources, times
        (self.own, self.c, self.b, self.a, self.zs, self.zr, self.far,
         self.own_sem, self.c_sem, self.b_sem, self.a_sem, self.z_sem, self.far_sem) = refs
        self.count = self.c.shape[0]
        self.kind = self.c.dtype
        self.z_count = self.zs.shape[1]

    def load(self, i, block):
        return pltpu.make_async_copy(block.at[:, self.place.core], self.own.at[i], self.own_sem.at[i])

    def core_copy(self, i, block):
        return remote(
            block.at[:, 1 - self.place.core], self.c.at[i], self.c_sem.at[i, 0], self.c_sem.at[i, 1], self.place.sibling
        )

    def second_copy(self, i, k):
        chunk = self.place.spot_b if k == 0 else self.place.spot_ab
        return remote(
            self.c.at[i, chunk], self.b.at[i, k], self.b_sem.at[i, 0, k], self.b_sem.at[i, 1, k], self.place.near_b
        )

    def third_copy(self, i):
        return remote(
            self.c.at[i, self.place.spot_a], self.a.at[i], self.a_sem.at[i, 0], self.a_sem.at[i, 1], self.place.near_a
        )

    def z_copy(self, i, d):
        other = self.place.zs[d]
        return remote(
            self.zs.at[i, other], self.zr.at[i, self.place.z], self.z_sem.at[i, 0, d],
            self.z_sem.at[i, 1, self.z_count - d], (self.place.dp, other),
        )

    def open(self, i):
        first = 0
        for source in self.sources:
            count = source.shape[0]

            @pl.when((i >= first) & (i < first + count))
            def _():
                block = source.at[jnp.clip(i - first, 0, count - 1)]
                self.core_copy(i, block).start()
                self.load(i, block).start()

            first += count

    def after_core(self, i):
        block = self.sources[0].at[0]
        self.core_copy(i, block).wait()
        self.load(i, block).wait()
        for k in range(4):
            self.c[i, k] = (self.c[i, k].astype(full) + self.own[i, k].astype(full)).astype(self.kind)
        self.second_copy(i, 0).start()
        self.second_copy(i, 1).start()

    def after_second(self, i):
        other, spot = self.place.spot_a, self.place.spot
        self.second_copy(i, 1).wait()
        self.c[i, other] = (self.c[i, other].astype(full) + self.b[i, 1].astype(full)).astype(self.kind)
        self.third_copy(i).start()
        self.second_copy(i, 0).wait()
        self.c[i, spot] = (self.c[i, spot].astype(full) + self.b[i, 0].astype(full)).astype(self.kind)

    def after_third(self, i):
        self.third_copy(i).wait()
        total = self.c[i, self.place.spot].astype(full) + self.a[i].astype(full)
        rows = total.shape[0] // self.z_count
        for k in range(self.z_count):
            piece = total[k * rows : (k + 1) * rows]
            self.zs[i, k] = fold(piece).astype(low) if self.kind == low else piece
        place = self.place
        for d in (1, 3):
            @pl.when(place.line_sends(d))
            def _():
                self.z_copy(i, d).start()

        @pl.when(jnp.logical_not(place.middle))
        def _():
            self.z_copy(i, 2).start()
            self.far_copy(i).start()
            opposite = self.z_count - 1 - place.z
            self.zr[i, opposite] = jnp.zeros(self.zr.shape[2:], self.kind)

    def far_copy(self, i):
        place = self.place
        return remote(
            self.zs.at[i, self.z_count - 1 - place.z], self.far.at[i], self.far_sem.at[i, 0], self.far_sem.at[i, 1],
            (place.dp, place.beside),
        )

    def relay(self, i):
        @pl.when(self.place.middle)
        def _():
            self.far_copy(i).wait_recv()
            across = self.place.across
            self.zs[i, across] = (self.zs[i, across].astype(full) + self.far[i].astype(full)).astype(self.kind)
            self.z_copy(i, 2).start()

    def finish(self, i):
        for d in range(1, self.z_count):
            @pl.when(self.place.line_sends(d))
            def _():
                self.z_copy(i, d).wait_send()

            @pl.when(self.place.line_receives(d))
            def _():
                self.z_copy(i, d).wait_recv()

        @pl.when(jnp.logical_not(self.place.middle))
        def _():
            self.far_copy(i).wait_send()

        total = self.zs[i, self.place.z].astype(full)
        for d in range(1, self.z_count):
            total = total + self.zr[i, self.place.zs[d]].astype(full)
        return total

    def tick(self, t):
        stages = (self.relay, self.after_third, self.after_second, self.after_core, self.open)
        run_due(list(zip(self.times[::-1], stages)), t)

    @property
    def last(self):
        return self.times[4][-1]


class LineGather:
    def __init__(self, place, source, target, first, local_sem, sem, z_count):
        self.place = place
        self.source = source.at[pl.ds(first, target.shape[1])]
        self.target, self.local_sem, self.sem, self.z_count = target, local_sem, sem, z_count

    def hop_copy(self, hop, way):
        dp, z = self.place.dp, self.place.z
        if way == 0:
            piece, other, coming = z - hop + 1, z + 1, z - hop
            sends = (piece >= 0) & (other < self.z_count)
            receives = coming >= 0
        else:
            piece, other, coming = z + hop - 1, z - 1, z + hop
            sends = (piece < self.z_count) & (other >= 0)
            receives = coming < self.z_count
        piece = jnp.clip(piece, 0, self.z_count - 1)
        other = jnp.clip(other, 0, self.z_count - 1)
        source = self.source if hop == 1 else self.target.at[piece]
        copy = remote(source, self.target.at[piece], self.sem.at[way, 0, hop - 1], self.sem.at[way, 1, hop - 1], (dp, other))
        return copy, sends, receives

    def local(self):
        return pltpu.make_async_copy(self.source, self.target.at[self.place.z], self.local_sem)

    def start(self, hop):
        if hop == 1:
            self.local().start()
        for way in range(2):
            copy, sends, _ = self.hop_copy(hop, way)

            @pl.when(sends)
            def _():
                copy.start()

    def wait(self, hop):
        if hop == 1:
            self.local().wait()
        for way in range(2):
            copy, sends, receives = self.hop_copy(hop, way)

            @pl.when(sends)
            def _():
                copy.wait_send()

            @pl.when(receives)
            def _():
                copy.wait_recv()

    def advance(self, hop):
        if hop > 1:
            self.wait(hop - 1)
        if hop < self.z_count:
            self.start(hop)


def gather_scratch(count, rows, width, z_count, kind=low):
    piece = (2 * rows // z_count, width // 2) if kind == low else (rows // z_count, width)
    return [
        pltpu.VMEM((count, z_count) + piece, kind),
        pltpu.SemaphoreType.DMA((count, 2, z_count)),
        pltpu.SemaphoreType.DMA((count, 2)),
        pltpu.SemaphoreType.DMA((count, 2, 2)),
        pltpu.SemaphoreType.DMA((count, 2)),
        pltpu.SemaphoreType.DMA((count, 2)),
    ]


GATHER_REFS = 6


class BlockGather:
    def __init__(self, place, source, whole, base, refs):
        self.place, self.source, self.whole, self.base = place, source, whole, base
        self.zr, self.z_sem, self.a_sem, self.b_sem, self.c_sem, self.far_sem = refs
        self.count, self.z_count = self.zr.shape[0], self.zr.shape[1]

    def z_copy(self, i, d):
        place = self.place
        return remote(
            self.source.at[i], self.zr.at[i, place.z], self.z_sem.at[i, 0, d], self.z_sem.at[i, 1, self.z_count - d],
            (place.dp, place.zs[d]),
        )

    def chunk(self, i, spot):
        return self.whole.at[self.base + i, spot, self.place.core]

    def first_copy(self, i):
        chunk = self.chunk(i, self.place.spot)
        return remote(chunk, chunk, self.a_sem.at[i, 0], self.a_sem.at[i, 1], self.place.near_a)

    def second_copy(self, i, k):
        chunk = self.chunk(i, self.place.spot if k == 0 else self.place.spot_a)
        return remote(chunk, chunk, self.b_sem.at[i, 0, k], self.b_sem.at[i, 1, k], self.place.near_b)

    def core_copy(self, i):
        chunks = self.whole.at[self.base + i, :, self.place.core]
        return remote(chunks, chunks, self.c_sem.at[i, 0], self.c_sem.at[i, 1], self.place.sibling)

    def far_copy(self, i):
        place = self.place
        piece = self.zr.at[i, place.across]
        return remote(piece, piece, self.far_sem.at[i, 0], self.far_sem.at[i, 1], (place.dp, place.beside))

    def announce(self, i):
        for d in range(1, self.z_count):
            @pl.when(self.place.line_sends(d))
            def _():
                self.z_copy(i, d).start()

        self.zr[i, self.place.z] = self.source[i]

    def forward(self, i):
        @pl.when(self.place.middle)
        def _():
            self.z_copy(i, 2).wait_recv()
            self.far_copy(i).start()

    def begin(self):
        for i in range(min(-ANNOUNCE, self.count)):
            self.announce(i)

    def open(self, i):
        place = self.place
        for d in range(1, self.z_count):
            @pl.when(place.line_sends(d))
            def _():
                self.z_copy(i, d).wait_send()

        for d in (1, 3):
            @pl.when(place.line_receives(d))
            def _():
                self.z_copy(i, d).wait_recv()

        @pl.when(place.middle)
        def _():
            self.far_copy(i).wait_send()

        @pl.when(jnp.logical_not(place.middle))
        def _():
            self.z_copy(i, 2).wait_recv()
            self.far_copy(i).wait_recv()

        pieces = [self.zr[i, k].astype(full) for k in range(self.z_count)]
        if self.zr.dtype == low:
            pieces = [unfold(piece) for piece in pieces]
        whole = jnp.concatenate(pieces, axis=0).astype(self.whole.dtype)
        self.whole[self.base + i, self.place.spot, self.place.core] = whole
        self.first_copy(i).start()
        self.second_copy(i, 0).start()

    def after_first(self, i):
        self.first_copy(i).wait()
        self.second_copy(i, 1).start()

    def after_second(self, i):
        self.second_copy(i, 0).wait()
        self.second_copy(i, 1).wait()
        self.core_copy(i).start()

    def close(self, i):
        self.core_copy(i).wait()

    def tick(self, t, done=None):
        def close(i):
            self.close(i)
            if done is not None:
                done(i)

        @pl.when(t == 0)
        def _():
            for i in range(min(-FORWARD, self.count)):
                self.forward(i)

        stages = (
            (SECOND, self.after_second), (FIRST, self.after_first), (0, self.open), (FORWARD, self.forward),
            (ANNOUNCE, self.announce), (CLOSE, close),
        )
        for late, stage in stages:
            @pl.when((t >= max(late, 0)) & (t - late < self.count))
            def _():
                stage(t - late)


def split_refs(refs, *counts):
    result, start = [], 0
    for count in counts:
        result.append(refs[start : start + count])
        start += count
    return result


class Side:
    def __init__(self, plan, sources, targets, sum_refs, line_refs, own=None):
        self.plan = plan
        sums = plan.sums
        blocks = [source.at[pl.ds(plan.skip, source.shape[0] - plan.skip)] for source in sources[:sums]]
        blocks += [own] if plan.own else []
        self.place = Place(plan.z_count) if plan.active else None
        self.sum = BlockSum(self.place, blocks, sum_refs, plan.times) if plan.total else None
        self.result = targets[0] if plan.total else None
        self.lines = line_gathers(self.place, plan.lines, sources[sums:], targets[bool(plan.total) :], line_refs, plan.z_count)

    def enter(self, now):
        if not self.plan.active:
            return

        @pl.when(now)
        def _():
            greet((self.place.chip_partners() if self.plan.total else []) + self.place.z_partners())
            for line in self.lines:
                line.advance(1)

    def tick(self, t):
        if self.plan.total:
            self.sum.tick(t)

    def leave(self, now, ticks):
        if not self.plan.active:
            return

        @pl.when(now)
        def _():
            if self.plan.total:
                if self.sum.last >= ticks:
                    lax.fori_loop(ticks, self.sum.last + 1, lambda t, carry: (self.tick(t), carry)[1], 0)
                for i in range(self.sum.count):
                    self.result[i] = self.sum.finish(i).astype(low)
            for line in self.lines:
                line.advance(self.plan.z_count)

    def advance(self, now, hop):
        if self.lines and hop < self.plan.z_count:
            @pl.when(now)
            def _():
                for line in self.lines:
                    line.advance(hop)


class Plan:
    def __init__(self, pending=None, lines=(), z_count=1, own=0, size=None, ready=(), skip=0):
        self.z_count = z_count
        self.sums = int(pending is not None)
        self.own, self.skip = own, skip
        self.total = own + (pending.shape[0] - skip if self.sums else 0)
        self.times = sum_times(ready) if self.total else None
        self.lines = [(first, count) for _, first, count in lines]
        self.active = bool(self.total or lines)
        self.arguments, self.results, self.result_specs, self.scratch = [], [], [], []
        if self.sums:
            self.arguments.append(pending)
        if self.total:
            part, width = size
            self.results.append(jax.ShapeDtypeStruct((self.total, 2 * part // z_count, width // 2), low))
            self.result_specs.append(
                pl.BlockSpec(self.results[0].shape, lambda i: (0, 0, 0), pipeline_mode=pl.Buffered(1))
            )
            self.scratch += sum_scratch(self.total, part, width, z_count)
        for basis, _, count in lines:
            self.arguments.append(basis)
            self.results.append(jax.ShapeDtypeStruct((z_count, count) + basis.shape[1:], low))
            self.result_specs.append(ANYWHERE)
        self.scratch += line_scratch(len(lines), z_count)
        self.argument_specs = [ANYWHERE] * len(self.arguments)

    def split(self, refs, inputs, outputs, scratch):
        count = len(self.lines)
        return split_refs(
            refs, inputs, self.sums + count, outputs, bool(self.total) + count, scratch,
            SUM_REFS * bool(self.total), 2 * bool(self.lines),
        )


def line_scratch(count, z_count):
    if not count:
        return []
    return [pltpu.SemaphoreType.DMA((count,)), pltpu.SemaphoreType.DMA((count, 2, 2, z_count - 1))]


def line_gathers(place, spans, sources, targets, refs, z_count):
    return [
        LineGather(place, source, target, first, refs[0].at[n], refs[1].at[n], z_count)
        for n, (source, target, (first, _)) in enumerate(zip(sources, targets, spans))
    ]


ANYWHERE = pl.BlockSpec(memory_space=pl.ANY)
IN_VMEM = pl.BlockSpec(memory_space=pltpu.VMEM)


def forward_kernel(plan, *refs):
    inputs, sources, outputs, targets, scratch, gather_refs, vec_refs, line_refs = plan.split(refs)
    x_ref, segc_ref, segr_ref, vec_ref, w_hbm = inputs
    (q_ref, k_ref, v_ref, ctxt_ref, lse_ref, x1_ref, inv1_ref, n1_ref, u_ref, gp_ref, x2_ref, inv2_ref,
     out_ref) = outputs
    w, bias, vt, n1_all, acc, w_sem = scratch
    s = pl.program_id(0)
    tokens, width = acc.shape
    rows_now = x_ref.shape[0]
    rows = tokens // rows_now
    inner = plan.inner
    local = plan.local
    gather = vec_gather = None
    place = Place(plan.z_count) if plan.gathered else None
    if plan.gathered:
        w_out, out_sem = targets[0], scratch_tail(plan, refs)
        gather = BlockGather(place, sources[0], w, local, gather_refs)
        if plan.vectors:
            vec_gather = BlockGather(place, sources[1], plan.vec_whole(refs), 0, vec_refs)
            vec_ref = targets[1]
    lines = line_gathers(place, plan.lines, sources[plan.line_at :], targets[plan.line_target_at :], line_refs, plan.z_count)

    def keep(i):
        return pltpu.make_async_copy(w.at[local + i], w_out.at[i], out_sem.at[i])

    def load(j):
        return pltpu.make_async_copy(w_hbm.at[plan.order[j]], w.at[j], w_sem.at[j])

    def matrix(j):
        return w[j].reshape(width, width)

    def arrive(j):
        if j < local:
            load(j).wait()

    def tick(t):
        if gather is not None:
            gather.tick(t, lambda i: keep(i).start())
            if vec_gather is not None:
                vec_gather.tick(t)

    pairs = width // PAIR
    row_ticks = plan.row_ticks

    @pl.when(s == 0)
    def _():
        for j in range(local):
            load(j).start()
        if gather is not None:
            greet(place.chip_partners() + place.z_partners())
            if vec_gather is not None:
                vec_gather.begin()
            gather.begin()
            lax.fori_loop(0, plan.lead, lambda t, carry: (tick(t), carry)[1], 0)
            for line in lines:
                line.advance(1)
            if vec_gather is not None:
                turned = vec_gather.whole[0].reshape(width, vec_gather.whole.shape[-1]).T
                for layer in range(2):
                    count = plan.vector_rows
                    targets[1 + layer][0:count, :] = turned[layer * count : (layer + 1) * count, :]
        for j in range(min(local, 3)):
            arrive(j)

    @pl.when(s < rows)
    def _():
        xin = x_ref[...].astype(low)
        bias[...] = segment_bias(segc_ref[0], segr_ref[0])
        q_ref[...] = (dot_nn(xin, matrix(0)) + vec_ref[0:1, :]).astype(low)
        k_ref[...] = dot_nn(xin, matrix(1)).astype(low)
        value = dot_nn(xin, matrix(2)) + vec_ref[1:2, :]
        v_ref[...] = value.astype(low)
        vt[...] = value.T.astype(low)
        masks = half_masks(low)

        def pair_step(p, carry):
            lanes = pl.ds(pl.multiple_of(p * PAIR, PAIR), PAIR)
            q_pair = q_ref[:, lanes] * jnp.asarray(HD ** (-0.5), low)
            k_pair = k_ref[:, lanes]
            for h in range(2):
                scores = dot_nt(k_pair, q_pair * masks[h]) + bias[...]
                largest = jnp.max(scores, axis=0, keepdims=True)
                expanded = jnp.exp(scores - largest)
                total = column_sum(expanded)
                here = pl.ds(pl.multiple_of(p * PAIR + h * HD, HD), HD)
                context = dot_nn(vt[here, :], expanded.astype(low)) * (1.0 / total)
                ctxt_ref[here, :] = context.astype(low)
                lse_ref[0, pl.ds(2 * p + h, 1), :] = largest + jnp.log(total)
            if gather is not None:
                spots = [n for n in range(pairs) if (n + 1) * row_ticks // pairs > n * row_ticks // pairs]
                now, which = looked_up(spots, p)

                @pl.when(now)
                def _():
                    tick(plan.lead + s * row_ticks + which)
            return carry

        lax.fori_loop(0, pairs, pair_step, 0)

        @pl.when(s == 0)
        def _():
            if local > 3:
                arrive(3)
            for line in lines:
                line.advance(2)

        context = ctxt_ref[...].astype(full).T.astype(low)
        attended = dot_nn(context, matrix(3)) + vec_ref[2:3, :]
        unit, inverse = norm_parts(x_ref[...].astype(full) + attended)
        x1_ref[...] = unit
        inv1_ref[...] = inverse
        normed = unit * vec_ref[3:4, :] + vec_ref[4:5, :]
        here = pl.ds(pl.multiple_of(s * rows_now, rows_now), rows_now)
        acc[here, :] = normed + vec_ref[5 + inner : 6 + inner, :]
        normed = normed.astype(low)
        n1_ref[...] = normed
        n1_all[here, :] = normed

    tile = tokens // 4
    starts, firsts = plan.step_ticks(rows * row_ticks)

    @pl.when(s >= rows)
    def _():
        c = s - rows

        @pl.when(c == 0)
        def _():
            for j in range(4, local):
                arrive(j)
            for line in lines:
                line.advance(3)

        start = sum(n * (c == k).astype(jnp.int32) for k, n in enumerate(starts))
        first = sum(n * (c == k).astype(jnp.int32) for k, n in enumerate(firsts))
        if gather is not None:
            lax.fori_loop(start, first, lambda t, carry: (tick(t), carry)[1], 0)

        def token_step(i, carry):
            for half in range(2):
                here = pl.ds(pl.multiple_of((2 * i + half) * tile, tile), tile)
                value, slope = gelu_parts(dot_nn(n1_all[here, :], matrix(4 + 2 * c)) + vec_ref[pl.ds(5 + c, 1), :])
                active = value.astype(low)
                u_ref[here, :] = active
                gp_ref[here, :] = slope.astype(low)
                acc[here, :] += dot_nn(active, matrix(5 + 2 * c))
            tick(first + i)
            return carry

        lax.fori_loop(0, 2, token_step, 0)

        @pl.when(c == inner - 1)
        def _():
            base = 5 + inner

            def last(i, carry):
                here = pl.ds(pl.multiple_of(i * tile, tile), tile)
                unit, inverse = norm_parts(acc[here, :])
                x2_ref[here, :] = unit
                inv2_ref[here, :] = inverse
                out_ref[here, :] = (
                    unit * vec_ref[base + 1 : base + 2, :] + vec_ref[base + 2 : base + 3, :]
                ).astype(out_ref.dtype)
                return carry

            lax.fori_loop(0, 4, last, 0)
            if gather is not None:
                last_tick = gather.count - 1 + CLOSE
                lax.fori_loop(firsts[-1] + 2, last_tick + 1, lambda t, carry: (tick(t), carry)[1], 0)
                for line in lines:
                    line.advance(plan.z_count)
                for i in range(gather.count):
                    keep(i).wait()


class ForwardPlan:
    def __init__(self, inner, local, shards=None, vec_shard=None, vector_rows=0, lines=(), lead=0, row_ticks=0, z_count=1):
        self.inner, self.local, self.lead, self.row_ticks, self.z_count = inner, local, lead, row_ticks, z_count
        self.vector_rows = vector_rows
        self.order = [0, 1, 2, 3]
        for c in range(inner):
            self.order += [4 + c, 4 + inner + c]
        self.gathered = 0 if shards is None else shards.shape[0]
        self.vectors = vec_shard is not None
        self.lines = [(first, count) for _, first, count in lines]
        self.line_at = int(self.gathered > 0) + int(self.vectors)
        self.line_target_at = int(self.gathered > 0) + 2 * int(self.vectors)
        self.arguments, self.argument_specs, self.results, self.result_specs, self.scratch = [], [], [], [], []
        shape = jax.ShapeDtypeStruct
        if self.gathered:
            width = 2 * shards.shape[2]
            self.arguments.append(shards)
            self.argument_specs.append(IN_VMEM)
            self.results.append(shape((self.gathered, 4, 2, width // 8, width), low))
            self.result_specs.append(ANYWHERE)
            self.scratch += gather_scratch(self.gathered, width // 8, width, z_count)
        if self.vectors:
            rows, lanes = vec_shard.shape[1:]
            self.arguments.append(vec_shard)
            self.argument_specs.append(IN_VMEM)
            for _ in range(2):
                self.results.append(shape((16, width), full))
                self.result_specs.append(pl.BlockSpec((16, width), lambda s: (0, 0)))
            self.scratch += gather_scratch(1, width // 8, lanes, z_count, full)
        for basis, _, count in lines:
            self.arguments.append(basis)
            self.argument_specs.append(ANYWHERE)
            self.results.append(shape((z_count, count) + basis.shape[1:], low))
            self.result_specs.append(ANYWHERE)
        self.scratch += line_scratch(len(lines), z_count)
        if self.gathered:
            self.scratch.append(pltpu.SemaphoreType.DMA((self.gathered,)))
        if self.vectors:
            self.scratch.append(pltpu.VMEM((1, 4, 2, width // 8, lanes), full))

    def step_ticks(self, row_ticks):
        starts, firsts = [], []
        now = self.lead + row_ticks
        for c in range(self.inner):
            starts.append(now)
            needed = 5 + 2 * c - self.local
            firsts.append(max(now, needed + CLOSE + 1) if self.gathered else now)
            now = firsts[-1] + 2
        return starts, firsts

    def split(self, refs):
        return split_refs(
            refs, 5, len(self.arguments), 13, len(self.results), 6, GATHER_REFS * bool(self.gathered),
            GATHER_REFS * self.vectors, 2 * bool(self.lines),
        )

    def vec_whole(self, refs):
        return refs[-1]


def scratch_tail(plan, refs):
    return refs[-2] if plan.vectors else refs[-1]


def forward_layer(hidden, seg_column, seg_row, vectors, weights, out_dtype, plan, identity=None):
    tokens, width = hidden.shape
    inner = plan.inner
    wide = width * inner
    rows = tokens // L
    heads = width // HD
    shape = jax.ShapeDtypeStruct

    def here(s):
        return jnp.minimum(s, rows - 1)

    def column(s):
        return jnp.maximum(s - rows, 0)

    def row_block(columns):
        return pl.BlockSpec((L, columns), lambda s: (here(s), 0))

    def whole(columns):
        return pl.BlockSpec((tokens, columns), lambda s: (0, 0), pipeline_mode=pl.Buffered(1))

    wide_block = pl.BlockSpec((tokens, width), lambda s: (0, column(s)))
    out_shape = (
        shape((tokens, width), low), shape((tokens, width), low), shape((tokens, width), low),
        shape((width, tokens), low), shape((rows, heads, L), full),
        shape((tokens, width), full), shape((tokens, 1), full), shape((tokens, width), low),
        shape((tokens, wide), low), shape((tokens, wide), low),
        shape((tokens, width), full), shape((tokens, 1), full), shape((tokens, width), out_dtype),
        *plan.results,
    )
    out_specs = (
        row_block(width), row_block(width), row_block(width),
        pl.BlockSpec((width, L), lambda s: (0, here(s))), pl.BlockSpec((1, heads, L), lambda s: (here(s), 0, 0)),
        row_block(width), row_block(1), row_block(width),
        wide_block, wide_block,
        whole(width), whole(1), whole(width),
        *plan.result_specs,
    )
    total = 4 + 2 * inner
    held = max(total, plan.local + plan.gathered)
    return pl.pallas_call(
        functools.partial(forward_kernel, plan),
        grid=(rows + inner,),
        out_shape=out_shape,
        in_specs=[
            row_block(width),
            pl.BlockSpec((1, L, 1), lambda s: (here(s), 0, 0)),
            pl.BlockSpec((1, 1, L), lambda s: (here(s), 0, 0)),
            pl.BlockSpec(vectors.shape, lambda s: (0, 0)),
            ANYWHERE,
            *plan.argument_specs,
        ],
        out_specs=out_specs,
        scratch_shapes=[
            pltpu.VMEM((held, 4, 2, width // 8, width), low),
            pltpu.VMEM((L, L), full),
            pltpu.VMEM((width, L), low),
            pltpu.VMEM((tokens, width), low),
            pltpu.VMEM((tokens, width), full),
            pltpu.SemaphoreType.DMA((total,)),
            *plan.scratch,
        ],
        compiler_params=pltpu.CompilerParams(
            dimension_semantics=("arbitrary",), vmem_limit_bytes=62 * MIB,
            collective_id=identity, has_side_effects=identity is not None,
        ),
        cost_estimate=pl.CostEstimate(
            flops=2 * tokens * width * width * total + 4 * tokens * L * width,
            bytes_accessed=40 * MIB,
            transcendentals=tokens * (L * heads + wide),
        ),
        name="layer_forward",
    )(hidden, seg_column, seg_row, vectors, weights.reshape(-1, 4, 2, width // 8, width), *plan.arguments)


WIDE_HEAD_TICKS, WIDE_STEP_TICKS = 2, 4


def wide_ready(own):
    return [WIDE_HEAD_TICKS + WIDE_STEP_TICKS * (n // 2) + 2 + n % 2 for n in range(own)]


def wide_back_kernel(plan, inner, *refs):
    inputs, sources, outputs, targets, scratch, sum_refs, line_refs = plan.split(refs, 11, 4, 11)
    up_hbm, x2_hbm, inv2_hbm, x1_hbm, inv1_hbm, n1_hbm, vec_ref, wup_ref, wdown_ref, u_ref, gp_ref = inputs
    dw_ref, dr1_ref, da_ref, dvec_ref = outputs
    n1t, dz, kept_dw, up_ref, x2_ref, inv2_ref, x1_ref, inv1_ref, n1_ref, tile_sem, load_sem = scratch
    dy, dn1 = da_ref, dr1_ref
    c = pl.program_id(0)
    steps = pl.num_programs(0)
    tokens, width = dn1.shape
    tile = tokens // 4
    base = 5 + inner
    side = Side(plan, sources, targets, sum_refs, line_refs, kept_dw)

    def tile_copies(i):
        rows = pl.ds(pl.multiple_of(i * tile, tile), tile)
        return [
            pltpu.make_async_copy(source.at[rows], target.at[rows], tile_sem.at[n, i])
            for n, (source, target) in enumerate(((up_hbm, up_ref), (x2_hbm, x2_ref), (inv2_hbm, inv2_ref)))
        ]

    late_copies = [
        pltpu.make_async_copy(source, target, load_sem.at[n])
        for n, (source, target) in enumerate(((n1_hbm, n1_ref), (x1_hbm, x1_ref), (inv1_hbm, inv1_ref)))
    ]

    @pl.when(c == 0)
    def _():
        for i in range(4):
            for copy in tile_copies(i):
                copy.start()
        for copy in late_copies:
            copy.start()

    side.enter(c == 0)

    @pl.when(c == 0)
    def _():
        gain = vec_ref[base + 1 : base + 2, :]

        def body(i, carry):
            for copy in tile_copies(i):
                copy.wait()
            gain_sum, shift_sum, bias_sum = carry
            rows = pl.ds(pl.multiple_of(i * tile, tile), tile)
            upstream = up_ref[rows, :].astype(full)
            unit = x2_ref[rows, :]
            back = norm_back(upstream, unit, inv2_ref[rows, :], gain)
            dn1[rows, :] = back
            branch = back.astype(low)
            dy[rows, :] = branch
            @pl.when(lax.rem(i, 2) == 1)
            def _():
                side.tick(lax.div(i, 2))

            return (
                gain_sum + column_sum(upstream * unit),
                shift_sum + column_sum(upstream),
                bias_sum + column_sum(branch.astype(full)),
            )

        zero = jnp.zeros((1, width), full)
        gain_sum, shift_sum, bias_sum = lax.fori_loop(0, 4, body, (zero, zero, zero))
        dvec_ref[...] = jnp.zeros(dvec_ref.shape, full)
        dvec_ref[base : base + 1, :] = bias_sum
        dvec_ref[base + 1 : base + 2, :] = gain_sum
        dvec_ref[base + 2 : base + 3, :] = shift_sum
        late_copies[0].wait()
        n1t[...] = n1_ref[...].astype(full).T.astype(low)

    first_tick = WIDE_HEAD_TICKS + WIDE_STEP_TICKS * c

    def token_step(i, carry):
        for half in range(2):
            rows = pl.ds(pl.multiple_of((2 * i + half) * tile, tile), tile)
            slope = gp_ref[rows, :].astype(full)
            piece = (dot_nt(dy[rows, :], wdown_ref[0]) * slope).astype(low)
            dz[rows, :] = piece
            dn1[rows, :] += dot_nt(piece, wup_ref[0])
            carry = carry + column_sum(piece.astype(full))
        side.tick(first_tick + i)
        return carry

    bias_sum = lax.fori_loop(0, 2, token_step, jnp.zeros((1, width), full))
    side.advance(c == 1, 2)
    side.advance(c == 3, 3)
    for j in range(inner):
        @pl.when(c == j)
        def _():
            dvec_ref[5 + j : 6 + j, :] = bias_sum

    def store(k, grad):
        if plan.own:
            @pl.when(2 * c + k < plan.own)
            def _():
                kept_dw[2 * c + k] = grad.reshape(kept_dw.shape[1:])

            @pl.when(2 * c + k >= plan.own)
            def _():
                dw_ref[k, 0] = grad
        else:
            dw_ref[k, 0] = grad

    store(0, dot_nn(n1t[...], dz[...]).astype(low))
    side.tick(first_tick + 2)
    store(1, dot_tn(u_ref[...], dy[...]).astype(low))
    side.tick(first_tick + 3)
    final_tick = WIDE_HEAD_TICKS + WIDE_STEP_TICKS * inner

    @pl.when(c == steps - 1)
    def _():
        for copy in late_copies[1:]:
            copy.wait()
        gain = vec_ref[3:4, :]

        def body(i, carry):
            gain_sum, shift_sum, bias_sum = carry
            rows = pl.ds(pl.multiple_of(i * tile, tile), tile)
            upstream = dn1[rows, :]
            unit = x1_ref[rows, :]
            back = norm_back(upstream, unit, inv1_ref[rows, :], gain)
            dr1_ref[rows, :] = back
            branch = back.astype(low)
            da_ref[rows, :] = branch
            @pl.when(lax.rem(i, 2) == 1)
            def _():
                side.tick(final_tick + lax.div(i, 2))

            return (
                gain_sum + column_sum(upstream * unit),
                shift_sum + column_sum(upstream),
                bias_sum + column_sum(branch.astype(full)),
            )

        zero = jnp.zeros((1, width), full)
        gain_sum, shift_sum, bias_sum = lax.fori_loop(0, 4, body, (zero, zero, zero))
        dvec_ref[2:3, :] = bias_sum
        dvec_ref[3:4, :] = gain_sum
        dvec_ref[4:5, :] = shift_sum

    side.leave(c == steps - 1, final_tick + 2)


def wide_back(upstream, kept, vectors, weights, places, plan, identity=None):
    x1, inv1, n1, u, gp, x2, inv2 = kept
    tokens, width = x1.shape
    up_start, down_start, stride = places
    inner = u.shape[1] // width
    shape = jax.ShapeDtypeStruct

    return pl.pallas_call(
        functools.partial(wide_back_kernel, plan, inner),
        grid=(inner,),
        out_shape=(
            shape((2, inner - plan.own // 2, width, width), low),
            shape((tokens, width), full), shape((tokens, width), low), shape((16, width), full),
            *plan.results,
        ),
        in_specs=[
            *[ANYWHERE] * 6,
            pl.BlockSpec(vectors.shape, lambda c: (0, 0), pipeline_mode=pl.Buffered(1)),
            pl.BlockSpec((1, width, width), lambda c: (up_start + stride * c, 0, 0)),
            pl.BlockSpec((1, width, width), lambda c: (down_start + stride * c, 0, 0)),
            pl.BlockSpec((tokens, width), lambda c: (0, c)),
            pl.BlockSpec((tokens, width), lambda c: (0, c)),
            *plan.argument_specs,
        ],
        out_specs=(
            pl.BlockSpec((2, 1, width, width), lambda c: (0, jnp.maximum(c - plan.own // 2, 0), 0, 0)),
            pl.BlockSpec((tokens, width), lambda c: (0, 0), pipeline_mode=pl.Buffered(1)),
            pl.BlockSpec((tokens, width), lambda c: (0, 0), pipeline_mode=pl.Buffered(1)),
            pl.BlockSpec((16, width), lambda c: (0, 0)),
            *plan.result_specs,
        ),
        scratch_shapes=[
            pltpu.VMEM((width, tokens), low),
            pltpu.VMEM((tokens, width), low),
            pltpu.VMEM((plan.own, 4, 2, width // 8, width) if plan.own else (8, 128), low),
            pltpu.VMEM((tokens, width), upstream.dtype),
            pltpu.VMEM((tokens, width), full),
            pltpu.VMEM((tokens, 1), full),
            pltpu.VMEM((tokens, width), full),
            pltpu.VMEM((tokens, 1), full),
            pltpu.VMEM((tokens, width), low),
            pltpu.SemaphoreType.DMA((3, 4)),
            pltpu.SemaphoreType.DMA((3,)),
            *plan.scratch,
        ],
        compiler_params=pltpu.CompilerParams(
            dimension_semantics=("arbitrary",), vmem_limit_bytes=60 * MIB,
            collective_id=identity, has_side_effects=identity is not None,
        ),
        cost_estimate=pl.CostEstimate(
            flops=8 * tokens * width * width * inner, bytes_accessed=50 * MIB, transcendentals=0
        ),
        name="wide_backward",
    )(upstream, x2, inv2, x1, inv1, n1, vectors, weights, weights, u, gp, *plan.arguments)


def attend_back_kernel(plan, *refs):
    inputs, sources, outputs, targets, scratch, sum_refs, line_refs = plan.split(refs, 11, 3, 14)
    da_hbm, dr1_ref, x_ref, q_ref, k_ref, v_ref, ctxt_hbm, lse_ref, segc_ref, segr_ref, w_hbm = inputs
    dw_ref, dx_ref, dvec_ref = outputs
    bias, dctx, kt, delta, dqt, xt, dq_all, dk_all, dv_all, dwo, da_ref, ctxt_ref, w_ref, load_sem = scratch
    r = pl.program_id(0)
    loads = [
        pltpu.make_async_copy(w_hbm.at[plan.start + 3], w_ref.at[3], load_sem.at[0]),
        pltpu.make_async_copy(da_hbm, da_ref, load_sem.at[1]),
        pltpu.make_async_copy(ctxt_hbm, ctxt_ref, load_sem.at[2]),
        pltpu.make_async_copy(w_hbm.at[pl.ds(plan.start, 3)], w_ref.at[pl.ds(0, 3)], load_sem.at[3]),
    ]

    @pl.when(r == 0)
    def _():
        for copy in loads:
            copy.start()

    side = Side(plan, sources, targets, sum_refs, line_refs, dwo)
    side.enter(r == 0)
    tokens, width = dr1_ref.shape
    pairs = width // PAIR
    ticks = pairs + 4

    def tick(n):
        side.tick(r * ticks + n)

    tick(0)
    here = pl.ds(pl.multiple_of(r * tokens, tokens), tokens)

    @pl.when(r == 0)
    def _():
        for copy in loads[:3]:
            copy.wait()
        grad = dot_nn(ctxt_ref[...], da_ref[...]).astype(low)
        if plan.own:
            dwo[0] = grad.reshape(dwo.shape[1:])
        else:
            dw_ref[3] = grad

    xt[:, here] = x_ref[...].astype(low).astype(full).T.astype(low)
    bias[...] = segment_bias(segc_ref[0], segr_ref[0])
    context_grad = dot_nt(da_ref[here, :], w_ref[3]).astype(low)
    dctx[...] = context_grad
    kt[...] = k_ref[...].astype(full).T.astype(low)
    products = context_grad.astype(full) * ctxt_ref[:, here].astype(full).T
    feature = lax.broadcasted_iota(jnp.int32, (16, width), 1)
    head = lax.broadcasted_iota(jnp.int32, (16, width), 0)
    member = ((feature >= head * HD) & (feature < (head + 1) * HD)).astype(full).astype(low)
    high = products.astype(low)
    rest = (products - high.astype(full)).astype(low)
    delta[...] = dot_nt(member, high) + dot_nt(member, rest)
    tick(1)
    masks = half_masks(low)
    scale = HD ** (-0.5)

    def pair_step(p, carry):
        lanes = pl.ds(pl.multiple_of(p * PAIR, PAIR), PAIR)
        q_pair = q_ref[:, lanes] * jnp.asarray(scale, low)
        k_pair = k_ref[:, lanes]
        v_pair = v_ref[:, lanes]
        g_pair = dctx[:, lanes]
        key_grad = jnp.zeros((tokens, PAIR), full)
        value_grad = jnp.zeros((tokens, PAIR), full)
        for h in range(2):
            q_half = q_pair * masks[h]
            g_half = g_pair * masks[h]
            scores = dot_nt(k_pair, q_half) + bias[...]
            attention = jnp.exp(scores - lse_ref[0, pl.ds(2 * p + h, 1), :])
            value_grad = value_grad + dot_nn(attention.astype(low), g_half)
            attention_grad = dot_nt(v_pair, g_half)
            score_grad = (attention * (attention_grad - delta[pl.ds(2 * p + h, 1), :])).astype(low)
            key_grad = key_grad + dot_nn(score_grad, q_half)
            rows = pl.ds(pl.multiple_of(p * PAIR + h * HD, HD), HD)
            dqt[rows, :] = dot_nn(kt[rows, :], score_grad) * scale
        dk_all[here, lanes] = key_grad.astype(low)
        dv_all[here, lanes] = value_grad.astype(low)
        tick(2 + p)
        side.advance((r == 0) & (p == 4), 2)
        side.advance((r == 1) & (p == 3), 3)
        return carry

    lax.fori_loop(0, pairs, pair_step, 0)
    tick(2 + pairs)

    @pl.when(r == 0)
    def _():
        loads[3].wait()

    query_grad = dqt[...].T.astype(low)
    dq_all[here, :] = query_grad
    key_grad = dk_all[here, :]
    value_grad = dv_all[here, :]
    dx_ref[...] = (
        dr1_ref[...]
        + dot_nt(query_grad, w_ref[0])
        + dot_nt(key_grad, w_ref[1])
        + dot_nt(value_grad, w_ref[2])
    )
    tick(3 + pairs)

    @pl.when(r == 0)
    def _():
        dvec_ref[...] = jnp.zeros(dvec_ref.shape, full)

    dvec_ref[0:1, :] += column_sum(query_grad.astype(full))
    dvec_ref[1:2, :] += column_sum(value_grad.astype(full))

    @pl.when(r == pl.num_programs(0) - 1)
    def _():
        for j, grad in enumerate((dq_all, dk_all, dv_all)):
            dw_ref[j] = dot_nn(xt[...], grad[...]).astype(low)
            side.tick(plan.rows * ticks + j)

    side.leave(r == pl.num_programs(0) - 1, plan.rows * ticks + 3)


def attend_back(da, dr1, hidden, kept, seg_column, seg_row, weights, start, plan, identity=None):
    q, k, v, ctxt, lse = kept
    tokens, width = da.shape
    rows = tokens // L
    heads = width // HD
    shape = jax.ShapeDtypeStruct
    plan.start, plan.rows = start, rows

    def row_block():
        return pl.BlockSpec((L, width), lambda r: (r, 0))

    return pl.pallas_call(
        functools.partial(attend_back_kernel, plan),
        grid=(rows,),
        out_shape=(
            shape((4 - plan.own, width, width), low), shape((tokens, width), full), shape((8, width), full),
            *plan.results,
        ),
        in_specs=[
            ANYWHERE,
            row_block(), row_block(), row_block(), row_block(), row_block(),
            ANYWHERE,
            pl.BlockSpec((1, heads, L), lambda r: (r, 0, 0)),
            pl.BlockSpec((1, L, 1), lambda r: (r, 0, 0)),
            pl.BlockSpec((1, 1, L), lambda r: (r, 0, 0)),
            ANYWHERE,
            *plan.argument_specs,
        ],
        out_specs=(
            pl.BlockSpec((4 - plan.own, width, width), lambda r: (0, 0, 0), pipeline_mode=pl.Buffered(1)),
            row_block(),
            pl.BlockSpec((8, width), lambda r: (0, 0)),
            *plan.result_specs,
        ),
        scratch_shapes=[
            pltpu.VMEM((L, L), full),
            pltpu.VMEM((L, width), low),
            pltpu.VMEM((width, L), low),
            pltpu.VMEM((16, L), full),
            pltpu.VMEM((width, L), full),
            pltpu.VMEM((width, tokens), low),
            pltpu.VMEM((tokens, width), low),
            pltpu.VMEM((tokens, width), low),
            pltpu.VMEM((tokens, width), low),
            pltpu.VMEM((1, 4, 2, width // 8, width) if plan.own else (8, 128), low),
            pltpu.VMEM((tokens, width), low),
            pltpu.VMEM((width, tokens), low),
            pltpu.VMEM((4, width, width), low),
            pltpu.SemaphoreType.DMA((4,)),
            *plan.scratch,
        ],
        compiler_params=pltpu.CompilerParams(
            dimension_semantics=("arbitrary",), vmem_limit_bytes=60 * MIB,
            collective_id=identity, has_side_effects=identity is not None,
        ),
        cost_estimate=pl.CostEstimate(
            flops=16 * tokens * width * width + 10 * tokens * L * width,
            bytes_accessed=30 * MIB,
            transcendentals=tokens * L * heads,
        ),
        name="attend_backward",
    )(da, dr1, hidden, q, k, v, ctxt, lse, seg_column, seg_row, weights, *plan.arguments)


def moments(rotated, first, second):
    first_new = beta_one * first + (1.0 - beta_one) * rotated
    second_new = beta_two * second + (1.0 - beta_two) * rotated * rotated
    direction = (
        first_new
        / (1.0 - beta_one**STEP)
        / (jnp.sqrt(second_new / (1.0 - beta_two**STEP)) + adam_epsilon)
    )
    return first_new, second_new, direction


def pack_lanes(piece):
    rows = piece.shape[0] // 2
    return jnp.concatenate([piece[:rows], piece[rows:]], axis=1)


def unpack_lanes(piece):
    columns = piece.shape[1] // 2
    return jnp.concatenate([piece[:, :columns], piece[:, columns:]], axis=0)


def optimizer_kernel(plan, *refs):
    spans = len(plan.spans)
    inputs, ready, dvecs, bases, lines_in, outputs, lines_out, scratch, sum_refs, vec_refs, line_refs = split_refs(
        refs, 6, plan.ready, plan.dvecs, plan.bases, spans, 5, spans, 21, SUM_REFS, SUM_REFS, 2 * bool(spans)
    )
    index_ref, place_ref, tail_hbm, first_hbm, second_hbm, blocks = inputs
    new_ref, low_ref, first_out, second_out, vec_out = outputs
    (store, left, right, first_in, second_in, g_out, g_in, t_out, t_in, e_out, e_in, w_out, w_in, vec_source,
     load_sem, g_sem, t_sem, e_sem, w_sem, left_sem, right_sem) = scratch
    slots, owners = g_in.shape[0], g_in.shape[1]
    z_count = t_in.shape[1]
    place = Place(z_count)
    dp, z = place.dp, place.z
    dps = [lax.rem(dp + d, owners) for d in range(owners)]
    count = blocks.shape[0]
    many = tail_hbm.shape[0]
    tail_times = [[many * stage + n for n in range(many)] for stage in range(5)]
    tail = BlockSum(place, [tail_hbm], sum_refs, tail_times)
    vec = BlockSum(place, [vec_source], vec_refs, [[many * stage + 1] for stage in range(5)])
    order = plan.free + [s for s in range(slots) if s not in plan.free]
    lines = line_gathers(place, plan.spans, lines_in, lines_out, line_refs, z_count)
    every = list(bases) + list(lines_out)
    late = [s for s in range(slots) if plan.left_map[s][0] >= len(bases)]

    def load(refs_map, target, sem, s):
        n, at = refs_map[s]
        return pltpu.make_async_copy(every[n].at[:, at], target.at[:, s], sem.at[s])

    def load_first(s):
        return pltpu.make_async_copy(first_hbm.at[s], first_in.at[s], load_sem.at[0, s])

    def load_second(s):
        return pltpu.make_async_copy(second_hbm.at[s], second_in.at[s], load_sem.at[1, s])

    for s in order:
        load(plan.right_map, right, right_sem, s).start()
        if s not in late:
            load(plan.left_map, left, left_sem, s).start()
        load_first(s).start()
        load_second(s).start()
    greet([(other, z) for other in dps[1:]] + place.z_partners())
    start = many
    for part in ready:
        store[start : start + part.shape[0]] = part[...]
        start += part.shape[0]
    store[0:many] = jnp.zeros((many,) + store.shape[1:], low)
    store[count] = jnp.zeros(store.shape[1:], low)
    rows = plan.vector_rows
    stacked = jnp.concatenate(
        [dvecs[0][0:2, :], dvecs[1][2:rows, :], dvecs[2][0:2, :], dvecs[3][2:rows, :],
         jnp.zeros((vec_source.shape[-1] - 2 * rows, blocks.shape[2]), full)], axis=0
    )
    vec_source[0] = stacked.T.reshape(vec_source.shape[1:])

    def g_copy(s, d):
        other = dps[d]
        return remote(g_out.at[s, d], g_in.at[s, dp], g_sem.at[0, s, d], g_sem.at[1, s, owners - d], (other, z))

    def t_copy(s, d):
        other = place.zs[d]
        return remote(t_out.at[s, d], t_in.at[s, z], t_sem.at[0, s, d], t_sem.at[1, s, z_count - d], (dp, other))

    def e_copy(s, d):
        other = place.zs[d]
        return remote(e_out.at[s, d], e_in.at[s, z], e_sem.at[0, s, d], e_sem.at[1, s, z_count - d], (dp, other))

    def w_copy(s, d):
        other = dps[d]
        return remote(
            w_out.at[s, other], w_in.at[s * owners + dp], w_sem.at[0, s, d], w_sem.at[1, s, owners - d], (other, z)
        )

    def send_out(s):
        for d in range(1, owners):
            g_out[s, d] = store[index_ref[s * owners + dps[d]]]
            g_copy(s, d).start()
        g_in[s, dp] = store[index_ref[s * owners + dp]]

    def turn(s):
        for d in range(1, owners):
            g_copy(s, d).wait()
        load(plan.right_map, right, right_sem, s).wait()
        grad = jnp.concatenate([unfold(g_in[s, c].astype(full)) for c in range(owners)], axis=0).astype(low)
        for d in range(1, z_count):
            t_out[s, d] = pack_lanes(dot_nt(right[place.zs[d], s], grad)).astype(low)
            t_copy(s, d).start()
        t_in[s, z] = pack_lanes(dot_nt(right[z, s], grad)).astype(low)

    def adapt(s):
        for d in range(1, z_count):
            t_copy(s, d).wait()
        load_first(s).wait()
        load_second(s).wait()
        load(plan.left_map, left, left_sem, s).wait()
        rotated = jnp.zeros(first_in.shape[1:], full)
        for f in range(z_count):
            rotated = rotated + dot_nn(unpack_lanes(t_in[s, f].astype(full)).astype(low), left[f, s])
        first_new, second_new, direction = moments(rotated, first_in[s], second_in[s])
        first_out[s] = first_new
        second_out[s] = second_new
        direction = direction.astype(low)
        for d in range(1, z_count):
            e_out[s, d] = pack_lanes(dot_nt(left[place.zs[d], s], direction)).astype(low)
            e_copy(s, d).start()
        e_in[s, z] = pack_lanes(dot_nt(left[z, s], direction)).astype(low)

    def step_back(s):
        for d in range(1, z_count):
            e_copy(s, d).wait()
        step = jnp.zeros((left.shape[2], left.shape[3]), full)
        for f in range(z_count):
            step = step + dot_nn(unpack_lanes(e_in[s, f].astype(full)).astype(low), right[f, s])
        share = step.shape[0] // owners
        for c in range(owners):
            w_out[s, c] = fold(step[c * share : (c + 1) * share]).astype(low)
        for d in range(1, owners):
            w_copy(s, d).start()
        w_in[s * owners + dp] = w_out[s, dp]

    def sums(stage):
        for t in range(many * stage, many * (stage + 1)):
            tail.tick(t)
            vec.tick(t)

    free = plan.free
    def advance(hop):
        for line in lines:
            line.advance(hop)

    sums(0)
    advance(1)
    for s in free:
        send_out(s)
    sums(1)
    for s in free:
        turn(s)
    sums(2)
    advance(2)
    for s in free:
        adapt(s)
    sums(3)
    sums(4)
    advance(3)
    for i in range(many):
        store[i] = tail.finish(i).astype(low)
    rest = order[len(free) :]
    for s in rest[:2]:
        send_out(s)
    for s in free:
        step_back(s)
    advance(z_count)
    for s in late:
        load(plan.left_map, left, left_sem, s).start()
    for k in range(len(rest) + 2):
        if k < len(rest):
            turn(rest[k])
            if k + 2 < len(rest):
                send_out(rest[k + 2])
        if 0 <= k - 1 < len(rest):
            adapt(rest[k - 1])
        if 0 <= k - 2 < len(rest):
            step_back(rest[k - 2])

    vec_out[...] = vec.finish(0)
    for s in range(slots):
        for d in range(1, owners):
            w_copy(s, d).wait()

    def block_step(b, carry):
        step = unfold(w_in[place_ref[b]].astype(full))
        block = blocks[b]
        new = block - matrix_rate * (step + weight_decay * block)
        new_ref[b] = new
        low_ref[b] = new.astype(low)
        return carry

    lax.fori_loop(0, count, block_step, 0)


class OptimizerPlan:
    def __init__(self, ready, dvecs, bases, spans, left_map, right_map, free, vector_rows):
        self.ready, self.dvecs, self.bases, self.spans = ready, dvecs, bases, spans
        self.left_map, self.right_map, self.free, self.vector_rows = left_map, right_map, free, vector_rows


def optimizer(
    index, places, tail, ready, dvecs, vector_rows, bases, lines, left_map, right_map, free, first, second, blocks,
    z_count, identity,
):
    slots, columns, width = first.shape
    owners = index.shape[0] // slots
    count, rows = blocks.shape[0], blocks.shape[1]
    span = bases[0].shape[2]
    lanes = 128
    shape = jax.ShapeDtypeStruct
    piece = (2 * rows, width // 2)
    tile = (span // 2, 2 * columns)
    smem = pl.BlockSpec(memory_space=pltpu.SMEM)
    spans = [(first_slot, amount) for _, first_slot, amount in lines]
    plan = OptimizerPlan(len(ready), len(dvecs), len(bases), spans, left_map, right_map, free, vector_rows)
    line_shapes = [shape((z_count, amount) + basis.shape[1:], low) for basis, _, amount in lines]
    return pl.pallas_call(
        functools.partial(optimizer_kernel, plan),
        out_shape=(
            shape(blocks.shape, full), shape(blocks.shape, low), shape(first.shape, full), shape(first.shape, full),
            shape((rows, lanes), full), *line_shapes,
        ),
        in_specs=[smem, smem, ANYWHERE, ANYWHERE, ANYWHERE, IN_VMEM]
        + [IN_VMEM] * (len(ready) + len(dvecs)) + [ANYWHERE] * (len(bases) + len(lines)),
        out_specs=(IN_VMEM,) * 5 + (ANYWHERE,) * len(lines),
        scratch_shapes=[
            pltpu.VMEM((count + 1,) + piece, low),
            pltpu.VMEM((z_count, slots, span, width), low),
            pltpu.VMEM((z_count, slots, columns, width), low),
            pltpu.VMEM((slots, columns, width), full),
            pltpu.VMEM((slots, columns, width), full),
            pltpu.VMEM((slots, owners) + piece, low),
            pltpu.VMEM((slots, owners) + piece, low),
            pltpu.VMEM((slots, z_count) + tile, low),
            pltpu.VMEM((slots, z_count) + tile, low),
            pltpu.VMEM((slots, z_count) + tile, low),
            pltpu.VMEM((slots, z_count) + tile, low),
            pltpu.VMEM((slots, owners) + piece, low),
            pltpu.VMEM((slots * owners,) + piece, low),
            pltpu.VMEM((1, owners // 2, 2, width // owners, lanes), full),
            pltpu.SemaphoreType.DMA((2, slots)),
            pltpu.SemaphoreType.DMA((2, slots, owners)),
            pltpu.SemaphoreType.DMA((2, slots, z_count)),
            pltpu.SemaphoreType.DMA((2, slots, z_count)),
            pltpu.SemaphoreType.DMA((2, slots, owners)),
            pltpu.SemaphoreType.DMA((slots,)),
            pltpu.SemaphoreType.DMA((slots,)),
            *sum_scratch(tail.shape[0], tail.shape[3], width, z_count),
            *sum_scratch(1, width // owners, lanes, z_count, full),
            *line_scratch(len(lines), z_count),
        ],
        compiler_params=pltpu.CompilerParams(
            vmem_limit_bytes=60 * MIB, collective_id=identity, has_side_effects=True
        ),
        cost_estimate=pl.CostEstimate(
            flops=8 * slots * span * width * width, bytes_accessed=40 * MIB, transcendentals=slots * width * columns
        ),
        name="optimizer",
    )(index, places, tail, first, second, blocks, *ready, *dvecs, *bases, *[basis for basis, _, _ in lines])


def slot_table(owner, slots, owner_rows):
    block_count = owner.shape[0]
    same_owner = owner[:, None] == owner[None, :]
    ordering = jnp.arange(block_count, dtype=jnp.int32)
    earlier = ordering[None, :] < ordering[:, None]
    ranking = jnp.sum(jnp.where(same_owner & earlier, 1, 0), axis=1).astype(jnp.int32)
    owner_match = owner[None, :] == jnp.arange(owner_rows, dtype=jnp.int32)[:, None]
    slot_match = ranking[None, :] == jnp.arange(slots, dtype=jnp.int32)[:, None]
    return jnp.where(slot_match[:, None, :] & owner_match[None, :, :], 1.0, 0.0).astype(full)


def scatter_sum(grads):
    blocks, width = grads.shape[0], grads.shape[2]
    cut = grads.reshape(blocks, lax.axis_size("dp"), -1, width).transpose(1, 0, 2, 3)
    outer = lax.psum_scatter(cut, "dp", scatter_dimension=0, tiled=False)
    blocks, rows, width = outer.shape
    count = lax.axis_size("fsdp")
    cut = outer.reshape(blocks, count, rows // count, width).transpose(1, 0, 2, 3)
    return lax.psum_scatter(cut, "fsdp", scatter_dimension=0, tiled=False)


def scatter_vectors(grads):
    rows, width = grads.shape
    count = lax.axis_size("dp") * lax.axis_size("fsdp")
    cut = grads.reshape(rows, count, width // count).transpose(1, 0, 2)
    return lax.psum_scatter(cut, ("dp", "fsdp"), scatter_dimension=0, tiled=False)


def gathering_program(
    tokens, segment, blocks, vectors, owner, left_basis, right_basis, rot_first, rot_second, cotangent, z_count
):
    layers, vector_rows = vectors.shape[:2]
    count, shard_rows, width = blocks.shape
    per_layer = count // layers
    inner = (per_layer - 4) // 2
    owners = lax.axis_size("dp")
    slots = rot_first.shape[0]
    part = width // owners
    lanes = 128
    seg_column, seg_row = segment[:, :, None], segment[:, None, :]

    order = [0, 1, 2, 3]
    for c in range(inner):
        order += [4 + c, 4 + inner + c]
    folded = blocks.astype(low).reshape(count, shard_rows, 2, width // 2).transpose(0, 2, 1, 3)
    folded = folded.reshape(count, 2 * shard_rows, width // 2)

    def pick(numbers):
        return jnp.stack([folded[j] for j in numbers])

    head = pick(order + [per_layer + j for j in order[:4]])
    rest = pick([per_layer + j for j in order[4:]])
    vec_shard = vectors.astype(low).astype(full).reshape(layers * vector_rows, shard_rows).T
    vec_shard = jnp.pad(vec_shard, ((0, 0), (0, lanes - layers * vector_rows)))[None]
    left_low = left_basis.reshape(slots, -1, width).astype(low)
    right_low = right_basis.transpose(0, 2, 1).astype(low)

    plan = ForwardPlan(
        inner, 0, head, vec_shard, vector_rows, [(right_low, 0, 2)], lead=9, row_ticks=3, z_count=z_count
    )
    empty_vec = jnp.zeros((16, width), full)
    results = forward_layer(tokens, seg_column, seg_row, empty_vec, jnp.zeros((1, width, width), low), full, plan, 6)
    kept_a = results[:12]
    hidden, weights_a, vec_a, vec_b, right_01 = results[12:]
    weights_a = weights_a.reshape(-1, width, width)
    plan = ForwardPlan(inner, 4, rest, lines=[(right_low, 2, 2)], lead=0, row_ticks=4, z_count=z_count)
    plan.order = [per_layer + j for j in range(4)]
    results = forward_layer(hidden, seg_column, seg_row, vec_b, weights_a, low, plan, 7)
    kept_b = results[:12]
    layer_out, weights_b, right_23 = results[12:]
    weights_b = weights_b.reshape(-1, width, width)

    def cut(grads):
        return grads.reshape(-1, owners // 2, 2, part, width)

    size = (part, width)
    own = 3
    skip = own % 2
    pending = 2 * inner - own

    plan = Plan(None, [(right_low, 4, 1), (left_low, 3, 1)], z_count, own, size, wide_ready(own))
    dw_wide, dr1, da, dvec_wide_b, wide_sum_b, right_4, left_3 = wide_back(
        cotangent, kept_b[5:], vec_b, weights_b, (0, 1, 2), plan, 1
    )
    ready = list(range(pending + 1))
    plan = Plan(cut(dw_wide), [(left_low, 4, 1)], z_count, 1, size, ready, skip)
    dw_attend, upstream, dvec_attend_b, attend_sum_b, left_4 = attend_back(
        da, dr1, hidden, kept_b[:5], seg_column, seg_row, weights_a, per_layer, plan, 2
    )
    plan = Plan(cut(dw_attend), [(left_low, 0, 1)], z_count, own, size, [0, 1, 2] + wide_ready(own))
    dw_wide, dr1, da, dvec_wide_a, wide_sum_a, left_0 = wide_back(
        upstream, kept_a[5:], vec_a, weights_a, (4, 5, 2), plan, 3
    )
    plan = Plan(cut(dw_wide), [(left_low, 1, 1)], z_count, 1, size, ready, skip)
    dw_attend, upstream, dvec_attend_a, attend_sum_a, left_1 = attend_back(
        da, dr1, tokens, kept_a[:5], seg_column, seg_row, weights_a, 0, plan, 5
    )

    three = list(range(3))
    early = [4 + n // 2 + inner * (n % 2) for n in range(own)]
    late = [4 + c + inner * k for k in range(2) for c in range(inner) if 2 * c + k >= own] + [3]
    held_order = three + late + [per_layer + j for j in three] + early + [per_layer + j for j in late + early]
    rank = jnp.asarray([held_order.index(j) for j in range(count)], jnp.int32)
    table = slot_table(owner, slots, owners).reshape(slots * owners, count)
    held = jnp.sum(table, axis=1)
    index = jnp.where(held > 0, jnp.sum(table * rank, axis=1), count).astype(jnp.int32)
    places = jnp.sum(table * jnp.arange(slots * owners, dtype=jnp.int32)[:, None], axis=0).astype(jnp.int32)
    bases = (right_01, right_23, right_4, left_0, left_1, left_3, left_4)
    right_map = [(0, 0), (0, 1), (1, 0), (1, 1), (2, 0)]
    left_map = [(3, 0), (4, 0), (7, 0), (5, 0), (6, 0)]
    free = list(range(3, slots))
    new_blocks, new_low, first_new, second_new, vec_sum, _ = optimizer(
        index, places, cut(dw_attend), (attend_sum_a, wide_sum_a, attend_sum_b, wide_sum_b),
        (dvec_attend_a, dvec_wide_a, dvec_attend_b, dvec_wide_b), vector_rows, bases, [(left_low, 2, 1)], left_map, right_map, free,
        rot_first.transpose(0, 2, 1), rot_second.transpose(0, 2, 1), blocks, z_count, 4,
    )
    first_new, second_new = first_new.transpose(0, 2, 1), second_new.transpose(0, 2, 1)
    vector_grad = vec_sum[:, : layers * vector_rows].T.reshape(layers, vector_rows, shard_rows)
    return layer_out, upstream, new_blocks, new_low, first_new, second_new, vector_grad


def plain_program(
    tokens, segment, blocks, vectors, owner, left_basis, right_basis, rot_first, rot_second, cotangent
):
    layers, vector_rows = vectors.shape[:2]
    per_layer = blocks.shape[0] // layers
    inner = (per_layer - 4) // 2
    width = blocks.shape[2]
    owner_rows = lax.axis_size("dp")
    slots = rot_first.shape[0]
    selector = slot_table(owner, slots, owner_rows)
    vector_parts = lax.all_gather(vectors.astype(low), ("dp", "fsdp"), axis=0, tiled=False)
    vector_full = vector_parts.transpose(1, 2, 0, 3).reshape(layers, vector_rows, width).astype(full)
    blocks_low, vector_full = lax.optimization_barrier((blocks.astype(low), vector_full))

    seg_column = segment[:, :, None]
    seg_row = segment[:, None, :]
    state = tokens
    kept = []
    for layer_index in range(layers):
        start = per_layer * layer_index
        weights = lax.all_gather(blocks_low[start : start + per_layer], ("dp", "fsdp"), axis=1, tiled=True)
        out_dtype = low if layer_index == layers - 1 else full
        results = forward_layer(
            state, seg_column, seg_row, vector_full[layer_index], weights, out_dtype, ForwardPlan(inner, per_layer)
        )
        kept.append((state, weights, results[:5], results[5:12]))
        state = results[12]
    layer_out = state
    upstream = cotangent
    right_low = lax.all_gather(right_basis.astype(low), "fsdp", axis=2, tiled=True)
    block_shards = [None] * layers
    vector_shards = [None] * layers
    for layer_index in reversed(range(layers)):
        hidden, weights, attend_kept, wide_kept = kept[layer_index]
        dw_wide, dr1, da, dvec_wide = wide_back(
            upstream, wide_kept, vector_full[layer_index], weights, (4, 4 + inner, 1), Plan()
        )
        wide_shard = scatter_sum(dw_wide.reshape(-1, width, width))
        dw_attend, upstream, dvec_attend = attend_back(
            da, dr1, hidden, attend_kept, seg_column, seg_row, weights, 0, Plan()
        )
        dvec = jnp.concatenate([dvec_attend[:2], dvec_wide[2:vector_rows]], axis=0)
        block_shards[layer_index] = jnp.concatenate([scatter_sum(dw_attend), wide_shard], axis=0)
        vector_shards[layer_index] = scatter_vectors(dvec)
    vector_grad = jnp.stack(vector_shards)
    block_grad = jnp.concatenate(block_shards, axis=0)
    outgoing = jnp.einsum("srk,kid->srid", selector.astype(low), block_grad, preferred_element_type=full)
    incoming = lax.all_to_all(outgoing.astype(low), "dp", split_axis=1, concat_axis=1, tiled=True)
    owned = incoming.reshape(slots, -1, width)
    turned = jnp.einsum("sik,skj->sij", owned, right_low, preferred_element_type=full).astype(low)
    left_rows = left_basis.reshape(slots, -1, width).astype(low)
    partial_sums = jnp.einsum("sra,srb->sab", left_rows, turned, preferred_element_type=full)
    rotated = lax.psum_scatter(
        partial_sums.astype(low), "fsdp", scatter_dimension=2, tiled=True
    ).astype(full)
    first_new, second_new, direction = moments(rotated, rot_first, rot_second)
    direction_full = lax.all_gather(direction.astype(low), "fsdp", axis=2, tiled=True)
    back_right = jnp.einsum("sab,scb->sac", direction_full, right_low, preferred_element_type=full)
    step_rows = jnp.einsum(
        "sia,sac->sic", left_rows, back_right.astype(low), preferred_element_type=full
    )
    returned = lax.all_to_all(
        step_rows.reshape(slots, owner_rows, -1, width).astype(low),
        "dp",
        split_axis=1,
        concat_axis=1,
        tiled=True,
    )
    step_shard = jnp.einsum("srk,srid->kid", selector.astype(low), returned, preferred_element_type=full)
    new_blocks = blocks - matrix_rate * (step_shard + weight_decay * blocks)
    return layer_out, upstream, new_blocks, new_blocks.astype(low), first_new, second_new, vector_grad


def shards(
    tokens,
    segment,
    blocks,
    vectors,
    owner,
    left_basis,
    right_basis,
    rot_first,
    rot_second,
    vec_first,
    vec_second,
    cotangent,
):
    operands = (
        tokens, segment, blocks, vectors, owner, left_basis, right_basis, rot_first, rot_second, cotangent
    )
    z_count = lax.axis_size("fsdp")
    if lax.axis_size("dp") == 8 and z_count == 4:
        results = gathering_program(*operands, z_count)
    else:
        results = plain_program(*operands)
    layer_out, upstream, new_blocks, new_low, first_new, second_new, vector_grad = results
    vector_first = beta_one * vec_first + (1.0 - beta_one) * vector_grad
    vector_second = beta_two * vec_second + (1.0 - beta_two) * vector_grad * vector_grad
    vector_step = (
        vector_first
        / (1.0 - beta_one**STEP)
        / (jnp.sqrt(vector_second / (1.0 - beta_two**STEP)) + adam_epsilon)
    )
    vector_new = vectors - vector_rate * (vector_step + weight_decay * vectors)
    return (
        layer_out,
        upstream,
        new_blocks,
        new_low,
        first_new,
        second_new,
        vector_first,
        vector_second,
        vector_new,
    )


def solution(mesh):
    return jax.shard_map(
        shards,
        mesh=mesh,
        in_specs=(
            P(("dp", "fsdp"), None),
            P(("dp", "fsdp"), None),
            P(None, ("dp", "fsdp"), None),
            P(None, None, ("dp", "fsdp")),
            P(),
            P("dp", None, "fsdp", None),
            P("dp", None, "fsdp"),
            P("dp", None, "fsdp"),
            P("dp", None, "fsdp"),
            P(None, None, ("dp", "fsdp")),
            P(None, None, ("dp", "fsdp")),
            P(("dp", "fsdp"), None),
        ),
        out_specs=(
            P(("dp", "fsdp"), None),
            P(("dp", "fsdp"), None),
            P(None, ("dp", "fsdp"), None),
            P(None, ("dp", "fsdp"), None),
            P("dp", None, "fsdp"),
            P("dp", None, "fsdp"),
            P(None, None, ("dp", "fsdp")),
            P(None, None, ("dp", "fsdp")),
            P(None, None, ("dp", "fsdp")),
        ),
        check_vma=False,
    )
```

```python
import functools

import jax
import jax.numpy as jnp
from jax import lax
from jax.experimental import pallas as pl
from jax.experimental.pallas import tpu as pltpu
from jax.sharding import PartitionSpec as P

H = 12
HD = 64
L = 512
STEP = 5
PAIR = 2 * HD
MIB = 1 << 20

beta_one = 0.5
beta_two = 0.5
adam_epsilon = 1e-08
norm_epsilon = 1e-06
matrix_rate = 0.03
vector_rate = 0.2
weight_decay = 0.01
masked_score = -1e30
low = jnp.bfloat16
full = jnp.float32


def dot_nn(a, b):
    return lax.dot_general(a, b, (((1,), (0,)), ((), ())), preferred_element_type=full)


def dot_nt(a, b):
    return lax.dot_general(a, b, (((1,), (1,)), ((), ())), preferred_element_type=full)


def dot_tn(a, b):
    return lax.dot_general(a, b, (((0,), (0,)), ((), ())), preferred_element_type=full)


def gelu_parts(z):
    size = jnp.abs(z) * 0.7071067811865476
    t = 1.0 / (1.0 + 0.3275911 * size)
    bell = jnp.exp(-0.5 * z * z)
    poly = ((((1.061405429 * t - 1.453152027) * t + 1.421413741) * t - 0.284496736) * t + 0.254829592) * t
    half_tail = 0.5 * poly * bell
    phi = jnp.where(z >= 0, 1.0 - half_tail, half_tail)
    return z * phi, phi + z * bell * 0.3989422804014327


def norm_parts(residual):
    average = jnp.mean(residual, axis=-1, keepdims=True)
    centered = residual - average
    inverse = lax.rsqrt(jnp.mean(centered * centered, axis=-1, keepdims=True) + norm_epsilon)
    return centered * inverse, inverse


def norm_back(upstream, unit, inverse, gain):
    scaled = upstream * gain
    return inverse * (
        scaled
        - jnp.mean(scaled, axis=-1, keepdims=True)
        - unit * jnp.mean(scaled * unit, axis=-1, keepdims=True)
    )


def column_sum(values):
    return jnp.sum(values, axis=0, keepdims=True)


def half_masks(dtype):
    lane = lax.broadcasted_iota(jnp.int32, (1, PAIR), 1)
    first = (lane < HD).astype(full)
    return first.astype(dtype), (1.0 - first).astype(dtype)


def segment_bias(seg_column, seg_row):
    return jnp.where(seg_column == seg_row, 0.0, masked_score)


class Place:
    def __init__(self, z_count):
        self.dp, self.z = lax.axis_index("dp"), lax.axis_index("fsdp")
        self.core, self.spot = lax.rem(self.dp, 2), lax.div(self.dp, 2)
        x_step = 1 - 2 * lax.rem(self.spot, 2)
        y_step = 2 - 4 * lax.div(self.spot, 2)
        self.spot_a = self.spot + (1 - self.core) * x_step + self.core * y_step
        self.spot_b = self.spot + self.core * x_step + (1 - self.core) * y_step
        self.spot_ab = self.spot + x_step + y_step
        self.sibling = (self.dp + 1 - 2 * self.core, self.z)
        self.near_a = (2 * self.spot_a + self.core, self.z)
        self.near_b = (2 * self.spot_b + self.core, self.z)
        self.z_count = z_count
        self.zs = [lax.rem(self.z + d, z_count) for d in range(z_count)]
        self.has_up, self.has_down = self.z < z_count - 1, self.z > 0
        self.middle = self.has_up & self.has_down
        self.across = lax.rem(self.z + 2, z_count)
        self.beside = jnp.where(self.z < 2, 1 - self.z, 5 - self.z)

    def line_sends(self, d):
        return {1: self.has_up, 2: self.z >= 0, 3: self.has_down}[d]

    def line_receives(self, d):
        return {1: self.has_down, 2: self.z >= 0, 3: self.has_up}[d]

    def chip_partners(self):
        return [self.sibling, self.near_a, self.near_b]

    def z_partners(self):
        return [(self.dp, other) for other in self.zs[1:]]


def greet(partners):
    barrier = pltpu.get_barrier_semaphore()
    for device in partners:
        pl.semaphore_signal(barrier, inc=1, device_id=device, device_id_type=pl.DeviceIdType.MESH)
    pl.semaphore_wait(barrier, len(partners))


def remote(source, target, send, receive, device):
    return pltpu.make_async_remote_copy(
        src_ref=source,
        dst_ref=target,
        send_sem=send,
        recv_sem=receive,
        device_id=device,
        device_id_type=pl.DeviceIdType.MESH,
    )


def fold(piece):
    half = piece.shape[1] // 2
    return jnp.concatenate([piece[:, :half], piece[:, half:]], axis=0)


def unfold(piece):
    rows = piece.shape[0] // 2
    return jnp.concatenate([piece[:rows], piece[rows:]], axis=1)


def looked_up(ticks, t):
    now = functools.reduce(jnp.logical_or, [t == tick for tick in ticks])
    which = sum(n * (t == tick).astype(jnp.int32) for n, tick in enumerate(ticks))
    return now, which


def run_due(stages, t):
    for ticks, stage in stages:
        if isinstance(t, int):
            if t in ticks:
                stage(ticks.index(t))
            continue
        now, block = looked_up(ticks, t)

        @pl.when(now)
        def _():
            stage(block)


def sum_times(ready):
    opens, cores, seconds = [], [], []
    for tick in ready:
        opens.append(max(tick, opens[-1] + 1) if opens else tick)
        cores.append(max(opens[-1] + 1, cores[-1] + 1) if cores else opens[-1] + 1)
        seconds.append(max(cores[-1] + 3, seconds[-1] + 3) if seconds else cores[-1] + 3)
    thirds = [tick + 2 for tick in seconds]
    return opens, cores, seconds, thirds, [tick + 2 for tick in thirds]


ANNOUNCE, FORWARD, FIRST, SECOND, CLOSE = -2, -1, 1, 2, 3


def sum_scratch(count, part, width, z_count, kind=low):
    piece = (2 * part // z_count, width // 2) if kind == low else (part // z_count, width)
    return [
        pltpu.VMEM((count, 4, part, width), kind),
        pltpu.VMEM((count, 4, part, width), kind),
        pltpu.VMEM((count, 2, part, width), kind),
        pltpu.VMEM((count, part, width), kind),
        pltpu.VMEM((count, z_count) + piece, kind),
        pltpu.VMEM((count, z_count) + piece, kind),
        pltpu.VMEM((count,) + piece, kind),
        pltpu.SemaphoreType.DMA((count,)),
        pltpu.SemaphoreType.DMA((count, 2)),
        pltpu.SemaphoreType.DMA((count, 2, 2)),
        pltpu.SemaphoreType.DMA((count, 2)),
        pltpu.SemaphoreType.DMA((count, 2, z_count)),
        pltpu.SemaphoreType.DMA((count, 2)),
    ]


SUM_REFS = 13


class BlockSum:
    def __init__(self, place, sources, refs, times):
        self.place, self.sources, self.times = place, sources, times
        (self.own, self.c, self.b, self.a, self.zs, self.zr, self.far,
         self.own_sem, self.c_sem, self.b_sem, self.a_sem, self.z_sem, self.far_sem) = refs
        self.count = self.c.shape[0]
        self.kind = self.c.dtype
        self.z_count = self.zs.shape[1]

    def load(self, i, block):
        return pltpu.make_async_copy(block.at[:, self.place.core], self.own.at[i], self.own_sem.at[i])

    def core_copy(self, i, block):
        return remote(
            block.at[:, 1 - self.place.core], self.c.at[i], self.c_sem.at[i, 0], self.c_sem.at[i, 1], self.place.sibling
        )

    def second_copy(self, i, k):
        chunk = self.place.spot_b if k == 0 else self.place.spot_ab
        return remote(
            self.c.at[i, chunk], self.b.at[i, k], self.b_sem.at[i, 0, k], self.b_sem.at[i, 1, k], self.place.near_b
        )

    def third_copy(self, i):
        return remote(
            self.c.at[i, self.place.spot_a], self.a.at[i], self.a_sem.at[i, 0], self.a_sem.at[i, 1], self.place.near_a
        )

    def z_copy(self, i, d):
        other = self.place.zs[d]
        return remote(
            self.zs.at[i, other], self.zr.at[i, self.place.z], self.z_sem.at[i, 0, d],
            self.z_sem.at[i, 1, self.z_count - d], (self.place.dp, other),
        )

    def open(self, i):
        first = 0
        for source in self.sources:
            count = source.shape[0]

            @pl.when((i >= first) & (i < first + count))
            def _():
                block = source.at[jnp.clip(i - first, 0, count - 1)]
                self.core_copy(i, block).start()
                self.load(i, block).start()

            first += count

    def after_core(self, i):
        block = self.sources[0].at[0]
        self.core_copy(i, block).wait()
        self.load(i, block).wait()
        for k in range(4):
            self.c[i, k] = (self.c[i, k].astype(full) + self.own[i, k].astype(full)).astype(self.kind)
        self.second_copy(i, 0).start()
        self.second_copy(i, 1).start()

    def after_second(self, i):
        other, spot = self.place.spot_a, self.place.spot
        self.second_copy(i, 1).wait()
        self.c[i, other] = (self.c[i, other].astype(full) + self.b[i, 1].astype(full)).astype(self.kind)
        self.third_copy(i).start()
        self.second_copy(i, 0).wait()
        self.c[i, spot] = (self.c[i, spot].astype(full) + self.b[i, 0].astype(full)).astype(self.kind)

    def after_third(self, i):
        self.third_copy(i).wait()
        total = self.c[i, self.place.spot].astype(full) + self.a[i].astype(full)
        rows = total.shape[0] // self.z_count
        for k in range(self.z_count):
            piece = total[k * rows : (k + 1) * rows]
            self.zs[i, k] = fold(piece).astype(low) if self.kind == low else piece
        place = self.place
        for d in (1, 3):
            @pl.when(place.line_sends(d))
            def _():
                self.z_copy(i, d).start()

        @pl.when(jnp.logical_not(place.middle))
        def _():
            self.z_copy(i, 2).start()
            self.far_copy(i).start()
            opposite = self.z_count - 1 - place.z
            self.zr[i, opposite] = jnp.zeros(self.zr.shape[2:], self.kind)

    def far_copy(self, i):
        place = self.place
        return remote(
            self.zs.at[i, self.z_count - 1 - place.z], self.far.at[i], self.far_sem.at[i, 0], self.far_sem.at[i, 1],
            (place.dp, place.beside),
        )

    def relay(self, i):
        @pl.when(self.place.middle)
        def _():
            self.far_copy(i).wait_recv()
            across = self.place.across
            self.zs[i, across] = (self.zs[i, across].astype(full) + self.far[i].astype(full)).astype(self.kind)
            self.z_copy(i, 2).start()

    def finish(self, i):
        for d in range(1, self.z_count):
            @pl.when(self.place.line_sends(d))
            def _():
                self.z_copy(i, d).wait_send()

            @pl.when(self.place.line_receives(d))
            def _():
                self.z_copy(i, d).wait_recv()

        @pl.when(jnp.logical_not(self.place.middle))
        def _():
            self.far_copy(i).wait_send()

        total = self.zs[i, self.place.z].astype(full)
        for d in range(1, self.z_count):
            total = total + self.zr[i, self.place.zs[d]].astype(full)
        return total

    def tick(self, t):
        stages = (self.relay, self.after_third, self.after_second, self.after_core, self.open)
        run_due(list(zip(self.times[::-1], stages)), t)

    @property
    def last(self):
        return self.times[4][-1]


class LineGather:
    def __init__(self, place, source, target, first, local_sem, sem, z_count):
        self.place = place
        self.source = source.at[pl.ds(first, target.shape[1])]
        self.target, self.local_sem, self.sem, self.z_count = target, local_sem, sem, z_count

    def hop_copy(self, hop, way):
        dp, z = self.place.dp, self.place.z
        if way == 0:
            piece, other, coming = z - hop + 1, z + 1, z - hop
            sends = (piece >= 0) & (other < self.z_count)
            receives = coming >= 0
        else:
            piece, other, coming = z + hop - 1, z - 1, z + hop
            sends = (piece < self.z_count) & (other >= 0)
            receives = coming < self.z_count
        piece = jnp.clip(piece, 0, self.z_count - 1)
        other = jnp.clip(other, 0, self.z_count - 1)
        source = self.source if hop == 1 else self.target.at[piece]
        copy = remote(source, self.target.at[piece], self.sem.at[way, 0, hop - 1], self.sem.at[way, 1, hop - 1], (dp, other))
        return copy, sends, receives

    def local(self):
        return pltpu.make_async_copy(self.source, self.target.at[self.place.z], self.local_sem)

    def start(self, hop):
        if hop == 1:
            self.local().start()
        for way in range(2):
            copy, sends, _ = self.hop_copy(hop, way)

            @pl.when(sends)
            def _():
                copy.start()

    def wait(self, hop):
        if hop == 1:
            self.local().wait()
        for way in range(2):
            copy, sends, receives = self.hop_copy(hop, way)

            @pl.when(sends)
            def _():
                copy.wait_send()

            @pl.when(receives)
            def _():
                copy.wait_recv()

    def advance(self, hop):
        if hop > 1:
            self.wait(hop - 1)
        if hop < self.z_count:
            self.start(hop)


def gather_scratch(count, group, rows, width, z_count, kind=low):
    piece = (2 * rows // z_count, width // 2) if kind == low else (rows // z_count, width)
    return [
        pltpu.VMEM((count, z_count, group) + piece, kind),
        pltpu.SemaphoreType.DMA((count, 2, z_count)),
        pltpu.SemaphoreType.DMA((count, 2)),
        pltpu.SemaphoreType.DMA((count, 2, 2)),
        pltpu.SemaphoreType.DMA((count, 2)),
        pltpu.SemaphoreType.DMA((count, 2)),
    ]


GATHER_REFS = 6


class BlockGather:
    def __init__(self, place, source, whole, base, refs):
        self.place, self.source, self.whole, self.base = place, source, whole, base
        self.zr, self.z_sem, self.a_sem, self.b_sem, self.c_sem, self.far_sem = refs
        self.count, self.z_count, self.group = self.zr.shape[:3]

    def blocks(self, i):
        return pl.ds(self.base + self.group * i, self.group)

    def z_copy(self, i, d):
        place = self.place
        return remote(
            self.source.at[i], self.zr.at[i, place.z], self.z_sem.at[i, 0, d], self.z_sem.at[i, 1, self.z_count - d],
            (place.dp, place.zs[d]),
        )

    def chunk(self, i, spot):
        return self.whole.at[self.blocks(i), spot, self.place.core]

    def first_copy(self, i):
        chunk = self.chunk(i, self.place.spot)
        return remote(chunk, chunk, self.a_sem.at[i, 0], self.a_sem.at[i, 1], self.place.near_a)

    def second_copy(self, i, k):
        chunk = self.chunk(i, self.place.spot if k == 0 else self.place.spot_a)
        return remote(chunk, chunk, self.b_sem.at[i, 0, k], self.b_sem.at[i, 1, k], self.place.near_b)

    def core_copy(self, i):
        chunks = self.whole.at[self.blocks(i), :, self.place.core]
        return remote(chunks, chunks, self.c_sem.at[i, 0], self.c_sem.at[i, 1], self.place.sibling)

    def far_copy(self, i):
        place = self.place
        piece = self.zr.at[i, place.across]
        return remote(piece, piece, self.far_sem.at[i, 0], self.far_sem.at[i, 1], (place.dp, place.beside))

    def announce(self, i):
        for d in range(1, self.z_count):
            @pl.when(self.place.line_sends(d))
            def _():
                self.z_copy(i, d).start()

        self.zr[i, self.place.z] = self.source[i]

    def forward(self, i):
        @pl.when(self.place.middle)
        def _():
            self.z_copy(i, 2).wait_recv()
            self.far_copy(i).start()

    def begin(self):
        for i in range(min(-ANNOUNCE, self.count)):
            self.announce(i)

    def open(self, i):
        place = self.place
        for d in range(1, self.z_count):
            @pl.when(place.line_sends(d))
            def _():
                self.z_copy(i, d).wait_send()

        for d in (1, 3):
            @pl.when(place.line_receives(d))
            def _():
                self.z_copy(i, d).wait_recv()

        @pl.when(place.middle)
        def _():
            self.far_copy(i).wait_send()

        @pl.when(jnp.logical_not(place.middle))
        def _():
            self.z_copy(i, 2).wait_recv()
            self.far_copy(i).wait_recv()

        for n in range(self.group):
            pieces = [self.zr[i, k, n].astype(full) for k in range(self.z_count)]
            if self.zr.dtype == low:
                pieces = [unfold(piece) for piece in pieces]
            whole = jnp.concatenate(pieces, axis=0).astype(self.whole.dtype)
            self.whole[self.base + self.group * i + n, place.spot, place.core] = whole
        self.first_copy(i).start()
        self.second_copy(i, 0).start()

    def after_first(self, i):
        self.first_copy(i).wait()
        self.second_copy(i, 1).start()

    def after_second(self, i):
        self.second_copy(i, 0).wait()
        self.second_copy(i, 1).wait()
        self.core_copy(i).start()

    def close(self, i):
        self.core_copy(i).wait()

    def tick(self, t, done=None):
        def close(i):
            self.close(i)
            if done is not None:
                done(i)

        @pl.when(t == 0)
        def _():
            for i in range(min(-FORWARD, self.count)):
                self.forward(i)

        stages = (
            (SECOND, self.after_second), (FIRST, self.after_first), (0, self.open), (FORWARD, self.forward),
            (ANNOUNCE, self.announce), (CLOSE, close),
        )
        for late, stage in stages:
            @pl.when((t >= max(late, 0)) & (t - late < self.count))
            def _():
                stage(t - late)


def split_refs(refs, *counts):
    result, start = [], 0
    for count in counts:
        result.append(refs[start : start + count])
        start += count
    return result


class Side:
    def __init__(self, plan, sources, targets, sum_refs, line_refs, own=None):
        self.plan = plan
        sums = plan.sums
        blocks = [source.at[pl.ds(plan.skip, source.shape[0] - plan.skip)] for source in sources[:sums]]
        blocks += [own] if plan.own else []
        self.place = Place(plan.z_count) if plan.active else None
        self.sum = BlockSum(self.place, blocks, sum_refs, plan.times) if plan.total else None
        self.result = targets[0] if plan.total else None
        self.lines = line_gathers(self.place, plan.lines, sources[sums:], targets[bool(plan.total) :], line_refs, plan.z_count)

    def enter(self, now):
        if not self.plan.active:
            return

        @pl.when(now)
        def _():
            greet((self.place.chip_partners() if self.plan.total else []) + self.place.z_partners())
            for line in self.lines:
                line.advance(1)

    def tick(self, t):
        if self.plan.total:
            self.sum.tick(t)

    def leave(self, now, ticks):
        if not self.plan.active:
            return

        @pl.when(now)
        def _():
            if self.plan.total:
                if self.sum.last >= ticks:
                    lax.fori_loop(ticks, self.sum.last + 1, lambda t, carry: (self.tick(t), carry)[1], 0)
                for i in range(self.sum.count):
                    self.result[i] = self.sum.finish(i).astype(low)
            for line in self.lines:
                line.advance(self.plan.z_count)

    def advance(self, now, hop):
        if self.lines and hop < self.plan.z_count:
            @pl.when(now)
            def _():
                for line in self.lines:
                    line.advance(hop)


class Plan:
    def __init__(self, pending=None, lines=(), z_count=1, own=0, size=None, ready=(), skip=0):
        self.z_count = z_count
        self.sums = int(pending is not None)
        self.own, self.skip = own, skip
        self.total = own + (pending.shape[0] - skip if self.sums else 0)
        self.times = sum_times(ready) if self.total else None
        self.lines = [(first, count) for _, first, count in lines]
        self.active = bool(self.total or lines)
        self.arguments, self.results, self.result_specs, self.scratch = [], [], [], []
        if self.sums:
            self.arguments.append(pending)
        if self.total:
            part, width = size
            self.results.append(jax.ShapeDtypeStruct((self.total, 2 * part // z_count, width // 2), low))
            self.result_specs.append(
                pl.BlockSpec(self.results[0].shape, lambda i: (0, 0, 0), pipeline_mode=pl.Buffered(1))
            )
            self.scratch += sum_scratch(self.total, part, width, z_count)
        for basis, _, count in lines:
            self.arguments.append(basis)
            self.results.append(jax.ShapeDtypeStruct((z_count, count) + basis.shape[1:], low))
            self.result_specs.append(ANYWHERE)
        self.scratch += line_scratch(len(lines), z_count)
        self.argument_specs = [ANYWHERE] * len(self.arguments)

    def split(self, refs, inputs, outputs, scratch):
        count = len(self.lines)
        return split_refs(
            refs, inputs, self.sums + count, outputs, bool(self.total) + count, scratch,
            SUM_REFS * bool(self.total), 2 * bool(self.lines),
        )


def line_scratch(count, z_count):
    if not count:
        return []
    return [pltpu.SemaphoreType.DMA((count,)), pltpu.SemaphoreType.DMA((count, 2, 2, z_count - 1))]


def line_gathers(place, spans, sources, targets, refs, z_count):
    return [
        LineGather(place, source, target, first, refs[0].at[n], refs[1].at[n], z_count)
        for n, (source, target, (first, _)) in enumerate(zip(sources, targets, spans))
    ]


ANYWHERE = pl.BlockSpec(memory_space=pl.ANY)
IN_VMEM = pl.BlockSpec(memory_space=pltpu.VMEM)


def forward_kernel(plan, *refs):
    inputs, sources, outputs, targets, scratch, gather_refs, vec_refs, line_refs = plan.split(refs)
    x_ref, segc_ref, segr_ref, vec_ref, w_hbm = inputs
    (q_ref, k_ref, v_ref, ctxt_ref, lse_ref, x1_ref, inv1_ref, n1_ref, u_ref, gp_ref, x2_ref, inv2_ref,
     out_ref) = outputs
    w, bias, vt, n1_all, acc, w_sem = scratch
    s = pl.program_id(0)
    tokens, width = acc.shape
    rows_now = x_ref.shape[0]
    rows = tokens // rows_now
    inner = plan.inner
    local = plan.local
    gather = vec_gather = None
    place = Place(plan.z_count) if plan.gathered else None
    if plan.gathered:
        w_out, out_sem = targets[0], scratch_tail(plan, refs)
        gather = BlockGather(place, sources[0], w, local, gather_refs)
        if plan.vectors:
            vec_gather = BlockGather(place, sources[1], plan.vec_whole(refs), 0, vec_refs)
            vec_ref = targets[1]
    lines = line_gathers(place, plan.lines, sources[plan.line_at :], targets[plan.line_target_at :], line_refs, plan.z_count)

    def keep(i):
        group = gather.group
        return pltpu.make_async_copy(w.at[gather.blocks(i)], w_out.at[pl.ds(group * i, group)], out_sem.at[i])

    def load(j):
        return pltpu.make_async_copy(w_hbm.at[plan.order[j]], w.at[j], w_sem.at[j])

    def matrix(j):
        return w[j].reshape(width, width)

    def arrive(j):
        if j < local:
            load(j).wait()

    def tick(t):
        if gather is not None:
            gather.tick(t, lambda i: keep(i).start())
            if vec_gather is not None:
                vec_gather.tick(t)

    pairs = width // PAIR
    row_ticks = plan.row_ticks

    @pl.when(s == 0)
    def _():
        for j in range(local):
            load(j).start()
        if gather is not None:
            greet(place.chip_partners() + place.z_partners())
            if vec_gather is not None:
                vec_gather.begin()
            gather.begin()
            lax.fori_loop(0, plan.lead, lambda t, carry: (tick(t), carry)[1], 0)
            for line in lines:
                line.advance(1)
            if vec_gather is not None:
                turned = vec_gather.whole[0].reshape(width, vec_gather.whole.shape[-1]).T
                for layer in range(2):
                    count = plan.vector_rows
                    targets[1 + layer][0:count, :] = turned[layer * count : (layer + 1) * count, :]
        for j in range(min(local, 3)):
            arrive(j)

    @pl.when(s < rows)
    def _():
        xin = x_ref[...].astype(low)
        bias[...] = segment_bias(segc_ref[0], segr_ref[0])
        q_ref[...] = (dot_nn(xin, matrix(0)) + vec_ref[0:1, :]).astype(low)
        k_ref[...] = dot_nn(xin, matrix(1)).astype(low)
        value = dot_nn(xin, matrix(2)) + vec_ref[1:2, :]
        v_ref[...] = value.astype(low)
        vt[...] = value.T.astype(low)
        masks = half_masks(low)

        def pair_step(p, carry):
            lanes = pl.ds(pl.multiple_of(p * PAIR, PAIR), PAIR)
            q_pair = q_ref[:, lanes] * jnp.asarray(HD ** (-0.5), low)
            k_pair = k_ref[:, lanes]
            for h in range(2):
                scores = dot_nt(k_pair, q_pair * masks[h]) + bias[...]
                largest = jnp.max(scores, axis=0, keepdims=True)
                expanded = jnp.exp(scores - largest)
                total = column_sum(expanded)
                here = pl.ds(pl.multiple_of(p * PAIR + h * HD, HD), HD)
                context = dot_nn(vt[here, :], expanded.astype(low)) * (1.0 / total)
                ctxt_ref[here, :] = context.astype(low)
                lse_ref[0, pl.ds(2 * p + h, 1), :] = largest + jnp.log(total)
            if gather is not None:
                spots = [n * pairs // row_ticks for n in range(row_ticks)]
                now, which = looked_up(spots, p)

                @pl.when(now)
                def _():
                    tick(plan.lead + s * row_ticks + which)
            return carry

        lax.fori_loop(0, pairs, pair_step, 0)

        @pl.when(s == 0)
        def _():
            if local > 3:
                arrive(3)
            for line in lines:
                line.advance(2)

        context = ctxt_ref[...].astype(full).T.astype(low)
        attended = dot_nn(context, matrix(3)) + vec_ref[2:3, :]
        unit, inverse = norm_parts(x_ref[...].astype(full) + attended)
        x1_ref[...] = unit
        inv1_ref[...] = inverse
        normed = unit * vec_ref[3:4, :] + vec_ref[4:5, :]
        here = pl.ds(pl.multiple_of(s * rows_now, rows_now), rows_now)
        acc[here, :] = normed + vec_ref[5 + inner : 6 + inner, :]
        normed = normed.astype(low)
        n1_ref[...] = normed
        n1_all[here, :] = normed

    tile = tokens // 4
    starts, firsts = plan.step_ticks(rows * row_ticks)

    @pl.when(s >= rows)
    def _():
        c = s - rows

        @pl.when(c == 0)
        def _():
            for j in range(4, local):
                arrive(j)
            for line in lines:
                line.advance(3)

        start = sum(n * (c == k).astype(jnp.int32) for k, n in enumerate(starts))
        first = sum(n * (c == k).astype(jnp.int32) for k, n in enumerate(firsts))
        if gather is not None:
            lax.fori_loop(start, first, lambda t, carry: (tick(t), carry)[1], 0)

        def token_step(i, carry):
            for half in range(2):
                here = pl.ds(pl.multiple_of((2 * i + half) * tile, tile), tile)
                value, slope = gelu_parts(dot_nn(n1_all[here, :], matrix(4 + 2 * c)) + vec_ref[pl.ds(5 + c, 1), :])
                active = value.astype(low)
                u_ref[here, :] = active
                gp_ref[here, :] = slope.astype(low)
                acc[here, :] += dot_nn(active, matrix(5 + 2 * c))
            return carry

        lax.fori_loop(0, 2, token_step, 0)
        tick(first)

        @pl.when(c == inner - 1)
        def _():
            base = 5 + inner

            def last(i, carry):
                here = pl.ds(pl.multiple_of(i * tile, tile), tile)
                unit, inverse = norm_parts(acc[here, :])
                x2_ref[here, :] = unit
                inv2_ref[here, :] = inverse
                out_ref[here, :] = (
                    unit * vec_ref[base + 1 : base + 2, :] + vec_ref[base + 2 : base + 3, :]
                ).astype(out_ref.dtype)
                return carry

            lax.fori_loop(0, 4, last, 0)
            if gather is not None:
                last_tick = gather.count - 1 + CLOSE
                lax.fori_loop(firsts[-1] + 1, last_tick + 1, lambda t, carry: (tick(t), carry)[1], 0)
                for line in lines:
                    line.advance(plan.z_count)
                for i in range(gather.count):
                    keep(i).wait()


class ForwardPlan:
    def __init__(self, inner, local, shards=None, vec_shard=None, vector_rows=0, lines=(), lead=0, row_ticks=0, z_count=1):
        self.inner, self.local, self.lead, self.row_ticks, self.z_count = inner, local, lead, row_ticks, z_count
        self.vector_rows = vector_rows
        self.order = [0, 1, 2, 3]
        for c in range(inner):
            self.order += [4 + c, 4 + inner + c]
        self.gathered, self.group = (0, 1) if shards is None else (shards.shape[0] * shards.shape[1], shards.shape[1])
        self.vectors = vec_shard is not None
        self.lines = [(first, count) for _, first, count in lines]
        self.line_at = int(self.gathered > 0) + int(self.vectors)
        self.line_target_at = int(self.gathered > 0) + 2 * int(self.vectors)
        self.arguments, self.argument_specs, self.results, self.result_specs, self.scratch = [], [], [], [], []
        shape = jax.ShapeDtypeStruct
        if self.gathered:
            width = 2 * shards.shape[3]
            self.arguments.append(shards)
            self.argument_specs.append(IN_VMEM)
            self.results.append(shape((self.gathered, 4, 2, width // 8, width), low))
            self.result_specs.append(ANYWHERE)
            self.scratch += gather_scratch(shards.shape[0], self.group, width // 8, width, z_count)
        if self.vectors:
            rows, lanes = vec_shard.shape[2:]
            self.arguments.append(vec_shard)
            self.argument_specs.append(IN_VMEM)
            for _ in range(2):
                self.results.append(shape((16, width), full))
                self.result_specs.append(pl.BlockSpec((16, width), lambda s: (0, 0)))
            self.scratch += gather_scratch(1, 1, width // 8, lanes, z_count, full)
        for basis, _, count in lines:
            self.arguments.append(basis)
            self.argument_specs.append(ANYWHERE)
            self.results.append(shape((z_count, count) + basis.shape[1:], low))
            self.result_specs.append(ANYWHERE)
        self.scratch += line_scratch(len(lines), z_count)
        if self.gathered:
            self.scratch.append(pltpu.SemaphoreType.DMA((self.gathered // self.group,)))
        if self.vectors:
            self.scratch.append(pltpu.VMEM((1, 4, 2, width // 8, lanes), full))

    def step_ticks(self, row_ticks):
        starts, firsts = [], []
        now = self.lead + row_ticks
        for c in range(self.inner):
            starts.append(now)
            needed = (5 + 2 * c - self.local) // self.group
            firsts.append(max(now, needed + CLOSE + 1) if self.gathered else now)
            now = firsts[-1] + 1
        return starts, firsts

    def split(self, refs):
        return split_refs(
            refs, 5, len(self.arguments), 13, len(self.results), 6, GATHER_REFS * bool(self.gathered),
            GATHER_REFS * self.vectors, 2 * bool(self.lines),
        )

    def vec_whole(self, refs):
        return refs[-1]


def scratch_tail(plan, refs):
    return refs[-2] if plan.vectors else refs[-1]


def forward_layer(hidden, seg_column, seg_row, vectors, weights, out_dtype, plan, identity=None):
    tokens, width = hidden.shape
    inner = plan.inner
    wide = width * inner
    rows = tokens // L
    heads = width // HD
    shape = jax.ShapeDtypeStruct

    def here(s):
        return jnp.minimum(s, rows - 1)

    def column(s):
        return jnp.maximum(s - rows, 0)

    def row_block(columns):
        return pl.BlockSpec((L, columns), lambda s: (here(s), 0))

    def whole(columns):
        return pl.BlockSpec((tokens, columns), lambda s: (0, 0), pipeline_mode=pl.Buffered(1))

    wide_block = pl.BlockSpec((tokens, width), lambda s: (0, column(s)))
    out_shape = (
        shape((tokens, width), low), shape((tokens, width), low), shape((tokens, width), low),
        shape((width, tokens), low), shape((rows, heads, L), full),
        shape((tokens, width), full), shape((tokens, 1), full), shape((tokens, width), low),
        shape((tokens, wide), low), shape((tokens, wide), low),
        shape((tokens, width), full), shape((tokens, 1), full), shape((tokens, width), out_dtype),
        *plan.results,
    )
    out_specs = (
        row_block(width), row_block(width), row_block(width),
        pl.BlockSpec((width, L), lambda s: (0, here(s))), pl.BlockSpec((1, heads, L), lambda s: (here(s), 0, 0)),
        row_block(width), row_block(1), row_block(width),
        wide_block, wide_block,
        whole(width), whole(1), whole(width),
        *plan.result_specs,
    )
    total = 4 + 2 * inner
    held = max(total, plan.local + plan.gathered)
    return pl.pallas_call(
        functools.partial(forward_kernel, plan),
        grid=(rows + inner,),
        out_shape=out_shape,
        in_specs=[
            row_block(width),
            pl.BlockSpec((1, L, 1), lambda s: (here(s), 0, 0)),
            pl.BlockSpec((1, 1, L), lambda s: (here(s), 0, 0)),
            pl.BlockSpec(vectors.shape, lambda s: (0, 0)),
            ANYWHERE,
            *plan.argument_specs,
        ],
        out_specs=out_specs,
        scratch_shapes=[
            pltpu.VMEM((held, 4, 2, width // 8, width), low),
            pltpu.VMEM((L, L), full),
            pltpu.VMEM((width, L), low),
            pltpu.VMEM((tokens, width), low),
            pltpu.VMEM((tokens, width), full),
            pltpu.SemaphoreType.DMA((total,)),
            *plan.scratch,
        ],
        compiler_params=pltpu.CompilerParams(
            dimension_semantics=("arbitrary",), vmem_limit_bytes=62 * MIB,
            collective_id=identity, has_side_effects=identity is not None,
        ),
        cost_estimate=pl.CostEstimate(
            flops=2 * tokens * width * width * total + 4 * tokens * L * width,
            bytes_accessed=40 * MIB,
            transcendentals=tokens * (L * heads + wide),
        ),
        name="layer_forward",
    )(hidden, seg_column, seg_row, vectors, weights.reshape(-1, 4, 2, width // 8, width), *plan.arguments)


WIDE_HEAD_TICKS, WIDE_STEP_TICKS = 2, 4


def wide_ready(own):
    return [WIDE_HEAD_TICKS + WIDE_STEP_TICKS * (n // 2) + 2 + n % 2 for n in range(own)]


def wide_back_kernel(plan, inner, *refs):
    inputs, sources, outputs, targets, scratch, sum_refs, line_refs = plan.split(refs, 11, 4, 11)
    up_hbm, x2_hbm, inv2_hbm, x1_hbm, inv1_hbm, n1_hbm, vec_ref, wup_ref, wdown_ref, u_ref, gp_ref = inputs
    dw_ref, dr1_ref, da_ref, dvec_ref = outputs
    n1t, dz, kept_dw, up_ref, x2_ref, inv2_ref, x1_ref, inv1_ref, n1_ref, tile_sem, load_sem = scratch
    dy, dn1 = da_ref, dr1_ref
    c = pl.program_id(0)
    steps = pl.num_programs(0)
    tokens, width = dn1.shape
    tile = tokens // 4
    base = 5 + inner
    side = Side(plan, sources, targets, sum_refs, line_refs, kept_dw)

    def tile_copies(i):
        rows = pl.ds(pl.multiple_of(i * tile, tile), tile)
        return [
            pltpu.make_async_copy(source.at[rows], target.at[rows], tile_sem.at[n, i])
            for n, (source, target) in enumerate(((up_hbm, up_ref), (x2_hbm, x2_ref), (inv2_hbm, inv2_ref)))
        ]

    late_copies = [
        pltpu.make_async_copy(source, target, load_sem.at[n])
        for n, (source, target) in enumerate(((n1_hbm, n1_ref), (x1_hbm, x1_ref), (inv1_hbm, inv1_ref)))
    ]

    @pl.when(c == 0)
    def _():
        for i in range(4):
            for copy in tile_copies(i):
                copy.start()
        for copy in late_copies:
            copy.start()

    side.enter(c == 0)

    @pl.when(c == 0)
    def _():
        gain = vec_ref[base + 1 : base + 2, :]

        def body(i, carry):
            for copy in tile_copies(i):
                copy.wait()
            gain_sum, shift_sum, bias_sum = carry
            rows = pl.ds(pl.multiple_of(i * tile, tile), tile)
            upstream = up_ref[rows, :].astype(full)
            unit = x2_ref[rows, :]
            back = norm_back(upstream, unit, inv2_ref[rows, :], gain)
            dn1[rows, :] = back
            branch = back.astype(low)
            dy[rows, :] = branch
            @pl.when(lax.rem(i, 2) == 1)
            def _():
                side.tick(lax.div(i, 2))

            return (
                gain_sum + column_sum(upstream * unit),
                shift_sum + column_sum(upstream),
                bias_sum + column_sum(branch.astype(full)),
            )

        zero = jnp.zeros((1, width), full)
        gain_sum, shift_sum, bias_sum = lax.fori_loop(0, 4, body, (zero, zero, zero))
        dvec_ref[...] = jnp.zeros(dvec_ref.shape, full)
        dvec_ref[base : base + 1, :] = bias_sum
        dvec_ref[base + 1 : base + 2, :] = gain_sum
        dvec_ref[base + 2 : base + 3, :] = shift_sum
        late_copies[0].wait()
        n1t[...] = n1_ref[...].astype(full).T.astype(low)

    first_tick = WIDE_HEAD_TICKS + WIDE_STEP_TICKS * c

    def token_step(i, carry):
        for half in range(2):
            rows = pl.ds(pl.multiple_of((2 * i + half) * tile, tile), tile)
            slope = gp_ref[rows, :].astype(full)
            piece = (dot_nt(dy[rows, :], wdown_ref[0]) * slope).astype(low)
            dz[rows, :] = piece
            dn1[rows, :] += dot_nt(piece, wup_ref[0])
            carry = carry + column_sum(piece.astype(full))
        side.tick(first_tick + i)
        return carry

    bias_sum = lax.fori_loop(0, 2, token_step, jnp.zeros((1, width), full))
    side.advance(c == 1, 2)
    side.advance(c == 3, 3)
    for j in range(inner):
        @pl.when(c == j)
        def _():
            dvec_ref[5 + j : 6 + j, :] = bias_sum

    def store(k, grad):
        if plan.own:
            @pl.when(2 * c + k < plan.own)
            def _():
                kept_dw[2 * c + k] = grad.reshape(kept_dw.shape[1:])

            @pl.when(2 * c + k >= plan.own)
            def _():
                dw_ref[k, 0] = grad
        else:
            dw_ref[k, 0] = grad

    store(0, dot_nn(n1t[...], dz[...]).astype(low))
    side.tick(first_tick + 2)
    store(1, dot_tn(u_ref[...], dy[...]).astype(low))
    side.tick(first_tick + 3)
    final_tick = WIDE_HEAD_TICKS + WIDE_STEP_TICKS * inner

    @pl.when(c == steps - 1)
    def _():
        for copy in late_copies[1:]:
            copy.wait()
        gain = vec_ref[3:4, :]

        def body(i, carry):
            gain_sum, shift_sum, bias_sum = carry
            rows = pl.ds(pl.multiple_of(i * tile, tile), tile)
            upstream = dn1[rows, :]
            unit = x1_ref[rows, :]
            back = norm_back(upstream, unit, inv1_ref[rows, :], gain)
            dr1_ref[rows, :] = back
            branch = back.astype(low)
            da_ref[rows, :] = branch
            @pl.when(lax.rem(i, 2) == 1)
            def _():
                side.tick(final_tick + lax.div(i, 2))

            return (
                gain_sum + column_sum(upstream * unit),
                shift_sum + column_sum(upstream),
                bias_sum + column_sum(branch.astype(full)),
            )

        zero = jnp.zeros((1, width), full)
        gain_sum, shift_sum, bias_sum = lax.fori_loop(0, 4, body, (zero, zero, zero))
        dvec_ref[2:3, :] = bias_sum
        dvec_ref[3:4, :] = gain_sum
        dvec_ref[4:5, :] = shift_sum

    side.leave(c == steps - 1, final_tick + 2)


def wide_back(upstream, kept, vectors, weights, places, plan, identity=None):
    x1, inv1, n1, u, gp, x2, inv2 = kept
    tokens, width = x1.shape
    up_start, down_start, stride = places
    inner = u.shape[1] // width
    shape = jax.ShapeDtypeStruct

    return pl.pallas_call(
        functools.partial(wide_back_kernel, plan, inner),
        grid=(inner,),
        out_shape=(
            shape((2, inner - plan.own // 2, width, width), low),
            shape((tokens, width), full), shape((tokens, width), low), shape((16, width), full),
            *plan.results,
        ),
        in_specs=[
            *[ANYWHERE] * 6,
            pl.BlockSpec(vectors.shape, lambda c: (0, 0), pipeline_mode=pl.Buffered(1)),
            pl.BlockSpec((1, width, width), lambda c: (up_start + stride * c, 0, 0)),
            pl.BlockSpec((1, width, width), lambda c: (down_start + stride * c, 0, 0)),
            pl.BlockSpec((tokens, width), lambda c: (0, c)),
            pl.BlockSpec((tokens, width), lambda c: (0, c)),
            *plan.argument_specs,
        ],
        out_specs=(
            pl.BlockSpec((2, 1, width, width), lambda c: (0, jnp.maximum(c - plan.own // 2, 0), 0, 0)),
            pl.BlockSpec((tokens, width), lambda c: (0, 0), pipeline_mode=pl.Buffered(1)),
            pl.BlockSpec((tokens, width), lambda c: (0, 0), pipeline_mode=pl.Buffered(1)),
            pl.BlockSpec((16, width), lambda c: (0, 0)),
            *plan.result_specs,
        ),
        scratch_shapes=[
            pltpu.VMEM((width, tokens), low),
            pltpu.VMEM((tokens, width), low),
            pltpu.VMEM((plan.own, 4, 2, width // 8, width) if plan.own else (8, 128), low),
            pltpu.VMEM((tokens, width), upstream.dtype),
            pltpu.VMEM((tokens, width), full),
            pltpu.VMEM((tokens, 1), full),
            pltpu.VMEM((tokens, width), full),
            pltpu.VMEM((tokens, 1), full),
            pltpu.VMEM((tokens, width), low),
            pltpu.SemaphoreType.DMA((3, 4)),
            pltpu.SemaphoreType.DMA((3,)),
            *plan.scratch,
        ],
        compiler_params=pltpu.CompilerParams(
            dimension_semantics=("arbitrary",), vmem_limit_bytes=60 * MIB,
            collective_id=identity, has_side_effects=identity is not None,
        ),
        cost_estimate=pl.CostEstimate(
            flops=8 * tokens * width * width * inner, bytes_accessed=50 * MIB, transcendentals=0
        ),
        name="wide_backward",
    )(upstream, x2, inv2, x1, inv1, n1, vectors, weights, weights, u, gp, *plan.arguments)


def attend_back_kernel(plan, *refs):
    inputs, sources, outputs, targets, scratch, sum_refs, line_refs = plan.split(refs, 11, 3, 14)
    da_hbm, dr1_ref, x_ref, q_ref, k_ref, v_ref, ctxt_hbm, lse_ref, segc_ref, segr_ref, w_hbm = inputs
    dw_ref, dx_ref, dvec_ref = outputs
    bias, dctx, kt, delta, dqt, xt, dq_all, dk_all, dv_all, dwo, da_ref, ctxt_ref, w_ref, load_sem = scratch
    r = pl.program_id(0)
    loads = [
        pltpu.make_async_copy(w_hbm.at[plan.start + 3], w_ref.at[3], load_sem.at[0]),
        pltpu.make_async_copy(da_hbm, da_ref, load_sem.at[1]),
        pltpu.make_async_copy(ctxt_hbm, ctxt_ref, load_sem.at[2]),
        pltpu.make_async_copy(w_hbm.at[pl.ds(plan.start, 3)], w_ref.at[pl.ds(0, 3)], load_sem.at[3]),
    ]

    @pl.when(r == 0)
    def _():
        for copy in loads:
            copy.start()

    side = Side(plan, sources, targets, sum_refs, line_refs, dwo)
    side.enter(r == 0)
    tokens, width = dr1_ref.shape
    pairs = width // PAIR
    ticks = pairs + 4

    def tick(n):
        side.tick(r * ticks + n)

    tick(0)
    here = pl.ds(pl.multiple_of(r * tokens, tokens), tokens)

    @pl.when(r == 0)
    def _():
        for copy in loads[:3]:
            copy.wait()
        grad = dot_nn(ctxt_ref[...], da_ref[...]).astype(low)
        if plan.own:
            dwo[0] = grad.reshape(dwo.shape[1:])
        else:
            dw_ref[3] = grad

    xt[:, here] = x_ref[...].astype(low).astype(full).T.astype(low)
    bias[...] = segment_bias(segc_ref[0], segr_ref[0])
    context_grad = dot_nt(da_ref[here, :], w_ref[3]).astype(low)
    dctx[...] = context_grad
    kt[...] = k_ref[...].astype(full).T.astype(low)
    products = context_grad.astype(full) * ctxt_ref[:, here].astype(full).T
    feature = lax.broadcasted_iota(jnp.int32, (16, width), 1)
    head = lax.broadcasted_iota(jnp.int32, (16, width), 0)
    member = ((feature >= head * HD) & (feature < (head + 1) * HD)).astype(full).astype(low)
    high = products.astype(low)
    rest = (products - high.astype(full)).astype(low)
    delta[...] = dot_nt(member, high) + dot_nt(member, rest)
    tick(1)
    masks = half_masks(low)
    scale = HD ** (-0.5)

    def pair_step(p, carry):
        lanes = pl.ds(pl.multiple_of(p * PAIR, PAIR), PAIR)
        q_pair = q_ref[:, lanes] * jnp.asarray(scale, low)
        k_pair = k_ref[:, lanes]
        v_pair = v_ref[:, lanes]
        g_pair = dctx[:, lanes]
        key_grad = jnp.zeros((tokens, PAIR), full)
        value_grad = jnp.zeros((tokens, PAIR), full)
        for h in range(2):
            q_half = q_pair * masks[h]
            g_half = g_pair * masks[h]
            scores = dot_nt(k_pair, q_half) + bias[...]
            attention = jnp.exp(scores - lse_ref[0, pl.ds(2 * p + h, 1), :])
            value_grad = value_grad + dot_nn(attention.astype(low), g_half)
            attention_grad = dot_nt(v_pair, g_half)
            score_grad = (attention * (attention_grad - delta[pl.ds(2 * p + h, 1), :])).astype(low)
            key_grad = key_grad + dot_nn(score_grad, q_half)
            rows = pl.ds(pl.multiple_of(p * PAIR + h * HD, HD), HD)
            dqt[rows, :] = dot_nn(kt[rows, :], score_grad) * scale
        dk_all[here, lanes] = key_grad.astype(low)
        dv_all[here, lanes] = value_grad.astype(low)
        tick(2 + p)
        side.advance((r == 0) & (p == 4), 2)
        side.advance((r == 1) & (p == 3), 3)
        return carry

    lax.fori_loop(0, pairs, pair_step, 0)
    tick(2 + pairs)

    @pl.when(r == 0)
    def _():
        loads[3].wait()

    query_grad = dqt[...].T.astype(low)
    dq_all[here, :] = query_grad
    key_grad = dk_all[here, :]
    value_grad = dv_all[here, :]
    dx_ref[...] = (
        dr1_ref[...]
        + dot_nt(query_grad, w_ref[0])
        + dot_nt(key_grad, w_ref[1])
        + dot_nt(value_grad, w_ref[2])
    )
    tick(3 + pairs)

    @pl.when(r == 0)
    def _():
        dvec_ref[...] = jnp.zeros(dvec_ref.shape, full)

    dvec_ref[0:1, :] += column_sum(query_grad.astype(full))
    dvec_ref[1:2, :] += column_sum(value_grad.astype(full))

    @pl.when(r == pl.num_programs(0) - 1)
    def _():
        for j, grad in enumerate((dq_all, dk_all, dv_all)):
            dw_ref[j] = dot_nn(xt[...], grad[...]).astype(low)
            side.tick(plan.rows * ticks + j)

    side.leave(r == pl.num_programs(0) - 1, plan.rows * ticks + 3)


def attend_back(da, dr1, hidden, kept, seg_column, seg_row, weights, start, plan, identity=None):
    q, k, v, ctxt, lse = kept
    tokens, width = da.shape
    rows = tokens // L
    heads = width // HD
    shape = jax.ShapeDtypeStruct
    plan.start, plan.rows = start, rows

    def row_block():
        return pl.BlockSpec((L, width), lambda r: (r, 0))

    return pl.pallas_call(
        functools.partial(attend_back_kernel, plan),
        grid=(rows,),
        out_shape=(
            shape((4 - plan.own, width, width), low), shape((tokens, width), full), shape((8, width), full),
            *plan.results,
        ),
        in_specs=[
            ANYWHERE,
            row_block(), row_block(), row_block(), row_block(), row_block(),
            ANYWHERE,
            pl.BlockSpec((1, heads, L), lambda r: (r, 0, 0)),
            pl.BlockSpec((1, L, 1), lambda r: (r, 0, 0)),
            pl.BlockSpec((1, 1, L), lambda r: (r, 0, 0)),
            ANYWHERE,
            *plan.argument_specs,
        ],
        out_specs=(
            pl.BlockSpec((4 - plan.own, width, width), lambda r: (0, 0, 0), pipeline_mode=pl.Buffered(1)),
            row_block(),
            pl.BlockSpec((8, width), lambda r: (0, 0)),
            *plan.result_specs,
        ),
        scratch_shapes=[
            pltpu.VMEM((L, L), full),
            pltpu.VMEM((L, width), low),
            pltpu.VMEM((width, L), low),
            pltpu.VMEM((16, L), full),
            pltpu.VMEM((width, L), full),
            pltpu.VMEM((width, tokens), low),
            pltpu.VMEM((tokens, width), low),
            pltpu.VMEM((tokens, width), low),
            pltpu.VMEM((tokens, width), low),
            pltpu.VMEM((1, 4, 2, width // 8, width) if plan.own else (8, 128), low),
            pltpu.VMEM((tokens, width), low),
            pltpu.VMEM((width, tokens), low),
            pltpu.VMEM((4, width, width), low),
            pltpu.SemaphoreType.DMA((4,)),
            *plan.scratch,
        ],
        compiler_params=pltpu.CompilerParams(
            dimension_semantics=("arbitrary",), vmem_limit_bytes=60 * MIB,
            collective_id=identity, has_side_effects=identity is not None,
        ),
        cost_estimate=pl.CostEstimate(
            flops=16 * tokens * width * width + 10 * tokens * L * width,
            bytes_accessed=30 * MIB,
            transcendentals=tokens * L * heads,
        ),
        name="attend_backward",
    )(da, dr1, hidden, q, k, v, ctxt, lse, seg_column, seg_row, weights, *plan.arguments)


def moments(rotated, first, second):
    first_new = beta_one * first + (1.0 - beta_one) * rotated
    second_new = beta_two * second + (1.0 - beta_two) * rotated * rotated
    direction = (
        first_new
        / (1.0 - beta_one**STEP)
        / (jnp.sqrt(second_new / (1.0 - beta_two**STEP)) + adam_epsilon)
    )
    return first_new, second_new, direction


def pack_lanes(piece):
    rows = piece.shape[0] // 2
    return jnp.concatenate([piece[:rows], piece[rows:]], axis=1)


def unpack_lanes(piece):
    columns = piece.shape[1] // 2
    return jnp.concatenate([piece[:, :columns], piece[:, columns:]], axis=0)


def optimizer_kernel(plan, *refs):
    spans = len(plan.spans)
    inputs, ready, dvecs, bases, lines_in, outputs, lines_out, scratch, sum_refs, vec_refs, line_refs = split_refs(
        refs, 6, plan.ready, plan.dvecs, plan.bases, spans, 5, spans, 21, SUM_REFS, SUM_REFS, 2 * bool(spans)
    )
    index_ref, place_ref, tail_hbm, first_hbm, second_hbm, blocks = inputs
    new_ref, low_ref, first_out, second_out, vec_out = outputs
    (store, left, right, first_in, second_in, g_out, g_in, t_out, t_in, e_out, e_in, w_out, w_in, vec_source,
     load_sem, g_sem, t_sem, e_sem, w_sem, left_sem, right_sem) = scratch
    slots, owners = g_in.shape[0], g_in.shape[1]
    z_count = t_in.shape[1]
    place = Place(z_count)
    dp, z = place.dp, place.z
    dps = [lax.rem(dp + d, owners) for d in range(owners)]
    count = blocks.shape[0]
    many = tail_hbm.shape[0]
    tail_times = [[many * stage + n for n in range(many)] for stage in range(5)]
    tail = BlockSum(place, [tail_hbm], sum_refs, tail_times)
    vec = BlockSum(place, [vec_source], vec_refs, [[many * stage + 1] for stage in range(5)])
    order = plan.free + [s for s in range(slots) if s not in plan.free]
    lines = line_gathers(place, plan.spans, lines_in, lines_out, line_refs, z_count)
    every = list(bases) + list(lines_out)
    late = [s for s in range(slots) if plan.left_map[s][0] >= len(bases)]

    def load(refs_map, target, sem, s):
        n, at = refs_map[s]
        return pltpu.make_async_copy(every[n].at[:, at], target.at[:, s], sem.at[s])

    def load_first(s):
        return pltpu.make_async_copy(first_hbm.at[s], first_in.at[s], load_sem.at[0, s])

    def load_second(s):
        return pltpu.make_async_copy(second_hbm.at[s], second_in.at[s], load_sem.at[1, s])

    for s in order:
        load(plan.right_map, right, right_sem, s).start()
        if s not in late:
            load(plan.left_map, left, left_sem, s).start()
        load_first(s).start()
        load_second(s).start()
    greet([(other, z) for other in dps[1:]] + place.z_partners())
    start = many
    for part in ready:
        store[start : start + part.shape[0]] = part[...]
        start += part.shape[0]
    store[0:many] = jnp.zeros((many,) + store.shape[1:], low)
    store[count] = jnp.zeros(store.shape[1:], low)
    rows = plan.vector_rows
    stacked = jnp.concatenate(
        [dvecs[0][0:2, :], dvecs[1][2:rows, :], dvecs[2][0:2, :], dvecs[3][2:rows, :],
         jnp.zeros((vec_source.shape[-1] - 2 * rows, blocks.shape[2]), full)], axis=0
    )
    vec_source[0] = stacked.T.reshape(vec_source.shape[1:])

    def g_copy(s, d):
        other = dps[d]
        return remote(g_out.at[s, d], g_in.at[s, dp], g_sem.at[0, s, d], g_sem.at[1, s, owners - d], (other, z))

    def t_copy(s, d):
        other = place.zs[d]
        return remote(t_out.at[s, d], t_in.at[s, z], t_sem.at[0, s, d], t_sem.at[1, s, z_count - d], (dp, other))

    def e_copy(s, d):
        other = place.zs[d]
        return remote(e_out.at[s, d], e_in.at[s, z], e_sem.at[0, s, d], e_sem.at[1, s, z_count - d], (dp, other))

    def w_copy(s, d):
        other = dps[d]
        return remote(
            w_out.at[s, other], w_in.at[s * owners + dp], w_sem.at[0, s, d], w_sem.at[1, s, owners - d], (other, z)
        )

    def send_out(s):
        for d in range(1, owners):
            g_out[s, d] = store[index_ref[s * owners + dps[d]]]
            g_copy(s, d).start()
        g_in[s, dp] = store[index_ref[s * owners + dp]]

    def turn(s):
        for d in range(1, owners):
            g_copy(s, d).wait()
        load(plan.right_map, right, right_sem, s).wait()
        grad = jnp.concatenate([unfold(g_in[s, c].astype(full)) for c in range(owners)], axis=0).astype(low)
        for d in range(1, z_count):
            t_out[s, d] = pack_lanes(dot_nt(right[place.zs[d], s], grad)).astype(low)
            t_copy(s, d).start()
        t_in[s, z] = pack_lanes(dot_nt(right[z, s], grad)).astype(low)

    def adapt(s):
        for d in range(1, z_count):
            t_copy(s, d).wait()
        load_first(s).wait()
        load_second(s).wait()
        load(plan.left_map, left, left_sem, s).wait()
        rotated = jnp.zeros(first_in.shape[1:], full)
        for f in range(z_count):
            rotated = rotated + dot_nn(unpack_lanes(t_in[s, f].astype(full)).astype(low), left[f, s])
        first_new, second_new, direction = moments(rotated, first_in[s], second_in[s])
        first_out[s] = first_new
        second_out[s] = second_new
        direction = direction.astype(low)
        for d in range(1, z_count):
            e_out[s, d] = pack_lanes(dot_nt(left[place.zs[d], s], direction)).astype(low)
            e_copy(s, d).start()
        e_in[s, z] = pack_lanes(dot_nt(left[z, s], direction)).astype(low)

    def step_back(s):
        for d in range(1, z_count):
            e_copy(s, d).wait()
        step = jnp.zeros((left.shape[2], left.shape[3]), full)
        for f in range(z_count):
            step = step + dot_nn(unpack_lanes(e_in[s, f].astype(full)).astype(low), right[f, s])
        share = step.shape[0] // owners
        for c in range(owners):
            w_out[s, c] = fold(step[c * share : (c + 1) * share]).astype(low)
        for d in range(1, owners):
            w_copy(s, d).start()
        w_in[s * owners + dp] = w_out[s, dp]

    def sums(stage):
        for t in range(many * stage, many * (stage + 1)):
            tail.tick(t)
            vec.tick(t)

    free = plan.free
    def advance(hop):
        for line in lines:
            line.advance(hop)

    sums(0)
    advance(1)
    for s in free:
        send_out(s)
    sums(1)
    for s in free:
        turn(s)
    sums(2)
    advance(2)
    for s in free:
        adapt(s)
    sums(3)
    sums(4)
    advance(3)
    for i in range(many):
        store[i] = tail.finish(i).astype(low)
    rest = order[len(free) :]
    for s in rest[:2]:
        send_out(s)
    for s in free:
        step_back(s)
    advance(z_count)
    for s in late:
        load(plan.left_map, left, left_sem, s).start()
    for k in range(len(rest) + 2):
        if k < len(rest):
            turn(rest[k])
            if k + 2 < len(rest):
                send_out(rest[k + 2])
        if 0 <= k - 1 < len(rest):
            adapt(rest[k - 1])
        if 0 <= k - 2 < len(rest):
            step_back(rest[k - 2])

    vec_out[...] = vec.finish(0)
    for s in range(slots):
        for d in range(1, owners):
            w_copy(s, d).wait()

    def block_step(b, carry):
        step = unfold(w_in[place_ref[b]].astype(full))
        block = blocks[b]
        new = block - matrix_rate * (step + weight_decay * block)
        new_ref[b] = new
        low_ref[b] = new.astype(low)
        return carry

    lax.fori_loop(0, count, block_step, 0)


class OptimizerPlan:
    def __init__(self, ready, dvecs, bases, spans, left_map, right_map, free, vector_rows):
        self.ready, self.dvecs, self.bases, self.spans = ready, dvecs, bases, spans
        self.left_map, self.right_map, self.free, self.vector_rows = left_map, right_map, free, vector_rows


def optimizer(
    index, places, tail, ready, dvecs, vector_rows, bases, lines, left_map, right_map, free, first, second, blocks,
    z_count, identity,
):
    slots, columns, width = first.shape
    owners = index.shape[0] // slots
    count, rows = blocks.shape[0], blocks.shape[1]
    span = bases[0].shape[2]
    lanes = 128
    shape = jax.ShapeDtypeStruct
    piece = (2 * rows, width // 2)
    tile = (span // 2, 2 * columns)
    smem = pl.BlockSpec(memory_space=pltpu.SMEM)
    spans = [(first_slot, amount) for _, first_slot, amount in lines]
    plan = OptimizerPlan(len(ready), len(dvecs), len(bases), spans, left_map, right_map, free, vector_rows)
    line_shapes = [shape((z_count, amount) + basis.shape[1:], low) for basis, _, amount in lines]
    return pl.pallas_call(
        functools.partial(optimizer_kernel, plan),
        out_shape=(
            shape(blocks.shape, full), shape(blocks.shape, low), shape(first.shape, full), shape(first.shape, full),
            shape((rows, lanes), full), *line_shapes,
        ),
        in_specs=[smem, smem, ANYWHERE, ANYWHERE, ANYWHERE, IN_VMEM]
        + [IN_VMEM] * (len(ready) + len(dvecs)) + [ANYWHERE] * (len(bases) + len(lines)),
        out_specs=(IN_VMEM,) * 5 + (ANYWHERE,) * len(lines),
        scratch_shapes=[
            pltpu.VMEM((count + 1,) + piece, low),
            pltpu.VMEM((z_count, slots, span, width), low),
            pltpu.VMEM((z_count, slots, columns, width), low),
            pltpu.VMEM((slots, columns, width), full),
            pltpu.VMEM((slots, columns, width), full),
            pltpu.VMEM((slots, owners) + piece, low),
            pltpu.VMEM((slots, owners) + piece, low),
            pltpu.VMEM((slots, z_count) + tile, low),
            pltpu.VMEM((slots, z_count) + tile, low),
            pltpu.VMEM((slots, z_count) + tile, low),
            pltpu.VMEM((slots, z_count) + tile, low),
            pltpu.VMEM((slots, owners) + piece, low),
            pltpu.VMEM((slots * owners,) + piece, low),
            pltpu.VMEM((1, owners // 2, 2, width // owners, lanes), full),
            pltpu.SemaphoreType.DMA((2, slots)),
            pltpu.SemaphoreType.DMA((2, slots, owners)),
            pltpu.SemaphoreType.DMA((2, slots, z_count)),
            pltpu.SemaphoreType.DMA((2, slots, z_count)),
            pltpu.SemaphoreType.DMA((2, slots, owners)),
            pltpu.SemaphoreType.DMA((slots,)),
            pltpu.SemaphoreType.DMA((slots,)),
            *sum_scratch(tail.shape[0], tail.shape[3], width, z_count),
            *sum_scratch(1, width // owners, lanes, z_count, full),
            *line_scratch(len(lines), z_count),
        ],
        compiler_params=pltpu.CompilerParams(
            vmem_limit_bytes=60 * MIB, collective_id=identity, has_side_effects=True
        ),
        cost_estimate=pl.CostEstimate(
            flops=8 * slots * span * width * width, bytes_accessed=40 * MIB, transcendentals=slots * width * columns
        ),
        name="optimizer",
    )(index, places, tail, first, second, blocks, *ready, *dvecs, *bases, *[basis for basis, _, _ in lines])


def slot_table(owner, slots, owner_rows):
    block_count = owner.shape[0]
    same_owner = owner[:, None] == owner[None, :]
    ordering = jnp.arange(block_count, dtype=jnp.int32)
    earlier = ordering[None, :] < ordering[:, None]
    ranking = jnp.sum(jnp.where(same_owner & earlier, 1, 0), axis=1).astype(jnp.int32)
    owner_match = owner[None, :] == jnp.arange(owner_rows, dtype=jnp.int32)[:, None]
    slot_match = ranking[None, :] == jnp.arange(slots, dtype=jnp.int32)[:, None]
    return jnp.where(slot_match[:, None, :] & owner_match[None, :, :], 1.0, 0.0).astype(full)


def scatter_sum(grads):
    blocks, width = grads.shape[0], grads.shape[2]
    cut = grads.reshape(blocks, lax.axis_size("dp"), -1, width).transpose(1, 0, 2, 3)
    outer = lax.psum_scatter(cut, "dp", scatter_dimension=0, tiled=False)
    blocks, rows, width = outer.shape
    count = lax.axis_size("fsdp")
    cut = outer.reshape(blocks, count, rows // count, width).transpose(1, 0, 2, 3)
    return lax.psum_scatter(cut, "fsdp", scatter_dimension=0, tiled=False)


def scatter_vectors(grads):
    rows, width = grads.shape
    count = lax.axis_size("dp") * lax.axis_size("fsdp")
    cut = grads.reshape(rows, count, width // count).transpose(1, 0, 2)
    return lax.psum_scatter(cut, ("dp", "fsdp"), scatter_dimension=0, tiled=False)


def gathering_program(
    tokens, segment, blocks, vectors, owner, left_basis, right_basis, rot_first, rot_second, cotangent, z_count
):
    layers, vector_rows = vectors.shape[:2]
    count, shard_rows, width = blocks.shape
    per_layer = count // layers
    inner = (per_layer - 4) // 2
    owners = lax.axis_size("dp")
    slots = rot_first.shape[0]
    part = width // owners
    lanes = 128
    seg_column, seg_row = segment[:, :, None], segment[:, None, :]

    order = [0, 1, 2, 3]
    for c in range(inner):
        order += [4 + c, 4 + inner + c]
    folded = blocks.astype(low).reshape(count, shard_rows, 2, width // 2).transpose(0, 2, 1, 3)
    folded = folded.reshape(count, 2 * shard_rows, width // 2)

    def pick(numbers):
        return jnp.stack([folded[j] for j in numbers]).reshape(len(numbers) // 2, 2, *folded.shape[1:])

    head = pick(order + [per_layer + j for j in order[:4]])
    rest = pick([per_layer + j for j in order[4:]])
    vec_shard = vectors.astype(low).astype(full).reshape(layers * vector_rows, shard_rows).T
    vec_shard = jnp.pad(vec_shard, ((0, 0), (0, lanes - layers * vector_rows)))[None, None]
    left_low = left_basis.reshape(slots, -1, width).astype(low)
    right_low = right_basis.transpose(0, 2, 1).astype(low)

    plan = ForwardPlan(
        inner, 0, head, vec_shard, vector_rows, [(right_low, 0, 2)], lead=5, row_ticks=1, z_count=z_count
    )
    empty_vec = jnp.zeros((16, width), full)
    results = forward_layer(tokens, seg_column, seg_row, empty_vec, jnp.zeros((1, width, width), low), full, plan, 6)
    kept_a = results[:12]
    hidden, weights_a, vec_a, vec_b, right_01 = results[12:]
    weights_a = weights_a.reshape(-1, width, width)
    plan = ForwardPlan(inner, 4, rest, lines=[(right_low, 2, 1)], lead=0, row_ticks=2, z_count=z_count)
    plan.order = [per_layer + j for j in range(4)]
    results = forward_layer(hidden, seg_column, seg_row, vec_b, weights_a, low, plan, 7)
    kept_b = results[:12]
    layer_out, weights_b, right_2 = results[12:]
    weights_b = weights_b.reshape(-1, width, width)

    def cut(grads):
        return grads.reshape(-1, owners // 2, 2, part, width)

    size = (part, width)
    own_b, own_a = 4, 3

    def left_over(own):
        return 2 * inner - own, own % 2

    plan = Plan(None, [(right_low, 3, 1)], z_count, own_b, size, wide_ready(own_b))
    dw_wide, dr1, da, dvec_wide_b, wide_sum_b, right_3 = wide_back(
        cotangent, kept_b[5:], vec_b, weights_b, (0, 1, 2), plan, 1
    )
    pending, skip = left_over(own_b)
    plan = Plan(cut(dw_wide), [(right_low, 4, 1), (left_low, 3, 1)], z_count, 1, size, list(range(pending + 1)), skip)
    dw_attend, upstream, dvec_attend_b, attend_sum_b, right_4, left_3 = attend_back(
        da, dr1, hidden, kept_b[:5], seg_column, seg_row, weights_a, per_layer, plan, 2
    )
    plan = Plan(
        cut(dw_attend), [(left_low, 4, 1), (left_low, 0, 1)], z_count, own_a, size, [0, 1, 2] + wide_ready(own_a)
    )
    dw_wide, dr1, da, dvec_wide_a, wide_sum_a, left_4, left_0 = wide_back(
        upstream, kept_a[5:], vec_a, weights_a, (4, 5, 2), plan, 3
    )
    pending, skip = left_over(own_a)
    plan = Plan(cut(dw_wide), [(left_low, 1, 1)], z_count, 1, size, list(range(pending + 1)), skip)
    dw_attend, upstream, dvec_attend_a, attend_sum_a, left_1 = attend_back(
        da, dr1, tokens, kept_a[:5], seg_column, seg_row, weights_a, 0, plan, 5
    )

    three = list(range(3))

    def early(own):
        return [4 + n // 2 + inner * (n % 2) for n in range(own)]

    def late(own):
        return [4 + c + inner * k for k in range(2) for c in range(inner) if 2 * c + k >= own] + [3]

    held_order = three + late(own_a) + [per_layer + j for j in three] + early(own_a)
    held_order += [per_layer + j for j in late(own_b) + early(own_b)]
    rank = jnp.asarray([held_order.index(j) for j in range(count)], jnp.int32)
    table = slot_table(owner, slots, owners).reshape(slots * owners, count)
    held = jnp.sum(table, axis=1)
    index = jnp.where(held > 0, jnp.sum(table * rank, axis=1), count).astype(jnp.int32)
    places = jnp.sum(table * jnp.arange(slots * owners, dtype=jnp.int32)[:, None], axis=0).astype(jnp.int32)
    bases = (right_01, right_2, right_3, right_4, left_0, left_1, left_3, left_4)
    right_map = [(0, 0), (0, 1), (1, 0), (2, 0), (3, 0)]
    left_map = [(4, 0), (5, 0), (8, 0), (6, 0), (7, 0)]
    free = list(range(3, slots))
    new_blocks, new_low, first_new, second_new, vec_sum, _ = optimizer(
        index, places, cut(dw_attend), (attend_sum_a, wide_sum_a, attend_sum_b, wide_sum_b),
        (dvec_attend_a, dvec_wide_a, dvec_attend_b, dvec_wide_b), vector_rows, bases, [(left_low, 2, 1)], left_map, right_map, free,
        rot_first.transpose(0, 2, 1), rot_second.transpose(0, 2, 1), blocks, z_count, 4,
    )
    first_new, second_new = first_new.transpose(0, 2, 1), second_new.transpose(0, 2, 1)
    vector_grad = vec_sum[:, : layers * vector_rows].T.reshape(layers, vector_rows, shard_rows)
    return layer_out, upstream, new_blocks, new_low, first_new, second_new, vector_grad


def plain_program(
    tokens, segment, blocks, vectors, owner, left_basis, right_basis, rot_first, rot_second, cotangent
):
    layers, vector_rows = vectors.shape[:2]
    per_layer = blocks.shape[0] // layers
    inner = (per_layer - 4) // 2
    width = blocks.shape[2]
    owner_rows = lax.axis_size("dp")
    slots = rot_first.shape[0]
    selector = slot_table(owner, slots, owner_rows)
    vector_parts = lax.all_gather(vectors.astype(low), ("dp", "fsdp"), axis=0, tiled=False)
    vector_full = vector_parts.transpose(1, 2, 0, 3).reshape(layers, vector_rows, width).astype(full)
    blocks_low, vector_full = lax.optimization_barrier((blocks.astype(low), vector_full))

    seg_column = segment[:, :, None]
    seg_row = segment[:, None, :]
    state = tokens
    kept = []
    for layer_index in range(layers):
        start = per_layer * layer_index
        weights = lax.all_gather(blocks_low[start : start + per_layer], ("dp", "fsdp"), axis=1, tiled=True)
        out_dtype = low if layer_index == layers - 1 else full
        results = forward_layer(
            state, seg_column, seg_row, vector_full[layer_index], weights, out_dtype, ForwardPlan(inner, per_layer)
        )
        kept.append((state, weights, results[:5], results[5:12]))
        state = results[12]
    layer_out = state
    upstream = cotangent
    right_low = lax.all_gather(right_basis.astype(low), "fsdp", axis=2, tiled=True)
    block_shards = [None] * layers
    vector_shards = [None] * layers
    for layer_index in reversed(range(layers)):
        hidden, weights, attend_kept, wide_kept = kept[layer_index]
        dw_wide, dr1, da, dvec_wide = wide_back(
            upstream, wide_kept, vector_full[layer_index], weights, (4, 4 + inner, 1), Plan()
        )
        wide_shard = scatter_sum(dw_wide.reshape(-1, width, width))
        dw_attend, upstream, dvec_attend = attend_back(
            da, dr1, hidden, attend_kept, seg_column, seg_row, weights, 0, Plan()
        )
        dvec = jnp.concatenate([dvec_attend[:2], dvec_wide[2:vector_rows]], axis=0)
        block_shards[layer_index] = jnp.concatenate([scatter_sum(dw_attend), wide_shard], axis=0)
        vector_shards[layer_index] = scatter_vectors(dvec)
    vector_grad = jnp.stack(vector_shards)
    block_grad = jnp.concatenate(block_shards, axis=0)
    outgoing = jnp.einsum("srk,kid->srid", selector.astype(low), block_grad, preferred_element_type=full)
    incoming = lax.all_to_all(outgoing.astype(low), "dp", split_axis=1, concat_axis=1, tiled=True)
    owned = incoming.reshape(slots, -1, width)
    turned = jnp.einsum("sik,skj->sij", owned, right_low, preferred_element_type=full).astype(low)
    left_rows = left_basis.reshape(slots, -1, width).astype(low)
    partial_sums = jnp.einsum("sra,srb->sab", left_rows, turned, preferred_element_type=full)
    rotated = lax.psum_scatter(
        partial_sums.astype(low), "fsdp", scatter_dimension=2, tiled=True
    ).astype(full)
    first_new, second_new, direction = moments(rotated, rot_first, rot_second)
    direction_full = lax.all_gather(direction.astype(low), "fsdp", axis=2, tiled=True)
    back_right = jnp.einsum("sab,scb->sac", direction_full, right_low, preferred_element_type=full)
    step_rows = jnp.einsum(
        "sia,sac->sic", left_rows, back_right.astype(low), preferred_element_type=full
    )
    returned = lax.all_to_all(
        step_rows.reshape(slots, owner_rows, -1, width).astype(low),
        "dp",
        split_axis=1,
        concat_axis=1,
        tiled=True,
    )
    step_shard = jnp.einsum("srk,srid->kid", selector.astype(low), returned, preferred_element_type=full)
    new_blocks = blocks - matrix_rate * (step_shard + weight_decay * blocks)
    return layer_out, upstream, new_blocks, new_blocks.astype(low), first_new, second_new, vector_grad


def shards(
    tokens,
    segment,
    blocks,
    vectors,
    owner,
    left_basis,
    right_basis,
    rot_first,
    rot_second,
    vec_first,
    vec_second,
    cotangent,
):
    operands = (
        tokens, segment, blocks, vectors, owner, left_basis, right_basis, rot_first, rot_second, cotangent
    )
    z_count = lax.axis_size("fsdp")
    if lax.axis_size("dp") == 8 and z_count == 4:
        results = gathering_program(*operands, z_count)
    else:
        results = plain_program(*operands)
    layer_out, upstream, new_blocks, new_low, first_new, second_new, vector_grad = results
    vector_first = beta_one * vec_first + (1.0 - beta_one) * vector_grad
    vector_second = beta_two * vec_second + (1.0 - beta_two) * vector_grad * vector_grad
    vector_step = (
        vector_first
        / (1.0 - beta_one**STEP)
        / (jnp.sqrt(vector_second / (1.0 - beta_two**STEP)) + adam_epsilon)
    )
    vector_new = vectors - vector_rate * (vector_step + weight_decay * vectors)
    return (
        layer_out,
        upstream,
        new_blocks,
        new_low,
        first_new,
        second_new,
        vector_first,
        vector_second,
        vector_new,
    )


def solution(mesh):
    return jax.shard_map(
        shards,
        mesh=mesh,
        in_specs=(
            P(("dp", "fsdp"), None),
            P(("dp", "fsdp"), None),
            P(None, ("dp", "fsdp"), None),
            P(None, None, ("dp", "fsdp")),
            P(),
            P("dp", None, "fsdp", None),
            P("dp", None, "fsdp"),
            P("dp", None, "fsdp"),
            P("dp", None, "fsdp"),
            P(None, None, ("dp", "fsdp")),
            P(None, None, ("dp", "fsdp")),
            P(("dp", "fsdp"), None),
        ),
        out_specs=(
            P(("dp", "fsdp"), None),
            P(("dp", "fsdp"), None),
            P(None, ("dp", "fsdp"), None),
            P(None, ("dp", "fsdp"), None),
            P("dp", None, "fsdp"),
            P("dp", None, "fsdp"),
            P(None, None, ("dp", "fsdp")),
            P(None, None, ("dp", "fsdp")),
            P(None, None, ("dp", "fsdp")),
        ),
        check_vma=False,
    )
```

```python
import functools

import jax
import jax.numpy as jnp
from jax import lax
from jax.experimental import pallas as pl
from jax.experimental.pallas import tpu as pltpu
from jax.sharding import PartitionSpec as P

H = 12
HD = 64
L = 512
STEP = 5
PAIR = 2 * HD
MIB = 1 << 20

beta_one = 0.5
beta_two = 0.5
adam_epsilon = 1e-08
norm_epsilon = 1e-06
matrix_rate = 0.03
vector_rate = 0.2
weight_decay = 0.01
masked_score = -1e30
low = jnp.bfloat16
full = jnp.float32


def dot_nn(a, b):
    return lax.dot_general(a, b, (((1,), (0,)), ((), ())), preferred_element_type=full)


def dot_nt(a, b):
    return lax.dot_general(a, b, (((1,), (1,)), ((), ())), preferred_element_type=full)


def dot_tn(a, b):
    return lax.dot_general(a, b, (((0,), (0,)), ((), ())), preferred_element_type=full)


def gelu_parts(z):
    size = jnp.abs(z) * 0.7071067811865476
    t = 1.0 / (1.0 + 0.3275911 * size)
    bell = jnp.exp(-0.5 * z * z)
    poly = ((((1.061405429 * t - 1.453152027) * t + 1.421413741) * t - 0.284496736) * t + 0.254829592) * t
    half_tail = 0.5 * poly * bell
    phi = jnp.where(z >= 0, 1.0 - half_tail, half_tail)
    return z * phi, phi + z * bell * 0.3989422804014327


def norm_parts(residual):
    average = jnp.mean(residual, axis=-1, keepdims=True)
    centered = residual - average
    inverse = lax.rsqrt(jnp.mean(centered * centered, axis=-1, keepdims=True) + norm_epsilon)
    return centered * inverse, inverse


def norm_back(upstream, unit, inverse, gain):
    scaled = upstream * gain
    return inverse * (
        scaled
        - jnp.mean(scaled, axis=-1, keepdims=True)
        - unit * jnp.mean(scaled * unit, axis=-1, keepdims=True)
    )


def column_sum(values):
    return jnp.sum(values, axis=0, keepdims=True)


def half_masks(dtype):
    lane = lax.broadcasted_iota(jnp.int32, (1, PAIR), 1)
    first = (lane < HD).astype(full)
    return first.astype(dtype), (1.0 - first).astype(dtype)


def segment_bias(seg_column, seg_row):
    return jnp.where(seg_column == seg_row, 0.0, masked_score)


class Place:
    def __init__(self, z_count):
        self.dp, self.z = lax.axis_index("dp"), lax.axis_index("fsdp")
        self.core, self.spot = lax.rem(self.dp, 2), lax.div(self.dp, 2)
        x_step = 1 - 2 * lax.rem(self.spot, 2)
        y_step = 2 - 4 * lax.div(self.spot, 2)
        self.spot_a = self.spot + (1 - self.core) * x_step + self.core * y_step
        self.spot_b = self.spot + self.core * x_step + (1 - self.core) * y_step
        self.spot_ab = self.spot + x_step + y_step
        self.sibling = (self.dp + 1 - 2 * self.core, self.z)
        self.near_a = (2 * self.spot_a + self.core, self.z)
        self.near_b = (2 * self.spot_b + self.core, self.z)
        self.z_count = z_count
        self.zs = [lax.rem(self.z + d, z_count) for d in range(z_count)]
        self.has_up, self.has_down = self.z < z_count - 1, self.z > 0
        self.middle = self.has_up & self.has_down
        self.across = lax.rem(self.z + 2, z_count)
        self.beside = jnp.where(self.z < 2, 1 - self.z, 5 - self.z)

    def line_sends(self, d):
        return {1: self.has_up, 2: self.z >= 0, 3: self.has_down}[d]

    def line_receives(self, d):
        return {1: self.has_down, 2: self.z >= 0, 3: self.has_up}[d]

    def chip_partners(self):
        return [self.sibling, self.near_a, self.near_b]

    def z_partners(self):
        return [(self.dp, other) for other in self.zs[1:]]


def greet(partners):
    barrier = pltpu.get_barrier_semaphore()
    for device in partners:
        pl.semaphore_signal(barrier, inc=1, device_id=device, device_id_type=pl.DeviceIdType.MESH)
    pl.semaphore_wait(barrier, len(partners))


def remote(source, target, send, receive, device):
    return pltpu.make_async_remote_copy(
        src_ref=source,
        dst_ref=target,
        send_sem=send,
        recv_sem=receive,
        device_id=device,
        device_id_type=pl.DeviceIdType.MESH,
    )


def fold(piece):
    half = piece.shape[1] // 2
    return jnp.concatenate([piece[:, :half], piece[:, half:]], axis=0)


def unfold(piece):
    rows = piece.shape[0] // 2
    return jnp.concatenate([piece[:rows], piece[rows:]], axis=1)


def looked_up(ticks, t):
    now = functools.reduce(jnp.logical_or, [t == tick for tick in ticks])
    which = sum(n * (t == tick).astype(jnp.int32) for n, tick in enumerate(ticks))
    return now, which


def run_due(stages, t):
    for ticks, stage in stages:
        if isinstance(t, int):
            if t in ticks:
                stage(ticks.index(t))
            continue
        now, block = looked_up(ticks, t)

        @pl.when(now)
        def _():
            stage(block)


def sum_times(ready):
    opens, cores, seconds = [], [], []
    for tick in ready:
        opens.append(max(tick, opens[-1] + 1) if opens else tick)
        cores.append(max(opens[-1] + 1, cores[-1] + 1) if cores else opens[-1] + 1)
        seconds.append(max(cores[-1] + 3, seconds[-1] + 3) if seconds else cores[-1] + 3)
    thirds = [tick + 2 for tick in seconds]
    return opens, cores, seconds, thirds, [tick + 2 for tick in thirds]


ANNOUNCE, FORWARD, FIRST, SECOND, CLOSE = -2, -1, 1, 2, 3


def sum_scratch(count, part, width, z_count, kind=low):
    piece = (2 * part // z_count, width // 2) if kind == low else (part // z_count, width)
    return [
        pltpu.VMEM((count, 4, part, width), kind),
        pltpu.VMEM((count, 4, part, width), kind),
        pltpu.VMEM((count, 2, part, width), kind),
        pltpu.VMEM((count, part, width), kind),
        pltpu.VMEM((count, z_count) + piece, kind),
        pltpu.VMEM((count, z_count) + piece, kind),
        pltpu.VMEM((count,) + piece, kind),
        pltpu.SemaphoreType.DMA((count,)),
        pltpu.SemaphoreType.DMA((count, 2)),
        pltpu.SemaphoreType.DMA((count, 2, 2)),
        pltpu.SemaphoreType.DMA((count, 2)),
        pltpu.SemaphoreType.DMA((count, 2, z_count)),
        pltpu.SemaphoreType.DMA((count, 2)),
    ]


SUM_REFS = 13


class BlockSum:
    def __init__(self, place, sources, refs, times):
        self.place, self.sources, self.times = place, sources, times
        (self.own, self.c, self.b, self.a, self.zs, self.zr, self.far,
         self.own_sem, self.c_sem, self.b_sem, self.a_sem, self.z_sem, self.far_sem) = refs
        self.count = self.c.shape[0]
        self.kind = self.c.dtype
        self.z_count = self.zs.shape[1]

    def load(self, i, block):
        return pltpu.make_async_copy(block.at[:, self.place.core], self.own.at[i], self.own_sem.at[i])

    def core_copy(self, i, block):
        return remote(
            block.at[:, 1 - self.place.core], self.c.at[i], self.c_sem.at[i, 0], self.c_sem.at[i, 1], self.place.sibling
        )

    def second_copy(self, i, k):
        chunk = self.place.spot_b if k == 0 else self.place.spot_ab
        return remote(
            self.c.at[i, chunk], self.b.at[i, k], self.b_sem.at[i, 0, k], self.b_sem.at[i, 1, k], self.place.near_b
        )

    def third_copy(self, i):
        return remote(
            self.c.at[i, self.place.spot_a], self.a.at[i], self.a_sem.at[i, 0], self.a_sem.at[i, 1], self.place.near_a
        )

    def z_copy(self, i, d):
        other = self.place.zs[d]
        return remote(
            self.zs.at[i, other], self.zr.at[i, self.place.z], self.z_sem.at[i, 0, d],
            self.z_sem.at[i, 1, self.z_count - d], (self.place.dp, other),
        )

    def open(self, i):
        first = 0
        for source in self.sources:
            count = source.shape[0]

            @pl.when((i >= first) & (i < first + count))
            def _():
                block = source.at[jnp.clip(i - first, 0, count - 1)]
                self.core_copy(i, block).start()
                self.load(i, block).start()

            first += count

    def after_core(self, i):
        block = self.sources[0].at[0]
        self.core_copy(i, block).wait()
        self.load(i, block).wait()

        def add(k, carry):
            self.c[i, k] = (self.c[i, k].astype(full) + self.own[i, k].astype(full)).astype(self.kind)
            return carry

        lax.fori_loop(0, 4, add, 0)
        self.second_copy(i, 0).start()
        self.second_copy(i, 1).start()

    def after_second(self, i):
        other, spot = self.place.spot_a, self.place.spot
        self.second_copy(i, 1).wait()
        self.c[i, other] = (self.c[i, other].astype(full) + self.b[i, 1].astype(full)).astype(self.kind)
        self.third_copy(i).start()
        self.second_copy(i, 0).wait()
        self.c[i, spot] = (self.c[i, spot].astype(full) + self.b[i, 0].astype(full)).astype(self.kind)

    def after_third(self, i):
        self.third_copy(i).wait()
        total = self.c[i, self.place.spot].astype(full) + self.a[i].astype(full)
        rows = total.shape[0] // self.z_count
        for k in range(self.z_count):
            piece = total[k * rows : (k + 1) * rows]
            self.zs[i, k] = fold(piece).astype(low) if self.kind == low else piece
        place = self.place
        for d in (1, 3):
            @pl.when(place.line_sends(d))
            def _():
                self.z_copy(i, d).start()

        @pl.when(jnp.logical_not(place.middle))
        def _():
            self.z_copy(i, 2).start()
            self.far_copy(i).start()
            opposite = self.z_count - 1 - place.z
            self.zr[i, opposite] = jnp.zeros(self.zr.shape[2:], self.kind)

    def far_copy(self, i):
        place = self.place
        return remote(
            self.zs.at[i, self.z_count - 1 - place.z], self.far.at[i], self.far_sem.at[i, 0], self.far_sem.at[i, 1],
            (place.dp, place.beside),
        )

    def relay(self, i):
        @pl.when(self.place.middle)
        def _():
            self.far_copy(i).wait_recv()
            across = self.place.across
            self.zs[i, across] = (self.zs[i, across].astype(full) + self.far[i].astype(full)).astype(self.kind)
            self.z_copy(i, 2).start()

    def finish(self, i):
        for d in range(1, self.z_count):
            @pl.when(self.place.line_sends(d))
            def _():
                self.z_copy(i, d).wait_send()

            @pl.when(self.place.line_receives(d))
            def _():
                self.z_copy(i, d).wait_recv()

        @pl.when(jnp.logical_not(self.place.middle))
        def _():
            self.far_copy(i).wait_send()

        total = self.zs[i, self.place.z].astype(full)
        for d in range(1, self.z_count):
            total = total + self.zr[i, self.place.zs[d]].astype(full)
        return total

    def tick(self, t):
        stages = (self.relay, self.after_third, self.after_second, self.after_core, self.open)
        run_due(list(zip(self.times[::-1], stages)), t)

    @property
    def last(self):
        return self.times[4][-1]


class LineGather:
    def __init__(self, place, source, target, first, local_sem, sem, z_count):
        self.place = place
        self.source = source.at[pl.ds(first, target.shape[1])]
        self.target, self.local_sem, self.sem, self.z_count = target, local_sem, sem, z_count

    def hop_copy(self, hop, way):
        dp, z = self.place.dp, self.place.z
        if way == 0:
            piece, other, coming = z - hop + 1, z + 1, z - hop
            sends = (piece >= 0) & (other < self.z_count)
            receives = coming >= 0
        else:
            piece, other, coming = z + hop - 1, z - 1, z + hop
            sends = (piece < self.z_count) & (other >= 0)
            receives = coming < self.z_count
        piece = jnp.clip(piece, 0, self.z_count - 1)
        other = jnp.clip(other, 0, self.z_count - 1)
        source = self.source if hop == 1 else self.target.at[piece]
        copy = remote(source, self.target.at[piece], self.sem.at[way, 0, hop - 1], self.sem.at[way, 1, hop - 1], (dp, other))
        return copy, sends, receives

    def local(self):
        return pltpu.make_async_copy(self.source, self.target.at[self.place.z], self.local_sem)

    def start(self, hop):
        if hop == 1:
            self.local().start()
        for way in range(2):
            copy, sends, _ = self.hop_copy(hop, way)

            @pl.when(sends)
            def _():
                copy.start()

    def wait(self, hop):
        if hop == 1:
            self.local().wait()
        for way in range(2):
            copy, sends, receives = self.hop_copy(hop, way)

            @pl.when(sends)
            def _():
                copy.wait_send()

            @pl.when(receives)
            def _():
                copy.wait_recv()

    def advance(self, hop):
        if hop > 1:
            self.wait(hop - 1)
        if hop < self.z_count:
            self.start(hop)


def gather_scratch(count, group, rows, width, z_count, kind=low):
    piece = (2 * rows // z_count, width // 2) if kind == low else (rows // z_count, width)
    return [
        pltpu.VMEM((count, z_count, group) + piece, kind),
        pltpu.SemaphoreType.DMA((count, 2, z_count)),
        pltpu.SemaphoreType.DMA((count, 2)),
        pltpu.SemaphoreType.DMA((count, 2, 2)),
        pltpu.SemaphoreType.DMA((count, 2)),
        pltpu.SemaphoreType.DMA((count, 2)),
    ]


GATHER_REFS = 6


class BlockGather:
    def __init__(self, place, source, whole, base, refs):
        self.place, self.source, self.whole, self.base = place, source, whole, base
        self.zr, self.z_sem, self.a_sem, self.b_sem, self.c_sem, self.far_sem = refs
        self.count, self.z_count, self.group = self.zr.shape[:3]

    def blocks(self, i):
        return pl.ds(self.base + self.group * i, self.group)

    def z_copy(self, i, d):
        place = self.place
        return remote(
            self.source.at[i], self.zr.at[i, place.z], self.z_sem.at[i, 0, d], self.z_sem.at[i, 1, self.z_count - d],
            (place.dp, place.zs[d]),
        )

    def chunk(self, i, spot):
        return self.whole.at[self.blocks(i), spot, self.place.core]

    def first_copy(self, i):
        chunk = self.chunk(i, self.place.spot)
        return remote(chunk, chunk, self.a_sem.at[i, 0], self.a_sem.at[i, 1], self.place.near_a)

    def second_copy(self, i, k):
        chunk = self.chunk(i, self.place.spot if k == 0 else self.place.spot_a)
        return remote(chunk, chunk, self.b_sem.at[i, 0, k], self.b_sem.at[i, 1, k], self.place.near_b)

    def core_copy(self, i):
        chunks = self.whole.at[self.blocks(i), :, self.place.core]
        return remote(chunks, chunks, self.c_sem.at[i, 0], self.c_sem.at[i, 1], self.place.sibling)

    def far_copy(self, i):
        place = self.place
        piece = self.zr.at[i, place.across]
        return remote(piece, piece, self.far_sem.at[i, 0], self.far_sem.at[i, 1], (place.dp, place.beside))

    def announce(self, i):
        for d in range(1, self.z_count):
            @pl.when(self.place.line_sends(d))
            def _():
                self.z_copy(i, d).start()

        self.zr[i, self.place.z] = self.source[i]

    def forward(self, i):
        @pl.when(self.place.middle)
        def _():
            self.z_copy(i, 2).wait_recv()
            self.far_copy(i).start()

    def begin(self):
        for i in range(min(-ANNOUNCE, self.count)):
            self.announce(i)

    def open(self, i):
        place = self.place
        for d in range(1, self.z_count):
            @pl.when(place.line_sends(d))
            def _():
                self.z_copy(i, d).wait_send()

        for d in (1, 3):
            @pl.when(place.line_receives(d))
            def _():
                self.z_copy(i, d).wait_recv()

        @pl.when(place.middle)
        def _():
            self.far_copy(i).wait_send()

        @pl.when(jnp.logical_not(place.middle))
        def _():
            self.z_copy(i, 2).wait_recv()
            self.far_copy(i).wait_recv()

        for n in range(self.group):
            pieces = [self.zr[i, k, n].astype(full) for k in range(self.z_count)]
            if self.zr.dtype == low:
                pieces = [unfold(piece) for piece in pieces]
            whole = jnp.concatenate(pieces, axis=0).astype(self.whole.dtype)
            self.whole[self.base + self.group * i + n, place.spot, place.core] = whole
        self.first_copy(i).start()
        self.second_copy(i, 0).start()

    def after_first(self, i):
        self.first_copy(i).wait()
        self.second_copy(i, 1).start()

    def after_second(self, i):
        self.second_copy(i, 0).wait()
        self.second_copy(i, 1).wait()
        self.core_copy(i).start()

    def close(self, i):
        self.core_copy(i).wait()

    def tick(self, t, done=None):
        def close(i):
            self.close(i)
            if done is not None:
                done(i)

        @pl.when(t == 0)
        def _():
            for i in range(min(-FORWARD, self.count)):
                self.forward(i)

        stages = (
            (SECOND, self.after_second), (FIRST, self.after_first), (0, self.open), (FORWARD, self.forward),
            (ANNOUNCE, self.announce), (CLOSE, close),
        )
        for late, stage in stages:
            @pl.when((t >= max(late, 0)) & (t - late < self.count))
            def _():
                stage(t - late)


def split_refs(refs, *counts):
    result, start = [], 0
    for count in counts:
        result.append(refs[start : start + count])
        start += count
    return result


class Side:
    def __init__(self, plan, sources, targets, sum_refs, line_refs, own=None):
        self.plan = plan
        sums = plan.sums
        blocks = [source.at[pl.ds(plan.skip, source.shape[0] - plan.skip)] for source in sources[:sums]]
        blocks += [own] if plan.own else []
        self.place = Place(plan.z_count) if plan.active else None
        self.sum = BlockSum(self.place, blocks, sum_refs, plan.times) if plan.total else None
        self.result = targets[0] if plan.total else None
        self.lines = line_gathers(self.place, plan.lines, sources[sums:], targets[bool(plan.total) :], line_refs, plan.z_count)

    def enter(self, now):
        if not self.plan.active:
            return

        @pl.when(now)
        def _():
            greet((self.place.chip_partners() if self.plan.total else []) + self.place.z_partners())
            for line in self.lines:
                line.advance(1)

    def tick(self, t):
        if self.plan.total:
            self.sum.tick(t)

    def leave(self, now, ticks):
        if not self.plan.active:
            return

        @pl.when(now)
        def _():
            if self.plan.total:
                if self.sum.last >= ticks:
                    lax.fori_loop(ticks, self.sum.last + 1, lambda t, carry: (self.tick(t), carry)[1], 0)
                for i in range(self.sum.count):
                    self.result[i] = self.sum.finish(i).astype(low)
            for line in self.lines:
                line.advance(self.plan.z_count)

    def advance(self, now, hop):
        if self.lines and hop < self.plan.z_count:
            @pl.when(now)
            def _():
                for line in self.lines:
                    line.advance(hop)


class Plan:
    def __init__(self, pending=None, lines=(), z_count=1, own=0, size=None, ready=(), skip=0):
        self.z_count = z_count
        self.sums = int(pending is not None)
        self.own, self.skip = own, skip
        self.total = own + (pending.shape[0] - skip if self.sums else 0)
        self.times = sum_times(ready) if self.total else None
        self.lines = [(first, count) for _, first, count in lines]
        self.active = bool(self.total or lines)
        self.arguments, self.results, self.result_specs, self.scratch = [], [], [], []
        if self.sums:
            self.arguments.append(pending)
        if self.total:
            part, width = size
            self.results.append(jax.ShapeDtypeStruct((self.total, 2 * part // z_count, width // 2), low))
            self.result_specs.append(
                pl.BlockSpec(self.results[0].shape, lambda i: (0, 0, 0), pipeline_mode=pl.Buffered(1))
            )
            self.scratch += sum_scratch(self.total, part, width, z_count)
        for basis, _, count in lines:
            self.arguments.append(basis)
            self.results.append(jax.ShapeDtypeStruct((z_count, count) + basis.shape[1:], low))
            self.result_specs.append(ANYWHERE)
        self.scratch += line_scratch(len(lines), z_count)
        self.argument_specs = [ANYWHERE] * len(self.arguments)

    def split(self, refs, inputs, outputs, scratch):
        count = len(self.lines)
        return split_refs(
            refs, inputs, self.sums + count, outputs, bool(self.total) + count, scratch,
            SUM_REFS * bool(self.total), 2 * bool(self.lines),
        )


def line_scratch(count, z_count):
    if not count:
        return []
    return [pltpu.SemaphoreType.DMA((count,)), pltpu.SemaphoreType.DMA((count, 2, 2, z_count - 1))]


def line_gathers(place, spans, sources, targets, refs, z_count):
    return [
        LineGather(place, source, target, first, refs[0].at[n], refs[1].at[n], z_count)
        for n, (source, target, (first, _)) in enumerate(zip(sources, targets, spans))
    ]


ANYWHERE = pl.BlockSpec(memory_space=pl.ANY)
IN_VMEM = pl.BlockSpec(memory_space=pltpu.VMEM)


def forward_kernel(plan, *refs):
    inputs, sources, outputs, targets, scratch, gather_refs, vec_refs, line_refs = plan.split(refs)
    x_ref, segc_ref, segr_ref, vec_ref, w_hbm = inputs
    (q_ref, k_ref, v_ref, ctxt_ref, lse_ref, x1_ref, inv1_ref, n1_ref, u_ref, gp_ref, x2_ref, inv2_ref,
     out_ref) = outputs
    w, bias, vt, n1_all, acc, w_sem = scratch
    s = pl.program_id(0)
    tokens, width = acc.shape
    rows_now = x_ref.shape[0]
    rows = tokens // rows_now
    inner = plan.inner
    local = plan.local
    gather = vec_gather = None
    place = Place(plan.z_count) if plan.gathered else None
    if plan.gathered:
        w_out, out_sem = targets[0], scratch_tail(plan, refs)
        gather = BlockGather(place, sources[0], w, local, gather_refs)
        if plan.vectors:
            vec_gather = BlockGather(place, sources[1], plan.vec_whole(refs), 0, vec_refs)
            vec_ref = targets[1]
    lines = line_gathers(place, plan.lines, sources[plan.line_at :], targets[plan.line_target_at :], line_refs, plan.z_count)

    def keep(i):
        group = gather.group
        return pltpu.make_async_copy(w.at[gather.blocks(i)], w_out.at[pl.ds(group * i, group)], out_sem.at[i])

    def load(j):
        return pltpu.make_async_copy(w_hbm.at[plan.order[j]], w.at[j], w_sem.at[j])

    def matrix(j):
        return w[j].reshape(width, width)

    def arrive(j):
        if j < local:
            load(j).wait()

    def tick(t):
        if gather is not None:
            gather.tick(t, lambda i: keep(i).start())
            if vec_gather is not None:
                vec_gather.tick(t)

    pairs = width // PAIR

    @pl.when(s == 0)
    def _():
        for j in range(local):
            load(j).start()
        if gather is not None:
            greet(place.chip_partners() + place.z_partners())
            if vec_gather is not None:
                vec_gather.begin()
            gather.begin()
        for j in range(min(local, 3)):
            arrive(j)

    def run_ticks(start, stop):
        if gather is not None:
            lax.fori_loop(start, stop, lambda t, carry: (tick(t), carry)[1], 0)

    def ready():
        for line in lines:
            line.advance(1)
        if vec_gather is not None:
            turned = vec_gather.whole[0].reshape(width, vec_gather.whole.shape[-1]).T
            for layer in range(2):
                count = plan.vector_rows
                targets[1 + layer][0:count, :] = turned[layer * count : (layer + 1) * count, :]

    def project():
        xin = x_ref[...].astype(low)
        bias[...] = segment_bias(segc_ref[0], segr_ref[0])
        q_ref[...] = (dot_nn(xin, matrix(0)) + vec_ref[0:1, :]).astype(low)
        k_ref[...] = dot_nn(xin, matrix(1)).astype(low)
        value = dot_nn(xin, matrix(2)) + vec_ref[1:2, :]
        v_ref[...] = value.astype(low)
        vt[...] = value.T.astype(low)

    def pair_step(p):
        masks = half_masks(low)
        lanes = pl.ds(pl.multiple_of(p * PAIR, PAIR), PAIR)
        q_pair = q_ref[:, lanes] * jnp.asarray(HD ** (-0.5), low)
        k_pair = k_ref[:, lanes]
        for h in range(2):
            scores = dot_nt(k_pair, q_pair * masks[h]) + bias[...]
            largest = jnp.max(scores, axis=0, keepdims=True)
            expanded = jnp.exp(scores - largest)
            total = column_sum(expanded)
            here = pl.ds(pl.multiple_of(p * PAIR + h * HD, HD), HD)
            context = dot_nn(vt[here, :], expanded.astype(low)) * (1.0 / total)
            ctxt_ref[here, :] = context.astype(low)
            lse_ref[0, pl.ds(2 * p + h, 1), :] = largest + jnp.log(total)

    def close_row():
        @pl.when(s == 0)
        def _():
            if local > 3:
                arrive(3)
            for line in lines:
                line.advance(2)

        context = ctxt_ref[...].astype(full).T.astype(low)
        attended = dot_nn(context, matrix(3)) + vec_ref[2:3, :]
        unit, inverse = norm_parts(x_ref[...].astype(full) + attended)
        x1_ref[...] = unit
        inv1_ref[...] = inverse
        normed = unit * vec_ref[3:4, :] + vec_ref[4:5, :]
        here = pl.ds(pl.multiple_of(s * rows_now, rows_now), rows_now)
        acc[here, :] = normed + vec_ref[5 + inner : 6 + inner, :]
        normed = normed.astype(low)
        n1_ref[...] = normed
        n1_all[here, :] = normed

    @pl.when(s < rows)
    def _():
        def position(n, carry):
            if gather is not None:
                here, which = looked_up(plan.row_positions, n)
                before = plan.lead + s * len(plan.row_positions) + which
                opening = (s == 0) & (n == 0)
                start = jnp.where(opening, 0, before)
                stop = jnp.where(opening, plan.lead, jnp.where(here, before + 1, before))
                run_ticks(start, stop)

                @pl.when(opening)
                def _():
                    ready()

            @pl.when(n == 0)
            def _():
                project()

            @pl.when((n >= 1) & (n <= pairs))
            def _():
                pair_step(n - 1)

            @pl.when(n == pairs + 1)
            def _():
                close_row()

            return carry

        lax.fori_loop(0, pairs + 2, position, 0)

    tile = tokens // 4
    starts, stops = plan.step_ticks(rows)

    @pl.when(s >= rows)
    def _():
        c = s - rows

        @pl.when(c == 0)
        def _():
            for j in range(4, local):
                arrive(j)
            for line in lines:
                line.advance(3)

        def token_step(i, carry):
            for half in range(2):
                here = pl.ds(pl.multiple_of((2 * i + half) * tile, tile), tile)
                value, slope = gelu_parts(dot_nn(n1_all[here, :], matrix(4 + 2 * c)) + vec_ref[pl.ds(5 + c, 1), :])
                active = value.astype(low)
                u_ref[here, :] = active
                gp_ref[here, :] = slope.astype(low)
                acc[here, :] += dot_nn(active, matrix(5 + 2 * c))
            return carry

        lax.fori_loop(0, 2, token_step, 0)

        @pl.when(c == inner - 1)
        def _():
            base = 5 + inner

            def last(i, carry):
                here = pl.ds(pl.multiple_of(i * tile, tile), tile)
                unit, inverse = norm_parts(acc[here, :])
                x2_ref[here, :] = unit
                inv2_ref[here, :] = inverse
                out_ref[here, :] = (
                    unit * vec_ref[base + 1 : base + 2, :] + vec_ref[base + 2 : base + 3, :]
                ).astype(out_ref.dtype)
                return carry

            lax.fori_loop(0, 4, last, 0)

        run_ticks(
            sum(n * (c == k).astype(jnp.int32) for k, n in enumerate(starts)),
            sum(n * (c == k).astype(jnp.int32) for k, n in enumerate(stops)),
        )

        @pl.when(c == inner - 1)
        def _():
            if gather is not None:
                for line in lines:
                    line.advance(plan.z_count)
                for i in range(gather.count):
                    keep(i).wait()


class ForwardPlan:
    def __init__(self, inner, local, shards=None, vec_shard=None, vector_rows=0, lines=(), lead=0, row_positions=(), z_count=1):
        self.inner, self.local, self.lead, self.row_positions, self.z_count = inner, local, lead, row_positions, z_count
        self.vector_rows = vector_rows
        self.order = [0, 1, 2, 3]
        for c in range(inner):
            self.order += [4 + c, 4 + inner + c]
        self.gathered, self.group = (0, 1) if shards is None else (shards.shape[0] * shards.shape[1], shards.shape[1])
        self.vectors = vec_shard is not None
        self.lines = [(first, count) for _, first, count in lines]
        self.line_at = int(self.gathered > 0) + int(self.vectors)
        self.line_target_at = int(self.gathered > 0) + 2 * int(self.vectors)
        self.arguments, self.argument_specs, self.results, self.result_specs, self.scratch = [], [], [], [], []
        shape = jax.ShapeDtypeStruct
        if self.gathered:
            width = 2 * shards.shape[3]
            self.arguments.append(shards)
            self.argument_specs.append(IN_VMEM)
            self.results.append(shape((self.gathered, 4, 2, width // 8, width), low))
            self.result_specs.append(ANYWHERE)
            self.scratch += gather_scratch(shards.shape[0], self.group, width // 8, width, z_count)
        if self.vectors:
            rows, lanes = vec_shard.shape[2:]
            self.arguments.append(vec_shard)
            self.argument_specs.append(IN_VMEM)
            for _ in range(2):
                self.results.append(shape((16, width), full))
                self.result_specs.append(pl.BlockSpec((16, width), lambda s: (0, 0)))
            self.scratch += gather_scratch(1, 1, width // 8, lanes, z_count, full)
        for basis, _, count in lines:
            self.arguments.append(basis)
            self.argument_specs.append(ANYWHERE)
            self.results.append(shape((z_count, count) + basis.shape[1:], low))
            self.result_specs.append(ANYWHERE)
        self.scratch += line_scratch(len(lines), z_count)
        if self.gathered:
            self.scratch.append(pltpu.SemaphoreType.DMA((self.gathered // self.group,)))
        if self.vectors:
            self.scratch.append(pltpu.VMEM((1, 4, 2, width // 8, lanes), full))

    def step_ticks(self, rows):
        now, starts, stops = self.lead + rows * len(self.row_positions), [], []
        for c in range(self.inner):
            starts.append(now)
            if not self.gathered:
                stops.append(now)
                continue
            if c == self.inner - 1:
                now = max(now, self.gathered // self.group + CLOSE)
            else:
                now = max(now + 1, (5 + 2 * (c + 1) - self.local) // self.group + CLOSE + 1)
            stops.append(now)
        return starts, stops

    def split(self, refs):
        return split_refs(
            refs, 5, len(self.arguments), 13, len(self.results), 6, GATHER_REFS * bool(self.gathered),
            GATHER_REFS * self.vectors, 2 * bool(self.lines),
        )

    def vec_whole(self, refs):
        return refs[-1]


def scratch_tail(plan, refs):
    return refs[-2] if plan.vectors else refs[-1]


def forward_layer(hidden, seg_column, seg_row, vectors, weights, out_dtype, plan, identity=None):
    tokens, width = hidden.shape
    inner = plan.inner
    wide = width * inner
    rows = tokens // L
    heads = width // HD
    shape = jax.ShapeDtypeStruct

    def here(s):
        return jnp.minimum(s, rows - 1)

    def column(s):
        return jnp.maximum(s - rows, 0)

    def row_block(columns):
        return pl.BlockSpec((L, columns), lambda s: (here(s), 0))

    def whole(columns):
        return pl.BlockSpec((tokens, columns), lambda s: (0, 0), pipeline_mode=pl.Buffered(1))

    wide_block = pl.BlockSpec((tokens, width), lambda s: (0, column(s)))
    out_shape = (
        shape((tokens, width), low), shape((tokens, width), low), shape((tokens, width), low),
        shape((width, tokens), low), shape((rows, heads, L), full),
        shape((tokens, width), full), shape((tokens, 1), full), shape((tokens, width), low),
        shape((tokens, wide), low), shape((tokens, wide), low),
        shape((tokens, width), full), shape((tokens, 1), full), shape((tokens, width), out_dtype),
        *plan.results,
    )
    out_specs = (
        row_block(width), row_block(width), row_block(width),
        pl.BlockSpec((width, L), lambda s: (0, here(s))), pl.BlockSpec((1, heads, L), lambda s: (here(s), 0, 0)),
        row_block(width), row_block(1), row_block(width),
        wide_block, wide_block,
        whole(width), whole(1), whole(width),
        *plan.result_specs,
    )
    total = 4 + 2 * inner
    held = max(total, plan.local + plan.gathered)
    return pl.pallas_call(
        functools.partial(forward_kernel, plan),
        grid=(rows + inner,),
        out_shape=out_shape,
        in_specs=[
            row_block(width),
            pl.BlockSpec((1, L, 1), lambda s: (here(s), 0, 0)),
            pl.BlockSpec((1, 1, L), lambda s: (here(s), 0, 0)),
            pl.BlockSpec(vectors.shape, lambda s: (0, 0)),
            ANYWHERE,
            *plan.argument_specs,
        ],
        out_specs=out_specs,
        scratch_shapes=[
            pltpu.VMEM((held, 4, 2, width // 8, width), low),
            pltpu.VMEM((L, L), full),
            pltpu.VMEM((width, L), low),
            pltpu.VMEM((tokens, width), low),
            pltpu.VMEM((tokens, width), full),
            pltpu.SemaphoreType.DMA((total,)),
            *plan.scratch,
        ],
        compiler_params=pltpu.CompilerParams(
            dimension_semantics=("arbitrary",), vmem_limit_bytes=62 * MIB,
            collective_id=identity, has_side_effects=identity is not None,
        ),
        cost_estimate=pl.CostEstimate(
            flops=2 * tokens * width * width * total + 4 * tokens * L * width,
            bytes_accessed=40 * MIB,
            transcendentals=tokens * (L * heads + wide),
        ),
        name="layer_forward",
    )(hidden, seg_column, seg_row, vectors, weights.reshape(-1, 4, 2, width // 8, width), *plan.arguments)


WIDE_STEP_TICKS = 5


def wide_ready(own):
    return [WIDE_STEP_TICKS * (n // 2) + 4 + n % 2 for n in range(own)]


def wide_back_kernel(plan, inner, *refs):
    inputs, sources, outputs, targets, scratch, sum_refs, line_refs = plan.split(refs, 11, 4, 11)
    up_hbm, x2_hbm, inv2_hbm, x1_hbm, inv1_hbm, n1_hbm, vec_ref, wup_ref, wdown_ref, u_ref, gp_ref = inputs
    dw_ref, dr1_ref, da_ref, dvec_ref = outputs
    n1t, dz, kept_dw, up_ref, x2_ref, inv2_ref, x1_ref, inv1_ref, n1_ref, tile_sem, load_sem = scratch
    dy, dn1 = da_ref, dr1_ref
    c = pl.program_id(0)
    steps = pl.num_programs(0)
    tokens, width = dn1.shape
    tile = tokens // 4
    base = 5 + inner
    side = Side(plan, sources, targets, sum_refs, line_refs, kept_dw)

    def tile_copies(i):
        rows = pl.ds(pl.multiple_of(i * tile, tile), tile)
        return [
            pltpu.make_async_copy(source.at[rows], target.at[rows], tile_sem.at[n, i])
            for n, (source, target) in enumerate(((up_hbm, up_ref), (x2_hbm, x2_ref), (inv2_hbm, inv2_ref)))
        ]

    late_copies = [
        pltpu.make_async_copy(source, target, load_sem.at[n])
        for n, (source, target) in enumerate(((n1_hbm, n1_ref), (x1_hbm, x1_ref), (inv1_hbm, inv1_ref)))
    ]

    @pl.when(c == 0)
    def _():
        for i in range(4):
            for copy in tile_copies(i):
                copy.start()
        for copy in late_copies:
            copy.start()

    side.enter(c == 0)

    def prepare():
        gain = vec_ref[base + 1 : base + 2, :]

        def body(i, carry):
            for copy in tile_copies(i):
                copy.wait()
            gain_sum, shift_sum, bias_sum = carry
            rows = pl.ds(pl.multiple_of(i * tile, tile), tile)
            upstream = up_ref[rows, :].astype(full)
            unit = x2_ref[rows, :]
            back = norm_back(upstream, unit, inv2_ref[rows, :], gain)
            dn1[rows, :] = back
            branch = back.astype(low)
            dy[rows, :] = branch
            return (
                gain_sum + column_sum(upstream * unit),
                shift_sum + column_sum(upstream),
                bias_sum + column_sum(branch.astype(full)),
            )

        zero = jnp.zeros((1, width), full)
        gain_sum, shift_sum, bias_sum = lax.fori_loop(0, 4, body, (zero, zero, zero))
        dvec_ref[...] = jnp.zeros(dvec_ref.shape, full)
        dvec_ref[base : base + 1, :] = bias_sum
        dvec_ref[base + 1 : base + 2, :] = gain_sum
        dvec_ref[base + 2 : base + 3, :] = shift_sum
        late_copies[0].wait()
        n1t[...] = n1_ref[...].astype(full).T.astype(low)

    def token_pair(i):
        bias_sum = jnp.zeros((1, width), full)
        for half in range(2):
            rows = pl.ds(pl.multiple_of((2 * i + half) * tile, tile), tile)
            slope = gp_ref[rows, :].astype(full)
            piece = (dot_nt(dy[rows, :], wdown_ref[0]) * slope).astype(low)
            dz[rows, :] = piece
            dn1[rows, :] += dot_nt(piece, wup_ref[0])
            bias_sum = bias_sum + column_sum(piece.astype(full))
        dvec_ref[pl.ds(5 + c, 1), :] += bias_sum

    def store(k, product):
        if plan.own:
            @pl.when(2 * c + k < plan.own)
            def _():
                kept_dw[2 * c + k] = product().reshape(kept_dw.shape[1:])

            @pl.when(2 * c + k >= plan.own)
            def _():
                dw_ref[k, 0] = product()
        else:
            dw_ref[k, 0] = product()

    def position(n, carry):
        side.tick(WIDE_STEP_TICKS * c + n)
        side.advance((c == 1) & (n == 1), 2)
        side.advance((c == 2) & (n == 4), 3)

        @pl.when((n == 0) & (c == 0))
        def _():
            prepare()

        @pl.when((n == 1) | (n == 2))
        def _():
            token_pair(n - 1)

        @pl.when(n == 3)
        def _():
            store(0, lambda: dot_nn(n1t[...], dz[...]).astype(low))

        @pl.when(n == 4)
        def _():
            store(1, lambda: dot_tn(u_ref[...], dy[...]).astype(low))

        return carry

    lax.fori_loop(0, WIDE_STEP_TICKS, position, 0)
    @pl.when(c == steps - 1)
    def _():
        for copy in late_copies[1:]:
            copy.wait()
        gain = vec_ref[3:4, :]

        def body(i, carry):
            gain_sum, shift_sum, bias_sum = carry
            rows = pl.ds(pl.multiple_of(i * tile, tile), tile)
            upstream = dn1[rows, :]
            unit = x1_ref[rows, :]
            back = norm_back(upstream, unit, inv1_ref[rows, :], gain)
            dr1_ref[rows, :] = back
            branch = back.astype(low)
            da_ref[rows, :] = branch
            return (
                gain_sum + column_sum(upstream * unit),
                shift_sum + column_sum(upstream),
                bias_sum + column_sum(branch.astype(full)),
            )

        zero = jnp.zeros((1, width), full)
        gain_sum, shift_sum, bias_sum = lax.fori_loop(0, 4, body, (zero, zero, zero))
        dvec_ref[2:3, :] = bias_sum
        dvec_ref[3:4, :] = gain_sum
        dvec_ref[4:5, :] = shift_sum

    side.leave(c == steps - 1, WIDE_STEP_TICKS * inner)


def wide_back(upstream, kept, vectors, weights, places, plan, identity=None):
    x1, inv1, n1, u, gp, x2, inv2 = kept
    tokens, width = x1.shape
    up_start, down_start, stride = places
    inner = u.shape[1] // width
    shape = jax.ShapeDtypeStruct

    return pl.pallas_call(
        functools.partial(wide_back_kernel, plan, inner),
        grid=(inner,),
        out_shape=(
            shape((2, inner - plan.own // 2, width, width), low),
            shape((tokens, width), full), shape((tokens, width), low), shape((16, width), full),
            *plan.results,
        ),
        in_specs=[
            *[ANYWHERE] * 6,
            pl.BlockSpec(vectors.shape, lambda c: (0, 0), pipeline_mode=pl.Buffered(1)),
            pl.BlockSpec((1, width, width), lambda c: (up_start + stride * c, 0, 0)),
            pl.BlockSpec((1, width, width), lambda c: (down_start + stride * c, 0, 0)),
            pl.BlockSpec((tokens, width), lambda c: (0, c)),
            pl.BlockSpec((tokens, width), lambda c: (0, c)),
            *plan.argument_specs,
        ],
        out_specs=(
            pl.BlockSpec((2, 1, width, width), lambda c: (0, jnp.maximum(c - plan.own // 2, 0), 0, 0)),
            pl.BlockSpec((tokens, width), lambda c: (0, 0), pipeline_mode=pl.Buffered(1)),
            pl.BlockSpec((tokens, width), lambda c: (0, 0), pipeline_mode=pl.Buffered(1)),
            pl.BlockSpec((16, width), lambda c: (0, 0)),
            *plan.result_specs,
        ),
        scratch_shapes=[
            pltpu.VMEM((width, tokens), low),
            pltpu.VMEM((tokens, width), low),
            pltpu.VMEM((plan.own, 4, 2, width // 8, width) if plan.own else (8, 128), low),
            pltpu.VMEM((tokens, width), upstream.dtype),
            pltpu.VMEM((tokens, width), full),
            pltpu.VMEM((tokens, 1), full),
            pltpu.VMEM((tokens, width), full),
            pltpu.VMEM((tokens, 1), full),
            pltpu.VMEM((tokens, width), low),
            pltpu.SemaphoreType.DMA((3, 4)),
            pltpu.SemaphoreType.DMA((3,)),
            *plan.scratch,
        ],
        compiler_params=pltpu.CompilerParams(
            dimension_semantics=("arbitrary",), vmem_limit_bytes=60 * MIB,
            collective_id=identity, has_side_effects=identity is not None,
        ),
        cost_estimate=pl.CostEstimate(
            flops=8 * tokens * width * width * inner, bytes_accessed=50 * MIB, transcendentals=0
        ),
        name="wide_backward",
    )(upstream, x2, inv2, x1, inv1, n1, vectors, weights, weights, u, gp, *plan.arguments)


def attend_back_kernel(plan, *refs):
    inputs, sources, outputs, targets, scratch, sum_refs, line_refs = plan.split(refs, 11, 3, 12)
    da_hbm, dr1_ref, x_ref, q_ref, k_ref, v_ref, ctxt_hbm, lse_ref, segc_ref, segr_ref, w_hbm = inputs
    dw_ref, dx_ref, dvec_ref = outputs
    bias, dctx, kt, delta, dqt, xt, grads, dwo, da_ref, ctxt_ref, w_ref, load_sem = scratch
    r = pl.program_id(0)
    loads = [
        pltpu.make_async_copy(w_hbm.at[plan.start + 3], w_ref.at[3], load_sem.at[0]),
        pltpu.make_async_copy(da_hbm, da_ref, load_sem.at[1]),
        pltpu.make_async_copy(ctxt_hbm, ctxt_ref, load_sem.at[2]),
        pltpu.make_async_copy(w_hbm.at[pl.ds(plan.start, 3)], w_ref.at[pl.ds(0, 3)], load_sem.at[3]),
    ]

    @pl.when(r == 0)
    def _():
        for copy in loads:
            copy.start()

    side = Side(plan, sources, targets, sum_refs, line_refs, dwo)
    side.enter(r == 0)
    tokens, width = dr1_ref.shape
    pairs = width // PAIR
    ticks = pairs + 5
    here = pl.ds(pl.multiple_of(r * tokens, tokens), tokens)
    masks = half_masks(low)
    scale = HD ** (-0.5)
    last_row = pl.num_programs(0) - 1

    def prepare():
        @pl.when(r == 0)
        def _():
            for copy in loads[:3]:
                copy.wait()
            grad = dot_nn(ctxt_ref[...], da_ref[...]).astype(low)
            if plan.own:
                dwo[0] = grad.reshape(dwo.shape[1:])
            else:
                dw_ref[3] = grad
            dvec_ref[...] = jnp.zeros(dvec_ref.shape, full)

        xt[:, here] = x_ref[...].astype(low).astype(full).T.astype(low)
        bias[...] = segment_bias(segc_ref[0], segr_ref[0])
        context_grad = dot_nt(da_ref[here, :], w_ref[3]).astype(low)
        dctx[...] = context_grad
        kt[...] = k_ref[...].astype(full).T.astype(low)
        products = context_grad.astype(full) * ctxt_ref[:, here].astype(full).T
        feature = lax.broadcasted_iota(jnp.int32, (16, width), 1)
        head = lax.broadcasted_iota(jnp.int32, (16, width), 0)
        member = ((feature >= head * HD) & (feature < (head + 1) * HD)).astype(full).astype(low)
        high = products.astype(low)
        rest = (products - high.astype(full)).astype(low)
        delta[...] = dot_nt(member, high) + dot_nt(member, rest)

    def pair_step(p):
        lanes = pl.ds(pl.multiple_of(p * PAIR, PAIR), PAIR)
        q_pair = q_ref[:, lanes] * jnp.asarray(scale, low)
        k_pair = k_ref[:, lanes]
        v_pair = v_ref[:, lanes]
        g_pair = dctx[:, lanes]
        key_grad = jnp.zeros((tokens, PAIR), full)
        value_grad = jnp.zeros((tokens, PAIR), full)
        for h in range(2):
            q_half = q_pair * masks[h]
            g_half = g_pair * masks[h]
            scores = dot_nt(k_pair, q_half) + bias[...]
            attention = jnp.exp(scores - lse_ref[0, pl.ds(2 * p + h, 1), :])
            value_grad = value_grad + dot_nn(attention.astype(low), g_half)
            attention_grad = dot_nt(v_pair, g_half)
            score_grad = (attention * (attention_grad - delta[pl.ds(2 * p + h, 1), :])).astype(low)
            key_grad = key_grad + dot_nn(score_grad, q_half)
            rows = pl.ds(pl.multiple_of(p * PAIR + h * HD, HD), HD)
            dqt[rows, :] = dot_nn(kt[rows, :], score_grad) * scale
        grads[1, here, lanes] = key_grad.astype(low)
        grads[2, here, lanes] = value_grad.astype(low)

    def inputs_step():
        @pl.when(r == 0)
        def _():
            loads[3].wait()

        query_grad = dqt[...].T.astype(low)
        grads[0, here, :] = query_grad
        value_grad = grads[2, here, :]
        dx_ref[...] = (
            dr1_ref[...]
            + dot_nt(query_grad, w_ref[0])
            + dot_nt(grads[1, here, :], w_ref[1])
            + dot_nt(value_grad, w_ref[2])
        )
        dvec_ref[0:1, :] += column_sum(query_grad.astype(full))
        dvec_ref[1:2, :] += column_sum(value_grad.astype(full))

    def position(n, carry):
        side.tick(r * ticks + n)
        side.advance((r == 0) & (n == 6), 2)
        side.advance((r == 1) & (n == 4), 3)

        @pl.when(n == 0)
        def _():
            prepare()

        @pl.when((n >= 1) & (n <= pairs))
        def _():
            pair_step(n - 1)

        @pl.when(n == pairs + 1)
        def _():
            inputs_step()

        @pl.when((n > pairs + 1) & (r == last_row))
        def _():
            j = n - (pairs + 2)
            dw_ref[j] = dot_nn(xt[...], grads[j]).astype(low)

        return carry

    lax.fori_loop(0, ticks, position, 0)
    side.leave(r == last_row, plan.rows * ticks)


def attend_back(da, dr1, hidden, kept, seg_column, seg_row, weights, start, plan, identity=None):
    q, k, v, ctxt, lse = kept
    tokens, width = da.shape
    rows = tokens // L
    heads = width // HD
    shape = jax.ShapeDtypeStruct
    plan.start, plan.rows = start, rows

    def row_block():
        return pl.BlockSpec((L, width), lambda r: (r, 0))

    return pl.pallas_call(
        functools.partial(attend_back_kernel, plan),
        grid=(rows,),
        out_shape=(
            shape((4 - plan.own, width, width), low), shape((tokens, width), full), shape((8, width), full),
            *plan.results,
        ),
        in_specs=[
            ANYWHERE,
            row_block(), row_block(), row_block(), row_block(), row_block(),
            ANYWHERE,
            pl.BlockSpec((1, heads, L), lambda r: (r, 0, 0)),
            pl.BlockSpec((1, L, 1), lambda r: (r, 0, 0)),
            pl.BlockSpec((1, 1, L), lambda r: (r, 0, 0)),
            ANYWHERE,
            *plan.argument_specs,
        ],
        out_specs=(
            pl.BlockSpec((4 - plan.own, width, width), lambda r: (0, 0, 0), pipeline_mode=pl.Buffered(1)),
            row_block(),
            pl.BlockSpec((8, width), lambda r: (0, 0)),
            *plan.result_specs,
        ),
        scratch_shapes=[
            pltpu.VMEM((L, L), full),
            pltpu.VMEM((L, width), low),
            pltpu.VMEM((width, L), low),
            pltpu.VMEM((16, L), full),
            pltpu.VMEM((width, L), full),
            pltpu.VMEM((width, tokens), low),
            pltpu.VMEM((3, tokens, width), low),
            pltpu.VMEM((1, 4, 2, width // 8, width) if plan.own else (8, 128), low),
            pltpu.VMEM((tokens, width), low),
            pltpu.VMEM((width, tokens), low),
            pltpu.VMEM((4, width, width), low),
            pltpu.SemaphoreType.DMA((4,)),
            *plan.scratch,
        ],
        compiler_params=pltpu.CompilerParams(
            dimension_semantics=("arbitrary",), vmem_limit_bytes=60 * MIB,
            collective_id=identity, has_side_effects=identity is not None,
        ),
        cost_estimate=pl.CostEstimate(
            flops=16 * tokens * width * width + 10 * tokens * L * width,
            bytes_accessed=30 * MIB,
            transcendentals=tokens * L * heads,
        ),
        name="attend_backward",
    )(da, dr1, hidden, q, k, v, ctxt, lse, seg_column, seg_row, weights, *plan.arguments)


def moments(rotated, first, second):
    first_new = beta_one * first + (1.0 - beta_one) * rotated
    second_new = beta_two * second + (1.0 - beta_two) * rotated * rotated
    direction = (
        first_new
        / (1.0 - beta_one**STEP)
        / (jnp.sqrt(second_new / (1.0 - beta_two**STEP)) + adam_epsilon)
    )
    return first_new, second_new, direction


def pack_lanes(piece):
    rows = piece.shape[0] // 2
    return jnp.concatenate([piece[:rows], piece[rows:]], axis=1)


def unpack_lanes(piece):
    columns = piece.shape[1] // 2
    return jnp.concatenate([piece[:, :columns], piece[:, columns:]], axis=0)


def optimizer_kernel(plan, *refs):
    spans = len(plan.spans)
    inputs, ready, dvecs, bases, lines_in, outputs, lines_out, scratch, sum_refs, vec_refs, line_refs = split_refs(
        refs, 6, plan.ready, plan.dvecs, plan.bases, spans, 5, spans, 21, SUM_REFS, SUM_REFS, 2 * bool(spans)
    )
    index_ref, place_ref, tail_hbm, first_hbm, second_hbm, blocks = inputs
    new_ref, low_ref, first_out, second_out, vec_out = outputs
    (store, left, right, first_in, second_in, g_out, g_in, t_out, t_in, e_out, e_in, w_out, w_in, vec_source,
     load_sem, g_sem, t_sem, e_sem, w_sem, left_sem, right_sem) = scratch
    slots, owners = g_in.shape[0], g_in.shape[1]
    z_count = t_in.shape[1]
    place = Place(z_count)
    dp, z = place.dp, place.z
    dps = [lax.rem(dp + d, owners) for d in range(owners)]
    count = blocks.shape[0]
    many = tail_hbm.shape[0]
    tail_times = [[many * stage + n for n in range(many)] for stage in range(5)]
    tail = BlockSum(place, [tail_hbm], sum_refs, tail_times)
    vec = BlockSum(place, [vec_source], vec_refs, [[many * stage + 1] for stage in range(5)])
    order = plan.free + [s for s in range(slots) if s not in plan.free]
    lines = line_gathers(place, plan.spans, lines_in, lines_out, line_refs, z_count)
    every = list(bases) + list(lines_out)
    late = [s for s in range(slots) if plan.left_map[s][0] >= len(bases)]

    def load(refs_map, target, sem, s):
        n, at = refs_map[s]
        return pltpu.make_async_copy(every[n].at[:, at], target.at[:, s], sem.at[s])

    def load_first(s):
        return pltpu.make_async_copy(first_hbm.at[s], first_in.at[s], load_sem.at[0, s])

    def load_second(s):
        return pltpu.make_async_copy(second_hbm.at[s], second_in.at[s], load_sem.at[1, s])

    for s in order:
        load(plan.right_map, right, right_sem, s).start()
        if s not in late:
            load(plan.left_map, left, left_sem, s).start()
        load_first(s).start()
        load_second(s).start()
    greet([(other, z) for other in dps[1:]] + place.z_partners())
    start = many
    for part in ready:
        store[start : start + part.shape[0]] = part[...]
        start += part.shape[0]
    store[0:many] = jnp.zeros((many,) + store.shape[1:], low)
    store[count] = jnp.zeros(store.shape[1:], low)
    rows = plan.vector_rows
    stacked = jnp.concatenate(
        [dvecs[0][0:2, :], dvecs[1][2:rows, :], dvecs[2][0:2, :], dvecs[3][2:rows, :],
         jnp.zeros((vec_source.shape[-1] - 2 * rows, blocks.shape[2]), full)], axis=0
    )
    vec_source[0] = stacked.T.reshape(vec_source.shape[1:])

    def g_copy(s, d):
        other = dps[d]
        return remote(g_out.at[s, d], g_in.at[s, dp], g_sem.at[0, s, d], g_sem.at[1, s, owners - d], (other, z))

    def t_copy(s, d):
        other = place.zs[d]
        return remote(t_out.at[s, d], t_in.at[s, z], t_sem.at[0, s, d], t_sem.at[1, s, z_count - d], (dp, other))

    def e_copy(s, d):
        other = place.zs[d]
        return remote(e_out.at[s, d], e_in.at[s, z], e_sem.at[0, s, d], e_sem.at[1, s, z_count - d], (dp, other))

    def w_copy(s, d):
        other = dps[d]
        return remote(
            w_out.at[s, other], w_in.at[s * owners + dp], w_sem.at[0, s, d], w_sem.at[1, s, owners - d], (other, z)
        )

    def send_out(s):
        for d in range(1, owners):
            g_out[s, d] = store[index_ref[s * owners + dps[d]]]
            g_copy(s, d).start()
        g_in[s, dp] = store[index_ref[s * owners + dp]]

    def turn(s):
        for d in range(1, owners):
            g_copy(s, d).wait()
        load(plan.right_map, right, right_sem, s).wait()
        grad = jnp.concatenate([unfold(g_in[s, c].astype(full)) for c in range(owners)], axis=0).astype(low)
        for d in range(1, z_count):
            t_out[s, d] = pack_lanes(dot_nt(right[place.zs[d], s], grad)).astype(low)
            t_copy(s, d).start()
        t_in[s, z] = pack_lanes(dot_nt(right[z, s], grad)).astype(low)

    def adapt(s):
        for d in range(1, z_count):
            t_copy(s, d).wait()
        load_first(s).wait()
        load_second(s).wait()
        load(plan.left_map, left, left_sem, s).wait()
        rotated = jnp.zeros(first_in.shape[1:], full)
        for f in range(z_count):
            rotated = rotated + dot_nn(unpack_lanes(t_in[s, f].astype(full)).astype(low), left[f, s])
        first_new, second_new, direction = moments(rotated, first_in[s], second_in[s])
        first_out[s] = first_new
        second_out[s] = second_new
        direction = direction.astype(low)
        for d in range(1, z_count):
            e_out[s, d] = pack_lanes(dot_nt(left[place.zs[d], s], direction)).astype(low)
            e_copy(s, d).start()
        e_in[s, z] = pack_lanes(dot_nt(left[z, s], direction)).astype(low)

    def step_back(s):
        for d in range(1, z_count):
            e_copy(s, d).wait()
        step = jnp.zeros((left.shape[2], left.shape[3]), full)
        for f in range(z_count):
            step = step + dot_nn(unpack_lanes(e_in[s, f].astype(full)).astype(low), right[f, s])
        share = step.shape[0] // owners
        for c in range(owners):
            w_out[s, c] = fold(step[c * share : (c + 1) * share]).astype(low)
        for d in range(1, owners):
            w_copy(s, d).start()
        w_in[s * owners + dp] = w_out[s, dp]

    def sums(stage):
        for t in range(many * stage, many * (stage + 1)):
            tail.tick(t)
            vec.tick(t)

    free = plan.free
    def advance(hop):
        for line in lines:
            line.advance(hop)

    sums(0)
    advance(1)
    for s in free:
        send_out(s)
    sums(1)
    for s in free:
        turn(s)
    sums(2)
    advance(2)
    for s in free:
        adapt(s)
    sums(3)
    sums(4)
    advance(3)
    for i in range(many):
        store[i] = tail.finish(i).astype(low)
    rest = order[len(free) :]
    for s in rest[:2]:
        send_out(s)
    for s in free:
        step_back(s)
    advance(z_count)
    for s in late:
        load(plan.left_map, left, left_sem, s).start()
    for k in range(len(rest) + 2):
        if k < len(rest):
            turn(rest[k])
            if k + 2 < len(rest):
                send_out(rest[k + 2])
        if 0 <= k - 1 < len(rest):
            adapt(rest[k - 1])
        if 0 <= k - 2 < len(rest):
            step_back(rest[k - 2])

    vec_out[...] = vec.finish(0)
    for s in range(slots):
        for d in range(1, owners):
            w_copy(s, d).wait()

    def block_step(b, carry):
        step = unfold(w_in[place_ref[b]].astype(full))
        block = blocks[b]
        new = block - matrix_rate * (step + weight_decay * block)
        new_ref[b] = new
        low_ref[b] = new.astype(low)
        return carry

    lax.fori_loop(0, count, block_step, 0)


class OptimizerPlan:
    def __init__(self, ready, dvecs, bases, spans, left_map, right_map, free, vector_rows):
        self.ready, self.dvecs, self.bases, self.spans = ready, dvecs, bases, spans
        self.left_map, self.right_map, self.free, self.vector_rows = left_map, right_map, free, vector_rows


def optimizer(
    index, places, tail, ready, dvecs, vector_rows, bases, lines, left_map, right_map, free, first, second, blocks,
    z_count, identity,
):
    slots, columns, width = first.shape
    owners = index.shape[0] // slots
    count, rows = blocks.shape[0], blocks.shape[1]
    span = bases[0].shape[2]
    lanes = 128
    shape = jax.ShapeDtypeStruct
    piece = (2 * rows, width // 2)
    tile = (span // 2, 2 * columns)
    smem = pl.BlockSpec(memory_space=pltpu.SMEM)
    spans = [(first_slot, amount) for _, first_slot, amount in lines]
    plan = OptimizerPlan(len(ready), len(dvecs), len(bases), spans, left_map, right_map, free, vector_rows)
    line_shapes = [shape((z_count, amount) + basis.shape[1:], low) for basis, _, amount in lines]
    return pl.pallas_call(
        functools.partial(optimizer_kernel, plan),
        out_shape=(
            shape(blocks.shape, full), shape(blocks.shape, low), shape(first.shape, full), shape(first.shape, full),
            shape((rows, lanes), full), *line_shapes,
        ),
        in_specs=[smem, smem, ANYWHERE, ANYWHERE, ANYWHERE, IN_VMEM]
        + [IN_VMEM] * (len(ready) + len(dvecs)) + [ANYWHERE] * (len(bases) + len(lines)),
        out_specs=(IN_VMEM,) * 5 + (ANYWHERE,) * len(lines),
        scratch_shapes=[
            pltpu.VMEM((count + 1,) + piece, low),
            pltpu.VMEM((z_count, slots, span, width), low),
            pltpu.VMEM((z_count, slots, columns, width), low),
            pltpu.VMEM((slots, columns, width), full),
            pltpu.VMEM((slots, columns, width), full),
            pltpu.VMEM((slots, owners) + piece, low),
            pltpu.VMEM((slots, owners) + piece, low),
            pltpu.VMEM((slots, z_count) + tile, low),
            pltpu.VMEM((slots, z_count) + tile, low),
            pltpu.VMEM((slots, z_count) + tile, low),
            pltpu.VMEM((slots, z_count) + tile, low),
            pltpu.VMEM((slots, owners) + piece, low),
            pltpu.VMEM((slots * owners,) + piece, low),
            pltpu.VMEM((1, owners // 2, 2, width // owners, lanes), full),
            pltpu.SemaphoreType.DMA((2, slots)),
            pltpu.SemaphoreType.DMA((2, slots, owners)),
            pltpu.SemaphoreType.DMA((2, slots, z_count)),
            pltpu.SemaphoreType.DMA((2, slots, z_count)),
            pltpu.SemaphoreType.DMA((2, slots, owners)),
            pltpu.SemaphoreType.DMA((slots,)),
            pltpu.SemaphoreType.DMA((slots,)),
            *sum_scratch(tail.shape[0], tail.shape[3], width, z_count),
            *sum_scratch(1, width // owners, lanes, z_count, full),
            *line_scratch(len(lines), z_count),
        ],
        compiler_params=pltpu.CompilerParams(
            vmem_limit_bytes=60 * MIB, collective_id=identity, has_side_effects=True
        ),
        cost_estimate=pl.CostEstimate(
            flops=8 * slots * span * width * width, bytes_accessed=40 * MIB, transcendentals=slots * width * columns
        ),
        name="optimizer",
    )(index, places, tail, first, second, blocks, *ready, *dvecs, *bases, *[basis for basis, _, _ in lines])


def slot_table(owner, slots, owner_rows):
    block_count = owner.shape[0]
    same_owner = owner[:, None] == owner[None, :]
    ordering = jnp.arange(block_count, dtype=jnp.int32)
    earlier = ordering[None, :] < ordering[:, None]
    ranking = jnp.sum(jnp.where(same_owner & earlier, 1, 0), axis=1).astype(jnp.int32)
    owner_match = owner[None, :] == jnp.arange(owner_rows, dtype=jnp.int32)[:, None]
    slot_match = ranking[None, :] == jnp.arange(slots, dtype=jnp.int32)[:, None]
    return jnp.where(slot_match[:, None, :] & owner_match[None, :, :], 1.0, 0.0).astype(full)


def scatter_sum(grads):
    blocks, width = grads.shape[0], grads.shape[2]
    cut = grads.reshape(blocks, lax.axis_size("dp"), -1, width).transpose(1, 0, 2, 3)
    outer = lax.psum_scatter(cut, "dp", scatter_dimension=0, tiled=False)
    blocks, rows, width = outer.shape
    count = lax.axis_size("fsdp")
    cut = outer.reshape(blocks, count, rows // count, width).transpose(1, 0, 2, 3)
    return lax.psum_scatter(cut, "fsdp", scatter_dimension=0, tiled=False)


def scatter_vectors(grads):
    rows, width = grads.shape
    count = lax.axis_size("dp") * lax.axis_size("fsdp")
    cut = grads.reshape(rows, count, width // count).transpose(1, 0, 2)
    return lax.psum_scatter(cut, ("dp", "fsdp"), scatter_dimension=0, tiled=False)


def gathering_program(
    tokens, segment, blocks, vectors, owner, left_basis, right_basis, rot_first, rot_second, cotangent, z_count
):
    layers, vector_rows = vectors.shape[:2]
    count, shard_rows, width = blocks.shape
    per_layer = count // layers
    inner = (per_layer - 4) // 2
    owners = lax.axis_size("dp")
    slots = rot_first.shape[0]
    part = width // owners
    lanes = 128
    seg_column, seg_row = segment[:, :, None], segment[:, None, :]

    order = [0, 1, 2, 3]
    for c in range(inner):
        order += [4 + c, 4 + inner + c]
    folded = blocks.astype(low).reshape(count, shard_rows, 2, width // 2).transpose(0, 2, 1, 3)
    folded = folded.reshape(count, 2 * shard_rows, width // 2)

    def pick(numbers):
        return jnp.stack([folded[j] for j in numbers]).reshape(len(numbers) // 2, 2, *folded.shape[1:])

    head = pick(order + [per_layer + j for j in order[:4]])
    rest = pick([per_layer + j for j in order[4:]])
    vec_shard = vectors.astype(low).astype(full).reshape(layers * vector_rows, shard_rows).T
    vec_shard = jnp.pad(vec_shard, ((0, 0), (0, lanes - layers * vector_rows)))[None, None]
    left_low = left_basis.reshape(slots, -1, width).astype(low)
    right_low = right_basis.transpose(0, 2, 1).astype(low)

    plan = ForwardPlan(
        inner, 0, head, vec_shard, vector_rows, [(right_low, 0, 2)], lead=5, row_positions=(1,), z_count=z_count
    )
    empty_vec = jnp.zeros((16, width), full)
    results = forward_layer(tokens, seg_column, seg_row, empty_vec, jnp.zeros((1, width, width), low), full, plan, 6)
    kept_a = results[:12]
    hidden, weights_a, vec_a, vec_b, right_01 = results[12:]
    weights_a = weights_a.reshape(-1, width, width)
    plan = ForwardPlan(inner, 4, rest, lines=[(right_low, 2, 1)], lead=0, row_positions=(1, 4), z_count=z_count)
    plan.order = [per_layer + j for j in range(4)]
    results = forward_layer(hidden, seg_column, seg_row, vec_b, weights_a, low, plan, 7)
    kept_b = results[:12]
    layer_out, weights_b, right_2 = results[12:]
    weights_b = weights_b.reshape(-1, width, width)

    def cut(grads):
        return grads.reshape(-1, owners // 2, 2, part, width)

    size = (part, width)
    own_b, own_a = 4, 3

    def left_over(own):
        return 2 * inner - own, own % 2

    plan = Plan(None, [(right_low, 3, 1)], z_count, own_b, size, wide_ready(own_b))
    dw_wide, dr1, da, dvec_wide_b, wide_sum_b, right_3 = wide_back(
        cotangent, kept_b[5:], vec_b, weights_b, (0, 1, 2), plan, 1
    )
    pending, skip = left_over(own_b)
    plan = Plan(cut(dw_wide), [(right_low, 4, 1), (left_low, 3, 1)], z_count, 1, size, list(range(pending + 1)), skip)
    dw_attend, upstream, dvec_attend_b, attend_sum_b, right_4, left_3 = attend_back(
        da, dr1, hidden, kept_b[:5], seg_column, seg_row, weights_a, per_layer, plan, 2
    )
    plan = Plan(
        cut(dw_attend), [(left_low, 4, 1), (left_low, 0, 1)], z_count, own_a, size, [0, 1, 2] + wide_ready(own_a)
    )
    dw_wide, dr1, da, dvec_wide_a, wide_sum_a, left_4, left_0 = wide_back(
        upstream, kept_a[5:], vec_a, weights_a, (4, 5, 2), plan, 3
    )
    pending, skip = left_over(own_a)
    plan = Plan(cut(dw_wide), [(left_low, 1, 1)], z_count, 1, size, list(range(pending + 1)), skip)
    dw_attend, upstream, dvec_attend_a, attend_sum_a, left_1 = attend_back(
        da, dr1, tokens, kept_a[:5], seg_column, seg_row, weights_a, 0, plan, 5
    )

    three = list(range(3))

    def early(own):
        return [4 + n // 2 + inner * (n % 2) for n in range(own)]

    def late(own):
        return [4 + c + inner * k for k in range(2) for c in range(inner) if 2 * c + k >= own] + [3]

    held_order = three + late(own_a) + [per_layer + j for j in three] + early(own_a)
    held_order += [per_layer + j for j in late(own_b) + early(own_b)]
    rank = jnp.asarray([held_order.index(j) for j in range(count)], jnp.int32)
    table = slot_table(owner, slots, owners).reshape(slots * owners, count)
    held = jnp.sum(table, axis=1)
    index = jnp.where(held > 0, jnp.sum(table * rank, axis=1), count).astype(jnp.int32)
    places = jnp.sum(table * jnp.arange(slots * owners, dtype=jnp.int32)[:, None], axis=0).astype(jnp.int32)
    bases = (right_01, right_2, right_3, right_4, left_0, left_1, left_3, left_4)
    right_map = [(0, 0), (0, 1), (1, 0), (2, 0), (3, 0)]
    left_map = [(4, 0), (5, 0), (8, 0), (6, 0), (7, 0)]
    free = list(range(3, slots))
    new_blocks, new_low, first_new, second_new, vec_sum, _ = optimizer(
        index, places, cut(dw_attend), (attend_sum_a, wide_sum_a, attend_sum_b, wide_sum_b),
        (dvec_attend_a, dvec_wide_a, dvec_attend_b, dvec_wide_b), vector_rows, bases, [(left_low, 2, 1)], left_map, right_map, free,
        rot_first.transpose(0, 2, 1), rot_second.transpose(0, 2, 1), blocks, z_count, 4,
    )
    first_new, second_new = first_new.transpose(0, 2, 1), second_new.transpose(0, 2, 1)
    vector_grad = vec_sum[:, : layers * vector_rows].T.reshape(layers, vector_rows, shard_rows)
    return layer_out, upstream, new_blocks, new_low, first_new, second_new, vector_grad


def plain_program(
    tokens, segment, blocks, vectors, owner, left_basis, right_basis, rot_first, rot_second, cotangent
):
    layers, vector_rows = vectors.shape[:2]
    per_layer = blocks.shape[0] // layers
    inner = (per_layer - 4) // 2
    width = blocks.shape[2]
    owner_rows = lax.axis_size("dp")
    slots = rot_first.shape[0]
    selector = slot_table(owner, slots, owner_rows)
    vector_parts = lax.all_gather(vectors.astype(low), ("dp", "fsdp"), axis=0, tiled=False)
    vector_full = vector_parts.transpose(1, 2, 0, 3).reshape(layers, vector_rows, width).astype(full)
    blocks_low, vector_full = lax.optimization_barrier((blocks.astype(low), vector_full))

    seg_column = segment[:, :, None]
    seg_row = segment[:, None, :]
    state = tokens
    kept = []
    for layer_index in range(layers):
        start = per_layer * layer_index
        weights = lax.all_gather(blocks_low[start : start + per_layer], ("dp", "fsdp"), axis=1, tiled=True)
        out_dtype = low if layer_index == layers - 1 else full
        results = forward_layer(
            state, seg_column, seg_row, vector_full[layer_index], weights, out_dtype, ForwardPlan(inner, per_layer)
        )
        kept.append((state, weights, results[:5], results[5:12]))
        state = results[12]
    layer_out = state
    upstream = cotangent
    right_low = lax.all_gather(right_basis.astype(low), "fsdp", axis=2, tiled=True)
    block_shards = [None] * layers
    vector_shards = [None] * layers
    for layer_index in reversed(range(layers)):
        hidden, weights, attend_kept, wide_kept = kept[layer_index]
        dw_wide, dr1, da, dvec_wide = wide_back(
            upstream, wide_kept, vector_full[layer_index], weights, (4, 4 + inner, 1), Plan()
        )
        wide_shard = scatter_sum(dw_wide.reshape(-1, width, width))
        dw_attend, upstream, dvec_attend = attend_back(
            da, dr1, hidden, attend_kept, seg_column, seg_row, weights, 0, Plan()
        )
        dvec = jnp.concatenate([dvec_attend[:2], dvec_wide[2:vector_rows]], axis=0)
        block_shards[layer_index] = jnp.concatenate([scatter_sum(dw_attend), wide_shard], axis=0)
        vector_shards[layer_index] = scatter_vectors(dvec)
    vector_grad = jnp.stack(vector_shards)
    block_grad = jnp.concatenate(block_shards, axis=0)
    outgoing = jnp.einsum("srk,kid->srid", selector.astype(low), block_grad, preferred_element_type=full)
    incoming = lax.all_to_all(outgoing.astype(low), "dp", split_axis=1, concat_axis=1, tiled=True)
    owned = incoming.reshape(slots, -1, width)
    turned = jnp.einsum("sik,skj->sij", owned, right_low, preferred_element_type=full).astype(low)
    left_rows = left_basis.reshape(slots, -1, width).astype(low)
    partial_sums = jnp.einsum("sra,srb->sab", left_rows, turned, preferred_element_type=full)
    rotated = lax.psum_scatter(
        partial_sums.astype(low), "fsdp", scatter_dimension=2, tiled=True
    ).astype(full)
    first_new, second_new, direction = moments(rotated, rot_first, rot_second)
    direction_full = lax.all_gather(direction.astype(low), "fsdp", axis=2, tiled=True)
    back_right = jnp.einsum("sab,scb->sac", direction_full, right_low, preferred_element_type=full)
    step_rows = jnp.einsum(
        "sia,sac->sic", left_rows, back_right.astype(low), preferred_element_type=full
    )
    returned = lax.all_to_all(
        step_rows.reshape(slots, owner_rows, -1, width).astype(low),
        "dp",
        split_axis=1,
        concat_axis=1,
        tiled=True,
    )
    step_shard = jnp.einsum("srk,srid->kid", selector.astype(low), returned, preferred_element_type=full)
    new_blocks = blocks - matrix_rate * (step_shard + weight_decay * blocks)
    return layer_out, upstream, new_blocks, new_blocks.astype(low), first_new, second_new, vector_grad


def shards(
    tokens,
    segment,
    blocks,
    vectors,
    owner,
    left_basis,
    right_basis,
    rot_first,
    rot_second,
    vec_first,
    vec_second,
    cotangent,
):
    operands = (
        tokens, segment, blocks, vectors, owner, left_basis, right_basis, rot_first, rot_second, cotangent
    )
    z_count = lax.axis_size("fsdp")
    if lax.axis_size("dp") == 8 and z_count == 4:
        results = gathering_program(*operands, z_count)
    else:
        results = plain_program(*operands)
    layer_out, upstream, new_blocks, new_low, first_new, second_new, vector_grad = results
    vector_first = beta_one * vec_first + (1.0 - beta_one) * vector_grad
    vector_second = beta_two * vec_second + (1.0 - beta_two) * vector_grad * vector_grad
    vector_step = (
        vector_first
        / (1.0 - beta_one**STEP)
        / (jnp.sqrt(vector_second / (1.0 - beta_two**STEP)) + adam_epsilon)
    )
    vector_new = vectors - vector_rate * (vector_step + weight_decay * vectors)
    return (
        layer_out,
        upstream,
        new_blocks,
        new_low,
        first_new,
        second_new,
        vector_first,
        vector_second,
        vector_new,
    )


def solution(mesh):
    return jax.shard_map(
        shards,
        mesh=mesh,
        in_specs=(
            P(("dp", "fsdp"), None),
            P(("dp", "fsdp"), None),
            P(None, ("dp", "fsdp"), None),
            P(None, None, ("dp", "fsdp")),
            P(),
            P("dp", None, "fsdp", None),
            P("dp", None, "fsdp"),
            P("dp", None, "fsdp"),
            P("dp", None, "fsdp"),
            P(None, None, ("dp", "fsdp")),
            P(None, None, ("dp", "fsdp")),
            P(("dp", "fsdp"), None),
        ),
        out_specs=(
            P(("dp", "fsdp"), None),
            P(("dp", "fsdp"), None),
            P(None, ("dp", "fsdp"), None),
            P(None, ("dp", "fsdp"), None),
            P("dp", None, "fsdp"),
            P("dp", None, "fsdp"),
            P(None, None, ("dp", "fsdp")),
            P(None, None, ("dp", "fsdp")),
            P(None, None, ("dp", "fsdp")),
        ),
        check_vma=False,
    )
```

```python
import functools

import jax
import jax.numpy as jnp
from jax import lax
from jax.experimental import pallas as pl
from jax.experimental.pallas import tpu as pltpu
from jax.sharding import PartitionSpec as P

H = 12
HD = 64
L = 512
STEP = 5
SEGS = 4
PAIR = 2 * HD
MIB = 1 << 20

beta_one = 0.5
beta_two = 0.5
adam_epsilon = 1e-08
norm_epsilon = 1e-06
matrix_rate = 0.03
vector_rate = 0.2
weight_decay = 0.01
masked_score = -1e30
low = jnp.bfloat16
full = jnp.float32


def dot_nn(a, b):
    return lax.dot_general(a, b, (((1,), (0,)), ((), ())), preferred_element_type=full)


def dot_nt(a, b):
    return lax.dot_general(a, b, (((1,), (1,)), ((), ())), preferred_element_type=full)


def dot_tn(a, b):
    return lax.dot_general(a, b, (((0,), (0,)), ((), ())), preferred_element_type=full)


def gelu_parts(z):
    t = pl.reciprocal(1.0 + 0.23164190 * jnp.abs(z), approx=True)
    square = z * z
    bell = jnp.exp2(-0.7213475204444817 * square)
    poly = ((((0.5307027145 * t - 0.7265760135) * t + 0.7107068705) * t - 0.142248368) * t + 0.127414796) * t
    tail = poly * bell
    phi = jnp.where(z >= 0, 1.0 - tail, tail)
    return z * phi, phi + (0.3989422804014327 * z) * bell


def norm_parts(residual):
    average = jnp.mean(residual, axis=-1, keepdims=True)
    centered = residual - average
    inverse = lax.rsqrt(jnp.mean(centered * centered, axis=-1, keepdims=True) + norm_epsilon)
    return centered * inverse, inverse


def norm_back(upstream, unit, inverse, gain):
    scaled = upstream * gain
    return inverse * (
        scaled
        - jnp.mean(scaled, axis=-1, keepdims=True)
        - unit * jnp.mean(scaled * unit, axis=-1, keepdims=True)
    )


def column_sum(values):
    return jnp.sum(values, axis=0, keepdims=True)


def half_masks(dtype):
    lane = lax.broadcasted_iota(jnp.int32, (1, PAIR), 1)
    first = (lane < HD).astype(full)
    return first.astype(dtype), (1.0 - first).astype(dtype)


def segment_codes(seg_column, masks):
    lane = lax.broadcasted_iota(jnp.int32, (1, PAIR), 1)
    lane = jnp.where(lane >= HD, lane - HD, lane)
    same = seg_column == lane
    key = jnp.where(same, 1.0, 0.0).astype(low)
    query = jnp.where(same | (lane >= SEGS), 0.0, masked_score).astype(low)
    return [key * masks[1 - h] for h in range(2)], [query * masks[1 - h] for h in range(2)]


class Place:
    def __init__(self, z_count):
        self.dp, self.z = lax.axis_index("dp"), lax.axis_index("fsdp")
        self.core, self.spot = lax.rem(self.dp, 2), lax.div(self.dp, 2)
        x_step = 1 - 2 * lax.rem(self.spot, 2)
        y_step = 2 - 4 * lax.div(self.spot, 2)
        self.spot_a = self.spot + (1 - self.core) * x_step + self.core * y_step
        self.spot_b = self.spot + self.core * x_step + (1 - self.core) * y_step
        self.spot_ab = self.spot + x_step + y_step
        self.sibling = (self.dp + 1 - 2 * self.core, self.z)
        self.near_a = (2 * self.spot_a + self.core, self.z)
        self.near_b = (2 * self.spot_b + self.core, self.z)
        self.z_count = z_count
        self.zs = [lax.rem(self.z + d, z_count) for d in range(z_count)]
        self.has_up, self.has_down = self.z < z_count - 1, self.z > 0
        self.middle = self.has_up & self.has_down
        self.across = lax.rem(self.z + 2, z_count)
        self.beside = jnp.where(self.z < 2, 1 - self.z, 5 - self.z)

    def line_sends(self, d):
        return {1: self.has_up, 2: self.z >= 0, 3: self.has_down}[d]

    def line_receives(self, d):
        return {1: self.has_down, 2: self.z >= 0, 3: self.has_up}[d]

    def chip_partners(self):
        return [self.sibling, self.near_a, self.near_b]

    def z_partners(self):
        return [(self.dp, other) for other in self.zs[1:]]


def greet(partners):
    barrier = pltpu.get_barrier_semaphore()
    for device in partners:
        pl.semaphore_signal(barrier, inc=1, device_id=device, device_id_type=pl.DeviceIdType.MESH)
    pl.semaphore_wait(barrier, len(partners))


def remote(source, target, send, receive, device):
    return pltpu.make_async_remote_copy(
        src_ref=source,
        dst_ref=target,
        send_sem=send,
        recv_sem=receive,
        device_id=device,
        device_id_type=pl.DeviceIdType.MESH,
    )


def fold(piece):
    half = piece.shape[1] // 2
    return jnp.concatenate([piece[:, :half], piece[:, half:]], axis=0)


def unfold(piece):
    rows = piece.shape[0] // 2
    return jnp.concatenate([piece[:rows], piece[rows:]], axis=1)


def looked_up(ticks, t):
    now = functools.reduce(jnp.logical_or, [t == tick for tick in ticks])
    which = sum(n * (t == tick).astype(jnp.int32) for n, tick in enumerate(ticks))
    return now, which


def run_due(stages, t):
    for ticks, stage in stages:
        if isinstance(t, int):
            if t in ticks:
                stage(ticks.index(t))
            continue
        now, block = looked_up(ticks, t)

        @pl.when(now)
        def _():
            stage(block)


def sum_times(ready):
    opens, cores, seconds = [], [], []
    for tick in ready:
        opens.append(max(tick, opens[-1] + 1) if opens else tick)
        cores.append(max(opens[-1] + 1, cores[-1] + 1) if cores else opens[-1] + 1)
        seconds.append(max(cores[-1] + 3, seconds[-1] + 3) if seconds else cores[-1] + 3)
    thirds = [tick + 2 for tick in seconds]
    return opens, cores, seconds, thirds, [tick + 2 for tick in thirds]


ANNOUNCE, FORWARD, FIRST, SECOND, CLOSE = -2, -1, 1, 2, 3


def sum_scratch(count, part, width, z_count, kind=low):
    piece = (2 * part // z_count, width // 2) if kind == low else (part // z_count, width)
    return [
        pltpu.VMEM((count, 4, part, width), kind),
        pltpu.VMEM((count, 4, part, width), kind),
        pltpu.VMEM((count, 2, part, width), kind),
        pltpu.VMEM((count, part, width), kind),
        pltpu.VMEM((count, z_count) + piece, kind),
        pltpu.VMEM((count, z_count) + piece, kind),
        pltpu.VMEM((count,) + piece, kind),
        pltpu.SemaphoreType.DMA((count,)),
        pltpu.SemaphoreType.DMA((count, 2)),
        pltpu.SemaphoreType.DMA((count, 2, 2)),
        pltpu.SemaphoreType.DMA((count, 2)),
        pltpu.SemaphoreType.DMA((count, 2, z_count)),
        pltpu.SemaphoreType.DMA((count, 2)),
    ]


SUM_REFS = 13


class BlockSum:
    def __init__(self, place, sources, refs, times):
        self.place, self.sources, self.times = place, sources, times
        (self.own, self.c, self.b, self.a, self.zs, self.zr, self.far,
         self.own_sem, self.c_sem, self.b_sem, self.a_sem, self.z_sem, self.far_sem) = refs
        self.count = self.c.shape[0]
        self.kind = self.c.dtype
        self.z_count = self.zs.shape[1]

    def load(self, i, block):
        return pltpu.make_async_copy(block.at[:, self.place.core], self.own.at[i], self.own_sem.at[i])

    def core_copy(self, i, block):
        return remote(
            block.at[:, 1 - self.place.core], self.c.at[i], self.c_sem.at[i, 0], self.c_sem.at[i, 1], self.place.sibling
        )

    def second_copy(self, i, k):
        chunk = self.place.spot_b if k == 0 else self.place.spot_ab
        return remote(
            self.c.at[i, chunk], self.b.at[i, k], self.b_sem.at[i, 0, k], self.b_sem.at[i, 1, k], self.place.near_b
        )

    def third_copy(self, i):
        return remote(
            self.c.at[i, self.place.spot_a], self.a.at[i], self.a_sem.at[i, 0], self.a_sem.at[i, 1], self.place.near_a
        )

    def z_copy(self, i, d):
        other = self.place.zs[d]
        return remote(
            self.zs.at[i, other], self.zr.at[i, self.place.z], self.z_sem.at[i, 0, d],
            self.z_sem.at[i, 1, self.z_count - d], (self.place.dp, other),
        )

    def open(self, i):
        first = 0
        for source in self.sources:
            count = source.shape[0]

            @pl.when((i >= first) & (i < first + count))
            def _():
                block = source.at[jnp.clip(i - first, 0, count - 1)]
                self.core_copy(i, block).start()
                self.load(i, block).start()

            first += count

    def after_core(self, i):
        block = self.sources[0].at[0]
        self.core_copy(i, block).wait()
        self.load(i, block).wait()

        def add(k, carry):
            self.c[i, k] = (self.c[i, k].astype(full) + self.own[i, k].astype(full)).astype(self.kind)
            return carry

        lax.fori_loop(0, 4, add, 0)
        self.second_copy(i, 0).start()
        self.second_copy(i, 1).start()

    def after_second(self, i):
        other, spot = self.place.spot_a, self.place.spot
        self.second_copy(i, 1).wait()
        self.c[i, other] = (self.c[i, other].astype(full) + self.b[i, 1].astype(full)).astype(self.kind)
        self.third_copy(i).start()
        self.second_copy(i, 0).wait()
        self.c[i, spot] = (self.c[i, spot].astype(full) + self.b[i, 0].astype(full)).astype(self.kind)

    def after_third(self, i):
        self.third_copy(i).wait()
        total = self.c[i, self.place.spot].astype(full) + self.a[i].astype(full)
        rows = total.shape[0] // self.z_count
        for k in range(self.z_count):
            piece = total[k * rows : (k + 1) * rows]
            self.zs[i, k] = fold(piece).astype(low) if self.kind == low else piece
        place = self.place
        for d in (1, 3):
            @pl.when(place.line_sends(d))
            def _():
                self.z_copy(i, d).start()

        @pl.when(jnp.logical_not(place.middle))
        def _():
            self.z_copy(i, 2).start()
            self.far_copy(i).start()
            opposite = self.z_count - 1 - place.z
            self.zr[i, opposite] = jnp.zeros(self.zr.shape[2:], self.kind)

    def far_copy(self, i):
        place = self.place
        return remote(
            self.zs.at[i, self.z_count - 1 - place.z], self.far.at[i], self.far_sem.at[i, 0], self.far_sem.at[i, 1],
            (place.dp, place.beside),
        )

    def relay(self, i):
        @pl.when(self.place.middle)
        def _():
            self.far_copy(i).wait_recv()
            across = self.place.across
            self.zs[i, across] = (self.zs[i, across].astype(full) + self.far[i].astype(full)).astype(self.kind)
            self.z_copy(i, 2).start()

    def finish(self, i):
        for d in range(1, self.z_count):
            @pl.when(self.place.line_sends(d))
            def _():
                self.z_copy(i, d).wait_send()

            @pl.when(self.place.line_receives(d))
            def _():
                self.z_copy(i, d).wait_recv()

        @pl.when(jnp.logical_not(self.place.middle))
        def _():
            self.far_copy(i).wait_send()

        total = self.zs[i, self.place.z].astype(full)
        for d in range(1, self.z_count):
            total = total + self.zr[i, self.place.zs[d]].astype(full)
        return total

    def tick(self, t):
        stages = (self.relay, self.after_third, self.after_second, self.after_core, self.open)
        run_due(list(zip(self.times[::-1], stages)), t)

    @property
    def last(self):
        return self.times[4][-1]


class LineGather:
    def __init__(self, place, source, target, first, local_sem, sem, z_count):
        self.place = place
        self.source = source.at[pl.ds(first, target.shape[1])]
        self.target, self.local_sem, self.sem, self.z_count = target, local_sem, sem, z_count

    def hop_copy(self, hop, way):
        dp, z = self.place.dp, self.place.z
        if way == 0:
            piece, other, coming = z - hop + 1, z + 1, z - hop
            sends = (piece >= 0) & (other < self.z_count)
            receives = coming >= 0
        else:
            piece, other, coming = z + hop - 1, z - 1, z + hop
            sends = (piece < self.z_count) & (other >= 0)
            receives = coming < self.z_count
        piece = jnp.clip(piece, 0, self.z_count - 1)
        other = jnp.clip(other, 0, self.z_count - 1)
        source = self.source if hop == 1 else self.target.at[piece]
        copy = remote(source, self.target.at[piece], self.sem.at[way, 0, hop - 1], self.sem.at[way, 1, hop - 1], (dp, other))
        return copy, sends, receives

    def local(self):
        return pltpu.make_async_copy(self.source, self.target.at[self.place.z], self.local_sem)

    def start(self, hop):
        if hop == 1:
            self.local().start()
        for way in range(2):
            copy, sends, _ = self.hop_copy(hop, way)

            @pl.when(sends)
            def _():
                copy.start()

    def wait(self, hop):
        if hop == 1:
            self.local().wait()
        for way in range(2):
            copy, sends, receives = self.hop_copy(hop, way)

            @pl.when(sends)
            def _():
                copy.wait_send()

            @pl.when(receives)
            def _():
                copy.wait_recv()

    def advance(self, hop):
        if hop > 1:
            self.wait(hop - 1)
        if hop < self.z_count:
            self.start(hop)


def gather_scratch(count, group, rows, width, z_count, kind=low):
    piece = (2 * rows // z_count, width // 2) if kind == low else (rows // z_count, width)
    return [
        pltpu.VMEM((count, z_count, group) + piece, kind),
        pltpu.SemaphoreType.DMA((count, 2, z_count)),
        pltpu.SemaphoreType.DMA((count, 2)),
        pltpu.SemaphoreType.DMA((count, 2, 2)),
        pltpu.SemaphoreType.DMA((count, 2)),
        pltpu.SemaphoreType.DMA((count, 2)),
    ]


GATHER_REFS = 6


class BlockGather:
    def __init__(self, place, source, whole, base, refs):
        self.place, self.source, self.whole, self.base = place, source, whole, base
        self.zr, self.z_sem, self.a_sem, self.b_sem, self.c_sem, self.far_sem = refs
        self.count, self.z_count, self.group = self.zr.shape[:3]

    def blocks(self, i):
        return pl.ds(self.base + self.group * i, self.group)

    def z_copy(self, i, d):
        place = self.place
        return remote(
            self.source.at[i], self.zr.at[i, place.z], self.z_sem.at[i, 0, d], self.z_sem.at[i, 1, self.z_count - d],
            (place.dp, place.zs[d]),
        )

    def chunk(self, i, spot):
        return self.whole.at[self.blocks(i), spot, self.place.core]

    def first_copy(self, i):
        chunk = self.chunk(i, self.place.spot)
        return remote(chunk, chunk, self.a_sem.at[i, 0], self.a_sem.at[i, 1], self.place.near_a)

    def second_copy(self, i, k):
        chunk = self.chunk(i, self.place.spot if k == 0 else self.place.spot_a)
        return remote(chunk, chunk, self.b_sem.at[i, 0, k], self.b_sem.at[i, 1, k], self.place.near_b)

    def core_copy(self, i):
        chunks = self.whole.at[self.blocks(i), :, self.place.core]
        return remote(chunks, chunks, self.c_sem.at[i, 0], self.c_sem.at[i, 1], self.place.sibling)

    def far_copy(self, i):
        place = self.place
        piece = self.zr.at[i, place.across]
        return remote(piece, piece, self.far_sem.at[i, 0], self.far_sem.at[i, 1], (place.dp, place.beside))

    def announce(self, i):
        for d in range(1, self.z_count):
            @pl.when(self.place.line_sends(d))
            def _():
                self.z_copy(i, d).start()

        self.zr[i, self.place.z] = self.source[i]

    def forward(self, i):
        @pl.when(self.place.middle)
        def _():
            self.z_copy(i, 2).wait_recv()
            self.far_copy(i).start()

    def begin(self):
        for i in range(min(-ANNOUNCE, self.count)):
            self.announce(i)

    def open(self, i):
        place = self.place
        for d in range(1, self.z_count):
            @pl.when(place.line_sends(d))
            def _():
                self.z_copy(i, d).wait_send()

        for d in (1, 3):
            @pl.when(place.line_receives(d))
            def _():
                self.z_copy(i, d).wait_recv()

        @pl.when(place.middle)
        def _():
            self.far_copy(i).wait_send()

        @pl.when(jnp.logical_not(place.middle))
        def _():
            self.z_copy(i, 2).wait_recv()
            self.far_copy(i).wait_recv()

        for n in range(self.group):
            pieces = [self.zr[i, k, n].astype(full) for k in range(self.z_count)]
            if self.zr.dtype == low:
                pieces = [unfold(piece) for piece in pieces]
            whole = jnp.concatenate(pieces, axis=0).astype(self.whole.dtype)
            self.whole[self.base + self.group * i + n, place.spot, place.core] = whole
        self.first_copy(i).start()
        self.second_copy(i, 0).start()

    def after_first(self, i):
        self.first_copy(i).wait()
        self.second_copy(i, 1).start()

    def after_second(self, i):
        self.second_copy(i, 0).wait()
        self.second_copy(i, 1).wait()
        self.core_copy(i).start()

    def close(self, i):
        self.core_copy(i).wait()

    def tick(self, t, done=None):
        def close(i):
            self.close(i)
            if done is not None:
                done(i)

        @pl.when(t == 0)
        def _():
            for i in range(min(-FORWARD, self.count)):
                self.forward(i)

        stages = (
            (SECOND, self.after_second), (FIRST, self.after_first), (0, self.open), (FORWARD, self.forward),
            (ANNOUNCE, self.announce), (CLOSE, close),
        )
        for late, stage in stages:
            @pl.when((t >= max(late, 0)) & (t - late < self.count))
            def _():
                stage(t - late)


def split_refs(refs, *counts):
    result, start = [], 0
    for count in counts:
        result.append(refs[start : start + count])
        start += count
    return result


class Side:
    def __init__(self, plan, sources, targets, sum_refs, line_refs, own=None):
        self.plan = plan
        sums = plan.sums
        blocks = [source.at[pl.ds(plan.skip, source.shape[0] - plan.skip)] for source in sources[:sums]]
        blocks += [own] if plan.own else []
        self.place = Place(plan.z_count) if plan.active else None
        self.sum = BlockSum(self.place, blocks, sum_refs, plan.times) if plan.total else None
        self.result = targets[0] if plan.total else None
        self.lines = line_gathers(self.place, plan.lines, sources[sums:], targets[bool(plan.total) :], line_refs, plan.z_count)

    def enter(self, now):
        if not self.plan.active:
            return

        @pl.when(now)
        def _():
            greet((self.place.chip_partners() if self.plan.total else []) + self.place.z_partners())
            for line in self.lines:
                line.advance(1)

    def tick(self, t):
        if self.plan.total:
            self.sum.tick(t)

    def leave(self, now, ticks):
        if not self.plan.active:
            return

        @pl.when(now)
        def _():
            if self.plan.total:
                if self.sum.last >= ticks:
                    lax.fori_loop(ticks, self.sum.last + 1, lambda t, carry: (self.tick(t), carry)[1], 0)
                for i in range(self.sum.count):
                    self.result[i] = self.sum.finish(i).astype(low)
            for line in self.lines:
                line.advance(self.plan.z_count)

    def advance(self, now, hop):
        if self.lines and hop < self.plan.z_count:
            @pl.when(now)
            def _():
                for line in self.lines:
                    line.advance(hop)


class Plan:
    def __init__(self, pending=None, lines=(), z_count=1, own=0, size=None, ready=(), skip=0):
        self.z_count = z_count
        self.sums = int(pending is not None)
        self.own, self.skip = own, skip
        self.total = own + (pending.shape[0] - skip if self.sums else 0)
        self.times = sum_times(ready) if self.total else None
        self.lines = [(first, count) for _, first, count in lines]
        self.active = bool(self.total or lines)
        self.arguments, self.results, self.result_specs, self.scratch = [], [], [], []
        if self.sums:
            self.arguments.append(pending)
        if self.total:
            part, width = size
            self.results.append(jax.ShapeDtypeStruct((self.total, 2 * part // z_count, width // 2), low))
            self.result_specs.append(
                pl.BlockSpec(self.results[0].shape, lambda i: (0, 0, 0), pipeline_mode=pl.Buffered(1))
            )
            self.scratch += sum_scratch(self.total, part, width, z_count)
        for basis, _, count in lines:
            self.arguments.append(basis)
            self.results.append(jax.ShapeDtypeStruct((z_count, count) + basis.shape[1:], low))
            self.result_specs.append(ANYWHERE)
        self.scratch += line_scratch(len(lines), z_count)
        self.argument_specs = [ANYWHERE] * len(self.arguments)

    def split(self, refs, inputs, outputs, scratch):
        count = len(self.lines)
        return split_refs(
            refs, inputs, self.sums + count, outputs, bool(self.total) + count, scratch,
            SUM_REFS * bool(self.total), 2 * bool(self.lines),
        )


def line_scratch(count, z_count):
    if not count:
        return []
    return [pltpu.SemaphoreType.DMA((count,)), pltpu.SemaphoreType.DMA((count, 2, 2, z_count - 1))]


def line_gathers(place, spans, sources, targets, refs, z_count):
    return [
        LineGather(place, source, target, first, refs[0].at[n], refs[1].at[n], z_count)
        for n, (source, target, (first, _)) in enumerate(zip(sources, targets, spans))
    ]


ANYWHERE = pl.BlockSpec(memory_space=pl.ANY)
IN_VMEM = pl.BlockSpec(memory_space=pltpu.VMEM)


def forward_kernel(plan, *refs):
    inputs, sources, outputs, targets, scratch, gather_refs, vec_refs, line_refs = plan.split(refs)
    x_ref, segc_ref, vec_ref, w_hbm = inputs
    (q_ref, k_ref, v_ref, ctxt_ref, lse_ref, x1_ref, inv1_ref, n1_ref, u_ref, gp_ref, x2_ref, inv2_ref,
     out_ref) = outputs
    w, codes, vt, n1_all, acc, w_sem = scratch
    s = pl.program_id(0)
    tokens, width = acc.shape
    rows_now = x_ref.shape[0]
    rows = tokens // rows_now
    inner = plan.inner
    local = plan.local
    gather = vec_gather = None
    place = Place(plan.z_count) if plan.gathered else None
    if plan.gathered:
        w_out, out_sem = targets[0], scratch_tail(plan, refs)
        gather = BlockGather(place, plan.folded(refs), w, local, gather_refs)
        if plan.vectors:
            vec_gather = BlockGather(place, sources[1], plan.vec_whole(refs), 0, vec_refs)
            vec_ref = targets[1]
    lines = line_gathers(place, plan.lines, sources[plan.line_at :], targets[plan.line_target_at :], line_refs, plan.z_count)

    def keep(i):
        group = gather.group
        return pltpu.make_async_copy(w.at[gather.blocks(i)], w_out.at[pl.ds(group * i, group)], out_sem.at[i])

    def load(j):
        return pltpu.make_async_copy(w_hbm.at[plan.order[j]], w.at[j], w_sem.at[j])

    def matrix(j):
        return w[j].reshape(width, width)

    def arrive(j):
        if j < local:
            load(j).wait()

    def tick(t):
        if gather is not None:
            gather.tick(t, lambda i: keep(i).start())
            if vec_gather is not None:
                vec_gather.tick(t)

    pairs = width // PAIR

    @pl.when(s == 0)
    def _():
        for j in range(local):
            load(j).start()
        if gather is not None:
            for n, number in enumerate(plan.numbers):
                gather.source[n // plan.group, n % plan.group] = fold(sources[0][number]).astype(low)
            greet(place.chip_partners() + place.z_partners())
            if vec_gather is not None:
                vec_gather.begin()
            gather.begin()
        for j in range(min(local, 3)):
            arrive(j)

    def run_ticks(start, stop):
        if gather is not None:
            lax.fori_loop(start, stop, lambda t, carry: (tick(t), carry)[1], 0)

    def ready():
        for line in lines:
            line.advance(1)
        if vec_gather is not None:
            turned = vec_gather.whole[0].reshape(width, vec_gather.whole.shape[-1]).T
            for layer in range(2):
                count = plan.vector_rows
                targets[1 + layer][0:count, :] = turned[layer * count : (layer + 1) * count, :]

    def project():
        xin = x_ref[...].astype(low)
        keys, queries = segment_codes(segc_ref[0], half_masks(low))
        for h in range(2):
            codes[0, h] = keys[h]
            codes[1, h] = queries[h]
        q_ref[...] = (dot_nn(xin, matrix(0)) + vec_ref[0:1, :]).astype(low)
        k_ref[...] = dot_nn(xin, matrix(1)).astype(low)
        value = dot_nn(xin, matrix(2)) + vec_ref[1:2, :]
        v_ref[...] = value.astype(low)
        turned = value.T.astype(low)
        for h in range(width // HD):
            vt[h, 0:HD] = turned[h * HD : (h + 1) * HD]
            vt[h, HD : HD + 16] = jnp.ones((16, turned.shape[1]), low)

    def pair_step(p):
        masks = half_masks(low)
        lanes = pl.ds(pl.multiple_of(p * PAIR, PAIR), PAIR)
        q_pair = q_ref[:, lanes] * jnp.asarray(HD ** (-0.5), low)
        k_pair = k_ref[:, lanes]
        for h in range(2):
            scores = dot_nt(k_pair * masks[h] + codes[0, h], q_pair * masks[h] + codes[1, h])
            largest = jnp.max(scores, axis=0, keepdims=True)
            expanded = jnp.exp(scores - largest)
            here = pl.ds(pl.multiple_of(p * PAIR + h * HD, HD), HD)
            product = dot_nn(vt[2 * p + h], expanded.astype(low))
            total = product[HD : HD + 1]
            ctxt_ref[here, :] = (product[0:HD] * (1.0 / total)).astype(low)
            lse_ref[0, pl.ds(2 * p + h, 1), :] = largest + jnp.log(total)

    def close_row():
        @pl.when(s == 0)
        def _():
            if local > 3:
                arrive(3)
            for line in lines:
                line.advance(2)

        context = ctxt_ref[...].astype(full).T.astype(low)
        attended = dot_nn(context, matrix(3)) + vec_ref[2:3, :]
        unit, inverse = norm_parts(x_ref[...].astype(full) + attended)
        x1_ref[...] = unit
        inv1_ref[...] = inverse
        normed = unit * vec_ref[3:4, :] + vec_ref[4:5, :]
        here = pl.ds(pl.multiple_of(s * rows_now, rows_now), rows_now)
        acc[here, :] = normed + vec_ref[5 + inner : 6 + inner, :]
        normed = normed.astype(low)
        n1_ref[...] = normed
        n1_all[here, :] = normed

    @pl.when(s < rows)
    def _():
        def position(n, carry):
            if gather is not None:
                here, which = looked_up(plan.row_positions, n)
                before = plan.lead + s * len(plan.row_positions) + which
                opening = (s == 0) & (n == 0)
                start = jnp.where(opening, 0, before)
                stop = jnp.where(opening, plan.lead, jnp.where(here, before + 1, before))
                run_ticks(start, stop)

                @pl.when(opening)
                def _():
                    ready()

            @pl.when(n == 0)
            def _():
                project()

            @pl.when((n >= 1) & (n <= pairs))
            def _():
                pair_step(n - 1)

            @pl.when(n == pairs + 1)
            def _():
                close_row()

            return carry

        lax.fori_loop(0, pairs + 2, position, 0)

    tile = tokens // 4
    starts, stops = plan.step_ticks(rows)

    @pl.when(s >= rows)
    def _():
        c = s - rows

        @pl.when(c == 0)
        def _():
            for j in range(4, local):
                arrive(j)
            for line in lines:
                line.advance(3)

        def token_step(i, carry):
            for half in range(2):
                here = pl.ds(pl.multiple_of((2 * i + half) * tile, tile), tile)
                value, slope = gelu_parts(dot_nn(n1_all[here, :], matrix(4 + 2 * c)) + vec_ref[pl.ds(5 + c, 1), :])
                active = value.astype(low)
                u_ref[here, :] = active
                gp_ref[here, :] = slope.astype(low)
                acc[here, :] += dot_nn(active, matrix(5 + 2 * c))
            return carry

        lax.fori_loop(0, 2, token_step, 0)

        @pl.when(c == inner - 1)
        def _():
            base = 5 + inner

            def last(i, carry):
                here = pl.ds(pl.multiple_of(i * tile, tile), tile)
                unit, inverse = norm_parts(acc[here, :])
                x2_ref[here, :] = unit
                inv2_ref[here, :] = inverse
                out_ref[here, :] = (
                    unit * vec_ref[base + 1 : base + 2, :] + vec_ref[base + 2 : base + 3, :]
                ).astype(out_ref.dtype)
                return carry

            lax.fori_loop(0, 4, last, 0)

        run_ticks(
            sum(n * (c == k).astype(jnp.int32) for k, n in enumerate(starts)),
            sum(n * (c == k).astype(jnp.int32) for k, n in enumerate(stops)),
        )

        @pl.when(c == inner - 1)
        def _():
            if gather is not None:
                for line in lines:
                    line.advance(plan.z_count)
                for i in range(gather.count):
                    keep(i).wait()


class ForwardPlan:
    def __init__(self, inner, local, blocks=None, numbers=(), vec_shard=None, vector_rows=0, lines=(), lead=0, row_positions=(), z_count=1):
        self.inner, self.local, self.lead, self.row_positions, self.z_count = inner, local, lead, row_positions, z_count
        self.vector_rows = vector_rows
        self.order = [0, 1, 2, 3]
        for c in range(inner):
            self.order += [4 + c, 4 + inner + c]
        self.numbers = list(numbers)
        self.gathered, self.group = len(self.numbers), 2
        self.vectors = vec_shard is not None
        self.lines = [(first, count) for _, first, count in lines]
        self.line_at = int(self.gathered > 0) + int(self.vectors)
        self.line_target_at = int(self.gathered > 0) + 2 * int(self.vectors)
        self.arguments, self.argument_specs, self.results, self.result_specs, self.scratch = [], [], [], [], []
        shape = jax.ShapeDtypeStruct
        if self.gathered:
            rows, width = blocks.shape[1:]
            groups = self.gathered // self.group
            self.arguments.append(blocks)
            self.argument_specs.append(IN_VMEM)
            self.results.append(shape((self.gathered, 4, 2, width // 8, width), low))
            self.result_specs.append(ANYWHERE)
            self.scratch += gather_scratch(groups, self.group, width // 8, width, z_count)
        if self.vectors:
            lanes = vec_shard.shape[3]
            self.arguments.append(vec_shard)
            self.argument_specs.append(IN_VMEM)
            for _ in range(2):
                self.results.append(shape((16, width), full))
                self.result_specs.append(pl.BlockSpec((16, width), lambda s: (0, 0)))
            self.scratch += gather_scratch(1, 1, width // 8, lanes, z_count, full)
        for basis, _, count in lines:
            self.arguments.append(basis)
            self.argument_specs.append(ANYWHERE)
            self.results.append(shape((z_count, count) + basis.shape[1:], low))
            self.result_specs.append(ANYWHERE)
        self.scratch += line_scratch(len(lines), z_count)
        if self.gathered:
            self.scratch.append(pltpu.SemaphoreType.DMA((self.gathered // self.group,)))
        if self.vectors:
            self.scratch.append(pltpu.VMEM((1, 4, 2, width // 8, lanes), full))
        if self.gathered:
            self.scratch.append(pltpu.VMEM((groups, self.group, 2 * rows, width // 2), low))

    def step_ticks(self, rows):
        now, starts, stops = self.lead + rows * len(self.row_positions), [], []
        for c in range(self.inner):
            starts.append(now)
            if not self.gathered:
                stops.append(now)
                continue
            if c == self.inner - 1:
                now = max(now, self.gathered // self.group + CLOSE)
            else:
                now = max(now + 1, (5 + 2 * (c + 1) - self.local) // self.group + CLOSE + 1)
            stops.append(now)
        return starts, stops

    def split(self, refs):
        return split_refs(
            refs, 4, len(self.arguments), 13, len(self.results), 6, GATHER_REFS * bool(self.gathered),
            GATHER_REFS * self.vectors, 2 * bool(self.lines),
        )

    def vec_whole(self, refs):
        return refs[-2]

    def folded(self, refs):
        return refs[-1]


def scratch_tail(plan, refs):
    return refs[-3] if plan.vectors else refs[-2]


def forward_layer(hidden, seg_column, vectors, weights, out_dtype, plan, identity=None):
    tokens, width = hidden.shape
    inner = plan.inner
    wide = width * inner
    rows = tokens // L
    heads = width // HD
    shape = jax.ShapeDtypeStruct

    def here(s):
        return jnp.minimum(s, rows - 1)

    def column(s):
        return jnp.maximum(s - rows, 0)

    def row_block(columns):
        return pl.BlockSpec((L, columns), lambda s: (here(s), 0))

    def whole(columns):
        return pl.BlockSpec((tokens, columns), lambda s: (0, 0), pipeline_mode=pl.Buffered(1))

    wide_block = pl.BlockSpec((tokens, width), lambda s: (0, column(s)))
    out_shape = (
        shape((tokens, width), low), shape((tokens, width), low), shape((tokens, width), low),
        shape((width, tokens), low), shape((rows, heads, L), full),
        shape((tokens, width), full), shape((tokens, 1), full), shape((tokens, width), low),
        shape((tokens, wide), low), shape((tokens, wide), low),
        shape((tokens, width), full), shape((tokens, 1), full), shape((tokens, width), out_dtype),
        *plan.results,
    )
    out_specs = (
        row_block(width), row_block(width), row_block(width),
        pl.BlockSpec((width, L), lambda s: (0, here(s))), pl.BlockSpec((1, heads, L), lambda s: (here(s), 0, 0)),
        row_block(width), row_block(1), row_block(width),
        wide_block, wide_block,
        whole(width), whole(1), whole(width),
        *plan.result_specs,
    )
    total = 4 + 2 * inner
    held = max(total, plan.local + plan.gathered)
    return pl.pallas_call(
        functools.partial(forward_kernel, plan),
        grid=(rows + inner,),
        out_shape=out_shape,
        in_specs=[
            row_block(width),
            pl.BlockSpec((1, L, 1), lambda s: (here(s), 0, 0)),
            pl.BlockSpec(vectors.shape, lambda s: (0, 0)),
            ANYWHERE,
            *plan.argument_specs,
        ],
        out_specs=out_specs,
        scratch_shapes=[
            pltpu.VMEM((held, 4, 2, width // 8, width), low),
            pltpu.VMEM((2, 2, L, PAIR), low),
            pltpu.VMEM((heads, HD + 16, L), low),
            pltpu.VMEM((tokens, width), low),
            pltpu.VMEM((tokens, width), full),
            pltpu.SemaphoreType.DMA((total,)),
            *plan.scratch,
        ],
        compiler_params=pltpu.CompilerParams(
            dimension_semantics=("arbitrary",), vmem_limit_bytes=62 * MIB,
            collective_id=identity, has_side_effects=identity is not None,
        ),
        cost_estimate=pl.CostEstimate(
            flops=2 * tokens * width * width * total + 4 * tokens * L * width,
            bytes_accessed=40 * MIB,
            transcendentals=tokens * (L * heads + wide),
        ),
        name="layer_forward",
    )(hidden, seg_column, vectors, weights.reshape(-1, 4, 2, width // 8, width), *plan.arguments)


WIDE_STEP_TICKS = 5


def wide_ready(own):
    return [WIDE_STEP_TICKS * (n // 2) + 4 + n % 2 for n in range(own)]


def wide_back_kernel(plan, inner, *refs):
    inputs, sources, outputs, targets, scratch, sum_refs, line_refs = plan.split(refs, 11, 4, 11)
    up_hbm, x2_hbm, inv2_hbm, x1_hbm, inv1_hbm, n1_hbm, vec_ref, wup_ref, wdown_ref, u_ref, gp_ref = inputs
    dw_ref, dr1_ref, da_ref, dvec_ref = outputs
    n1t, dz, kept_dw, up_ref, x2_ref, inv2_ref, x1_ref, inv1_ref, n1_ref, tile_sem, load_sem = scratch
    dy, dn1 = da_ref, dr1_ref
    c = pl.program_id(0)
    steps = pl.num_programs(0)
    tokens, width = dn1.shape
    tile = tokens // 4
    base = 5 + inner
    side = Side(plan, sources, targets, sum_refs, line_refs, kept_dw)

    def tile_copies(i):
        rows = pl.ds(pl.multiple_of(i * tile, tile), tile)
        return [
            pltpu.make_async_copy(source.at[rows], target.at[rows], tile_sem.at[n, i])
            for n, (source, target) in enumerate(((up_hbm, up_ref), (x2_hbm, x2_ref), (inv2_hbm, inv2_ref)))
        ]

    late_copies = [
        pltpu.make_async_copy(source, target, load_sem.at[n])
        for n, (source, target) in enumerate(((n1_hbm, n1_ref), (x1_hbm, x1_ref), (inv1_hbm, inv1_ref)))
    ]

    @pl.when(c == 0)
    def _():
        for i in range(4):
            for copy in tile_copies(i):
                copy.start()
        for copy in late_copies:
            copy.start()

    side.enter(c == 0)

    def prepare():
        gain = vec_ref[base + 1 : base + 2, :]

        def body(i, carry):
            for copy in tile_copies(i):
                copy.wait()
            gain_sum, shift_sum, bias_sum = carry
            rows = pl.ds(pl.multiple_of(i * tile, tile), tile)
            upstream = up_ref[rows, :].astype(full)
            unit = x2_ref[rows, :]
            back = norm_back(upstream, unit, inv2_ref[rows, :], gain)
            dn1[rows, :] = back
            branch = back.astype(low)
            dy[rows, :] = branch
            return (
                gain_sum + column_sum(upstream * unit),
                shift_sum + column_sum(upstream),
                bias_sum + column_sum(branch.astype(full)),
            )

        zero = jnp.zeros((1, width), full)
        gain_sum, shift_sum, bias_sum = lax.fori_loop(0, 4, body, (zero, zero, zero))
        dvec_ref[...] = jnp.zeros(dvec_ref.shape, full)
        dvec_ref[base : base + 1, :] = bias_sum
        dvec_ref[base + 1 : base + 2, :] = gain_sum
        dvec_ref[base + 2 : base + 3, :] = shift_sum
        late_copies[0].wait()
        n1t[...] = n1_ref[...].astype(full).T.astype(low)

    def token_pair(i):
        bias_sum = jnp.zeros((1, width), full)
        for half in range(2):
            rows = pl.ds(pl.multiple_of((2 * i + half) * tile, tile), tile)
            slope = gp_ref[rows, :].astype(full)
            piece = (dot_nt(dy[rows, :], wdown_ref[0]) * slope).astype(low)
            dz[rows, :] = piece
            dn1[rows, :] += dot_nt(piece, wup_ref[0])
            bias_sum = bias_sum + column_sum(piece.astype(full))
        dvec_ref[pl.ds(5 + c, 1), :] += bias_sum

    def store(k, product):
        if plan.own:
            @pl.when(2 * c + k < plan.own)
            def _():
                kept_dw[2 * c + k] = product().reshape(kept_dw.shape[1:])

            @pl.when(2 * c + k >= plan.own)
            def _():
                dw_ref[k, 0] = product()
        else:
            dw_ref[k, 0] = product()

    def position(n, carry):
        side.tick(WIDE_STEP_TICKS * c + n)
        side.advance((c == 1) & (n == 1), 2)
        side.advance((c == 2) & (n == 4), 3)

        @pl.when((n == 0) & (c == 0))
        def _():
            prepare()

        @pl.when((n == 1) | (n == 2))
        def _():
            token_pair(n - 1)

        @pl.when(n == 3)
        def _():
            store(0, lambda: dot_nn(n1t[...], dz[...]).astype(low))

        @pl.when(n == 4)
        def _():
            store(1, lambda: dot_tn(u_ref[...], dy[...]).astype(low))

        return carry

    lax.fori_loop(0, WIDE_STEP_TICKS, position, 0)
    @pl.when(c == steps - 1)
    def _():
        for copy in late_copies[1:]:
            copy.wait()
        gain = vec_ref[3:4, :]

        def body(i, carry):
            gain_sum, shift_sum, bias_sum = carry
            rows = pl.ds(pl.multiple_of(i * tile, tile), tile)
            upstream = dn1[rows, :]
            unit = x1_ref[rows, :]
            back = norm_back(upstream, unit, inv1_ref[rows, :], gain)
            dr1_ref[rows, :] = back
            branch = back.astype(low)
            da_ref[rows, :] = branch
            return (
                gain_sum + column_sum(upstream * unit),
                shift_sum + column_sum(upstream),
                bias_sum + column_sum(branch.astype(full)),
            )

        zero = jnp.zeros((1, width), full)
        gain_sum, shift_sum, bias_sum = lax.fori_loop(0, 4, body, (zero, zero, zero))
        dvec_ref[2:3, :] = bias_sum
        dvec_ref[3:4, :] = gain_sum
        dvec_ref[4:5, :] = shift_sum

    side.leave(c == steps - 1, WIDE_STEP_TICKS * inner)


def wide_back(upstream, kept, vectors, weights, places, plan, identity=None):
    x1, inv1, n1, u, gp, x2, inv2 = kept
    tokens, width = x1.shape
    up_start, down_start, stride = places
    inner = u.shape[1] // width
    shape = jax.ShapeDtypeStruct

    return pl.pallas_call(
        functools.partial(wide_back_kernel, plan, inner),
        grid=(inner,),
        out_shape=(
            shape((2, inner - plan.own // 2, width, width), low),
            shape((tokens, width), full), shape((tokens, width), low), shape((16, width), full),
            *plan.results,
        ),
        in_specs=[
            *[ANYWHERE] * 6,
            pl.BlockSpec(vectors.shape, lambda c: (0, 0), pipeline_mode=pl.Buffered(1)),
            pl.BlockSpec((1, width, width), lambda c: (up_start + stride * c, 0, 0)),
            pl.BlockSpec((1, width, width), lambda c: (down_start + stride * c, 0, 0)),
            pl.BlockSpec((tokens, width), lambda c: (0, c)),
            pl.BlockSpec((tokens, width), lambda c: (0, c)),
            *plan.argument_specs,
        ],
        out_specs=(
            pl.BlockSpec((2, 1, width, width), lambda c: (0, jnp.maximum(c - plan.own // 2, 0), 0, 0)),
            pl.BlockSpec((tokens, width), lambda c: (0, 0), pipeline_mode=pl.Buffered(1)),
            pl.BlockSpec((tokens, width), lambda c: (0, 0), pipeline_mode=pl.Buffered(1)),
            pl.BlockSpec((16, width), lambda c: (0, 0)),
            *plan.result_specs,
        ),
        scratch_shapes=[
            pltpu.VMEM((width, tokens), low),
            pltpu.VMEM((tokens, width), low),
            pltpu.VMEM((plan.own, 4, 2, width // 8, width) if plan.own else (8, 128), low),
            pltpu.VMEM((tokens, width), upstream.dtype),
            pltpu.VMEM((tokens, width), full),
            pltpu.VMEM((tokens, 1), full),
            pltpu.VMEM((tokens, width), full),
            pltpu.VMEM((tokens, 1), full),
            pltpu.VMEM((tokens, width), low),
            pltpu.SemaphoreType.DMA((3, 4)),
            pltpu.SemaphoreType.DMA((3,)),
            *plan.scratch,
        ],
        compiler_params=pltpu.CompilerParams(
            dimension_semantics=("arbitrary",), vmem_limit_bytes=60 * MIB,
            collective_id=identity, has_side_effects=identity is not None,
        ),
        cost_estimate=pl.CostEstimate(
            flops=8 * tokens * width * width * inner, bytes_accessed=50 * MIB, transcendentals=0
        ),
        name="wide_backward",
    )(upstream, x2, inv2, x1, inv1, n1, vectors, weights, weights, u, gp, *plan.arguments)


def attend_back_kernel(plan, *refs):
    inputs, sources, outputs, targets, scratch, sum_refs, line_refs = plan.split(refs, 10, 3, 12)
    da_hbm, dr1_ref, x_ref, q_ref, k_ref, v_ref, ctxt_hbm, lse_ref, segc_ref, w_hbm = inputs
    dw_ref, dx_ref, dvec_ref = outputs
    codes, dctx, kt, delta, dqt, xt, grads, dwo, da_ref, ctxt_ref, w_ref, load_sem = scratch
    r = pl.program_id(0)
    loads = [
        pltpu.make_async_copy(w_hbm.at[plan.start + 3], w_ref.at[3], load_sem.at[0]),
        pltpu.make_async_copy(da_hbm, da_ref, load_sem.at[1]),
        pltpu.make_async_copy(ctxt_hbm, ctxt_ref, load_sem.at[2]),
        pltpu.make_async_copy(w_hbm.at[pl.ds(plan.start, 3)], w_ref.at[pl.ds(0, 3)], load_sem.at[3]),
    ]

    @pl.when(r == 0)
    def _():
        for copy in loads:
            copy.start()

    side = Side(plan, sources, targets, sum_refs, line_refs, dwo)
    side.enter(r == 0)
    tokens, width = dr1_ref.shape
    pairs = width // PAIR
    ticks = pairs + 5
    here = pl.ds(pl.multiple_of(r * tokens, tokens), tokens)
    masks = half_masks(low)
    scale = HD ** (-0.5)
    last_row = pl.num_programs(0) - 1

    def prepare():
        @pl.when(r == 0)
        def _():
            for copy in loads[:3]:
                copy.wait()
            grad = dot_nn(ctxt_ref[...], da_ref[...]).astype(low)
            if plan.own:
                dwo[0] = grad.reshape(dwo.shape[1:])
            else:
                dw_ref[3] = grad
            dvec_ref[...] = jnp.zeros(dvec_ref.shape, full)

        xt[:, here] = x_ref[...].astype(low).astype(full).T.astype(low)
        keys, queries = segment_codes(segc_ref[0], masks)
        for h in range(2):
            codes[0, h] = keys[h]
            codes[1, h] = queries[h]
        context_grad = dot_nt(da_ref[here, :], w_ref[3]).astype(low)
        dctx[...] = context_grad
        kt[...] = k_ref[...].astype(full).T.astype(low)
        products = context_grad.astype(full) * ctxt_ref[:, here].astype(full).T
        feature = lax.broadcasted_iota(jnp.int32, (16, width), 1)
        head = lax.broadcasted_iota(jnp.int32, (16, width), 0)
        member = ((feature >= head * HD) & (feature < (head + 1) * HD)).astype(full).astype(low)
        high = products.astype(low)
        rest = (products - high.astype(full)).astype(low)
        delta[...] = dot_nt(member, high) + dot_nt(member, rest)

    def pair_step(p):
        lanes = pl.ds(pl.multiple_of(p * PAIR, PAIR), PAIR)
        q_pair = q_ref[:, lanes] * jnp.asarray(scale, low)
        k_pair = k_ref[:, lanes]
        v_pair = v_ref[:, lanes]
        g_pair = dctx[:, lanes]
        key_grad = jnp.zeros((tokens, PAIR), full)
        value_grad = jnp.zeros((tokens, PAIR), full)
        for h in range(2):
            q_half = q_pair * masks[h]
            g_half = g_pair * masks[h]
            scores = dot_nt(k_pair * masks[h] + codes[0, h], q_half + codes[1, h])
            attention = jnp.exp(scores - lse_ref[0, pl.ds(2 * p + h, 1), :]).astype(low)
            value_grad = value_grad + dot_nn(attention, g_half)
            attention_grad = dot_nt(v_pair, g_half)
            score_grad = attention * (attention_grad - delta[pl.ds(2 * p + h, 1), :]).astype(low)
            key_grad = key_grad + dot_nn(score_grad, q_half)
            rows = pl.ds(pl.multiple_of(p * PAIR + h * HD, HD), HD)
            dqt[rows, :] = dot_nn(kt[rows, :], score_grad) * scale
        grads[1, here, lanes] = key_grad.astype(low)
        grads[2, here, lanes] = value_grad.astype(low)

    def inputs_step():
        @pl.when(r == 0)
        def _():
            loads[3].wait()

        query_grad = dqt[...].T.astype(low)
        grads[0, here, :] = query_grad
        value_grad = grads[2, here, :]
        dx_ref[...] = (
            dr1_ref[...]
            + dot_nt(query_grad, w_ref[0])
            + dot_nt(grads[1, here, :], w_ref[1])
            + dot_nt(value_grad, w_ref[2])
        )
        dvec_ref[0:1, :] += column_sum(query_grad.astype(full))
        dvec_ref[1:2, :] += column_sum(value_grad.astype(full))

    def position(n, carry):
        side.tick(r * ticks + n)
        side.advance((r == 0) & (n == 6), 2)
        side.advance((r == 1) & (n == 4), 3)

        @pl.when(n == 0)
        def _():
            prepare()

        @pl.when((n >= 1) & (n <= pairs))
        def _():
            pair_step(n - 1)

        @pl.when(n == pairs + 1)
        def _():
            inputs_step()

        @pl.when((n > pairs + 1) & (r == last_row))
        def _():
            j = n - (pairs + 2)
            dw_ref[j] = dot_nn(xt[...], grads[j]).astype(low)

        return carry

    lax.fori_loop(0, ticks, position, 0)
    side.leave(r == last_row, plan.rows * ticks)


def attend_back(da, dr1, hidden, kept, seg_column, weights, start, plan, identity=None):
    q, k, v, ctxt, lse = kept
    tokens, width = da.shape
    rows = tokens // L
    heads = width // HD
    shape = jax.ShapeDtypeStruct
    plan.start, plan.rows = start, rows

    def row_block():
        return pl.BlockSpec((L, width), lambda r: (r, 0))

    return pl.pallas_call(
        functools.partial(attend_back_kernel, plan),
        grid=(rows,),
        out_shape=(
            shape((4 - plan.own, width, width), low), shape((tokens, width), full), shape((8, width), full),
            *plan.results,
        ),
        in_specs=[
            ANYWHERE,
            row_block(), row_block(), row_block(), row_block(), row_block(),
            ANYWHERE,
            pl.BlockSpec((1, heads, L), lambda r: (r, 0, 0)),
            pl.BlockSpec((1, L, 1), lambda r: (r, 0, 0)),
            ANYWHERE,
            *plan.argument_specs,
        ],
        out_specs=(
            pl.BlockSpec((4 - plan.own, width, width), lambda r: (0, 0, 0), pipeline_mode=pl.Buffered(1)),
            row_block(),
            pl.BlockSpec((8, width), lambda r: (0, 0)),
            *plan.result_specs,
        ),
        scratch_shapes=[
            pltpu.VMEM((2, 2, L, PAIR), low),
            pltpu.VMEM((L, width), low),
            pltpu.VMEM((width, L), low),
            pltpu.VMEM((16, L), full),
            pltpu.VMEM((width, L), full),
            pltpu.VMEM((width, tokens), low),
            pltpu.VMEM((3, tokens, width), low),
            pltpu.VMEM((1, 4, 2, width // 8, width) if plan.own else (8, 128), low),
            pltpu.VMEM((tokens, width), low),
            pltpu.VMEM((width, tokens), low),
            pltpu.VMEM((4, width, width), low),
            pltpu.SemaphoreType.DMA((4,)),
            *plan.scratch,
        ],
        compiler_params=pltpu.CompilerParams(
            dimension_semantics=("arbitrary",), vmem_limit_bytes=60 * MIB,
            collective_id=identity, has_side_effects=identity is not None,
        ),
        cost_estimate=pl.CostEstimate(
            flops=16 * tokens * width * width + 10 * tokens * L * width,
            bytes_accessed=30 * MIB,
            transcendentals=tokens * L * heads,
        ),
        name="attend_backward",
    )(da, dr1, hidden, q, k, v, ctxt, lse, seg_column, weights, *plan.arguments)


def moments(rotated, first, second):
    first_new = beta_one * first + (1.0 - beta_one) * rotated
    second_new = beta_two * second + (1.0 - beta_two) * rotated * rotated
    direction = (
        first_new
        / (1.0 - beta_one**STEP)
        / (jnp.sqrt(second_new / (1.0 - beta_two**STEP)) + adam_epsilon)
    )
    return first_new, second_new, direction


def pack_lanes(piece):
    rows = piece.shape[0] // 2
    return jnp.concatenate([piece[:rows], piece[rows:]], axis=1)


def unpack_lanes(piece):
    columns = piece.shape[1] // 2
    return jnp.concatenate([piece[:, :columns], piece[:, columns:]], axis=0)


def optimizer_kernel(plan, *refs):
    spans = len(plan.spans)
    inputs, ready, dvecs, bases, lines_in, outputs, lines_out, scratch, sum_refs, vec_refs, line_refs = split_refs(
        refs, 6, plan.ready, plan.dvecs, plan.bases, spans, 5, spans, 21, SUM_REFS, SUM_REFS, 2 * bool(spans)
    )
    index_ref, place_ref, tail_hbm, first_hbm, second_hbm, blocks = inputs
    new_ref, low_ref, first_out, second_out, vec_out = outputs
    (store, left, right, first_in, second_in, g_out, g_in, t_out, t_in, e_out, e_in, w_out, w_in, vec_source,
     load_sem, g_sem, t_sem, e_sem, w_sem, left_sem, right_sem) = scratch
    slots, owners = g_in.shape[0], g_in.shape[1]
    z_count = t_in.shape[1]
    place = Place(z_count)
    dp, z = place.dp, place.z
    dps = [lax.rem(dp + d, owners) for d in range(owners)]
    count = blocks.shape[0]
    many = tail_hbm.shape[0]
    tail_times = [[many * stage + n for n in range(many)] for stage in range(5)]
    tail = BlockSum(place, [tail_hbm], sum_refs, tail_times)
    vec = BlockSum(place, [vec_source], vec_refs, [[many * stage + 1] for stage in range(5)])
    order = plan.free + [s for s in range(slots) if s not in plan.free]
    lines = line_gathers(place, plan.spans, lines_in, lines_out, line_refs, z_count)
    every = list(bases) + list(lines_out)
    late = [s for s in range(slots) if plan.left_map[s][0] >= len(bases)]

    def load(refs_map, target, sem, s):
        n, at = refs_map[s]
        return pltpu.make_async_copy(every[n].at[:, at], target.at[:, s], sem.at[s])

    def load_first(s):
        return pltpu.make_async_copy(first_hbm.at[s], first_in.at[s], load_sem.at[0, s])

    def load_second(s):
        return pltpu.make_async_copy(second_hbm.at[s], second_in.at[s], load_sem.at[1, s])

    for s in order:
        load(plan.right_map, right, right_sem, s).start()
        if s not in late:
            load(plan.left_map, left, left_sem, s).start()
        load_first(s).start()
        load_second(s).start()
    greet([(other, z) for other in dps[1:]] + place.z_partners())
    start = many
    for part in ready:
        store[start : start + part.shape[0]] = part[...]
        start += part.shape[0]
    store[0:many] = jnp.zeros((many,) + store.shape[1:], low)
    store[count] = jnp.zeros(store.shape[1:], low)
    rows = plan.vector_rows
    stacked = jnp.concatenate(
        [dvecs[0][0:2, :], dvecs[1][2:rows, :], dvecs[2][0:2, :], dvecs[3][2:rows, :],
         jnp.zeros((vec_source.shape[-1] - 2 * rows, blocks.shape[2]), full)], axis=0
    )
    vec_source[0] = stacked.T.reshape(vec_source.shape[1:])

    def g_copy(s, d):
        other = dps[d]
        return remote(g_out.at[s, d], g_in.at[s, dp], g_sem.at[0, s, d], g_sem.at[1, s, owners - d], (other, z))

    def t_copy(s, d):
        other = place.zs[d]
        return remote(t_out.at[s, d], t_in.at[s, z], t_sem.at[0, s, d], t_sem.at[1, s, z_count - d], (dp, other))

    def e_copy(s, d):
        other = place.zs[d]
        return remote(e_out.at[s, d], e_in.at[s, z], e_sem.at[0, s, d], e_sem.at[1, s, z_count - d], (dp, other))

    def w_copy(s, d):
        other = dps[d]
        return remote(
            w_out.at[s, other], w_in.at[s * owners + dp], w_sem.at[0, s, d], w_sem.at[1, s, owners - d], (other, z)
        )

    def send_out(s):
        for d in range(1, owners):
            g_out[s, d] = store[index_ref[s * owners + dps[d]]]
            g_copy(s, d).start()
        g_in[s, dp] = store[index_ref[s * owners + dp]]

    def turn(s):
        for d in range(1, owners):
            g_copy(s, d).wait()
        load(plan.right_map, right, right_sem, s).wait()
        grad = jnp.concatenate([unfold(g_in[s, c].astype(full)) for c in range(owners)], axis=0).astype(low)
        for d in range(1, z_count):
            t_out[s, d] = pack_lanes(dot_nt(right[place.zs[d], s], grad)).astype(low)
            t_copy(s, d).start()
        t_in[s, z] = pack_lanes(dot_nt(right[z, s], grad)).astype(low)

    def adapt(s):
        for d in range(1, z_count):
            t_copy(s, d).wait()
        load_first(s).wait()
        load_second(s).wait()
        load(plan.left_map, left, left_sem, s).wait()
        rotated = jnp.zeros(first_in.shape[1:], full)
        for f in range(z_count):
            rotated = rotated + dot_nn(unpack_lanes(t_in[s, f].astype(full)).astype(low), left[f, s])
        first_new, second_new, direction = moments(rotated, first_in[s], second_in[s])
        first_out[s] = first_new
        second_out[s] = second_new
        direction = direction.astype(low)
        for d in range(1, z_count):
            e_out[s, d] = pack_lanes(dot_nt(left[place.zs[d], s], direction)).astype(low)
            e_copy(s, d).start()
        e_in[s, z] = pack_lanes(dot_nt(left[z, s], direction)).astype(low)

    def step_back(s):
        for d in range(1, z_count):
            e_copy(s, d).wait()
        step = jnp.zeros((left.shape[2], left.shape[3]), full)
        for f in range(z_count):
            step = step + dot_nn(unpack_lanes(e_in[s, f].astype(full)).astype(low), right[f, s])
        share = step.shape[0] // owners
        for c in range(owners):
            w_out[s, c] = fold(step[c * share : (c + 1) * share]).astype(low)
        for d in range(1, owners):
            w_copy(s, d).start()
        w_in[s * owners + dp] = w_out[s, dp]

    def sums(stage):
        for t in range(many * stage, many * (stage + 1)):
            tail.tick(t)
            vec.tick(t)

    free = plan.free
    def advance(hop):
        for line in lines:
            line.advance(hop)

    sums(0)
    advance(1)
    for s in free:
        send_out(s)
    sums(1)
    for s in free:
        turn(s)
    sums(2)
    advance(2)
    for s in free:
        adapt(s)
    sums(3)
    sums(4)
    advance(3)
    for i in range(many):
        store[i] = tail.finish(i).astype(low)
    rest = order[len(free) :]
    for s in rest[:2]:
        send_out(s)
    for s in free:
        step_back(s)
    advance(z_count)
    for s in late:
        load(plan.left_map, left, left_sem, s).start()
    for k in range(len(rest) + 2):
        if k < len(rest):
            turn(rest[k])
            if k + 2 < len(rest):
                send_out(rest[k + 2])
        if 0 <= k - 1 < len(rest):
            adapt(rest[k - 1])
        if 0 <= k - 2 < len(rest):
            step_back(rest[k - 2])

    vec_out[...] = vec.finish(0)
    for s in range(slots):
        for d in range(1, owners):
            w_copy(s, d).wait()

    def block_step(b, carry):
        step = unfold(w_in[place_ref[b]].astype(full))
        block = blocks[b]
        new = block - matrix_rate * (step + weight_decay * block)
        new_ref[b] = new
        low_ref[b] = new.astype(low)
        return carry

    lax.fori_loop(0, count, block_step, 0)


class OptimizerPlan:
    def __init__(self, ready, dvecs, bases, spans, left_map, right_map, free, vector_rows):
        self.ready, self.dvecs, self.bases, self.spans = ready, dvecs, bases, spans
        self.left_map, self.right_map, self.free, self.vector_rows = left_map, right_map, free, vector_rows


def optimizer(
    index, places, tail, ready, dvecs, vector_rows, bases, lines, left_map, right_map, free, first, second, blocks,
    z_count, identity,
):
    slots, columns, width = first.shape
    owners = index.shape[0] // slots
    count, rows = blocks.shape[0], blocks.shape[1]
    span = bases[0].shape[2]
    lanes = 128
    shape = jax.ShapeDtypeStruct
    piece = (2 * rows, width // 2)
    tile = (span // 2, 2 * columns)
    smem = pl.BlockSpec(memory_space=pltpu.SMEM)
    spans = [(first_slot, amount) for _, first_slot, amount in lines]
    plan = OptimizerPlan(len(ready), len(dvecs), len(bases), spans, left_map, right_map, free, vector_rows)
    line_shapes = [shape((z_count, amount) + basis.shape[1:], low) for basis, _, amount in lines]
    return pl.pallas_call(
        functools.partial(optimizer_kernel, plan),
        out_shape=(
            shape(blocks.shape, full), shape(blocks.shape, low), shape(first.shape, full), shape(first.shape, full),
            shape((rows, lanes), full), *line_shapes,
        ),
        in_specs=[smem, smem, ANYWHERE, ANYWHERE, ANYWHERE, IN_VMEM]
        + [IN_VMEM] * (len(ready) + len(dvecs)) + [ANYWHERE] * (len(bases) + len(lines)),
        out_specs=(IN_VMEM,) * 5 + (ANYWHERE,) * len(lines),
        scratch_shapes=[
            pltpu.VMEM((count + 1,) + piece, low),
            pltpu.VMEM((z_count, slots, span, width), low),
            pltpu.VMEM((z_count, slots, columns, width), low),
            pltpu.VMEM((slots, columns, width), full),
            pltpu.VMEM((slots, columns, width), full),
            pltpu.VMEM((slots, owners) + piece, low),
            pltpu.VMEM((slots, owners) + piece, low),
            pltpu.VMEM((slots, z_count) + tile, low),
            pltpu.VMEM((slots, z_count) + tile, low),
            pltpu.VMEM((slots, z_count) + tile, low),
            pltpu.VMEM((slots, z_count) + tile, low),
            pltpu.VMEM((slots, owners) + piece, low),
            pltpu.VMEM((slots * owners,) + piece, low),
            pltpu.VMEM((1, owners // 2, 2, width // owners, lanes), full),
            pltpu.SemaphoreType.DMA((2, slots)),
            pltpu.SemaphoreType.DMA((2, slots, owners)),
            pltpu.SemaphoreType.DMA((2, slots, z_count)),
            pltpu.SemaphoreType.DMA((2, slots, z_count)),
            pltpu.SemaphoreType.DMA((2, slots, owners)),
            pltpu.SemaphoreType.DMA((slots,)),
            pltpu.SemaphoreType.DMA((slots,)),
            *sum_scratch(tail.shape[0], tail.shape[3], width, z_count),
            *sum_scratch(1, width // owners, lanes, z_count, full),
            *line_scratch(len(lines), z_count),
        ],
        compiler_params=pltpu.CompilerParams(
            vmem_limit_bytes=60 * MIB, collective_id=identity, has_side_effects=True
        ),
        cost_estimate=pl.CostEstimate(
            flops=8 * slots * span * width * width, bytes_accessed=40 * MIB, transcendentals=slots * width * columns
        ),
        name="optimizer",
    )(index, places, tail, first, second, blocks, *ready, *dvecs, *bases, *[basis for basis, _, _ in lines])


def slot_table(owner, slots, owner_rows):
    block_count = owner.shape[0]
    same_owner = owner[:, None] == owner[None, :]
    ordering = jnp.arange(block_count, dtype=jnp.int32)
    earlier = ordering[None, :] < ordering[:, None]
    ranking = jnp.sum(jnp.where(same_owner & earlier, 1, 0), axis=1).astype(jnp.int32)
    owner_match = owner[None, :] == jnp.arange(owner_rows, dtype=jnp.int32)[:, None]
    slot_match = ranking[None, :] == jnp.arange(slots, dtype=jnp.int32)[:, None]
    return jnp.where(slot_match[:, None, :] & owner_match[None, :, :], 1.0, 0.0).astype(full)


def scatter_sum(grads):
    blocks, width = grads.shape[0], grads.shape[2]
    cut = grads.reshape(blocks, lax.axis_size("dp"), -1, width).transpose(1, 0, 2, 3)
    outer = lax.psum_scatter(cut, "dp", scatter_dimension=0, tiled=False)
    blocks, rows, width = outer.shape
    count = lax.axis_size("fsdp")
    cut = outer.reshape(blocks, count, rows // count, width).transpose(1, 0, 2, 3)
    return lax.psum_scatter(cut, "fsdp", scatter_dimension=0, tiled=False)


def scatter_vectors(grads):
    rows, width = grads.shape
    count = lax.axis_size("dp") * lax.axis_size("fsdp")
    cut = grads.reshape(rows, count, width // count).transpose(1, 0, 2)
    return lax.psum_scatter(cut, ("dp", "fsdp"), scatter_dimension=0, tiled=False)


def gathering_program(
    tokens, segment, blocks, vectors, owner, left_basis, right_basis, rot_first, rot_second, cotangent, z_count
):
    layers, vector_rows = vectors.shape[:2]
    count, shard_rows, width = blocks.shape
    per_layer = count // layers
    inner = (per_layer - 4) // 2
    owners = lax.axis_size("dp")
    slots = rot_first.shape[0]
    part = width // owners
    lanes = 128
    seg_column = segment[:, :, None]

    order = [0, 1, 2, 3]
    for c in range(inner):
        order += [4 + c, 4 + inner + c]
    head = order + [per_layer + j for j in order[:4]]
    rest = [per_layer + j for j in order[4:]]
    vec_shard = vectors.astype(low).astype(full).reshape(layers * vector_rows, shard_rows).T
    vec_shard = jnp.pad(vec_shard, ((0, 0), (0, lanes - layers * vector_rows)))[None, None]
    left_low = left_basis.reshape(slots, -1, width).astype(low)
    right_low = right_basis.transpose(0, 2, 1).astype(low)

    plan = ForwardPlan(
        inner, 0, blocks, head, vec_shard, vector_rows, [(right_low, 0, 2)], lead=5, row_positions=(1,), z_count=z_count
    )
    empty_vec = jnp.zeros((16, width), full)
    results = forward_layer(tokens, seg_column, empty_vec, jnp.zeros((1, width, width), low), full, plan, 6)
    kept_a = results[:12]
    hidden, weights_a, vec_a, vec_b, right_01 = results[12:]
    weights_a = weights_a.reshape(-1, width, width)
    plan = ForwardPlan(inner, 4, blocks, rest, lines=[(right_low, 2, 1)], lead=0, row_positions=(1, 4), z_count=z_count)
    plan.order = [per_layer + j for j in range(4)]
    results = forward_layer(hidden, seg_column, vec_b, weights_a, low, plan, 7)
    kept_b = results[:12]
    layer_out, weights_b, right_2 = results[12:]
    weights_b = weights_b.reshape(-1, width, width)

    def cut(grads):
        return grads.reshape(-1, owners // 2, 2, part, width)

    size = (part, width)
    own_b, own_a = 4, 3

    def left_over(own):
        return 2 * inner - own, own % 2

    plan = Plan(None, [(right_low, 3, 1)], z_count, own_b, size, wide_ready(own_b))
    dw_wide, dr1, da, dvec_wide_b, wide_sum_b, right_3 = wide_back(
        cotangent, kept_b[5:], vec_b, weights_b, (0, 1, 2), plan, 1
    )
    pending, skip = left_over(own_b)
    plan = Plan(cut(dw_wide), [(right_low, 4, 1), (left_low, 3, 1)], z_count, 1, size, list(range(pending + 1)), skip)
    dw_attend, upstream, dvec_attend_b, attend_sum_b, right_4, left_3 = attend_back(
        da, dr1, hidden, kept_b[:5], seg_column, weights_a, per_layer, plan, 2
    )
    plan = Plan(
        cut(dw_attend), [(left_low, 4, 1), (left_low, 0, 1)], z_count, own_a, size, [0, 1, 2] + wide_ready(own_a)
    )
    dw_wide, dr1, da, dvec_wide_a, wide_sum_a, left_4, left_0 = wide_back(
        upstream, kept_a[5:], vec_a, weights_a, (4, 5, 2), plan, 3
    )
    pending, skip = left_over(own_a)
    plan = Plan(cut(dw_wide), [(left_low, 1, 1)], z_count, 1, size, list(range(pending + 1)), skip)
    dw_attend, upstream, dvec_attend_a, attend_sum_a, left_1 = attend_back(
        da, dr1, tokens, kept_a[:5], seg_column, weights_a, 0, plan, 5
    )

    three = list(range(3))

    def early(own):
        return [4 + n // 2 + inner * (n % 2) for n in range(own)]

    def late(own):
        return [4 + c + inner * k for k in range(2) for c in range(inner) if 2 * c + k >= own] + [3]

    held_order = three + late(own_a) + [per_layer + j for j in three] + early(own_a)
    held_order += [per_layer + j for j in late(own_b) + early(own_b)]
    rank = jnp.asarray([held_order.index(j) for j in range(count)], jnp.int32)
    table = slot_table(owner, slots, owners).reshape(slots * owners, count)
    held = jnp.sum(table, axis=1)
    index = jnp.where(held > 0, jnp.sum(table * rank, axis=1), count).astype(jnp.int32)
    places = jnp.sum(table * jnp.arange(slots * owners, dtype=jnp.int32)[:, None], axis=0).astype(jnp.int32)
    bases = (right_01, right_2, right_3, right_4, left_0, left_1, left_3, left_4)
    right_map = [(0, 0), (0, 1), (1, 0), (2, 0), (3, 0)]
    left_map = [(4, 0), (5, 0), (8, 0), (6, 0), (7, 0)]
    free = list(range(3, slots))
    new_blocks, new_low, first_new, second_new, vec_sum, _ = optimizer(
        index, places, cut(dw_attend), (attend_sum_a, wide_sum_a, attend_sum_b, wide_sum_b),
        (dvec_attend_a, dvec_wide_a, dvec_attend_b, dvec_wide_b), vector_rows, bases, [(left_low, 2, 1)], left_map, right_map, free,
        rot_first.transpose(0, 2, 1), rot_second.transpose(0, 2, 1), blocks, z_count, 4,
    )
    first_new, second_new = first_new.transpose(0, 2, 1), second_new.transpose(0, 2, 1)
    vector_grad = vec_sum[:, : layers * vector_rows].T.reshape(layers, vector_rows, shard_rows)
    return layer_out, upstream, new_blocks, new_low, first_new, second_new, vector_grad


def plain_program(
    tokens, segment, blocks, vectors, owner, left_basis, right_basis, rot_first, rot_second, cotangent
):
    layers, vector_rows = vectors.shape[:2]
    per_layer = blocks.shape[0] // layers
    inner = (per_layer - 4) // 2
    width = blocks.shape[2]
    owner_rows = lax.axis_size("dp")
    slots = rot_first.shape[0]
    selector = slot_table(owner, slots, owner_rows)
    vector_parts = lax.all_gather(vectors.astype(low), ("dp", "fsdp"), axis=0, tiled=False)
    vector_full = vector_parts.transpose(1, 2, 0, 3).reshape(layers, vector_rows, width).astype(full)
    blocks_low, vector_full = lax.optimization_barrier((blocks.astype(low), vector_full))

    seg_column = segment[:, :, None]
    state = tokens
    kept = []
    for layer_index in range(layers):
        start = per_layer * layer_index
        weights = lax.all_gather(blocks_low[start : start + per_layer], ("dp", "fsdp"), axis=1, tiled=True)
        out_dtype = low if layer_index == layers - 1 else full
        results = forward_layer(
            state, seg_column, vector_full[layer_index], weights, out_dtype, ForwardPlan(inner, per_layer)
        )
        kept.append((state, weights, results[:5], results[5:12]))
        state = results[12]
    layer_out = state
    upstream = cotangent
    right_low = lax.all_gather(right_basis.astype(low), "fsdp", axis=2, tiled=True)
    block_shards = [None] * layers
    vector_shards = [None] * layers
    for layer_index in reversed(range(layers)):
        hidden, weights, attend_kept, wide_kept = kept[layer_index]
        dw_wide, dr1, da, dvec_wide = wide_back(
            upstream, wide_kept, vector_full[layer_index], weights, (4, 4 + inner, 1), Plan()
        )
        wide_shard = scatter_sum(dw_wide.reshape(-1, width, width))
        dw_attend, upstream, dvec_attend = attend_back(
            da, dr1, hidden, attend_kept, seg_column, weights, 0, Plan()
        )
        dvec = jnp.concatenate([dvec_attend[:2], dvec_wide[2:vector_rows]], axis=0)
        block_shards[layer_index] = jnp.concatenate([scatter_sum(dw_attend), wide_shard], axis=0)
        vector_shards[layer_index] = scatter_vectors(dvec)
    vector_grad = jnp.stack(vector_shards)
    block_grad = jnp.concatenate(block_shards, axis=0)
    outgoing = jnp.einsum("srk,kid->srid", selector.astype(low), block_grad, preferred_element_type=full)
    incoming = lax.all_to_all(outgoing.astype(low), "dp", split_axis=1, concat_axis=1, tiled=True)
    owned = incoming.reshape(slots, -1, width)
    turned = jnp.einsum("sik,skj->sij", owned, right_low, preferred_element_type=full).astype(low)
    left_rows = left_basis.reshape(slots, -1, width).astype(low)
    partial_sums = jnp.einsum("sra,srb->sab", left_rows, turned, preferred_element_type=full)
    rotated = lax.psum_scatter(
        partial_sums.astype(low), "fsdp", scatter_dimension=2, tiled=True
    ).astype(full)
    first_new, second_new, direction = moments(rotated, rot_first, rot_second)
    direction_full = lax.all_gather(direction.astype(low), "fsdp", axis=2, tiled=True)
    back_right = jnp.einsum("sab,scb->sac", direction_full, right_low, preferred_element_type=full)
    step_rows = jnp.einsum(
        "sia,sac->sic", left_rows, back_right.astype(low), preferred_element_type=full
    )
    returned = lax.all_to_all(
        step_rows.reshape(slots, owner_rows, -1, width).astype(low),
        "dp",
        split_axis=1,
        concat_axis=1,
        tiled=True,
    )
    step_shard = jnp.einsum("srk,srid->kid", selector.astype(low), returned, preferred_element_type=full)
    new_blocks = blocks - matrix_rate * (step_shard + weight_decay * blocks)
    return layer_out, upstream, new_blocks, new_blocks.astype(low), first_new, second_new, vector_grad


def shards(
    tokens,
    segment,
    blocks,
    vectors,
    owner,
    left_basis,
    right_basis,
    rot_first,
    rot_second,
    vec_first,
    vec_second,
    cotangent,
):
    operands = (
        tokens, segment, blocks, vectors, owner, left_basis, right_basis, rot_first, rot_second, cotangent
    )
    z_count = lax.axis_size("fsdp")
    if lax.axis_size("dp") == 8 and z_count == 4:
        results = gathering_program(*operands, z_count)
    else:
        results = plain_program(*operands)
    layer_out, upstream, new_blocks, new_low, first_new, second_new, vector_grad = results
    vector_first = beta_one * vec_first + (1.0 - beta_one) * vector_grad
    vector_second = beta_two * vec_second + (1.0 - beta_two) * vector_grad * vector_grad
    vector_step = (
        vector_first
        / (1.0 - beta_one**STEP)
        / (jnp.sqrt(vector_second / (1.0 - beta_two**STEP)) + adam_epsilon)
    )
    vector_new = vectors - vector_rate * (vector_step + weight_decay * vectors)
    return (
        layer_out,
        upstream,
        new_blocks,
        new_low,
        first_new,
        second_new,
        vector_first,
        vector_second,
        vector_new,
    )


def solution(mesh):
    return jax.shard_map(
        shards,
        mesh=mesh,
        in_specs=(
            P(("dp", "fsdp"), None),
            P(("dp", "fsdp"), None),
            P(None, ("dp", "fsdp"), None),
            P(None, None, ("dp", "fsdp")),
            P(),
            P("dp", None, "fsdp", None),
            P("dp", None, "fsdp"),
            P("dp", None, "fsdp"),
            P("dp", None, "fsdp"),
            P(None, None, ("dp", "fsdp")),
            P(None, None, ("dp", "fsdp")),
            P(("dp", "fsdp"), None),
        ),
        out_specs=(
            P(("dp", "fsdp"), None),
            P(("dp", "fsdp"), None),
            P(None, ("dp", "fsdp"), None),
            P(None, ("dp", "fsdp"), None),
            P("dp", None, "fsdp"),
            P("dp", None, "fsdp"),
            P(None, None, ("dp", "fsdp")),
            P(None, None, ("dp", "fsdp")),
            P(None, None, ("dp", "fsdp")),
        ),
        check_vma=False,
    )
```

```python
import functools

import jax
import jax.numpy as jnp
from jax import lax
from jax.experimental import pallas as pl
from jax.experimental.pallas import tpu as pltpu
from jax.sharding import PartitionSpec as P

H = 12
HD = 64
L = 512
STEP = 5
SEGS = 4
PAIR = 2 * HD
MIB = 1 << 20

beta_one = 0.5
beta_two = 0.5
adam_epsilon = 1e-08
norm_epsilon = 1e-06
matrix_rate = 0.03
vector_rate = 0.2
weight_decay = 0.01
masked_score = -1e30
low = jnp.bfloat16
full = jnp.float32


def dot_nn(a, b):
    return lax.dot_general(a, b, (((1,), (0,)), ((), ())), preferred_element_type=full)


def dot_nt(a, b):
    return lax.dot_general(a, b, (((1,), (1,)), ((), ())), preferred_element_type=full)


def dot_tn(a, b):
    return lax.dot_general(a, b, (((0,), (0,)), ((), ())), preferred_element_type=full)


def gelu_parts(z):
    t = pl.reciprocal(1.0 + 0.23164190 * jnp.abs(z), approx=True)
    square = z * z
    bell = jnp.exp2(-0.7213475204444817 * square)
    poly = ((((0.5307027145 * t - 0.7265760135) * t + 0.7107068705) * t - 0.142248368) * t + 0.127414796) * t
    tail = poly * bell
    phi = jnp.where(z >= 0, 1.0 - tail, tail)
    return z * phi, phi + (0.3989422804014327 * z) * bell


def norm_parts(residual):
    average = jnp.mean(residual, axis=-1, keepdims=True)
    centered = residual - average
    inverse = lax.rsqrt(jnp.mean(centered * centered, axis=-1, keepdims=True) + norm_epsilon)
    return centered * inverse, inverse


def norm_back(upstream, unit, inverse, gain):
    scaled = upstream * gain
    return inverse * (
        scaled
        - jnp.mean(scaled, axis=-1, keepdims=True)
        - unit * jnp.mean(scaled * unit, axis=-1, keepdims=True)
    )


def column_sum(values):
    return jnp.sum(values, axis=0, keepdims=True)


def half_masks(dtype):
    lane = lax.broadcasted_iota(jnp.int32, (1, PAIR), 1)
    first = (lane < HD).astype(full)
    return first.astype(dtype), (1.0 - first).astype(dtype)


def segment_codes(seg_column, masks):
    lane = lax.broadcasted_iota(jnp.int32, (1, PAIR), 1)
    lane = jnp.where(lane >= HD, lane - HD, lane)
    same = seg_column == lane
    key = jnp.where(same, 1.0, 0.0).astype(low)
    query = jnp.where(same | (lane >= SEGS), 0.0, masked_score).astype(low)
    return [key * masks[1 - h] for h in range(2)], [query * masks[1 - h] for h in range(2)]


class Place:
    def __init__(self, z_count):
        self.dp, self.z = lax.axis_index("dp"), lax.axis_index("fsdp")
        self.core, self.spot = lax.rem(self.dp, 2), lax.div(self.dp, 2)
        x_step = 1 - 2 * lax.rem(self.spot, 2)
        y_step = 2 - 4 * lax.div(self.spot, 2)
        self.spot_a = self.spot + (1 - self.core) * x_step + self.core * y_step
        self.spot_b = self.spot + self.core * x_step + (1 - self.core) * y_step
        self.spot_ab = self.spot + x_step + y_step
        self.sibling = (self.dp + 1 - 2 * self.core, self.z)
        self.near_a = (2 * self.spot_a + self.core, self.z)
        self.near_b = (2 * self.spot_b + self.core, self.z)
        self.z_count = z_count
        self.zs = [lax.rem(self.z + d, z_count) for d in range(z_count)]
        self.has_up, self.has_down = self.z < z_count - 1, self.z > 0
        self.middle = self.has_up & self.has_down
        self.across = lax.rem(self.z + 2, z_count)
        self.beside = jnp.where(self.z < 2, 1 - self.z, 5 - self.z)

    def line_sends(self, d):
        return {1: self.has_up, 2: self.z >= 0, 3: self.has_down}[d]

    def line_receives(self, d):
        return {1: self.has_down, 2: self.z >= 0, 3: self.has_up}[d]

    def chip_partners(self):
        return [self.sibling, self.near_a, self.near_b]

    def z_partners(self):
        return [(self.dp, other) for other in self.zs[1:]]


def greet(partners):
    barrier = pltpu.get_barrier_semaphore()
    for device in partners:
        pl.semaphore_signal(barrier, inc=1, device_id=device, device_id_type=pl.DeviceIdType.MESH)
    pl.semaphore_wait(barrier, len(partners))


def remote(source, target, send, receive, device):
    return pltpu.make_async_remote_copy(
        src_ref=source,
        dst_ref=target,
        send_sem=send,
        recv_sem=receive,
        device_id=device,
        device_id_type=pl.DeviceIdType.MESH,
    )


def fold(piece):
    half = piece.shape[1] // 2
    return jnp.concatenate([piece[:, :half], piece[:, half:]], axis=0)


def unfold(piece):
    rows = piece.shape[0] // 2
    return jnp.concatenate([piece[:rows], piece[rows:]], axis=1)


def looked_up(ticks, t):
    now = functools.reduce(jnp.logical_or, [t == tick for tick in ticks])
    which = sum(n * (t == tick).astype(jnp.int32) for n, tick in enumerate(ticks))
    return now, which


def run_due(stages, t):
    for ticks, stage in stages:
        if isinstance(t, int):
            if t in ticks:
                stage(ticks.index(t))
            continue
        now, block = looked_up(ticks, t)

        @pl.when(now)
        def _():
            stage(block)


def sum_times(ready):
    opens, cores, seconds = [], [], []
    for tick in ready:
        opens.append(max(tick, opens[-1] + 1) if opens else tick)
        cores.append(max(opens[-1] + 1, cores[-1] + 1) if cores else opens[-1] + 1)
        seconds.append(max(cores[-1] + 3, seconds[-1] + 3) if seconds else cores[-1] + 3)
    thirds = [tick + 2 for tick in seconds]
    return opens, cores, seconds, thirds, [tick + 2 for tick in thirds]


ANNOUNCE, FORWARD, FIRST, SECOND, CLOSE = -2, -1, 1, 2, 3


def sum_scratch(count, part, width, z_count, kind=low):
    piece = (2 * part // z_count, width // 2) if kind == low else (part // z_count, width)
    return [
        pltpu.VMEM((count, 4, part, width), kind),
        pltpu.VMEM((count, 4, part, width), kind),
        pltpu.VMEM((count, 2, part, width), kind),
        pltpu.VMEM((count, part, width), kind),
        pltpu.VMEM((count, z_count) + piece, kind),
        pltpu.VMEM((count, z_count) + piece, kind),
        pltpu.VMEM((count,) + piece, kind),
        pltpu.SemaphoreType.DMA((count,)),
        pltpu.SemaphoreType.DMA((count, 2)),
        pltpu.SemaphoreType.DMA((count, 2, 2)),
        pltpu.SemaphoreType.DMA((count, 2)),
        pltpu.SemaphoreType.DMA((count, 2, z_count)),
        pltpu.SemaphoreType.DMA((count, 2)),
    ]


SUM_REFS = 13


class BlockSum:
    def __init__(self, place, sources, refs, times):
        self.place, self.sources, self.times = place, sources, times
        (self.own, self.c, self.b, self.a, self.zs, self.zr, self.far,
         self.own_sem, self.c_sem, self.b_sem, self.a_sem, self.z_sem, self.far_sem) = refs
        self.count = self.c.shape[0]
        self.kind = self.c.dtype
        self.z_count = self.zs.shape[1]

    def load(self, i, block):
        return pltpu.make_async_copy(block.at[:, self.place.core], self.own.at[i], self.own_sem.at[i])

    def core_copy(self, i, block):
        return remote(
            block.at[:, 1 - self.place.core], self.c.at[i], self.c_sem.at[i, 0], self.c_sem.at[i, 1], self.place.sibling
        )

    def second_copy(self, i, k):
        chunk = self.place.spot_b if k == 0 else self.place.spot_ab
        return remote(
            self.c.at[i, chunk], self.b.at[i, k], self.b_sem.at[i, 0, k], self.b_sem.at[i, 1, k], self.place.near_b
        )

    def third_copy(self, i):
        return remote(
            self.c.at[i, self.place.spot_a], self.a.at[i], self.a_sem.at[i, 0], self.a_sem.at[i, 1], self.place.near_a
        )

    def z_copy(self, i, d):
        other = self.place.zs[d]
        return remote(
            self.zs.at[i, other], self.zr.at[i, self.place.z], self.z_sem.at[i, 0, d],
            self.z_sem.at[i, 1, self.z_count - d], (self.place.dp, other),
        )

    def open(self, i):
        first = 0
        for source in self.sources:
            count = source.shape[0]

            @pl.when((i >= first) & (i < first + count))
            def _():
                block = source.at[jnp.clip(i - first, 0, count - 1)]
                self.core_copy(i, block).start()
                self.load(i, block).start()

            first += count

    def after_core(self, i):
        block = self.sources[0].at[0]
        self.core_copy(i, block).wait()
        self.load(i, block).wait()

        def add(k, carry):
            self.c[i, k] = (self.c[i, k].astype(full) + self.own[i, k].astype(full)).astype(self.kind)
            return carry

        lax.fori_loop(0, 4, add, 0)
        self.second_copy(i, 0).start()
        self.second_copy(i, 1).start()

    def after_second(self, i):
        other, spot = self.place.spot_a, self.place.spot
        self.second_copy(i, 1).wait()
        self.c[i, other] = (self.c[i, other].astype(full) + self.b[i, 1].astype(full)).astype(self.kind)
        self.third_copy(i).start()
        self.second_copy(i, 0).wait()
        self.c[i, spot] = (self.c[i, spot].astype(full) + self.b[i, 0].astype(full)).astype(self.kind)

    def after_third(self, i):
        self.third_copy(i).wait()
        total = self.c[i, self.place.spot].astype(full) + self.a[i].astype(full)
        rows = total.shape[0] // self.z_count
        for k in range(self.z_count):
            piece = total[k * rows : (k + 1) * rows]
            self.zs[i, k] = fold(piece).astype(low) if self.kind == low else piece
        place = self.place
        for d in (1, 3):
            @pl.when(place.line_sends(d))
            def _():
                self.z_copy(i, d).start()

        @pl.when(jnp.logical_not(place.middle))
        def _():
            self.z_copy(i, 2).start()
            self.far_copy(i).start()
            opposite = self.z_count - 1 - place.z
            self.zr[i, opposite] = jnp.zeros(self.zr.shape[2:], self.kind)

    def far_copy(self, i):
        place = self.place
        return remote(
            self.zs.at[i, self.z_count - 1 - place.z], self.far.at[i], self.far_sem.at[i, 0], self.far_sem.at[i, 1],
            (place.dp, place.beside),
        )

    def relay(self, i):
        @pl.when(self.place.middle)
        def _():
            self.far_copy(i).wait_recv()
            across = self.place.across
            self.zs[i, across] = (self.zs[i, across].astype(full) + self.far[i].astype(full)).astype(self.kind)
            self.z_copy(i, 2).start()

    def finish(self, i):
        for d in range(1, self.z_count):
            @pl.when(self.place.line_sends(d))
            def _():
                self.z_copy(i, d).wait_send()

            @pl.when(self.place.line_receives(d))
            def _():
                self.z_copy(i, d).wait_recv()

        @pl.when(jnp.logical_not(self.place.middle))
        def _():
            self.far_copy(i).wait_send()

        total = self.zs[i, self.place.z].astype(full)
        for d in range(1, self.z_count):
            total = total + self.zr[i, self.place.zs[d]].astype(full)
        return total

    def tick(self, t):
        stages = (self.relay, self.after_third, self.after_second, self.after_core, self.open)
        run_due(list(zip(self.times[::-1], stages)), t)

    @property
    def last(self):
        return self.times[4][-1]


class LineGather:
    def __init__(self, place, source, target, first, local_sem, sem, z_count):
        self.place = place
        self.source = source.at[pl.ds(first, target.shape[1])]
        self.target, self.local_sem, self.sem, self.z_count = target, local_sem, sem, z_count

    def copies(self):
        place = self.place
        here = self.target.at[place.z]
        result = [pltpu.make_async_copy(self.source, here, self.local_sem)]
        for d in range(1, self.z_count):
            send, receive = self.sem.at[0, d - 1], self.sem.at[1, self.z_count - d - 1]
            result.append(remote(self.source, here, send, receive, (place.dp, place.zs[d])))
        return result

    def start(self):
        for copy in self.copies():
            copy.start()

    def wait(self):
        for copy in self.copies():
            copy.wait()


def gather_scratch(count, group, rows, width, z_count, kind=low):
    piece = (2 * rows // z_count, width // 2) if kind == low else (rows // z_count, width)
    return [
        pltpu.VMEM((count, z_count, group) + piece, kind),
        pltpu.SemaphoreType.DMA((count, 2, z_count)),
        pltpu.SemaphoreType.DMA((count, 2)),
        pltpu.SemaphoreType.DMA((count, 2, 2)),
        pltpu.SemaphoreType.DMA((count, 2)),
        pltpu.SemaphoreType.DMA((count, 2)),
    ]


GATHER_REFS = 6


class BlockGather:
    def __init__(self, place, source, whole, base, refs):
        self.place, self.source, self.whole, self.base = place, source, whole, base
        self.zr, self.z_sem, self.a_sem, self.b_sem, self.c_sem, self.far_sem = refs
        self.count, self.z_count, self.group = self.zr.shape[:3]

    def blocks(self, i):
        return pl.ds(self.base + self.group * i, self.group)

    def z_copy(self, i, d):
        place = self.place
        return remote(
            self.source.at[i], self.zr.at[i, place.z], self.z_sem.at[i, 0, d], self.z_sem.at[i, 1, self.z_count - d],
            (place.dp, place.zs[d]),
        )

    def chunk(self, i, spot):
        return self.whole.at[self.blocks(i), spot, self.place.core]

    def first_copy(self, i):
        chunk = self.chunk(i, self.place.spot)
        return remote(chunk, chunk, self.a_sem.at[i, 0], self.a_sem.at[i, 1], self.place.near_a)

    def second_copy(self, i, k):
        chunk = self.chunk(i, self.place.spot if k == 0 else self.place.spot_a)
        return remote(chunk, chunk, self.b_sem.at[i, 0, k], self.b_sem.at[i, 1, k], self.place.near_b)

    def core_copy(self, i):
        chunks = self.whole.at[self.blocks(i), :, self.place.core]
        return remote(chunks, chunks, self.c_sem.at[i, 0], self.c_sem.at[i, 1], self.place.sibling)

    def far_copy(self, i):
        place = self.place
        piece = self.zr.at[i, place.across]
        return remote(piece, piece, self.far_sem.at[i, 0], self.far_sem.at[i, 1], (place.dp, place.beside))

    def announce(self, i):
        for d in range(1, self.z_count):
            @pl.when(self.place.line_sends(d))
            def _():
                self.z_copy(i, d).start()

        self.zr[i, self.place.z] = self.source[i]

    def forward(self, i):
        @pl.when(self.place.middle)
        def _():
            self.z_copy(i, 2).wait_recv()
            self.far_copy(i).start()

    def begin(self):
        for i in range(min(-ANNOUNCE, self.count)):
            self.announce(i)

    def open(self, i):
        place = self.place
        for d in range(1, self.z_count):
            @pl.when(place.line_sends(d))
            def _():
                self.z_copy(i, d).wait_send()

        for d in (1, 3):
            @pl.when(place.line_receives(d))
            def _():
                self.z_copy(i, d).wait_recv()

        @pl.when(place.middle)
        def _():
            self.far_copy(i).wait_send()

        @pl.when(jnp.logical_not(place.middle))
        def _():
            self.z_copy(i, 2).wait_recv()
            self.far_copy(i).wait_recv()

        for n in range(self.group):
            pieces = [self.zr[i, k, n].astype(full) for k in range(self.z_count)]
            if self.zr.dtype == low:
                pieces = [unfold(piece) for piece in pieces]
            whole = jnp.concatenate(pieces, axis=0).astype(self.whole.dtype)
            self.whole[self.base + self.group * i + n, place.spot, place.core] = whole
        self.first_copy(i).start()
        self.second_copy(i, 0).start()

    def after_first(self, i):
        self.first_copy(i).wait()
        self.second_copy(i, 1).start()

    def after_second(self, i):
        self.second_copy(i, 0).wait()
        self.second_copy(i, 1).wait()
        self.core_copy(i).start()

    def close(self, i):
        self.core_copy(i).wait()

    def tick(self, t, done=None):
        def close(i):
            self.close(i)
            if done is not None:
                done(i)

        @pl.when(t == 0)
        def _():
            for i in range(min(-FORWARD, self.count)):
                self.forward(i)

        stages = (
            (SECOND, self.after_second), (FIRST, self.after_first), (0, self.open), (FORWARD, self.forward),
            (ANNOUNCE, self.announce), (CLOSE, close),
        )
        for late, stage in stages:
            @pl.when((t >= max(late, 0)) & (t - late < self.count))
            def _():
                stage(t - late)


def split_refs(refs, *counts):
    result, start = [], 0
    for count in counts:
        result.append(refs[start : start + count])
        start += count
    return result


class Side:
    def __init__(self, plan, sources, targets, sum_refs, line_refs, own=None):
        self.plan = plan
        sums = plan.sums
        blocks = [source.at[pl.ds(plan.skip, source.shape[0] - plan.skip)] for source in sources[:sums]]
        blocks += [own] if plan.own else []
        self.place = Place(plan.z_count) if plan.active else None
        self.sum = BlockSum(self.place, blocks, sum_refs, plan.times) if plan.total else None
        self.result = targets[0] if plan.total else None
        self.lines = line_gathers(self.place, plan.lines, sources[sums:], targets[bool(plan.total) :], line_refs, plan.z_count)

    def enter(self, now):
        if not self.plan.active:
            return

        @pl.when(now)
        def _():
            greet((self.place.chip_partners() if self.plan.total else []) + self.place.z_partners())
            for line in self.lines:
                line.start()

    def tick(self, t):
        if self.plan.total:
            self.sum.tick(t)

    def leave(self, now, ticks):
        if not self.plan.active:
            return

        @pl.when(now)
        def _():
            if self.plan.total:
                if self.sum.last >= ticks:
                    lax.fori_loop(ticks, self.sum.last + 1, lambda t, carry: (self.tick(t), carry)[1], 0)
                for i in range(self.sum.count):
                    self.result[i] = self.sum.finish(i).astype(low)
            for line in self.lines:
                line.wait()


class Plan:
    def __init__(self, pending=None, lines=(), z_count=1, own=0, size=None, ready=(), skip=0):
        self.z_count = z_count
        self.sums = int(pending is not None)
        self.own, self.skip = own, skip
        self.total = own + (pending.shape[0] - skip if self.sums else 0)
        self.times = sum_times(ready) if self.total else None
        self.lines = [(first, count) for _, first, count in lines]
        self.active = bool(self.total or lines)
        self.arguments, self.results, self.result_specs, self.scratch = [], [], [], []
        if self.sums:
            self.arguments.append(pending)
        if self.total:
            part, width = size
            self.results.append(jax.ShapeDtypeStruct((self.total, 2 * part // z_count, width // 2), low))
            self.result_specs.append(
                pl.BlockSpec(self.results[0].shape, lambda i: (0, 0, 0), pipeline_mode=pl.Buffered(1))
            )
            self.scratch += sum_scratch(self.total, part, width, z_count)
        for basis, _, count in lines:
            self.arguments.append(basis)
            self.results.append(jax.ShapeDtypeStruct((z_count, count) + basis.shape[1:], low))
            self.result_specs.append(ANYWHERE)
        self.scratch += line_scratch(len(lines), z_count)
        self.argument_specs = [ANYWHERE] * len(self.arguments)

    def split(self, refs, inputs, outputs, scratch):
        count = len(self.lines)
        return split_refs(
            refs, inputs, self.sums + count, outputs, bool(self.total) + count, scratch,
            SUM_REFS * bool(self.total), 2 * bool(self.lines),
        )


def line_scratch(count, z_count):
    if not count:
        return []
    return [pltpu.SemaphoreType.DMA((count,)), pltpu.SemaphoreType.DMA((count, 2, z_count - 1))]


def line_gathers(place, spans, sources, targets, refs, z_count):
    return [
        LineGather(place, source, target, first, refs[0].at[n], refs[1].at[n], z_count)
        for n, (source, target, (first, _)) in enumerate(zip(sources, targets, spans))
    ]


ANYWHERE = pl.BlockSpec(memory_space=pl.ANY)
IN_VMEM = pl.BlockSpec(memory_space=pltpu.VMEM)


def forward_kernel(plan, *refs):
    inputs, sources, outputs, targets, scratch, gather_refs, vec_refs, line_refs = plan.split(refs)
    x_ref, segc_ref, vec_ref, w_hbm = inputs
    (q_ref, k_ref, v_ref, ctxt_ref, lse_ref, x1_ref, inv1_ref, n1_ref, u_ref, gp_ref, x2_ref, inv2_ref,
     out_ref) = outputs
    w, codes, vt, n1_all, acc, w_sem = scratch
    s = pl.program_id(0)
    tokens, width = acc.shape
    rows_now = x_ref.shape[0]
    rows = tokens // rows_now
    inner = plan.inner
    local = plan.local
    gather = vec_gather = None
    place = Place(plan.z_count) if plan.gathered else None
    if plan.gathered:
        w_out, out_sem = targets[0], scratch_tail(plan, refs)
        gather = BlockGather(place, plan.folded(refs), w, local, gather_refs)
        if plan.vectors:
            vec_gather = BlockGather(place, sources[1], plan.vec_whole(refs), 0, vec_refs)
            vec_ref = targets[1]
    lines = line_gathers(place, plan.lines, sources[plan.line_at :], targets[plan.line_target_at :], line_refs, plan.z_count)

    def keep(i):
        group = gather.group
        return pltpu.make_async_copy(w.at[gather.blocks(i)], w_out.at[pl.ds(group * i, group)], out_sem.at[i])

    def load(j):
        return pltpu.make_async_copy(w_hbm.at[plan.order[j]], w.at[j], w_sem.at[j])

    def matrix(j):
        return w[j].reshape(width, width)

    def arrive(j):
        if j < local:
            load(j).wait()

    def tick(t):
        if gather is not None:
            gather.tick(t, lambda i: keep(i).start())
            if vec_gather is not None:
                vec_gather.tick(t)

    pairs = width // PAIR

    @pl.when(s == 0)
    def _():
        for j in range(local):
            load(j).start()
        if gather is not None:
            for n, number in enumerate(plan.numbers):
                gather.source[n // plan.group, n % plan.group] = fold(sources[0][number]).astype(low)
            greet(place.chip_partners() + place.z_partners())
            if vec_gather is not None:
                vec_gather.begin()
            gather.begin()
        for j in range(min(local, 3)):
            arrive(j)

    def run_ticks(start, stop):
        if gather is not None:
            lax.fori_loop(start, stop, lambda t, carry: (tick(t), carry)[1], 0)

    def ready():
        for line in lines:
            line.start()
        if vec_gather is not None:
            turned = vec_gather.whole[0].reshape(width, vec_gather.whole.shape[-1]).T
            for layer in range(2):
                count = plan.vector_rows
                targets[1 + layer][0:count, :] = turned[layer * count : (layer + 1) * count, :]

    def project():
        xin = x_ref[...].astype(low)
        keys, queries = segment_codes(segc_ref[0], half_masks(low))
        for h in range(2):
            codes[0, h] = keys[h]
            codes[1, h] = queries[h]
        q_ref[...] = (dot_nn(xin, matrix(0)) + vec_ref[0:1, :]).astype(low)
        k_ref[...] = dot_nn(xin, matrix(1)).astype(low)
        value = dot_nn(xin, matrix(2)) + vec_ref[1:2, :]
        v_ref[...] = value.astype(low)
        turned = value.T.astype(low)
        for h in range(width // HD):
            vt[h, 0:HD] = turned[h * HD : (h + 1) * HD]
            vt[h, HD : HD + 16] = jnp.ones((16, turned.shape[1]), low)

    def pair_step(p):
        masks = half_masks(low)
        lanes = pl.ds(pl.multiple_of(p * PAIR, PAIR), PAIR)
        q_pair = q_ref[:, lanes] * jnp.asarray(HD ** (-0.5), low)
        k_pair = k_ref[:, lanes]
        for h in range(2):
            scores = dot_nt(k_pair * masks[h] + codes[0, h], q_pair * masks[h] + codes[1, h])
            largest = jnp.max(scores, axis=0, keepdims=True)
            expanded = jnp.exp(scores - largest)
            here = pl.ds(pl.multiple_of(p * PAIR + h * HD, HD), HD)
            product = dot_nn(vt[2 * p + h], expanded.astype(low))
            total = product[HD : HD + 1]
            ctxt_ref[here, :] = (product[0:HD] * (1.0 / total)).astype(low)
            lse_ref[0, pl.ds(2 * p + h, 1), :] = largest + jnp.log(total)

    def close_row():
        @pl.when(s == 0)
        def _():
            if local > 3:
                arrive(3)

        context = ctxt_ref[...].astype(full).T.astype(low)
        attended = dot_nn(context, matrix(3)) + vec_ref[2:3, :]
        unit, inverse = norm_parts(x_ref[...].astype(full) + attended)
        x1_ref[...] = unit
        inv1_ref[...] = inverse
        normed = unit * vec_ref[3:4, :] + vec_ref[4:5, :]
        here = pl.ds(pl.multiple_of(s * rows_now, rows_now), rows_now)
        acc[here, :] = normed + vec_ref[5 + inner : 6 + inner, :]
        normed = normed.astype(low)
        n1_ref[...] = normed
        n1_all[here, :] = normed

    @pl.when(s < rows)
    def _():
        def position(n, carry):
            if gather is not None:
                here, which = looked_up(plan.row_positions, n)
                before = plan.lead + s * len(plan.row_positions) + which
                opening = (s == 0) & (n == 0)
                start = jnp.where(opening, 0, before)
                stop = jnp.where(opening, plan.lead, jnp.where(here, before + 1, before))
                run_ticks(start, stop)

                @pl.when(opening)
                def _():
                    ready()

            @pl.when(n == 0)
            def _():
                project()

            @pl.when((n >= 1) & (n <= pairs))
            def _():
                pair_step(n - 1)

            @pl.when(n == pairs + 1)
            def _():
                close_row()

            return carry

        lax.fori_loop(0, pairs + 2, position, 0)

    tile = tokens // 4
    starts, stops = plan.step_ticks(rows)

    @pl.when(s >= rows)
    def _():
        c = s - rows

        @pl.when(c == 0)
        def _():
            for j in range(4, local):
                arrive(j)

        def token_step(i, carry):
            for half in range(2):
                here = pl.ds(pl.multiple_of((2 * i + half) * tile, tile), tile)
                value, slope = gelu_parts(dot_nn(n1_all[here, :], matrix(4 + 2 * c)) + vec_ref[pl.ds(5 + c, 1), :])
                active = value.astype(low)
                u_ref[here, :] = active
                gp_ref[here, :] = slope.astype(low)
                acc[here, :] += dot_nn(active, matrix(5 + 2 * c))
            return carry

        lax.fori_loop(0, 2, token_step, 0)

        @pl.when(c == inner - 1)
        def _():
            base = 5 + inner

            def last(i, carry):
                here = pl.ds(pl.multiple_of(i * tile, tile), tile)
                unit, inverse = norm_parts(acc[here, :])
                x2_ref[here, :] = unit
                inv2_ref[here, :] = inverse
                out_ref[here, :] = (
                    unit * vec_ref[base + 1 : base + 2, :] + vec_ref[base + 2 : base + 3, :]
                ).astype(out_ref.dtype)
                return carry

            lax.fori_loop(0, 4, last, 0)

        run_ticks(
            sum(n * (c == k).astype(jnp.int32) for k, n in enumerate(starts)),
            sum(n * (c == k).astype(jnp.int32) for k, n in enumerate(stops)),
        )

        @pl.when(c == inner - 1)
        def _():
            if gather is not None:
                for line in lines:
                    line.wait()
                for i in range(gather.count):
                    keep(i).wait()


class ForwardPlan:
    def __init__(self, inner, local, blocks=None, numbers=(), vec_shard=None, vector_rows=0, lines=(), lead=0, row_positions=(), z_count=1):
        self.inner, self.local, self.lead, self.row_positions, self.z_count = inner, local, lead, row_positions, z_count
        self.vector_rows = vector_rows
        self.order = [0, 1, 2, 3]
        for c in range(inner):
            self.order += [4 + c, 4 + inner + c]
        self.numbers = list(numbers)
        self.gathered, self.group = len(self.numbers), 2
        self.vectors = vec_shard is not None
        self.lines = [(first, count) for _, first, count in lines]
        self.line_at = int(self.gathered > 0) + int(self.vectors)
        self.line_target_at = int(self.gathered > 0) + 2 * int(self.vectors)
        self.arguments, self.argument_specs, self.results, self.result_specs, self.scratch = [], [], [], [], []
        shape = jax.ShapeDtypeStruct
        if self.gathered:
            rows, width = blocks.shape[1:]
            groups = self.gathered // self.group
            self.arguments.append(blocks)
            self.argument_specs.append(IN_VMEM)
            self.results.append(shape((self.gathered, 4, 2, width // 8, width), low))
            self.result_specs.append(ANYWHERE)
            self.scratch += gather_scratch(groups, self.group, width // 8, width, z_count)
        if self.vectors:
            lanes = vec_shard.shape[3]
            self.arguments.append(vec_shard)
            self.argument_specs.append(IN_VMEM)
            for _ in range(2):
                self.results.append(shape((16, width), full))
                self.result_specs.append(pl.BlockSpec((16, width), lambda s: (0, 0)))
            self.scratch += gather_scratch(1, 1, width // 8, lanes, z_count, full)
        for basis, _, count in lines:
            self.arguments.append(basis)
            self.argument_specs.append(ANYWHERE)
            self.results.append(shape((z_count, count) + basis.shape[1:], low))
            self.result_specs.append(ANYWHERE)
        self.scratch += line_scratch(len(lines), z_count)
        if self.gathered:
            self.scratch.append(pltpu.SemaphoreType.DMA((self.gathered // self.group,)))
        if self.vectors:
            self.scratch.append(pltpu.VMEM((1, 4, 2, width // 8, lanes), full))
        if self.gathered:
            self.scratch.append(pltpu.VMEM((groups, self.group, 2 * rows, width // 2), low))

    def step_ticks(self, rows):
        now, starts, stops = self.lead + rows * len(self.row_positions), [], []
        for c in range(self.inner):
            starts.append(now)
            if not self.gathered:
                stops.append(now)
                continue
            if c == self.inner - 1:
                now = max(now, self.gathered // self.group + CLOSE)
            else:
                now = max(now + 1, (5 + 2 * (c + 1) - self.local) // self.group + CLOSE + 1)
            stops.append(now)
        return starts, stops

    def split(self, refs):
        return split_refs(
            refs, 4, len(self.arguments), 13, len(self.results), 6, GATHER_REFS * bool(self.gathered),
            GATHER_REFS * self.vectors, 2 * bool(self.lines),
        )

    def vec_whole(self, refs):
        return refs[-2]

    def folded(self, refs):
        return refs[-1]


def scratch_tail(plan, refs):
    return refs[-3] if plan.vectors else refs[-2]


def forward_layer(hidden, seg_column, vectors, weights, out_dtype, plan, identity=None):
    tokens, width = hidden.shape
    inner = plan.inner
    wide = width * inner
    rows = tokens // L
    heads = width // HD
    shape = jax.ShapeDtypeStruct

    def here(s):
        return jnp.minimum(s, rows - 1)

    def column(s):
        return jnp.maximum(s - rows, 0)

    def row_block(columns):
        return pl.BlockSpec((L, columns), lambda s: (here(s), 0))

    def whole(columns):
        return pl.BlockSpec((tokens, columns), lambda s: (0, 0), pipeline_mode=pl.Buffered(1))

    wide_block = pl.BlockSpec((tokens, width), lambda s: (0, column(s)))
    out_shape = (
        shape((tokens, width), low), shape((tokens, width), low), shape((tokens, width), low),
        shape((width, tokens), low), shape((rows, heads, L), full),
        shape((tokens, width), full), shape((tokens, 1), full), shape((tokens, width), low),
        shape((tokens, wide), low), shape((tokens, wide), low),
        shape((tokens, width), full), shape((tokens, 1), full), shape((tokens, width), out_dtype),
        *plan.results,
    )
    out_specs = (
        row_block(width), row_block(width), row_block(width),
        pl.BlockSpec((width, L), lambda s: (0, here(s))), pl.BlockSpec((1, heads, L), lambda s: (here(s), 0, 0)),
        row_block(width), row_block(1), row_block(width),
        wide_block, wide_block,
        whole(width), whole(1), whole(width),
        *plan.result_specs,
    )
    if plan.local:
        weights = weights.reshape(-1, 4, 2, width // 8, width)
    total = 4 + 2 * inner
    held = max(total, plan.local + plan.gathered)
    return pl.pallas_call(
        functools.partial(forward_kernel, plan),
        grid=(rows + inner,),
        out_shape=out_shape,
        in_specs=[
            row_block(width),
            pl.BlockSpec((1, L, 1), lambda s: (here(s), 0, 0)),
            pl.BlockSpec(vectors.shape, lambda s: (0, 0)),
            ANYWHERE,
            *plan.argument_specs,
        ],
        out_specs=out_specs,
        scratch_shapes=[
            pltpu.VMEM((held, 4, 2, width // 8, width), low),
            pltpu.VMEM((2, 2, L, PAIR), low),
            pltpu.VMEM((heads, HD + 16, L), low),
            pltpu.VMEM((tokens, width), low),
            pltpu.VMEM((tokens, width), full),
            pltpu.SemaphoreType.DMA((total,)),
            *plan.scratch,
        ],
        compiler_params=pltpu.CompilerParams(
            dimension_semantics=("arbitrary",), vmem_limit_bytes=62 * MIB,
            collective_id=identity, has_side_effects=identity is not None,
        ),
        cost_estimate=pl.CostEstimate(
            flops=2 * tokens * width * width * total + 4 * tokens * L * width,
            bytes_accessed=40 * MIB,
            transcendentals=tokens * (L * heads + wide),
        ),
        name="layer_forward",
    )(hidden, seg_column, vectors, weights, *plan.arguments)


WIDE_STEP_TICKS = 5


def wide_ready(own):
    return [WIDE_STEP_TICKS * (n // 2) + 4 + n % 2 for n in range(own)]


def wide_back_kernel(plan, inner, *refs):
    inputs, sources, outputs, targets, scratch, sum_refs, line_refs = plan.split(refs, 11, 4, 11)
    up_hbm, x2_hbm, inv2_hbm, x1_hbm, inv1_hbm, n1_hbm, vec_ref, wup_ref, wdown_ref, u_ref, gp_ref = inputs
    dw_ref, dr1_ref, da_ref, dvec_ref = outputs
    n1t, dz, kept_dw, up_ref, x2_ref, inv2_ref, x1_ref, inv1_ref, n1_ref, tile_sem, load_sem = scratch
    dy, dn1 = da_ref, dr1_ref
    c = pl.program_id(0)
    steps = pl.num_programs(0)
    tokens, width = dn1.shape
    tile = tokens // 4
    base = 5 + inner
    side = Side(plan, sources, targets, sum_refs, line_refs, kept_dw)

    def tile_copies(i):
        rows = pl.ds(pl.multiple_of(i * tile, tile), tile)
        return [
            pltpu.make_async_copy(source.at[rows], target.at[rows], tile_sem.at[n, i])
            for n, (source, target) in enumerate(((up_hbm, up_ref), (x2_hbm, x2_ref), (inv2_hbm, inv2_ref)))
        ]

    late_copies = [
        pltpu.make_async_copy(source, target, load_sem.at[n])
        for n, (source, target) in enumerate(((n1_hbm, n1_ref), (x1_hbm, x1_ref), (inv1_hbm, inv1_ref)))
    ]

    @pl.when(c == 0)
    def _():
        for i in range(4):
            for copy in tile_copies(i):
                copy.start()
        for copy in late_copies:
            copy.start()

    side.enter(c == 0)

    def prepare():
        gain = vec_ref[base + 1 : base + 2, :]

        def body(i, carry):
            for copy in tile_copies(i):
                copy.wait()
            gain_sum, shift_sum, bias_sum = carry
            rows = pl.ds(pl.multiple_of(i * tile, tile), tile)
            upstream = up_ref[rows, :].astype(full)
            unit = x2_ref[rows, :]
            back = norm_back(upstream, unit, inv2_ref[rows, :], gain)
            dn1[rows, :] = back
            branch = back.astype(low)
            dy[rows, :] = branch
            return (
                gain_sum + column_sum(upstream * unit),
                shift_sum + column_sum(upstream),
                bias_sum + column_sum(branch.astype(full)),
            )

        zero = jnp.zeros((1, width), full)
        gain_sum, shift_sum, bias_sum = lax.fori_loop(0, 4, body, (zero, zero, zero))
        dvec_ref[...] = jnp.zeros(dvec_ref.shape, full)
        dvec_ref[base : base + 1, :] = bias_sum
        dvec_ref[base + 1 : base + 2, :] = gain_sum
        dvec_ref[base + 2 : base + 3, :] = shift_sum
        late_copies[0].wait()
        n1t[...] = n1_ref[...].astype(full).T.astype(low)

    def token_pair(i):
        bias_sum = jnp.zeros((1, width), full)
        for half in range(2):
            rows = pl.ds(pl.multiple_of((2 * i + half) * tile, tile), tile)
            slope = gp_ref[rows, :].astype(full)
            piece = (dot_nt(dy[rows, :], wdown_ref[0]) * slope).astype(low)
            dz[rows, :] = piece
            dn1[rows, :] += dot_nt(piece, wup_ref[0])
            bias_sum = bias_sum + column_sum(piece.astype(full))
        dvec_ref[pl.ds(5 + c, 1), :] += bias_sum

    def store(k, product):
        if plan.own:
            @pl.when(2 * c + k < plan.own)
            def _():
                kept_dw[2 * c + k] = product().reshape(kept_dw.shape[1:])

            @pl.when(2 * c + k >= plan.own)
            def _():
                dw_ref[k, 0] = product()
        else:
            dw_ref[k, 0] = product()

    def position(n, carry):
        side.tick(WIDE_STEP_TICKS * c + n)

        @pl.when((n == 0) & (c == 0))
        def _():
            prepare()

        @pl.when((n == 1) | (n == 2))
        def _():
            token_pair(n - 1)

        @pl.when(n == 3)
        def _():
            store(0, lambda: dot_nn(n1t[...], dz[...]).astype(low))

        @pl.when(n == 4)
        def _():
            store(1, lambda: dot_tn(u_ref[...], dy[...]).astype(low))

        return carry

    lax.fori_loop(0, WIDE_STEP_TICKS, position, 0)
    @pl.when(c == steps - 1)
    def _():
        for copy in late_copies[1:]:
            copy.wait()
        gain = vec_ref[3:4, :]

        def body(i, carry):
            gain_sum, shift_sum, bias_sum = carry
            rows = pl.ds(pl.multiple_of(i * tile, tile), tile)
            upstream = dn1[rows, :]
            unit = x1_ref[rows, :]
            back = norm_back(upstream, unit, inv1_ref[rows, :], gain)
            dr1_ref[rows, :] = back
            branch = back.astype(low)
            da_ref[rows, :] = branch
            return (
                gain_sum + column_sum(upstream * unit),
                shift_sum + column_sum(upstream),
                bias_sum + column_sum(branch.astype(full)),
            )

        zero = jnp.zeros((1, width), full)
        gain_sum, shift_sum, bias_sum = lax.fori_loop(0, 4, body, (zero, zero, zero))
        dvec_ref[2:3, :] = bias_sum
        dvec_ref[3:4, :] = gain_sum
        dvec_ref[4:5, :] = shift_sum

    side.leave(c == steps - 1, WIDE_STEP_TICKS * inner)


def wide_back(upstream, kept, vectors, weights, places, plan, identity=None):
    x1, inv1, n1, u, gp, x2, inv2 = kept
    tokens, width = x1.shape
    up_start, down_start, stride = places
    inner = u.shape[1] // width
    shape = jax.ShapeDtypeStruct

    return pl.pallas_call(
        functools.partial(wide_back_kernel, plan, inner),
        grid=(inner,),
        out_shape=(
            shape((2, inner - plan.own // 2, width, width), low),
            shape((tokens, width), full), shape((tokens, width), low), shape((16, width), full),
            *plan.results,
        ),
        in_specs=[
            *[ANYWHERE] * 6,
            pl.BlockSpec(vectors.shape, lambda c: (0, 0), pipeline_mode=pl.Buffered(1)),
            pl.BlockSpec((1, width, width), lambda c: (up_start + stride * c, 0, 0)),
            pl.BlockSpec((1, width, width), lambda c: (down_start + stride * c, 0, 0)),
            pl.BlockSpec((tokens, width), lambda c: (0, c)),
            pl.BlockSpec((tokens, width), lambda c: (0, c)),
            *plan.argument_specs,
        ],
        out_specs=(
            pl.BlockSpec((2, 1, width, width), lambda c: (0, jnp.maximum(c - plan.own // 2, 0), 0, 0)),
            pl.BlockSpec((tokens, width), lambda c: (0, 0), pipeline_mode=pl.Buffered(1)),
            pl.BlockSpec((tokens, width), lambda c: (0, 0), pipeline_mode=pl.Buffered(1)),
            pl.BlockSpec((16, width), lambda c: (0, 0)),
            *plan.result_specs,
        ),
        scratch_shapes=[
            pltpu.VMEM((width, tokens), low),
            pltpu.VMEM((tokens, width), low),
            pltpu.VMEM((plan.own, 4, 2, width // 8, width) if plan.own else (8, 128), low),
            pltpu.VMEM((tokens, width), upstream.dtype),
            pltpu.VMEM((tokens, width), full),
            pltpu.VMEM((tokens, 1), full),
            pltpu.VMEM((tokens, width), full),
            pltpu.VMEM((tokens, 1), full),
            pltpu.VMEM((tokens, width), low),
            pltpu.SemaphoreType.DMA((3, 4)),
            pltpu.SemaphoreType.DMA((3,)),
            *plan.scratch,
        ],
        compiler_params=pltpu.CompilerParams(
            dimension_semantics=("arbitrary",), vmem_limit_bytes=60 * MIB,
            collective_id=identity, has_side_effects=identity is not None,
        ),
        cost_estimate=pl.CostEstimate(
            flops=8 * tokens * width * width * inner, bytes_accessed=50 * MIB, transcendentals=0
        ),
        name="wide_backward",
    )(upstream, x2, inv2, x1, inv1, n1, vectors, weights, weights, u, gp, *plan.arguments)


def attend_back_kernel(plan, *refs):
    inputs, sources, outputs, targets, scratch, sum_refs, line_refs = plan.split(refs, 10, 3, 12)
    da_hbm, dr1_ref, x_ref, q_ref, k_ref, v_ref, ctxt_hbm, lse_ref, segc_ref, w_hbm = inputs
    dw_ref, dx_ref, dvec_ref = outputs
    codes, dctx, kt, delta, dqt, xt, grads, dwo, da_ref, ctxt_ref, w_ref, load_sem = scratch
    r = pl.program_id(0)
    loads = [
        pltpu.make_async_copy(w_hbm.at[plan.start + 3], w_ref.at[3], load_sem.at[0]),
        pltpu.make_async_copy(da_hbm, da_ref, load_sem.at[1]),
        pltpu.make_async_copy(ctxt_hbm, ctxt_ref, load_sem.at[2]),
        pltpu.make_async_copy(w_hbm.at[pl.ds(plan.start, 3)], w_ref.at[pl.ds(0, 3)], load_sem.at[3]),
    ]

    @pl.when(r == 0)
    def _():
        for copy in loads:
            copy.start()

    side = Side(plan, sources, targets, sum_refs, line_refs, dwo)
    side.enter(r == 0)
    tokens, width = dr1_ref.shape
    pairs = width // PAIR
    ticks = pairs + 5
    here = pl.ds(pl.multiple_of(r * tokens, tokens), tokens)
    masks = half_masks(low)
    scale = HD ** (-0.5)
    last_row = pl.num_programs(0) - 1

    def prepare():
        @pl.when(r == 0)
        def _():
            for copy in loads[:3]:
                copy.wait()
            grad = dot_nn(ctxt_ref[...], da_ref[...]).astype(low)
            if plan.own:
                dwo[0] = grad.reshape(dwo.shape[1:])
            else:
                dw_ref[3] = grad
            dvec_ref[...] = jnp.zeros(dvec_ref.shape, full)

        xt[:, here] = x_ref[...].astype(low).astype(full).T.astype(low)
        keys, queries = segment_codes(segc_ref[0], masks)
        for h in range(2):
            codes[0, h] = keys[h]
            codes[1, h] = queries[h]
        context_grad = dot_nt(da_ref[here, :], w_ref[3]).astype(low)
        dctx[...] = context_grad
        kt[...] = k_ref[...].astype(full).T.astype(low)
        products = context_grad.astype(full) * ctxt_ref[:, here].astype(full).T
        feature = lax.broadcasted_iota(jnp.int32, (16, width), 1)
        head = lax.broadcasted_iota(jnp.int32, (16, width), 0)
        member = ((feature >= head * HD) & (feature < (head + 1) * HD)).astype(full).astype(low)
        high = products.astype(low)
        rest = (products - high.astype(full)).astype(low)
        delta[...] = dot_nt(member, high) + dot_nt(member, rest)

    def pair_step(p):
        lanes = pl.ds(pl.multiple_of(p * PAIR, PAIR), PAIR)
        q_pair = q_ref[:, lanes] * jnp.asarray(scale, low)
        k_pair = k_ref[:, lanes]
        v_pair = v_ref[:, lanes]
        g_pair = dctx[:, lanes]
        key_grad = jnp.zeros((tokens, PAIR), full)
        value_grad = jnp.zeros((tokens, PAIR), full)
        for h in range(2):
            q_half = q_pair * masks[h]
            g_half = g_pair * masks[h]
            scores = dot_nt(k_pair * masks[h] + codes[0, h], q_half + codes[1, h])
            attention = jnp.exp(scores - lse_ref[0, pl.ds(2 * p + h, 1), :]).astype(low)
            value_grad = value_grad + dot_nn(attention, g_half)
            attention_grad = dot_nt(v_pair, g_half)
            score_grad = attention * (attention_grad - delta[pl.ds(2 * p + h, 1), :]).astype(low)
            key_grad = key_grad + dot_nn(score_grad, q_half)
            rows = pl.ds(pl.multiple_of(p * PAIR + h * HD, HD), HD)
            dqt[rows, :] = dot_nn(kt[rows, :], score_grad) * scale
        grads[1, here, lanes] = key_grad.astype(low)
        grads[2, here, lanes] = value_grad.astype(low)

    def inputs_step():
        @pl.when(r == 0)
        def _():
            loads[3].wait()

        query_grad = dqt[...].T.astype(low)
        grads[0, here, :] = query_grad
        value_grad = grads[2, here, :]
        dx_ref[...] = (
            dr1_ref[...]
            + dot_nt(query_grad, w_ref[0])
            + dot_nt(grads[1, here, :], w_ref[1])
            + dot_nt(value_grad, w_ref[2])
        )
        dvec_ref[0:1, :] += column_sum(query_grad.astype(full))
        dvec_ref[1:2, :] += column_sum(value_grad.astype(full))

    def position(n, carry):
        side.tick(r * ticks + n)

        @pl.when(n == 0)
        def _():
            prepare()

        @pl.when((n >= 1) & (n <= pairs))
        def _():
            pair_step(n - 1)

        @pl.when(n == pairs + 1)
        def _():
            inputs_step()

        @pl.when((n > pairs + 1) & (r == last_row))
        def _():
            j = n - (pairs + 2)
            dw_ref[j] = dot_nn(xt[...], grads[j]).astype(low)

        return carry

    lax.fori_loop(0, ticks, position, 0)
    side.leave(r == last_row, plan.rows * ticks)


def attend_back(da, dr1, hidden, kept, seg_column, weights, start, plan, identity=None):
    q, k, v, ctxt, lse = kept
    tokens, width = da.shape
    rows = tokens // L
    heads = width // HD
    shape = jax.ShapeDtypeStruct
    plan.start, plan.rows = start, rows

    def row_block():
        return pl.BlockSpec((L, width), lambda r: (r, 0))

    return pl.pallas_call(
        functools.partial(attend_back_kernel, plan),
        grid=(rows,),
        out_shape=(
            shape((4 - plan.own, width, width), low), shape((tokens, width), full), shape((8, width), full),
            *plan.results,
        ),
        in_specs=[
            ANYWHERE,
            row_block(), row_block(), row_block(), row_block(), row_block(),
            ANYWHERE,
            pl.BlockSpec((1, heads, L), lambda r: (r, 0, 0)),
            pl.BlockSpec((1, L, 1), lambda r: (r, 0, 0)),
            ANYWHERE,
            *plan.argument_specs,
        ],
        out_specs=(
            pl.BlockSpec((4 - plan.own, width, width), lambda r: (0, 0, 0), pipeline_mode=pl.Buffered(1)),
            row_block(),
            pl.BlockSpec((8, width), lambda r: (0, 0)),
            *plan.result_specs,
        ),
        scratch_shapes=[
            pltpu.VMEM((2, 2, L, PAIR), low),
            pltpu.VMEM((L, width), low),
            pltpu.VMEM((width, L), low),
            pltpu.VMEM((16, L), full),
            pltpu.VMEM((width, L), full),
            pltpu.VMEM((width, tokens), low),
            pltpu.VMEM((3, tokens, width), low),
            pltpu.VMEM((1, 4, 2, width // 8, width) if plan.own else (8, 128), low),
            pltpu.VMEM((tokens, width), low),
            pltpu.VMEM((width, tokens), low),
            pltpu.VMEM((4, width, width), low),
            pltpu.SemaphoreType.DMA((4,)),
            *plan.scratch,
        ],
        compiler_params=pltpu.CompilerParams(
            dimension_semantics=("arbitrary",), vmem_limit_bytes=60 * MIB,
            collective_id=identity, has_side_effects=identity is not None,
        ),
        cost_estimate=pl.CostEstimate(
            flops=16 * tokens * width * width + 10 * tokens * L * width,
            bytes_accessed=30 * MIB,
            transcendentals=tokens * L * heads,
        ),
        name="attend_backward",
    )(da, dr1, hidden, q, k, v, ctxt, lse, seg_column, weights, *plan.arguments)


def moments(rotated, first, second):
    first_new = beta_one * first + (1.0 - beta_one) * rotated
    second_new = beta_two * second + (1.0 - beta_two) * rotated * rotated
    direction = (
        first_new
        / (1.0 - beta_one**STEP)
        / (jnp.sqrt(second_new / (1.0 - beta_two**STEP)) + adam_epsilon)
    )
    return first_new, second_new, direction


def pack_lanes(piece):
    rows = piece.shape[0] // 2
    return jnp.concatenate([piece[:rows], piece[rows:]], axis=1)


def unpack_lanes(piece):
    columns = piece.shape[1] // 2
    return jnp.concatenate([piece[:, :columns], piece[:, columns:]], axis=0)


def optimizer_kernel(plan, *refs):
    spans = len(plan.spans)
    inputs, ready, dvecs, bases, lines_in, outputs, lines_out, scratch, sum_refs, vec_refs, line_refs = split_refs(
        refs, 6, plan.ready, plan.dvecs, plan.bases, spans, 5, spans, 21, SUM_REFS, SUM_REFS, 2 * bool(spans)
    )
    index_ref, place_ref, tail_hbm, first_hbm, second_hbm, blocks = inputs
    new_ref, low_ref, first_out, second_out, vec_out = outputs
    (store, left, right, first_in, second_in, g_out, g_in, t_out, t_in, e_out, e_in, w_out, w_in, vec_source,
     load_sem, g_sem, t_sem, e_sem, w_sem, left_sem, right_sem) = scratch
    slots, owners = g_in.shape[0], g_in.shape[1]
    z_count = t_in.shape[1]
    place = Place(z_count)
    dp, z = place.dp, place.z
    dps = [lax.rem(dp + d, owners) for d in range(owners)]
    count = blocks.shape[0]
    many = tail_hbm.shape[0]
    tail_times = [[many * stage + n for n in range(many)] for stage in range(5)]
    tail = BlockSum(place, [tail_hbm], sum_refs, tail_times)
    vec = BlockSum(place, [vec_source], vec_refs, [[many * stage + 1] for stage in range(5)])
    order = plan.free + [s for s in range(slots) if s not in plan.free]
    lines = line_gathers(place, plan.spans, lines_in, lines_out, line_refs, z_count)
    every = list(bases) + list(lines_out)
    late = [s for s in range(slots) if plan.left_map[s][0] >= len(bases)]

    def load(refs_map, target, sem, s):
        n, at = refs_map[s]
        return pltpu.make_async_copy(every[n].at[:, at], target.at[:, s], sem.at[s])

    def load_first(s):
        return pltpu.make_async_copy(first_hbm.at[s], first_in.at[s], load_sem.at[0, s])

    def load_second(s):
        return pltpu.make_async_copy(second_hbm.at[s], second_in.at[s], load_sem.at[1, s])

    for s in order:
        load(plan.right_map, right, right_sem, s).start()
        if s not in late:
            load(plan.left_map, left, left_sem, s).start()
        load_first(s).start()
        load_second(s).start()
    greet([(other, z) for other in dps[1:]] + place.z_partners())
    start = many
    for part in ready:
        store[start : start + part.shape[0]] = part[...]
        start += part.shape[0]
    store[0:many] = jnp.zeros((many,) + store.shape[1:], low)
    store[count] = jnp.zeros(store.shape[1:], low)
    rows = plan.vector_rows
    stacked = jnp.concatenate(
        [dvecs[0][0:2, :], dvecs[1][2:rows, :], dvecs[2][0:2, :], dvecs[3][2:rows, :],
         jnp.zeros((vec_source.shape[-1] - 2 * rows, blocks.shape[2]), full)], axis=0
    )
    vec_source[0] = stacked.T.reshape(vec_source.shape[1:])

    def g_copy(s, d):
        other = dps[d]
        return remote(g_out.at[s, d], g_in.at[s, dp], g_sem.at[0, s, d], g_sem.at[1, s, owners - d], (other, z))

    def t_copy(s, d):
        other = place.zs[d]
        return remote(t_out.at[s, d], t_in.at[s, z], t_sem.at[0, s, d], t_sem.at[1, s, z_count - d], (dp, other))

    def e_copy(s, d):
        other = place.zs[d]
        return remote(e_out.at[s, d], e_in.at[s, z], e_sem.at[0, s, d], e_sem.at[1, s, z_count - d], (dp, other))

    def w_copy(s, d):
        other = dps[d]
        return remote(
            w_out.at[s, other], w_in.at[s * owners + dp], w_sem.at[0, s, d], w_sem.at[1, s, owners - d], (other, z)
        )

    def send_out(s):
        for d in range(1, owners):
            g_out[s, d] = store[index_ref[s * owners + dps[d]]]
            g_copy(s, d).start()
        g_in[s, dp] = store[index_ref[s * owners + dp]]

    def turn(s):
        for d in range(1, owners):
            g_copy(s, d).wait()
        load(plan.right_map, right, right_sem, s).wait()
        grad = jnp.concatenate([unfold(g_in[s, c].astype(full)) for c in range(owners)], axis=0).astype(low)
        for d in range(1, z_count):
            t_out[s, d] = pack_lanes(dot_nt(right[place.zs[d], s], grad)).astype(low)
            t_copy(s, d).start()
        t_in[s, z] = pack_lanes(dot_nt(right[z, s], grad)).astype(low)

    def adapt(s):
        for d in range(1, z_count):
            t_copy(s, d).wait()
        load_first(s).wait()
        load_second(s).wait()
        load(plan.left_map, left, left_sem, s).wait()
        rotated = jnp.zeros(first_in.shape[1:], full)
        for f in range(z_count):
            rotated = rotated + dot_nn(unpack_lanes(t_in[s, f].astype(full)).astype(low), left[f, s])
        first_new, second_new, direction = moments(rotated, first_in[s], second_in[s])
        first_out[s] = first_new
        second_out[s] = second_new
        direction = direction.astype(low)
        for d in range(1, z_count):
            e_out[s, d] = pack_lanes(dot_nt(left[place.zs[d], s], direction)).astype(low)
            e_copy(s, d).start()
        e_in[s, z] = pack_lanes(dot_nt(left[z, s], direction)).astype(low)

    def step_back(s):
        for d in range(1, z_count):
            e_copy(s, d).wait()
        step = jnp.zeros((left.shape[2], left.shape[3]), full)
        for f in range(z_count):
            step = step + dot_nn(unpack_lanes(e_in[s, f].astype(full)).astype(low), right[f, s])
        share = step.shape[0] // owners
        for c in range(owners):
            w_out[s, c] = fold(step[c * share : (c + 1) * share]).astype(low)
        for d in range(1, owners):
            w_copy(s, d).start()
        w_in[s * owners + dp] = w_out[s, dp]

    def sums(stage):
        for t in range(many * stage, many * (stage + 1)):
            tail.tick(t)
            vec.tick(t)

    free = plan.free
    sums(0)
    for line in lines:
        line.start()
    for s in free:
        send_out(s)
    sums(1)
    for s in free:
        turn(s)
    sums(2)
    for s in free:
        adapt(s)
    sums(3)
    sums(4)
    for i in range(many):
        store[i] = tail.finish(i).astype(low)
    rest = order[len(free) :]
    for s in rest[:2]:
        send_out(s)
    for s in free:
        step_back(s)
    for line in lines:
        line.wait()
    for s in late:
        load(plan.left_map, left, left_sem, s).start()
    for k in range(len(rest) + 2):
        if k < len(rest):
            turn(rest[k])
            if k + 2 < len(rest):
                send_out(rest[k + 2])
        if 0 <= k - 1 < len(rest):
            adapt(rest[k - 1])
        if 0 <= k - 2 < len(rest):
            step_back(rest[k - 2])

    vec_out[...] = vec.finish(0)
    for s in range(slots):
        for d in range(1, owners):
            w_copy(s, d).wait()

    def block_step(b, carry):
        step = unfold(w_in[place_ref[b]].astype(full))
        block = blocks[b]
        new = block - matrix_rate * (step + weight_decay * block)
        new_ref[b] = new
        low_ref[b] = new.astype(low)
        return carry

    lax.fori_loop(0, count, block_step, 0)


class OptimizerPlan:
    def __init__(self, ready, dvecs, bases, spans, left_map, right_map, free, vector_rows):
        self.ready, self.dvecs, self.bases, self.spans = ready, dvecs, bases, spans
        self.left_map, self.right_map, self.free, self.vector_rows = left_map, right_map, free, vector_rows


def optimizer(
    index, places, tail, ready, dvecs, vector_rows, bases, lines, left_map, right_map, free, first, second, blocks,
    z_count, identity,
):
    slots, columns, width = first.shape
    owners = index.shape[0] // slots
    count, rows = blocks.shape[0], blocks.shape[1]
    span = bases[0].shape[2]
    lanes = 128
    shape = jax.ShapeDtypeStruct
    piece = (2 * rows, width // 2)
    tile = (span // 2, 2 * columns)
    smem = pl.BlockSpec(memory_space=pltpu.SMEM)
    spans = [(first_slot, amount) for _, first_slot, amount in lines]
    plan = OptimizerPlan(len(ready), len(dvecs), len(bases), spans, left_map, right_map, free, vector_rows)
    line_shapes = [shape((z_count, amount) + basis.shape[1:], low) for basis, _, amount in lines]
    return pl.pallas_call(
        functools.partial(optimizer_kernel, plan),
        out_shape=(
            shape(blocks.shape, full), shape(blocks.shape, low), shape(first.shape, full), shape(first.shape, full),
            shape((rows, lanes), full), *line_shapes,
        ),
        in_specs=[smem, smem, ANYWHERE, ANYWHERE, ANYWHERE, IN_VMEM]
        + [IN_VMEM] * (len(ready) + len(dvecs)) + [ANYWHERE] * (len(bases) + len(lines)),
        out_specs=(IN_VMEM,) * 5 + (ANYWHERE,) * len(lines),
        scratch_shapes=[
            pltpu.VMEM((count + 1,) + piece, low),
            pltpu.VMEM((z_count, slots, span, width), low),
            pltpu.VMEM((z_count, slots, columns, width), low),
            pltpu.VMEM((slots, columns, width), full),
            pltpu.VMEM((slots, columns, width), full),
            pltpu.VMEM((slots, owners) + piece, low),
            pltpu.VMEM((slots, owners) + piece, low),
            pltpu.VMEM((slots, z_count) + tile, low),
            pltpu.VMEM((slots, z_count) + tile, low),
            pltpu.VMEM((slots, z_count) + tile, low),
            pltpu.VMEM((slots, z_count) + tile, low),
            pltpu.VMEM((slots, owners) + piece, low),
            pltpu.VMEM((slots * owners,) + piece, low),
            pltpu.VMEM((1, owners // 2, 2, width // owners, lanes), full),
            pltpu.SemaphoreType.DMA((2, slots)),
            pltpu.SemaphoreType.DMA((2, slots, owners)),
            pltpu.SemaphoreType.DMA((2, slots, z_count)),
            pltpu.SemaphoreType.DMA((2, slots, z_count)),
            pltpu.SemaphoreType.DMA((2, slots, owners)),
            pltpu.SemaphoreType.DMA((slots,)),
            pltpu.SemaphoreType.DMA((slots,)),
            *sum_scratch(tail.shape[0], tail.shape[3], width, z_count),
            *sum_scratch(1, width // owners, lanes, z_count, full),
            *line_scratch(len(lines), z_count),
        ],
        compiler_params=pltpu.CompilerParams(
            vmem_limit_bytes=60 * MIB, collective_id=identity, has_side_effects=True
        ),
        cost_estimate=pl.CostEstimate(
            flops=8 * slots * span * width * width, bytes_accessed=40 * MIB, transcendentals=slots * width * columns
        ),
        name="optimizer",
    )(index, places, tail, first, second, blocks, *ready, *dvecs, *bases, *[basis for basis, _, _ in lines])


def slot_table(owner, slots, owner_rows):
    block_count = owner.shape[0]
    same_owner = owner[:, None] == owner[None, :]
    ordering = jnp.arange(block_count, dtype=jnp.int32)
    earlier = ordering[None, :] < ordering[:, None]
    ranking = jnp.sum(jnp.where(same_owner & earlier, 1, 0), axis=1).astype(jnp.int32)
    owner_match = owner[None, :] == jnp.arange(owner_rows, dtype=jnp.int32)[:, None]
    slot_match = ranking[None, :] == jnp.arange(slots, dtype=jnp.int32)[:, None]
    return jnp.where(slot_match[:, None, :] & owner_match[None, :, :], 1.0, 0.0).astype(full)


def scatter_sum(grads):
    blocks, width = grads.shape[0], grads.shape[2]
    cut = grads.reshape(blocks, lax.axis_size("dp"), -1, width).transpose(1, 0, 2, 3)
    outer = lax.psum_scatter(cut, "dp", scatter_dimension=0, tiled=False)
    blocks, rows, width = outer.shape
    count = lax.axis_size("fsdp")
    cut = outer.reshape(blocks, count, rows // count, width).transpose(1, 0, 2, 3)
    return lax.psum_scatter(cut, "fsdp", scatter_dimension=0, tiled=False)


def scatter_vectors(grads):
    rows, width = grads.shape
    count = lax.axis_size("dp") * lax.axis_size("fsdp")
    cut = grads.reshape(rows, count, width // count).transpose(1, 0, 2)
    return lax.psum_scatter(cut, ("dp", "fsdp"), scatter_dimension=0, tiled=False)


def gathering_program(
    tokens, segment, blocks, vectors, owner, left_basis, right_basis, rot_first, rot_second, cotangent, z_count
):
    layers, vector_rows = vectors.shape[:2]
    count, shard_rows, width = blocks.shape
    per_layer = count // layers
    inner = (per_layer - 4) // 2
    owners = lax.axis_size("dp")
    slots = rot_first.shape[0]
    part = width // owners
    lanes = 128
    seg_column = segment[:, :, None]

    order = [0, 1, 2, 3]
    for c in range(inner):
        order += [4 + c, 4 + inner + c]
    head = order + [per_layer + j for j in order[:4]]
    rest = [per_layer + j for j in order[4:]]
    vec_shard = vectors.astype(low).astype(full).reshape(layers * vector_rows, shard_rows).T
    vec_shard = jnp.pad(vec_shard, ((0, 0), (0, lanes - layers * vector_rows)))[None, None]
    left_low = left_basis.reshape(slots, -1, width).astype(low)
    right_low = right_basis.transpose(0, 2, 1).astype(low)

    plan = ForwardPlan(
        inner, 0, blocks, head, vec_shard, vector_rows, [(right_low, 0, 2)], lead=5, row_positions=(1,), z_count=z_count
    )
    empty_vec = jnp.zeros((16, width), full)
    results = forward_layer(tokens, seg_column, empty_vec, empty_vec, full, plan, 6)
    kept_a = results[:12]
    hidden, weights_a, vec_a, vec_b, right_01 = results[12:]
    weights_a = weights_a.reshape(-1, width, width)
    plan = ForwardPlan(inner, 4, blocks, rest, lines=[(right_low, 2, 2)], lead=0, row_positions=(1, 4), z_count=z_count)
    plan.order = [per_layer + j for j in range(4)]
    results = forward_layer(hidden, seg_column, vec_b, weights_a, low, plan, 7)
    kept_b = results[:12]
    layer_out, weights_b, right_23 = results[12:]
    weights_b = weights_b.reshape(-1, width, width)

    def cut(grads):
        return grads.reshape(-1, owners // 2, 2, part, width)

    size = (part, width)
    own_b, own_a = 4, 3

    def left_over(own):
        return 2 * inner - own, own % 2

    plan = Plan(None, [(right_low, 4, 1)], z_count, own_b, size, wide_ready(own_b))
    dw_wide, dr1, da, dvec_wide_b, wide_sum_b, right_4 = wide_back(
        cotangent, kept_b[5:], vec_b, weights_b, (0, 1, 2), plan, 1
    )
    pending, skip = left_over(own_b)
    plan = Plan(cut(dw_wide), [(left_low, 3, 1)], z_count, 1, size, list(range(pending + 1)), skip)
    dw_attend, upstream, dvec_attend_b, attend_sum_b, left_3 = attend_back(
        da, dr1, hidden, kept_b[:5], seg_column, weights_a, per_layer, plan, 2
    )
    plan = Plan(
        cut(dw_attend), [(left_low, 4, 1), (left_low, 0, 1)], z_count, own_a, size, [0, 1, 2] + wide_ready(own_a)
    )
    dw_wide, dr1, da, dvec_wide_a, wide_sum_a, left_4, left_0 = wide_back(
        upstream, kept_a[5:], vec_a, weights_a, (4, 5, 2), plan, 3
    )
    pending, skip = left_over(own_a)
    plan = Plan(cut(dw_wide), [(left_low, 1, 1)], z_count, 1, size, list(range(pending + 1)), skip)
    dw_attend, upstream, dvec_attend_a, attend_sum_a, left_1 = attend_back(
        da, dr1, tokens, kept_a[:5], seg_column, weights_a, 0, plan, 5
    )

    three = list(range(3))

    def early(own):
        return [4 + n // 2 + inner * (n % 2) for n in range(own)]

    def late(own):
        return [4 + c + inner * k for k in range(2) for c in range(inner) if 2 * c + k >= own] + [3]

    held_order = three + late(own_a) + [per_layer + j for j in three] + early(own_a)
    held_order += [per_layer + j for j in late(own_b) + early(own_b)]
    rank = jnp.asarray([held_order.index(j) for j in range(count)], jnp.int32)
    table = slot_table(owner, slots, owners).reshape(slots * owners, count)
    held = jnp.sum(table, axis=1)
    index = jnp.where(held > 0, jnp.sum(table * rank, axis=1), count).astype(jnp.int32)
    places = jnp.sum(table * jnp.arange(slots * owners, dtype=jnp.int32)[:, None], axis=0).astype(jnp.int32)
    bases = (right_01, right_23, right_4, left_0, left_1, left_3, left_4)
    right_map = [(0, 0), (0, 1), (1, 0), (1, 1), (2, 0)]
    left_map = [(3, 0), (4, 0), (7, 0), (5, 0), (6, 0)]
    free = list(range(3, slots))
    new_blocks, new_low, first_new, second_new, vec_sum, _ = optimizer(
        index, places, cut(dw_attend), (attend_sum_a, wide_sum_a, attend_sum_b, wide_sum_b),
        (dvec_attend_a, dvec_wide_a, dvec_attend_b, dvec_wide_b), vector_rows, bases, [(left_low, 2, 1)], left_map, right_map, free,
        rot_first.transpose(0, 2, 1), rot_second.transpose(0, 2, 1), blocks, z_count, 4,
    )
    first_new, second_new = first_new.transpose(0, 2, 1), second_new.transpose(0, 2, 1)
    vector_grad = vec_sum[:, : layers * vector_rows].T.reshape(layers, vector_rows, shard_rows)
    return layer_out, upstream, new_blocks, new_low, first_new, second_new, vector_grad


def plain_program(
    tokens, segment, blocks, vectors, owner, left_basis, right_basis, rot_first, rot_second, cotangent
):
    layers, vector_rows = vectors.shape[:2]
    per_layer = blocks.shape[0] // layers
    inner = (per_layer - 4) // 2
    width = blocks.shape[2]
    owner_rows = lax.axis_size("dp")
    slots = rot_first.shape[0]
    selector = slot_table(owner, slots, owner_rows)
    vector_parts = lax.all_gather(vectors.astype(low), ("dp", "fsdp"), axis=0, tiled=False)
    vector_full = vector_parts.transpose(1, 2, 0, 3).reshape(layers, vector_rows, width).astype(full)
    blocks_low, vector_full = lax.optimization_barrier((blocks.astype(low), vector_full))

    seg_column = segment[:, :, None]
    state = tokens
    kept = []
    for layer_index in range(layers):
        start = per_layer * layer_index
        weights = lax.all_gather(blocks_low[start : start + per_layer], ("dp", "fsdp"), axis=1, tiled=True)
        out_dtype = low if layer_index == layers - 1 else full
        results = forward_layer(
            state, seg_column, vector_full[layer_index], weights, out_dtype, ForwardPlan(inner, per_layer)
        )
        kept.append((state, weights, results[:5], results[5:12]))
        state = results[12]
    layer_out = state
    upstream = cotangent
    right_low = lax.all_gather(right_basis.astype(low), "fsdp", axis=2, tiled=True)
    block_shards = [None] * layers
    vector_shards = [None] * layers
    for layer_index in reversed(range(layers)):
        hidden, weights, attend_kept, wide_kept = kept[layer_index]
        dw_wide, dr1, da, dvec_wide = wide_back(
            upstream, wide_kept, vector_full[layer_index], weights, (4, 4 + inner, 1), Plan()
        )
        wide_shard = scatter_sum(dw_wide.reshape(-1, width, width))
        dw_attend, upstream, dvec_attend = attend_back(
            da, dr1, hidden, attend_kept, seg_column, weights, 0, Plan()
        )
        dvec = jnp.concatenate([dvec_attend[:2], dvec_wide[2:vector_rows]], axis=0)
        block_shards[layer_index] = jnp.concatenate([scatter_sum(dw_attend), wide_shard], axis=0)
        vector_shards[layer_index] = scatter_vectors(dvec)
    vector_grad = jnp.stack(vector_shards)
    block_grad = jnp.concatenate(block_shards, axis=0)
    outgoing = jnp.einsum("srk,kid->srid", selector.astype(low), block_grad, preferred_element_type=full)
    incoming = lax.all_to_all(outgoing.astype(low), "dp", split_axis=1, concat_axis=1, tiled=True)
    owned = incoming.reshape(slots, -1, width)
    turned = jnp.einsum("sik,skj->sij", owned, right_low, preferred_element_type=full).astype(low)
    left_rows = left_basis.reshape(slots, -1, width).astype(low)
    partial_sums = jnp.einsum("sra,srb->sab", left_rows, turned, preferred_element_type=full)
    rotated = lax.psum_scatter(
        partial_sums.astype(low), "fsdp", scatter_dimension=2, tiled=True
    ).astype(full)
    first_new, second_new, direction = moments(rotated, rot_first, rot_second)
    direction_full = lax.all_gather(direction.astype(low), "fsdp", axis=2, tiled=True)
    back_right = jnp.einsum("sab,scb->sac", direction_full, right_low, preferred_element_type=full)
    step_rows = jnp.einsum(
        "sia,sac->sic", left_rows, back_right.astype(low), preferred_element_type=full
    )
    returned = lax.all_to_all(
        step_rows.reshape(slots, owner_rows, -1, width).astype(low),
        "dp",
        split_axis=1,
        concat_axis=1,
        tiled=True,
    )
    step_shard = jnp.einsum("srk,srid->kid", selector.astype(low), returned, preferred_element_type=full)
    new_blocks = blocks - matrix_rate * (step_shard + weight_decay * blocks)
    return layer_out, upstream, new_blocks, new_blocks.astype(low), first_new, second_new, vector_grad


def shards(
    tokens,
    segment,
    blocks,
    vectors,
    owner,
    left_basis,
    right_basis,
    rot_first,
    rot_second,
    vec_first,
    vec_second,
    cotangent,
):
    operands = (
        tokens, segment, blocks, vectors, owner, left_basis, right_basis, rot_first, rot_second, cotangent
    )
    z_count = lax.axis_size("fsdp")
    if lax.axis_size("dp") == 8 and z_count == 4:
        results = gathering_program(*operands, z_count)
    else:
        results = plain_program(*operands)
    layer_out, upstream, new_blocks, new_low, first_new, second_new, vector_grad = results
    vector_first = beta_one * vec_first + (1.0 - beta_one) * vector_grad
    vector_second = beta_two * vec_second + (1.0 - beta_two) * vector_grad * vector_grad
    vector_step = (
        vector_first
        / (1.0 - beta_one**STEP)
        / (jnp.sqrt(vector_second / (1.0 - beta_two**STEP)) + adam_epsilon)
    )
    vector_new = vectors - vector_rate * (vector_step + weight_decay * vectors)
    return (
        layer_out,
        upstream,
        new_blocks,
        new_low,
        first_new,
        second_new,
        vector_first,
        vector_second,
        vector_new,
    )


def solution(mesh):
    return jax.shard_map(
        shards,
        mesh=mesh,
        in_specs=(
            P(("dp", "fsdp"), None),
            P(("dp", "fsdp"), None),
            P(None, ("dp", "fsdp"), None),
            P(None, None, ("dp", "fsdp")),
            P(),
            P("dp", None, "fsdp", None),
            P("dp", None, "fsdp"),
            P("dp", None, "fsdp"),
            P("dp", None, "fsdp"),
            P(None, None, ("dp", "fsdp")),
            P(None, None, ("dp", "fsdp")),
            P(("dp", "fsdp"), None),
        ),
        out_specs=(
            P(("dp", "fsdp"), None),
            P(("dp", "fsdp"), None),
            P(None, ("dp", "fsdp"), None),
            P(None, ("dp", "fsdp"), None),
            P("dp", None, "fsdp"),
            P("dp", None, "fsdp"),
            P(None, None, ("dp", "fsdp")),
            P(None, None, ("dp", "fsdp")),
            P(None, None, ("dp", "fsdp")),
        ),
        check_vma=False,
    )
```

```python
import functools

import jax
import jax.numpy as jnp
from jax import lax
from jax.experimental import pallas as pl
from jax.experimental.pallas import tpu as pltpu
from jax.sharding import PartitionSpec as P

H = 12
HD = 64
L = 512
STEP = 5
SEGS = 4
PAIR = 2 * HD
MIB = 1 << 20

beta_one = 0.5
beta_two = 0.5
adam_epsilon = 1e-08
norm_epsilon = 1e-06
matrix_rate = 0.03
vector_rate = 0.2
weight_decay = 0.01
masked_score = -1e30
low = jnp.bfloat16
full = jnp.float32


def dot_nn(a, b):
    return lax.dot_general(a, b, (((1,), (0,)), ((), ())), preferred_element_type=full)


def dot_nt(a, b):
    return lax.dot_general(a, b, (((1,), (1,)), ((), ())), preferred_element_type=full)


def dot_tn(a, b):
    return lax.dot_general(a, b, (((0,), (0,)), ((), ())), preferred_element_type=full)


def gelu_parts(z):
    t = pl.reciprocal(1.0 + 0.23164190 * jnp.abs(z), approx=True)
    square = z * z
    bell = jnp.exp2(-0.7213475204444817 * square)
    poly = ((((0.5307027145 * t - 0.7265760135) * t + 0.7107068705) * t - 0.142248368) * t + 0.127414796) * t
    tail = poly * bell
    phi = jnp.where(z >= 0, 1.0 - tail, tail)
    return z * phi, phi + (0.3989422804014327 * z) * bell


def norm_parts(residual):
    average = jnp.mean(residual, axis=-1, keepdims=True)
    centered = residual - average
    inverse = lax.rsqrt(jnp.mean(centered * centered, axis=-1, keepdims=True) + norm_epsilon)
    return centered * inverse, inverse


def norm_back(upstream, unit, inverse, gain):
    scaled = upstream * gain
    return inverse * (
        scaled
        - jnp.mean(scaled, axis=-1, keepdims=True)
        - unit * jnp.mean(scaled * unit, axis=-1, keepdims=True)
    )


def column_sum(values):
    return jnp.sum(values, axis=0, keepdims=True)


def half_masks(dtype):
    lane = lax.broadcasted_iota(jnp.int32, (1, PAIR), 1)
    first = (lane < HD).astype(full)
    return first.astype(dtype), (1.0 - first).astype(dtype)


def segment_codes(seg_column, masks):
    lane = lax.broadcasted_iota(jnp.int32, (1, PAIR), 1)
    lane = jnp.where(lane >= HD, lane - HD, lane)
    same = seg_column == lane
    key = jnp.where(same, 1.0, 0.0).astype(low)
    query = jnp.where(same | (lane >= SEGS), 0.0, masked_score).astype(low)
    return [key * masks[1 - h] for h in range(2)], [query * masks[1 - h] for h in range(2)]


class Place:
    def __init__(self, z_count):
        self.dp, self.z = lax.axis_index("dp"), lax.axis_index("fsdp")
        self.core, self.spot = lax.rem(self.dp, 2), lax.div(self.dp, 2)
        x_step = 1 - 2 * lax.rem(self.spot, 2)
        y_step = 2 - 4 * lax.div(self.spot, 2)
        self.spot_a = self.spot + (1 - self.core) * x_step + self.core * y_step
        self.spot_b = self.spot + self.core * x_step + (1 - self.core) * y_step
        self.spot_ab = self.spot + x_step + y_step
        self.sibling = (self.dp + 1 - 2 * self.core, self.z)
        self.near_a = (2 * self.spot_a + self.core, self.z)
        self.near_b = (2 * self.spot_b + self.core, self.z)
        self.z_count = z_count
        self.zs = [lax.rem(self.z + d, z_count) for d in range(z_count)]
        self.has_up, self.has_down = self.z < z_count - 1, self.z > 0
        self.middle = self.has_up & self.has_down
        self.across = lax.rem(self.z + 2, z_count)
        self.beside = jnp.where(self.z < 2, 1 - self.z, 5 - self.z)

    def line_sends(self, d):
        return {1: self.has_up, 2: self.z >= 0, 3: self.has_down}[d]

    def line_receives(self, d):
        return {1: self.has_down, 2: self.z >= 0, 3: self.has_up}[d]

    def chip_partners(self):
        return [self.sibling, self.near_a, self.near_b]

    def z_partners(self):
        return [(self.dp, other) for other in self.zs[1:]]


def greet(partners):
    barrier = pltpu.get_barrier_semaphore()
    for device in partners:
        pl.semaphore_signal(barrier, inc=1, device_id=device, device_id_type=pl.DeviceIdType.MESH)
    pl.semaphore_wait(barrier, len(partners))


def remote(source, target, send, receive, device):
    return pltpu.make_async_remote_copy(
        src_ref=source,
        dst_ref=target,
        send_sem=send,
        recv_sem=receive,
        device_id=device,
        device_id_type=pl.DeviceIdType.MESH,
    )


def fold(piece):
    half = piece.shape[1] // 2
    return jnp.concatenate([piece[:, :half], piece[:, half:]], axis=0)


def unfold(piece):
    rows = piece.shape[0] // 2
    return jnp.concatenate([piece[:rows], piece[rows:]], axis=1)


def looked_up(ticks, t):
    now = functools.reduce(jnp.logical_or, [t == tick for tick in ticks])
    which = sum(n * (t == tick).astype(jnp.int32) for n, tick in enumerate(ticks))
    return now, which


def run_due(stages, t):
    for ticks, stage in stages:
        if isinstance(t, int):
            if t in ticks:
                stage(ticks.index(t))
            continue
        now, block = looked_up(ticks, t)

        @pl.when(now)
        def _():
            stage(block)


def sum_times(ready):
    opens, cores, seconds = [], [], []
    for tick in ready:
        opens.append(max(tick, opens[-1] + 1) if opens else tick)
        cores.append(max(opens[-1] + 1, cores[-1] + 1) if cores else opens[-1] + 1)
        seconds.append(max(cores[-1] + 3, seconds[-1] + 3) if seconds else cores[-1] + 3)
    thirds = [tick + 2 for tick in seconds]
    return opens, cores, seconds, thirds, [tick + 2 for tick in thirds]


ANNOUNCE, FORWARD, FIRST, SECOND, CLOSE = -2, -1, 1, 2, 3


def sum_scratch(count, part, width, z_count, kind=low):
    piece = (2 * part // z_count, width // 2) if kind == low else (part // z_count, width)
    return [
        pltpu.VMEM((count, 4, part, width), kind),
        pltpu.VMEM((count, 4, part, width), kind),
        pltpu.VMEM((count, 2, part, width), kind),
        pltpu.VMEM((count, part, width), kind),
        pltpu.VMEM((count, z_count) + piece, kind),
        pltpu.VMEM((count, z_count) + piece, kind),
        pltpu.VMEM((count,) + piece, kind),
        pltpu.SemaphoreType.DMA((count,)),
        pltpu.SemaphoreType.DMA((count, 2)),
        pltpu.SemaphoreType.DMA((count, 2, 2)),
        pltpu.SemaphoreType.DMA((count, 2)),
        pltpu.SemaphoreType.DMA((count, 2, z_count)),
        pltpu.SemaphoreType.DMA((count, 2)),
    ]


SUM_REFS = 13


class BlockSum:
    def __init__(self, place, sources, refs, times):
        self.place, self.sources, self.times = place, sources, times
        (self.own, self.c, self.b, self.a, self.zs, self.zr, self.far,
         self.own_sem, self.c_sem, self.b_sem, self.a_sem, self.z_sem, self.far_sem) = refs
        self.count = self.c.shape[0]
        self.kind = self.c.dtype
        self.z_count = self.zs.shape[1]

    def load(self, i, block):
        return pltpu.make_async_copy(block.at[:, self.place.core], self.own.at[i], self.own_sem.at[i])

    def core_copy(self, i, block):
        return remote(
            block.at[:, 1 - self.place.core], self.c.at[i], self.c_sem.at[i, 0], self.c_sem.at[i, 1], self.place.sibling
        )

    def second_copy(self, i, k):
        chunk = self.place.spot_b if k == 0 else self.place.spot_ab
        return remote(
            self.c.at[i, chunk], self.b.at[i, k], self.b_sem.at[i, 0, k], self.b_sem.at[i, 1, k], self.place.near_b
        )

    def third_copy(self, i):
        return remote(
            self.c.at[i, self.place.spot_a], self.a.at[i], self.a_sem.at[i, 0], self.a_sem.at[i, 1], self.place.near_a
        )

    def z_copy(self, i, d):
        other = self.place.zs[d]
        return remote(
            self.zs.at[i, other], self.zr.at[i, self.place.z], self.z_sem.at[i, 0, d],
            self.z_sem.at[i, 1, self.z_count - d], (self.place.dp, other),
        )

    def open(self, i):
        first = 0
        for source in self.sources:
            count = source.shape[0]

            @pl.when((i >= first) & (i < first + count))
            def _():
                block = source.at[jnp.clip(i - first, 0, count - 1)]
                self.core_copy(i, block).start()
                self.load(i, block).start()

            first += count

    def after_core(self, i):
        block = self.sources[0].at[0]
        self.core_copy(i, block).wait()
        self.load(i, block).wait()

        def add(k, carry):
            self.c[i, k] = (self.c[i, k].astype(full) + self.own[i, k].astype(full)).astype(self.kind)
            return carry

        lax.fori_loop(0, 4, add, 0)
        self.second_copy(i, 0).start()
        self.second_copy(i, 1).start()

    def after_second(self, i):
        other, spot = self.place.spot_a, self.place.spot
        self.second_copy(i, 1).wait()
        self.c[i, other] = (self.c[i, other].astype(full) + self.b[i, 1].astype(full)).astype(self.kind)
        self.third_copy(i).start()
        self.second_copy(i, 0).wait()
        self.c[i, spot] = (self.c[i, spot].astype(full) + self.b[i, 0].astype(full)).astype(self.kind)

    def after_third(self, i):
        self.third_copy(i).wait()
        total = self.c[i, self.place.spot].astype(full) + self.a[i].astype(full)
        rows = total.shape[0] // self.z_count
        for k in range(self.z_count):
            piece = total[k * rows : (k + 1) * rows]
            self.zs[i, k] = fold(piece).astype(low) if self.kind == low else piece
        place = self.place
        for d in (1, 3):
            @pl.when(place.line_sends(d))
            def _():
                self.z_copy(i, d).start()

        @pl.when(jnp.logical_not(place.middle))
        def _():
            self.z_copy(i, 2).start()
            self.far_copy(i).start()
            opposite = self.z_count - 1 - place.z
            self.zr[i, opposite] = jnp.zeros(self.zr.shape[2:], self.kind)

    def far_copy(self, i):
        place = self.place
        return remote(
            self.zs.at[i, self.z_count - 1 - place.z], self.far.at[i], self.far_sem.at[i, 0], self.far_sem.at[i, 1],
            (place.dp, place.beside),
        )

    def relay(self, i):
        @pl.when(self.place.middle)
        def _():
            self.far_copy(i).wait_recv()
            across = self.place.across
            self.zs[i, across] = (self.zs[i, across].astype(full) + self.far[i].astype(full)).astype(self.kind)
            self.z_copy(i, 2).start()

    def finish(self, i):
        for d in range(1, self.z_count):
            @pl.when(self.place.line_sends(d))
            def _():
                self.z_copy(i, d).wait_send()

            @pl.when(self.place.line_receives(d))
            def _():
                self.z_copy(i, d).wait_recv()

        @pl.when(jnp.logical_not(self.place.middle))
        def _():
            self.far_copy(i).wait_send()

        total = self.zs[i, self.place.z].astype(full)
        for d in range(1, self.z_count):
            total = total + self.zr[i, self.place.zs[d]].astype(full)
        return total

    def tick(self, t):
        stages = (self.relay, self.after_third, self.after_second, self.after_core, self.open)
        run_due(list(zip(self.times[::-1], stages)), t)

    @property
    def last(self):
        return self.times[4][-1]


class LineGather:
    def __init__(self, place, source, target, first, local_sem, sem, z_count):
        self.place = place
        self.source = source.at[pl.ds(first, target.shape[1])]
        self.target, self.local_sem, self.sem, self.z_count = target, local_sem, sem, z_count

    def hop_copy(self, hop, way):
        dp, z = self.place.dp, self.place.z
        if way == 0:
            piece, other, coming = z - hop + 1, z + 1, z - hop
            sends = (piece >= 0) & (other < self.z_count)
            receives = coming >= 0
        else:
            piece, other, coming = z + hop - 1, z - 1, z + hop
            sends = (piece < self.z_count) & (other >= 0)
            receives = coming < self.z_count
        piece = jnp.clip(piece, 0, self.z_count - 1)
        other = jnp.clip(other, 0, self.z_count - 1)
        source = self.source if hop == 1 else self.target.at[piece]
        copy = remote(source, self.target.at[piece], self.sem.at[way, 0, hop - 1], self.sem.at[way, 1, hop - 1], (dp, other))
        return copy, sends, receives

    def local(self):
        return pltpu.make_async_copy(self.source, self.target.at[self.place.z], self.local_sem)

    def start(self, hop):
        if hop == 1:
            self.local().start()
        for way in range(2):
            copy, sends, _ = self.hop_copy(hop, way)

            @pl.when(sends)
            def _():
                copy.start()

    def wait(self, hop):
        if hop == 1:
            self.local().wait()
        for way in range(2):
            copy, sends, receives = self.hop_copy(hop, way)

            @pl.when(sends)
            def _():
                copy.wait_send()

            @pl.when(receives)
            def _():
                copy.wait_recv()

    def advance(self, hop):
        if hop > 1:
            self.wait(hop - 1)
        if hop < self.z_count:
            self.start(hop)


def gather_scratch(count, group, rows, width, z_count, kind=low):
    piece = (2 * rows // z_count, width // 2) if kind == low else (rows // z_count, width)
    return [
        pltpu.VMEM((count, z_count, group) + piece, kind),
        pltpu.SemaphoreType.DMA((count, 2, z_count)),
        pltpu.SemaphoreType.DMA((count, 2)),
        pltpu.SemaphoreType.DMA((count, 2, 2)),
        pltpu.SemaphoreType.DMA((count, 2)),
        pltpu.SemaphoreType.DMA((count, 2)),
    ]


GATHER_REFS = 6


class BlockGather:
    def __init__(self, place, source, whole, base, refs):
        self.place, self.source, self.whole, self.base = place, source, whole, base
        self.zr, self.z_sem, self.a_sem, self.b_sem, self.c_sem, self.far_sem = refs
        self.count, self.z_count, self.group = self.zr.shape[:3]

    def blocks(self, i):
        return pl.ds(self.base + self.group * i, self.group)

    def z_copy(self, i, d):
        place = self.place
        return remote(
            self.source.at[i], self.zr.at[i, place.z], self.z_sem.at[i, 0, d], self.z_sem.at[i, 1, self.z_count - d],
            (place.dp, place.zs[d]),
        )

    def chunk(self, i, spot):
        return self.whole.at[self.blocks(i), spot, self.place.core]

    def first_copy(self, i):
        chunk = self.chunk(i, self.place.spot)
        return remote(chunk, chunk, self.a_sem.at[i, 0], self.a_sem.at[i, 1], self.place.near_a)

    def second_copy(self, i, k):
        chunk = self.chunk(i, self.place.spot if k == 0 else self.place.spot_a)
        return remote(chunk, chunk, self.b_sem.at[i, 0, k], self.b_sem.at[i, 1, k], self.place.near_b)

    def core_copy(self, i):
        chunks = self.whole.at[self.blocks(i), :, self.place.core]
        return remote(chunks, chunks, self.c_sem.at[i, 0], self.c_sem.at[i, 1], self.place.sibling)

    def far_copy(self, i):
        place = self.place
        piece = self.zr.at[i, place.across]
        return remote(piece, piece, self.far_sem.at[i, 0], self.far_sem.at[i, 1], (place.dp, place.beside))

    def announce(self, i):
        for d in range(1, self.z_count):
            @pl.when(self.place.line_sends(d))
            def _():
                self.z_copy(i, d).start()

        self.zr[i, self.place.z] = self.source[i]

    def forward(self, i):
        @pl.when(self.place.middle)
        def _():
            self.z_copy(i, 2).wait_recv()
            self.far_copy(i).start()

    def begin(self):
        for i in range(min(-ANNOUNCE, self.count)):
            self.announce(i)

    def open(self, i):
        place = self.place
        for d in range(1, self.z_count):
            @pl.when(place.line_sends(d))
            def _():
                self.z_copy(i, d).wait_send()

        for d in (1, 3):
            @pl.when(place.line_receives(d))
            def _():
                self.z_copy(i, d).wait_recv()

        @pl.when(place.middle)
        def _():
            self.far_copy(i).wait_send()

        @pl.when(jnp.logical_not(place.middle))
        def _():
            self.z_copy(i, 2).wait_recv()
            self.far_copy(i).wait_recv()

        for n in range(self.group):
            pieces = [self.zr[i, k, n].astype(full) for k in range(self.z_count)]
            if self.zr.dtype == low:
                pieces = [unfold(piece) for piece in pieces]
            whole = jnp.concatenate(pieces, axis=0).astype(self.whole.dtype)
            self.whole[self.base + self.group * i + n, place.spot, place.core] = whole
        self.first_copy(i).start()
        self.second_copy(i, 0).start()

    def after_first(self, i):
        self.first_copy(i).wait()
        self.second_copy(i, 1).start()

    def after_second(self, i):
        self.second_copy(i, 0).wait()
        self.second_copy(i, 1).wait()
        self.core_copy(i).start()

    def close(self, i):
        self.core_copy(i).wait()

    def tick(self, t, done=None):
        def close(i):
            self.close(i)
            if done is not None:
                done(i)

        @pl.when(t == 0)
        def _():
            for i in range(min(-FORWARD, self.count)):
                self.forward(i)

        stages = (
            (SECOND, self.after_second), (FIRST, self.after_first), (0, self.open), (FORWARD, self.forward),
            (ANNOUNCE, self.announce), (CLOSE, close),
        )
        for late, stage in stages:
            @pl.when((t >= max(late, 0)) & (t - late < self.count))
            def _():
                stage(t - late)


def split_refs(refs, *counts):
    result, start = [], 0
    for count in counts:
        result.append(refs[start : start + count])
        start += count
    return result


class Side:
    def __init__(self, plan, sources, targets, sum_refs, line_refs, own=None):
        self.plan = plan
        sums = plan.sums
        blocks = [source.at[pl.ds(plan.skip, source.shape[0] - plan.skip)] for source in sources[:sums]]
        blocks += [own] if plan.own else []
        self.place = Place(plan.z_count) if plan.active else None
        self.sum = BlockSum(self.place, blocks, sum_refs, plan.times) if plan.total else None
        self.result = targets[0] if plan.total else None
        self.lines = line_gathers(self.place, plan.lines, sources[sums:], targets[bool(plan.total) :], line_refs, plan.z_count)

    def enter(self, now):
        if not self.plan.active:
            return

        @pl.when(now)
        def _():
            greet((self.place.chip_partners() if self.plan.total else []) + self.place.z_partners())
            for line in self.lines:
                line.advance(1)

    def tick(self, t):
        if self.plan.total:
            self.sum.tick(t)

    def leave(self, now, ticks):
        if not self.plan.active:
            return

        @pl.when(now)
        def _():
            if self.plan.total:
                if self.sum.last >= ticks:
                    lax.fori_loop(ticks, self.sum.last + 1, lambda t, carry: (self.tick(t), carry)[1], 0)
                for i in range(self.sum.count):
                    self.result[i] = self.sum.finish(i).astype(low)
            for line in self.lines:
                line.advance(self.plan.z_count)

    def advance(self, now, hop):
        if self.lines and hop < self.plan.z_count:
            @pl.when(now)
            def _():
                for line in self.lines:
                    line.advance(hop)


class Plan:
    def __init__(self, pending=None, lines=(), z_count=1, own=0, size=None, ready=(), skip=0):
        self.z_count = z_count
        self.sums = int(pending is not None)
        self.own, self.skip = own, skip
        self.total = own + (pending.shape[0] - skip if self.sums else 0)
        self.times = sum_times(ready) if self.total else None
        self.lines = [(first, count) for _, first, count in lines]
        self.active = bool(self.total or lines)
        self.arguments, self.results, self.result_specs, self.scratch = [], [], [], []
        if self.sums:
            self.arguments.append(pending)
        if self.total:
            part, width = size
            self.results.append(jax.ShapeDtypeStruct((self.total, 2 * part // z_count, width // 2), low))
            self.result_specs.append(
                pl.BlockSpec(self.results[0].shape, lambda i: (0, 0, 0), pipeline_mode=pl.Buffered(1))
            )
            self.scratch += sum_scratch(self.total, part, width, z_count)
        for basis, _, count in lines:
            self.arguments.append(basis)
            self.results.append(jax.ShapeDtypeStruct((z_count, count) + basis.shape[1:], low))
            self.result_specs.append(ANYWHERE)
        self.scratch += line_scratch(len(lines), z_count)
        self.argument_specs = [ANYWHERE] * len(self.arguments)

    def split(self, refs, inputs, outputs, scratch):
        count = len(self.lines)
        return split_refs(
            refs, inputs, self.sums + count, outputs, bool(self.total) + count, scratch,
            SUM_REFS * bool(self.total), 2 * bool(self.lines),
        )


def line_scratch(count, z_count):
    if not count:
        return []
    return [pltpu.SemaphoreType.DMA((count,)), pltpu.SemaphoreType.DMA((count, 2, 2, z_count - 1))]


def line_gathers(place, spans, sources, targets, refs, z_count):
    return [
        LineGather(place, source, target, first, refs[0].at[n], refs[1].at[n], z_count)
        for n, (source, target, (first, _)) in enumerate(zip(sources, targets, spans))
    ]


ANYWHERE = pl.BlockSpec(memory_space=pl.ANY)
IN_VMEM = pl.BlockSpec(memory_space=pltpu.VMEM)


def forward_kernel(plan, *refs):
    inputs, sources, outputs, targets, scratch, gather_refs, vec_refs, line_refs = plan.split(refs)
    x_ref, segc_ref, vec_ref, w_hbm = inputs
    (q_ref, k_ref, v_ref, ctxt_ref, lse_ref, x1_ref, inv1_ref, n1_ref, u_ref, gp_ref, x2_ref, inv2_ref,
     out_ref) = outputs
    w, codes, vt, n1_all, acc, w_sem = scratch
    s = pl.program_id(0)
    tokens, width = acc.shape
    rows_now = x_ref.shape[0]
    rows = tokens // rows_now
    inner = plan.inner
    local = plan.local
    gather = vec_gather = None
    place = Place(plan.z_count) if plan.gathered else None
    if plan.gathered:
        w_out, out_sem = targets[0], scratch_tail(plan, refs)
        gather = BlockGather(place, plan.folded(refs), w, local, gather_refs)
        if plan.vectors:
            vec_gather = BlockGather(place, sources[1], plan.vec_whole(refs), 0, vec_refs)
            vec_ref = targets[1]
    line_sources = sources[plan.line_at :]
    if plan.casts:
        wide_bases, low_bases = sources[-2:], targets[-2:]
        cast_in, cast_out, cast_sem = plan.cast_scratch(refs)
        line_sources = [low_bases[1]] * len(plan.lines)
    lines = line_gathers(place, plan.lines, line_sources, targets[plan.line_target_at :], line_refs, plan.z_count)

    def cast_slot(n):
        loads = [pltpu.make_async_copy(wide_bases[k].at[n], cast_in.at[k], cast_sem.at[0, k]) for k in range(2)]
        stores = [pltpu.make_async_copy(cast_out.at[k], low_bases[k].at[n], cast_sem.at[1, k]) for k in range(2)]
        for copy in loads:
            copy.start()
        for k in range(2):
            loads[k].wait()
            cast_out[k] = cast_in[k].astype(low)
            stores[k].start()
        for copy in stores:
            copy.wait()

    def keep(i):
        group = gather.group
        return pltpu.make_async_copy(w.at[gather.blocks(i)], w_out.at[pl.ds(group * i, group)], out_sem.at[i])

    def load(j):
        return pltpu.make_async_copy(w_hbm.at[plan.order[j]], w.at[j], w_sem.at[j])

    def matrix(j):
        return w[j].reshape(width, width)

    def arrive(j):
        if j < local:
            load(j).wait()

    def tick(t):
        if gather is not None:
            gather.tick(t, lambda i: keep(i).start())
            if vec_gather is not None:
                vec_gather.tick(t)

    pairs = width // PAIR

    @pl.when(s == 0)
    def _():
        for j in range(local):
            load(j).start()
        if gather is not None:
            for n, number in enumerate(plan.numbers):
                gather.source[n // plan.group, n % plan.group] = fold(sources[0][number]).astype(low)
            greet(place.chip_partners() + place.z_partners())
            if vec_gather is not None:
                vec_gather.begin()
            gather.begin()
        for j in range(min(local, 3)):
            arrive(j)

    def run_ticks(start, stop, casting=False):
        def body(t, carry):
            tick(t)
            if casting:
                @pl.when((s == 0) & (t < plan.casts))
                def _():
                    cast_slot(t)
            return carry

        if gather is not None:
            lax.fori_loop(start, stop, body, 0)

    def ready():
        for line in lines:
            line.advance(1)
        if vec_gather is not None:
            turned = vec_gather.whole[0].reshape(width, vec_gather.whole.shape[-1]).T
            for layer in range(2):
                count = plan.vector_rows
                targets[1 + layer][0:count, :] = turned[layer * count : (layer + 1) * count, :]

    def project():
        xin = x_ref[...].astype(low)
        keys, queries = segment_codes(segc_ref[0], half_masks(low))
        for h in range(2):
            codes[0, h] = keys[h]
            codes[1, h] = queries[h]
        q_ref[...] = (dot_nn(xin, matrix(0)) + vec_ref[0:1, :]).astype(low)
        k_ref[...] = dot_nn(xin, matrix(1)).astype(low)
        value = dot_nn(xin, matrix(2)) + vec_ref[1:2, :]
        v_ref[...] = value.astype(low)
        turned = value.T.astype(low)
        for h in range(width // HD):
            vt[h, 0:HD] = turned[h * HD : (h + 1) * HD]
            vt[h, HD : HD + 16] = jnp.ones((16, turned.shape[1]), low)

    def pair_step(p):
        masks = half_masks(low)
        lanes = pl.ds(pl.multiple_of(p * PAIR, PAIR), PAIR)
        q_pair = q_ref[:, lanes] * jnp.asarray(HD ** (-0.5), low)
        k_pair = k_ref[:, lanes]
        for h in range(2):
            scores = dot_nt(k_pair * masks[h] + codes[0, h], q_pair * masks[h] + codes[1, h])
            largest = jnp.max(scores, axis=0, keepdims=True)
            expanded = jnp.exp(scores - largest)
            here = pl.ds(pl.multiple_of(p * PAIR + h * HD, HD), HD)
            product = dot_nn(vt[2 * p + h], expanded.astype(low))
            total = product[HD : HD + 1]
            ctxt_ref[here, :] = (product[0:HD] * (1.0 / total)).astype(low)
            lse_ref[0, pl.ds(2 * p + h, 1), :] = largest + jnp.log(total)

    def close_row():
        @pl.when(s == 0)
        def _():
            if local > 3:
                arrive(3)
            for line in lines:
                line.advance(2)

        context = ctxt_ref[...].astype(full).T.astype(low)
        attended = dot_nn(context, matrix(3)) + vec_ref[2:3, :]
        unit, inverse = norm_parts(x_ref[...].astype(full) + attended)
        x1_ref[...] = unit
        inv1_ref[...] = inverse
        normed = unit * vec_ref[3:4, :] + vec_ref[4:5, :]
        here = pl.ds(pl.multiple_of(s * rows_now, rows_now), rows_now)
        acc[here, :] = normed + vec_ref[5 + inner : 6 + inner, :]
        normed = normed.astype(low)
        n1_ref[...] = normed
        n1_all[here, :] = normed

    @pl.when(s < rows)
    def _():
        def position(n, carry):
            if gather is not None:
                here, which = looked_up(plan.row_positions, n)
                before = plan.lead + s * len(plan.row_positions) + which
                opening = (s == 0) & (n == 0)
                start = jnp.where(opening, 0, before)
                stop = jnp.where(opening, plan.lead, jnp.where(here, before + 1, before))
                run_ticks(start, stop, plan.casts > 0)

                @pl.when(opening)
                def _():
                    ready()

            @pl.when(n == 0)
            def _():
                project()

            @pl.when((n >= 1) & (n <= pairs))
            def _():
                pair_step(n - 1)

            @pl.when(n == pairs + 1)
            def _():
                close_row()

            return carry

        lax.fori_loop(0, pairs + 2, position, 0)

    tile = tokens // 4
    starts, stops = plan.step_ticks(rows)

    @pl.when(s >= rows)
    def _():
        c = s - rows

        @pl.when(c == 0)
        def _():
            for j in range(4, local):
                arrive(j)
            for line in lines:
                line.advance(3)

        def token_step(i, carry):
            for half in range(2):
                here = pl.ds(pl.multiple_of((2 * i + half) * tile, tile), tile)
                value, slope = gelu_parts(dot_nn(n1_all[here, :], matrix(4 + 2 * c)) + vec_ref[pl.ds(5 + c, 1), :])
                active = value.astype(low)
                u_ref[here, :] = active
                gp_ref[here, :] = slope.astype(low)
                acc[here, :] += dot_nn(active, matrix(5 + 2 * c))
            return carry

        lax.fori_loop(0, 2, token_step, 0)

        @pl.when(c == inner - 1)
        def _():
            base = 5 + inner

            def last(i, carry):
                here = pl.ds(pl.multiple_of(i * tile, tile), tile)
                unit, inverse = norm_parts(acc[here, :])
                x2_ref[here, :] = unit
                inv2_ref[here, :] = inverse
                out_ref[here, :] = (
                    unit * vec_ref[base + 1 : base + 2, :] + vec_ref[base + 2 : base + 3, :]
                ).astype(out_ref.dtype)
                return carry

            lax.fori_loop(0, 4, last, 0)

        run_ticks(
            sum(n * (c == k).astype(jnp.int32) for k, n in enumerate(starts)),
            sum(n * (c == k).astype(jnp.int32) for k, n in enumerate(stops)),
        )

        @pl.when(c == inner - 1)
        def _():
            if gather is not None:
                for line in lines:
                    line.advance(plan.z_count)
                for i in range(gather.count):
                    keep(i).wait()


class ForwardPlan:
    def __init__(
        self, inner, local, blocks=None, numbers=(), vec_shard=None, vector_rows=0, lines=(), lead=0, row_positions=(), z_count=1,
        wide_bases=(),
    ):
        self.inner, self.local, self.lead, self.row_positions, self.z_count = inner, local, lead, row_positions, z_count
        self.vector_rows = vector_rows
        self.order = [0, 1, 2, 3]
        for c in range(inner):
            self.order += [4 + c, 4 + inner + c]
        self.numbers = list(numbers)
        self.gathered, self.group = len(self.numbers), 2
        self.vectors = vec_shard is not None
        self.lines = [(first, count) for _, first, count in lines]
        self.line_at = int(self.gathered > 0) + int(self.vectors)
        self.line_target_at = int(self.gathered > 0) + 2 * int(self.vectors)
        self.arguments, self.argument_specs, self.results, self.result_specs, self.scratch = [], [], [], [], []
        shape = jax.ShapeDtypeStruct
        if self.gathered:
            rows, width = blocks.shape[1:]
            groups = self.gathered // self.group
            self.arguments.append(blocks)
            self.argument_specs.append(IN_VMEM)
            self.results.append(shape((self.gathered, 4, 2, width // 8, width), low))
            self.result_specs.append(ANYWHERE)
            self.scratch += gather_scratch(groups, self.group, width // 8, width, z_count)
        if self.vectors:
            lanes = vec_shard.shape[3]
            self.arguments.append(vec_shard)
            self.argument_specs.append(IN_VMEM)
            for _ in range(2):
                self.results.append(shape((16, width), full))
                self.result_specs.append(pl.BlockSpec((16, width), lambda s: (0, 0)))
            self.scratch += gather_scratch(1, 1, width // 8, lanes, z_count, full)
        self.casts = wide_bases[0].shape[0] if wide_bases else 0
        for basis, _, count in lines:
            if not self.casts:
                self.arguments.append(basis)
                self.argument_specs.append(ANYWHERE)
            self.results.append(shape((z_count, count) + basis.shape[1:], low))
            self.result_specs.append(ANYWHERE)
        for basis in wide_bases:
            self.arguments.append(basis)
            self.argument_specs.append(ANYWHERE)
            self.results.append(shape(basis.shape, low))
            self.result_specs.append(ANYWHERE)
        self.scratch += line_scratch(len(lines), z_count)
        if self.casts:
            self.scratch += [
                pltpu.VMEM((2,) + wide_bases[0].shape[1:], full),
                pltpu.VMEM((2,) + wide_bases[0].shape[1:], low),
                pltpu.SemaphoreType.DMA((2, 2)),
            ]
        if self.gathered:
            self.scratch.append(pltpu.SemaphoreType.DMA((self.gathered // self.group,)))
        if self.vectors:
            self.scratch.append(pltpu.VMEM((1, 4, 2, width // 8, lanes), full))
        if self.gathered:
            self.scratch.append(pltpu.VMEM((groups, self.group, 2 * rows, width // 2), low))

    def step_ticks(self, rows):
        now, starts, stops = self.lead + rows * len(self.row_positions), [], []
        for c in range(self.inner):
            starts.append(now)
            if not self.gathered:
                stops.append(now)
                continue
            if c == self.inner - 1:
                now = max(now, self.gathered // self.group + CLOSE)
            else:
                now = max(now + 1, (5 + 2 * (c + 1) - self.local) // self.group + CLOSE + 1)
            stops.append(now)
        return starts, stops

    def split(self, refs):
        return split_refs(
            refs, 4, len(self.arguments), 13, len(self.results), 6, GATHER_REFS * bool(self.gathered),
            GATHER_REFS * self.vectors, 2 * bool(self.lines),
        )

    def vec_whole(self, refs):
        return refs[-2]

    def folded(self, refs):
        return refs[-1]

    def cast_scratch(self, refs):
        return refs[-6:-3]


def scratch_tail(plan, refs):
    return refs[-3] if plan.vectors else refs[-2]


def forward_layer(hidden, seg_column, vectors, weights, out_dtype, plan, identity=None):
    tokens, width = hidden.shape
    inner = plan.inner
    wide = width * inner
    rows = tokens // L
    heads = width // HD
    shape = jax.ShapeDtypeStruct

    def here(s):
        return jnp.minimum(s, rows - 1)

    def column(s):
        return jnp.maximum(s - rows, 0)

    def row_block(columns):
        return pl.BlockSpec((L, columns), lambda s: (here(s), 0))

    def whole(columns):
        return pl.BlockSpec((tokens, columns), lambda s: (0, 0), pipeline_mode=pl.Buffered(1))

    wide_block = pl.BlockSpec((tokens, width), lambda s: (0, column(s)))
    out_shape = (
        shape((tokens, width), low), shape((tokens, width), low), shape((tokens, width), low),
        shape((width, tokens), low), shape((rows, heads, L), full),
        shape((tokens, width), full), shape((tokens, 1), full), shape((tokens, width), low),
        shape((tokens, wide), low), shape((tokens, wide), low),
        shape((tokens, width), full), shape((tokens, 1), full), shape((tokens, width), out_dtype),
        *plan.results,
    )
    out_specs = (
        row_block(width), row_block(width), row_block(width),
        pl.BlockSpec((width, L), lambda s: (0, here(s))), pl.BlockSpec((1, heads, L), lambda s: (here(s), 0, 0)),
        row_block(width), row_block(1), row_block(width),
        wide_block, wide_block,
        whole(width), whole(1), whole(width),
        *plan.result_specs,
    )
    if plan.local:
        weights = weights.reshape(-1, 4, 2, width // 8, width)
    total = 4 + 2 * inner
    held = max(total, plan.local + plan.gathered)
    return pl.pallas_call(
        functools.partial(forward_kernel, plan),
        grid=(rows + inner,),
        out_shape=out_shape,
        in_specs=[
            row_block(width),
            pl.BlockSpec((1, L, 1), lambda s: (here(s), 0, 0)),
            pl.BlockSpec(vectors.shape, lambda s: (0, 0)),
            ANYWHERE,
            *plan.argument_specs,
        ],
        out_specs=out_specs,
        scratch_shapes=[
            pltpu.VMEM((held, 4, 2, width // 8, width), low),
            pltpu.VMEM((2, 2, L, PAIR), low),
            pltpu.VMEM((heads, HD + 16, L), low),
            pltpu.VMEM((tokens, width), low),
            pltpu.VMEM((tokens, width), full),
            pltpu.SemaphoreType.DMA((total,)),
            *plan.scratch,
        ],
        compiler_params=pltpu.CompilerParams(
            dimension_semantics=("arbitrary",), vmem_limit_bytes=62 * MIB,
            collective_id=identity, has_side_effects=identity is not None,
        ),
        cost_estimate=pl.CostEstimate(
            flops=2 * tokens * width * width * total + 4 * tokens * L * width,
            bytes_accessed=40 * MIB,
            transcendentals=tokens * (L * heads + wide),
        ),
        name="layer_forward",
    )(hidden, seg_column, vectors, weights, *plan.arguments)


WIDE_STEP_TICKS = 5


def wide_ready(own):
    return [WIDE_STEP_TICKS * (n // 2) + 4 + n % 2 for n in range(own)]


def wide_back_kernel(plan, inner, *refs):
    inputs, sources, outputs, targets, scratch, sum_refs, line_refs = plan.split(refs, 11, 4, 11)
    up_hbm, x2_hbm, inv2_hbm, x1_hbm, inv1_hbm, n1_hbm, vec_ref, wup_ref, wdown_ref, u_ref, gp_ref = inputs
    dw_ref, dr1_ref, da_ref, dvec_ref = outputs
    n1t, dz, kept_dw, up_ref, x2_ref, inv2_ref, x1_ref, inv1_ref, n1_ref, tile_sem, load_sem = scratch
    dy, dn1 = da_ref, dr1_ref
    c = pl.program_id(0)
    steps = pl.num_programs(0)
    tokens, width = dn1.shape
    tile = tokens // 4
    base = 5 + inner
    side = Side(plan, sources, targets, sum_refs, line_refs, kept_dw)

    def tile_copies(i):
        rows = pl.ds(pl.multiple_of(i * tile, tile), tile)
        return [
            pltpu.make_async_copy(source.at[rows], target.at[rows], tile_sem.at[n, i])
            for n, (source, target) in enumerate(((up_hbm, up_ref), (x2_hbm, x2_ref), (inv2_hbm, inv2_ref)))
        ]

    late_copies = [
        pltpu.make_async_copy(source, target, load_sem.at[n])
        for n, (source, target) in enumerate(((n1_hbm, n1_ref), (x1_hbm, x1_ref), (inv1_hbm, inv1_ref)))
    ]

    @pl.when(c == 0)
    def _():
        for i in range(4):
            for copy in tile_copies(i):
                copy.start()
        for copy in late_copies:
            copy.start()

    side.enter(c == 0)

    def prepare():
        gain = vec_ref[base + 1 : base + 2, :]

        def body(i, carry):
            for copy in tile_copies(i):
                copy.wait()
            gain_sum, shift_sum, bias_sum = carry
            rows = pl.ds(pl.multiple_of(i * tile, tile), tile)
            upstream = up_ref[rows, :].astype(full)
            unit = x2_ref[rows, :]
            back = norm_back(upstream, unit, inv2_ref[rows, :], gain)
            dn1[rows, :] = back
            branch = back.astype(low)
            dy[rows, :] = branch
            return (
                gain_sum + column_sum(upstream * unit),
                shift_sum + column_sum(upstream),
                bias_sum + column_sum(branch.astype(full)),
            )

        zero = jnp.zeros((1, width), full)
        gain_sum, shift_sum, bias_sum = lax.fori_loop(0, 4, body, (zero, zero, zero))
        dvec_ref[...] = jnp.zeros(dvec_ref.shape, full)
        dvec_ref[base : base + 1, :] = bias_sum
        dvec_ref[base + 1 : base + 2, :] = gain_sum
        dvec_ref[base + 2 : base + 3, :] = shift_sum
        late_copies[0].wait()
        n1t[...] = n1_ref[...].astype(full).T.astype(low)

    def token_pair(i):
        bias_sum = jnp.zeros((1, width), full)
        for half in range(2):
            rows = pl.ds(pl.multiple_of((2 * i + half) * tile, tile), tile)
            slope = gp_ref[rows, :].astype(full)
            piece = (dot_nt(dy[rows, :], wdown_ref[0]) * slope).astype(low)
            dz[rows, :] = piece
            dn1[rows, :] += dot_nt(piece, wup_ref[0])
            bias_sum = bias_sum + column_sum(piece.astype(full))
        dvec_ref[pl.ds(5 + c, 1), :] += bias_sum

    def store(k, product):
        if plan.own:
            @pl.when(2 * c + k < plan.own)
            def _():
                kept_dw[2 * c + k] = product().reshape(kept_dw.shape[1:])

            @pl.when(2 * c + k >= plan.own)
            def _():
                dw_ref[k, 0] = product()
        else:
            dw_ref[k, 0] = product()

    def position(n, carry):
        side.tick(WIDE_STEP_TICKS * c + n)
        side.advance((c == 1) & (n == 1), 2)
        side.advance((c == 2) & (n == 4), 3)

        @pl.when((n == 0) & (c == 0))
        def _():
            prepare()

        @pl.when((n == 1) | (n == 2))
        def _():
            token_pair(n - 1)

        @pl.when(n == 3)
        def _():
            store(0, lambda: dot_nn(n1t[...], dz[...]).astype(low))

        @pl.when(n == 4)
        def _():
            store(1, lambda: dot_tn(u_ref[...], dy[...]).astype(low))

        return carry

    lax.fori_loop(0, WIDE_STEP_TICKS, position, 0)
    @pl.when(c == steps - 1)
    def _():
        for copy in late_copies[1:]:
            copy.wait()
        gain = vec_ref[3:4, :]

        def body(i, carry):
            gain_sum, shift_sum, bias_sum = carry
            rows = pl.ds(pl.multiple_of(i * tile, tile), tile)
            upstream = dn1[rows, :]
            unit = x1_ref[rows, :]
            back = norm_back(upstream, unit, inv1_ref[rows, :], gain)
            dr1_ref[rows, :] = back
            branch = back.astype(low)
            da_ref[rows, :] = branch
            return (
                gain_sum + column_sum(upstream * unit),
                shift_sum + column_sum(upstream),
                bias_sum + column_sum(branch.astype(full)),
            )

        zero = jnp.zeros((1, width), full)
        gain_sum, shift_sum, bias_sum = lax.fori_loop(0, 4, body, (zero, zero, zero))
        dvec_ref[2:3, :] = bias_sum
        dvec_ref[3:4, :] = gain_sum
        dvec_ref[4:5, :] = shift_sum

    side.leave(c == steps - 1, WIDE_STEP_TICKS * inner)


def wide_back(upstream, kept, vectors, weights, places, plan, identity=None):
    x1, inv1, n1, u, gp, x2, inv2 = kept
    tokens, width = x1.shape
    up_start, down_start, stride = places
    inner = u.shape[1] // width
    shape = jax.ShapeDtypeStruct

    return pl.pallas_call(
        functools.partial(wide_back_kernel, plan, inner),
        grid=(inner,),
        out_shape=(
            shape((2, inner - plan.own // 2, width, width), low),
            shape((tokens, width), full), shape((tokens, width), low), shape((16, width), full),
            *plan.results,
        ),
        in_specs=[
            *[ANYWHERE] * 6,
            pl.BlockSpec(vectors.shape, lambda c: (0, 0), pipeline_mode=pl.Buffered(1)),
            pl.BlockSpec((1, width, width), lambda c: (up_start + stride * c, 0, 0)),
            pl.BlockSpec((1, width, width), lambda c: (down_start + stride * c, 0, 0)),
            pl.BlockSpec((tokens, width), lambda c: (0, c)),
            pl.BlockSpec((tokens, width), lambda c: (0, c)),
            *plan.argument_specs,
        ],
        out_specs=(
            pl.BlockSpec((2, 1, width, width), lambda c: (0, jnp.maximum(c - plan.own // 2, 0), 0, 0)),
            pl.BlockSpec((tokens, width), lambda c: (0, 0), pipeline_mode=pl.Buffered(1)),
            pl.BlockSpec((tokens, width), lambda c: (0, 0), pipeline_mode=pl.Buffered(1)),
            pl.BlockSpec((16, width), lambda c: (0, 0)),
            *plan.result_specs,
        ),
        scratch_shapes=[
            pltpu.VMEM((width, tokens), low),
            pltpu.VMEM((tokens, width), low),
            pltpu.VMEM((plan.own, 4, 2, width // 8, width) if plan.own else (8, 128), low),
            pltpu.VMEM((tokens, width), upstream.dtype),
            pltpu.VMEM((tokens, width), full),
            pltpu.VMEM((tokens, 1), full),
            pltpu.VMEM((tokens, width), full),
            pltpu.VMEM((tokens, 1), full),
            pltpu.VMEM((tokens, width), low),
            pltpu.SemaphoreType.DMA((3, 4)),
            pltpu.SemaphoreType.DMA((3,)),
            *plan.scratch,
        ],
        compiler_params=pltpu.CompilerParams(
            dimension_semantics=("arbitrary",), vmem_limit_bytes=60 * MIB,
            collective_id=identity, has_side_effects=identity is not None,
        ),
        cost_estimate=pl.CostEstimate(
            flops=8 * tokens * width * width * inner, bytes_accessed=50 * MIB, transcendentals=0
        ),
        name="wide_backward",
    )(upstream, x2, inv2, x1, inv1, n1, vectors, weights, weights, u, gp, *plan.arguments)


def attend_back_kernel(plan, *refs):
    inputs, sources, outputs, targets, scratch, sum_refs, line_refs = plan.split(refs, 10, 3, 12)
    da_hbm, dr1_ref, x_ref, q_ref, k_ref, v_ref, ctxt_hbm, lse_ref, segc_ref, w_hbm = inputs
    dw_ref, dx_ref, dvec_ref = outputs
    codes, dctx, kt, delta, dqt, xt, grads, dwo, da_ref, ctxt_ref, w_ref, load_sem = scratch
    r = pl.program_id(0)
    loads = [
        pltpu.make_async_copy(w_hbm.at[plan.start + 3], w_ref.at[3], load_sem.at[0]),
        pltpu.make_async_copy(da_hbm, da_ref, load_sem.at[1]),
        pltpu.make_async_copy(ctxt_hbm, ctxt_ref, load_sem.at[2]),
        pltpu.make_async_copy(w_hbm.at[pl.ds(plan.start, 3)], w_ref.at[pl.ds(0, 3)], load_sem.at[3]),
    ]

    @pl.when(r == 0)
    def _():
        for copy in loads:
            copy.start()

    side = Side(plan, sources, targets, sum_refs, line_refs, dwo)
    side.enter(r == 0)
    tokens, width = dr1_ref.shape
    pairs = width // PAIR
    ticks = pairs + 5
    here = pl.ds(pl.multiple_of(r * tokens, tokens), tokens)
    masks = half_masks(low)
    scale = HD ** (-0.5)
    last_row = pl.num_programs(0) - 1

    def prepare():
        @pl.when(r == 0)
        def _():
            for copy in loads[:3]:
                copy.wait()
            grad = dot_nn(ctxt_ref[...], da_ref[...]).astype(low)
            if plan.own:
                dwo[0] = grad.reshape(dwo.shape[1:])
            else:
                dw_ref[3] = grad
            dvec_ref[...] = jnp.zeros(dvec_ref.shape, full)

        xt[:, here] = x_ref[...].astype(low).astype(full).T.astype(low)
        keys, queries = segment_codes(segc_ref[0], masks)
        for h in range(2):
            codes[0, h] = keys[h]
            codes[1, h] = queries[h]
        context_grad = dot_nt(da_ref[here, :], w_ref[3]).astype(low)
        dctx[...] = context_grad
        kt[...] = k_ref[...].astype(full).T.astype(low)
        products = context_grad.astype(full) * ctxt_ref[:, here].astype(full).T
        feature = lax.broadcasted_iota(jnp.int32, (16, width), 1)
        head = lax.broadcasted_iota(jnp.int32, (16, width), 0)
        member = ((feature >= head * HD) & (feature < (head + 1) * HD)).astype(full).astype(low)
        high = products.astype(low)
        rest = (products - high.astype(full)).astype(low)
        delta[...] = dot_nt(member, high) + dot_nt(member, rest)

    def pair_step(p):
        lanes = pl.ds(pl.multiple_of(p * PAIR, PAIR), PAIR)
        q_pair = q_ref[:, lanes] * jnp.asarray(scale, low)
        k_pair = k_ref[:, lanes]
        v_pair = v_ref[:, lanes]
        g_pair = dctx[:, lanes]
        key_grad = jnp.zeros((tokens, PAIR), full)
        value_grad = jnp.zeros((tokens, PAIR), full)
        for h in range(2):
            q_half = q_pair * masks[h]
            g_half = g_pair * masks[h]
            scores = dot_nt(k_pair * masks[h] + codes[0, h], q_half + codes[1, h])
            attention = jnp.exp(scores - lse_ref[0, pl.ds(2 * p + h, 1), :]).astype(low)
            value_grad = value_grad + dot_nn(attention, g_half)
            attention_grad = dot_nt(v_pair, g_half)
            score_grad = attention * (attention_grad - delta[pl.ds(2 * p + h, 1), :]).astype(low)
            key_grad = key_grad + dot_nn(score_grad, q_half)
            rows = pl.ds(pl.multiple_of(p * PAIR + h * HD, HD), HD)
            dqt[rows, :] = dot_nn(kt[rows, :], score_grad) * scale
        grads[1, here, lanes] = key_grad.astype(low)
        grads[2, here, lanes] = value_grad.astype(low)

    def inputs_step():
        @pl.when(r == 0)
        def _():
            loads[3].wait()

        query_grad = dqt[...].T.astype(low)
        grads[0, here, :] = query_grad
        value_grad = grads[2, here, :]
        dx_ref[...] = (
            dr1_ref[...]
            + dot_nt(query_grad, w_ref[0])
            + dot_nt(grads[1, here, :], w_ref[1])
            + dot_nt(value_grad, w_ref[2])
        )
        dvec_ref[0:1, :] += column_sum(query_grad.astype(full))
        dvec_ref[1:2, :] += column_sum(value_grad.astype(full))

    def position(n, carry):
        side.tick(r * ticks + n)
        side.advance((r == 0) & (n == 6), 2)
        side.advance((r == 1) & (n == 4), 3)

        @pl.when(n == 0)
        def _():
            prepare()

        @pl.when((n >= 1) & (n <= pairs))
        def _():
            pair_step(n - 1)

        @pl.when(n == pairs + 1)
        def _():
            inputs_step()

        @pl.when((n > pairs + 1) & (r == last_row))
        def _():
            j = n - (pairs + 2)
            dw_ref[j] = dot_nn(xt[...], grads[j]).astype(low)

        return carry

    lax.fori_loop(0, ticks, position, 0)
    side.leave(r == last_row, plan.rows * ticks)


def attend_back(da, dr1, hidden, kept, seg_column, weights, start, plan, identity=None):
    q, k, v, ctxt, lse = kept
    tokens, width = da.shape
    rows = tokens // L
    heads = width // HD
    shape = jax.ShapeDtypeStruct
    plan.start, plan.rows = start, rows

    def row_block():
        return pl.BlockSpec((L, width), lambda r: (r, 0))

    return pl.pallas_call(
        functools.partial(attend_back_kernel, plan),
        grid=(rows,),
        out_shape=(
            shape((4 - plan.own, width, width), low), shape((tokens, width), full), shape((8, width), full),
            *plan.results,
        ),
        in_specs=[
            ANYWHERE,
            row_block(), row_block(), row_block(), row_block(), row_block(),
            ANYWHERE,
            pl.BlockSpec((1, heads, L), lambda r: (r, 0, 0)),
            pl.BlockSpec((1, L, 1), lambda r: (r, 0, 0)),
            ANYWHERE,
            *plan.argument_specs,
        ],
        out_specs=(
            pl.BlockSpec((4 - plan.own, width, width), lambda r: (0, 0, 0), pipeline_mode=pl.Buffered(1)),
            row_block(),
            pl.BlockSpec((8, width), lambda r: (0, 0)),
            *plan.result_specs,
        ),
        scratch_shapes=[
            pltpu.VMEM((2, 2, L, PAIR), low),
            pltpu.VMEM((L, width), low),
            pltpu.VMEM((width, L), low),
            pltpu.VMEM((16, L), full),
            pltpu.VMEM((width, L), full),
            pltpu.VMEM((width, tokens), low),
            pltpu.VMEM((3, tokens, width), low),
            pltpu.VMEM((1, 4, 2, width // 8, width) if plan.own else (8, 128), low),
            pltpu.VMEM((tokens, width), low),
            pltpu.VMEM((width, tokens), low),
            pltpu.VMEM((4, width, width), low),
            pltpu.SemaphoreType.DMA((4,)),
            *plan.scratch,
        ],
        compiler_params=pltpu.CompilerParams(
            dimension_semantics=("arbitrary",), vmem_limit_bytes=60 * MIB,
            collective_id=identity, has_side_effects=identity is not None,
        ),
        cost_estimate=pl.CostEstimate(
            flops=16 * tokens * width * width + 10 * tokens * L * width,
            bytes_accessed=30 * MIB,
            transcendentals=tokens * L * heads,
        ),
        name="attend_backward",
    )(da, dr1, hidden, q, k, v, ctxt, lse, seg_column, weights, *plan.arguments)


def moments(rotated, first, second):
    first_new = beta_one * first + (1.0 - beta_one) * rotated
    second_new = beta_two * second + (1.0 - beta_two) * rotated * rotated
    direction = (
        first_new
        / (1.0 - beta_one**STEP)
        / (jnp.sqrt(second_new / (1.0 - beta_two**STEP)) + adam_epsilon)
    )
    return first_new, second_new, direction


def pack_lanes(piece):
    rows = piece.shape[0] // 2
    return jnp.concatenate([piece[:rows], piece[rows:]], axis=1)


def unpack_lanes(piece):
    columns = piece.shape[1] // 2
    return jnp.concatenate([piece[:, :columns], piece[:, columns:]], axis=0)


def optimizer_kernel(plan, *refs):
    spans = len(plan.spans)
    inputs, ready, dvecs, bases, lines_in, outputs, lines_out, scratch, sum_refs, vec_refs, line_refs = split_refs(
        refs, 6, plan.ready, plan.dvecs, plan.bases, spans, 5, spans, 21, SUM_REFS, SUM_REFS, 2 * bool(spans)
    )
    index_ref, place_ref, tail_hbm, first_hbm, second_hbm, blocks = inputs
    new_ref, low_ref, first_out, second_out, vec_out = outputs
    (store, left, right, first_in, second_in, g_out, g_in, t_out, t_in, e_out, e_in, w_out, w_in, vec_source,
     load_sem, g_sem, t_sem, e_sem, w_sem, left_sem, right_sem) = scratch
    slots, owners = g_in.shape[0], g_in.shape[1]
    z_count = t_in.shape[1]
    place = Place(z_count)
    dp, z = place.dp, place.z
    dps = [lax.rem(dp + d, owners) for d in range(owners)]
    count = blocks.shape[0]
    many = tail_hbm.shape[0]
    tail_times = [[many * stage + n for n in range(many)] for stage in range(5)]
    tail = BlockSum(place, [tail_hbm], sum_refs, tail_times)
    vec = BlockSum(place, [vec_source], vec_refs, [[many * stage + 1] for stage in range(5)])
    order = plan.free + [s for s in range(slots) if s not in plan.free]
    lines = line_gathers(place, plan.spans, lines_in, lines_out, line_refs, z_count)
    every = list(bases) + list(lines_out)
    late = [s for s in range(slots) if plan.left_map[s][0] >= len(bases)]

    def load(refs_map, target, sem, s):
        n, at = refs_map[s]
        return pltpu.make_async_copy(every[n].at[:, at], target.at[:, s], sem.at[s])

    def load_first(s):
        return pltpu.make_async_copy(first_hbm.at[s], first_in.at[s], load_sem.at[0, s])

    def load_second(s):
        return pltpu.make_async_copy(second_hbm.at[s], second_in.at[s], load_sem.at[1, s])

    for s in order:
        load(plan.right_map, right, right_sem, s).start()
        if s not in late:
            load(plan.left_map, left, left_sem, s).start()
        load_first(s).start()
        load_second(s).start()
    greet([(other, z) for other in dps[1:]] + place.z_partners())
    start = many
    for part in ready:
        store[start : start + part.shape[0]] = part[...]
        start += part.shape[0]
    store[0:many] = jnp.zeros((many,) + store.shape[1:], low)
    store[count] = jnp.zeros(store.shape[1:], low)
    rows = plan.vector_rows
    stacked = jnp.concatenate(
        [dvecs[0][0:2, :], dvecs[1][2:rows, :], dvecs[2][0:2, :], dvecs[3][2:rows, :],
         jnp.zeros((vec_source.shape[-1] - 2 * rows, blocks.shape[2]), full)], axis=0
    )
    vec_source[0] = stacked.T.reshape(vec_source.shape[1:])

    def g_copy(s, d):
        other = dps[d]
        return remote(g_out.at[s, d], g_in.at[s, dp], g_sem.at[0, s, d], g_sem.at[1, s, owners - d], (other, z))

    def t_copy(s, d):
        other = place.zs[d]
        return remote(t_out.at[s, d], t_in.at[s, z], t_sem.at[0, s, d], t_sem.at[1, s, z_count - d], (dp, other))

    def e_copy(s, d):
        other = place.zs[d]
        return remote(e_out.at[s, d], e_in.at[s, z], e_sem.at[0, s, d], e_sem.at[1, s, z_count - d], (dp, other))

    def w_copy(s, d):
        other = dps[d]
        return remote(
            w_out.at[s, other], w_in.at[s * owners + dp], w_sem.at[0, s, d], w_sem.at[1, s, owners - d], (other, z)
        )

    def send_out(s):
        for d in range(1, owners):
            g_out[s, d] = store[index_ref[s * owners + dps[d]]]
            g_copy(s, d).start()
        g_in[s, dp] = store[index_ref[s * owners + dp]]

    def turn(s):
        for d in range(1, owners):
            g_copy(s, d).wait()
        load(plan.right_map, right, right_sem, s).wait()
        grad = jnp.concatenate([unfold(g_in[s, c].astype(full)) for c in range(owners)], axis=0).astype(low)
        for d in range(1, z_count):
            t_out[s, d] = pack_lanes(dot_nt(right[place.zs[d], s], grad)).astype(low)
            t_copy(s, d).start()
        t_in[s, z] = pack_lanes(dot_nt(right[z, s], grad)).astype(low)

    def adapt(s):
        for d in range(1, z_count):
            t_copy(s, d).wait()
        load_first(s).wait()
        load_second(s).wait()
        load(plan.left_map, left, left_sem, s).wait()
        rotated = jnp.zeros(first_in.shape[1:], full)
        for f in range(z_count):
            rotated = rotated + dot_nn(unpack_lanes(t_in[s, f].astype(full)).astype(low), left[f, s])
        first_new, second_new, direction = moments(rotated, first_in[s], second_in[s])
        first_out[s] = first_new
        second_out[s] = second_new
        direction = direction.astype(low)
        for d in range(1, z_count):
            e_out[s, d] = pack_lanes(dot_nt(left[place.zs[d], s], direction)).astype(low)
            e_copy(s, d).start()
        e_in[s, z] = pack_lanes(dot_nt(left[z, s], direction)).astype(low)

    def step_back(s):
        for d in range(1, z_count):
            e_copy(s, d).wait()
        step = jnp.zeros((left.shape[2], left.shape[3]), full)
        for f in range(z_count):
            step = step + dot_nn(unpack_lanes(e_in[s, f].astype(full)).astype(low), right[f, s])
        share = step.shape[0] // owners
        for c in range(owners):
            w_out[s, c] = fold(step[c * share : (c + 1) * share]).astype(low)
        for d in range(1, owners):
            w_copy(s, d).start()
        w_in[s * owners + dp] = w_out[s, dp]

    def sums(stage):
        for t in range(many * stage, many * (stage + 1)):
            tail.tick(t)
            vec.tick(t)

    free = plan.free
    def advance(hop):
        for line in lines:
            line.advance(hop)

    sums(0)
    advance(1)
    for s in free:
        send_out(s)
    sums(1)
    for s in free:
        turn(s)
    sums(2)
    advance(2)
    for s in free:
        adapt(s)
    sums(3)
    sums(4)
    advance(3)
    for i in range(many):
        store[i] = tail.finish(i).astype(low)
    rest = order[len(free) :]
    for s in rest[:2]:
        send_out(s)
    for s in free:
        step_back(s)
    advance(z_count)
    for s in late:
        load(plan.left_map, left, left_sem, s).start()
    for k in range(len(rest) + 2):
        if k < len(rest):
            turn(rest[k])
            if k + 2 < len(rest):
                send_out(rest[k + 2])
        if 0 <= k - 1 < len(rest):
            adapt(rest[k - 1])
        if 0 <= k - 2 < len(rest):
            step_back(rest[k - 2])

    vec_out[...] = vec.finish(0)
    for s in range(slots):
        for d in range(1, owners):
            w_copy(s, d).wait()

    def block_step(b, carry):
        step = unfold(w_in[place_ref[b]].astype(full))
        block = blocks[b]
        new = block - matrix_rate * (step + weight_decay * block)
        new_ref[b] = new
        low_ref[b] = new.astype(low)
        return carry

    lax.fori_loop(0, count, block_step, 0)


class OptimizerPlan:
    def __init__(self, ready, dvecs, bases, spans, left_map, right_map, free, vector_rows):
        self.ready, self.dvecs, self.bases, self.spans = ready, dvecs, bases, spans
        self.left_map, self.right_map, self.free, self.vector_rows = left_map, right_map, free, vector_rows


def optimizer(
    index, places, tail, ready, dvecs, vector_rows, bases, lines, left_map, right_map, free, first, second, blocks,
    z_count, identity,
):
    slots, columns, width = first.shape
    owners = index.shape[0] // slots
    count, rows = blocks.shape[0], blocks.shape[1]
    span = bases[0].shape[2]
    lanes = 128
    shape = jax.ShapeDtypeStruct
    piece = (2 * rows, width // 2)
    tile = (span // 2, 2 * columns)
    smem = pl.BlockSpec(memory_space=pltpu.SMEM)
    spans = [(first_slot, amount) for _, first_slot, amount in lines]
    plan = OptimizerPlan(len(ready), len(dvecs), len(bases), spans, left_map, right_map, free, vector_rows)
    line_shapes = [shape((z_count, amount) + basis.shape[1:], low) for basis, _, amount in lines]
    return pl.pallas_call(
        functools.partial(optimizer_kernel, plan),
        out_shape=(
            shape(blocks.shape, full), shape(blocks.shape, low), shape(first.shape, full), shape(first.shape, full),
            shape((rows, lanes), full), *line_shapes,
        ),
        in_specs=[smem, smem, ANYWHERE, ANYWHERE, ANYWHERE, IN_VMEM]
        + [IN_VMEM] * (len(ready) + len(dvecs)) + [ANYWHERE] * (len(bases) + len(lines)),
        out_specs=(IN_VMEM,) * 5 + (ANYWHERE,) * len(lines),
        scratch_shapes=[
            pltpu.VMEM((count + 1,) + piece, low),
            pltpu.VMEM((z_count, slots, span, width), low),
            pltpu.VMEM((z_count, slots, columns, width), low),
            pltpu.VMEM((slots, columns, width), full),
            pltpu.VMEM((slots, columns, width), full),
            pltpu.VMEM((slots, owners) + piece, low),
            pltpu.VMEM((slots, owners) + piece, low),
            pltpu.VMEM((slots, z_count) + tile, low),
            pltpu.VMEM((slots, z_count) + tile, low),
            pltpu.VMEM((slots, z_count) + tile, low),
            pltpu.VMEM((slots, z_count) + tile, low),
            pltpu.VMEM((slots, owners) + piece, low),
            pltpu.VMEM((slots * owners,) + piece, low),
            pltpu.VMEM((1, owners // 2, 2, width // owners, lanes), full),
            pltpu.SemaphoreType.DMA((2, slots)),
            pltpu.SemaphoreType.DMA((2, slots, owners)),
            pltpu.SemaphoreType.DMA((2, slots, z_count)),
            pltpu.SemaphoreType.DMA((2, slots, z_count)),
            pltpu.SemaphoreType.DMA((2, slots, owners)),
            pltpu.SemaphoreType.DMA((slots,)),
            pltpu.SemaphoreType.DMA((slots,)),
            *sum_scratch(tail.shape[0], tail.shape[3], width, z_count),
            *sum_scratch(1, width // owners, lanes, z_count, full),
            *line_scratch(len(lines), z_count),
        ],
        compiler_params=pltpu.CompilerParams(
            vmem_limit_bytes=60 * MIB, collective_id=identity, has_side_effects=True
        ),
        cost_estimate=pl.CostEstimate(
            flops=8 * slots * span * width * width, bytes_accessed=40 * MIB, transcendentals=slots * width * columns
        ),
        name="optimizer",
    )(index, places, tail, first, second, blocks, *ready, *dvecs, *bases, *[basis for basis, _, _ in lines])


def slot_table(owner, slots, owner_rows):
    block_count = owner.shape[0]
    same_owner = owner[:, None] == owner[None, :]
    ordering = jnp.arange(block_count, dtype=jnp.int32)
    earlier = ordering[None, :] < ordering[:, None]
    ranking = jnp.sum(jnp.where(same_owner & earlier, 1, 0), axis=1).astype(jnp.int32)
    owner_match = owner[None, :] == jnp.arange(owner_rows, dtype=jnp.int32)[:, None]
    slot_match = ranking[None, :] == jnp.arange(slots, dtype=jnp.int32)[:, None]
    return jnp.where(slot_match[:, None, :] & owner_match[None, :, :], 1.0, 0.0).astype(full)


def scatter_sum(grads):
    blocks, width = grads.shape[0], grads.shape[2]
    cut = grads.reshape(blocks, lax.axis_size("dp"), -1, width).transpose(1, 0, 2, 3)
    outer = lax.psum_scatter(cut, "dp", scatter_dimension=0, tiled=False)
    blocks, rows, width = outer.shape
    count = lax.axis_size("fsdp")
    cut = outer.reshape(blocks, count, rows // count, width).transpose(1, 0, 2, 3)
    return lax.psum_scatter(cut, "fsdp", scatter_dimension=0, tiled=False)


def scatter_vectors(grads):
    rows, width = grads.shape
    count = lax.axis_size("dp") * lax.axis_size("fsdp")
    cut = grads.reshape(rows, count, width // count).transpose(1, 0, 2)
    return lax.psum_scatter(cut, ("dp", "fsdp"), scatter_dimension=0, tiled=False)


def gathering_program(
    tokens, segment, blocks, vectors, owner, left_basis, right_basis, rot_first, rot_second, cotangent, z_count
):
    layers, vector_rows = vectors.shape[:2]
    count, shard_rows, width = blocks.shape
    per_layer = count // layers
    inner = (per_layer - 4) // 2
    owners = lax.axis_size("dp")
    slots = rot_first.shape[0]
    part = width // owners
    lanes = 128
    seg_column = segment[:, :, None]

    order = [0, 1, 2, 3]
    for c in range(inner):
        order += [4 + c, 4 + inner + c]
    head = order + [per_layer + j for j in order[:4]]
    rest = [per_layer + j for j in order[4:]]
    vec_shard = vectors.astype(low).astype(full).reshape(layers * vector_rows, shard_rows).T
    vec_shard = jnp.pad(vec_shard, ((0, 0), (0, lanes - layers * vector_rows)))[None, None]
    wide_bases = (left_basis.reshape(slots, -1, width), right_basis.transpose(0, 2, 1))

    plan = ForwardPlan(
        inner, 0, blocks, head, vec_shard, vector_rows, [(wide_bases[1], 0, 2)], lead=5, row_positions=(1,),
        z_count=z_count, wide_bases=wide_bases,
    )
    empty_vec = jnp.zeros((16, width), full)
    results = forward_layer(tokens, seg_column, empty_vec, empty_vec, full, plan, 6)
    kept_a = results[:12]
    hidden, weights_a, vec_a, vec_b, right_01, left_low, right_low = results[12:]
    weights_a = weights_a.reshape(-1, width, width)
    plan = ForwardPlan(inner, 4, blocks, rest, lines=[(right_low, 2, 1)], lead=0, row_positions=(1, 4), z_count=z_count)
    plan.order = [per_layer + j for j in range(4)]
    results = forward_layer(hidden, seg_column, vec_b, weights_a, low, plan, 7)
    kept_b = results[:12]
    _, weights_b, right_2 = results[12:]
    gain, shift = vec_b[vector_rows - 2 : vector_rows - 1], vec_b[vector_rows - 1 : vector_rows]
    layer_out = (results[10] * gain + shift).astype(low)
    weights_b = weights_b.reshape(-1, width, width)

    def cut(grads):
        return grads.reshape(-1, owners // 2, 2, part, width)

    size = (part, width)
    own_b, own_a = 4, 3

    def left_over(own):
        return 2 * inner - own, own % 2

    plan = Plan(None, [(right_low, 3, 1)], z_count, own_b, size, wide_ready(own_b))
    dw_wide, dr1, da, dvec_wide_b, wide_sum_b, right_3 = wide_back(
        cotangent, kept_b[5:], vec_b, weights_b, (0, 1, 2), plan, 1
    )
    pending, skip = left_over(own_b)
    plan = Plan(cut(dw_wide), [(right_low, 4, 1), (left_low, 3, 1)], z_count, 1, size, list(range(pending + 1)), skip)
    dw_attend, upstream, dvec_attend_b, attend_sum_b, right_4, left_3 = attend_back(
        da, dr1, hidden, kept_b[:5], seg_column, weights_a, per_layer, plan, 2
    )
    plan = Plan(
        cut(dw_attend), [(left_low, 4, 1), (left_low, 0, 1)], z_count, own_a, size, [0, 1, 2] + wide_ready(own_a)
    )
    dw_wide, dr1, da, dvec_wide_a, wide_sum_a, left_4, left_0 = wide_back(
        upstream, kept_a[5:], vec_a, weights_a, (4, 5, 2), plan, 3
    )
    pending, skip = left_over(own_a)
    plan = Plan(cut(dw_wide), [(left_low, 1, 1)], z_count, 1, size, list(range(pending + 1)), skip)
    dw_attend, upstream, dvec_attend_a, attend_sum_a, left_1 = attend_back(
        da, dr1, tokens, kept_a[:5], seg_column, weights_a, 0, plan, 5
    )

    three = list(range(3))

    def early(own):
        return [4 + n // 2 + inner * (n % 2) for n in range(own)]

    def late(own):
        return [4 + c + inner * k for k in range(2) for c in range(inner) if 2 * c + k >= own] + [3]

    held_order = three + late(own_a) + [per_layer + j for j in three] + early(own_a)
    held_order += [per_layer + j for j in late(own_b) + early(own_b)]
    rank = jnp.asarray([held_order.index(j) for j in range(count)], jnp.int32)
    table = slot_table(owner, slots, owners).reshape(slots * owners, count)
    held = jnp.sum(table, axis=1)
    index = jnp.where(held > 0, jnp.sum(table * rank, axis=1), count).astype(jnp.int32)
    places = jnp.sum(table * jnp.arange(slots * owners, dtype=jnp.int32)[:, None], axis=0).astype(jnp.int32)
    bases = (right_01, right_2, right_3, right_4, left_0, left_1, left_3, left_4)
    right_map = [(0, 0), (0, 1), (1, 0), (2, 0), (3, 0)]
    left_map = [(4, 0), (5, 0), (8, 0), (6, 0), (7, 0)]
    free = list(range(3, slots))
    new_blocks, new_low, first_new, second_new, vec_sum, _ = optimizer(
        index, places, cut(dw_attend), (attend_sum_a, wide_sum_a, attend_sum_b, wide_sum_b),
        (dvec_attend_a, dvec_wide_a, dvec_attend_b, dvec_wide_b), vector_rows, bases, [(left_low, 2, 1)], left_map, right_map, free,
        rot_first.transpose(0, 2, 1), rot_second.transpose(0, 2, 1), blocks, z_count, 4,
    )
    first_new, second_new = first_new.transpose(0, 2, 1), second_new.transpose(0, 2, 1)
    vector_grad = vec_sum[:, : layers * vector_rows].T.reshape(layers, vector_rows, shard_rows)
    return layer_out, upstream, new_blocks, new_low, first_new, second_new, vector_grad


def plain_program(
    tokens, segment, blocks, vectors, owner, left_basis, right_basis, rot_first, rot_second, cotangent
):
    layers, vector_rows = vectors.shape[:2]
    per_layer = blocks.shape[0] // layers
    inner = (per_layer - 4) // 2
    width = blocks.shape[2]
    owner_rows = lax.axis_size("dp")
    slots = rot_first.shape[0]
    selector = slot_table(owner, slots, owner_rows)
    vector_parts = lax.all_gather(vectors.astype(low), ("dp", "fsdp"), axis=0, tiled=False)
    vector_full = vector_parts.transpose(1, 2, 0, 3).reshape(layers, vector_rows, width).astype(full)
    blocks_low, vector_full = lax.optimization_barrier((blocks.astype(low), vector_full))

    seg_column = segment[:, :, None]
    state = tokens
    kept = []
    for layer_index in range(layers):
        start = per_layer * layer_index
        weights = lax.all_gather(blocks_low[start : start + per_layer], ("dp", "fsdp"), axis=1, tiled=True)
        out_dtype = low if layer_index == layers - 1 else full
        results = forward_layer(
            state, seg_column, vector_full[layer_index], weights, out_dtype, ForwardPlan(inner, per_layer)
        )
        kept.append((state, weights, results[:5], results[5:12]))
        state = results[12]
    layer_out = state
    upstream = cotangent
    right_low = lax.all_gather(right_basis.astype(low), "fsdp", axis=2, tiled=True)
    block_shards = [None] * layers
    vector_shards = [None] * layers
    for layer_index in reversed(range(layers)):
        hidden, weights, attend_kept, wide_kept = kept[layer_index]
        dw_wide, dr1, da, dvec_wide = wide_back(
            upstream, wide_kept, vector_full[layer_index], weights, (4, 4 + inner, 1), Plan()
        )
        wide_shard = scatter_sum(dw_wide.reshape(-1, width, width))
        dw_attend, upstream, dvec_attend = attend_back(
            da, dr1, hidden, attend_kept, seg_column, weights, 0, Plan()
        )
        dvec = jnp.concatenate([dvec_attend[:2], dvec_wide[2:vector_rows]], axis=0)
        block_shards[layer_index] = jnp.concatenate([scatter_sum(dw_attend), wide_shard], axis=0)
        vector_shards[layer_index] = scatter_vectors(dvec)
    vector_grad = jnp.stack(vector_shards)
    block_grad = jnp.concatenate(block_shards, axis=0)
    outgoing = jnp.einsum("srk,kid->srid", selector.astype(low), block_grad, preferred_element_type=full)
    incoming = lax.all_to_all(outgoing.astype(low), "dp", split_axis=1, concat_axis=1, tiled=True)
    owned = incoming.reshape(slots, -1, width)
    turned = jnp.einsum("sik,skj->sij", owned, right_low, preferred_element_type=full).astype(low)
    left_rows = left_basis.reshape(slots, -1, width).astype(low)
    partial_sums = jnp.einsum("sra,srb->sab", left_rows, turned, preferred_element_type=full)
    rotated = lax.psum_scatter(
        partial_sums.astype(low), "fsdp", scatter_dimension=2, tiled=True
    ).astype(full)
    first_new, second_new, direction = moments(rotated, rot_first, rot_second)
    direction_full = lax.all_gather(direction.astype(low), "fsdp", axis=2, tiled=True)
    back_right = jnp.einsum("sab,scb->sac", direction_full, right_low, preferred_element_type=full)
    step_rows = jnp.einsum(
        "sia,sac->sic", left_rows, back_right.astype(low), preferred_element_type=full
    )
    returned = lax.all_to_all(
        step_rows.reshape(slots, owner_rows, -1, width).astype(low),
        "dp",
        split_axis=1,
        concat_axis=1,
        tiled=True,
    )
    step_shard = jnp.einsum("srk,srid->kid", selector.astype(low), returned, preferred_element_type=full)
    new_blocks = blocks - matrix_rate * (step_shard + weight_decay * blocks)
    return layer_out, upstream, new_blocks, new_blocks.astype(low), first_new, second_new, vector_grad


def shards(
    tokens,
    segment,
    blocks,
    vectors,
    owner,
    left_basis,
    right_basis,
    rot_first,
    rot_second,
    vec_first,
    vec_second,
    cotangent,
):
    operands = (
        tokens, segment, blocks, vectors, owner, left_basis, right_basis, rot_first, rot_second, cotangent
    )
    z_count = lax.axis_size("fsdp")
    if lax.axis_size("dp") == 8 and z_count == 4:
        results = gathering_program(*operands, z_count)
    else:
        results = plain_program(*operands)
    layer_out, upstream, new_blocks, new_low, first_new, second_new, vector_grad = results
    vector_first = beta_one * vec_first + (1.0 - beta_one) * vector_grad
    vector_second = beta_two * vec_second + (1.0 - beta_two) * vector_grad * vector_grad
    vector_step = (
        vector_first
        / (1.0 - beta_one**STEP)
        / (jnp.sqrt(vector_second / (1.0 - beta_two**STEP)) + adam_epsilon)
    )
    vector_new = vectors - vector_rate * (vector_step + weight_decay * vectors)
    return (
        layer_out,
        upstream,
        new_blocks,
        new_low,
        first_new,
        second_new,
        vector_first,
        vector_second,
        vector_new,
    )


def solution(mesh):
    return jax.shard_map(
        shards,
        mesh=mesh,
        in_specs=(
            P(("dp", "fsdp"), None),
            P(("dp", "fsdp"), None),
            P(None, ("dp", "fsdp"), None),
            P(None, None, ("dp", "fsdp")),
            P(),
            P("dp", None, "fsdp", None),
            P("dp", None, "fsdp"),
            P("dp", None, "fsdp"),
            P("dp", None, "fsdp"),
            P(None, None, ("dp", "fsdp")),
            P(None, None, ("dp", "fsdp")),
            P(("dp", "fsdp"), None),
        ),
        out_specs=(
            P(("dp", "fsdp"), None),
            P(("dp", "fsdp"), None),
            P(None, ("dp", "fsdp"), None),
            P(None, ("dp", "fsdp"), None),
            P("dp", None, "fsdp"),
            P("dp", None, "fsdp"),
            P(None, None, ("dp", "fsdp")),
            P(None, None, ("dp", "fsdp")),
            P(None, None, ("dp", "fsdp")),
        ),
        check_vma=False,
    )
```

```python
import functools

import jax
import jax.numpy as jnp
from jax import lax
from jax.experimental import pallas as pl
from jax.experimental.pallas import tpu as pltpu
from jax.sharding import PartitionSpec as P

H = 12
HD = 64
L = 512
STEP = 5
SEGS = 4
PAIR = 2 * HD
MIB = 1 << 20

beta_one = 0.5
beta_two = 0.5
adam_epsilon = 1e-08
norm_epsilon = 1e-06
matrix_rate = 0.03
vector_rate = 0.2
weight_decay = 0.01
masked_score = -1e30
low = jnp.bfloat16
full = jnp.float32


def dot_nn(a, b):
    return lax.dot_general(a, b, (((1,), (0,)), ((), ())), preferred_element_type=full)


def dot_nt(a, b):
    return lax.dot_general(a, b, (((1,), (1,)), ((), ())), preferred_element_type=full)


def dot_tn(a, b):
    return lax.dot_general(a, b, (((0,), (0,)), ((), ())), preferred_element_type=full)


def gelu_parts(z):
    t = pl.reciprocal(1.0 + 0.23164190 * jnp.abs(z), approx=True)
    square = z * z
    bell = jnp.exp2(-0.7213475204444817 * square)
    poly = ((((0.5307027145 * t - 0.7265760135) * t + 0.7107068705) * t - 0.142248368) * t + 0.127414796) * t
    tail = poly * bell
    phi = jnp.where(z >= 0, 1.0 - tail, tail)
    return z * phi, phi + (0.3989422804014327 * z) * bell


def norm_parts(residual):
    average = jnp.mean(residual, axis=-1, keepdims=True)
    centered = residual - average
    inverse = lax.rsqrt(jnp.mean(centered * centered, axis=-1, keepdims=True) + norm_epsilon)
    return centered * inverse, inverse


def norm_back(upstream, unit, inverse, gain):
    scaled = upstream * gain
    return inverse * (
        scaled
        - jnp.mean(scaled, axis=-1, keepdims=True)
        - unit * jnp.mean(scaled * unit, axis=-1, keepdims=True)
    )


def column_sum(values):
    return jnp.sum(values, axis=0, keepdims=True)


def half_masks(dtype):
    lane = lax.broadcasted_iota(jnp.int32, (1, PAIR), 1)
    first = (lane < HD).astype(full)
    return first.astype(dtype), (1.0 - first).astype(dtype)


def segment_codes(seg_column, masks):
    lane = lax.broadcasted_iota(jnp.int32, (1, PAIR), 1)
    lane = jnp.where(lane >= HD, lane - HD, lane)
    same = seg_column == lane
    key = jnp.where(same, 1.0, 0.0).astype(low)
    query = jnp.where(same | (lane >= SEGS), 0.0, masked_score).astype(low)
    return [key * masks[1 - h] for h in range(2)], [query * masks[1 - h] for h in range(2)]


class Place:
    def __init__(self, z_count):
        self.dp, self.z = lax.axis_index("dp"), lax.axis_index("fsdp")
        self.core, self.spot = lax.rem(self.dp, 2), lax.div(self.dp, 2)
        x_step = 1 - 2 * lax.rem(self.spot, 2)
        y_step = 2 - 4 * lax.div(self.spot, 2)
        self.spot_a = self.spot + (1 - self.core) * x_step + self.core * y_step
        self.spot_b = self.spot + self.core * x_step + (1 - self.core) * y_step
        self.spot_ab = self.spot + x_step + y_step
        self.sibling = (self.dp + 1 - 2 * self.core, self.z)
        self.near_a = (2 * self.spot_a + self.core, self.z)
        self.near_b = (2 * self.spot_b + self.core, self.z)
        self.z_count = z_count
        self.zs = [lax.rem(self.z + d, z_count) for d in range(z_count)]
        self.has_up, self.has_down = self.z < z_count - 1, self.z > 0
        self.middle = self.has_up & self.has_down
        self.across = lax.rem(self.z + 2, z_count)
        self.beside = jnp.where(self.z < 2, 1 - self.z, 5 - self.z)

    def line_sends(self, d):
        return {1: self.has_up, 2: self.z >= 0, 3: self.has_down}[d]

    def line_receives(self, d):
        return {1: self.has_down, 2: self.z >= 0, 3: self.has_up}[d]

    def chip_partners(self):
        return [self.sibling, self.near_a, self.near_b]

    def z_partners(self):
        return [(self.dp, other) for other in self.zs[1:]]


def greet(partners):
    barrier = pltpu.get_barrier_semaphore()
    for device in partners:
        pl.semaphore_signal(barrier, inc=1, device_id=device, device_id_type=pl.DeviceIdType.MESH)
    pl.semaphore_wait(barrier, len(partners))


def remote(source, target, send, receive, device):
    return pltpu.make_async_remote_copy(
        src_ref=source,
        dst_ref=target,
        send_sem=send,
        recv_sem=receive,
        device_id=device,
        device_id_type=pl.DeviceIdType.MESH,
    )


def fold(piece):
    half = piece.shape[1] // 2
    return jnp.concatenate([piece[:, :half], piece[:, half:]], axis=0)


def unfold(piece):
    rows = piece.shape[0] // 2
    return jnp.concatenate([piece[:rows], piece[rows:]], axis=1)


def looked_up(ticks, t):
    now = functools.reduce(jnp.logical_or, [t == tick for tick in ticks])
    which = sum(n * (t == tick).astype(jnp.int32) for n, tick in enumerate(ticks))
    return now, which


def run_due(stages, t):
    for ticks, stage in stages:
        if isinstance(t, int):
            if t in ticks:
                stage(ticks.index(t))
            continue
        now, block = looked_up(ticks, t)

        @pl.when(now)
        def _():
            stage(block)


def sum_times(ready):
    opens, cores, seconds = [], [], []
    for tick in ready:
        opens.append(max(tick, opens[-1] + 1) if opens else tick)
        cores.append(max(opens[-1] + 1, cores[-1] + 1) if cores else opens[-1] + 1)
        seconds.append(max(cores[-1] + 3, seconds[-1] + 3) if seconds else cores[-1] + 3)
    thirds = [tick + 2 for tick in seconds]
    return opens, cores, seconds, thirds, [tick + 2 for tick in thirds]


ANNOUNCE, FORWARD, FIRST, SECOND, CLOSE = -2, -1, 1, 2, 3


def sum_scratch(count, part, width, z_count, kind=low):
    piece = (2 * part // z_count, width // 2) if kind == low else (part // z_count, width)
    return [
        pltpu.VMEM((count, 4, part, width), kind),
        pltpu.VMEM((count, 4, part, width), kind),
        pltpu.VMEM((count, 2, part, width), kind),
        pltpu.VMEM((count, part, width), kind),
        pltpu.VMEM((count, z_count) + piece, kind),
        pltpu.VMEM((count, z_count) + piece, kind),
        pltpu.VMEM((count,) + piece, kind),
        pltpu.SemaphoreType.DMA((count,)),
        pltpu.SemaphoreType.DMA((count, 2)),
        pltpu.SemaphoreType.DMA((count, 2, 2)),
        pltpu.SemaphoreType.DMA((count, 2)),
        pltpu.SemaphoreType.DMA((count, 2, z_count)),
        pltpu.SemaphoreType.DMA((count, 2)),
    ]


SUM_REFS = 13


class BlockSum:
    def __init__(self, place, sources, refs, times):
        self.place, self.sources, self.times = place, sources, times
        (self.own, self.c, self.b, self.a, self.zs, self.zr, self.far,
         self.own_sem, self.c_sem, self.b_sem, self.a_sem, self.z_sem, self.far_sem) = refs
        self.count = self.c.shape[0]
        self.kind = self.c.dtype
        self.z_count = self.zs.shape[1]

    def load(self, i, block):
        return pltpu.make_async_copy(block.at[:, self.place.core], self.own.at[i], self.own_sem.at[i])

    def core_copy(self, i, block):
        return remote(
            block.at[:, 1 - self.place.core], self.c.at[i], self.c_sem.at[i, 0], self.c_sem.at[i, 1], self.place.sibling
        )

    def second_copy(self, i, k):
        chunk = self.place.spot_b if k == 0 else self.place.spot_ab
        return remote(
            self.c.at[i, chunk], self.b.at[i, k], self.b_sem.at[i, 0, k], self.b_sem.at[i, 1, k], self.place.near_b
        )

    def third_copy(self, i):
        return remote(
            self.c.at[i, self.place.spot_a], self.a.at[i], self.a_sem.at[i, 0], self.a_sem.at[i, 1], self.place.near_a
        )

    def z_copy(self, i, d):
        other = self.place.zs[d]
        return remote(
            self.zs.at[i, other], self.zr.at[i, self.place.z], self.z_sem.at[i, 0, d],
            self.z_sem.at[i, 1, self.z_count - d], (self.place.dp, other),
        )

    def open(self, i):
        first = 0
        for source in self.sources:
            count = source.shape[0]

            @pl.when((i >= first) & (i < first + count))
            def _():
                block = source.at[jnp.clip(i - first, 0, count - 1)]
                self.core_copy(i, block).start()
                self.load(i, block).start()

            first += count

    def after_core(self, i):
        block = self.sources[0].at[0]
        self.core_copy(i, block).wait()
        self.load(i, block).wait()

        def add(k, carry):
            self.c[i, k] = (self.c[i, k].astype(full) + self.own[i, k].astype(full)).astype(self.kind)
            return carry

        lax.fori_loop(0, 4, add, 0)
        self.second_copy(i, 0).start()
        self.second_copy(i, 1).start()

    def after_second(self, i):
        other, spot = self.place.spot_a, self.place.spot
        self.second_copy(i, 1).wait()
        self.c[i, other] = (self.c[i, other].astype(full) + self.b[i, 1].astype(full)).astype(self.kind)
        self.third_copy(i).start()
        self.second_copy(i, 0).wait()
        self.c[i, spot] = (self.c[i, spot].astype(full) + self.b[i, 0].astype(full)).astype(self.kind)

    def after_third(self, i):
        self.third_copy(i).wait()
        total = self.c[i, self.place.spot].astype(full) + self.a[i].astype(full)
        rows = total.shape[0] // self.z_count
        for k in range(self.z_count):
            piece = total[k * rows : (k + 1) * rows]
            self.zs[i, k] = fold(piece).astype(low) if self.kind == low else piece
        place = self.place
        for d in (1, 3):
            @pl.when(place.line_sends(d))
            def _():
                self.z_copy(i, d).start()

        @pl.when(jnp.logical_not(place.middle))
        def _():
            self.z_copy(i, 2).start()
            self.far_copy(i).start()
            opposite = self.z_count - 1 - place.z
            self.zr[i, opposite] = jnp.zeros(self.zr.shape[2:], self.kind)

    def far_copy(self, i):
        place = self.place
        return remote(
            self.zs.at[i, self.z_count - 1 - place.z], self.far.at[i], self.far_sem.at[i, 0], self.far_sem.at[i, 1],
            (place.dp, place.beside),
        )

    def relay(self, i):
        @pl.when(self.place.middle)
        def _():
            self.far_copy(i).wait_recv()
            across = self.place.across
            self.zs[i, across] = (self.zs[i, across].astype(full) + self.far[i].astype(full)).astype(self.kind)
            self.z_copy(i, 2).start()

    def finish(self, i):
        for d in range(1, self.z_count):
            @pl.when(self.place.line_sends(d))
            def _():
                self.z_copy(i, d).wait_send()

            @pl.when(self.place.line_receives(d))
            def _():
                self.z_copy(i, d).wait_recv()

        @pl.when(jnp.logical_not(self.place.middle))
        def _():
            self.far_copy(i).wait_send()

        total = self.zs[i, self.place.z].astype(full)
        for d in range(1, self.z_count):
            total = total + self.zr[i, self.place.zs[d]].astype(full)
        return total

    def tick(self, t):
        stages = (self.relay, self.after_third, self.after_second, self.after_core, self.open)
        run_due(list(zip(self.times[::-1], stages)), t)

    @property
    def last(self):
        return self.times[4][-1]


class LineGather:
    def __init__(self, place, source, target, first, local_sem, sem, z_count):
        self.place = place
        self.source = source.at[pl.ds(first, target.shape[1])]
        self.target, self.local_sem, self.sem, self.z_count = target, local_sem, sem, z_count

    def hop_copy(self, hop, way):
        dp, z = self.place.dp, self.place.z
        if way == 0:
            piece, other, coming = z - hop + 1, z + 1, z - hop
            sends = (piece >= 0) & (other < self.z_count)
            receives = coming >= 0
        else:
            piece, other, coming = z + hop - 1, z - 1, z + hop
            sends = (piece < self.z_count) & (other >= 0)
            receives = coming < self.z_count
        piece = jnp.clip(piece, 0, self.z_count - 1)
        other = jnp.clip(other, 0, self.z_count - 1)
        source = self.source if hop == 1 else self.target.at[piece]
        copy = remote(source, self.target.at[piece], self.sem.at[way, 0, hop - 1], self.sem.at[way, 1, hop - 1], (dp, other))
        return copy, sends, receives

    def local(self):
        return pltpu.make_async_copy(self.source, self.target.at[self.place.z], self.local_sem)

    def start(self, hop):
        if hop == 1:
            self.local().start()
        for way in range(2):
            copy, sends, _ = self.hop_copy(hop, way)

            @pl.when(sends)
            def _():
                copy.start()

    def wait(self, hop):
        if hop == 1:
            self.local().wait()
        for way in range(2):
            copy, sends, receives = self.hop_copy(hop, way)

            @pl.when(sends)
            def _():
                copy.wait_send()

            @pl.when(receives)
            def _():
                copy.wait_recv()

    def advance(self, hop):
        if hop > 1:
            self.wait(hop - 1)
        if hop < self.z_count:
            self.start(hop)


def gather_scratch(count, group, rows, width, z_count, kind=low):
    piece = (2 * rows // z_count, width // 2) if kind == low else (rows // z_count, width)
    return [
        pltpu.VMEM((count, z_count, group) + piece, kind),
        pltpu.SemaphoreType.DMA((count, 2, z_count)),
        pltpu.SemaphoreType.DMA((count, 2)),
        pltpu.SemaphoreType.DMA((count, 2, 2)),
        pltpu.SemaphoreType.DMA((count, 2)),
        pltpu.SemaphoreType.DMA((count, 2)),
    ]


GATHER_REFS = 6


class BlockGather:
    def __init__(self, place, source, whole, base, refs):
        self.place, self.source, self.whole, self.base = place, source, whole, base
        self.zr, self.z_sem, self.a_sem, self.b_sem, self.c_sem, self.far_sem = refs
        self.count, self.z_count, self.group = self.zr.shape[:3]

    def blocks(self, i):
        return pl.ds(self.base + self.group * i, self.group)

    def z_copy(self, i, d):
        place = self.place
        return remote(
            self.source.at[i], self.zr.at[i, place.z], self.z_sem.at[i, 0, d], self.z_sem.at[i, 1, self.z_count - d],
            (place.dp, place.zs[d]),
        )

    def chunk(self, i, spot):
        return self.whole.at[self.blocks(i), spot, self.place.core]

    def first_copy(self, i):
        chunk = self.chunk(i, self.place.spot)
        return remote(chunk, chunk, self.a_sem.at[i, 0], self.a_sem.at[i, 1], self.place.near_a)

    def second_copy(self, i, k):
        chunk = self.chunk(i, self.place.spot if k == 0 else self.place.spot_a)
        return remote(chunk, chunk, self.b_sem.at[i, 0, k], self.b_sem.at[i, 1, k], self.place.near_b)

    def core_copy(self, i):
        chunks = self.whole.at[self.blocks(i), :, self.place.core]
        return remote(chunks, chunks, self.c_sem.at[i, 0], self.c_sem.at[i, 1], self.place.sibling)

    def far_copy(self, i):
        place = self.place
        piece = self.zr.at[i, place.across]
        return remote(piece, piece, self.far_sem.at[i, 0], self.far_sem.at[i, 1], (place.dp, place.beside))

    def announce(self, i):
        for d in range(1, self.z_count):
            @pl.when(self.place.line_sends(d))
            def _():
                self.z_copy(i, d).start()

        self.zr[i, self.place.z] = self.source[i]

    def forward(self, i):
        @pl.when(self.place.middle)
        def _():
            self.z_copy(i, 2).wait_recv()
            self.far_copy(i).start()

    def begin(self):
        for i in range(min(-ANNOUNCE, self.count)):
            self.announce(i)

    def open(self, i):
        place = self.place
        for d in range(1, self.z_count):
            @pl.when(place.line_sends(d))
            def _():
                self.z_copy(i, d).wait_send()

        for d in (1, 3):
            @pl.when(place.line_receives(d))
            def _():
                self.z_copy(i, d).wait_recv()

        @pl.when(place.middle)
        def _():
            self.far_copy(i).wait_send()

        @pl.when(jnp.logical_not(place.middle))
        def _():
            self.z_copy(i, 2).wait_recv()
            self.far_copy(i).wait_recv()

        for n in range(self.group):
            pieces = [self.zr[i, k, n].astype(full) for k in range(self.z_count)]
            if self.zr.dtype == low:
                pieces = [unfold(piece) for piece in pieces]
            whole = jnp.concatenate(pieces, axis=0).astype(self.whole.dtype)
            self.whole[self.base + self.group * i + n, place.spot, place.core] = whole
        self.first_copy(i).start()
        self.second_copy(i, 0).start()

    def after_first(self, i):
        self.first_copy(i).wait()
        self.second_copy(i, 1).start()

    def after_second(self, i):
        self.second_copy(i, 0).wait()
        self.second_copy(i, 1).wait()
        self.core_copy(i).start()

    def close(self, i):
        self.core_copy(i).wait()

    def tick(self, t, done=None):
        def close(i):
            self.close(i)
            if done is not None:
                done(i)

        @pl.when(t == 0)
        def _():
            for i in range(min(-FORWARD, self.count)):
                self.forward(i)

        stages = (
            (SECOND, self.after_second), (FIRST, self.after_first), (0, self.open), (FORWARD, self.forward),
            (ANNOUNCE, self.announce), (CLOSE, close),
        )
        for late, stage in stages:
            @pl.when((t >= max(late, 0)) & (t - late < self.count))
            def _():
                stage(t - late)


def split_refs(refs, *counts):
    result, start = [], 0
    for count in counts:
        result.append(refs[start : start + count])
        start += count
    return result


class Side:
    def __init__(self, plan, sources, targets, sum_refs, line_refs, own=None):
        self.plan = plan
        sums = plan.sums
        blocks = [source.at[pl.ds(plan.skip, source.shape[0] - plan.skip)] for source in sources[:sums]]
        blocks += [own] if plan.own else []
        self.place = Place(plan.z_count) if plan.active else None
        self.sum = BlockSum(self.place, blocks, sum_refs, plan.times) if plan.total else None
        self.result = targets[0] if plan.total else None
        self.lines = line_gathers(self.place, plan.lines, sources[sums:], targets[bool(plan.total) :], line_refs, plan.z_count)

    def enter(self, now):
        if not self.plan.active:
            return

        @pl.when(now)
        def _():
            greet((self.place.chip_partners() if self.plan.total else []) + self.place.z_partners())
            for line in self.lines:
                line.advance(1)

    def tick(self, t):
        if self.plan.total:
            self.sum.tick(t)

    def leave(self, now, ticks):
        if not self.plan.active:
            return

        @pl.when(now)
        def _():
            if self.plan.total:
                if self.sum.last >= ticks:
                    lax.fori_loop(ticks, self.sum.last + 1, lambda t, carry: (self.tick(t), carry)[1], 0)
                for i in range(self.sum.count):
                    self.result[i] = self.sum.finish(i).astype(low)
            for line in self.lines:
                line.advance(self.plan.z_count)

    def advance(self, now, hop):
        if self.lines and hop < self.plan.z_count:
            @pl.when(now)
            def _():
                for line in self.lines:
                    line.advance(hop)


class Plan:
    def __init__(self, pending=None, lines=(), z_count=1, own=0, size=None, ready=(), skip=0):
        self.z_count = z_count
        self.sums = int(pending is not None)
        self.own, self.skip = own, skip
        self.total = own + (pending.shape[0] - skip if self.sums else 0)
        self.times = sum_times(ready) if self.total else None
        self.lines = [(first, count) for _, first, count in lines]
        self.active = bool(self.total or lines)
        self.arguments, self.results, self.result_specs, self.scratch = [], [], [], []
        if self.sums:
            self.arguments.append(pending)
        if self.total:
            part, width = size
            self.results.append(jax.ShapeDtypeStruct((self.total, 2 * part // z_count, width // 2), low))
            self.result_specs.append(
                pl.BlockSpec(self.results[0].shape, lambda i: (0, 0, 0), pipeline_mode=pl.Buffered(1))
            )
            self.scratch += sum_scratch(self.total, part, width, z_count)
        for basis, _, count in lines:
            self.arguments.append(basis)
            self.results.append(jax.ShapeDtypeStruct((z_count, count) + basis.shape[1:], low))
            self.result_specs.append(ANYWHERE)
        self.scratch += line_scratch(len(lines), z_count)
        self.argument_specs = [ANYWHERE] * len(self.arguments)

    def split(self, refs, inputs, outputs, scratch):
        count = len(self.lines)
        return split_refs(
            refs, inputs, self.sums + count, outputs, bool(self.total) + count, scratch,
            SUM_REFS * bool(self.total), 2 * bool(self.lines),
        )


def line_scratch(count, z_count):
    if not count:
        return []
    return [pltpu.SemaphoreType.DMA((count,)), pltpu.SemaphoreType.DMA((count, 2, 2, z_count - 1))]


def line_gathers(place, spans, sources, targets, refs, z_count):
    return [
        LineGather(place, source, target, first, refs[0].at[n], refs[1].at[n], z_count)
        for n, (source, target, (first, _)) in enumerate(zip(sources, targets, spans))
    ]


ANYWHERE = pl.BlockSpec(memory_space=pl.ANY)
IN_VMEM = pl.BlockSpec(memory_space=pltpu.VMEM)


def forward_kernel(plan, *refs):
    inputs, sources, outputs, targets, scratch, gather_refs, vec_refs, line_refs = plan.split(refs)
    x_ref, segc_ref, vec_ref, w_hbm = inputs
    (q_ref, k_ref, v_ref, ctxt_ref, lse_ref, x1_ref, inv1_ref, n1_ref, u_ref, gp_ref, x2_ref, inv2_ref,
     out_ref) = outputs
    w, codes, vt, n1_all, acc, w_sem = scratch
    s = pl.program_id(0)
    tokens, width = acc.shape
    rows_now = x_ref.shape[0]
    rows = tokens // rows_now
    inner = plan.inner
    local = plan.local
    gather = vec_gather = None
    place = Place(plan.z_count) if plan.gathered else None
    if plan.gathered:
        w_out, out_sem = targets[0], scratch_tail(plan, refs)
        gather = BlockGather(place, plan.folded(refs), w, local, gather_refs)
        if plan.vectors:
            vec_gather = BlockGather(place, sources[1], plan.vec_whole(refs), 0, vec_refs)
            vec_ref = targets[1]
    line_sources = sources[plan.line_at :]
    if plan.casts:
        wide_bases, low_bases = sources[-2:], targets[-2:]
        cast_in, cast_out, cast_sem = plan.cast_scratch(refs)
        line_sources = [low_bases[1]] * len(plan.lines)
    lines = line_gathers(place, plan.lines, line_sources, targets[plan.line_target_at :], line_refs, plan.z_count)

    def cast_slot(n):
        loads = [pltpu.make_async_copy(wide_bases[k].at[n], cast_in.at[k], cast_sem.at[0, k]) for k in range(2)]
        stores = [pltpu.make_async_copy(cast_out.at[k], low_bases[k].at[n], cast_sem.at[1, k]) for k in range(2)]
        for copy in loads:
            copy.start()
        for k in range(2):
            loads[k].wait()
            cast_out[k] = cast_in[k].astype(low)
            stores[k].start()
        for copy in stores:
            copy.wait()

    def keep(i):
        group = gather.group
        return pltpu.make_async_copy(w.at[gather.blocks(i)], w_out.at[pl.ds(group * i, group)], out_sem.at[i])

    def load(j):
        return pltpu.make_async_copy(w_hbm.at[plan.order[j]], w.at[j], w_sem.at[j])

    def matrix(j):
        return w[j].reshape(width, width)

    def arrive(j):
        if j < local:
            load(j).wait()

    def tick(t):
        if gather is not None:
            gather.tick(t, lambda i: keep(i).start())
            if vec_gather is not None:
                vec_gather.tick(t)

    pairs = width // PAIR

    @pl.when(s == 0)
    def _():
        for j in range(local):
            load(j).start()
        if gather is not None:
            for n, number in enumerate(plan.numbers):
                gather.source[n // plan.group, n % plan.group] = fold(sources[0][number]).astype(low)
            greet(place.chip_partners() + place.z_partners())
            if vec_gather is not None:
                vec_gather.begin()
            gather.begin()
        for j in range(min(local, 3)):
            arrive(j)

    def run_ticks(start, stop, casting=False):
        def body(t, carry):
            tick(t)
            if casting:
                @pl.when((s == 0) & (t < plan.casts))
                def _():
                    cast_slot(t)
            return carry

        if gather is not None:
            lax.fori_loop(start, stop, body, 0)

    def ready():
        for line in lines:
            line.advance(1)
        if vec_gather is not None:
            turned = vec_gather.whole[0].reshape(width, vec_gather.whole.shape[-1]).T
            for layer in range(2):
                count = plan.vector_rows
                targets[1 + layer][0:count, :] = turned[layer * count : (layer + 1) * count, :]

    def project():
        xin = x_ref[...].astype(low)
        keys, queries = segment_codes(segc_ref[0], half_masks(low))
        for h in range(2):
            codes[0, h] = keys[h]
            codes[1, h] = queries[h]
        q_ref[...] = (dot_nn(xin, matrix(0)) + vec_ref[0:1, :]).astype(low)
        k_ref[...] = dot_nn(xin, matrix(1)).astype(low)
        value = dot_nn(xin, matrix(2)) + vec_ref[1:2, :]
        v_ref[...] = value.astype(low)
        turned = value.T.astype(low)
        for h in range(width // HD):
            vt[h, 0:HD] = turned[h * HD : (h + 1) * HD]
            vt[h, HD : HD + 16] = jnp.ones((16, turned.shape[1]), low)

    def pair_step(p):
        masks = half_masks(low)
        lanes = pl.ds(pl.multiple_of(p * PAIR, PAIR), PAIR)
        q_pair = q_ref[:, lanes] * jnp.asarray(HD ** (-0.5), low)
        k_pair = k_ref[:, lanes]
        for h in range(2):
            scores = dot_nt(k_pair * masks[h] + codes[0, h], q_pair * masks[h] + codes[1, h])
            largest = jnp.max(scores, axis=0, keepdims=True)
            expanded = jnp.exp(scores - largest)
            here = pl.ds(pl.multiple_of(p * PAIR + h * HD, HD), HD)
            product = dot_nn(vt[2 * p + h], expanded.astype(low))
            total = product[HD : HD + 1]
            ctxt_ref[here, :] = (product[0:HD] * (1.0 / total)).astype(low)
            lse_ref[0, pl.ds(2 * p + h, 1), :] = largest + jnp.log(total)

    def close_row():
        @pl.when(s == 0)
        def _():
            if local > 3:
                arrive(3)
            for line in lines:
                line.advance(2)

        context = ctxt_ref[...].astype(full).T.astype(low)
        attended = dot_nn(context, matrix(3)) + vec_ref[2:3, :]
        unit, inverse = norm_parts(x_ref[...].astype(full) + attended)
        x1_ref[...] = unit
        inv1_ref[...] = inverse
        normed = unit * vec_ref[3:4, :] + vec_ref[4:5, :]
        here = pl.ds(pl.multiple_of(s * rows_now, rows_now), rows_now)
        acc[here, :] = normed + vec_ref[5 + inner : 6 + inner, :]
        normed = normed.astype(low)
        n1_ref[...] = normed
        n1_all[here, :] = normed

    @pl.when(s < rows)
    def _():
        def position(n, carry):
            if gather is not None:
                here, which = looked_up(plan.row_positions, n)
                before = plan.lead + s * len(plan.row_positions) + which
                opening = (s == 0) & (n == 0)
                start = jnp.where(opening, 0, before)
                stop = jnp.where(opening, plan.lead, jnp.where(here, before + 1, before))
                run_ticks(start, stop, plan.casts > 0)

                @pl.when(opening)
                def _():
                    ready()

            @pl.when(n == 0)
            def _():
                project()

            @pl.when((n >= 1) & (n <= pairs))
            def _():
                pair_step(n - 1)

            @pl.when(n == pairs + 1)
            def _():
                close_row()

            return carry

        lax.fori_loop(0, pairs + 2, position, 0)

    tile = tokens // 4
    starts, stops = plan.step_ticks(rows)

    @pl.when(s >= rows)
    def _():
        c = s - rows

        @pl.when(c == 0)
        def _():
            for j in range(4, local):
                arrive(j)
            for line in lines:
                line.advance(3)

        def token_step(i, carry):
            for half in range(2):
                here = pl.ds(pl.multiple_of((2 * i + half) * tile, tile), tile)
                value, slope = gelu_parts(dot_nn(n1_all[here, :], matrix(4 + 2 * c)) + vec_ref[pl.ds(5 + c, 1), :])
                active = value.astype(low)
                u_ref[here, :] = active
                gp_ref[here, :] = slope.astype(low)
                acc[here, :] += dot_nn(active, matrix(5 + 2 * c))
            return carry

        lax.fori_loop(0, 2, token_step, 0)

        @pl.when(c == inner - 1)
        def _():
            base = 5 + inner

            def last(i, carry):
                here = pl.ds(pl.multiple_of(i * tile, tile), tile)
                unit, inverse = norm_parts(acc[here, :])
                x2_ref[here, :] = unit
                inv2_ref[here, :] = inverse
                out_ref[here, :] = (
                    unit * vec_ref[base + 1 : base + 2, :] + vec_ref[base + 2 : base + 3, :]
                ).astype(out_ref.dtype)
                return carry

            lax.fori_loop(0, 4, last, 0)

        run_ticks(
            sum(n * (c == k).astype(jnp.int32) for k, n in enumerate(starts)),
            sum(n * (c == k).astype(jnp.int32) for k, n in enumerate(stops)),
        )

        @pl.when(c == inner - 1)
        def _():
            if gather is not None:
                for line in lines:
                    line.advance(plan.z_count)
                for i in range(gather.count):
                    keep(i).wait()


class ForwardPlan:
    def __init__(
        self, inner, local, blocks=None, numbers=(), vec_shard=None, vector_rows=0, lines=(), lead=0, row_positions=(), z_count=1,
        wide_bases=(),
    ):
        self.inner, self.local, self.lead, self.row_positions, self.z_count = inner, local, lead, row_positions, z_count
        self.vector_rows = vector_rows
        self.order = [0, 1, 2, 3]
        for c in range(inner):
            self.order += [4 + c, 4 + inner + c]
        self.numbers = list(numbers)
        self.gathered, self.group = len(self.numbers), 2
        self.vectors = vec_shard is not None
        self.lines = [(first, count) for _, first, count in lines]
        self.line_at = int(self.gathered > 0) + int(self.vectors)
        self.line_target_at = int(self.gathered > 0) + 2 * int(self.vectors)
        self.arguments, self.argument_specs, self.results, self.result_specs, self.scratch = [], [], [], [], []
        shape = jax.ShapeDtypeStruct
        if self.gathered:
            rows, width = blocks.shape[1:]
            groups = self.gathered // self.group
            self.arguments.append(blocks)
            self.argument_specs.append(IN_VMEM)
            self.results.append(shape((self.gathered, 4, 2, width // 8, width), low))
            self.result_specs.append(ANYWHERE)
            self.scratch += gather_scratch(groups, self.group, width // 8, width, z_count)
        if self.vectors:
            lanes = vec_shard.shape[3]
            self.arguments.append(vec_shard)
            self.argument_specs.append(IN_VMEM)
            for _ in range(2):
                self.results.append(shape((16, width), full))
                self.result_specs.append(pl.BlockSpec((16, width), lambda s: (0, 0)))
            self.scratch += gather_scratch(1, 1, width // 8, lanes, z_count, full)
        self.casts = wide_bases[0].shape[0] if wide_bases else 0
        for basis, _, count in lines:
            if not self.casts:
                self.arguments.append(basis)
                self.argument_specs.append(ANYWHERE)
            self.results.append(shape((z_count, count) + basis.shape[1:], low))
            self.result_specs.append(ANYWHERE)
        for basis in wide_bases:
            self.arguments.append(basis)
            self.argument_specs.append(ANYWHERE)
            self.results.append(shape(basis.shape, low))
            self.result_specs.append(ANYWHERE)
        self.scratch += line_scratch(len(lines), z_count)
        if self.casts:
            self.scratch += [
                pltpu.VMEM((2,) + wide_bases[0].shape[1:], full),
                pltpu.VMEM((2,) + wide_bases[0].shape[1:], low),
                pltpu.SemaphoreType.DMA((2, 2)),
            ]
        if self.gathered:
            self.scratch.append(pltpu.SemaphoreType.DMA((self.gathered // self.group,)))
        if self.vectors:
            self.scratch.append(pltpu.VMEM((1, 4, 2, width // 8, lanes), full))
        if self.gathered:
            self.scratch.append(pltpu.VMEM((groups, self.group, 2 * rows, width // 2), low))

    def step_ticks(self, rows):
        now, starts, stops = self.lead + rows * len(self.row_positions), [], []
        for c in range(self.inner):
            starts.append(now)
            if not self.gathered:
                stops.append(now)
                continue
            if c == self.inner - 1:
                now = max(now, self.gathered // self.group + CLOSE)
            else:
                now = max(now + 1, (5 + 2 * (c + 1) - self.local) // self.group + CLOSE + 1)
            stops.append(now)
        return starts, stops

    def split(self, refs):
        return split_refs(
            refs, 4, len(self.arguments), 13, len(self.results), 6, GATHER_REFS * bool(self.gathered),
            GATHER_REFS * self.vectors, 2 * bool(self.lines),
        )

    def vec_whole(self, refs):
        return refs[-2]

    def folded(self, refs):
        return refs[-1]

    def cast_scratch(self, refs):
        return refs[-6:-3]


def scratch_tail(plan, refs):
    return refs[-3] if plan.vectors else refs[-2]


def forward_layer(hidden, seg_column, vectors, weights, out_dtype, plan, identity=None):
    tokens, width = hidden.shape
    inner = plan.inner
    wide = width * inner
    rows = tokens // L
    heads = width // HD
    shape = jax.ShapeDtypeStruct

    def here(s):
        return jnp.minimum(s, rows - 1)

    def column(s):
        return jnp.maximum(s - rows, 0)

    def row_block(columns):
        return pl.BlockSpec((L, columns), lambda s: (here(s), 0))

    def whole(columns):
        return pl.BlockSpec((tokens, columns), lambda s: (0, 0), pipeline_mode=pl.Buffered(1))

    wide_block = pl.BlockSpec((tokens, width), lambda s: (0, column(s)))
    out_shape = (
        shape((tokens, width), low), shape((tokens, width), low), shape((tokens, width), low),
        shape((width, tokens), low), shape((rows, heads, L), full),
        shape((tokens, width), full), shape((tokens, 1), full), shape((tokens, width), low),
        shape((tokens, wide), low), shape((tokens, wide), low),
        shape((tokens, width), full), shape((tokens, 1), full), shape((tokens, width), out_dtype),
        *plan.results,
    )
    out_specs = (
        row_block(width), row_block(width), row_block(width),
        pl.BlockSpec((width, L), lambda s: (0, here(s))), pl.BlockSpec((1, heads, L), lambda s: (here(s), 0, 0)),
        row_block(width), row_block(1), row_block(width),
        wide_block, wide_block,
        whole(width), whole(1), whole(width),
        *plan.result_specs,
    )
    if plan.local:
        weights = weights.reshape(-1, 4, 2, width // 8, width)
    total = 4 + 2 * inner
    held = max(total, plan.local + plan.gathered)
    return pl.pallas_call(
        functools.partial(forward_kernel, plan),
        grid=(rows + inner,),
        out_shape=out_shape,
        in_specs=[
            row_block(width),
            pl.BlockSpec((1, L, 1), lambda s: (here(s), 0, 0)),
            pl.BlockSpec(vectors.shape, lambda s: (0, 0)),
            ANYWHERE,
            *plan.argument_specs,
        ],
        out_specs=out_specs,
        scratch_shapes=[
            pltpu.VMEM((held, 4, 2, width // 8, width), low),
            pltpu.VMEM((2, 2, L, PAIR), low),
            pltpu.VMEM((heads, HD + 16, L), low),
            pltpu.VMEM((tokens, width), low),
            pltpu.VMEM((tokens, width), full),
            pltpu.SemaphoreType.DMA((total,)),
            *plan.scratch,
        ],
        compiler_params=pltpu.CompilerParams(
            dimension_semantics=("arbitrary",), vmem_limit_bytes=62 * MIB,
            collective_id=identity, has_side_effects=identity is not None,
        ),
        cost_estimate=pl.CostEstimate(
            flops=2 * tokens * width * width * total + 4 * tokens * L * width,
            bytes_accessed=40 * MIB,
            transcendentals=tokens * (L * heads + wide),
        ),
        name="layer_forward",
    )(hidden, seg_column, vectors, weights, *plan.arguments)


WIDE_STEP_TICKS = 5


def wide_ready(own):
    return [WIDE_STEP_TICKS * (n // 2) + 4 + n % 2 for n in range(own)]


def wide_back_kernel(plan, inner, *refs):
    inputs, sources, outputs, targets, scratch, sum_refs, line_refs = plan.split(refs, 11, 4, 11)
    up_hbm, x2_hbm, inv2_hbm, x1_hbm, inv1_hbm, n1_hbm, vec_ref, wup_ref, wdown_ref, u_ref, gp_ref = inputs
    dw_ref, dr1_ref, da_ref, dvec_ref = outputs
    n1t, dz, kept_dw, up_ref, x2_ref, inv2_ref, x1_ref, inv1_ref, n1_ref, tile_sem, load_sem = scratch
    dy, dn1 = da_ref, dr1_ref
    c = pl.program_id(0)
    steps = pl.num_programs(0)
    tokens, width = dn1.shape
    tile = tokens // 4
    base = 5 + inner
    side = Side(plan, sources, targets, sum_refs, line_refs, kept_dw)

    def tile_copies(i):
        rows = pl.ds(pl.multiple_of(i * tile, tile), tile)
        return [
            pltpu.make_async_copy(source.at[rows], target.at[rows], tile_sem.at[n, i])
            for n, (source, target) in enumerate(((up_hbm, up_ref), (x2_hbm, x2_ref), (inv2_hbm, inv2_ref)))
        ]

    late_copies = [
        pltpu.make_async_copy(source, target, load_sem.at[n])
        for n, (source, target) in enumerate(((n1_hbm, n1_ref), (x1_hbm, x1_ref), (inv1_hbm, inv1_ref)))
    ]

    @pl.when(c == 0)
    def _():
        for i in range(4):
            for copy in tile_copies(i):
                copy.start()
        for copy in late_copies:
            copy.start()

    side.enter(c == 0)

    def prepare():
        gain = vec_ref[base + 1 : base + 2, :]

        def body(i, carry):
            for copy in tile_copies(i):
                copy.wait()
            gain_sum, shift_sum, bias_sum = carry
            rows = pl.ds(pl.multiple_of(i * tile, tile), tile)
            upstream = up_ref[rows, :].astype(full)
            unit = x2_ref[rows, :]
            back = norm_back(upstream, unit, inv2_ref[rows, :], gain)
            dn1[rows, :] = back
            branch = back.astype(low)
            dy[rows, :] = branch
            return (
                gain_sum + column_sum(upstream * unit),
                shift_sum + column_sum(upstream),
                bias_sum + column_sum(branch.astype(full)),
            )

        zero = jnp.zeros((1, width), full)
        gain_sum, shift_sum, bias_sum = lax.fori_loop(0, 4, body, (zero, zero, zero))
        dvec_ref[...] = jnp.zeros(dvec_ref.shape, full)
        dvec_ref[base : base + 1, :] = bias_sum
        dvec_ref[base + 1 : base + 2, :] = gain_sum
        dvec_ref[base + 2 : base + 3, :] = shift_sum
        late_copies[0].wait()
        n1t[...] = n1_ref[...].astype(full).T.astype(low)

    def token_pair(i):
        bias_sum = jnp.zeros((1, width), full)
        for half in range(2):
            rows = pl.ds(pl.multiple_of((2 * i + half) * tile, tile), tile)
            slope = gp_ref[rows, :].astype(full)
            piece = (dot_nt(dy[rows, :], wdown_ref[0]) * slope).astype(low)
            dz[rows, :] = piece
            dn1[rows, :] += dot_nt(piece, wup_ref[0])
            bias_sum = bias_sum + column_sum(piece.astype(full))
        dvec_ref[pl.ds(5 + c, 1), :] += bias_sum

    def store(k, product):
        if plan.own:
            @pl.when(2 * c + k < plan.own)
            def _():
                kept_dw[2 * c + k] = product().reshape(kept_dw.shape[1:])

            @pl.when(2 * c + k >= plan.own)
            def _():
                dw_ref[k, 0] = product()
        else:
            dw_ref[k, 0] = product()

    def position(n, carry):
        side.tick(WIDE_STEP_TICKS * c + n)
        side.advance((c == 1) & (n == 1), 2)
        side.advance((c == 2) & (n == 4), 3)

        @pl.when((n == 0) & (c == 0))
        def _():
            prepare()

        @pl.when((n == 1) | (n == 2))
        def _():
            token_pair(n - 1)

        @pl.when(n == 3)
        def _():
            store(0, lambda: dot_nn(n1t[...], dz[...]).astype(low))

        @pl.when(n == 4)
        def _():
            store(1, lambda: dot_tn(u_ref[...], dy[...]).astype(low))

        return carry

    lax.fori_loop(0, WIDE_STEP_TICKS, position, 0)
    @pl.when(c == steps - 1)
    def _():
        for copy in late_copies[1:]:
            copy.wait()
        gain = vec_ref[3:4, :]

        def body(i, carry):
            gain_sum, shift_sum, bias_sum = carry
            rows = pl.ds(pl.multiple_of(i * tile, tile), tile)
            upstream = dn1[rows, :]
            unit = x1_ref[rows, :]
            back = norm_back(upstream, unit, inv1_ref[rows, :], gain)
            dr1_ref[rows, :] = back
            branch = back.astype(low)
            da_ref[rows, :] = branch
            return (
                gain_sum + column_sum(upstream * unit),
                shift_sum + column_sum(upstream),
                bias_sum + column_sum(branch.astype(full)),
            )

        zero = jnp.zeros((1, width), full)
        gain_sum, shift_sum, bias_sum = lax.fori_loop(0, 4, body, (zero, zero, zero))
        dvec_ref[2:3, :] = bias_sum
        dvec_ref[3:4, :] = gain_sum
        dvec_ref[4:5, :] = shift_sum

    side.leave(c == steps - 1, WIDE_STEP_TICKS * inner)


def wide_back(upstream, kept, vectors, weights, places, plan, identity=None):
    x1, inv1, n1, u, gp, x2, inv2 = kept
    tokens, width = x1.shape
    up_start, down_start, stride = places
    inner = u.shape[1] // width
    shape = jax.ShapeDtypeStruct

    return pl.pallas_call(
        functools.partial(wide_back_kernel, plan, inner),
        grid=(inner,),
        out_shape=(
            shape((2, inner - plan.own // 2, width, width), low),
            shape((tokens, width), full), shape((tokens, width), low), shape((16, width), full),
            *plan.results,
        ),
        in_specs=[
            *[ANYWHERE] * 6,
            pl.BlockSpec(vectors.shape, lambda c: (0, 0), pipeline_mode=pl.Buffered(1)),
            pl.BlockSpec((1, width, width), lambda c: (up_start + stride * c, 0, 0)),
            pl.BlockSpec((1, width, width), lambda c: (down_start + stride * c, 0, 0)),
            pl.BlockSpec((tokens, width), lambda c: (0, c)),
            pl.BlockSpec((tokens, width), lambda c: (0, c)),
            *plan.argument_specs,
        ],
        out_specs=(
            pl.BlockSpec((2, 1, width, width), lambda c: (0, jnp.maximum(c - plan.own // 2, 0), 0, 0)),
            pl.BlockSpec((tokens, width), lambda c: (0, 0), pipeline_mode=pl.Buffered(1)),
            pl.BlockSpec((tokens, width), lambda c: (0, 0), pipeline_mode=pl.Buffered(1)),
            pl.BlockSpec((16, width), lambda c: (0, 0)),
            *plan.result_specs,
        ),
        scratch_shapes=[
            pltpu.VMEM((width, tokens), low),
            pltpu.VMEM((tokens, width), low),
            pltpu.VMEM((plan.own, 4, 2, width // 8, width) if plan.own else (8, 128), low),
            pltpu.VMEM((tokens, width), upstream.dtype),
            pltpu.VMEM((tokens, width), full),
            pltpu.VMEM((tokens, 1), full),
            pltpu.VMEM((tokens, width), full),
            pltpu.VMEM((tokens, 1), full),
            pltpu.VMEM((tokens, width), low),
            pltpu.SemaphoreType.DMA((3, 4)),
            pltpu.SemaphoreType.DMA((3,)),
            *plan.scratch,
        ],
        compiler_params=pltpu.CompilerParams(
            dimension_semantics=("arbitrary",), vmem_limit_bytes=60 * MIB,
            collective_id=identity, has_side_effects=identity is not None,
        ),
        cost_estimate=pl.CostEstimate(
            flops=8 * tokens * width * width * inner, bytes_accessed=50 * MIB, transcendentals=0
        ),
        name="wide_backward",
    )(upstream, x2, inv2, x1, inv1, n1, vectors, weights, weights, u, gp, *plan.arguments)


def attend_back_kernel(plan, *refs):
    inputs, sources, outputs, targets, scratch, sum_refs, line_refs = plan.split(refs, 10, 3, 12)
    da_hbm, dr1_ref, x_ref, q_ref, k_ref, v_ref, ctxt_hbm, lse_ref, segc_ref, w_hbm = inputs
    dw_ref, dx_ref, dvec_ref = outputs
    codes, dctx, kt, delta, dqt, xt, grads, dwo, da_ref, ctxt_ref, w_ref, load_sem = scratch
    r = pl.program_id(0)
    loads = [
        pltpu.make_async_copy(w_hbm.at[plan.start + 3], w_ref.at[3], load_sem.at[0]),
        pltpu.make_async_copy(da_hbm, da_ref, load_sem.at[1]),
        pltpu.make_async_copy(ctxt_hbm, ctxt_ref, load_sem.at[2]),
        pltpu.make_async_copy(w_hbm.at[pl.ds(plan.start, 3)], w_ref.at[pl.ds(0, 3)], load_sem.at[3]),
    ]

    @pl.when(r == 0)
    def _():
        for copy in loads:
            copy.start()

    side = Side(plan, sources, targets, sum_refs, line_refs, dwo)
    side.enter(r == 0)
    tokens, width = dr1_ref.shape
    pairs = width // PAIR
    ticks = pairs + 5
    here = pl.ds(pl.multiple_of(r * tokens, tokens), tokens)
    masks = half_masks(low)
    scale = HD ** (-0.5)
    last_row = pl.num_programs(0) - 1

    def prepare():
        @pl.when(r == 0)
        def _():
            for copy in loads[:3]:
                copy.wait()
            grad = dot_nn(ctxt_ref[...], da_ref[...]).astype(low)
            if plan.own:
                dwo[0] = grad.reshape(dwo.shape[1:])
            else:
                dw_ref[3] = grad
            dvec_ref[...] = jnp.zeros(dvec_ref.shape, full)

        xt[:, here] = x_ref[...].astype(low).astype(full).T.astype(low)
        keys, queries = segment_codes(segc_ref[0], masks)
        for h in range(2):
            codes[0, h] = keys[h]
            codes[1, h] = queries[h]
        context_grad = dot_nt(da_ref[here, :], w_ref[3]).astype(low)
        dctx[...] = context_grad
        kt[...] = k_ref[...].astype(full).T.astype(low)
        products = context_grad.astype(full) * ctxt_ref[:, here].astype(full).T
        feature = lax.broadcasted_iota(jnp.int32, (16, width), 1)
        head = lax.broadcasted_iota(jnp.int32, (16, width), 0)
        member = ((feature >= head * HD) & (feature < (head + 1) * HD)).astype(full).astype(low)
        high = products.astype(low)
        rest = (products - high.astype(full)).astype(low)
        delta[...] = dot_nt(member, high) + dot_nt(member, rest)

    def pair_step(p):
        lanes = pl.ds(pl.multiple_of(p * PAIR, PAIR), PAIR)
        q_pair = q_ref[:, lanes] * jnp.asarray(scale, low)
        k_pair = k_ref[:, lanes]
        v_pair = v_ref[:, lanes]
        g_pair = dctx[:, lanes]
        key_grad = jnp.zeros((tokens, PAIR), full)
        value_grad = jnp.zeros((tokens, PAIR), full)
        for h in range(2):
            q_half = q_pair * masks[h]
            g_half = g_pair * masks[h]
            scores = dot_nt(k_pair * masks[h] + codes[0, h], q_half + codes[1, h])
            attention = jnp.exp(scores - lse_ref[0, pl.ds(2 * p + h, 1), :]).astype(low)
            value_grad = value_grad + dot_nn(attention, g_half)
            attention_grad = dot_nt(v_pair, g_half)
            score_grad = attention * (attention_grad - delta[pl.ds(2 * p + h, 1), :]).astype(low)
            key_grad = key_grad + dot_nn(score_grad, q_half)
            rows = pl.ds(pl.multiple_of(p * PAIR + h * HD, HD), HD)
            dqt[rows, :] = dot_nn(kt[rows, :], score_grad) * scale
        grads[1, here, lanes] = key_grad.astype(low)
        grads[2, here, lanes] = value_grad.astype(low)

    def inputs_step():
        @pl.when(r == 0)
        def _():
            loads[3].wait()

        query_grad = dqt[...].T.astype(low)
        grads[0, here, :] = query_grad
        value_grad = grads[2, here, :]
        dx_ref[...] = (
            dr1_ref[...]
            + dot_nt(query_grad, w_ref[0])
            + dot_nt(grads[1, here, :], w_ref[1])
            + dot_nt(value_grad, w_ref[2])
        )
        dvec_ref[0:1, :] += column_sum(query_grad.astype(full))
        dvec_ref[1:2, :] += column_sum(value_grad.astype(full))

    def position(n, carry):
        side.tick(r * ticks + n)
        side.advance((r == 0) & (n == 6), 2)
        side.advance((r == 1) & (n == 4), 3)

        @pl.when(n == 0)
        def _():
            prepare()

        @pl.when((n >= 1) & (n <= pairs))
        def _():
            pair_step(n - 1)

        @pl.when(n == pairs + 1)
        def _():
            inputs_step()

        @pl.when((n > pairs + 1) & (r == last_row))
        def _():
            j = n - (pairs + 2)
            dw_ref[j] = dot_nn(xt[...], grads[j]).astype(low)

        return carry

    lax.fori_loop(0, ticks, position, 0)
    side.leave(r == last_row, plan.rows * ticks)


def attend_back(da, dr1, hidden, kept, seg_column, weights, start, plan, identity=None):
    q, k, v, ctxt, lse = kept
    tokens, width = da.shape
    rows = tokens // L
    heads = width // HD
    shape = jax.ShapeDtypeStruct
    plan.start, plan.rows = start, rows

    def row_block():
        return pl.BlockSpec((L, width), lambda r: (r, 0))

    return pl.pallas_call(
        functools.partial(attend_back_kernel, plan),
        grid=(rows,),
        out_shape=(
            shape((4 - plan.own, width, width), low), shape((tokens, width), full), shape((8, width), full),
            *plan.results,
        ),
        in_specs=[
            ANYWHERE,
            row_block(), row_block(), row_block(), row_block(), row_block(),
            ANYWHERE,
            pl.BlockSpec((1, heads, L), lambda r: (r, 0, 0)),
            pl.BlockSpec((1, L, 1), lambda r: (r, 0, 0)),
            ANYWHERE,
            *plan.argument_specs,
        ],
        out_specs=(
            pl.BlockSpec((4 - plan.own, width, width), lambda r: (0, 0, 0), pipeline_mode=pl.Buffered(1)),
            row_block(),
            pl.BlockSpec((8, width), lambda r: (0, 0)),
            *plan.result_specs,
        ),
        scratch_shapes=[
            pltpu.VMEM((2, 2, L, PAIR), low),
            pltpu.VMEM((L, width), low),
            pltpu.VMEM((width, L), low),
            pltpu.VMEM((16, L), full),
            pltpu.VMEM((width, L), full),
            pltpu.VMEM((width, tokens), low),
            pltpu.VMEM((3, tokens, width), low),
            pltpu.VMEM((1, 4, 2, width // 8, width) if plan.own else (8, 128), low),
            pltpu.VMEM((tokens, width), low),
            pltpu.VMEM((width, tokens), low),
            pltpu.VMEM((4, width, width), low),
            pltpu.SemaphoreType.DMA((4,)),
            *plan.scratch,
        ],
        compiler_params=pltpu.CompilerParams(
            dimension_semantics=("arbitrary",), vmem_limit_bytes=60 * MIB,
            collective_id=identity, has_side_effects=identity is not None,
        ),
        cost_estimate=pl.CostEstimate(
            flops=16 * tokens * width * width + 10 * tokens * L * width,
            bytes_accessed=30 * MIB,
            transcendentals=tokens * L * heads,
        ),
        name="attend_backward",
    )(da, dr1, hidden, q, k, v, ctxt, lse, seg_column, weights, *plan.arguments)


def moments(rotated, first, second):
    first_new = beta_one * first + (1.0 - beta_one) * rotated
    second_new = beta_two * second + (1.0 - beta_two) * rotated * rotated
    direction = (
        first_new
        / (1.0 - beta_one**STEP)
        / (jnp.sqrt(second_new / (1.0 - beta_two**STEP)) + adam_epsilon)
    )
    return first_new, second_new, direction


def pack_lanes(piece):
    rows = piece.shape[0] // 2
    return jnp.concatenate([piece[:rows], piece[rows:]], axis=1)


def unpack_lanes(piece):
    columns = piece.shape[1] // 2
    return jnp.concatenate([piece[:, :columns], piece[:, columns:]], axis=0)


def optimizer_kernel(plan, *refs):
    spans = len(plan.spans)
    inputs, ready, dvecs, bases, lines_in, outputs, lines_out, scratch, sum_refs, vec_refs, line_refs = split_refs(
        refs, 6, plan.ready, plan.dvecs, plan.bases, spans, 5, spans, 21, SUM_REFS, SUM_REFS, 2 * bool(spans)
    )
    index_ref, place_ref, tail_hbm, first_hbm, second_hbm, blocks = inputs
    new_ref, low_ref, first_out, second_out, vec_out = outputs
    (store, left, right, first_in, second_in, g_out, g_in, t_out, t_in, e_out, e_in, w_out, w_in, vec_source,
     load_sem, g_sem, t_sem, e_sem, w_sem, left_sem, right_sem) = scratch
    slots, owners = g_in.shape[0], g_in.shape[1]
    z_count = t_in.shape[1]
    place = Place(z_count)
    dp, z = place.dp, place.z
    dps = [lax.rem(dp + d, owners) for d in range(owners)]
    count = blocks.shape[0]
    many = tail_hbm.shape[0]
    tail_times = [[many * stage + n for n in range(many)] for stage in range(5)]
    tail = BlockSum(place, [tail_hbm], sum_refs, tail_times)
    vec = BlockSum(place, [vec_source], vec_refs, [[many * stage + 1] for stage in range(5)])
    order = plan.free + [s for s in range(slots) if s not in plan.free]
    lines = line_gathers(place, plan.spans, lines_in, lines_out, line_refs, z_count)
    every = list(bases) + list(lines_out)
    late = [s for s in range(slots) if plan.left_map[s][0] >= len(bases)]

    def load(refs_map, target, sem, s):
        n, at = refs_map[s]
        return pltpu.make_async_copy(every[n].at[:, at], target.at[:, s], sem.at[s])

    def load_first(s):
        return pltpu.make_async_copy(first_hbm.at[s], first_in.at[s], load_sem.at[0, s])

    def load_second(s):
        return pltpu.make_async_copy(second_hbm.at[s], second_in.at[s], load_sem.at[1, s])

    for s in order:
        load(plan.right_map, right, right_sem, s).start()
        if s not in late:
            load(plan.left_map, left, left_sem, s).start()
        load_first(s).start()
        load_second(s).start()
    greet([(other, z) for other in dps[1:]] + place.z_partners())
    start = many
    for part in ready:
        store[start : start + part.shape[0]] = part[...]
        start += part.shape[0]
    store[0:many] = jnp.zeros((many,) + store.shape[1:], low)
    store[count] = jnp.zeros(store.shape[1:], low)
    rows = plan.vector_rows
    stacked = jnp.concatenate(
        [dvecs[0][0:2, :], dvecs[1][2:rows, :], dvecs[2][0:2, :], dvecs[3][2:rows, :],
         jnp.zeros((vec_source.shape[-1] - 2 * rows, blocks.shape[2]), full)], axis=0
    )
    vec_source[0] = stacked.T.reshape(vec_source.shape[1:])

    def g_copy(s, d):
        other = dps[d]
        return remote(g_out.at[s, d], g_in.at[s, dp], g_sem.at[0, s, d], g_sem.at[1, s, owners - d], (other, z))

    def t_copy(s, d):
        other = place.zs[d]
        return remote(t_out.at[s, d], t_in.at[s, z], t_sem.at[0, s, d], t_sem.at[1, s, z_count - d], (dp, other))

    def e_copy(s, d):
        other = place.zs[d]
        return remote(e_out.at[s, d], e_in.at[s, z], e_sem.at[0, s, d], e_sem.at[1, s, z_count - d], (dp, other))

    def w_copy(s, d):
        other = dps[d]
        return remote(
            w_out.at[s, other], w_in.at[s * owners + dp], w_sem.at[0, s, d], w_sem.at[1, s, owners - d], (other, z)
        )

    def send_out(s):
        for d in range(1, owners):
            g_out[s, d] = store[index_ref[s * owners + dps[d]]]
            g_copy(s, d).start()
        g_in[s, dp] = store[index_ref[s * owners + dp]]

    def turn(s):
        for d in range(1, owners):
            g_copy(s, d).wait()
        load(plan.right_map, right, right_sem, s).wait()
        grad = jnp.concatenate([unfold(g_in[s, c].astype(full)) for c in range(owners)], axis=0).astype(low)
        for d in range(1, z_count):
            t_out[s, d] = pack_lanes(dot_nt(right[place.zs[d], s], grad)).astype(low)
            t_copy(s, d).start()
        t_in[s, z] = pack_lanes(dot_nt(right[z, s], grad)).astype(low)

    def adapt(s):
        for d in range(1, z_count):
            t_copy(s, d).wait()
        load_first(s).wait()
        load_second(s).wait()
        load(plan.left_map, left, left_sem, s).wait()
        rotated = jnp.zeros(first_in.shape[1:], full)
        for f in range(z_count):
            rotated = rotated + dot_nn(unpack_lanes(t_in[s, f].astype(full)).astype(low), left[f, s])
        first_new, second_new, direction = moments(rotated, first_in[s], second_in[s])
        first_out[s] = first_new
        second_out[s] = second_new
        direction = direction.astype(low)
        for d in range(1, z_count):
            e_out[s, d] = pack_lanes(dot_nt(left[place.zs[d], s], direction)).astype(low)
            e_copy(s, d).start()
        e_in[s, z] = pack_lanes(dot_nt(left[z, s], direction)).astype(low)

    def step_back(s):
        for d in range(1, z_count):
            e_copy(s, d).wait()
        step = jnp.zeros((left.shape[2], left.shape[3]), full)
        for f in range(z_count):
            step = step + dot_nn(unpack_lanes(e_in[s, f].astype(full)).astype(low), right[f, s])
        share = step.shape[0] // owners
        for c in range(owners):
            w_out[s, c] = fold(step[c * share : (c + 1) * share]).astype(low)
        for d in range(1, owners):
            w_copy(s, d).start()
        w_in[s * owners + dp] = w_out[s, dp]

    def sums(stage):
        for t in range(many * stage, many * (stage + 1)):
            tail.tick(t)
            vec.tick(t)

    free = plan.free
    def advance(hop):
        for line in lines:
            line.advance(hop)

    sums(0)
    advance(1)
    for s in free:
        send_out(s)
    sums(1)
    for s in free:
        turn(s)
    sums(2)
    advance(2)
    for s in free:
        adapt(s)
    sums(3)
    sums(4)
    advance(3)
    for i in range(many):
        store[i] = tail.finish(i).astype(low)
    rest = order[len(free) :]
    for s in rest[:2]:
        send_out(s)
    for s in free:
        step_back(s)
    advance(z_count)
    for s in late:
        load(plan.left_map, left, left_sem, s).start()
    for k in range(len(rest) + 2):
        if k < len(rest):
            turn(rest[k])
            if k + 2 < len(rest):
                send_out(rest[k + 2])
        if 0 <= k - 1 < len(rest):
            adapt(rest[k - 1])
        if 0 <= k - 2 < len(rest):
            step_back(rest[k - 2])

    vec_out[...] = vec.finish(0)
    for s in range(slots):
        for d in range(1, owners):
            w_copy(s, d).wait()

    def block_step(b, carry):
        step = unfold(w_in[place_ref[b]].astype(full))
        block = blocks[b]
        new = block - matrix_rate * (step + weight_decay * block)
        new_ref[b] = new
        low_ref[b] = new.astype(low)
        return carry

    lax.fori_loop(0, count, block_step, 0)


class OptimizerPlan:
    def __init__(self, ready, dvecs, bases, spans, left_map, right_map, free, vector_rows):
        self.ready, self.dvecs, self.bases, self.spans = ready, dvecs, bases, spans
        self.left_map, self.right_map, self.free, self.vector_rows = left_map, right_map, free, vector_rows


def optimizer(
    index, places, tail, ready, dvecs, vector_rows, bases, lines, left_map, right_map, free, first, second, blocks,
    z_count, identity,
):
    slots, columns, width = first.shape
    owners = index.shape[0] // slots
    count, rows = blocks.shape[0], blocks.shape[1]
    span = bases[0].shape[2]
    lanes = 128
    shape = jax.ShapeDtypeStruct
    piece = (2 * rows, width // 2)
    tile = (span // 2, 2 * columns)
    smem = pl.BlockSpec(memory_space=pltpu.SMEM)
    spans = [(first_slot, amount) for _, first_slot, amount in lines]
    plan = OptimizerPlan(len(ready), len(dvecs), len(bases), spans, left_map, right_map, free, vector_rows)
    line_shapes = [shape((z_count, amount) + basis.shape[1:], low) for basis, _, amount in lines]
    return pl.pallas_call(
        functools.partial(optimizer_kernel, plan),
        out_shape=(
            shape(blocks.shape, full), shape(blocks.shape, low), shape(first.shape, full), shape(first.shape, full),
            shape((rows, lanes), full), *line_shapes,
        ),
        in_specs=[smem, smem, ANYWHERE, ANYWHERE, ANYWHERE, IN_VMEM]
        + [IN_VMEM] * (len(ready) + len(dvecs)) + [ANYWHERE] * (len(bases) + len(lines)),
        out_specs=(IN_VMEM,) * 5 + (ANYWHERE,) * len(lines),
        scratch_shapes=[
            pltpu.VMEM((count + 1,) + piece, low),
            pltpu.VMEM((z_count, slots, span, width), low),
            pltpu.VMEM((z_count, slots, columns, width), low),
            pltpu.VMEM((slots, columns, width), full),
            pltpu.VMEM((slots, columns, width), full),
            pltpu.VMEM((slots, owners) + piece, low),
            pltpu.VMEM((slots, owners) + piece, low),
            pltpu.VMEM((slots, z_count) + tile, low),
            pltpu.VMEM((slots, z_count) + tile, low),
            pltpu.VMEM((slots, z_count) + tile, low),
            pltpu.VMEM((slots, z_count) + tile, low),
            pltpu.VMEM((slots, owners) + piece, low),
            pltpu.VMEM((slots * owners,) + piece, low),
            pltpu.VMEM((1, owners // 2, 2, width // owners, lanes), full),
            pltpu.SemaphoreType.DMA((2, slots)),
            pltpu.SemaphoreType.DMA((2, slots, owners)),
            pltpu.SemaphoreType.DMA((2, slots, z_count)),
            pltpu.SemaphoreType.DMA((2, slots, z_count)),
            pltpu.SemaphoreType.DMA((2, slots, owners)),
            pltpu.SemaphoreType.DMA((slots,)),
            pltpu.SemaphoreType.DMA((slots,)),
            *sum_scratch(tail.shape[0], tail.shape[3], width, z_count),
            *sum_scratch(1, width // owners, lanes, z_count, full),
            *line_scratch(len(lines), z_count),
        ],
        compiler_params=pltpu.CompilerParams(
            vmem_limit_bytes=60 * MIB, collective_id=identity, has_side_effects=True
        ),
        cost_estimate=pl.CostEstimate(
            flops=8 * slots * span * width * width, bytes_accessed=40 * MIB, transcendentals=slots * width * columns
        ),
        name="optimizer",
    )(index, places, tail, first, second, blocks, *ready, *dvecs, *bases, *[basis for basis, _, _ in lines])


def slot_table(owner, slots, owner_rows):
    block_count = owner.shape[0]
    same_owner = owner[:, None] == owner[None, :]
    ordering = jnp.arange(block_count, dtype=jnp.int32)
    earlier = ordering[None, :] < ordering[:, None]
    ranking = jnp.sum(jnp.where(same_owner & earlier, 1, 0), axis=1).astype(jnp.int32)
    owner_match = owner[None, :] == jnp.arange(owner_rows, dtype=jnp.int32)[:, None]
    slot_match = ranking[None, :] == jnp.arange(slots, dtype=jnp.int32)[:, None]
    return jnp.where(slot_match[:, None, :] & owner_match[None, :, :], 1.0, 0.0).astype(full)


def scatter_sum(grads):
    blocks, width = grads.shape[0], grads.shape[2]
    cut = grads.reshape(blocks, lax.axis_size("dp"), -1, width).transpose(1, 0, 2, 3)
    outer = lax.psum_scatter(cut, "dp", scatter_dimension=0, tiled=False)
    blocks, rows, width = outer.shape
    count = lax.axis_size("fsdp")
    cut = outer.reshape(blocks, count, rows // count, width).transpose(1, 0, 2, 3)
    return lax.psum_scatter(cut, "fsdp", scatter_dimension=0, tiled=False)


def scatter_vectors(grads):
    rows, width = grads.shape
    count = lax.axis_size("dp") * lax.axis_size("fsdp")
    cut = grads.reshape(rows, count, width // count).transpose(1, 0, 2)
    return lax.psum_scatter(cut, ("dp", "fsdp"), scatter_dimension=0, tiled=False)


def gathering_program(
    tokens, segment, blocks, vectors, owner, left_basis, right_basis, rot_first, rot_second, cotangent, z_count
):
    layers, vector_rows = vectors.shape[:2]
    count, shard_rows, width = blocks.shape
    per_layer = count // layers
    inner = (per_layer - 4) // 2
    owners = lax.axis_size("dp")
    slots = rot_first.shape[0]
    part = width // owners
    lanes = 128
    seg_column = segment[:, :, None]

    order = [0, 1, 2, 3]
    for c in range(inner):
        order += [4 + c, 4 + inner + c]
    head = order + [per_layer + j for j in order[:4]]
    rest = [per_layer + j for j in order[4:]]
    vec_shard = vectors.astype(low).astype(full).reshape(layers * vector_rows, shard_rows).T
    vec_shard = jnp.pad(vec_shard, ((0, 0), (0, lanes - layers * vector_rows)))[None, None]
    wide_bases = (left_basis.reshape(slots, -1, width), right_basis.transpose(0, 2, 1))

    plan = ForwardPlan(
        inner, 0, blocks, head, vec_shard, vector_rows, [(wide_bases[1], 0, 1)], lead=5, row_positions=(1,),
        z_count=z_count, wide_bases=wide_bases,
    )
    empty_vec = jnp.zeros((16, width), full)
    results = forward_layer(tokens, seg_column, empty_vec, empty_vec, full, plan, 6)
    kept_a = results[:12]
    hidden, weights_a, vec_a, vec_b, right_0, left_low, right_low = results[12:]
    weights_a = weights_a.reshape(-1, width, width)
    plan = ForwardPlan(inner, 4, blocks, rest, lines=[(right_low, 2, 1)], lead=0, row_positions=(1, 4), z_count=z_count)
    plan.order = [per_layer + j for j in range(4)]
    results = forward_layer(hidden, seg_column, vec_b, weights_a, low, plan, 7)
    kept_b = results[:12]
    _, weights_b, right_2 = results[12:]
    gain, shift = vec_b[vector_rows - 2 : vector_rows - 1], vec_b[vector_rows - 1 : vector_rows]
    layer_out = (results[10] * gain + shift).astype(low)
    weights_b = weights_b.reshape(-1, width, width)

    def cut(grads):
        return grads.reshape(-1, owners // 2, 2, part, width)

    size = (part, width)
    own_b, own_a = 4, 3

    def left_over(own):
        return 2 * inner - own, own % 2

    plan = Plan(None, [(right_low, 3, 1)], z_count, own_b, size, wide_ready(own_b))
    dw_wide, dr1, da, dvec_wide_b, wide_sum_b, right_3 = wide_back(
        cotangent, kept_b[5:], vec_b, weights_b, (0, 1, 2), plan, 1
    )
    pending, skip = left_over(own_b)
    plan = Plan(cut(dw_wide), [(right_low, 4, 1), (left_low, 3, 1)], z_count, 1, size, list(range(pending + 1)), skip)
    dw_attend, upstream, dvec_attend_b, attend_sum_b, right_4, left_3 = attend_back(
        da, dr1, hidden, kept_b[:5], seg_column, weights_a, per_layer, plan, 2
    )
    plan = Plan(
        cut(dw_attend), [(left_low, 4, 1), (left_low, 0, 1)], z_count, own_a, size, [0, 1, 2] + wide_ready(own_a)
    )
    dw_wide, dr1, da, dvec_wide_a, wide_sum_a, left_4, left_0 = wide_back(
        upstream, kept_a[5:], vec_a, weights_a, (4, 5, 2), plan, 3
    )
    pending, skip = left_over(own_a)
    plan = Plan(cut(dw_wide), [(left_low, 1, 1), (right_low, 1, 1)], z_count, 1, size, list(range(pending + 1)), skip)
    dw_attend, upstream, dvec_attend_a, attend_sum_a, left_1, right_1 = attend_back(
        da, dr1, tokens, kept_a[:5], seg_column, weights_a, 0, plan, 5
    )

    three = list(range(3))

    def early(own):
        return [4 + n // 2 + inner * (n % 2) for n in range(own)]

    def late(own):
        return [4 + c + inner * k for k in range(2) for c in range(inner) if 2 * c + k >= own] + [3]

    held_order = three + late(own_a) + [per_layer + j for j in three] + early(own_a)
    held_order += [per_layer + j for j in late(own_b) + early(own_b)]
    rank = jnp.asarray([held_order.index(j) for j in range(count)], jnp.int32)
    table = slot_table(owner, slots, owners).reshape(slots * owners, count)
    held = jnp.sum(table, axis=1)
    index = jnp.where(held > 0, jnp.sum(table * rank, axis=1), count).astype(jnp.int32)
    places = jnp.sum(table * jnp.arange(slots * owners, dtype=jnp.int32)[:, None], axis=0).astype(jnp.int32)
    bases = (right_0, right_2, right_3, right_4, left_0, left_1, left_3, left_4, right_1)
    right_map = [(0, 0), (8, 0), (1, 0), (2, 0), (3, 0)]
    left_map = [(4, 0), (5, 0), (9, 0), (6, 0), (7, 0)]
    free = list(range(3, slots))
    new_blocks, new_low, first_new, second_new, vec_sum, _ = optimizer(
        index, places, cut(dw_attend), (attend_sum_a, wide_sum_a, attend_sum_b, wide_sum_b),
        (dvec_attend_a, dvec_wide_a, dvec_attend_b, dvec_wide_b), vector_rows, bases, [(left_low, 2, 1)], left_map, right_map, free,
        rot_first.transpose(0, 2, 1), rot_second.transpose(0, 2, 1), blocks, z_count, 4,
    )
    first_new, second_new = first_new.transpose(0, 2, 1), second_new.transpose(0, 2, 1)
    vector_grad = vec_sum[:, : layers * vector_rows].T.reshape(layers, vector_rows, shard_rows)
    return layer_out, upstream, new_blocks, new_low, first_new, second_new, vector_grad


def plain_program(
    tokens, segment, blocks, vectors, owner, left_basis, right_basis, rot_first, rot_second, cotangent
):
    layers, vector_rows = vectors.shape[:2]
    per_layer = blocks.shape[0] // layers
    inner = (per_layer - 4) // 2
    width = blocks.shape[2]
    owner_rows = lax.axis_size("dp")
    slots = rot_first.shape[0]
    selector = slot_table(owner, slots, owner_rows)
    vector_parts = lax.all_gather(vectors.astype(low), ("dp", "fsdp"), axis=0, tiled=False)
    vector_full = vector_parts.transpose(1, 2, 0, 3).reshape(layers, vector_rows, width).astype(full)
    blocks_low, vector_full = lax.optimization_barrier((blocks.astype(low), vector_full))

    seg_column = segment[:, :, None]
    state = tokens
    kept = []
    for layer_index in range(layers):
        start = per_layer * layer_index
        weights = lax.all_gather(blocks_low[start : start + per_layer], ("dp", "fsdp"), axis=1, tiled=True)
        out_dtype = low if layer_index == layers - 1 else full
        results = forward_layer(
            state, seg_column, vector_full[layer_index], weights, out_dtype, ForwardPlan(inner, per_layer)
        )
        kept.append((state, weights, results[:5], results[5:12]))
        state = results[12]
    layer_out = state
    upstream = cotangent
    right_low = lax.all_gather(right_basis.astype(low), "fsdp", axis=2, tiled=True)
    block_shards = [None] * layers
    vector_shards = [None] * layers
    for layer_index in reversed(range(layers)):
        hidden, weights, attend_kept, wide_kept = kept[layer_index]
        dw_wide, dr1, da, dvec_wide = wide_back(
            upstream, wide_kept, vector_full[layer_index], weights, (4, 4 + inner, 1), Plan()
        )
        wide_shard = scatter_sum(dw_wide.reshape(-1, width, width))
        dw_attend, upstream, dvec_attend = attend_back(
            da, dr1, hidden, attend_kept, seg_column, weights, 0, Plan()
        )
        dvec = jnp.concatenate([dvec_attend[:2], dvec_wide[2:vector_rows]], axis=0)
        block_shards[layer_index] = jnp.concatenate([scatter_sum(dw_attend), wide_shard], axis=0)
        vector_shards[layer_index] = scatter_vectors(dvec)
    vector_grad = jnp.stack(vector_shards)
    block_grad = jnp.concatenate(block_shards, axis=0)
    outgoing = jnp.einsum("srk,kid->srid", selector.astype(low), block_grad, preferred_element_type=full)
    incoming = lax.all_to_all(outgoing.astype(low), "dp", split_axis=1, concat_axis=1, tiled=True)
    owned = incoming.reshape(slots, -1, width)
    turned = jnp.einsum("sik,skj->sij", owned, right_low, preferred_element_type=full).astype(low)
    left_rows = left_basis.reshape(slots, -1, width).astype(low)
    partial_sums = jnp.einsum("sra,srb->sab", left_rows, turned, preferred_element_type=full)
    rotated = lax.psum_scatter(
        partial_sums.astype(low), "fsdp", scatter_dimension=2, tiled=True
    ).astype(full)
    first_new, second_new, direction = moments(rotated, rot_first, rot_second)
    direction_full = lax.all_gather(direction.astype(low), "fsdp", axis=2, tiled=True)
    back_right = jnp.einsum("sab,scb->sac", direction_full, right_low, preferred_element_type=full)
    step_rows = jnp.einsum(
        "sia,sac->sic", left_rows, back_right.astype(low), preferred_element_type=full
    )
    returned = lax.all_to_all(
        step_rows.reshape(slots, owner_rows, -1, width).astype(low),
        "dp",
        split_axis=1,
        concat_axis=1,
        tiled=True,
    )
    step_shard = jnp.einsum("srk,srid->kid", selector.astype(low), returned, preferred_element_type=full)
    new_blocks = blocks - matrix_rate * (step_shard + weight_decay * blocks)
    return layer_out, upstream, new_blocks, new_blocks.astype(low), first_new, second_new, vector_grad


def shards(
    tokens,
    segment,
    blocks,
    vectors,
    owner,
    left_basis,
    right_basis,
    rot_first,
    rot_second,
    vec_first,
    vec_second,
    cotangent,
):
    operands = (
        tokens, segment, blocks, vectors, owner, left_basis, right_basis, rot_first, rot_second, cotangent
    )
    z_count = lax.axis_size("fsdp")
    if lax.axis_size("dp") == 8 and z_count == 4:
        results = gathering_program(*operands, z_count)
    else:
        results = plain_program(*operands)
    layer_out, upstream, new_blocks, new_low, first_new, second_new, vector_grad = results
    vector_first = beta_one * vec_first + (1.0 - beta_one) * vector_grad
    vector_second = beta_two * vec_second + (1.0 - beta_two) * vector_grad * vector_grad
    vector_step = (
        vector_first
        / (1.0 - beta_one**STEP)
        / (jnp.sqrt(vector_second / (1.0 - beta_two**STEP)) + adam_epsilon)
    )
    vector_new = vectors - vector_rate * (vector_step + weight_decay * vectors)
    return (
        layer_out,
        upstream,
        new_blocks,
        new_low,
        first_new,
        second_new,
        vector_first,
        vector_second,
        vector_new,
    )


def solution(mesh):
    return jax.shard_map(
        shards,
        mesh=mesh,
        in_specs=(
            P(("dp", "fsdp"), None),
            P(("dp", "fsdp"), None),
            P(None, ("dp", "fsdp"), None),
            P(None, None, ("dp", "fsdp")),
            P(),
            P("dp", None, "fsdp", None),
            P("dp", None, "fsdp"),
            P("dp", None, "fsdp"),
            P("dp", None, "fsdp"),
            P(None, None, ("dp", "fsdp")),
            P(None, None, ("dp", "fsdp")),
            P(("dp", "fsdp"), None),
        ),
        out_specs=(
            P(("dp", "fsdp"), None),
            P(("dp", "fsdp"), None),
            P(None, ("dp", "fsdp"), None),
            P(None, ("dp", "fsdp"), None),
            P("dp", None, "fsdp"),
            P("dp", None, "fsdp"),
            P(None, None, ("dp", "fsdp")),
            P(None, None, ("dp", "fsdp")),
            P(None, None, ("dp", "fsdp")),
        ),
        check_vma=False,
    )
```
